32 devices in a mesh: wide: 8 (over z, x), narrow: 4 (over y, core).
Axes of the slice: x: 2, y: 2, z: 4, core: 2. Of those that a mesh axis runs over, the one named last changes fastest.
Arguments:
- tokens: bfloat16 [4, 1024, 2048], P('narrow', 'wide'), may hold values from -6 to 6
- attn_gain: bfloat16 [2048], P(('wide', 'narrow')), may hold values from 0.25 to 1.75
- w_query: bfloat16 [2048, 2048], P(('wide', 'narrow')), may hold values from -0.1875 to 0.1875
- w_key: bfloat16 [2048, 512], P(('wide', 'narrow')), may hold values from -0.1875 to 0.1875
- w_value: bfloat16 [2048, 512], P(('wide', 'narrow')), may hold values from -0.125 to 0.125
- w_out: bfloat16 [2048, 2048], P(('wide', 'narrow')), may hold values from -0.5 to 0.5
- mlp_gain: bfloat16 [2048], P(('wide', 'narrow')), may hold values from 0.25 to 1.75
- w_gate: bfloat16 [2048, 5632], P(('wide', 'narrow')), may hold values from -0.125 to 0.125
- w_up: bfloat16 [2048, 5632], P(('wide', 'narrow')), may hold values from -0.125 to 0.125
- w_down: bfloat16 [5632, 2048], P(('wide', 'narrow')), may hold values from -0.15625 to 0.15625
- keep_mask: int32 [4], P('narrow'), may hold values 0 or 1
- group_ids: int32 [4, 1024], P('narrow', 'wide'), may hold values from 0 to 1
- positions: int32 [4, 1024], P('narrow', 'wide'), may hold values from 0 to 2046, as said below
- exit_scale: float32 [2], replicated, may hold values from 0.5 to 2
- out_grad: bfloat16 [4, 1024, 2048], P('narrow', 'wide'), may hold values from -6 to 6
Outputs:
- output: bfloat16 [4, 1024, 2048], P('narrow', 'wide')
- token_grad: bfloat16 [4, 1024, 2048], P('narrow', 'wide')
- grad_attn_gain: float32 [2048], P(('wide', 'narrow'))
- grad_w_query: float32 [2048, 2048], P(('wide', 'narrow'))
- grad_w_key: float32 [2048, 512], P(('wide', 'narrow'))
- grad_w_value: float32 [2048, 512], P(('wide', 'narrow'))
- grad_w_out: float32 [2048, 2048], P(('wide', 'narrow'))
- grad_mlp_gain: float32 [2048], P(('wide', 'narrow'))
- grad_w_gate: float32 [2048, 5632], P(('wide', 'narrow'))
- grad_w_up: float32 [2048, 5632], P(('wide', 'narrow'))
- grad_w_down: float32 [5632, 2048], P(('wide', 'narrow'))
The draws below stay inside these ranges and needn't reach their ends.
Inputs may be any that keep to these rules, and one draw needn't show every extreme that they name: In each sequence positions start at 0 and rise by 1 or 2 from one token to the next.
All inputs are finite; a program needn't handle non-finite values. No bound on the sum of `keep_mask` on one device may be relied on, other than what follows from the above.
Results may differ from the reference program's by a relative error of at most 0.023.
Values may be sent and summed in bfloat16 or wider, within the bound.
A program may use at most 384 MiB of HBM per device.

```python
import math
import jax
import jax.numpy as jnp
from jax import lax

D = 2048
HEADS = 16
KVH = 4
HD = 128
FF = 5632
GROUPS = 2
LENGTH = 1024
SEQUENCES = 4


def draw_positions(key, part):
    key = jax.random.fold_in(key, 11)
    step_key, pick_key = jax.random.split(key)
    increments = jax.random.randint(step_key, (SEQUENCES, LENGTH), 1, 3)
    chosen = jax.random.randint(pick_key, (), 0, SEQUENCES)
    rows = jnp.arange(SEQUENCES, dtype=jnp.int32)[:, None]
    increments = jnp.where(rows == chosen, 2, increments)
    return (jnp.cumsum(increments, axis=1) - increments[:, :1]).astype(jnp.int32)


def place_ends(array, key, low, top_value):
    extent = array.shape
    index_at = [jax.random.randint(jax.random.fold_in(key, axis), (), 0, extent[axis]) for axis in range(len(extent))]
    array = array.at[tuple(index_at)].set(low)
    longest = extent.index(max(extent))
    index_at[longest] = (index_at[longest] + 1) % extent[longest]
    return array.at[tuple(index_at)].set(top_value)


def levels(stream_key, dims, cuts, least, largest):
    def one(dim, shards_of):
        steps = jax.random.uniform(jax.random.fold_in(jax.random.fold_in(stream_key, 6), dim), (shards_of,), jnp.float32, least / len(cuts), largest / len(cuts))
        return jnp.repeat(jnp.exp(steps), dims[dim] // shards_of).reshape((-1,) + (1,) * (len(dims) - dim - 1))

    level = one(*cuts[0])
    for cut in cuts[1:]:
        level = level * one(*cut)
    return level


def normal_values(rng, extent, width, reach, shards=(), held_as=jnp.bfloat16):
    values = jax.random.normal(rng, extent, jnp.float32) * width
    if len(shards) > 0:
        values = levels(rng, extent, shards, -0.22, 0.18) * values
    return jnp.clip(values, min=-reach, max=reach).astype(held_as)


def setup_inputs(seed: int = 0) -> dict:
    seeds = jax.random.split(jax.random.key(seed), 16)
    return {
        "tokens": normal_values(seeds[0], (SEQUENCES, LENGTH, D), 1.0, 6.0, ((0, 4), (1, 8))),
        "attn_gain": jnp.clip(1.0 + 0.15 * jax.random.normal(seeds[1], (D,), jnp.float32), 0.25, 1.75).astype(jnp.bfloat16),
        "w_query": normal_values(seeds[2], (D, HEADS * HD), (D // 2) ** -0.5, 0.1875, ((0, 32),)),
        "w_key": normal_values(seeds[3], (D, KVH * HD), (D // 2) ** -0.5, 0.1875, ((0, 32),)),
        "w_value": normal_values(seeds[4], (D, KVH * HD), D ** -0.5, 0.125, ((0, 32),)),
        "w_out": normal_values(seeds[5], (HEADS * HD, D), (HEADS * HD // 16) ** -0.5, 0.5, ((0, 32),)),
        "mlp_gain": jnp.clip(1.0 + 0.15 * jax.random.normal(seeds[6], (D,), jnp.float32), 0.25, 1.75).astype(jnp.bfloat16),
        "w_gate": normal_values(seeds[7], (D, FF), D ** -0.5, 0.125, ((0, 32),)),
        "w_up": normal_values(seeds[8], (D, FF), D ** -0.5, 0.125, ((0, 32),)),
        "w_down": normal_values(seeds[9], (FF, D), (FF // 4) ** -0.5, 0.15625, ((0, 32),)),
        "keep_mask": place_ends((jax.random.randint(seeds[10], (SEQUENCES,), 0, 4) < 3).astype(jnp.int32), jax.random.fold_in(seeds[10], 1), 0, 1),
        "group_ids": place_ends(jax.random.randint(seeds[11], (SEQUENCES, LENGTH), 0, GROUPS), jax.random.fold_in(seeds[11], 1), 0, GROUPS - 1).astype(jnp.int32),
        "positions": draw_positions(jax.random.fold_in(seeds[15], 71), 0),
        "exit_scale": jnp.clip(jnp.exp(jax.random.uniform(seeds[13], (GROUPS,), jnp.float32, math.log(0.5), math.log(2.0))), 0.5, 2.0),
        "out_grad": normal_values(seeds[14], (SEQUENCES, LENGTH, D), 1.0, 6.0, ((0, 4), (1, 8))),
    }


epsilon = 1e-05
highest = lax.Precision.HIGHEST

@jax.custom_vjp
def low(v):
    return lax.optimization_barrier(v.astype(jnp.bfloat16)).astype(jnp.float32)

@jax.custom_vjp
def low_back(v):
    return v

def low_keep(v):
    return (low(v), None)

def low_pass(kept, grad):
    return (grad,)

def back_keep(v):
    return (v, None)

def back_low(kept, grad):
    return (low(grad),)
low.defvjp(low_keep, low_pass)
low_back.defvjp(back_keep, back_low)

def product(left, right):
    return jnp.dot(left, right, precision=highest, preferred_element_type=jnp.float32)

def rotate(vectors, token_pos, direction):
    half_size = vectors.shape[-1] // 2
    freqs = 10000.0 ** (-2.0 * jnp.arange(half_size, dtype=jnp.float32) / vectors.shape[-1])
    angles = token_pos.astype(jnp.float32)[:, None] * freqs[None, :]
    cosine = jnp.cos(angles)[:, None, :]
    sine = direction * jnp.sin(angles)[:, None, :]
    first_half = vectors[..., :half_size]
    second_half = vectors[..., half_size:]
    return jnp.concatenate([first_half * cosine - second_half * sine, second_half * cosine + first_half * sine], axis=-1)

def normed(values, gain):
    inverse = lax.rsqrt(lax.optimization_barrier(jnp.mean(values * values, axis=-1, keepdims=True)) + epsilon)
    return values * inverse * gain

def attention(queries, key_heads, value_heads):
    length = queries.shape[0]
    rows_block = math.gcd(length, 512)
    score_scale = 1.0 / math.sqrt(HD)
    key_index = jnp.arange(length, dtype=jnp.int32)

    def query_block(block_index):
        first_row = block_index * rows_block
        query_part = lax.dynamic_slice_in_dim(queries, first_row, rows_block, 0)
        scores = jnp.einsum('tkgd,jkd->kgtj', query_part, key_heads, precision=highest) * score_scale
        scores = low_back(scores)
        query_index = first_row + jnp.arange(rows_block, dtype=jnp.int32)
        allowed = key_index[None, :] <= query_index[:, None]
        scores = jnp.where(allowed, scores, -1e+30)
        row_peak = lax.optimization_barrier(jnp.max(scores, axis=-1, keepdims=True))
        weights = jnp.exp(scores - row_peak)
        probabilities = low(weights / lax.optimization_barrier(jnp.sum(weights, axis=-1, keepdims=True)))
        attended = jnp.einsum('kgtj,jkd->tkgd', probabilities, value_heads, precision=highest)
        return attended.reshape(rows_block, -1)
    blocks = lax.map(jax.checkpoint(query_block), jnp.arange(length // rows_block, dtype=jnp.int32))
    return blocks.reshape(length, -1)

def whole_layer(inputs, weight_list, keep_value, token_pos):
    attn_gain, w_query, w_key, w_value, w_out, mlp_gain, w_gate, w_up, w_down = weight_list
    length = inputs.shape[0]
    group_size = HEADS // KVH
    first_norm = low(normed(inputs, attn_gain))
    query_pre = low_back(product(first_norm, w_query)).reshape(length, HEADS, HD)
    key_pre = low_back(product(first_norm, w_key)).reshape(length, KVH, HD)
    value_heads = low(low_back(product(first_norm, w_value))).reshape(length, KVH, HD)
    queries = low(rotate(query_pre, token_pos, 1.0)).reshape(length, KVH, group_size, HD)
    key_heads = low(rotate(key_pre, token_pos, 1.0))
    attended = low(low_back(attention(queries, key_heads, value_heads)))
    middle = inputs + keep_value * low_back(product(attended, w_out))
    second_norm = low(normed(middle, mlp_gain))
    gate_value = low_back(product(second_norm, w_gate))
    up_value = low_back(product(second_norm, w_up))
    hidden = low(gate_value * jax.nn.sigmoid(gate_value) * up_value)
    return middle + keep_value * low_back(product(hidden, w_down))

def reference(tokens, attn_gain, w_query, w_key, w_value, w_out, mlp_gain, w_gate, w_up, w_down, keep_mask, group_ids, positions, exit_scale, out_grad):
    weight_list = tuple((weight.astype(jnp.float32) for weight in (attn_gain, w_query, w_key, w_value, w_out, mlp_gain, w_gate, w_up, w_down)))

    def per_sequence(totals, seq_item):
        inputs, keep_flag, token_pos, token_group, cotangent = seq_item
        keep_value = keep_flag.astype(jnp.float32)

        def forward(values, *weights):
            return whole_layer(values, weights, keep_value, token_pos)
        result, pullback = jax.vjp(forward, inputs.astype(jnp.float32), *weight_list)
        scaled = cotangent.astype(jnp.float32) * exit_scale[token_group][:, None]
        gradients = pullback(scaled)
        totals = tuple((running + gradient for running, gradient in zip(totals, gradients[1:])))
        return (totals, (result.astype(jnp.bfloat16), gradients[0].astype(jnp.bfloat16)))
    start_totals = tuple((jnp.zeros_like(weight) for weight in weight_list))
    totals, outputs = lax.scan(per_sequence, start_totals, (tokens, keep_mask, positions, group_ids, out_grad))
    return (outputs[0], outputs[1], totals[0], totals[1], totals[2], totals[3], totals[4], totals[5], totals[6], totals[7], totals[8])
```

```python
import math

import jax
import jax.numpy as jnp
from jax import lax
from jax.sharding import PartitionSpec as P

HEADS = 16
KVH = 4
HD = 128


epsilon = 1e-05


def rotate(vectors, token_pos, direction):
    half_size = vectors.shape[-1] // 2
    freqs = 10000.0 ** (-2.0 * jnp.arange(half_size, dtype=jnp.float32) / vectors.shape[-1])
    angles = token_pos.astype(jnp.float32)[:, None] * freqs[None, :]
    cosine = jnp.cos(angles)[:, None, :]
    sine = direction * jnp.sin(angles)[:, None, :]
    first_half = vectors[..., :half_size]
    second_half = vectors[..., half_size:]
    return jnp.concatenate(
        [first_half * cosine - second_half * sine, second_half * cosine + first_half * sine],
        axis=-1,
    )


def split_blocks(piece_arr, seq_count, kv_heads, head_dim):
    piece_len = piece_arr.shape[1]
    block_len = math.gcd(piece_len, 512)
    shaped = piece_arr.reshape(seq_count, piece_len // block_len, block_len, kv_heads, head_dim)
    return shaped.transpose(1, 0, 2, 3, 4)


def add_rows(whole_arr, update, first_row):
    current = lax.dynamic_slice_in_dim(whole_arr, first_row, update.shape[1], 1)
    return lax.dynamic_update_slice_in_dim(whole_arr, current + update, first_row, 1)


def over_rows(left, right):
    return lax.dot_general(
        left, right, (((0,), (0,)), ((), ())), preferred_element_type=jnp.float32
    )


def against(left, right):
    return lax.dot_general(
        left, right, (((1,), (1,)), ((), ())), preferred_element_type=jnp.float32
    )


def unchanged(carried):
    return carried


def general_body(
    tokens,
    attn_gain,
    w_query,
    w_key,
    w_value,
    w_out,
    mlp_gain,
    w_gate,
    w_up,
    w_down,
    keep_mask,
    group_ids,
    positions,
    exit_scale,
    out_grad,
):
    seq_count, span_len, model_width = tokens.shape
    kv_heads = KVH
    head_dim = HD
    head_count = HEADS
    group_size = head_count // kv_heads
    row_count = seq_count * span_len
    stripe = group_size * span_len
    wide_count = lax.axis_size("wide")
    wide_place = lax.axis_index("wide")
    full_len = span_len * wide_count
    score_scale = 1.0 / math.sqrt(head_dim)
    gain_one, query_w, key_w, value_w, out_w = (
        lax.all_gather(attn_gain, ("wide", "narrow"), axis=0, tiled=True),
        lax.all_gather(w_query, ("wide", "narrow"), axis=0, tiled=True),
        lax.all_gather(w_key, ("wide", "narrow"), axis=0, tiled=True),
        lax.all_gather(w_value, ("wide", "narrow"), axis=0, tiled=True),
        lax.all_gather(w_out, ("wide", "narrow"), axis=0, tiled=True),
    )
    inputs = tokens.astype(jnp.float32).reshape(row_count, model_width)
    token_pos = positions.reshape(row_count)
    keep_rows = jnp.repeat(keep_mask.astype(jnp.float32), span_len)[:, None]
    inverse_one = lax.rsqrt(jnp.mean(inputs * inputs, axis=-1, keepdims=True) + epsilon)
    first_norm = (inputs * inverse_one * gain_one.astype(jnp.float32)).astype(jnp.bfloat16)
    query_pre = jnp.dot(first_norm, query_w, preferred_element_type=jnp.float32).reshape(
        row_count, head_count, head_dim
    )
    key_pre = jnp.dot(first_norm, key_w, preferred_element_type=jnp.float32).reshape(
        row_count, kv_heads, head_dim
    )
    query_rows = rotate(query_pre, token_pos, 1.0).astype(jnp.bfloat16)
    key_heads = (
        rotate(key_pre, token_pos, 1.0)
        .astype(jnp.bfloat16)
        .reshape(seq_count, span_len, kv_heads * head_dim)
    )
    value_heads = (
        jnp.dot(first_norm, value_w, preferred_element_type=jnp.float32)
        .astype(jnp.bfloat16)
        .reshape(seq_count, span_len, kv_heads * head_dim)
    )
    queries = (
        query_rows.reshape(seq_count, span_len, kv_heads, group_size, head_dim)
        .transpose(0, 2, 3, 1, 4)
        .reshape(seq_count, kv_heads, stripe, head_dim)
    )
    query_index = wide_place * span_len + jnp.arange(stripe, dtype=jnp.int32) % span_len
    last_query = wide_place * span_len + span_len - 1

    def block_scores(key_block, key_first):
        scores = (
            jnp.einsum("skrd,sjkd->skrj", queries, key_block, preferred_element_type=jnp.float32)
            * score_scale
        )
        key_index = key_first + jnp.arange(key_block.shape[1], dtype=jnp.int32)
        allowed = key_index[None, :] <= query_index[:, None]
        return (scores, allowed)

    start_forward = (
        jnp.full((seq_count, kv_heads, stripe), -1e30, jnp.float32),
        jnp.zeros((seq_count, kv_heads, stripe), jnp.float32),
        jnp.zeros((seq_count, kv_heads, stripe, head_dim), jnp.float32),
    )
    running = start_forward
    pieces = (
        lax.all_gather(key_heads, "wide", axis=1, tiled=True),
        lax.all_gather(value_heads, "wide", axis=1, tiled=True),
    )
    key_blocks = split_blocks(pieces[0], seq_count, kv_heads, head_dim)
    value_blocks = split_blocks(pieces[1], seq_count, kv_heads, head_dim)
    block_len = key_blocks.shape[2]

    def advance(carried, block_item):
        key_block, value_block, block_index = block_item
        key_first = block_index * block_len

        def compute_block(current):
            run_max, run_sum, run_acc = current
            scores, allowed = block_scores(key_block, key_first)
            scores = jnp.where(allowed, scores, -1e30)
            new_max = jnp.maximum(run_max, jnp.max(scores, axis=-1))
            factor = jnp.exp(run_max - new_max)
            weights = jnp.where(allowed, jnp.exp(scores - new_max[..., None]), 0.0)
            new_sum = run_sum * factor + jnp.sum(weights, axis=-1)
            new_acc = run_acc * factor[..., None] + jnp.einsum(
                "skrj,sjkd->skrd",
                weights.astype(jnp.bfloat16),
                value_block,
                preferred_element_type=jnp.float32,
            )
            return (new_max, new_sum, new_acc)

        return (lax.cond(key_first <= last_query, compute_block, unchanged, carried), None)

    running, _ = lax.scan(
        advance,
        running,
        (key_blocks, value_blocks, jnp.arange(key_blocks.shape[0], dtype=jnp.int32)),
    )
    run_max, run_sum, run_acc = running
    attended = run_acc / run_sum[..., None]
    log_total = run_max + jnp.log(run_sum)
    attended_rows = (
        attended.reshape(seq_count, kv_heads, group_size, span_len, head_dim)
        .transpose(0, 3, 1, 2, 4)
        .reshape(row_count, head_count * head_dim)
        .astype(jnp.bfloat16)
    )
    middle = inputs + keep_rows * jnp.dot(attended_rows, out_w, preferred_element_type=jnp.float32)
    gain_two, gate_w, up_w, down_w = (
        lax.all_gather(mlp_gain, ("wide", "narrow"), axis=0, tiled=True),
        lax.all_gather(w_gate, ("wide", "narrow"), axis=0, tiled=True),
        lax.all_gather(w_up, ("wide", "narrow"), axis=0, tiled=True),
        lax.all_gather(w_down, ("wide", "narrow"), axis=0, tiled=True),
    )
    inverse_two = lax.rsqrt(jnp.mean(middle * middle, axis=-1, keepdims=True) + epsilon)
    second_norm = (middle * inverse_two * gain_two.astype(jnp.float32)).astype(jnp.bfloat16)
    gate_value = jnp.dot(second_norm, gate_w, preferred_element_type=jnp.float32)
    up_value = jnp.dot(second_norm, up_w, preferred_element_type=jnp.float32)
    gate_sigmoid = jax.nn.sigmoid(gate_value)
    swish_value = gate_value * gate_sigmoid
    hidden = (swish_value * up_value).astype(jnp.bfloat16)
    output = (
        middle + keep_rows * jnp.dot(hidden, down_w, preferred_element_type=jnp.float32)
    ).astype(jnp.bfloat16)
    group_match = (
        group_ids.reshape(row_count)[:, None]
        == jnp.arange(exit_scale.shape[0], dtype=jnp.int32)[None, :]
    )
    token_scale = jnp.sum(jnp.where(group_match, exit_scale[None, :], 0.0), axis=1, keepdims=True)
    upstream = out_grad.astype(jnp.float32).reshape(row_count, model_width) * token_scale
    gain_two, gate_w, up_w, down_w = (
        lax.all_gather(mlp_gain, ("wide", "narrow"), axis=0, tiled=True),
        lax.all_gather(w_gate, ("wide", "narrow"), axis=0, tiled=True),
        lax.all_gather(w_up, ("wide", "narrow"), axis=0, tiled=True),
        lax.all_gather(w_down, ("wide", "narrow"), axis=0, tiled=True),
    )
    mixed_grad = (keep_rows * upstream).astype(jnp.bfloat16)
    grad_down = over_rows(hidden, mixed_grad)
    hidden_grad = against(mixed_grad, down_w)
    gate_grad = (
        hidden_grad * up_value * gate_sigmoid * (1.0 + gate_value * (1.0 - gate_sigmoid))
    ).astype(jnp.bfloat16)
    up_grad = (hidden_grad * swish_value).astype(jnp.bfloat16)
    grad_gate = over_rows(second_norm, gate_grad)
    grad_up = over_rows(second_norm, up_grad)
    norm_grad = against(gate_grad, gate_w) + against(up_grad, up_w)
    grad_gain_two = jnp.sum(norm_grad * middle * inverse_two, axis=0)
    scaled_two = gain_two.astype(jnp.float32) * norm_grad
    middle_grad = (
        upstream
        + inverse_two * scaled_two
        - middle
        * (inverse_two * inverse_two * inverse_two)
        * jnp.mean(scaled_two * middle, axis=-1, keepdims=True)
    )
    gain_two_share, gate_share, up_share, down_share = (
        lax.psum_scatter(grad_gain_two, ("wide", "narrow"), scatter_dimension=0, tiled=True),
        lax.psum_scatter(grad_gate, ("wide", "narrow"), scatter_dimension=0, tiled=True),
        lax.psum_scatter(grad_up, ("wide", "narrow"), scatter_dimension=0, tiled=True),
        lax.psum_scatter(grad_down, ("wide", "narrow"), scatter_dimension=0, tiled=True),
    )
    gain_one, query_w, key_w, value_w, out_w = (
        lax.all_gather(attn_gain, ("wide", "narrow"), axis=0, tiled=True),
        lax.all_gather(w_query, ("wide", "narrow"), axis=0, tiled=True),
        lax.all_gather(w_key, ("wide", "narrow"), axis=0, tiled=True),
        lax.all_gather(w_value, ("wide", "narrow"), axis=0, tiled=True),
        lax.all_gather(w_out, ("wide", "narrow"), axis=0, tiled=True),
    )
    branch_grad = (keep_rows * middle_grad).astype(jnp.bfloat16)
    grad_out = over_rows(attended_rows, branch_grad)
    attended_grad = against(branch_grad, out_w).astype(jnp.bfloat16)
    grouped_grad = (
        attended_grad.reshape(seq_count, span_len, kv_heads, group_size, head_dim)
        .transpose(0, 2, 3, 1, 4)
        .reshape(seq_count, kv_heads, stripe, head_dim)
    )
    row_delta = jnp.sum(grouped_grad.astype(jnp.float32) * attended, axis=-1)
    start_backward = (
        jnp.zeros((seq_count, kv_heads, stripe, head_dim), jnp.float32),
        jnp.zeros((seq_count, full_len, kv_heads * head_dim), jnp.float32),
        jnp.zeros((seq_count, full_len, kv_heads * head_dim), jnp.float32),
    )
    running = start_backward
    pieces = (
        lax.all_gather(key_heads, "wide", axis=1, tiled=True),
        lax.all_gather(value_heads, "wide", axis=1, tiled=True),
    )
    key_blocks = split_blocks(pieces[0], seq_count, kv_heads, head_dim)
    value_blocks = split_blocks(pieces[1], seq_count, kv_heads, head_dim)
    fold_block_len = key_blocks.shape[2]

    def advance(carried, block_item):
        key_block, value_block, block_index = block_item
        key_first = block_index * fold_block_len

        def compute_block(current):
            query_acc, key_acc, value_acc = current
            scores, allowed = block_scores(key_block, key_first)
            probabilities = jnp.where(allowed, jnp.exp(scores - log_total[..., None]), 0.0)
            value_part = jnp.einsum(
                "skrj,skrd->sjkd",
                probabilities.astype(jnp.bfloat16),
                grouped_grad,
                preferred_element_type=jnp.float32,
            )
            prob_grad = jnp.einsum(
                "skrd,sjkd->skrj", grouped_grad, value_block, preferred_element_type=jnp.float32
            )
            score_grad = (probabilities * (prob_grad - row_delta[..., None])).astype(jnp.bfloat16)
            query_acc = (
                query_acc
                + jnp.einsum(
                    "skrj,sjkd->skrd", score_grad, key_block, preferred_element_type=jnp.float32
                )
                * score_scale
            )
            key_part = (
                jnp.einsum(
                    "skrj,skrd->sjkd", score_grad, queries, preferred_element_type=jnp.float32
                )
                * score_scale
            )
            key_acc = add_rows(
                key_acc, key_part.reshape(seq_count, fold_block_len, kv_heads * head_dim), key_first
            )
            value_acc = add_rows(
                value_acc,
                value_part.reshape(seq_count, fold_block_len, kv_heads * head_dim),
                key_first,
            )
            return (query_acc, key_acc, value_acc)

        return (lax.cond(key_first <= last_query, compute_block, unchanged, carried), None)

    running, _ = lax.scan(
        advance,
        running,
        (key_blocks, value_blocks, jnp.arange(key_blocks.shape[0], dtype=jnp.int32)),
    )
    query_acc, key_acc, value_acc = running
    key_sum, value_sum = (
        lax.psum_scatter(
            key_acc.astype(jnp.bfloat16), "wide", scatter_dimension=1, tiled=True
        ).astype(jnp.float32),
        lax.psum_scatter(
            value_acc.astype(jnp.bfloat16), "wide", scatter_dimension=1, tiled=True
        ).astype(jnp.float32),
    )
    query_back = (
        query_acc.reshape(seq_count, kv_heads, group_size, span_len, head_dim)
        .transpose(0, 3, 1, 2, 4)
        .reshape(row_count, head_count, head_dim)
    )
    query_grad = (
        rotate(query_back, token_pos, -1.0)
        .reshape(row_count, head_count * head_dim)
        .astype(jnp.bfloat16)
    )
    key_grad = (
        rotate(key_sum.reshape(row_count, kv_heads, head_dim), token_pos, -1.0)
        .reshape(row_count, kv_heads * head_dim)
        .astype(jnp.bfloat16)
    )
    value_grad = value_sum.reshape(row_count, kv_heads * head_dim).astype(jnp.bfloat16)
    grad_query = over_rows(first_norm, query_grad)
    grad_key = over_rows(first_norm, key_grad)
    grad_value = over_rows(first_norm, value_grad)
    input_norm_grad = (
        against(query_grad, query_w) + against(key_grad, key_w) + against(value_grad, value_w)
    )
    grad_gain_one = jnp.sum(input_norm_grad * inputs * inverse_one, axis=0)
    scaled_one = gain_one.astype(jnp.float32) * input_norm_grad
    input_grad = (
        middle_grad
        + inverse_one * scaled_one
        - inputs
        * (inverse_one * inverse_one * inverse_one)
        * jnp.mean(scaled_one * inputs, axis=-1, keepdims=True)
    )
    gain_one_share, query_share, key_share, value_share, out_share = (
        lax.psum_scatter(grad_gain_one, ("wide", "narrow"), scatter_dimension=0, tiled=True),
        lax.psum_scatter(grad_query, ("wide", "narrow"), scatter_dimension=0, tiled=True),
        lax.psum_scatter(grad_key, ("wide", "narrow"), scatter_dimension=0, tiled=True),
        lax.psum_scatter(grad_value, ("wide", "narrow"), scatter_dimension=0, tiled=True),
        lax.psum_scatter(grad_out, ("wide", "narrow"), scatter_dimension=0, tiled=True),
    )
    return (
        output.reshape(seq_count, span_len, model_width),
        input_grad.astype(jnp.bfloat16).reshape(seq_count, span_len, model_width),
        gain_one_share,
        query_share,
        key_share,
        value_share,
        out_share,
        gain_two_share,
        gate_share,
        up_share,
        down_share,
    )


def group_body(
    tokens,
    attn_gain,
    w_query,
    w_key,
    w_value,
    w_out,
    mlp_gain,
    w_gate,
    w_up,
    w_down,
    keep_mask,
    group_ids,
    positions,
    exit_scale,
    out_grad,
):
    _, span_len, model_width = tokens.shape
    wide_count = lax.axis_size("wide")
    narrow_count = lax.axis_size("narrow")
    wide_place = lax.axis_index("wide")
    device_count = wide_count * narrow_count
    rows_each = w_query.shape[0]
    full_len = span_len * wide_count
    score_scale = 1.0 / math.sqrt(HD)
    head_each = HEADS // wide_count
    q_cols = head_each * HD
    ff_cols = w_gate.shape[1] // wide_count
    kv_share = wide_count // KVH
    f32 = jnp.float32
    bf16 = jnp.bfloat16

    def spread(values):
        return lax.all_gather(values, "wide", axis=0, tiled=True)

    def collect(values):
        return lax.psum_scatter(values.astype(bf16), "wide", scatter_dimension=0, tiled=True)

    def by_columns(weight, columns):
        return weight.reshape(rows_each, -1, columns).transpose(1, 0, 2)

    pack_attn = jnp.concatenate(
        [
            by_columns(w_query, q_cols),
            jnp.repeat(by_columns(w_key, HD), kv_share, axis=0),
            jnp.repeat(by_columns(w_value, HD), kv_share, axis=0),
        ],
        axis=2,
    )
    pack_ff = jnp.concatenate([by_columns(w_gate, ff_cols), by_columns(w_up, ff_cols)], axis=2)

    def share_columns(pack):
        got = lax.all_to_all(pack, "wide", 0, 0, tiled=True)
        full = lax.all_gather(got, "narrow", axis=1)
        return full.reshape(model_width, pack.shape[2])

    qkv_w = share_columns(pack_attn)
    ff_w = share_columns(pack_ff)
    out_w = lax.all_gather(w_out, "narrow", axis=0, tiled=True)
    down_w = lax.all_gather(w_down, "narrow", axis=0, tiled=True)
    gains = lax.all_gather(jnp.stack([attn_gain, mlp_gain]), ("wide", "narrow"), axis=1, tiled=True)
    gain_one = gains[0].astype(f32)
    gain_two = gains[1].astype(f32)

    own_x = tokens[0].astype(f32)
    keep = keep_mask[0].astype(f32)
    group_match = group_ids[0][:, None] == jnp.arange(exit_scale.shape[0], dtype=jnp.int32)[None, :]
    token_scale = jnp.sum(jnp.where(group_match, exit_scale[None, :], 0.0), axis=1, keepdims=True)
    upstream = out_grad[0].astype(f32) * token_scale
    mixed_grad = spread((keep * upstream).astype(bf16))

    inputs = spread(tokens[0]).astype(f32)
    token_pos = lax.all_gather(positions[0], "wide", axis=0, tiled=True)
    inverse_all = lax.rsqrt(jnp.mean(inputs * inputs, axis=-1, keepdims=True) + epsilon)
    first_norm = (inputs * inverse_all * gain_one).astype(bf16)
    qkv = jnp.dot(first_norm, qkv_w, preferred_element_type=f32)
    queries = rotate(qkv[:, :q_cols].reshape(full_len, head_each, HD), token_pos, 1.0).astype(bf16)
    keys = rotate(qkv[:, q_cols : q_cols + HD].reshape(full_len, 1, HD), token_pos, 1.0)[:, 0].astype(bf16)
    values = qkv[:, q_cols + HD :].astype(bf16)
    scores = jnp.einsum("tgd,jd->gtj", queries, keys, preferred_element_type=f32) * score_scale
    place = jnp.arange(full_len, dtype=jnp.int32)
    allowed = place[None, :] <= place[:, None]
    scores = jnp.where(allowed, scores, -1e30)
    weights = jnp.exp(scores - jnp.max(scores, axis=-1, keepdims=True))
    probabilities = weights / jnp.sum(weights, axis=-1, keepdims=True)
    rounded_probs = probabilities.astype(bf16)
    attended = jnp.einsum("gtj,jd->tgd", rounded_probs, values, preferred_element_type=f32)
    attended_rows = attended.reshape(full_len, q_cols).astype(bf16)
    branch = collect(jnp.dot(attended_rows, out_w, preferred_element_type=f32))
    middle = own_x + keep * branch.astype(f32)
    inverse_two = lax.rsqrt(jnp.mean(middle * middle, axis=-1, keepdims=True) + epsilon)
    second_norm = spread((middle * inverse_two * gain_two).astype(bf16))
    gate_up = jnp.dot(second_norm, ff_w, preferred_element_type=f32)
    gate_value = gate_up[:, :ff_cols]
    up_value = gate_up[:, ff_cols:]
    gate_sigmoid = jax.nn.sigmoid(gate_value)
    swish_value = gate_value * gate_sigmoid
    hidden = (swish_value * up_value).astype(bf16)
    hidden_grad = against(mixed_grad, down_w)
    gate_grad = hidden_grad * up_value * gate_sigmoid * (1.0 + gate_value * (1.0 - gate_sigmoid))
    up_grad = hidden_grad * swish_value
    both_grad = jnp.concatenate([gate_grad, up_grad], axis=1).astype(bf16)
    norm_grad = collect(against(both_grad, ff_w)).astype(f32)
    mixed = collect(jnp.dot(hidden, down_w, preferred_element_type=f32)).astype(f32)
    output = (middle + keep * mixed).astype(bf16)
    grad_gain_two = jnp.sum(norm_grad * middle * inverse_two, axis=0)
    scaled_two = gain_two * norm_grad
    middle_grad = (
        upstream
        + inverse_two * scaled_two
        - middle
        * (inverse_two * inverse_two * inverse_two)
        * jnp.mean(scaled_two * middle, axis=-1, keepdims=True)
    )
    branch_grad = spread((keep * middle_grad).astype(bf16))
    attended_grad = against(branch_grad, out_w).astype(bf16).reshape(full_len, head_each, HD)
    prob_grad = jnp.einsum("tgd,jd->gtj", attended_grad, values, preferred_element_type=f32)
    delta = jnp.sum(attended_grad.astype(f32) * attended, axis=-1).T[..., None]
    score_grad = (probabilities * (prob_grad - delta)).astype(bf16)
    query_back = jnp.einsum("gtj,jd->tgd", score_grad, keys, preferred_element_type=f32) * score_scale
    key_back = jnp.einsum("gtj,tgd->jd", score_grad, queries, preferred_element_type=f32) * score_scale
    value_back = jnp.einsum("gtj,tgd->jd", rounded_probs, attended_grad, preferred_element_type=f32)
    qkv_grad = jnp.concatenate(
        [
            rotate(query_back, token_pos, -1.0).reshape(full_len, q_cols),
            rotate(key_back[:, None], token_pos, -1.0)[:, 0],
            value_back,
        ],
        axis=1,
    ).astype(bf16)
    input_norm_grad = collect(against(qkv_grad, qkv_w)).astype(f32)
    inverse_one = lax.rsqrt(jnp.mean(own_x * own_x, axis=-1, keepdims=True) + epsilon)
    grad_gain_one = jnp.sum(input_norm_grad * own_x * inverse_one, axis=0)
    scaled_one = gain_one * input_norm_grad
    input_grad = (
        middle_grad
        + inverse_one * scaled_one
        - own_x
        * (inverse_one * inverse_one * inverse_one)
        * jnp.mean(scaled_one * own_x, axis=-1, keepdims=True)
    )

    def return_columns(grad):
        summed = lax.psum_scatter(
            grad.astype(bf16).reshape(wide_count, narrow_count, rows_each, -1),
            "narrow",
            scatter_dimension=1,
            tiled=False,
        )
        return lax.all_to_all(summed, "wide", 0, 0, tiled=True)

    def side_by_side(blocks):
        return blocks.transpose(1, 0, 2).reshape(rows_each, -1)

    qkv_back = return_columns(over_rows(first_norm, qkv_grad)).astype(f32)
    ff_back = return_columns(over_rows(second_norm, both_grad)).astype(f32)
    kv_back = qkv_back[:, :, q_cols:].reshape(KVH, kv_share, rows_each, 2 * HD).sum(axis=1)
    grad_out = lax.psum_scatter(
        over_rows(attended_rows, branch_grad).astype(bf16), "narrow", scatter_dimension=0, tiled=True
    ).astype(f32)
    grad_down = lax.psum_scatter(
        over_rows(hidden, mixed_grad).astype(bf16), "narrow", scatter_dimension=0, tiled=True
    ).astype(f32)
    gain_grads = lax.psum_scatter(
        jnp.stack([grad_gain_one, grad_gain_two]), ("wide", "narrow"), scatter_dimension=1, tiled=True
    )
    return (
        output[None],
        input_grad.astype(bf16)[None],
        gain_grads[0],
        side_by_side(qkv_back[:, :, :q_cols]),
        side_by_side(kv_back[:, :, :HD]),
        side_by_side(kv_back[:, :, HD:]),
        grad_out,
        gain_grads[1],
        side_by_side(ff_back[:, :, :ff_cols]),
        side_by_side(ff_back[:, :, ff_cols:]),
        grad_down,
    )


def solution(mesh):
    placed = (
        P("narrow", "wide", None),
        P(("wide", "narrow")),
        P(("wide", "narrow"), None),
        P(("wide", "narrow"), None),
        P(("wide", "narrow"), None),
        P(("wide", "narrow"), None),
        P(("wide", "narrow")),
        P(("wide", "narrow"), None),
        P(("wide", "narrow"), None),
        P(("wide", "narrow"), None),
        P("narrow"),
        P("narrow", "wide"),
        P("narrow", "wide"),
        P(),
        P("narrow", "wide", None),
    )
    wide_count = mesh.shape["wide"]
    grouped = mesh.shape["narrow"] == 4 and HEADS % wide_count == 0 and wide_count % KVH == 0
    return jax.shard_map(
        group_body if grouped else general_body,
        mesh=mesh,
        in_specs=placed,
        out_specs=(
            P("narrow", "wide", None),
            P("narrow", "wide", None),
            P(("wide", "narrow")),
            P(("wide", "narrow"), None),
            P(("wide", "narrow"), None),
            P(("wide", "narrow"), None),
            P(("wide", "narrow"), None),
            P(("wide", "narrow")),
            P(("wide", "narrow"), None),
            P(("wide", "narrow"), None),
            P(("wide", "narrow"), None),
        ),
        check_vma=False,
    )
```

```python
import math

import jax
import jax.numpy as jnp
from jax import lax
from jax.sharding import Mesh
from jax.sharding import PartitionSpec as P

HEADS = 16
KVH = 4
HD = 128


epsilon = 1e-05


def rotate(vectors, token_pos, direction):
    half_size = vectors.shape[-1] // 2
    freqs = 10000.0 ** (-2.0 * jnp.arange(half_size, dtype=jnp.float32) / vectors.shape[-1])
    angles = token_pos.astype(jnp.float32)[:, None] * freqs[None, :]
    cosine = jnp.cos(angles)[:, None, :]
    sine = direction * jnp.sin(angles)[:, None, :]
    first_half = vectors[..., :half_size]
    second_half = vectors[..., half_size:]
    return jnp.concatenate(
        [first_half * cosine - second_half * sine, second_half * cosine + first_half * sine],
        axis=-1,
    )


def split_blocks(piece_arr, seq_count, kv_heads, head_dim):
    piece_len = piece_arr.shape[1]
    block_len = math.gcd(piece_len, 512)
    shaped = piece_arr.reshape(seq_count, piece_len // block_len, block_len, kv_heads, head_dim)
    return shaped.transpose(1, 0, 2, 3, 4)


def add_rows(whole_arr, update, first_row):
    current = lax.dynamic_slice_in_dim(whole_arr, first_row, update.shape[1], 1)
    return lax.dynamic_update_slice_in_dim(whole_arr, current + update, first_row, 1)


def over_rows(left, right):
    return lax.dot_general(
        left, right, (((0,), (0,)), ((), ())), preferred_element_type=jnp.float32
    )


def against(left, right):
    return lax.dot_general(
        left, right, (((1,), (1,)), ((), ())), preferred_element_type=jnp.float32
    )


def unchanged(carried):
    return carried


def general_body(
    tokens,
    attn_gain,
    w_query,
    w_key,
    w_value,
    w_out,
    mlp_gain,
    w_gate,
    w_up,
    w_down,
    keep_mask,
    group_ids,
    positions,
    exit_scale,
    out_grad,
):
    seq_count, span_len, model_width = tokens.shape
    kv_heads = KVH
    head_dim = HD
    head_count = HEADS
    group_size = head_count // kv_heads
    row_count = seq_count * span_len
    stripe = group_size * span_len
    wide_count = lax.axis_size("wide")
    wide_place = lax.axis_index("wide")
    full_len = span_len * wide_count
    score_scale = 1.0 / math.sqrt(head_dim)
    gain_one, query_w, key_w, value_w, out_w = (
        lax.all_gather(attn_gain, ("wide", "narrow"), axis=0, tiled=True),
        lax.all_gather(w_query, ("wide", "narrow"), axis=0, tiled=True),
        lax.all_gather(w_key, ("wide", "narrow"), axis=0, tiled=True),
        lax.all_gather(w_value, ("wide", "narrow"), axis=0, tiled=True),
        lax.all_gather(w_out, ("wide", "narrow"), axis=0, tiled=True),
    )
    inputs = tokens.astype(jnp.float32).reshape(row_count, model_width)
    token_pos = positions.reshape(row_count)
    keep_rows = jnp.repeat(keep_mask.astype(jnp.float32), span_len)[:, None]
    inverse_one = lax.rsqrt(jnp.mean(inputs * inputs, axis=-1, keepdims=True) + epsilon)
    first_norm = (inputs * inverse_one * gain_one.astype(jnp.float32)).astype(jnp.bfloat16)
    query_pre = jnp.dot(first_norm, query_w, preferred_element_type=jnp.float32).reshape(
        row_count, head_count, head_dim
    )
    key_pre = jnp.dot(first_norm, key_w, preferred_element_type=jnp.float32).reshape(
        row_count, kv_heads, head_dim
    )
    query_rows = rotate(query_pre, token_pos, 1.0).astype(jnp.bfloat16)
    key_heads = (
        rotate(key_pre, token_pos, 1.0)
        .astype(jnp.bfloat16)
        .reshape(seq_count, span_len, kv_heads * head_dim)
    )
    value_heads = (
        jnp.dot(first_norm, value_w, preferred_element_type=jnp.float32)
        .astype(jnp.bfloat16)
        .reshape(seq_count, span_len, kv_heads * head_dim)
    )
    queries = (
        query_rows.reshape(seq_count, span_len, kv_heads, group_size, head_dim)
        .transpose(0, 2, 3, 1, 4)
        .reshape(seq_count, kv_heads, stripe, head_dim)
    )
    query_index = wide_place * span_len + jnp.arange(stripe, dtype=jnp.int32) % span_len
    last_query = wide_place * span_len + span_len - 1

    def block_scores(key_block, key_first):
        scores = (
            jnp.einsum("skrd,sjkd->skrj", queries, key_block, preferred_element_type=jnp.float32)
            * score_scale
        )
        key_index = key_first + jnp.arange(key_block.shape[1], dtype=jnp.int32)
        allowed = key_index[None, :] <= query_index[:, None]
        return (scores, allowed)

    start_forward = (
        jnp.full((seq_count, kv_heads, stripe), -1e30, jnp.float32),
        jnp.zeros((seq_count, kv_heads, stripe), jnp.float32),
        jnp.zeros((seq_count, kv_heads, stripe, head_dim), jnp.float32),
    )
    running = start_forward
    pieces = (
        lax.all_gather(key_heads, "wide", axis=1, tiled=True),
        lax.all_gather(value_heads, "wide", axis=1, tiled=True),
    )
    key_blocks = split_blocks(pieces[0], seq_count, kv_heads, head_dim)
    value_blocks = split_blocks(pieces[1], seq_count, kv_heads, head_dim)
    block_len = key_blocks.shape[2]

    def advance(carried, block_item):
        key_block, value_block, block_index = block_item
        key_first = block_index * block_len

        def compute_block(current):
            run_max, run_sum, run_acc = current
            scores, allowed = block_scores(key_block, key_first)
            scores = jnp.where(allowed, scores, -1e30)
            new_max = jnp.maximum(run_max, jnp.max(scores, axis=-1))
            factor = jnp.exp(run_max - new_max)
            weights = jnp.where(allowed, jnp.exp(scores - new_max[..., None]), 0.0)
            new_sum = run_sum * factor + jnp.sum(weights, axis=-1)
            new_acc = run_acc * factor[..., None] + jnp.einsum(
                "skrj,sjkd->skrd",
                weights.astype(jnp.bfloat16),
                value_block,
                preferred_element_type=jnp.float32,
            )
            return (new_max, new_sum, new_acc)

        return (lax.cond(key_first <= last_query, compute_block, unchanged, carried), None)

    running, _ = lax.scan(
        advance,
        running,
        (key_blocks, value_blocks, jnp.arange(key_blocks.shape[0], dtype=jnp.int32)),
    )
    run_max, run_sum, run_acc = running
    attended = run_acc / run_sum[..., None]
    log_total = run_max + jnp.log(run_sum)
    attended_rows = (
        attended.reshape(seq_count, kv_heads, group_size, span_len, head_dim)
        .transpose(0, 3, 1, 2, 4)
        .reshape(row_count, head_count * head_dim)
        .astype(jnp.bfloat16)
    )
    middle = inputs + keep_rows * jnp.dot(attended_rows, out_w, preferred_element_type=jnp.float32)
    gain_two, gate_w, up_w, down_w = (
        lax.all_gather(mlp_gain, ("wide", "narrow"), axis=0, tiled=True),
        lax.all_gather(w_gate, ("wide", "narrow"), axis=0, tiled=True),
        lax.all_gather(w_up, ("wide", "narrow"), axis=0, tiled=True),
        lax.all_gather(w_down, ("wide", "narrow"), axis=0, tiled=True),
    )
    inverse_two = lax.rsqrt(jnp.mean(middle * middle, axis=-1, keepdims=True) + epsilon)
    second_norm = (middle * inverse_two * gain_two.astype(jnp.float32)).astype(jnp.bfloat16)
    gate_value = jnp.dot(second_norm, gate_w, preferred_element_type=jnp.float32)
    up_value = jnp.dot(second_norm, up_w, preferred_element_type=jnp.float32)
    gate_sigmoid = jax.nn.sigmoid(gate_value)
    swish_value = gate_value * gate_sigmoid
    hidden = (swish_value * up_value).astype(jnp.bfloat16)
    output = (
        middle + keep_rows * jnp.dot(hidden, down_w, preferred_element_type=jnp.float32)
    ).astype(jnp.bfloat16)
    group_match = (
        group_ids.reshape(row_count)[:, None]
        == jnp.arange(exit_scale.shape[0], dtype=jnp.int32)[None, :]
    )
    token_scale = jnp.sum(jnp.where(group_match, exit_scale[None, :], 0.0), axis=1, keepdims=True)
    upstream = out_grad.astype(jnp.float32).reshape(row_count, model_width) * token_scale
    gain_two, gate_w, up_w, down_w = (
        lax.all_gather(mlp_gain, ("wide", "narrow"), axis=0, tiled=True),
        lax.all_gather(w_gate, ("wide", "narrow"), axis=0, tiled=True),
        lax.all_gather(w_up, ("wide", "narrow"), axis=0, tiled=True),
        lax.all_gather(w_down, ("wide", "narrow"), axis=0, tiled=True),
    )
    mixed_grad = (keep_rows * upstream).astype(jnp.bfloat16)
    grad_down = over_rows(hidden, mixed_grad)
    hidden_grad = against(mixed_grad, down_w)
    gate_grad = (
        hidden_grad * up_value * gate_sigmoid * (1.0 + gate_value * (1.0 - gate_sigmoid))
    ).astype(jnp.bfloat16)
    up_grad = (hidden_grad * swish_value).astype(jnp.bfloat16)
    grad_gate = over_rows(second_norm, gate_grad)
    grad_up = over_rows(second_norm, up_grad)
    norm_grad = against(gate_grad, gate_w) + against(up_grad, up_w)
    grad_gain_two = jnp.sum(norm_grad * middle * inverse_two, axis=0)
    scaled_two = gain_two.astype(jnp.float32) * norm_grad
    middle_grad = (
        upstream
        + inverse_two * scaled_two
        - middle
        * (inverse_two * inverse_two * inverse_two)
        * jnp.mean(scaled_two * middle, axis=-1, keepdims=True)
    )
    gain_two_share, gate_share, up_share, down_share = (
        lax.psum_scatter(grad_gain_two, ("wide", "narrow"), scatter_dimension=0, tiled=True),
        lax.psum_scatter(grad_gate, ("wide", "narrow"), scatter_dimension=0, tiled=True),
        lax.psum_scatter(grad_up, ("wide", "narrow"), scatter_dimension=0, tiled=True),
        lax.psum_scatter(grad_down, ("wide", "narrow"), scatter_dimension=0, tiled=True),
    )
    gain_one, query_w, key_w, value_w, out_w = (
        lax.all_gather(attn_gain, ("wide", "narrow"), axis=0, tiled=True),
        lax.all_gather(w_query, ("wide", "narrow"), axis=0, tiled=True),
        lax.all_gather(w_key, ("wide", "narrow"), axis=0, tiled=True),
        lax.all_gather(w_value, ("wide", "narrow"), axis=0, tiled=True),
        lax.all_gather(w_out, ("wide", "narrow"), axis=0, tiled=True),
    )
    branch_grad = (keep_rows * middle_grad).astype(jnp.bfloat16)
    grad_out = over_rows(attended_rows, branch_grad)
    attended_grad = against(branch_grad, out_w).astype(jnp.bfloat16)
    grouped_grad = (
        attended_grad.reshape(seq_count, span_len, kv_heads, group_size, head_dim)
        .transpose(0, 2, 3, 1, 4)
        .reshape(seq_count, kv_heads, stripe, head_dim)
    )
    row_delta = jnp.sum(grouped_grad.astype(jnp.float32) * attended, axis=-1)
    start_backward = (
        jnp.zeros((seq_count, kv_heads, stripe, head_dim), jnp.float32),
        jnp.zeros((seq_count, full_len, kv_heads * head_dim), jnp.float32),
        jnp.zeros((seq_count, full_len, kv_heads * head_dim), jnp.float32),
    )
    running = start_backward
    pieces = (
        lax.all_gather(key_heads, "wide", axis=1, tiled=True),
        lax.all_gather(value_heads, "wide", axis=1, tiled=True),
    )
    key_blocks = split_blocks(pieces[0], seq_count, kv_heads, head_dim)
    value_blocks = split_blocks(pieces[1], seq_count, kv_heads, head_dim)
    fold_block_len = key_blocks.shape[2]

    def advance(carried, block_item):
        key_block, value_block, block_index = block_item
        key_first = block_index * fold_block_len

        def compute_block(current):
            query_acc, key_acc, value_acc = current
            scores, allowed = block_scores(key_block, key_first)
            probabilities = jnp.where(allowed, jnp.exp(scores - log_total[..., None]), 0.0)
            value_part = jnp.einsum(
                "skrj,skrd->sjkd",
                probabilities.astype(jnp.bfloat16),
                grouped_grad,
                preferred_element_type=jnp.float32,
            )
            prob_grad = jnp.einsum(
                "skrd,sjkd->skrj", grouped_grad, value_block, preferred_element_type=jnp.float32
            )
            score_grad = (probabilities * (prob_grad - row_delta[..., None])).astype(jnp.bfloat16)
            query_acc = (
                query_acc
                + jnp.einsum(
                    "skrj,sjkd->skrd", score_grad, key_block, preferred_element_type=jnp.float32
                )
                * score_scale
            )
            key_part = (
                jnp.einsum(
                    "skrj,skrd->sjkd", score_grad, queries, preferred_element_type=jnp.float32
                )
                * score_scale
            )
            key_acc = add_rows(
                key_acc, key_part.reshape(seq_count, fold_block_len, kv_heads * head_dim), key_first
            )
            value_acc = add_rows(
                value_acc,
                value_part.reshape(seq_count, fold_block_len, kv_heads * head_dim),
                key_first,
            )
            return (query_acc, key_acc, value_acc)

        return (lax.cond(key_first <= last_query, compute_block, unchanged, carried), None)

    running, _ = lax.scan(
        advance,
        running,
        (key_blocks, value_blocks, jnp.arange(key_blocks.shape[0], dtype=jnp.int32)),
    )
    query_acc, key_acc, value_acc = running
    key_sum, value_sum = (
        lax.psum_scatter(
            key_acc.astype(jnp.bfloat16), "wide", scatter_dimension=1, tiled=True
        ).astype(jnp.float32),
        lax.psum_scatter(
            value_acc.astype(jnp.bfloat16), "wide", scatter_dimension=1, tiled=True
        ).astype(jnp.float32),
    )
    query_back = (
        query_acc.reshape(seq_count, kv_heads, group_size, span_len, head_dim)
        .transpose(0, 3, 1, 2, 4)
        .reshape(row_count, head_count, head_dim)
    )
    query_grad = (
        rotate(query_back, token_pos, -1.0)
        .reshape(row_count, head_count * head_dim)
        .astype(jnp.bfloat16)
    )
    key_grad = (
        rotate(key_sum.reshape(row_count, kv_heads, head_dim), token_pos, -1.0)
        .reshape(row_count, kv_heads * head_dim)
        .astype(jnp.bfloat16)
    )
    value_grad = value_sum.reshape(row_count, kv_heads * head_dim).astype(jnp.bfloat16)
    grad_query = over_rows(first_norm, query_grad)
    grad_key = over_rows(first_norm, key_grad)
    grad_value = over_rows(first_norm, value_grad)
    input_norm_grad = (
        against(query_grad, query_w) + against(key_grad, key_w) + against(value_grad, value_w)
    )
    grad_gain_one = jnp.sum(input_norm_grad * inputs * inverse_one, axis=0)
    scaled_one = gain_one.astype(jnp.float32) * input_norm_grad
    input_grad = (
        middle_grad
        + inverse_one * scaled_one
        - inputs
        * (inverse_one * inverse_one * inverse_one)
        * jnp.mean(scaled_one * inputs, axis=-1, keepdims=True)
    )
    gain_one_share, query_share, key_share, value_share, out_share = (
        lax.psum_scatter(grad_gain_one, ("wide", "narrow"), scatter_dimension=0, tiled=True),
        lax.psum_scatter(grad_query, ("wide", "narrow"), scatter_dimension=0, tiled=True),
        lax.psum_scatter(grad_key, ("wide", "narrow"), scatter_dimension=0, tiled=True),
        lax.psum_scatter(grad_value, ("wide", "narrow"), scatter_dimension=0, tiled=True),
        lax.psum_scatter(grad_out, ("wide", "narrow"), scatter_dimension=0, tiled=True),
    )
    return (
        output.reshape(seq_count, span_len, model_width),
        input_grad.astype(jnp.bfloat16).reshape(seq_count, span_len, model_width),
        gain_one_share,
        query_share,
        key_share,
        value_share,
        out_share,
        gain_two_share,
        gate_share,
        up_share,
        down_share,
    )


def line_body(
    tokens,
    attn_gain,
    w_query,
    w_key,
    w_value,
    w_out,
    mlp_gain,
    w_gate,
    w_up,
    w_down,
    keep_mask,
    group_ids,
    positions,
    exit_scale,
    out_grad,
):
    f32 = jnp.float32
    bf16 = jnp.bfloat16
    _, span_len, model_width = tokens.shape
    line = lax.axis_size("z")
    place = lax.axis_index("z")
    side = lax.axis_index("x")
    near = lax.axis_size("x") * lax.axis_size("y") * lax.axis_size("c")
    rows_each = w_query.shape[0]
    heads = HEADS // line
    q_cols = heads * HD
    ff_cols = w_gate.shape[1] // line
    group_len = span_len * line
    score_scale = 1.0 / math.sqrt(HD)

    def shift(values, axis, step):
        size = lax.axis_size(axis)
        return lax.ppermute(values, axis, [(i, (i + step) % size) for i in range(size)])

    def halves(values):
        cut = values.shape[0] // 2
        return [values[:cut], values[cut:]]

    def ring_pieces(values):
        parts = [[part] for part in halves(values)]
        for _ in range(line - 1):
            for index, part in enumerate(parts):
                part.append(shift(part[-1], "z", 1 - 2 * index))
        return [[parts[0][k], parts[1][(line - k) % line]] for k in range(line)]

    def ring_gather(values):
        return jnp.concatenate(sum(ring_pieces(values), []), axis=0)

    def ring_blocks(values):
        return [jnp.concatenate(pieces, axis=0) for pieces in ring_pieces(values)]

    def ring_sum(blocks):
        totals = []
        for index in range(2):
            step = 2 * index - 1
            total = None
            for hop in range(line):
                k = (line - 1 - hop) % line if index == 0 else (hop + 1) % line
                own = halves(blocks[k])[index]
                total = own if total is None else (shift(total, "z", step).astype(f32) + own.astype(f32))
                if hop < line - 1:
                    total = total.astype(bf16)
            totals.append(total)
        return jnp.concatenate(totals, axis=0)

    def pick(values, index, dim):
        return lax.dynamic_index_in_dim(values, index, dim, keepdims=False)

    def by_columns(weight, columns):
        return weight.reshape(rows_each, line, columns).transpose(1, 0, 2)

    def natural(blocks):
        return jnp.take(blocks, (place - jnp.arange(line, dtype=jnp.int32)) % line, axis=0)

    def turn(pack):
        got = [pick(pack, place, 0)]
        for k in range(1, line):
            got.append(shift(pick(pack, (place + k) % line, 0), "z", k))
        return jnp.stack(got)

    def near_gather(values, dim):
        return lax.all_gather(values, ("x", "y", "c"), axis=dim)

    pack_attn = jnp.concatenate(
        [by_columns(w_query, q_cols), by_columns(w_key, HD), by_columns(w_value, HD)], axis=2
    )
    pack_ff = jnp.concatenate([by_columns(w_gate, ff_cols), by_columns(w_up, ff_cols)], axis=2)
    qkv_w = near_gather(natural(turn(pack_attn)), 1).reshape(model_width, q_cols + 2 * HD)
    gains = lax.all_gather(jnp.stack([attn_gain, mlp_gain]), ("z", "x", "y", "c"), axis=1, tiled=True)
    gain_one = gains[0].astype(f32)
    gain_two = gains[1].astype(f32)
    inputs = ring_gather(tokens[0]).astype(f32)
    relative = (place - jnp.arange(line, dtype=jnp.int32)) % line
    inside = jnp.arange(span_len, dtype=jnp.int32)

    def token_index(which):
        return ((relative[:, None] * 2 + which) * span_len + inside[None, :]).reshape(group_len)

    token_pos = lax.all_gather(positions[0], "z", axis=0)
    token_pos = natural(token_pos).reshape(group_len)
    own_x = tokens[0].astype(f32)
    keep = keep_mask[0].astype(f32)
    group_match = group_ids[0][:, None] == jnp.arange(exit_scale.shape[0], dtype=jnp.int32)[None, :]
    token_scale = jnp.sum(jnp.where(group_match, exit_scale[None, :], 0.0), axis=1, keepdims=True)
    upstream = out_grad[0].astype(f32) * token_scale

    inverse_all = lax.rsqrt(jnp.mean(inputs * inputs, axis=-1, keepdims=True) + epsilon)
    first_norm = (inputs * inverse_all * gain_one).astype(bf16)
    qkv = jnp.dot(first_norm, qkv_w, preferred_element_type=f32)
    queries = rotate(qkv[:, :q_cols].reshape(group_len, heads, HD), token_pos, 1.0).astype(bf16)
    own_kv = jnp.concatenate(
        [
            rotate(qkv[:, q_cols : q_cols + HD].reshape(group_len, 1, HD), token_pos, 1.0)[:, 0],
            qkv[:, q_cols + HD :],
        ],
        axis=1,
    ).astype(bf16)
    out_w = lax.all_gather(w_out, ("x", "y", "c"), axis=0, tiled=True)
    out_w = ring_gather(out_w)
    both_kv = jnp.concatenate([own_kv, shift(own_kv, "x", 1)], axis=0)
    keys = both_kv[:, :HD]
    values = both_kv[:, HD:]
    query_index = token_index(side)
    key_index = jnp.concatenate([query_index, token_index(1 - side)])
    scores = jnp.einsum("tgd,jd->gtj", queries, keys, preferred_element_type=f32) * score_scale
    allowed = key_index[None, :] <= query_index[:, None]
    scores = jnp.where(allowed, scores, -1e30)
    weights = jnp.exp(scores - jnp.max(scores, axis=-1, keepdims=True))
    probabilities = weights / jnp.sum(weights, axis=-1, keepdims=True)
    rounded_probs = probabilities.astype(bf16)
    attended = jnp.einsum("gtj,jd->tgd", rounded_probs, values, preferred_element_type=f32)
    own_attended = attended.reshape(group_len, q_cols).astype(bf16)

    def turned(block, k):
        return jnp.roll(block.reshape(line, span_len, q_cols), k, axis=0).reshape(group_len, q_cols)

    gathered = ring_blocks(own_attended)
    attended_rows = jnp.concatenate([turned(block, k) for k, block in enumerate(gathered)], axis=1)
    branch = jnp.dot(attended_rows, out_w, preferred_element_type=f32)
    middle_all = inputs + keep * branch
    inverse_mid = lax.rsqrt(jnp.mean(middle_all * middle_all, axis=-1, keepdims=True) + epsilon)
    second_norm = (middle_all * inverse_mid * gain_two).astype(bf16)
    middle = middle_all[:span_len]
    inverse_two = inverse_mid[:span_len]

    ff_w = near_gather(natural(turn(pack_ff)), 1).reshape(model_width, 2 * ff_cols)
    down_w = lax.all_gather(w_down, ("x", "y", "c"), axis=0, tiled=True)
    mixed_grad = ring_gather((keep * upstream).astype(bf16))
    gate_up = jnp.dot(second_norm, ff_w, preferred_element_type=f32)
    gate_value = gate_up[:, :ff_cols]
    up_value = gate_up[:, ff_cols:]
    gate_sigmoid = jax.nn.sigmoid(gate_value)
    swish_value = gate_value * gate_sigmoid
    hidden = (swish_value * up_value).astype(bf16)
    hidden_grad = against(mixed_grad, down_w)
    gate_grad = hidden_grad * up_value * gate_sigmoid * (1.0 + gate_value * (1.0 - gate_sigmoid))
    up_grad = hidden_grad * swish_value
    both_grad = jnp.concatenate([gate_grad, up_grad], axis=1).astype(bf16)

    def split(values):
        return [values[k * span_len : (k + 1) * span_len] for k in range(line)]

    norm_grad = ring_sum(split(against(both_grad, ff_w).astype(bf16)))
    mixed = ring_sum(split(jnp.dot(hidden, down_w, preferred_element_type=f32).astype(bf16)))
    output = (middle + keep * mixed).astype(bf16)
    scaled_two = gain_two * norm_grad
    middle_grad = (
        upstream
        + inverse_two * scaled_two
        - middle
        * (inverse_two * inverse_two * inverse_two)
        * jnp.mean(scaled_two * middle, axis=-1, keepdims=True)
    )
    branch_grad = (keep * middle_grad).astype(bf16)
    own_grad = against(branch_grad, out_w).astype(bf16)
    grad_blocks = [own_grad[:, :q_cols]]
    for k in range(1, line):
        back = line - k
        grad_blocks.append(shift(own_grad[:, back * q_cols : (back + 1) * q_cols], "z", -back))
    attended_grad = jnp.concatenate(grad_blocks, axis=0).reshape(group_len, heads, HD)
    prob_grad = jnp.einsum("tgd,jd->gtj", attended_grad, values, preferred_element_type=f32)
    delta = jnp.sum(attended_grad.astype(f32) * attended, axis=-1).T[..., None]
    score_grad = (probabilities * (prob_grad - delta)).astype(bf16)
    query_back = jnp.einsum("gtj,jd->tgd", score_grad, keys, preferred_element_type=f32) * score_scale
    key_back = jnp.einsum("gtj,tgd->jd", score_grad, queries, preferred_element_type=f32) * score_scale
    value_back = jnp.einsum("gtj,tgd->jd", rounded_probs, attended_grad, preferred_element_type=f32)
    kv_back = jnp.concatenate([key_back, value_back], axis=1)
    kv_back = kv_back[:group_len] + shift(kv_back[group_len:].astype(bf16), "x", 1).astype(f32)
    qkv_grad = jnp.concatenate(
        [
            rotate(query_back, token_pos, -1.0).reshape(group_len, q_cols),
            rotate(kv_back[:, None, :HD], token_pos, -1.0)[:, 0],
            kv_back[:, HD:],
        ],
        axis=1,
    ).astype(bf16)
    input_norm_grad = ring_sum(split(against(qkv_grad, qkv_w).astype(bf16)))
    inverse_one = inverse_all[:span_len]
    scaled_one = gain_one * input_norm_grad
    input_grad = (
        middle_grad
        + inverse_one * scaled_one
        - own_x
        * (inverse_one * inverse_one * inverse_one)
        * jnp.mean(scaled_one * own_x, axis=-1, keepdims=True)
    )

    def pair_sum(values, axis, dim):
        mine = pick(values, lax.axis_index(axis), dim).astype(f32)
        other = pick(values, 1 - lax.axis_index(axis), dim)
        return (mine + shift(other, axis, 1).astype(f32)).astype(bf16)

    def near_sum(values):
        lead = values.ndim - 5
        values = pair_sum(values, "c", lead + 2)
        cut = values.shape[-1] // 256 * 128
        left = pair_sum(pair_sum(values[..., :cut], "x", lead), "y", lead)
        right = pair_sum(pair_sum(values[..., cut:], "y", lead + 1), "x", lead)
        return jnp.concatenate([left, right], axis=-1)

    def return_columns(grad):
        summed = near_sum(grad.astype(bf16).reshape(line, 2, 2, 2, rows_each, -1))
        return natural(turn(summed)).astype(f32)

    def side_by_side(blocks):
        return blocks.transpose(1, 0, 2).reshape(rows_each, -1)

    ff_back = return_columns(over_rows(second_norm, both_grad))
    grad_down = near_sum(
        over_rows(hidden, mixed_grad).astype(bf16).reshape(2, 2, 2, -1, model_width)
    ).astype(f32)
    grad_out = near_sum(
        over_rows(attended_rows[:span_len], branch_grad)
        .astype(bf16)
        .reshape(line, 2, 2, 2, rows_each, model_width)
    )
    grad_out = ring_sum([grad_out[k] for k in range(line)])
    qkv_back = return_columns(over_rows(first_norm, qkv_grad))
    grad_query = side_by_side(qkv_back[:, :, :q_cols])
    grad_key = side_by_side(qkv_back[:, :, q_cols : q_cols + HD])
    grad_value = side_by_side(qkv_back[:, :, q_cols + HD :])
    grad_gate = side_by_side(ff_back[:, :, :ff_cols])
    grad_up = side_by_side(ff_back[:, :, ff_cols:])

    def gain_grad(pairs, gain):
        total = sum(jnp.sum(weight.astype(f32) * grad, axis=1) for weight, grad in pairs)
        return total / gain.astype(f32)

    return (
        output[None],
        input_grad.astype(bf16)[None],
        gain_grad([(w_query, grad_query), (w_key, grad_key), (w_value, grad_value)], attn_gain),
        grad_query,
        grad_key,
        grad_value,
        grad_out,
        gain_grad([(w_gate, grad_gate), (w_up, grad_up)], mlp_gain),
        grad_gate,
        grad_up,
        grad_down,
    )


def solution(mesh):
    wide, narrow = mesh.shape["wide"], mesh.shape["narrow"]
    if wide == 2 * KVH and narrow == 4:
        mesh = Mesh(mesh.devices.reshape(wide // 2, 2, 2, 2), ("z", "x", "y", "c"))
        body, wide, narrow = line_body, ("z", "x"), ("y", "c")
    else:
        body, wide, narrow = general_body, ("wide",), ("narrow",)
    token_spec = P(narrow, wide, None)
    id_spec = P(narrow, wide)
    gain_spec = P(wide + narrow)
    weight_spec = P(wide + narrow, None)
    return jax.shard_map(
        body,
        mesh=mesh,
        in_specs=(
            token_spec,
            gain_spec,
            weight_spec,
            weight_spec,
            weight_spec,
            weight_spec,
            gain_spec,
            weight_spec,
            weight_spec,
            weight_spec,
            P(narrow),
            id_spec,
            id_spec,
            P(),
            token_spec,
        ),
        out_specs=(
            token_spec,
            token_spec,
            gain_spec,
            weight_spec,
            weight_spec,
            weight_spec,
            weight_spec,
            gain_spec,
            weight_spec,
            weight_spec,
            weight_spec,
        ),
        check_vma=False,
    )
```

```python
import functools
import math

import jax
import jax.numpy as jnp
from jax import lax
from jax.experimental import pallas as pl
from jax.experimental.pallas import tpu as pltpu
from jax.sharding import Mesh
from jax.sharding import PartitionSpec as P

HEADS = 16
KVH = 4
HD = 128


epsilon = 1e-05


def rotate(vectors, token_pos, direction):
    half_size = vectors.shape[-1] // 2
    freqs = 10000.0 ** (-2.0 * jnp.arange(half_size, dtype=jnp.float32) / vectors.shape[-1])
    angles = token_pos.astype(jnp.float32)[:, None] * freqs[None, :]
    cosine = jnp.cos(angles)[:, None, :]
    sine = direction * jnp.sin(angles)[:, None, :]
    first_half = vectors[..., :half_size]
    second_half = vectors[..., half_size:]
    return jnp.concatenate(
        [first_half * cosine - second_half * sine, second_half * cosine + first_half * sine],
        axis=-1,
    )


def split_blocks(piece_arr, seq_count, kv_heads, head_dim):
    piece_len = piece_arr.shape[1]
    block_len = math.gcd(piece_len, 512)
    shaped = piece_arr.reshape(seq_count, piece_len // block_len, block_len, kv_heads, head_dim)
    return shaped.transpose(1, 0, 2, 3, 4)


def add_rows(whole_arr, update, first_row):
    current = lax.dynamic_slice_in_dim(whole_arr, first_row, update.shape[1], 1)
    return lax.dynamic_update_slice_in_dim(whole_arr, current + update, first_row, 1)


def over_rows(left, right):
    return lax.dot_general(
        left, right, (((0,), (0,)), ((), ())), preferred_element_type=jnp.float32
    )


def against(left, right):
    return lax.dot_general(
        left, right, (((1,), (1,)), ((), ())), preferred_element_type=jnp.float32
    )


def unchanged(carried):
    return carried


MESH = pl.DeviceIdType.MESH
AXES = ("z", "x", "y", "c")


class Links:
    def __init__(self, send_sems, recv_sems, line):
        self.send_sems, self.recv_sems, self.line = send_sems, recv_sems, line
        self.z, self.x, self.y, self.c = (lax.axis_index(name) for name in AXES)
        self.slot = self.x * 4 + self.y * 2 + self.c
        self.used = 0
        self.sent = []

    def device(self, to):
        if to == "x":
            return (self.z, 1 - self.x, self.y, self.c)
        if to == "y":
            return (self.z, self.x, 1 - self.y, self.c)
        if to == "c":
            return (self.z, self.x, self.y, 1 - self.c)
        return (self.along(to), self.x, self.y, self.c)

    def along(self, step):
        return lax.rem(self.z + step + self.line, self.line)

    def other(self, to):
        slot = self.slot
        for name in to:
            bit = {"x": 4, "y": 2, "c": 1}[name]
            here = {"x": self.x, "y": self.y, "c": self.c}[name]
            slot = slot + bit * (1 - 2 * here)
        return slot

    def meet(self, targets):
        barrier = pltpu.get_barrier_semaphore()
        for to in targets:
            pl.semaphore_signal(barrier, inc=1, device_id=self.device(to), device_id_type=MESH)
        pl.semaphore_wait(barrier, len(targets))

    def send(self, source, target, to):
        copy = pltpu.make_async_remote_copy(
            src_ref=source,
            dst_ref=target,
            send_sem=self.send_sems.at[self.used],
            recv_sem=self.recv_sems.at[self.used],
            device_id=self.device(to),
            device_id_type=MESH,
        )
        copy.start()
        self.used += 1
        self.sent.append(copy)
        return copy

    def keep(self, source, target):
        copy = pltpu.make_async_copy(source, target, self.send_sems.at[self.used])
        copy.start()
        self.used += 1
        return copy

    def finish(self):
        for copy in self.sent:
            copy.wait_send()


class NearGather:
    def __init__(self, links, slot):
        self.links, self.slot = links, slot
        self.got = {}

    def offer(self, block, source):
        target = self.slot(block, self.links.slot)
        for to in ("x", "y", "c"):
            self.got[block, to] = self.links.send(source, target, to)

    def relay(self, block, first):
        links = self.links
        for to, then in (("x", "y"), ("y", "x")):
            self.got[block, to].wait_recv()
            place = self.slot(block, links.other(to))
            self.got[block, to + "c"] = links.send(place, place, "c")
            if to == first:
                self.got[block, "xy"] = links.send(place, place, then)

    def close(self, block):
        self.got[block, "xy"].wait_recv()
        place = self.slot(block, self.links.other("xy"))
        self.got[block, "xyc"] = self.links.send(place, place, "c")

    def wait(self, blocks):
        for block in blocks:
            for to in ("c", "xc", "yc", "xyc"):
                self.got[block, to].wait_recv()


class RingGather:
    def __init__(self, links, source, place, pieces=4):
        self.links, self.source, self.place, self.pieces = links, source, place, pieces
        self.rows = source.shape[0] // pieces
        self.last = [None] * pieces

    def step(self, number):
        for piece in range(self.pieces):
            way = 1 if piece < self.pieces // 2 else -1
            rows = pl.ds(piece * self.rows, self.rows)
            place = self.place(self.links.along(-way * number), rows)
            if number > 0:
                self.last[piece].wait_recv()
            if number < self.links.line - 1:
                origin = self.source.at[rows] if number == 0 else place
                self.last[piece] = self.links.send(origin, place, way)


def first_kernel(line, x_ref, pos_ref, pack_ref, xs_ref, poss_ref, qkv_ref, send_sems, recv_sems):
    links = Links(send_sems, recv_sems, line)
    far = [1, line - 1] + list(range(2, line - 1))
    links.meet(["x", "y", "c"] + far)
    qkv = NearGather(links, lambda block, place: qkv_ref.at[links.along(-block), place])
    ring = RingGather(links, x_ref, lambda block, rows: xs_ref.at[block, rows])
    here = links.slot
    local = [
        links.keep(x_ref, xs_ref.at[links.z]),
        links.keep(pos_ref, poss_ref.at[links.z]),
        links.keep(pack_ref.at[links.z], qkv_ref.at[links.z, here]),
    ]
    turned = {k: links.send(pack_ref.at[links.along(k)], qkv_ref.at[links.z, here], k) for k in far}
    placed = [links.send(pos_ref, poss_ref.at[links.z], k) for k in far]
    ring.step(0)
    qkv.offer(0, pack_ref.at[links.z])
    for k in far:
        turned[k].wait_recv()
        qkv.offer(k, qkv_ref.at[links.along(-k), here])
    ring.step(1)
    for k in [0] + far:
        qkv.relay(k, "x" if k < line // 2 else "y")
    ring.step(2)
    for k in [0] + far:
        qkv.close(k)
    ring.step(3)
    qkv.wait(range(line))
    for copy in placed:
        copy.wait_recv()
    links.finish()
    for copy in local:
        copy.wait()


def ring_kernel(line, x_ref, xs_ref, send_sems, recv_sems):
    links = Links(send_sems, recv_sems, line)
    columns = x_ref.shape[1]
    links.meet([1, line - 1])

    def place(block, rows):
        return xs_ref.at[rows, pl.ds(pl.multiple_of(block * columns, columns), columns)]

    ring = RingGather(links, x_ref, place)
    local = links.keep(x_ref, place(links.z, pl.ds(0, x_ref.shape[0])))
    for number in range(line):
        ring.step(number)
    links.finish()
    local.wait()


def sum_kernel(line, pieces, parts_ref, total_ref, got, made, send_sems, recv_sems):
    links = Links(send_sems, recv_sems, line)
    links.meet([1, line - 1])
    rows = parts_ref.shape[1] // pieces
    last = [None] * pieces
    for number in range(line):
        for piece in range(pieces):
            way = 1 if piece < pieces // 2 else -1
            block = links.along(-way * (number + 1))
            where = pl.ds(piece * rows, rows)
            if number == 0:
                source = parts_ref.at[block, where]
            else:
                last[piece].wait_recv()
                total = got[number - 1, where].astype(jnp.float32) + parts_ref[
                    block, where
                ].astype(jnp.float32)
                if number == line - 1:
                    total_ref[where] = total
                    continue
                made[number - 1, where] = total.astype(made.dtype)
                source = made.at[number - 1, where]
            last[piece] = links.send(source, got.at[number, where], way)
    links.finish()


def turn_kernel(line, rows_ref, columns_ref, send_sems, recv_sems):
    links = Links(send_sems, recv_sems, line)
    far = [1, line - 1] + list(range(2, line - 1))
    links.meet(far)
    columns = columns_ref.shape[2]

    def part(block):
        return rows_ref.at[:, pl.ds(pl.multiple_of(block * columns, columns), columns)]

    local = links.keep(part(links.z), columns_ref.at[links.z])
    for k in far:
        links.send(part(links.along(k)), columns_ref.at[links.z], k)
    for copy in links.sent:
        copy.wait_recv()
    links.finish()
    local.wait()


def link_call(kernel, collective_id, copies, shapes, arguments, spaces=None, scratch=()):
    any_space = pl.BlockSpec(memory_space=pl.ANY)
    vmem = pl.BlockSpec(memory_space=pltpu.VMEM)
    spec = vmem if spaces == "vmem" else any_space
    many = isinstance(shapes, tuple)
    return pl.pallas_call(
        kernel,
        out_shape=shapes,
        in_specs=[spec] * len(arguments),
        out_specs=(spec,) * len(shapes) if many else spec,
        scratch_shapes=list(scratch)
        + [pltpu.SemaphoreType.DMA((copies,)), pltpu.SemaphoreType.DMA((copies,))],
        compiler_params=pltpu.CompilerParams(
            collective_id=collective_id, has_side_effects=True, vmem_limit_bytes=32 * 2**20
        ),
    )(*arguments)


def first_gather(tokens, positions, pack, line):
    return link_call(
        functools.partial(first_kernel, line),
        0,
        64,
        (
            jax.ShapeDtypeStruct((line,) + tokens.shape, tokens.dtype),
            jax.ShapeDtypeStruct((line,) + positions.shape, positions.dtype),
            jax.ShapeDtypeStruct((line, 8) + pack.shape[1:], pack.dtype),
        ),
        (tokens, positions, pack),
    )


def gather_columns(values, line):
    return link_call(
        functools.partial(ring_kernel, line),
        1,
        4 * line,
        jax.ShapeDtypeStruct((values.shape[0], line * values.shape[1]), values.dtype),
        (values,),
    )


def sum_blocks(parts, line):
    shape = parts.shape[1:]
    return link_call(
        functools.partial(sum_kernel, line, 4),
        2,
        4 * line,
        jax.ShapeDtypeStruct(shape, jnp.float32),
        (parts,),
        "vmem",
        [
            pltpu.VMEM((line - 1,) + shape, parts.dtype),
            pltpu.VMEM((line - 2,) + shape, parts.dtype),
        ],
    )


def turn_rows(values, line):
    return link_call(
        functools.partial(turn_kernel, line),
        3,
        line,
        jax.ShapeDtypeStruct((line, values.shape[0], values.shape[1] // line), values.dtype),
        (values,),
    )


def general_body(
    tokens,
    attn_gain,
    w_query,
    w_key,
    w_value,
    w_out,
    mlp_gain,
    w_gate,
    w_up,
    w_down,
    keep_mask,
    group_ids,
    positions,
    exit_scale,
    out_grad,
):
    seq_count, span_len, model_width = tokens.shape
    kv_heads = KVH
    head_dim = HD
    head_count = HEADS
    group_size = head_count // kv_heads
    row_count = seq_count * span_len
    stripe = group_size * span_len
    wide_count = lax.axis_size("wide")
    wide_place = lax.axis_index("wide")
    full_len = span_len * wide_count
    score_scale = 1.0 / math.sqrt(head_dim)
    gain_one, query_w, key_w, value_w, out_w = (
        lax.all_gather(attn_gain, ("wide", "narrow"), axis=0, tiled=True),
        lax.all_gather(w_query, ("wide", "narrow"), axis=0, tiled=True),
        lax.all_gather(w_key, ("wide", "narrow"), axis=0, tiled=True),
        lax.all_gather(w_value, ("wide", "narrow"), axis=0, tiled=True),
        lax.all_gather(w_out, ("wide", "narrow"), axis=0, tiled=True),
    )
    inputs = tokens.astype(jnp.float32).reshape(row_count, model_width)
    token_pos = positions.reshape(row_count)
    keep_rows = jnp.repeat(keep_mask.astype(jnp.float32), span_len)[:, None]
    inverse_one = lax.rsqrt(jnp.mean(inputs * inputs, axis=-1, keepdims=True) + epsilon)
    first_norm = (inputs * inverse_one * gain_one.astype(jnp.float32)).astype(jnp.bfloat16)
    query_pre = jnp.dot(first_norm, query_w, preferred_element_type=jnp.float32).reshape(
        row_count, head_count, head_dim
    )
    key_pre = jnp.dot(first_norm, key_w, preferred_element_type=jnp.float32).reshape(
        row_count, kv_heads, head_dim
    )
    query_rows = rotate(query_pre, token_pos, 1.0).astype(jnp.bfloat16)
    key_heads = (
        rotate(key_pre, token_pos, 1.0)
        .astype(jnp.bfloat16)
        .reshape(seq_count, span_len, kv_heads * head_dim)
    )
    value_heads = (
        jnp.dot(first_norm, value_w, preferred_element_type=jnp.float32)
        .astype(jnp.bfloat16)
        .reshape(seq_count, span_len, kv_heads * head_dim)
    )
    queries = (
        query_rows.reshape(seq_count, span_len, kv_heads, group_size, head_dim)
        .transpose(0, 2, 3, 1, 4)
        .reshape(seq_count, kv_heads, stripe, head_dim)
    )
    query_index = wide_place * span_len + jnp.arange(stripe, dtype=jnp.int32) % span_len
    last_query = wide_place * span_len + span_len - 1

    def block_scores(key_block, key_first):
        scores = (
            jnp.einsum("skrd,sjkd->skrj", queries, key_block, preferred_element_type=jnp.float32)
            * score_scale
        )
        key_index = key_first + jnp.arange(key_block.shape[1], dtype=jnp.int32)
        allowed = key_index[None, :] <= query_index[:, None]
        return (scores, allowed)

    start_forward = (
        jnp.full((seq_count, kv_heads, stripe), -1e30, jnp.float32),
        jnp.zeros((seq_count, kv_heads, stripe), jnp.float32),
        jnp.zeros((seq_count, kv_heads, stripe, head_dim), jnp.float32),
    )
    running = start_forward
    pieces = (
        lax.all_gather(key_heads, "wide", axis=1, tiled=True),
        lax.all_gather(value_heads, "wide", axis=1, tiled=True),
    )
    key_blocks = split_blocks(pieces[0], seq_count, kv_heads, head_dim)
    value_blocks = split_blocks(pieces[1], seq_count, kv_heads, head_dim)
    block_len = key_blocks.shape[2]

    def advance(carried, block_item):
        key_block, value_block, block_index = block_item
        key_first = block_index * block_len

        def compute_block(current):
            run_max, run_sum, run_acc = current
            scores, allowed = block_scores(key_block, key_first)
            scores = jnp.where(allowed, scores, -1e30)
            new_max = jnp.maximum(run_max, jnp.max(scores, axis=-1))
            factor = jnp.exp(run_max - new_max)
            weights = jnp.where(allowed, jnp.exp(scores - new_max[..., None]), 0.0)
            new_sum = run_sum * factor + jnp.sum(weights, axis=-1)
            new_acc = run_acc * factor[..., None] + jnp.einsum(
                "skrj,sjkd->skrd",
                weights.astype(jnp.bfloat16),
                value_block,
                preferred_element_type=jnp.float32,
            )
            return (new_max, new_sum, new_acc)

        return (lax.cond(key_first <= last_query, compute_block, unchanged, carried), None)

    running, _ = lax.scan(
        advance,
        running,
        (key_blocks, value_blocks, jnp.arange(key_blocks.shape[0], dtype=jnp.int32)),
    )
    run_max, run_sum, run_acc = running
    attended = run_acc / run_sum[..., None]
    log_total = run_max + jnp.log(run_sum)
    attended_rows = (
        attended.reshape(seq_count, kv_heads, group_size, span_len, head_dim)
        .transpose(0, 3, 1, 2, 4)
        .reshape(row_count, head_count * head_dim)
        .astype(jnp.bfloat16)
    )
    middle = inputs + keep_rows * jnp.dot(attended_rows, out_w, preferred_element_type=jnp.float32)
    gain_two, gate_w, up_w, down_w = (
        lax.all_gather(mlp_gain, ("wide", "narrow"), axis=0, tiled=True),
        lax.all_gather(w_gate, ("wide", "narrow"), axis=0, tiled=True),
        lax.all_gather(w_up, ("wide", "narrow"), axis=0, tiled=True),
        lax.all_gather(w_down, ("wide", "narrow"), axis=0, tiled=True),
    )
    inverse_two = lax.rsqrt(jnp.mean(middle * middle, axis=-1, keepdims=True) + epsilon)
    second_norm = (middle * inverse_two * gain_two.astype(jnp.float32)).astype(jnp.bfloat16)
    gate_value = jnp.dot(second_norm, gate_w, preferred_element_type=jnp.float32)
    up_value = jnp.dot(second_norm, up_w, preferred_element_type=jnp.float32)
    gate_sigmoid = jax.nn.sigmoid(gate_value)
    swish_value = gate_value * gate_sigmoid
    hidden = (swish_value * up_value).astype(jnp.bfloat16)
    output = (
        middle + keep_rows * jnp.dot(hidden, down_w, preferred_element_type=jnp.float32)
    ).astype(jnp.bfloat16)
    group_match = (
        group_ids.reshape(row_count)[:, None]
        == jnp.arange(exit_scale.shape[0], dtype=jnp.int32)[None, :]
    )
    token_scale = jnp.sum(jnp.where(group_match, exit_scale[None, :], 0.0), axis=1, keepdims=True)
    upstream = out_grad.astype(jnp.float32).reshape(row_count, model_width) * token_scale
    gain_two, gate_w, up_w, down_w = (
        lax.all_gather(mlp_gain, ("wide", "narrow"), axis=0, tiled=True),
        lax.all_gather(w_gate, ("wide", "narrow"), axis=0, tiled=True),
        lax.all_gather(w_up, ("wide", "narrow"), axis=0, tiled=True),
        lax.all_gather(w_down, ("wide", "narrow"), axis=0, tiled=True),
    )
    mixed_grad = (keep_rows * upstream).astype(jnp.bfloat16)
    grad_down = over_rows(hidden, mixed_grad)
    hidden_grad = against(mixed_grad, down_w)
    gate_grad = (
        hidden_grad * up_value * gate_sigmoid * (1.0 + gate_value * (1.0 - gate_sigmoid))
    ).astype(jnp.bfloat16)
    up_grad = (hidden_grad * swish_value).astype(jnp.bfloat16)
    grad_gate = over_rows(second_norm, gate_grad)
    grad_up = over_rows(second_norm, up_grad)
    norm_grad = against(gate_grad, gate_w) + against(up_grad, up_w)
    grad_gain_two = jnp.sum(norm_grad * middle * inverse_two, axis=0)
    scaled_two = gain_two.astype(jnp.float32) * norm_grad
    middle_grad = (
        upstream
        + inverse_two * scaled_two
        - middle
        * (inverse_two * inverse_two * inverse_two)
        * jnp.mean(scaled_two * middle, axis=-1, keepdims=True)
    )
    gain_two_share, gate_share, up_share, down_share = (
        lax.psum_scatter(grad_gain_two, ("wide", "narrow"), scatter_dimension=0, tiled=True),
        lax.psum_scatter(grad_gate, ("wide", "narrow"), scatter_dimension=0, tiled=True),
        lax.psum_scatter(grad_up, ("wide", "narrow"), scatter_dimension=0, tiled=True),
        lax.psum_scatter(grad_down, ("wide", "narrow"), scatter_dimension=0, tiled=True),
    )
    gain_one, query_w, key_w, value_w, out_w = (
        lax.all_gather(attn_gain, ("wide", "narrow"), axis=0, tiled=True),
        lax.all_gather(w_query, ("wide", "narrow"), axis=0, tiled=True),
        lax.all_gather(w_key, ("wide", "narrow"), axis=0, tiled=True),
        lax.all_gather(w_value, ("wide", "narrow"), axis=0, tiled=True),
        lax.all_gather(w_out, ("wide", "narrow"), axis=0, tiled=True),
    )
    branch_grad = (keep_rows * middle_grad).astype(jnp.bfloat16)
    grad_out = over_rows(attended_rows, branch_grad)
    attended_grad = against(branch_grad, out_w).astype(jnp.bfloat16)
    grouped_grad = (
        attended_grad.reshape(seq_count, span_len, kv_heads, group_size, head_dim)
        .transpose(0, 2, 3, 1, 4)
        .reshape(seq_count, kv_heads, stripe, head_dim)
    )
    row_delta = jnp.sum(grouped_grad.astype(jnp.float32) * attended, axis=-1)
    start_backward = (
        jnp.zeros((seq_count, kv_heads, stripe, head_dim), jnp.float32),
        jnp.zeros((seq_count, full_len, kv_heads * head_dim), jnp.float32),
        jnp.zeros((seq_count, full_len, kv_heads * head_dim), jnp.float32),
    )
    running = start_backward
    pieces = (
        lax.all_gather(key_heads, "wide", axis=1, tiled=True),
        lax.all_gather(value_heads, "wide", axis=1, tiled=True),
    )
    key_blocks = split_blocks(pieces[0], seq_count, kv_heads, head_dim)
    value_blocks = split_blocks(pieces[1], seq_count, kv_heads, head_dim)
    fold_block_len = key_blocks.shape[2]

    def advance(carried, block_item):
        key_block, value_block, block_index = block_item
        key_first = block_index * fold_block_len

        def compute_block(current):
            query_acc, key_acc, value_acc = current
            scores, allowed = block_scores(key_block, key_first)
            probabilities = jnp.where(allowed, jnp.exp(scores - log_total[..., None]), 0.0)
            value_part = jnp.einsum(
                "skrj,skrd->sjkd",
                probabilities.astype(jnp.bfloat16),
                grouped_grad,
                preferred_element_type=jnp.float32,
            )
            prob_grad = jnp.einsum(
                "skrd,sjkd->skrj", grouped_grad, value_block, preferred_element_type=jnp.float32
            )
            score_grad = (probabilities * (prob_grad - row_delta[..., None])).astype(jnp.bfloat16)
            query_acc = (
                query_acc
                + jnp.einsum(
                    "skrj,sjkd->skrd", score_grad, key_block, preferred_element_type=jnp.float32
                )
                * score_scale
            )
            key_part = (
                jnp.einsum(
                    "skrj,skrd->sjkd", score_grad, queries, preferred_element_type=jnp.float32
                )
                * score_scale
            )
            key_acc = add_rows(
                key_acc, key_part.reshape(seq_count, fold_block_len, kv_heads * head_dim), key_first
            )
            value_acc = add_rows(
                value_acc,
                value_part.reshape(seq_count, fold_block_len, kv_heads * head_dim),
                key_first,
            )
            return (query_acc, key_acc, value_acc)

        return (lax.cond(key_first <= last_query, compute_block, unchanged, carried), None)

    running, _ = lax.scan(
        advance,
        running,
        (key_blocks, value_blocks, jnp.arange(key_blocks.shape[0], dtype=jnp.int32)),
    )
    query_acc, key_acc, value_acc = running
    key_sum, value_sum = (
        lax.psum_scatter(
            key_acc.astype(jnp.bfloat16), "wide", scatter_dimension=1, tiled=True
        ).astype(jnp.float32),
        lax.psum_scatter(
            value_acc.astype(jnp.bfloat16), "wide", scatter_dimension=1, tiled=True
        ).astype(jnp.float32),
    )
    query_back = (
        query_acc.reshape(seq_count, kv_heads, group_size, span_len, head_dim)
        .transpose(0, 3, 1, 2, 4)
        .reshape(row_count, head_count, head_dim)
    )
    query_grad = (
        rotate(query_back, token_pos, -1.0)
        .reshape(row_count, head_count * head_dim)
        .astype(jnp.bfloat16)
    )
    key_grad = (
        rotate(key_sum.reshape(row_count, kv_heads, head_dim), token_pos, -1.0)
        .reshape(row_count, kv_heads * head_dim)
        .astype(jnp.bfloat16)
    )
    value_grad = value_sum.reshape(row_count, kv_heads * head_dim).astype(jnp.bfloat16)
    grad_query = over_rows(first_norm, query_grad)
    grad_key = over_rows(first_norm, key_grad)
    grad_value = over_rows(first_norm, value_grad)
    input_norm_grad = (
        against(query_grad, query_w) + against(key_grad, key_w) + against(value_grad, value_w)
    )
    grad_gain_one = jnp.sum(input_norm_grad * inputs * inverse_one, axis=0)
    scaled_one = gain_one.astype(jnp.float32) * input_norm_grad
    input_grad = (
        middle_grad
        + inverse_one * scaled_one
        - inputs
        * (inverse_one * inverse_one * inverse_one)
        * jnp.mean(scaled_one * inputs, axis=-1, keepdims=True)
    )
    gain_one_share, query_share, key_share, value_share, out_share = (
        lax.psum_scatter(grad_gain_one, ("wide", "narrow"), scatter_dimension=0, tiled=True),
        lax.psum_scatter(grad_query, ("wide", "narrow"), scatter_dimension=0, tiled=True),
        lax.psum_scatter(grad_key, ("wide", "narrow"), scatter_dimension=0, tiled=True),
        lax.psum_scatter(grad_value, ("wide", "narrow"), scatter_dimension=0, tiled=True),
        lax.psum_scatter(grad_out, ("wide", "narrow"), scatter_dimension=0, tiled=True),
    )
    return (
        output.reshape(seq_count, span_len, model_width),
        input_grad.astype(jnp.bfloat16).reshape(seq_count, span_len, model_width),
        gain_one_share,
        query_share,
        key_share,
        value_share,
        out_share,
        gain_two_share,
        gate_share,
        up_share,
        down_share,
    )


def line_body(
    tokens,
    attn_gain,
    w_query,
    w_key,
    w_value,
    w_out,
    mlp_gain,
    w_gate,
    w_up,
    w_down,
    keep_mask,
    group_ids,
    positions,
    exit_scale,
    out_grad,
):
    f32 = jnp.float32
    bf16 = jnp.bfloat16
    _, span_len, model_width = tokens.shape
    line = lax.axis_size("z")
    place = lax.axis_index("z")
    side = lax.axis_index("x")
    near = lax.axis_size("x") * lax.axis_size("y") * lax.axis_size("c")
    rows_each = w_query.shape[0]
    heads = HEADS // line
    q_cols = heads * HD
    ff_cols = w_gate.shape[1] // line
    group_len = span_len * line
    score_scale = 1.0 / math.sqrt(HD)

    def shift(values, axis, step):
        size = lax.axis_size(axis)
        return lax.ppermute(values, axis, [(i, (i + step) % size) for i in range(size)])

    def after(values, first):
        return lax.optimization_barrier((values, first))[0]

    def pick(values, index, dim):
        return lax.dynamic_index_in_dim(values, index, dim, keepdims=False)

    def back_order(blocks):
        return jnp.take(blocks, (place - jnp.arange(line, dtype=jnp.int32)) % line, axis=0)

    def ring_gather(values):
        cut = values.shape[0] // 2
        up, down = [values[:cut]], [values[cut:]]
        for _ in range(line - 1):
            up.append(shift(up[-1], "z", 1))
            down.append(shift(down[-1], "z", -1))
        pairs = [jnp.concatenate([up[k], down[(line - k) % line]], axis=0) for k in range(line)]
        return back_order(jnp.stack(pairs))

    def ring_sum(blocks):
        cut = blocks.shape[1] // 2
        totals = []
        for step in (1, -1):
            total = None
            for hop in range(line):
                own = pick(blocks, (place - step * (hop + 1)) % line, 0)
                own = own[:cut] if step == 1 else own[cut:]
                total = own if total is None else shift(total, "z", step).astype(f32) + own.astype(f32)
                if hop < line - 1:
                    total = total.astype(bf16)
            totals.append(total)
        return jnp.concatenate(totals, axis=0)

    def by_columns(weight, columns):
        return weight.reshape(rows_each, line, columns).transpose(1, 0, 2)

    def turn(pack):
        got = [pick(pack, place, 0)]
        for k in range(1, line):
            got.append(shift(pick(pack, (place + k) % line, 0), "z", k))
        return back_order(jnp.stack(got))

    gains = jnp.stack([attn_gain, mlp_gain] + [jnp.zeros_like(attn_gain)] * (HD - 2), axis=1)
    pack_attn = jnp.concatenate(
        [
            by_columns(w_query, q_cols),
            by_columns(w_key, HD),
            by_columns(w_value, HD),
            jnp.broadcast_to(gains[None], (line,) + gains.shape),
        ],
        axis=2,
    )
    place_rows = jnp.broadcast_to(positions[0].astype(f32)[None, :], (8, span_len))
    x_blocks, place_blocks, near_w = first_gather(tokens[0], place_rows, pack_attn, line)
    inputs = x_blocks.reshape(group_len, model_width).astype(f32)
    token_pos = place_blocks[:, 0].reshape(group_len)
    near_w = near_w.reshape(model_width, -1)
    qkv_w = near_w[:, : q_cols + 2 * HD]
    gain_rows = near_w[:, q_cols + 2 * HD : q_cols + 2 * HD + 2].astype(f32).T
    gain_one, gain_two = gain_rows[:1], gain_rows[1:]

    out_w = lax.all_gather(w_out, ("z", "x", "y", "c"), axis=0, tiled=True)
    down_w = lax.all_gather(w_down, ("x", "y", "c"), axis=0, tiled=True)
    pack_ff = jnp.concatenate([by_columns(w_gate, ff_cols), by_columns(w_up, ff_cols)], axis=2)
    turned_ff = turn(after(pack_ff, x_blocks))
    ff_w = lax.all_gather(turned_ff, ("x", "y", "c"), axis=1).reshape(model_width, 2 * ff_cols)

    own_x = tokens[0].astype(f32)
    keep = keep_mask[0].astype(f32)
    group_match = group_ids[0][:, None] == jnp.arange(exit_scale.shape[0], dtype=jnp.int32)[None, :]
    token_scale = jnp.sum(jnp.where(group_match, exit_scale[None, :], 0.0), axis=1, keepdims=True)
    upstream = out_grad[0].astype(f32) * token_scale
    mixed_grad = ring_gather((keep * upstream).astype(bf16)).reshape(group_len, model_width)

    inside = jnp.arange(span_len, dtype=jnp.int32)
    block_first = jnp.arange(line, dtype=jnp.int32) * (2 * span_len)

    def token_index(which):
        return (block_first[:, None] + which * span_len + inside[None, :]).reshape(group_len)

    inverse_all = lax.rsqrt(jnp.mean(inputs * inputs, axis=-1, keepdims=True) + epsilon)
    first_norm = (inputs * inverse_all * gain_one).astype(bf16)
    qkv = jnp.dot(first_norm, qkv_w, preferred_element_type=f32)
    queries = rotate(qkv[:, :q_cols].reshape(group_len, heads, HD), token_pos, 1.0).astype(bf16)
    own_kv = jnp.concatenate(
        [
            rotate(qkv[:, q_cols : q_cols + HD].reshape(group_len, 1, HD), token_pos, 1.0)[:, 0],
            qkv[:, q_cols + HD :],
        ],
        axis=1,
    ).astype(bf16)
    both_kv = jnp.concatenate([own_kv, shift(own_kv, "x", 1)], axis=0)
    keys = both_kv[:, :HD]
    values = both_kv[:, HD:]
    query_index = token_index(side)
    key_index = jnp.concatenate([query_index, token_index(1 - side)])
    scores = jnp.einsum("tgd,jd->gtj", queries, keys, preferred_element_type=f32) * score_scale
    allowed = key_index[None, :] <= query_index[:, None]
    scores = jnp.where(allowed, scores, -1e30)
    weights = jnp.exp(scores - jnp.max(scores, axis=-1, keepdims=True))
    probabilities = weights / jnp.sum(weights, axis=-1, keepdims=True)
    rounded_probs = probabilities.astype(bf16)
    attended = jnp.einsum("gtj,jd->tgd", rounded_probs, values, preferred_element_type=f32)
    own_attended = attended.reshape(group_len, q_cols).astype(bf16)

    def own_rows(values):
        return lax.dynamic_slice_in_dim(values, place * span_len, span_len, 0)

    attended_rows = gather_columns(own_attended, line)
    branch = jnp.dot(attended_rows, out_w, preferred_element_type=f32)
    middle_all = inputs + keep * branch
    inverse_mid = lax.rsqrt(jnp.mean(middle_all * middle_all, axis=-1, keepdims=True) + epsilon)
    second_norm = (middle_all * inverse_mid * gain_two).astype(bf16)
    middle = own_rows(middle_all)
    inverse_two = own_rows(inverse_mid)

    gate_up = jnp.dot(second_norm, ff_w, preferred_element_type=f32)
    gate_value = gate_up[:, :ff_cols]
    up_value = gate_up[:, ff_cols:]
    gate_sigmoid = jax.nn.sigmoid(gate_value)
    swish_value = gate_value * gate_sigmoid
    hidden = (swish_value * up_value).astype(bf16)
    hidden_grad = against(mixed_grad, down_w)
    gate_grad = hidden_grad * up_value * gate_sigmoid * (1.0 + gate_value * (1.0 - gate_sigmoid))
    up_grad = hidden_grad * swish_value
    both_grad = jnp.concatenate([gate_grad, up_grad], axis=1).astype(bf16)

    def split(values):
        return values.astype(bf16).reshape(line, span_len, model_width)

    def pair_sum(values, axis, dim):
        mine = pick(values, lax.axis_index(axis), dim).astype(f32)
        other = pick(values, 1 - lax.axis_index(axis), dim)
        return (mine + shift(other, axis, 1).astype(f32)).astype(bf16)

    def core_sum(values):
        return pair_sum(values, "c", values.ndim - 3)

    def near_sum(values):
        lead = values.ndim - 4
        cut = values.shape[-1] // 256 * 128
        left = pair_sum(pair_sum(values[..., :cut], "x", lead), "y", lead)
        right = pair_sum(pair_sum(values[..., cut:], "y", lead + 1), "x", lead)
        return jnp.concatenate([left, right], axis=-1)

    grad_ff = over_rows(second_norm, both_grad).astype(bf16)
    grad_ff = core_sum(grad_ff.reshape(line, 2, 2, 2, rows_each, -1))
    grad_down = over_rows(hidden, mixed_grad).astype(bf16)
    grad_down = core_sum(grad_down.reshape(2, 2, 2, -1, model_width))
    norm_grad = sum_blocks(split(against(both_grad, ff_w)), line)
    scaled_two = gain_two * norm_grad
    middle_grad = (
        upstream
        + inverse_two * scaled_two
        - middle
        * (inverse_two * inverse_two * inverse_two)
        * jnp.mean(scaled_two * middle, axis=-1, keepdims=True)
    )
    branch_grad = (keep * middle_grad).astype(bf16)
    own_grad = against(branch_grad, out_w).astype(bf16)
    attended_grad = turn_rows(own_grad, line).reshape(group_len, heads, HD)
    mixed_parts = jnp.dot(hidden, down_w, preferred_element_type=f32)
    mixed = ring_sum(split(after(mixed_parts, norm_grad)))
    output = (middle + keep * mixed).astype(bf16)
    prob_grad = jnp.einsum("tgd,jd->gtj", attended_grad, values, preferred_element_type=f32)
    delta = jnp.sum(attended_grad.astype(f32) * attended, axis=-1).T[..., None]
    score_grad = (probabilities * (prob_grad - delta)).astype(bf16)
    query_back = jnp.einsum("gtj,jd->tgd", score_grad, keys, preferred_element_type=f32) * score_scale
    key_back = jnp.einsum("gtj,tgd->jd", score_grad, queries, preferred_element_type=f32) * score_scale
    value_back = jnp.einsum("gtj,tgd->jd", rounded_probs, attended_grad, preferred_element_type=f32)
    kv_back = jnp.concatenate([key_back, value_back], axis=1)
    kv_back = kv_back[:group_len] + shift(kv_back[group_len:].astype(bf16), "x", 1).astype(f32)
    qkv_grad = jnp.concatenate(
        [
            rotate(query_back, token_pos, -1.0).reshape(group_len, q_cols),
            rotate(kv_back[:, None, :HD], token_pos, -1.0)[:, 0],
            kv_back[:, HD:],
        ],
        axis=1,
    ).astype(bf16)
    input_norm_grad = sum_blocks(split(against(qkv_grad, qkv_w)), line)
    inverse_one = own_rows(inverse_all)
    scaled_one = gain_one * input_norm_grad
    input_grad = (
        middle_grad
        + inverse_one * scaled_one
        - own_x
        * (inverse_one * inverse_one * inverse_one)
        * jnp.mean(scaled_one * own_x, axis=-1, keepdims=True)
    )

    def side_by_side(blocks):
        return blocks.transpose(1, 0, 2).reshape(rows_each, -1)

    ff_back = turn(near_sum(grad_ff)).astype(f32)
    grad_down = near_sum(grad_down).astype(f32)
    grad_out = over_rows(own_rows(attended_rows), branch_grad).astype(bf16)
    grad_out = near_sum(core_sum(grad_out.reshape(line, 2, 2, 2, rows_each, model_width)))
    grad_out = ring_sum(grad_out)
    grad_qkv = over_rows(first_norm, qkv_grad).astype(bf16)
    grad_qkv = near_sum(core_sum(grad_qkv.reshape(line, 2, 2, 2, rows_each, -1)))
    qkv_back = turn(grad_qkv).astype(f32)
    grad_query = side_by_side(qkv_back[:, :, :q_cols])
    grad_key = side_by_side(qkv_back[:, :, q_cols : q_cols + HD])
    grad_value = side_by_side(qkv_back[:, :, q_cols + HD :])
    grad_gate = side_by_side(ff_back[:, :, :ff_cols])
    grad_up = side_by_side(ff_back[:, :, ff_cols:])

    def gain_grad(pairs, gain):
        total = sum(jnp.sum(weight.astype(f32) * grad, axis=1) for weight, grad in pairs)
        return total / gain.astype(f32)

    return (
        output[None],
        input_grad.astype(bf16)[None],
        gain_grad([(w_query, grad_query), (w_key, grad_key), (w_value, grad_value)], attn_gain),
        grad_query,
        grad_key,
        grad_value,
        grad_out,
        gain_grad([(w_gate, grad_gate), (w_up, grad_up)], mlp_gain),
        grad_gate,
        grad_up,
        grad_down,
    )


def solution(mesh):
    wide, narrow = mesh.shape["wide"], mesh.shape["narrow"]
    if wide == 2 * KVH and narrow == 4:
        mesh = Mesh(mesh.devices.reshape(wide // 2, 2, 2, 2), ("z", "x", "y", "c"))
        body, wide, narrow = line_body, ("z", "x"), ("y", "c")
    else:
        body, wide, narrow = general_body, ("wide",), ("narrow",)
    token_spec = P(narrow, wide, None)
    id_spec = P(narrow, wide)
    gain_spec = P(wide + narrow)
    weight_spec = P(wide + narrow, None)
    return jax.shard_map(
        body,
        mesh=mesh,
        in_specs=(
            token_spec,
            gain_spec,
            weight_spec,
            weight_spec,
            weight_spec,
            weight_spec,
            gain_spec,
            weight_spec,
            weight_spec,
            weight_spec,
            P(narrow),
            id_spec,
            id_spec,
            P(),
            token_spec,
        ),
        out_specs=(
            token_spec,
            token_spec,
            gain_spec,
            weight_spec,
            weight_spec,
            weight_spec,
            weight_spec,
            gain_spec,
            weight_spec,
            weight_spec,
            weight_spec,
        ),
        check_vma=False,
    )
```

```python
import functools
import math

import jax
import jax.numpy as jnp
from jax import lax
from jax.experimental import pallas as pl
from jax.experimental.pallas import tpu as pltpu
from jax.sharding import Mesh
from jax.sharding import PartitionSpec as P

HEADS = 16
KVH = 4
HD = 128


epsilon = 1e-05


def rotate(vectors, token_pos, direction):
    half_size = vectors.shape[-1] // 2
    freqs = 10000.0 ** (-2.0 * jnp.arange(half_size, dtype=jnp.float32) / vectors.shape[-1])
    angles = token_pos.astype(jnp.float32)[:, None] * freqs[None, :]
    cosine = jnp.cos(angles)[:, None, :]
    sine = direction * jnp.sin(angles)[:, None, :]
    first_half = vectors[..., :half_size]
    second_half = vectors[..., half_size:]
    return jnp.concatenate(
        [first_half * cosine - second_half * sine, second_half * cosine + first_half * sine],
        axis=-1,
    )


def split_blocks(piece_arr, seq_count, kv_heads, head_dim):
    piece_len = piece_arr.shape[1]
    block_len = math.gcd(piece_len, 512)
    shaped = piece_arr.reshape(seq_count, piece_len // block_len, block_len, kv_heads, head_dim)
    return shaped.transpose(1, 0, 2, 3, 4)


def add_rows(whole_arr, update, first_row):
    current = lax.dynamic_slice_in_dim(whole_arr, first_row, update.shape[1], 1)
    return lax.dynamic_update_slice_in_dim(whole_arr, current + update, first_row, 1)


def over_rows(left, right):
    return lax.dot_general(
        left, right, (((0,), (0,)), ((), ())), preferred_element_type=jnp.float32
    )


def against(left, right):
    return lax.dot_general(
        left, right, (((1,), (1,)), ((), ())), preferred_element_type=jnp.float32
    )


def unchanged(carried):
    return carried


MESH = pl.DeviceIdType.MESH
AXES = ("z", "x", "y", "c")


class Links:
    def __init__(self, send_sems, recv_sems, line):
        self.send_sems, self.recv_sems, self.line = send_sems, recv_sems, line
        self.z, self.x, self.y, self.c = (lax.axis_index(name) for name in AXES)
        self.slot = self.x * 4 + self.y * 2 + self.c
        self.used = 0
        self.sent = []

    def device(self, to):
        if to == "x":
            return (self.z, 1 - self.x, self.y, self.c)
        if to == "y":
            return (self.z, self.x, 1 - self.y, self.c)
        if to == "c":
            return (self.z, self.x, self.y, 1 - self.c)
        return (self.along(to), self.x, self.y, self.c)

    def along(self, step):
        return lax.rem(self.z + step + self.line, self.line)

    def other(self, to):
        slot = self.slot
        for name in to:
            bit = {"x": 4, "y": 2, "c": 1}[name]
            here = {"x": self.x, "y": self.y, "c": self.c}[name]
            slot = slot + bit * (1 - 2 * here)
        return slot

    def meet(self, targets):
        barrier = pltpu.get_barrier_semaphore()
        for to in targets:
            pl.semaphore_signal(barrier, inc=1, device_id=self.device(to), device_id_type=MESH)
        pl.semaphore_wait(barrier, len(targets))

    def send(self, source, target, to):
        copy = pltpu.make_async_remote_copy(
            src_ref=source,
            dst_ref=target,
            send_sem=self.send_sems.at[self.used],
            recv_sem=self.recv_sems.at[self.used],
            device_id=self.device(to),
            device_id_type=MESH,
        )
        copy.start()
        self.used += 1
        self.sent.append(copy)
        return copy

    def keep(self, source, target):
        copy = pltpu.make_async_copy(source, target, self.send_sems.at[self.used])
        copy.start()
        self.used += 1
        return copy

    def finish(self):
        for copy in self.sent:
            copy.wait_send()


class NearGather:
    def __init__(self, links, slot):
        self.links, self.slot = links, slot
        self.got = {}

    def offer(self, block, source):
        target = self.slot(block, self.links.slot)
        for to in ("x", "y", "c"):
            self.got[block, to] = self.links.send(source, target, to)

    def relay(self, block, first):
        links = self.links
        for to, then in (("x", "y"), ("y", "x")):
            self.got[block, to].wait_recv()
            place = self.slot(block, links.other(to))
            self.got[block, to + "c"] = links.send(place, place, "c")
            if to == first:
                self.got[block, "xy"] = links.send(place, place, then)

    def close(self, block):
        self.got[block, "xy"].wait_recv()
        place = self.slot(block, self.links.other("xy"))
        self.got[block, "xyc"] = self.links.send(place, place, "c")

    def wait(self, blocks):
        for block in blocks:
            for to in ("c", "xc", "yc", "xyc"):
                self.got[block, to].wait_recv()


class RingGather:
    def __init__(self, links, source, place, pieces=4):
        self.links, self.source, self.place, self.pieces = links, source, place, pieces
        self.rows = source.shape[0] // pieces
        self.last = [None] * pieces

    def step(self, number):
        for piece in range(self.pieces):
            way = 1 if piece < self.pieces // 2 else -1
            rows = pl.ds(piece * self.rows, self.rows)
            place = self.place(self.links.along(-way * number), rows)
            if number > 0:
                self.last[piece].wait_recv()
            if number < self.links.line - 1:
                origin = self.source.at[rows] if number == 0 else place
                self.last[piece] = self.links.send(origin, place, way)


def first_kernel(line, x_ref, pos_ref, pack_ref, xs_ref, poss_ref, qkv_ref, send_sems, recv_sems):
    links = Links(send_sems, recv_sems, line)
    far = [1, line - 1] + list(range(2, line - 1))
    links.meet(["x", "y", "c"] + far)
    qkv = NearGather(links, lambda block, place: qkv_ref.at[links.along(-block), place])
    ring = RingGather(links, x_ref, lambda block, rows: xs_ref.at[block, rows])
    here = links.slot
    local = [
        links.keep(x_ref, xs_ref.at[links.z]),
        links.keep(pos_ref, poss_ref.at[links.z]),
        links.keep(pack_ref.at[links.z], qkv_ref.at[links.z, here]),
    ]
    turned = {k: links.send(pack_ref.at[links.along(k)], qkv_ref.at[links.z, here], k) for k in far}
    placed = [links.send(pos_ref, poss_ref.at[links.z], k) for k in far]
    ring.step(0)
    qkv.offer(0, pack_ref.at[links.z])
    for k in far:
        turned[k].wait_recv()
        qkv.offer(k, qkv_ref.at[links.along(-k), here])
    ring.step(1)
    for k in [0] + far:
        qkv.relay(k, "x" if k < line // 2 else "y")
    ring.step(2)
    for k in [0] + far:
        qkv.close(k)
    ring.step(3)
    qkv.wait(range(line))
    for copy in placed:
        copy.wait_recv()
    links.finish()
    for copy in local:
        copy.wait()


def second_kernel(line, att_ref, mix_ref, ff_ref, atts_ref, mixs_ref, ffs_ref, send_sems, recv_sems):
    links = Links(send_sems, recv_sems, line)
    links.meet(["x", "y", "c", 1, line - 1])
    columns = att_ref.shape[1]

    def place(block, rows):
        return atts_ref.at[rows, pl.ds(pl.multiple_of(block * columns, columns), columns)]

    rings = [
        RingGather(links, att_ref, place),
        RingGather(links, mix_ref, lambda block, rows: mixs_ref.at[block, rows]),
    ]
    near = NearGather(links, lambda block, slot: ffs_ref.at[block, slot])
    local = [
        links.keep(att_ref, place(links.z, pl.ds(0, att_ref.shape[0]))),
        links.keep(mix_ref, mixs_ref.at[links.z]),
    ]

    def step(number):
        for ring in rings:
            ring.step(number)

    step(0)
    for block in range(line):
        near.offer(block, ff_ref.at[block])
        local.append(links.keep(ff_ref.at[block], ffs_ref.at[block, links.slot]))
    for block in range(line):
        if block == line // 2:
            step(1)
        near.relay(block, "x" if block % 2 == 0 else "y")
    step(2)
    for block in range(line):
        near.close(block)
    step(3)
    near.wait(range(line))
    links.finish()
    for copy in local:
        copy.wait()


def add_rows_of(target, values, count):
    def add(index, carry):
        rows = pl.ds(pl.multiple_of(index * 16, 16), 16)
        target[rows] = target[rows] + values[rows]
        return carry

    lax.fori_loop(0, count // 16, add, 0)


class NearSum:
    def __init__(self, links, source, own, from_core, from_first, from_second, first):
        self.links, self.source, self.own, self.first = links, source, own, first
        self.from_core, self.from_first, self.from_second = from_core, from_first, from_second

    def start(self):
        links = self.links
        self.local = links.keep(self.source(links.c), self.own)
        self.copy = links.send(self.source(1 - links.c), self.from_core, "c")

    def add(self, target, values):
        add_rows_of(target, values, target.shape[0])

    def core_done(self):
        links = self.links
        self.copy.wait_recv()
        self.local.wait()
        for x in range(2):
            for y in range(2):
                self.add(self.own.at[x, y], self.from_core.at[x, y])
        if self.first == "x":
            self.copy = links.send(self.own.at[1 - links.x], self.from_first, "x")
        else:
            self.copy = links.send(self.own.at[:, 1 - links.y], self.from_first, "y")

    def first_done(self):
        links = self.links
        self.copy.wait_recv()
        for other in range(2):
            place = (links.x, other) if self.first == "x" else (other, links.y)
            self.add(self.own.at[place], self.from_first.at[other])
        if self.first == "x":
            self.copy = links.send(self.own.at[links.x, 1 - links.y], self.from_second, "y")
        else:
            self.copy = links.send(self.own.at[1 - links.x, links.y], self.from_second, "x")

    def second_done(self):
        self.copy.wait_recv()
        total = self.own.at[self.links.x, self.links.y]
        self.add(total, self.from_second)
        return total


def sum_space(blocks, rows, columns):
    shape = (rows, columns)
    return [
        pltpu.VMEM((blocks, 2, 2) + shape, jnp.bfloat16),
        pltpu.VMEM((blocks, 2, 2) + shape, jnp.bfloat16),
        pltpu.VMEM((blocks, 2) + shape, jnp.bfloat16),
        pltpu.VMEM((blocks,) + shape, jnp.bfloat16),
    ]


class RingSum:
    def __init__(self, links, parts, total, got, made, pieces=4):
        self.links, self.parts, self.total, self.got, self.made = links, parts, total, got, made
        self.pieces, self.last = pieces, [None] * pieces
        self.rows = parts.shape[1] // pieces

    def step(self, number):
        links = self.links
        for piece in range(self.pieces):
            way = 1 if piece < self.pieces // 2 else -1
            block = links.along(-way * (number + 1))
            where = pl.ds(piece * self.rows, self.rows)
            if number == 0:
                source = self.parts.at[block, where]
            else:
                self.last[piece].wait_recv()
                total = self.got[number - 1, where].astype(jnp.float32) + self.parts[
                    block, where
                ].astype(jnp.float32)
                if number == links.line - 1:
                    self.total[where] = total
                    continue
                self.made[number - 1, where] = total.astype(self.made.dtype)
                source = self.made.at[number - 1, where]
            self.last[piece] = links.send(source, self.got.at[number, where], way)


def ring_space(line, shape):
    return [pltpu.VMEM((line - 1,) + shape, jnp.bfloat16), pltpu.VMEM((line - 2,) + shape, jnp.bfloat16)]


def third_kernel(
    line, cuts, parts_ref, down_ref, total_ref, sum_ref, got, made, *scratch
):
    space, (send_sems, recv_sems) = scratch[:-2], scratch[-2:]
    links = Links(send_sems, recv_sems, line)
    links.meet(["x", "y", "c", 1, line - 1])
    ring = RingSum(links, parts_ref, total_ref, got, made)
    ring.step(0)
    items = []
    for index, (low, high) in enumerate(cuts):
        rows = pl.ds(low, high - low)
        own, core, first, second = space[4 * index : 4 * index + 4]
        items.append(
            NearSum(
                links,
                lambda c, rows=rows: down_ref.at[:, :, c, rows],
                own.at[0],
                core.at[0],
                first.at[0],
                second.at[0],
                "xy"[index % 2],
            )
        )
    for item in items:
        item.start()
    for item in items:
        item.core_done()
    ring.step(1)
    for item in items:
        item.first_done()
    ring.step(2)
    for item, (low, high) in zip(items, cuts):
        sum_ref[low:high] = item.second_done()[...]
    ring.step(3)
    links.finish()


def last_kernel(line, parts_ref, ff_ref, out_ref, qkv_ref, total_ref, ffs_ref, outs_ref, qkvs_ref, got, made, *scratch):
    space, (send_sems, recv_sems) = scratch[:-2], scratch[-2:]
    links = Links(send_sems, recv_sems, line)
    far = [1, line - 1] + list(range(2, line - 1))
    links.meet(["x", "y", "c"] + far)
    ring = RingSum(links, parts_ref, total_ref, got, made)
    ring.step(0)
    items = []
    for kind, (source, target) in enumerate(((ff_ref, ffs_ref), (out_ref, outs_ref), (qkv_ref, qkvs_ref))):
        own, core, first, second = space[4 * kind : 4 * kind + 4]
        for index, k in enumerate(far + [0]):
            item = NearSum(
                links,
                lambda c, source=source, k=k: source.at[links.along(k), :, :, c],
                own.at[index],
                core.at[index],
                first.at[index],
                second.at[index],
                "xy"[index % 2],
            )
            items.append((item, target, k))
    for item, _, _ in items:
        item.start()
    arrived, local = [], []

    def turn(item, target, k):
        total = item.second_done()
        if k == 0:
            local.append(links.keep(total, target.at[links.z]))
        else:
            arrived.append(links.send(total, target.at[links.z], k))

    pairs = [items[index : index + 2] for index in range(0, len(items), 2)]
    for number in range(len(pairs) + 2):
        if number < len(pairs):
            for item in pairs[number]:
                item[0].core_done()
        if 1 <= number < line:
            ring.step(number)
        if 1 <= number <= len(pairs):
            for item in pairs[number - 1]:
                item[0].first_done()
        if number >= 2:
            for item in pairs[number - 2]:
                turn(*item)
    for copy in arrived:
        copy.wait_recv()
    links.finish()
    for copy in local:
        copy.wait()


def turn_kernel(line, rows_ref, columns_ref, send_sems, recv_sems):
    links = Links(send_sems, recv_sems, line)
    far = [1, line - 1] + list(range(2, line - 1))
    links.meet(far)
    columns = columns_ref.shape[2]

    def part(block):
        return rows_ref.at[:, pl.ds(pl.multiple_of(block * columns, columns), columns)]

    local = links.keep(part(links.z), columns_ref.at[links.z])
    for k in far:
        links.send(part(links.along(k)), columns_ref.at[links.z], k)
    for copy in links.sent:
        copy.wait_recv()
    links.finish()
    local.wait()


def link_call(kernel, collective_id, copies, shapes, arguments, spaces=None, scratch=(), vmem=16):
    any_space = pl.BlockSpec(memory_space=pl.ANY)
    near_space = pl.BlockSpec(memory_space=pltpu.VMEM)
    many = isinstance(shapes, tuple)
    if spaces is None:
        spaces = "h" * (len(arguments) + (len(shapes) if many else 1))
    specs = [near_space if space == "v" else any_space for space in spaces]
    return pl.pallas_call(
        kernel,
        out_shape=shapes,
        in_specs=specs[: len(arguments)],
        out_specs=tuple(specs[len(arguments) :]) if many else specs[-1],
        scratch_shapes=list(scratch)
        + [pltpu.SemaphoreType.DMA((copies,)), pltpu.SemaphoreType.DMA((copies,))],
        compiler_params=pltpu.CompilerParams(
            collective_id=collective_id, has_side_effects=True, vmem_limit_bytes=vmem * 2**20
        ),
    )(*arguments)


def first_gather(tokens, positions, pack, line):
    return link_call(
        functools.partial(first_kernel, line),
        0,
        64,
        (
            jax.ShapeDtypeStruct((line,) + tokens.shape, tokens.dtype),
            jax.ShapeDtypeStruct((line,) + positions.shape, positions.dtype),
            jax.ShapeDtypeStruct((line, 8) + pack.shape[1:], pack.dtype),
        ),
        (tokens, positions, pack),
    )


def second_gather(attended, mixed, pack, line):
    return link_call(
        functools.partial(second_kernel, line),
        1,
        96,
        (
            jax.ShapeDtypeStruct((attended.shape[0], line * attended.shape[1]), attended.dtype),
            jax.ShapeDtypeStruct((line,) + mixed.shape, mixed.dtype),
            jax.ShapeDtypeStruct((line, 8) + pack.shape[1:], pack.dtype),
        ),
        (attended, mixed, pack),
    )


def third_sum(parts, grad_down, line):
    shape = parts.shape[1:]
    rows, columns = grad_down.shape[3:]
    half = (rows // 2 + 15) // 16 * 16
    cuts = ((0, half), (half, rows))
    return link_call(
        functools.partial(third_kernel, line, cuts),
        2,
        64,
        (jax.ShapeDtypeStruct(shape, jnp.float32), jax.ShapeDtypeStruct((rows, columns), jnp.bfloat16)),
        (parts, grad_down),
        "vhvv",
        ring_space(line, shape) + sum((sum_space(1, high - low, columns) for low, high in cuts), []),
        vmem=40,
    )


def last_sum(parts, grad_ff, grad_out, grad_qkv, line):
    shape = parts.shape[1:]
    grads = (grad_ff, grad_out, grad_qkv)
    return link_call(
        functools.partial(last_kernel, line),
        4,
        96,
        (jax.ShapeDtypeStruct(shape, jnp.float32),)
        + tuple(jax.ShapeDtypeStruct((line,) + grad.shape[4:], grad.dtype) for grad in grads),
        (parts,) + grads,
        "vhhhvhhh",
        ring_space(line, shape) + sum((sum_space(line, *grad.shape[4:]) for grad in grads), []),
        vmem=58,
    )


def turn_rows(values, line):
    return link_call(
        functools.partial(turn_kernel, line),
        3,
        line,
        jax.ShapeDtypeStruct((line, values.shape[0], values.shape[1] // line), values.dtype),
        (values,),
    )


def general_body(
    tokens,
    attn_gain,
    w_query,
    w_key,
    w_value,
    w_out,
    mlp_gain,
    w_gate,
    w_up,
    w_down,
    keep_mask,
    group_ids,
    positions,
    exit_scale,
    out_grad,
):
    seq_count, span_len, model_width = tokens.shape
    kv_heads = KVH
    head_dim = HD
    head_count = HEADS
    group_size = head_count // kv_heads
    row_count = seq_count * span_len
    stripe = group_size * span_len
    wide_count = lax.axis_size("wide")
    wide_place = lax.axis_index("wide")
    full_len = span_len * wide_count
    score_scale = 1.0 / math.sqrt(head_dim)
    gain_one, query_w, key_w, value_w, out_w = (
        lax.all_gather(attn_gain, ("wide", "narrow"), axis=0, tiled=True),
        lax.all_gather(w_query, ("wide", "narrow"), axis=0, tiled=True),
        lax.all_gather(w_key, ("wide", "narrow"), axis=0, tiled=True),
        lax.all_gather(w_value, ("wide", "narrow"), axis=0, tiled=True),
        lax.all_gather(w_out, ("wide", "narrow"), axis=0, tiled=True),
    )
    inputs = tokens.astype(jnp.float32).reshape(row_count, model_width)
    token_pos = positions.reshape(row_count)
    keep_rows = jnp.repeat(keep_mask.astype(jnp.float32), span_len)[:, None]
    inverse_one = lax.rsqrt(jnp.mean(inputs * inputs, axis=-1, keepdims=True) + epsilon)
    first_norm = (inputs * inverse_one * gain_one.astype(jnp.float32)).astype(jnp.bfloat16)
    query_pre = jnp.dot(first_norm, query_w, preferred_element_type=jnp.float32).reshape(
        row_count, head_count, head_dim
    )
    key_pre = jnp.dot(first_norm, key_w, preferred_element_type=jnp.float32).reshape(
        row_count, kv_heads, head_dim
    )
    query_rows = rotate(query_pre, token_pos, 1.0).astype(jnp.bfloat16)
    key_heads = (
        rotate(key_pre, token_pos, 1.0)
        .astype(jnp.bfloat16)
        .reshape(seq_count, span_len, kv_heads * head_dim)
    )
    value_heads = (
        jnp.dot(first_norm, value_w, preferred_element_type=jnp.float32)
        .astype(jnp.bfloat16)
        .reshape(seq_count, span_len, kv_heads * head_dim)
    )
    queries = (
        query_rows.reshape(seq_count, span_len, kv_heads, group_size, head_dim)
        .transpose(0, 2, 3, 1, 4)
        .reshape(seq_count, kv_heads, stripe, head_dim)
    )
    query_index = wide_place * span_len + jnp.arange(stripe, dtype=jnp.int32) % span_len
    last_query = wide_place * span_len + span_len - 1

    def block_scores(key_block, key_first):
        scores = (
            jnp.einsum("skrd,sjkd->skrj", queries, key_block, preferred_element_type=jnp.float32)
            * score_scale
        )
        key_index = key_first + jnp.arange(key_block.shape[1], dtype=jnp.int32)
        allowed = key_index[None, :] <= query_index[:, None]
        return (scores, allowed)

    start_forward = (
        jnp.full((seq_count, kv_heads, stripe), -1e30, jnp.float32),
        jnp.zeros((seq_count, kv_heads, stripe), jnp.float32),
        jnp.zeros((seq_count, kv_heads, stripe, head_dim), jnp.float32),
    )
    running = start_forward
    pieces = (
        lax.all_gather(key_heads, "wide", axis=1, tiled=True),
        lax.all_gather(value_heads, "wide", axis=1, tiled=True),
    )
    key_blocks = split_blocks(pieces[0], seq_count, kv_heads, head_dim)
    value_blocks = split_blocks(pieces[1], seq_count, kv_heads, head_dim)
    block_len = key_blocks.shape[2]

    def advance(carried, block_item):
        key_block, value_block, block_index = block_item
        key_first = block_index * block_len

        def compute_block(current):
            run_max, run_sum, run_acc = current
            scores, allowed = block_scores(key_block, key_first)
            scores = jnp.where(allowed, scores, -1e30)
            new_max = jnp.maximum(run_max, jnp.max(scores, axis=-1))
            factor = jnp.exp(run_max - new_max)
            weights = jnp.where(allowed, jnp.exp(scores - new_max[..., None]), 0.0)
            new_sum = run_sum * factor + jnp.sum(weights, axis=-1)
            new_acc = run_acc * factor[..., None] + jnp.einsum(
                "skrj,sjkd->skrd",
                weights.astype(jnp.bfloat16),
                value_block,
                preferred_element_type=jnp.float32,
            )
            return (new_max, new_sum, new_acc)

        return (lax.cond(key_first <= last_query, compute_block, unchanged, carried), None)

    running, _ = lax.scan(
        advance,
        running,
        (key_blocks, value_blocks, jnp.arange(key_blocks.shape[0], dtype=jnp.int32)),
    )
    run_max, run_sum, run_acc = running
    attended = run_acc / run_sum[..., None]
    log_total = run_max + jnp.log(run_sum)
    attended_rows = (
        attended.reshape(seq_count, kv_heads, group_size, span_len, head_dim)
        .transpose(0, 3, 1, 2, 4)
        .reshape(row_count, head_count * head_dim)
        .astype(jnp.bfloat16)
    )
    middle = inputs + keep_rows * jnp.dot(attended_rows, out_w, preferred_element_type=jnp.float32)
    gain_two, gate_w, up_w, down_w = (
        lax.all_gather(mlp_gain, ("wide", "narrow"), axis=0, tiled=True),
        lax.all_gather(w_gate, ("wide", "narrow"), axis=0, tiled=True),
        lax.all_gather(w_up, ("wide", "narrow"), axis=0, tiled=True),
        lax.all_gather(w_down, ("wide", "narrow"), axis=0, tiled=True),
    )
    inverse_two = lax.rsqrt(jnp.mean(middle * middle, axis=-1, keepdims=True) + epsilon)
    second_norm = (middle * inverse_two * gain_two.astype(jnp.float32)).astype(jnp.bfloat16)
    gate_value = jnp.dot(second_norm, gate_w, preferred_element_type=jnp.float32)
    up_value = jnp.dot(second_norm, up_w, preferred_element_type=jnp.float32)
    gate_sigmoid = jax.nn.sigmoid(gate_value)
    swish_value = gate_value * gate_sigmoid
    hidden = (swish_value * up_value).astype(jnp.bfloat16)
    output = (
        middle + keep_rows * jnp.dot(hidden, down_w, preferred_element_type=jnp.float32)
    ).astype(jnp.bfloat16)
    group_match = (
        group_ids.reshape(row_count)[:, None]
        == jnp.arange(exit_scale.shape[0], dtype=jnp.int32)[None, :]
    )
    token_scale = jnp.sum(jnp.where(group_match, exit_scale[None, :], 0.0), axis=1, keepdims=True)
    upstream = out_grad.astype(jnp.float32).reshape(row_count, model_width) * token_scale
    gain_two, gate_w, up_w, down_w = (
        lax.all_gather(mlp_gain, ("wide", "narrow"), axis=0, tiled=True),
        lax.all_gather(w_gate, ("wide", "narrow"), axis=0, tiled=True),
        lax.all_gather(w_up, ("wide", "narrow"), axis=0, tiled=True),
        lax.all_gather(w_down, ("wide", "narrow"), axis=0, tiled=True),
    )
    mixed_grad = (keep_rows * upstream).astype(jnp.bfloat16)
    grad_down = over_rows(hidden, mixed_grad)
    hidden_grad = against(mixed_grad, down_w)
    gate_grad = (
        hidden_grad * up_value * gate_sigmoid * (1.0 + gate_value * (1.0 - gate_sigmoid))
    ).astype(jnp.bfloat16)
    up_grad = (hidden_grad * swish_value).astype(jnp.bfloat16)
    grad_gate = over_rows(second_norm, gate_grad)
    grad_up = over_rows(second_norm, up_grad)
    norm_grad = against(gate_grad, gate_w) + against(up_grad, up_w)
    grad_gain_two = jnp.sum(norm_grad * middle * inverse_two, axis=0)
    scaled_two = gain_two.astype(jnp.float32) * norm_grad
    middle_grad = (
        upstream
        + inverse_two * scaled_two
        - middle
        * (inverse_two * inverse_two * inverse_two)
        * jnp.mean(scaled_two * middle, axis=-1, keepdims=True)
    )
    gain_two_share, gate_share, up_share, down_share = (
        lax.psum_scatter(grad_gain_two, ("wide", "narrow"), scatter_dimension=0, tiled=True),
        lax.psum_scatter(grad_gate, ("wide", "narrow"), scatter_dimension=0, tiled=True),
        lax.psum_scatter(grad_up, ("wide", "narrow"), scatter_dimension=0, tiled=True),
        lax.psum_scatter(grad_down, ("wide", "narrow"), scatter_dimension=0, tiled=True),
    )
    gain_one, query_w, key_w, value_w, out_w = (
        lax.all_gather(attn_gain, ("wide", "narrow"), axis=0, tiled=True),
        lax.all_gather(w_query, ("wide", "narrow"), axis=0, tiled=True),
        lax.all_gather(w_key, ("wide", "narrow"), axis=0, tiled=True),
        lax.all_gather(w_value, ("wide", "narrow"), axis=0, tiled=True),
        lax.all_gather(w_out, ("wide", "narrow"), axis=0, tiled=True),
    )
    branch_grad = (keep_rows * middle_grad).astype(jnp.bfloat16)
    grad_out = over_rows(attended_rows, branch_grad)
    attended_grad = against(branch_grad, out_w).astype(jnp.bfloat16)
    grouped_grad = (
        attended_grad.reshape(seq_count, span_len, kv_heads, group_size, head_dim)
        .transpose(0, 2, 3, 1, 4)
        .reshape(seq_count, kv_heads, stripe, head_dim)
    )
    row_delta = jnp.sum(grouped_grad.astype(jnp.float32) * attended, axis=-1)
    start_backward = (
        jnp.zeros((seq_count, kv_heads, stripe, head_dim), jnp.float32),
        jnp.zeros((seq_count, full_len, kv_heads * head_dim), jnp.float32),
        jnp.zeros((seq_count, full_len, kv_heads * head_dim), jnp.float32),
    )
    running = start_backward
    pieces = (
        lax.all_gather(key_heads, "wide", axis=1, tiled=True),
        lax.all_gather(value_heads, "wide", axis=1, tiled=True),
    )
    key_blocks = split_blocks(pieces[0], seq_count, kv_heads, head_dim)
    value_blocks = split_blocks(pieces[1], seq_count, kv_heads, head_dim)
    fold_block_len = key_blocks.shape[2]

    def advance(carried, block_item):
        key_block, value_block, block_index = block_item
        key_first = block_index * fold_block_len

        def compute_block(current):
            query_acc, key_acc, value_acc = current
            scores, allowed = block_scores(key_block, key_first)
            probabilities = jnp.where(allowed, jnp.exp(scores - log_total[..., None]), 0.0)
            value_part = jnp.einsum(
                "skrj,skrd->sjkd",
                probabilities.astype(jnp.bfloat16),
                grouped_grad,
                preferred_element_type=jnp.float32,
            )
            prob_grad = jnp.einsum(
                "skrd,sjkd->skrj", grouped_grad, value_block, preferred_element_type=jnp.float32
            )
            score_grad = (probabilities * (prob_grad - row_delta[..., None])).astype(jnp.bfloat16)
            query_acc = (
                query_acc
                + jnp.einsum(
                    "skrj,sjkd->skrd", score_grad, key_block, preferred_element_type=jnp.float32
                )
                * score_scale
            )
            key_part = (
                jnp.einsum(
                    "skrj,skrd->sjkd", score_grad, queries, preferred_element_type=jnp.float32
                )
                * score_scale
            )
            key_acc = add_rows(
                key_acc, key_part.reshape(seq_count, fold_block_len, kv_heads * head_dim), key_first
            )
            value_acc = add_rows(
                value_acc,
                value_part.reshape(seq_count, fold_block_len, kv_heads * head_dim),
                key_first,
            )
            return (query_acc, key_acc, value_acc)

        return (lax.cond(key_first <= last_query, compute_block, unchanged, carried), None)

    running, _ = lax.scan(
        advance,
        running,
        (key_blocks, value_blocks, jnp.arange(key_blocks.shape[0], dtype=jnp.int32)),
    )
    query_acc, key_acc, value_acc = running
    key_sum, value_sum = (
        lax.psum_scatter(
            key_acc.astype(jnp.bfloat16), "wide", scatter_dimension=1, tiled=True
        ).astype(jnp.float32),
        lax.psum_scatter(
            value_acc.astype(jnp.bfloat16), "wide", scatter_dimension=1, tiled=True
        ).astype(jnp.float32),
    )
    query_back = (
        query_acc.reshape(seq_count, kv_heads, group_size, span_len, head_dim)
        .transpose(0, 3, 1, 2, 4)
        .reshape(row_count, head_count, head_dim)
    )
    query_grad = (
        rotate(query_back, token_pos, -1.0)
        .reshape(row_count, head_count * head_dim)
        .astype(jnp.bfloat16)
    )
    key_grad = (
        rotate(key_sum.reshape(row_count, kv_heads, head_dim), token_pos, -1.0)
        .reshape(row_count, kv_heads * head_dim)
        .astype(jnp.bfloat16)
    )
    value_grad = value_sum.reshape(row_count, kv_heads * head_dim).astype(jnp.bfloat16)
    grad_query = over_rows(first_norm, query_grad)
    grad_key = over_rows(first_norm, key_grad)
    grad_value = over_rows(first_norm, value_grad)
    input_norm_grad = (
        against(query_grad, query_w) + against(key_grad, key_w) + against(value_grad, value_w)
    )
    grad_gain_one = jnp.sum(input_norm_grad * inputs * inverse_one, axis=0)
    scaled_one = gain_one.astype(jnp.float32) * input_norm_grad
    input_grad = (
        middle_grad
        + inverse_one * scaled_one
        - inputs
        * (inverse_one * inverse_one * inverse_one)
        * jnp.mean(scaled_one * inputs, axis=-1, keepdims=True)
    )
    gain_one_share, query_share, key_share, value_share, out_share = (
        lax.psum_scatter(grad_gain_one, ("wide", "narrow"), scatter_dimension=0, tiled=True),
        lax.psum_scatter(grad_query, ("wide", "narrow"), scatter_dimension=0, tiled=True),
        lax.psum_scatter(grad_key, ("wide", "narrow"), scatter_dimension=0, tiled=True),
        lax.psum_scatter(grad_value, ("wide", "narrow"), scatter_dimension=0, tiled=True),
        lax.psum_scatter(grad_out, ("wide", "narrow"), scatter_dimension=0, tiled=True),
    )
    return (
        output.reshape(seq_count, span_len, model_width),
        input_grad.astype(jnp.bfloat16).reshape(seq_count, span_len, model_width),
        gain_one_share,
        query_share,
        key_share,
        value_share,
        out_share,
        gain_two_share,
        gate_share,
        up_share,
        down_share,
    )


def line_body(
    tokens,
    attn_gain,
    w_query,
    w_key,
    w_value,
    w_out,
    mlp_gain,
    w_gate,
    w_up,
    w_down,
    keep_mask,
    group_ids,
    positions,
    exit_scale,
    out_grad,
):
    f32 = jnp.float32
    bf16 = jnp.bfloat16
    _, span_len, model_width = tokens.shape
    line = lax.axis_size("z")
    place = lax.axis_index("z")
    side = lax.axis_index("x")
    near = lax.axis_size("x") * lax.axis_size("y") * lax.axis_size("c")
    rows_each = w_query.shape[0]
    heads = HEADS // line
    q_cols = heads * HD
    ff_cols = w_gate.shape[1] // line
    group_len = span_len * line
    score_scale = 1.0 / math.sqrt(HD)

    def shift(values, axis, step):
        size = lax.axis_size(axis)
        return lax.ppermute(values, axis, [(i, (i + step) % size) for i in range(size)])

    def after(values, first):
        return lax.optimization_barrier((values, first))[0]

    def pick(values, index, dim):
        return lax.dynamic_index_in_dim(values, index, dim, keepdims=False)

    def back_order(blocks):
        return jnp.take(blocks, (place - jnp.arange(line, dtype=jnp.int32)) % line, axis=0)

    def ring_sum(blocks):
        total = pick(blocks, (place - 1) % line, 0)
        for hop in range(1, line):
            own = pick(blocks, (place - 1 - hop) % line, 0)
            total = shift(total, "z", 1).astype(f32) + own.astype(f32)
            if hop < line - 1:
                total = total.astype(bf16)
        return total

    def by_columns(weight, columns):
        return weight.reshape(rows_each, line, columns).transpose(1, 0, 2)

    def turn(pack):
        got = [pick(pack, place, 0)]
        for k in range(1, line):
            got.append(shift(pick(pack, (place + k) % line, 0), "z", k))
        return back_order(jnp.stack(got))

    gains = jnp.stack([attn_gain, mlp_gain] + [jnp.zeros_like(attn_gain)] * (HD - 2), axis=1)
    pack_attn = jnp.concatenate(
        [
            by_columns(w_query, q_cols),
            by_columns(w_key, HD),
            by_columns(w_value, HD),
            jnp.broadcast_to(gains[None], (line,) + gains.shape),
        ],
        axis=2,
    )
    place_rows = jnp.broadcast_to(positions[0].astype(f32)[None, :], (8, span_len))
    x_blocks, place_blocks, near_w = first_gather(tokens[0], place_rows, pack_attn, line)
    inputs = x_blocks.reshape(group_len, model_width).astype(f32)
    token_pos = place_blocks[:, 0].reshape(group_len)
    near_w = near_w.reshape(model_width, -1)
    qkv_w = near_w[:, : q_cols + 2 * HD]
    gain_rows = near_w[:, q_cols + 2 * HD : q_cols + 2 * HD + 2].astype(f32).T
    gain_one, gain_two = gain_rows[:1], gain_rows[1:]

    out_w = lax.all_gather(w_out, ("z", "x", "y", "c"), axis=0, tiled=True)
    down_w = lax.all_gather(w_down, ("x", "y", "c"), axis=0, tiled=True)
    pack_ff = jnp.concatenate([by_columns(w_gate, ff_cols), by_columns(w_up, ff_cols)], axis=2)
    turned_ff = turn(after(pack_ff, x_blocks))

    own_x = tokens[0].astype(f32)
    keep = keep_mask[0].astype(f32)
    group_match = group_ids[0][:, None] == jnp.arange(exit_scale.shape[0], dtype=jnp.int32)[None, :]
    token_scale = jnp.sum(jnp.where(group_match, exit_scale[None, :], 0.0), axis=1, keepdims=True)
    upstream = out_grad[0].astype(f32) * token_scale

    inside = jnp.arange(span_len, dtype=jnp.int32)
    block_first = jnp.arange(line, dtype=jnp.int32) * (2 * span_len)

    def token_index(which):
        return (block_first[:, None] + which * span_len + inside[None, :]).reshape(group_len)

    inverse_all = lax.rsqrt(jnp.mean(inputs * inputs, axis=-1, keepdims=True) + epsilon)
    first_norm = (inputs * inverse_all * gain_one).astype(bf16)
    qkv = jnp.dot(first_norm, qkv_w, preferred_element_type=f32)
    queries = rotate(qkv[:, :q_cols].reshape(group_len, heads, HD), token_pos, 1.0).astype(bf16)
    own_kv = jnp.concatenate(
        [
            rotate(qkv[:, q_cols : q_cols + HD].reshape(group_len, 1, HD), token_pos, 1.0)[:, 0],
            qkv[:, q_cols + HD :],
        ],
        axis=1,
    ).astype(bf16)
    both_kv = jnp.concatenate([own_kv, shift(own_kv, "x", 1)], axis=0)
    keys = both_kv[:, :HD]
    values = both_kv[:, HD:]
    query_index = token_index(side)
    key_index = jnp.concatenate([query_index, token_index(1 - side)])
    scores = jnp.einsum("tgd,jd->gtj", queries, keys, preferred_element_type=f32) * score_scale
    allowed = key_index[None, :] <= query_index[:, None]
    scores = jnp.where(allowed, scores, -1e30)
    weights = jnp.exp(scores - jnp.max(scores, axis=-1, keepdims=True))
    probabilities = weights / jnp.sum(weights, axis=-1, keepdims=True)
    rounded_probs = probabilities.astype(bf16)
    attended = jnp.einsum("gtj,jd->tgd", rounded_probs, values, preferred_element_type=f32)
    own_attended = attended.reshape(group_len, q_cols).astype(bf16)

    def own_rows(values):
        return lax.dynamic_slice_in_dim(values, place * span_len, span_len, 0)

    attended_rows, mixed_grad, ff_w = second_gather(
        own_attended, (keep * upstream).astype(bf16), turned_ff, line
    )
    mixed_grad = mixed_grad.reshape(group_len, model_width)
    ff_w = ff_w.reshape(model_width, 2 * ff_cols)
    branch = jnp.dot(attended_rows, out_w, preferred_element_type=f32)
    middle_all = inputs + keep * branch
    inverse_mid = lax.rsqrt(jnp.mean(middle_all * middle_all, axis=-1, keepdims=True) + epsilon)
    second_norm = (middle_all * inverse_mid * gain_two).astype(bf16)
    middle = own_rows(middle_all)
    inverse_two = own_rows(inverse_mid)

    gate_up = jnp.dot(second_norm, ff_w, preferred_element_type=f32)
    gate_value = gate_up[:, :ff_cols]
    up_value = gate_up[:, ff_cols:]
    gate_sigmoid = jax.nn.sigmoid(gate_value)
    swish_value = gate_value * gate_sigmoid
    hidden = (swish_value * up_value).astype(bf16)
    hidden_grad = against(mixed_grad, down_w)
    gate_grad = hidden_grad * up_value * gate_sigmoid * (1.0 + gate_value * (1.0 - gate_sigmoid))
    up_grad = hidden_grad * swish_value
    both_grad = jnp.concatenate([gate_grad, up_grad], axis=1).astype(bf16)

    def split(values):
        return values.astype(bf16).reshape(line, span_len, model_width)

    grad_down = over_rows(hidden, mixed_grad).astype(bf16).reshape(2, 2, 2, -1, model_width)
    norm_grad, grad_down = third_sum(split(against(both_grad, ff_w)), grad_down, line)
    grad_down = grad_down.astype(f32)
    grad_ff = over_rows(second_norm, after(both_grad, norm_grad)).astype(bf16)
    scaled_two = gain_two * norm_grad
    middle_grad = (
        upstream
        + inverse_two * scaled_two
        - middle
        * (inverse_two * inverse_two * inverse_two)
        * jnp.mean(scaled_two * middle, axis=-1, keepdims=True)
    )
    branch_grad = (keep * middle_grad).astype(bf16)
    own_grad = against(branch_grad, out_w).astype(bf16)
    attended_grad = turn_rows(own_grad, line).reshape(group_len, heads, HD)
    mixed_parts = jnp.dot(hidden, down_w, preferred_element_type=f32)
    mixed = ring_sum(split(after(mixed_parts, norm_grad)))
    output = (middle + keep * mixed).astype(bf16)
    prob_grad = jnp.einsum("tgd,jd->gtj", attended_grad, values, preferred_element_type=f32)
    delta = jnp.sum(attended_grad.astype(f32) * attended, axis=-1).T[..., None]
    score_grad = (probabilities * (prob_grad - delta)).astype(bf16)
    query_back = jnp.einsum("gtj,jd->tgd", score_grad, keys, preferred_element_type=f32) * score_scale
    key_back = jnp.einsum("gtj,tgd->jd", score_grad, queries, preferred_element_type=f32) * score_scale
    value_back = jnp.einsum("gtj,tgd->jd", rounded_probs, attended_grad, preferred_element_type=f32)
    kv_back = jnp.concatenate([key_back, value_back], axis=1)
    kv_back = kv_back[:group_len] + shift(kv_back[group_len:].astype(bf16), "x", 1).astype(f32)
    qkv_grad = jnp.concatenate(
        [
            rotate(query_back, token_pos, -1.0).reshape(group_len, q_cols),
            rotate(kv_back[:, None, :HD], token_pos, -1.0)[:, 0],
            kv_back[:, HD:],
        ],
        axis=1,
    ).astype(bf16)
    grad_out = over_rows(own_rows(attended_rows), branch_grad).astype(bf16)
    grad_qkv = over_rows(first_norm, qkv_grad).astype(bf16)

    def by_place(grad):
        return grad.reshape(line, 2, 2, 2, rows_each, grad.shape[1])

    input_norm_grad, ff_back, out_back, qkv_back = last_sum(
        split(against(qkv_grad, qkv_w)), by_place(grad_ff), by_place(grad_out), by_place(grad_qkv), line
    )
    ff_back = ff_back.astype(f32)
    qkv_back = qkv_back.astype(f32)
    grad_out = jnp.sum(out_back.astype(f32), axis=0)
    inverse_one = own_rows(inverse_all)
    scaled_one = gain_one * input_norm_grad
    input_grad = (
        middle_grad
        + inverse_one * scaled_one
        - own_x
        * (inverse_one * inverse_one * inverse_one)
        * jnp.mean(scaled_one * own_x, axis=-1, keepdims=True)
    )

    def side_by_side(blocks):
        return blocks.transpose(1, 0, 2).reshape(rows_each, -1)

    grad_query = side_by_side(qkv_back[:, :, :q_cols])
    grad_key = side_by_side(qkv_back[:, :, q_cols : q_cols + HD])
    grad_value = side_by_side(qkv_back[:, :, q_cols + HD :])
    grad_gate = side_by_side(ff_back[:, :, :ff_cols])
    grad_up = side_by_side(ff_back[:, :, ff_cols:])

    def gain_grad(pairs, gain):
        total = sum(jnp.sum(weight.astype(f32) * grad, axis=1) for weight, grad in pairs)
        return total / gain.astype(f32)

    return (
        output[None],
        input_grad.astype(bf16)[None],
        gain_grad([(w_query, grad_query), (w_key, grad_key), (w_value, grad_value)], attn_gain),
        grad_query,
        grad_key,
        grad_value,
        grad_out,
        gain_grad([(w_gate, grad_gate), (w_up, grad_up)], mlp_gain),
        grad_gate,
        grad_up,
        grad_down,
    )


def solution(mesh):
    wide, narrow = mesh.shape["wide"], mesh.shape["narrow"]
    if wide == 2 * KVH and narrow == 4:
        mesh = Mesh(mesh.devices.reshape(wide // 2, 2, 2, 2), ("z", "x", "y", "c"))
        body, wide, narrow = line_body, ("z", "x"), ("y", "c")
    else:
        body, wide, narrow = general_body, ("wide",), ("narrow",)
    token_spec = P(narrow, wide, None)
    id_spec = P(narrow, wide)
    gain_spec = P(wide + narrow)
    weight_spec = P(wide + narrow, None)
    return jax.shard_map(
        body,
        mesh=mesh,
        in_specs=(
            token_spec,
            gain_spec,
            weight_spec,
            weight_spec,
            weight_spec,
            weight_spec,
            gain_spec,
            weight_spec,
            weight_spec,
            weight_spec,
            P(narrow),
            id_spec,
            id_spec,
            P(),
            token_spec,
        ),
        out_specs=(
            token_spec,
            token_spec,
            gain_spec,
            weight_spec,
            weight_spec,
            weight_spec,
            weight_spec,
            gain_spec,
            weight_spec,
            weight_spec,
            weight_spec,
        ),
        check_vma=False,
    )
```

```python
import functools
import math

import jax
import jax.numpy as jnp
from jax import lax
from jax.experimental import pallas as pl
from jax.experimental.pallas import tpu as pltpu
from jax.sharding import Mesh
from jax.sharding import PartitionSpec as P

HEADS = 16
KVH = 4
HD = 128


epsilon = 1e-05


def rotate(vectors, token_pos, direction):
    half_size = vectors.shape[-1] // 2
    freqs = 10000.0 ** (-2.0 * jnp.arange(half_size, dtype=jnp.float32) / vectors.shape[-1])
    angles = token_pos.astype(jnp.float32)[:, None] * freqs[None, :]
    cosine = jnp.cos(angles)[:, None, :]
    sine = direction * jnp.sin(angles)[:, None, :]
    first_half = vectors[..., :half_size]
    second_half = vectors[..., half_size:]
    return jnp.concatenate(
        [first_half * cosine - second_half * sine, second_half * cosine + first_half * sine],
        axis=-1,
    )


def split_blocks(piece_arr, seq_count, kv_heads, head_dim):
    piece_len = piece_arr.shape[1]
    block_len = math.gcd(piece_len, 512)
    shaped = piece_arr.reshape(seq_count, piece_len // block_len, block_len, kv_heads, head_dim)
    return shaped.transpose(1, 0, 2, 3, 4)


def add_rows(whole_arr, update, first_row):
    current = lax.dynamic_slice_in_dim(whole_arr, first_row, update.shape[1], 1)
    return lax.dynamic_update_slice_in_dim(whole_arr, current + update, first_row, 1)


def over_rows(left, right):
    return lax.dot_general(
        left, right, (((0,), (0,)), ((), ())), preferred_element_type=jnp.float32
    )


def against(left, right):
    return lax.dot_general(
        left, right, (((1,), (1,)), ((), ())), preferred_element_type=jnp.float32
    )


def unchanged(carried):
    return carried


MESH = pl.DeviceIdType.MESH
AXES = ("z", "x", "y", "c")


class Links:
    def __init__(self, send_sems, recv_sems, line):
        self.send_sems, self.recv_sems, self.line = send_sems, recv_sems, line
        self.z, self.x, self.y, self.c = (lax.axis_index(name) for name in AXES)
        self.slot = self.x * 4 + self.y * 2 + self.c
        self.used = 0
        self.sent = []

    def device(self, to):
        if to == "x":
            return (self.z, 1 - self.x, self.y, self.c)
        if to == "y":
            return (self.z, self.x, 1 - self.y, self.c)
        if to == "c":
            return (self.z, self.x, self.y, 1 - self.c)
        return (self.along(to), self.x, self.y, self.c)

    def along(self, step):
        return lax.rem(self.z + step + self.line, self.line)

    def other(self, to):
        slot = self.slot
        for name in to:
            bit = {"x": 4, "y": 2, "c": 1}[name]
            here = {"x": self.x, "y": self.y, "c": self.c}[name]
            slot = slot + bit * (1 - 2 * here)
        return slot

    def meet(self, targets):
        barrier = pltpu.get_barrier_semaphore()
        for to in targets:
            pl.semaphore_signal(barrier, inc=1, device_id=self.device(to), device_id_type=MESH)
        pl.semaphore_wait(barrier, len(targets))

    def send(self, source, target, to):
        copy = pltpu.make_async_remote_copy(
            src_ref=source,
            dst_ref=target,
            send_sem=self.send_sems.at[self.used],
            recv_sem=self.recv_sems.at[self.used],
            device_id=self.device(to),
            device_id_type=MESH,
        )
        copy.start()
        self.used += 1
        self.sent.append(copy)
        return copy

    def keep(self, source, target):
        copy = pltpu.make_async_copy(source, target, self.send_sems.at[self.used])
        copy.start()
        self.used += 1
        return copy

    def finish(self):
        for copy in self.sent:
            copy.wait_send()


class NearGather:
    def __init__(self, links, slot):
        self.links, self.slot = links, slot
        self.got = {}

    def offer(self, block, source):
        target = self.slot(block, self.links.slot)
        for to in ("x", "y", "c"):
            self.got[block, to] = self.links.send(source, target, to)

    def relay(self, block, first):
        links = self.links
        for to, then in (("x", "y"), ("y", "x")):
            self.got[block, to].wait_recv()
            place = self.slot(block, links.other(to))
            self.got[block, to + "c"] = links.send(place, place, "c")
            if to == first:
                self.got[block, "xy"] = links.send(place, place, then)

    def close(self, block):
        self.got[block, "xy"].wait_recv()
        place = self.slot(block, self.links.other("xy"))
        self.got[block, "xyc"] = self.links.send(place, place, "c")

    def wait(self, blocks):
        for block in blocks:
            for to in ("c", "xc", "yc", "xyc"):
                self.got[block, to].wait_recv()


class RingGather:
    def __init__(self, links, source, place, pieces=4):
        self.links, self.source, self.place, self.pieces = links, source, place, pieces
        self.rows = source.shape[0] // pieces
        self.last = [None] * pieces

    def step(self, number):
        for piece in range(self.pieces):
            way = 1 if piece < self.pieces // 2 else -1
            rows = pl.ds(piece * self.rows, self.rows)
            place = self.place(self.links.along(-way * number), rows)
            if number > 0:
                self.last[piece].wait_recv()
            if number < self.links.line - 1:
                origin = self.source.at[rows] if number == 0 else place
                self.last[piece] = self.links.send(origin, place, way)


def first_kernel(
    line,
    x_ref,
    table_ref,
    pack_ref,
    ff_ref,
    mix_ref,
    xs_ref,
    weight_ref,
    gain_ref,
    norm_ref,
    query_ref,
    kv_ref,
    peak_ref,
    turn_ref,
    atts_ref,
    mixs_ref,
    ffs_ref,
    x_all,
    tables,
    weights,
    gains,
    norm,
    turns,
    flat,
    query,
    kv,
    peak,
    att,
    send_sems,
    recv_sems,
):
    f32, bf16 = jnp.float32, jnp.bfloat16
    links = Links(send_sems, recv_sems, line)
    far = [1, line - 1] + list(range(2, line - 1))
    links.meet(["x", "y", "c"] + far)
    here = links.slot
    span_len, width = x_ref.shape
    group_len = line * span_len
    rows_each = ff_ref.shape[1]
    q_cols = query.shape[1]
    heads = q_cols // HD
    local = []

    near = NearGather(links, lambda block, place: weights.at[links.along(-block), place])
    far_ff = NearGather(links, lambda block, place: ffs_ref.at[links.along(-block), place])
    ring = RingGather(links, x_ref, lambda block, rows: x_all.at[block, rows])
    own = [
        links.keep(x_ref, x_all.at[links.z]),
        links.keep(table_ref, tables.at[links.z]),
        links.keep(pack_ref.at[links.z], weights.at[links.z, here]),
    ]
    turned = {k: links.send(pack_ref.at[links.along(k)], weights.at[links.z, here], k) for k in far}
    placed = [links.send(table_ref, tables.at[links.z], k) for k in far]
    ring.step(0)
    near.offer(0, pack_ref.at[links.z])
    local.append(links.keep(ff_ref.at[links.z], ffs_ref.at[links.z, here]))
    local.append(links.keep(mix_ref, mixs_ref.at[links.z]))
    for k in far:
        turned[k].wait_recv()
        near.offer(k, weights.at[links.along(-k), here])
    ring.step(1)
    for k in [0] + far:
        near.relay(k, "x" if k < line // 2 else "y")
    far_ff.offer(0, ff_ref.at[links.z])
    ring.step(2)
    turned_ff = {k: links.send(ff_ref.at[links.along(k)], ffs_ref.at[links.z, here], k) for k in far}
    for k in [0] + far:
        near.close(k)
    for copy in own:
        copy.wait()
    for copy in placed:
        copy.wait_recv()

    lane = lax.broadcasted_iota(jnp.int32, (span_len, HD), 1)
    for block in range(line):
        table = tables[block]
        swapped = pltpu.roll(table, HD // 2, 1)
        rows = slice(block * span_len, (block + 1) * span_len)
        turns[0, rows] = jnp.where(lane < HD // 2, table, swapped)
        turns[1, rows] = jnp.where(lane < HD // 2, -swapped, table)
    local.append(links.keep(turns, turn_ref))
    near.wait(range(line))
    for index in range(line * 4):
        z, q = divmod(index, 4)
        for which in range(2):
            lanes = slice(which * HD, (which + 1) * HD)
            both = [weights[z, 2 * q + c, rows_each : rows_each + 16, lanes].astype(f32) for c in range(2)]
            gains[which, :, index * HD : (index + 1) * HD] = both[0] + both[1]
    local.append(links.keep(weights, weight_ref))
    local.append(links.keep(gains, gain_ref))
    ring.step(3)
    local.append(links.keep(x_all, xs_ref))

    def normalise(index, carry):
        block = index // (span_len // 16)
        rows = pl.ds(pl.multiple_of(lax.rem(index, span_len // 16) * 16, 16), 16)
        values = x_all[block, rows].astype(f32)
        inverse = lax.rsqrt(jnp.mean(values * values, axis=-1, keepdims=True) + epsilon)
        target = pl.ds(pl.multiple_of(index * 16, 16), 16)
        norm[target] = (values * inverse * gains[0]).astype(bf16)
        return carry

    lax.fori_loop(0, group_len // 16, normalise, 0)
    local.append(links.keep(norm, norm_ref))

    def project(low, high):
        step = group_len // 2
        for part in range(2):
            rows = slice(part * step, (part + 1) * step)
            total = None
            for z in range(line):
                weight = weights[z, :, :rows_each, low:high].reshape(8 * rows_each, high - low)
                term = jnp.dot(
                    norm[rows, z * 8 * rows_each : (z + 1) * 8 * rows_each],
                    weight,
                    preferred_element_type=f32,
                )
                total = term if total is None else total + term
            flat[rows, low:high] = total

    def turn(values, rows):
        return values * turns[0, rows] + pltpu.roll(values, HD // 2, 1) * turns[1, rows]

    project(q_cols, q_cols + 2 * HD)
    for block in range(line):
        rows = slice(block * span_len, (block + 1) * span_len)
        kv[0, rows, :HD] = turn(flat[rows, q_cols : q_cols + HD], rows).astype(bf16)
        kv[0, rows, HD:] = flat[rows, q_cols + HD : q_cols + 2 * HD].astype(bf16)
    exchange = links.send(kv.at[0], kv.at[1], "x")
    project(0, q_cols)
    for block in range(line):
        rows = slice(block * span_len, (block + 1) * span_len)
        for head in range(heads):
            lanes = slice(head * HD, (head + 1) * HD)
            query[rows, lanes] = turn(flat[rows, lanes], rows).astype(bf16)
    local.append(links.keep(query, query_ref))
    exchange.wait_recv()
    local.append(links.keep(kv, kv_ref))

    scale = 1.0 / math.sqrt(HD)
    peak[...] = jnp.zeros_like(peak)

    def attend(head, carry):
        lanes = pl.ds(pl.multiple_of(head * HD, HD), HD)
        for block in range(line):
            rows = slice(block * span_len, (block + 1) * span_len)
            reach = (block + 1) * span_len
            part = query[rows, lanes]
            row = lax.broadcasted_iota(jnp.int32, (span_len, reach), 0) + block * span_len
            column = lax.broadcasted_iota(jnp.int32, (span_len, reach), 1)
            allowed = (column <= row, column < (block + links.x) * span_len)
            scores = []
            for half in range(2):
                score = lax.dot_general(
                    part, kv[half, :reach, :HD], (((1,), (1,)), ((), ())), preferred_element_type=f32
                )
                scores.append(jnp.where(allowed[half], score * scale, -1e30))
            top = jnp.maximum(
                jnp.max(scores[0], axis=-1, keepdims=True), jnp.max(scores[1], axis=-1, keepdims=True)
            )
            total, mixed = None, None
            for half in range(2):
                weight = jnp.exp(scores[half] - top)
                count = jnp.sum(weight, axis=-1, keepdims=True)
                term = jnp.dot(weight.astype(bf16), kv[half, :reach, HD:], preferred_element_type=f32)
                total = count if total is None else total + count
                mixed = term if mixed is None else mixed + term
            att[rows, lanes] = (mixed / total).astype(bf16)
            spot = lax.broadcasted_iota(jnp.int32, (span_len, HD), 1) == head
            peak[rows] = jnp.where(spot, top + jnp.log(total), peak[rows])
        return carry

    lax.fori_loop(0, heads, attend, 0)
    local.append(links.keep(peak, peak_ref))

    def place(block, rows):
        return atts_ref.at[rows, pl.ds(pl.multiple_of(block * q_cols, q_cols), q_cols)]

    att_ring = RingGather(links, att, place)
    mix_ring = RingGather(links, mix_ref, lambda block, rows: mixs_ref.at[block, rows])
    local.append(links.keep(att, place(links.z, pl.ds(0, group_len))))
    att_ring.step(0)
    for k in far:
        turned_ff[k].wait_recv()
        far_ff.offer(k, ffs_ref.at[links.along(-k), here])
    far_ff.relay(0, "x")
    far_ff.close(0)
    att_ring.step(1)
    mix_ring.step(0)
    for k in far:
        far_ff.relay(k, "x" if k < line // 2 else "y")
    att_ring.step(2)
    mix_ring.step(1)
    for k in far:
        far_ff.close(k)
    att_ring.step(3)
    mix_ring.step(2)
    mix_ring.step(3)
    far_ff.wait(range(line))
    links.finish()
    for copy in local:
        copy.wait()


def add_rows_of(target, values, count):
    def add(index, carry):
        rows = pl.ds(pl.multiple_of(index * 16, 16), 16)
        target[rows] = target[rows] + values[rows]
        return carry

    lax.fori_loop(0, count // 16, add, 0)


class NearSum:
    def __init__(self, links, source, own, from_core, from_first, from_second, first):
        self.links, self.source, self.own, self.first = links, source, own, first
        self.from_core, self.from_first, self.from_second = from_core, from_first, from_second

    def start(self):
        links = self.links
        self.local = links.keep(self.source(links.c), self.own)
        self.copy = links.send(self.source(1 - links.c), self.from_core, "c")

    def add(self, target, values):
        add_rows_of(target, values, target.shape[0])

    def core_done(self):
        links = self.links
        self.copy.wait_recv()
        self.local.wait()
        for x in range(2):
            for y in range(2):
                self.add(self.own.at[x, y], self.from_core.at[x, y])
        if self.first == "x":
            self.copy = links.send(self.own.at[1 - links.x], self.from_first, "x")
        else:
            self.copy = links.send(self.own.at[:, 1 - links.y], self.from_first, "y")

    def first_done(self):
        links = self.links
        self.copy.wait_recv()
        for other in range(2):
            place = (links.x, other) if self.first == "x" else (other, links.y)
            self.add(self.own.at[place], self.from_first.at[other])
        if self.first == "x":
            self.copy = links.send(self.own.at[links.x, 1 - links.y], self.from_second, "y")
        else:
            self.copy = links.send(self.own.at[1 - links.x, links.y], self.from_second, "x")

    def second_done(self):
        self.copy.wait_recv()
        total = self.own.at[self.links.x, self.links.y]
        self.add(total, self.from_second)
        return total


def sum_space(blocks, rows, columns):
    shape = (rows, columns)
    return [
        pltpu.VMEM((blocks, 2, 2) + shape, jnp.bfloat16),
        pltpu.VMEM((blocks, 2, 2) + shape, jnp.bfloat16),
        pltpu.VMEM((blocks, 2) + shape, jnp.bfloat16),
        pltpu.VMEM((blocks,) + shape, jnp.bfloat16),
    ]


class RingSum:
    def __init__(self, links, parts, total, got, made, pieces=4):
        self.links, self.parts, self.total, self.got, self.made = links, parts, total, got, made
        self.pieces, self.last = pieces, [None] * pieces
        self.rows = parts.shape[1] // pieces

    def step(self, number):
        links = self.links
        for piece in range(self.pieces):
            way = 1 if piece < self.pieces // 2 else -1
            block = links.along(-way * (number + 1))
            where = pl.ds(piece * self.rows, self.rows)
            if number == 0:
                source = self.parts.at[block, where]
            else:
                self.last[piece].wait_recv()
                total = self.got[number - 1, where].astype(jnp.float32) + self.parts[
                    block, where
                ].astype(jnp.float32)
                if number == links.line - 1:
                    self.total[where] = total
                    continue
                self.made[number - 1, where] = total.astype(self.made.dtype)
                source = self.made.at[number - 1, where]
            self.last[piece] = links.send(source, self.got.at[number, where], way)


def ring_space(line, shape):
    return [pltpu.VMEM((line - 1,) + shape, jnp.bfloat16), pltpu.VMEM((line - 2,) + shape, jnp.bfloat16)]


def third_kernel(
    line, cuts, parts_ref, down_ref, total_ref, sum_ref, got, made, *scratch
):
    space, (send_sems, recv_sems) = scratch[:-2], scratch[-2:]
    links = Links(send_sems, recv_sems, line)
    links.meet(["x", "y", "c", 1, line - 1])
    ring = RingSum(links, parts_ref, total_ref, got, made)
    ring.step(0)
    items = []
    for index, (low, high) in enumerate(cuts):
        rows = pl.ds(low, high - low)
        own, core, first, second = space[4 * index : 4 * index + 4]
        items.append(
            NearSum(
                links,
                lambda c, rows=rows: down_ref.at[:, :, c, rows],
                own.at[0],
                core.at[0],
                first.at[0],
                second.at[0],
                "xy"[index % 2],
            )
        )
    for item in items:
        item.start()
    for item in items:
        item.core_done()
    ring.step(1)
    for item in items:
        item.first_done()
    ring.step(2)
    for item, (low, high) in zip(items, cuts):
        sum_ref[low:high] = item.second_done()[...]
    ring.step(3)
    links.finish()


def last_kernel(line, parts_ref, ff_ref, out_ref, qkv_ref, total_ref, ffs_ref, outs_ref, qkvs_ref, got, made, *scratch):
    space, (send_sems, recv_sems) = scratch[:-2], scratch[-2:]
    links = Links(send_sems, recv_sems, line)
    far = [1, line - 1] + list(range(2, line - 1))
    links.meet(["x", "y", "c"] + far)
    ring = RingSum(links, parts_ref, total_ref, got, made)
    ring.step(0)
    items = []
    for kind, (source, target) in enumerate(((ff_ref, ffs_ref), (out_ref, outs_ref), (qkv_ref, qkvs_ref))):
        own, core, first, second = space[4 * kind : 4 * kind + 4]
        for index, k in enumerate(far + [0]):
            item = NearSum(
                links,
                lambda c, source=source, k=k: source.at[links.along(k), :, :, c],
                own.at[index],
                core.at[index],
                first.at[index],
                second.at[index],
                "xy"[index % 2],
            )
            items.append((item, target, k))
    for item, _, _ in items:
        item.start()
    arrived, local = [], []

    def turn(item, target, k):
        total = item.second_done()
        if k == 0:
            local.append(links.keep(total, target.at[links.z]))
        else:
            arrived.append(links.send(total, target.at[links.z], k))

    pairs = [items[index : index + 2] for index in range(0, len(items), 2)]
    for number in range(len(pairs) + 2):
        if number < len(pairs):
            for item in pairs[number]:
                item[0].core_done()
        if 1 <= number < line:
            ring.step(number)
        if 1 <= number <= len(pairs):
            for item in pairs[number - 1]:
                item[0].first_done()
        if number >= 2:
            for item in pairs[number - 2]:
                turn(*item)
    for copy in arrived:
        copy.wait_recv()
    links.finish()
    for copy in local:
        copy.wait()


def turn_kernel(line, rows_ref, columns_ref, send_sems, recv_sems):
    links = Links(send_sems, recv_sems, line)
    far = [1, line - 1] + list(range(2, line - 1))
    links.meet(far)
    columns = columns_ref.shape[2]

    def part(block):
        return rows_ref.at[:, pl.ds(pl.multiple_of(block * columns, columns), columns)]

    local = links.keep(part(links.z), columns_ref.at[links.z])
    for k in far:
        links.send(part(links.along(k)), columns_ref.at[links.z], k)
    for copy in links.sent:
        copy.wait_recv()
    links.finish()
    local.wait()


def link_call(kernel, collective_id, copies, shapes, arguments, spaces=None, scratch=(), vmem=16):
    any_space = pl.BlockSpec(memory_space=pl.ANY)
    near_space = pl.BlockSpec(memory_space=pltpu.VMEM)
    many = isinstance(shapes, tuple)
    if spaces is None:
        spaces = "h" * (len(arguments) + (len(shapes) if many else 1))
    specs = [near_space if space == "v" else any_space for space in spaces]
    return pl.pallas_call(
        kernel,
        out_shape=shapes,
        in_specs=specs[: len(arguments)],
        out_specs=tuple(specs[len(arguments) :]) if many else specs[-1],
        scratch_shapes=list(scratch)
        + [pltpu.SemaphoreType.DMA((copies,)), pltpu.SemaphoreType.DMA((copies,))],
        compiler_params=pltpu.CompilerParams(
            collective_id=collective_id, has_side_effects=True, vmem_limit_bytes=vmem * 2**20
        ),
    )(*arguments)


def forward_call(tokens, table, pack, pack_ff, mixed, line):
    span_len, width = tokens.shape
    group_len = line * span_len
    rows_each = pack_ff.shape[1]
    qkv_cols = pack.shape[2]
    q_cols = qkv_cols - 2 * HD
    f32, bf16 = jnp.float32, jnp.bfloat16
    outs = (
        ((line, span_len, width), bf16),
        ((line, 8) + pack.shape[1:], bf16),
        ((2, 16, width), f32),
        ((group_len, width), bf16),
        ((group_len, q_cols), bf16),
        ((2, group_len, 2 * HD), bf16),
        ((group_len, HD), f32),
        ((2, group_len, HD), f32),
        ((group_len, line * q_cols), bf16),
        ((line, span_len, width), bf16),
        ((line, 8) + pack_ff.shape[1:], bf16),
    )
    return link_call(
        functools.partial(first_kernel, line),
        0,
        176,
        tuple(jax.ShapeDtypeStruct(*out) for out in outs),
        (tokens, table, pack, pack_ff, mixed),
        scratch=[
            pltpu.VMEM((line, span_len, width), bf16),
            pltpu.VMEM((line,) + table.shape, f32),
            pltpu.VMEM((line, 8) + pack.shape[1:], bf16),
            pltpu.VMEM((2, 16, width), f32),
            pltpu.VMEM((group_len, width), bf16),
            pltpu.VMEM((2, group_len, HD), f32),
            pltpu.VMEM((group_len, qkv_cols), f32),
            pltpu.VMEM((group_len, q_cols), bf16),
            pltpu.VMEM((2, group_len, 2 * HD), bf16),
            pltpu.VMEM((group_len, HD), f32),
            pltpu.VMEM((group_len, q_cols), bf16),
        ],
        vmem=48,
    )


def third_sum(parts, grad_down, line):
    shape = parts.shape[1:]
    rows, columns = grad_down.shape[3:]
    half = (rows // 2 + 15) // 16 * 16
    cuts = ((0, half), (half, rows))
    return link_call(
        functools.partial(third_kernel, line, cuts),
        2,
        64,
        (jax.ShapeDtypeStruct(shape, jnp.float32), jax.ShapeDtypeStruct((rows, columns), jnp.bfloat16)),
        (parts, grad_down),
        "vhvv",
        ring_space(line, shape) + sum((sum_space(1, high - low, columns) for low, high in cuts), []),
        vmem=40,
    )


def last_sum(parts, grad_ff, grad_out, grad_qkv, line):
    shape = parts.shape[1:]
    grads = (grad_ff, grad_out, grad_qkv)
    return link_call(
        functools.partial(last_kernel, line),
        4,
        96,
        (jax.ShapeDtypeStruct(shape, jnp.float32),)
        + tuple(jax.ShapeDtypeStruct((line,) + grad.shape[4:], grad.dtype) for grad in grads),
        (parts,) + grads,
        "vhhhvhhh",
        ring_space(line, shape) + sum((sum_space(line, *grad.shape[4:]) for grad in grads), []),
        vmem=58,
    )


def turn_rows(values, line):
    return link_call(
        functools.partial(turn_kernel, line),
        3,
        line,
        jax.ShapeDtypeStruct((line, values.shape[0], values.shape[1] // line), values.dtype),
        (values,),
    )


def general_body(
    tokens,
    attn_gain,
    w_query,
    w_key,
    w_value,
    w_out,
    mlp_gain,
    w_gate,
    w_up,
    w_down,
    keep_mask,
    group_ids,
    positions,
    exit_scale,
    out_grad,
):
    seq_count, span_len, model_width = tokens.shape
    kv_heads = KVH
    head_dim = HD
    head_count = HEADS
    group_size = head_count // kv_heads
    row_count = seq_count * span_len
    stripe = group_size * span_len
    wide_count = lax.axis_size("wide")
    wide_place = lax.axis_index("wide")
    full_len = span_len * wide_count
    score_scale = 1.0 / math.sqrt(head_dim)
    gain_one, query_w, key_w, value_w, out_w = (
        lax.all_gather(attn_gain, ("wide", "narrow"), axis=0, tiled=True),
        lax.all_gather(w_query, ("wide", "narrow"), axis=0, tiled=True),
        lax.all_gather(w_key, ("wide", "narrow"), axis=0, tiled=True),
        lax.all_gather(w_value, ("wide", "narrow"), axis=0, tiled=True),
        lax.all_gather(w_out, ("wide", "narrow"), axis=0, tiled=True),
    )
    inputs = tokens.astype(jnp.float32).reshape(row_count, model_width)
    token_pos = positions.reshape(row_count)
    keep_rows = jnp.repeat(keep_mask.astype(jnp.float32), span_len)[:, None]
    inverse_one = lax.rsqrt(jnp.mean(inputs * inputs, axis=-1, keepdims=True) + epsilon)
    first_norm = (inputs * inverse_one * gain_one.astype(jnp.float32)).astype(jnp.bfloat16)
    query_pre = jnp.dot(first_norm, query_w, preferred_element_type=jnp.float32).reshape(
        row_count, head_count, head_dim
    )
    key_pre = jnp.dot(first_norm, key_w, preferred_element_type=jnp.float32).reshape(
        row_count, kv_heads, head_dim
    )
    query_rows = rotate(query_pre, token_pos, 1.0).astype(jnp.bfloat16)
    key_heads = (
        rotate(key_pre, token_pos, 1.0)
        .astype(jnp.bfloat16)
        .reshape(seq_count, span_len, kv_heads * head_dim)
    )
    value_heads = (
        jnp.dot(first_norm, value_w, preferred_element_type=jnp.float32)
        .astype(jnp.bfloat16)
        .reshape(seq_count, span_len, kv_heads * head_dim)
    )
    queries = (
        query_rows.reshape(seq_count, span_len, kv_heads, group_size, head_dim)
        .transpose(0, 2, 3, 1, 4)
        .reshape(seq_count, kv_heads, stripe, head_dim)
    )
    query_index = wide_place * span_len + jnp.arange(stripe, dtype=jnp.int32) % span_len
    last_query = wide_place * span_len + span_len - 1

    def block_scores(key_block, key_first):
        scores = (
            jnp.einsum("skrd,sjkd->skrj", queries, key_block, preferred_element_type=jnp.float32)
            * score_scale
        )
        key_index = key_first + jnp.arange(key_block.shape[1], dtype=jnp.int32)
        allowed = key_index[None, :] <= query_index[:, None]
        return (scores, allowed)

    start_forward = (
        jnp.full((seq_count, kv_heads, stripe), -1e30, jnp.float32),
        jnp.zeros((seq_count, kv_heads, stripe), jnp.float32),
        jnp.zeros((seq_count, kv_heads, stripe, head_dim), jnp.float32),
    )
    running = start_forward
    pieces = (
        lax.all_gather(key_heads, "wide", axis=1, tiled=True),
        lax.all_gather(value_heads, "wide", axis=1, tiled=True),
    )
    key_blocks = split_blocks(pieces[0], seq_count, kv_heads, head_dim)
    value_blocks = split_blocks(pieces[1], seq_count, kv_heads, head_dim)
    block_len = key_blocks.shape[2]

    def advance(carried, block_item):
        key_block, value_block, block_index = block_item
        key_first = block_index * block_len

        def compute_block(current):
            run_max, run_sum, run_acc = current
            scores, allowed = block_scores(key_block, key_first)
            scores = jnp.where(allowed, scores, -1e30)
            new_max = jnp.maximum(run_max, jnp.max(scores, axis=-1))
            factor = jnp.exp(run_max - new_max)
            weights = jnp.where(allowed, jnp.exp(scores - new_max[..., None]), 0.0)
            new_sum = run_sum * factor + jnp.sum(weights, axis=-1)
            new_acc = run_acc * factor[..., None] + jnp.einsum(
                "skrj,sjkd->skrd",
                weights.astype(jnp.bfloat16),
                value_block,
                preferred_element_type=jnp.float32,
            )
            return (new_max, new_sum, new_acc)

        return (lax.cond(key_first <= last_query, compute_block, unchanged, carried), None)

    running, _ = lax.scan(
        advance,
        running,
        (key_blocks, value_blocks, jnp.arange(key_blocks.shape[0], dtype=jnp.int32)),
    )
    run_max, run_sum, run_acc = running
    attended = run_acc / run_sum[..., None]
    log_total = run_max + jnp.log(run_sum)
    attended_rows = (
        attended.reshape(seq_count, kv_heads, group_size, span_len, head_dim)
        .transpose(0, 3, 1, 2, 4)
        .reshape(row_count, head_count * head_dim)
        .astype(jnp.bfloat16)
    )
    middle = inputs + keep_rows * jnp.dot(attended_rows, out_w, preferred_element_type=jnp.float32)
    gain_two, gate_w, up_w, down_w = (
        lax.all_gather(mlp_gain, ("wide", "narrow"), axis=0, tiled=True),
        lax.all_gather(w_gate, ("wide", "narrow"), axis=0, tiled=True),
        lax.all_gather(w_up, ("wide", "narrow"), axis=0, tiled=True),
        lax.all_gather(w_down, ("wide", "narrow"), axis=0, tiled=True),
    )
    inverse_two = lax.rsqrt(jnp.mean(middle * middle, axis=-1, keepdims=True) + epsilon)
    second_norm = (middle * inverse_two * gain_two.astype(jnp.float32)).astype(jnp.bfloat16)
    gate_value = jnp.dot(second_norm, gate_w, preferred_element_type=jnp.float32)
    up_value = jnp.dot(second_norm, up_w, preferred_element_type=jnp.float32)
    gate_sigmoid = jax.nn.sigmoid(gate_value)
    swish_value = gate_value * gate_sigmoid
    hidden = (swish_value * up_value).astype(jnp.bfloat16)
    output = (
        middle + keep_rows * jnp.dot(hidden, down_w, preferred_element_type=jnp.float32)
    ).astype(jnp.bfloat16)
    group_match = (
        group_ids.reshape(row_count)[:, None]
        == jnp.arange(exit_scale.shape[0], dtype=jnp.int32)[None, :]
    )
    token_scale = jnp.sum(jnp.where(group_match, exit_scale[None, :], 0.0), axis=1, keepdims=True)
    upstream = out_grad.astype(jnp.float32).reshape(row_count, model_width) * token_scale
    gain_two, gate_w, up_w, down_w = (
        lax.all_gather(mlp_gain, ("wide", "narrow"), axis=0, tiled=True),
        lax.all_gather(w_gate, ("wide", "narrow"), axis=0, tiled=True),
        lax.all_gather(w_up, ("wide", "narrow"), axis=0, tiled=True),
        lax.all_gather(w_down, ("wide", "narrow"), axis=0, tiled=True),
    )
    mixed_grad = (keep_rows * upstream).astype(jnp.bfloat16)
    grad_down = over_rows(hidden, mixed_grad)
    hidden_grad = against(mixed_grad, down_w)
    gate_grad = (
        hidden_grad * up_value * gate_sigmoid * (1.0 + gate_value * (1.0 - gate_sigmoid))
    ).astype(jnp.bfloat16)
    up_grad = (hidden_grad * swish_value).astype(jnp.bfloat16)
    grad_gate = over_rows(second_norm, gate_grad)
    grad_up = over_rows(second_norm, up_grad)
    norm_grad = against(gate_grad, gate_w) + against(up_grad, up_w)
    grad_gain_two = jnp.sum(norm_grad * middle * inverse_two, axis=0)
    scaled_two = gain_two.astype(jnp.float32) * norm_grad
    middle_grad = (
        upstream
        + inverse_two * scaled_two
        - middle
        * (inverse_two * inverse_two * inverse_two)
        * jnp.mean(scaled_two * middle, axis=-1, keepdims=True)
    )
    gain_two_share, gate_share, up_share, down_share = (
        lax.psum_scatter(grad_gain_two, ("wide", "narrow"), scatter_dimension=0, tiled=True),
        lax.psum_scatter(grad_gate, ("wide", "narrow"), scatter_dimension=0, tiled=True),
        lax.psum_scatter(grad_up, ("wide", "narrow"), scatter_dimension=0, tiled=True),
        lax.psum_scatter(grad_down, ("wide", "narrow"), scatter_dimension=0, tiled=True),
    )
    gain_one, query_w, key_w, value_w, out_w = (
        lax.all_gather(attn_gain, ("wide", "narrow"), axis=0, tiled=True),
        lax.all_gather(w_query, ("wide", "narrow"), axis=0, tiled=True),
        lax.all_gather(w_key, ("wide", "narrow"), axis=0, tiled=True),
        lax.all_gather(w_value, ("wide", "narrow"), axis=0, tiled=True),
        lax.all_gather(w_out, ("wide", "narrow"), axis=0, tiled=True),
    )
    branch_grad = (keep_rows * middle_grad).astype(jnp.bfloat16)
    grad_out = over_rows(attended_rows, branch_grad)
    attended_grad = against(branch_grad, out_w).astype(jnp.bfloat16)
    grouped_grad = (
        attended_grad.reshape(seq_count, span_len, kv_heads, group_size, head_dim)
        .transpose(0, 2, 3, 1, 4)
        .reshape(seq_count, kv_heads, stripe, head_dim)
    )
    row_delta = jnp.sum(grouped_grad.astype(jnp.float32) * attended, axis=-1)
    start_backward = (
        jnp.zeros((seq_count, kv_heads, stripe, head_dim), jnp.float32),
        jnp.zeros((seq_count, full_len, kv_heads * head_dim), jnp.float32),
        jnp.zeros((seq_count, full_len, kv_heads * head_dim), jnp.float32),
    )
    running = start_backward
    pieces = (
        lax.all_gather(key_heads, "wide", axis=1, tiled=True),
        lax.all_gather(value_heads, "wide", axis=1, tiled=True),
    )
    key_blocks = split_blocks(pieces[0], seq_count, kv_heads, head_dim)
    value_blocks = split_blocks(pieces[1], seq_count, kv_heads, head_dim)
    fold_block_len = key_blocks.shape[2]

    def advance(carried, block_item):
        key_block, value_block, block_index = block_item
        key_first = block_index * fold_block_len

        def compute_block(current):
            query_acc, key_acc, value_acc = current
            scores, allowed = block_scores(key_block, key_first)
            probabilities = jnp.where(allowed, jnp.exp(scores - log_total[..., None]), 0.0)
            value_part = jnp.einsum(
                "skrj,skrd->sjkd",
                probabilities.astype(jnp.bfloat16),
                grouped_grad,
                preferred_element_type=jnp.float32,
            )
            prob_grad = jnp.einsum(
                "skrd,sjkd->skrj", grouped_grad, value_block, preferred_element_type=jnp.float32
            )
            score_grad = (probabilities * (prob_grad - row_delta[..., None])).astype(jnp.bfloat16)
            query_acc = (
                query_acc
                + jnp.einsum(
                    "skrj,sjkd->skrd", score_grad, key_block, preferred_element_type=jnp.float32
                )
                * score_scale
            )
            key_part = (
                jnp.einsum(
                    "skrj,skrd->sjkd", score_grad, queries, preferred_element_type=jnp.float32
                )
                * score_scale
            )
            key_acc = add_rows(
                key_acc, key_part.reshape(seq_count, fold_block_len, kv_heads * head_dim), key_first
            )
            value_acc = add_rows(
                value_acc,
                value_part.reshape(seq_count, fold_block_len, kv_heads * head_dim),
                key_first,
            )
            return (query_acc, key_acc, value_acc)

        return (lax.cond(key_first <= last_query, compute_block, unchanged, carried), None)

    running, _ = lax.scan(
        advance,
        running,
        (key_blocks, value_blocks, jnp.arange(key_blocks.shape[0], dtype=jnp.int32)),
    )
    query_acc, key_acc, value_acc = running
    key_sum, value_sum = (
        lax.psum_scatter(
            key_acc.astype(jnp.bfloat16), "wide", scatter_dimension=1, tiled=True
        ).astype(jnp.float32),
        lax.psum_scatter(
            value_acc.astype(jnp.bfloat16), "wide", scatter_dimension=1, tiled=True
        ).astype(jnp.float32),
    )
    query_back = (
        query_acc.reshape(seq_count, kv_heads, group_size, span_len, head_dim)
        .transpose(0, 3, 1, 2, 4)
        .reshape(row_count, head_count, head_dim)
    )
    query_grad = (
        rotate(query_back, token_pos, -1.0)
        .reshape(row_count, head_count * head_dim)
        .astype(jnp.bfloat16)
    )
    key_grad = (
        rotate(key_sum.reshape(row_count, kv_heads, head_dim), token_pos, -1.0)
        .reshape(row_count, kv_heads * head_dim)
        .astype(jnp.bfloat16)
    )
    value_grad = value_sum.reshape(row_count, kv_heads * head_dim).astype(jnp.bfloat16)
    grad_query = over_rows(first_norm, query_grad)
    grad_key = over_rows(first_norm, key_grad)
    grad_value = over_rows(first_norm, value_grad)
    input_norm_grad = (
        against(query_grad, query_w) + against(key_grad, key_w) + against(value_grad, value_w)
    )
    grad_gain_one = jnp.sum(input_norm_grad * inputs * inverse_one, axis=0)
    scaled_one = gain_one.astype(jnp.float32) * input_norm_grad
    input_grad = (
        middle_grad
        + inverse_one * scaled_one
        - inputs
        * (inverse_one * inverse_one * inverse_one)
        * jnp.mean(scaled_one * inputs, axis=-1, keepdims=True)
    )
    gain_one_share, query_share, key_share, value_share, out_share = (
        lax.psum_scatter(grad_gain_one, ("wide", "narrow"), scatter_dimension=0, tiled=True),
        lax.psum_scatter(grad_query, ("wide", "narrow"), scatter_dimension=0, tiled=True),
        lax.psum_scatter(grad_key, ("wide", "narrow"), scatter_dimension=0, tiled=True),
        lax.psum_scatter(grad_value, ("wide", "narrow"), scatter_dimension=0, tiled=True),
        lax.psum_scatter(grad_out, ("wide", "narrow"), scatter_dimension=0, tiled=True),
    )
    return (
        output.reshape(seq_count, span_len, model_width),
        input_grad.astype(jnp.bfloat16).reshape(seq_count, span_len, model_width),
        gain_one_share,
        query_share,
        key_share,
        value_share,
        out_share,
        gain_two_share,
        gate_share,
        up_share,
        down_share,
    )


def line_body(
    tokens,
    attn_gain,
    w_query,
    w_key,
    w_value,
    w_out,
    mlp_gain,
    w_gate,
    w_up,
    w_down,
    keep_mask,
    group_ids,
    positions,
    exit_scale,
    out_grad,
):
    f32 = jnp.float32
    bf16 = jnp.bfloat16
    _, span_len, model_width = tokens.shape
    line = lax.axis_size("z")
    place = lax.axis_index("z")
    side = lax.axis_index("x")
    near = lax.axis_size("x") * lax.axis_size("y") * lax.axis_size("c")
    rows_each = w_query.shape[0]
    heads = HEADS // line
    q_cols = heads * HD
    ff_cols = w_gate.shape[1] // line
    group_len = span_len * line
    score_scale = 1.0 / math.sqrt(HD)

    def shift(values, axis, step):
        size = lax.axis_size(axis)
        return lax.ppermute(values, axis, [(i, (i + step) % size) for i in range(size)])

    def after(values, first):
        return lax.optimization_barrier((values, first))[0]

    def pick(values, index, dim):
        return lax.dynamic_index_in_dim(values, index, dim, keepdims=False)

    def by_columns(weight, columns):
        return weight.reshape(rows_each, line, columns).transpose(1, 0, 2)

    out_w = lax.all_gather(w_out, ("z", "x", "y", "c"), axis=0, tiled=True)
    down_w = lax.all_gather(w_down, ("x", "y", "c"), axis=0, tiled=True)
    own_x = tokens[0].astype(f32)
    keep = keep_mask[0].astype(f32)
    group_match = group_ids[0][:, None] == jnp.arange(exit_scale.shape[0], dtype=jnp.int32)[None, :]
    token_scale = jnp.sum(jnp.where(group_match, exit_scale[None, :], 0.0), axis=1, keepdims=True)
    upstream = out_grad[0].astype(f32) * token_scale

    core = lax.axis_index("c")
    gain_row = jnp.zeros((q_cols + 2 * HD,), bf16)
    gain_row = lax.dynamic_update_slice_in_dim(gain_row, attn_gain, core * rows_each, 0)
    gain_row = lax.dynamic_update_slice_in_dim(gain_row, mlp_gain, HD + core * rows_each, 0)
    gain_rows = jnp.broadcast_to(gain_row, (line, 16, gain_row.shape[0]))
    pack_attn = jnp.concatenate(
        [by_columns(w_query, q_cols), by_columns(w_key, HD), by_columns(w_value, HD)], axis=2
    )
    pack_attn = jnp.concatenate([pack_attn, gain_rows], axis=1)
    pack_ff = jnp.concatenate([by_columns(w_gate, ff_cols), by_columns(w_up, ff_cols)], axis=2)
    freqs = 10000.0 ** (-2.0 * jnp.arange(HD // 2, dtype=f32) / HD)
    angles = positions[0].astype(f32)[:, None] * freqs[None, :]
    table = jnp.concatenate([jnp.cos(angles), jnp.sin(angles)], axis=1)
    (
        x_blocks,
        near_w,
        gain_all,
        first_norm,
        queries,
        both_kv,
        log_total,
        turns,
        attended_rows,
        mixed_grad,
        ff_w,
    ) = forward_call(tokens[0], table, pack_attn, pack_ff, (keep * upstream).astype(bf16), line)
    inputs = x_blocks.reshape(group_len, model_width).astype(f32)
    qkv_w = near_w[:, :, :rows_each].reshape(model_width, q_cols + 2 * HD)
    gain_one, gain_two = gain_all[0, :1], gain_all[1, :1]
    mixed_grad = mixed_grad.reshape(group_len, model_width)
    ff_w = ff_w.reshape(model_width, 2 * ff_cols)
    queries = queries.reshape(group_len, heads, HD)
    both_kv = both_kv.reshape(2 * group_len, 2 * HD)
    keys = both_kv[:, :HD]
    values = both_kv[:, HD:]

    def own_rows(values):
        return lax.dynamic_slice_in_dim(values, place * span_len, span_len, 0)

    branch = jnp.dot(attended_rows, out_w, preferred_element_type=f32)
    middle_all = inputs + keep * branch
    inverse_mid = lax.rsqrt(jnp.mean(middle_all * middle_all, axis=-1, keepdims=True) + epsilon)
    second_norm = (middle_all * inverse_mid * gain_two).astype(bf16)
    middle = own_rows(middle_all)
    inverse_two = own_rows(inverse_mid)

    gate_up = jnp.dot(second_norm, ff_w, preferred_element_type=f32)
    gate_value = gate_up[:, :ff_cols]
    up_value = gate_up[:, ff_cols:]
    gate_sigmoid = jax.nn.sigmoid(gate_value)
    swish_value = gate_value * gate_sigmoid
    hidden = (swish_value * up_value).astype(bf16)
    hidden_grad = against(mixed_grad, down_w)
    gate_grad = hidden_grad * up_value * gate_sigmoid * (1.0 + gate_value * (1.0 - gate_sigmoid))
    up_grad = hidden_grad * swish_value
    both_grad = jnp.concatenate([gate_grad, up_grad], axis=1).astype(bf16)

    def split(values):
        return values.astype(bf16).reshape(line, span_len, model_width)

    grad_down = over_rows(hidden, mixed_grad).astype(bf16).reshape(2, 2, 2, -1, model_width)
    norm_grad, grad_down = third_sum(split(against(both_grad, ff_w)), grad_down, line)
    grad_down = grad_down.astype(f32)
    grad_ff = over_rows(second_norm, after(both_grad, norm_grad)).astype(bf16)
    scaled_two = gain_two * norm_grad
    middle_grad = (
        upstream
        + inverse_two * scaled_two
        - middle
        * (inverse_two * inverse_two * inverse_two)
        * jnp.mean(scaled_two * middle, axis=-1, keepdims=True)
    )
    branch_grad = (keep * middle_grad).astype(bf16)
    own_grad = against(branch_grad, out_w).astype(bf16)
    attended_grad = turn_rows(own_grad, line).reshape(group_len, heads, HD)
    mixed_parts = split(jnp.dot(hidden, after(down_w, norm_grad), preferred_element_type=f32))

    def mixed_hop(total, hop, first):
        total = after(shift(total.astype(bf16), "z", 1), first).astype(f32)
        return total + pick(mixed_parts, (place - 1 - hop) % line, 0).astype(f32)

    mixed = mixed_hop(pick(mixed_parts, (place - 1) % line, 0), 1, attended_grad)
    inside = jnp.arange(span_len, dtype=jnp.int32)
    block_first = jnp.arange(line, dtype=jnp.int32) * (2 * span_len)

    def token_index(which):
        return (block_first[:, None] + which * span_len + inside[None, :]).reshape(group_len)

    query_index = token_index(side)
    key_index = jnp.concatenate([query_index, token_index(1 - side)])
    allowed = key_index[None, :] <= query_index[:, None]
    scores = jnp.einsum("tgd,jd->gtj", queries, keys, preferred_element_type=f32) * score_scale
    probabilities = jnp.where(allowed, jnp.exp(scores - log_total[:, :heads].T[..., None]), 0.0)
    rounded_probs = probabilities.astype(bf16)
    prob_grad = jnp.einsum("tgd,jd->gtj", attended_grad, values, preferred_element_type=f32)
    own_attended = lax.dynamic_slice_in_dim(attended_rows, place * q_cols, q_cols, 1)
    attended = own_attended.reshape(group_len, heads, HD).astype(f32)
    delta = jnp.sum(attended_grad.astype(f32) * attended, axis=-1).T[..., None]
    score_grad = (probabilities * (prob_grad - delta)).astype(bf16)
    for hop in range(2, line - 1):
        mixed = mixed_hop(mixed, hop, score_grad)
    query_back = jnp.einsum("gtj,jd->tgd", score_grad, keys, preferred_element_type=f32) * score_scale
    key_back = jnp.einsum("gtj,tgd->jd", score_grad, queries, preferred_element_type=f32) * score_scale
    value_back = jnp.einsum("gtj,tgd->jd", rounded_probs, attended_grad, preferred_element_type=f32)
    kv_back = jnp.concatenate([key_back, value_back], axis=1)
    kv_back = kv_back[:group_len] + shift(kv_back[group_len:].astype(bf16), "x", 1).astype(f32)

    def turn_back(vectors):
        swapped = jnp.concatenate([vectors[..., HD // 2 :], vectors[..., : HD // 2]], axis=-1)
        return vectors * turns[0][:, None] - swapped * turns[1][:, None]

    qkv_grad = jnp.concatenate(
        [
            turn_back(query_back).reshape(group_len, q_cols),
            turn_back(kv_back[:, None, :HD])[:, 0],
            kv_back[:, HD:],
        ],
        axis=1,
    ).astype(bf16)
    grad_out = over_rows(own_rows(attended_rows), branch_grad).astype(bf16)
    grad_qkv = over_rows(first_norm, qkv_grad).astype(bf16)

    def by_place(grad):
        return grad.reshape(line, 2, 2, 2, rows_each, grad.shape[1])

    input_norm_grad, ff_back, out_back, qkv_back = last_sum(
        split(against(qkv_grad, qkv_w)), by_place(grad_ff), by_place(grad_out), by_place(grad_qkv), line
    )
    mixed = mixed_hop(mixed, line - 1, input_norm_grad)
    output = (middle + keep * mixed).astype(bf16)
    ff_back = ff_back.astype(f32)
    qkv_back = qkv_back.astype(f32)
    grad_out = jnp.sum(out_back.astype(f32), axis=0)
    inverse_one = lax.rsqrt(jnp.mean(own_x * own_x, axis=-1, keepdims=True) + epsilon)
    scaled_one = gain_one * input_norm_grad
    input_grad = (
        middle_grad
        + inverse_one * scaled_one
        - own_x
        * (inverse_one * inverse_one * inverse_one)
        * jnp.mean(scaled_one * own_x, axis=-1, keepdims=True)
    )

    def side_by_side(blocks):
        return blocks.transpose(1, 0, 2).reshape(rows_each, -1)

    grad_query = side_by_side(qkv_back[:, :, :q_cols])
    grad_key = side_by_side(qkv_back[:, :, q_cols : q_cols + HD])
    grad_value = side_by_side(qkv_back[:, :, q_cols + HD :])
    grad_gate = side_by_side(ff_back[:, :, :ff_cols])
    grad_up = side_by_side(ff_back[:, :, ff_cols:])

    def gain_grad(pairs, gain):
        total = sum(jnp.sum(weight.astype(f32) * grad, axis=1) for weight, grad in pairs)
        return total / gain.astype(f32)

    return (
        output[None],
        input_grad.astype(bf16)[None],
        gain_grad([(w_query, grad_query), (w_key, grad_key), (w_value, grad_value)], attn_gain),
        grad_query,
        grad_key,
        grad_value,
        grad_out,
        gain_grad([(w_gate, grad_gate), (w_up, grad_up)], mlp_gain),
        grad_gate,
        grad_up,
        grad_down,
    )


def solution(mesh):
    wide, narrow = mesh.shape["wide"], mesh.shape["narrow"]
    if wide == 2 * KVH and narrow == 4:
        mesh = Mesh(mesh.devices.reshape(wide // 2, 2, 2, 2), ("z", "x", "y", "c"))
        body, wide, narrow = line_body, ("z", "x"), ("y", "c")
    else:
        body, wide, narrow = general_body, ("wide",), ("narrow",)
    token_spec = P(narrow, wide, None)
    id_spec = P(narrow, wide)
    gain_spec = P(wide + narrow)
    weight_spec = P(wide + narrow, None)
    return jax.shard_map(
        body,
        mesh=mesh,
        in_specs=(
            token_spec,
            gain_spec,
            weight_spec,
            weight_spec,
            weight_spec,
            weight_spec,
            gain_spec,
            weight_spec,
            weight_spec,
            weight_spec,
            P(narrow),
            id_spec,
            id_spec,
            P(),
            token_spec,
        ),
        out_specs=(
            token_spec,
            token_spec,
            gain_spec,
            weight_spec,
            weight_spec,
            weight_spec,
            weight_spec,
            gain_spec,
            weight_spec,
            weight_spec,
            weight_spec,
        ),
        check_vma=False,
    )
```

```python
import functools
import math

import jax
import jax.numpy as jnp
from jax import lax
from jax.experimental import pallas as pl
from jax.experimental.pallas import tpu as pltpu
from jax.sharding import Mesh
from jax.sharding import PartitionSpec as P

HEADS = 16
KVH = 4
HD = 128


epsilon = 1e-05


def rotate(vectors, token_pos, direction):
    half_size = vectors.shape[-1] // 2
    freqs = 10000.0 ** (-2.0 * jnp.arange(half_size, dtype=jnp.float32) / vectors.shape[-1])
    angles = token_pos.astype(jnp.float32)[:, None] * freqs[None, :]
    cosine = jnp.cos(angles)[:, None, :]
    sine = direction * jnp.sin(angles)[:, None, :]
    first_half = vectors[..., :half_size]
    second_half = vectors[..., half_size:]
    return jnp.concatenate(
        [first_half * cosine - second_half * sine, second_half * cosine + first_half * sine],
        axis=-1,
    )


def split_blocks(piece_arr, seq_count, kv_heads, head_dim):
    piece_len = piece_arr.shape[1]
    block_len = math.gcd(piece_len, 512)
    shaped = piece_arr.reshape(seq_count, piece_len // block_len, block_len, kv_heads, head_dim)
    return shaped.transpose(1, 0, 2, 3, 4)


def add_rows(whole_arr, update, first_row):
    current = lax.dynamic_slice_in_dim(whole_arr, first_row, update.shape[1], 1)
    return lax.dynamic_update_slice_in_dim(whole_arr, current + update, first_row, 1)


def over_rows(left, right):
    return lax.dot_general(
        left, right, (((0,), (0,)), ((), ())), preferred_element_type=jnp.float32
    )


def against(left, right):
    return lax.dot_general(
        left, right, (((1,), (1,)), ((), ())), preferred_element_type=jnp.float32
    )


def unchanged(carried):
    return carried


MESH = pl.DeviceIdType.MESH
AXES = ("z", "x", "y", "c")


class Links:
    def __init__(self, send_sems, recv_sems, line):
        self.send_sems, self.recv_sems, self.line = send_sems, recv_sems, line
        self.z, self.x, self.y, self.c = (lax.axis_index(name) for name in AXES)
        self.slot = self.x * 4 + self.y * 2 + self.c
        self.used = 0
        self.sent = []

    def device(self, to):
        if to == "x":
            return (self.z, 1 - self.x, self.y, self.c)
        if to == "y":
            return (self.z, self.x, 1 - self.y, self.c)
        if to == "c":
            return (self.z, self.x, self.y, 1 - self.c)
        return (self.along(to), self.x, self.y, self.c)

    def along(self, step):
        return lax.rem(self.z + step + self.line, self.line)

    def other(self, to):
        slot = self.slot
        for name in to:
            bit = {"x": 4, "y": 2, "c": 1}[name]
            here = {"x": self.x, "y": self.y, "c": self.c}[name]
            slot = slot + bit * (1 - 2 * here)
        return slot

    def meet(self, targets):
        barrier = pltpu.get_barrier_semaphore()
        for to in targets:
            pl.semaphore_signal(barrier, inc=1, device_id=self.device(to), device_id_type=MESH)
        pl.semaphore_wait(barrier, len(targets))

    def send(self, source, target, to):
        copy = pltpu.make_async_remote_copy(
            src_ref=source,
            dst_ref=target,
            send_sem=self.send_sems.at[self.used],
            recv_sem=self.recv_sems.at[self.used],
            device_id=self.device(to),
            device_id_type=MESH,
        )
        copy.start()
        self.used += 1
        self.sent.append(copy)
        return copy

    def keep(self, source, target):
        copy = pltpu.make_async_copy(source, target, self.send_sems.at[self.used])
        copy.start()
        self.used += 1
        return copy

    def finish(self):
        for copy in self.sent:
            copy.wait_send()


class NearGather:
    def __init__(self, links, slot):
        self.links, self.slot = links, slot
        self.got = {}

    def offer(self, block, source):
        target = self.slot(block, self.links.slot)
        for to in ("x", "y", "c"):
            self.got[block, to] = self.links.send(source, target, to)

    def relay(self, block, first):
        links = self.links
        for to, then in (("x", "y"), ("y", "x")):
            self.got[block, to].wait_recv()
            place = self.slot(block, links.other(to))
            self.got[block, to + "c"] = links.send(place, place, "c")
            if to == first:
                self.got[block, "xy"] = links.send(place, place, then)

    def close(self, block):
        self.got[block, "xy"].wait_recv()
        place = self.slot(block, self.links.other("xy"))
        self.got[block, "xyc"] = self.links.send(place, place, "c")

    def wait(self, blocks):
        for block in blocks:
            for to in ("c", "xc", "yc", "xyc"):
                self.got[block, to].wait_recv()


class RingGather:
    def __init__(self, links, source, place, pieces=4):
        self.links, self.source, self.place, self.pieces = links, source, place, pieces
        self.rows = source.shape[0] // pieces
        self.last = [None] * pieces

    def step(self, number):
        for piece in range(self.pieces):
            way = 1 if piece < self.pieces // 2 else -1
            rows = pl.ds(piece * self.rows, self.rows)
            place = self.place(self.links.along(-way * number), rows)
            if number > 0:
                self.last[piece].wait_recv()
            if number < self.links.line - 1:
                origin = self.source.at[rows] if number == 0 else place
                self.last[piece] = self.links.send(origin, place, way)


def first_kernel(
    line,
    x_ref,
    table_ref,
    pack_ref,
    ff_ref,
    mix_ref,
    xs_ref,
    weight_ref,
    gain_ref,
    norm_ref,
    query_ref,
    kv_ref,
    peak_ref,
    turn_ref,
    atts_ref,
    mixs_ref,
    ffs_ref,
    x_all,
    tables,
    weights,
    gains,
    norm,
    turns,
    flat,
    query,
    kv,
    peak,
    att,
    send_sems,
    recv_sems,
):
    f32, bf16 = jnp.float32, jnp.bfloat16
    links = Links(send_sems, recv_sems, line)
    far = [1, line - 1] + list(range(2, line - 1))
    links.meet(["x", "y", "c"] + far)
    here = links.slot
    span_len, width = x_ref.shape
    group_len = line * span_len
    rows_each = ff_ref.shape[1]
    q_cols = query.shape[1]
    heads = q_cols // HD
    local = []

    near = NearGather(links, lambda block, place: weights.at[links.along(-block), place])
    far_ff = NearGather(links, lambda block, place: ffs_ref.at[links.along(-block), place])
    ring = RingGather(links, x_ref, lambda block, rows: x_all.at[block, rows])
    own = [
        links.keep(x_ref, x_all.at[links.z]),
        links.keep(table_ref, tables.at[links.z]),
        links.keep(pack_ref.at[links.z], weights.at[links.z, here]),
    ]
    turned = {k: links.send(pack_ref.at[links.along(k)], weights.at[links.z, here], k) for k in far}
    placed = [links.send(table_ref, tables.at[links.z], k) for k in far]
    ring.step(0)
    near.offer(0, pack_ref.at[links.z])
    local.append(links.keep(ff_ref.at[links.z], ffs_ref.at[links.z, here]))
    local.append(links.keep(mix_ref, mixs_ref.at[links.z]))
    for k in far:
        turned[k].wait_recv()
        near.offer(k, weights.at[links.along(-k), here])
    ring.step(1)
    for k in [0] + far:
        near.relay(k, "x" if k < line // 2 else "y")
    far_ff.offer(0, ff_ref.at[links.z])
    ring.step(2)
    turned_ff = {k: links.send(ff_ref.at[links.along(k)], ffs_ref.at[links.z, here], k) for k in far}
    for k in [0] + far:
        near.close(k)
    for copy in own:
        copy.wait()
    for copy in placed:
        copy.wait_recv()

    lane = lax.broadcasted_iota(jnp.int32, (span_len, HD), 1)
    for block in range(line):
        table = tables[block]
        swapped = pltpu.roll(table, HD // 2, 1)
        rows = slice(block * span_len, (block + 1) * span_len)
        turns[0, rows] = jnp.where(lane < HD // 2, table, swapped)
        turns[1, rows] = jnp.where(lane < HD // 2, -swapped, table)
    local.append(links.keep(turns, turn_ref))
    near.wait(range(line))
    for index in range(line * 4):
        z, q = divmod(index, 4)
        for which in range(2):
            lanes = slice(which * HD, (which + 1) * HD)
            both = [weights[z, 2 * q + c, rows_each : rows_each + 16, lanes].astype(f32) for c in range(2)]
            gains[which, :, index * HD : (index + 1) * HD] = both[0] + both[1]
    local.append(links.keep(weights, weight_ref))
    local.append(links.keep(gains, gain_ref))
    ring.step(3)
    local.append(links.keep(x_all, xs_ref))

    def normalise(index, carry):
        block = index // (span_len // 16)
        rows = pl.ds(pl.multiple_of(lax.rem(index, span_len // 16) * 16, 16), 16)
        values = x_all[block, rows].astype(f32)
        inverse = lax.rsqrt(jnp.mean(values * values, axis=-1, keepdims=True) + epsilon)
        target = pl.ds(pl.multiple_of(index * 16, 16), 16)
        norm[target] = (values * inverse * gains[0]).astype(bf16)
        return carry

    lax.fori_loop(0, group_len // 16, normalise, 0)
    local.append(links.keep(norm, norm_ref))

    def project(low, high):
        step = group_len // 2
        for part in range(2):
            rows = slice(part * step, (part + 1) * step)
            total = None
            for z in range(line):
                weight = weights[z, :, :rows_each, low:high].reshape(8 * rows_each, high - low)
                term = jnp.dot(
                    norm[rows, z * 8 * rows_each : (z + 1) * 8 * rows_each],
                    weight,
                    preferred_element_type=f32,
                )
                total = term if total is None else total + term
            flat[rows, low:high] = total

    def turn(values, rows):
        return values * turns[0, rows] + pltpu.roll(values, HD // 2, 1) * turns[1, rows]

    project(q_cols, q_cols + 2 * HD)
    for block in range(line):
        rows = slice(block * span_len, (block + 1) * span_len)
        kv[0, rows, :HD] = turn(flat[rows, q_cols : q_cols + HD], rows).astype(bf16)
        kv[0, rows, HD:] = flat[rows, q_cols + HD : q_cols + 2 * HD].astype(bf16)
    exchange = links.send(kv.at[0], kv.at[1], "x")
    project(0, q_cols)
    for block in range(line):
        rows = slice(block * span_len, (block + 1) * span_len)
        for head in range(heads):
            lanes = slice(head * HD, (head + 1) * HD)
            query[rows, lanes] = turn(flat[rows, lanes], rows).astype(bf16)
    local.append(links.keep(query, query_ref))
    exchange.wait_recv()
    local.append(links.keep(kv, kv_ref))

    scale = 1.0 / math.sqrt(HD)
    peak[...] = jnp.zeros_like(peak)

    def attend(head, carry):
        lanes = pl.ds(pl.multiple_of(head * HD, HD), HD)
        for block in range(line):
            rows = slice(block * span_len, (block + 1) * span_len)
            reach = (block + 1) * span_len
            part = query[rows, lanes]
            row = lax.broadcasted_iota(jnp.int32, (span_len, reach), 0) + block * span_len
            column = lax.broadcasted_iota(jnp.int32, (span_len, reach), 1)
            allowed = (column <= row, column < (block + links.x) * span_len)
            scores = []
            for half in range(2):
                score = lax.dot_general(
                    part, kv[half, :reach, :HD], (((1,), (1,)), ((), ())), preferred_element_type=f32
                )
                scores.append(jnp.where(allowed[half], score * scale, -1e30))
            top = jnp.maximum(
                jnp.max(scores[0], axis=-1, keepdims=True), jnp.max(scores[1], axis=-1, keepdims=True)
            )
            total, mixed = None, None
            for half in range(2):
                weight = jnp.exp(scores[half] - top)
                count = jnp.sum(weight, axis=-1, keepdims=True)
                term = jnp.dot(weight.astype(bf16), kv[half, :reach, HD:], preferred_element_type=f32)
                total = count if total is None else total + count
                mixed = term if mixed is None else mixed + term
            att[rows, lanes] = (mixed / total).astype(bf16)
            spot = lax.broadcasted_iota(jnp.int32, (span_len, HD), 1) == head
            peak[rows] = jnp.where(spot, top + jnp.log(total), peak[rows])
        return carry

    lax.fori_loop(0, heads, attend, 0)
    local.append(links.keep(peak, peak_ref))

    def place(block, rows):
        return atts_ref.at[rows, pl.ds(pl.multiple_of(block * q_cols, q_cols), q_cols)]

    att_ring = RingGather(links, att, place)
    mix_ring = RingGather(links, mix_ref, lambda block, rows: mixs_ref.at[block, rows])
    local.append(links.keep(att, place(links.z, pl.ds(0, group_len))))
    att_ring.step(0)
    mix_ring.step(0)
    for k in far:
        turned_ff[k].wait_recv()
        far_ff.offer(k, ffs_ref.at[links.along(-k), here])
    far_ff.relay(0, "x")
    far_ff.close(0)
    far_ff.relay(far[0], "x")
    att_ring.step(1)
    mix_ring.step(1)
    for k in far[1:]:
        far_ff.relay(k, "x" if k < line // 2 else "y")
    att_ring.step(2)
    mix_ring.step(2)
    for k in far:
        far_ff.close(k)
    att_ring.step(3)
    mix_ring.step(3)
    far_ff.wait(range(line))
    links.finish()
    for copy in local:
        copy.wait()


def add_rows_of(target, values, count):
    def add(index, carry):
        rows = pl.ds(pl.multiple_of(index * 16, 16), 16)
        target[rows] = target[rows] + values[rows]
        return carry

    lax.fori_loop(0, count // 16, add, 0)


class NearSum:
    def __init__(self, links, source, own, from_core, from_first, from_second, first, in_place=False):
        self.links, self.source, self.own, self.first = links, source, own, first
        self.in_place = in_place
        self.from_core, self.from_first, self.from_second = from_core, from_first, from_second

    def start(self):
        links = self.links
        if not self.in_place:
            self.local = links.keep(self.source(links.c), self.own)
        self.copy = links.send(self.source(1 - links.c), self.from_core, "c")

    def add(self, target, values):
        add_rows_of(target, values, target.shape[0])

    def core_done(self):
        links = self.links
        self.copy.wait_recv()
        if not self.in_place:
            self.local.wait()
        for x in range(2):
            for y in range(2):
                self.add(self.own.at[x, y], self.from_core.at[x, y])
        if self.first == "x":
            self.copy = links.send(self.own.at[1 - links.x], self.from_first, "x")
        else:
            self.copy = links.send(self.own.at[:, 1 - links.y], self.from_first, "y")

    def first_done(self):
        links = self.links
        self.copy.wait_recv()
        for other in range(2):
            place = (links.x, other) if self.first == "x" else (other, links.y)
            self.add(self.own.at[place], self.from_first.at[other])
        if self.first == "x":
            self.copy = links.send(self.own.at[links.x, 1 - links.y], self.from_second, "y")
        else:
            self.copy = links.send(self.own.at[1 - links.x, links.y], self.from_second, "x")

    def second_done(self):
        self.copy.wait_recv()
        total = self.own.at[self.links.x, self.links.y]
        self.add(total, self.from_second)
        return total


def sum_space(blocks, rows, columns):
    shape = (rows, columns)
    return [
        pltpu.VMEM((blocks, 2, 2) + shape, jnp.bfloat16),
        pltpu.VMEM((blocks, 2, 2) + shape, jnp.bfloat16),
        pltpu.VMEM((blocks, 2) + shape, jnp.bfloat16),
        pltpu.VMEM((blocks,) + shape, jnp.bfloat16),
    ]


class RingSum:
    def __init__(self, links, parts, total, got, made, pieces=4):
        self.links, self.parts, self.total, self.got, self.made = links, parts, total, got, made
        self.pieces, self.last = pieces, [None] * pieces
        self.rows = parts.shape[1] // pieces

    def step(self, number):
        links = self.links
        for piece in range(self.pieces):
            way = 1 if piece < self.pieces // 2 else -1
            block = links.along(-way * (number + 1))
            where = pl.ds(piece * self.rows, self.rows)
            if number == 0:
                source = self.parts.at[block, where]
            else:
                self.last[piece].wait_recv()
                total = self.got[number - 1, where].astype(jnp.float32) + self.parts[
                    block, where
                ].astype(jnp.float32)
                if number == links.line - 1:
                    self.total[where] = total
                    continue
                made, place = (self.parts, block) if self.made is None else (self.made, number - 1)
                made[place, where] = total.astype(made.dtype)
                source = made.at[place, where]
            self.last[piece] = links.send(source, self.got.at[number, where], way)


def ring_space(line, shape):
    return [pltpu.VMEM((line - 1,) + shape, jnp.bfloat16), pltpu.VMEM((line - 2,) + shape, jnp.bfloat16)]


def third_kernel(
    line, cuts, parts_ref, down_ref, total_ref, sum_ref, got, made, *scratch
):
    space, (send_sems, recv_sems) = scratch[:-2], scratch[-2:]
    links = Links(send_sems, recv_sems, line)
    links.meet(["x", "y", "c", 1, line - 1])
    ring = RingSum(links, parts_ref, total_ref, got, made)
    ring.step(0)
    items = []
    for index, (low, high) in enumerate(cuts):
        rows = pl.ds(low, high - low)
        own, core, first, second = space[4 * index : 4 * index + 4]
        items.append(
            NearSum(
                links,
                lambda c, rows=rows: down_ref.at[:, :, c, rows],
                own.at[0],
                core.at[0],
                first.at[0],
                second.at[0],
                "xy"[index % 2],
            )
        )
    for item in items:
        item.start()
    for item in items:
        item.core_done()
    ring.step(1)
    for item in items:
        item.first_done()
    ring.step(2)
    for item, (low, high) in zip(items, cuts):
        sum_ref[low:high] = item.second_done()[...]
    ring.step(3)
    links.finish()


def link_call(kernel, collective_id, copies, shapes, arguments, spaces=None, scratch=(), vmem=16):
    any_space = pl.BlockSpec(memory_space=pl.ANY)
    near_space = pl.BlockSpec(memory_space=pltpu.VMEM)
    many = isinstance(shapes, tuple)
    if spaces is None:
        spaces = "h" * (len(arguments) + (len(shapes) if many else 1))
    specs = [near_space if space == "v" else any_space for space in spaces]
    return pl.pallas_call(
        kernel,
        out_shape=shapes,
        in_specs=specs[: len(arguments)],
        out_specs=tuple(specs[len(arguments) :]) if many else specs[-1],
        scratch_shapes=list(scratch)
        + [pltpu.SemaphoreType.DMA((copies,)), pltpu.SemaphoreType.DMA((copies,))],
        compiler_params=pltpu.CompilerParams(
            collective_id=collective_id, has_side_effects=True, vmem_limit_bytes=vmem * 2**20
        ),
    )(*arguments)


def forward_call(tokens, table, pack, pack_ff, mixed, line):
    span_len, width = tokens.shape
    group_len = line * span_len
    rows_each = pack_ff.shape[1]
    qkv_cols = pack.shape[2]
    q_cols = qkv_cols - 2 * HD
    f32, bf16 = jnp.float32, jnp.bfloat16
    outs = (
        ((line, span_len, width), bf16),
        ((line, 8) + pack.shape[1:], bf16),
        ((2, 16, width), f32),
        ((group_len, width), bf16),
        ((group_len, q_cols), bf16),
        ((2, group_len, 2 * HD), bf16),
        ((group_len, HD), f32),
        ((2, group_len, HD), f32),
        ((group_len, line * q_cols), bf16),
        ((line, span_len, width), bf16),
        ((line, 8) + pack_ff.shape[1:], bf16),
    )
    return link_call(
        functools.partial(first_kernel, line),
        0,
        176,
        tuple(jax.ShapeDtypeStruct(*out) for out in outs),
        (tokens, table, pack, pack_ff, mixed),
        scratch=[
            pltpu.VMEM((line, span_len, width), bf16),
            pltpu.VMEM((line,) + table.shape, f32),
            pltpu.VMEM((line, 8) + pack.shape[1:], bf16),
            pltpu.VMEM((2, 16, width), f32),
            pltpu.VMEM((group_len, width), bf16),
            pltpu.VMEM((2, group_len, HD), f32),
            pltpu.VMEM((group_len, qkv_cols), f32),
            pltpu.VMEM((group_len, q_cols), bf16),
            pltpu.VMEM((2, group_len, 2 * HD), bf16),
            pltpu.VMEM((group_len, HD), f32),
            pltpu.VMEM((group_len, q_cols), bf16),
        ],
        vmem=48,
    )


def third_sum(parts, grad_down, line):
    shape = parts.shape[1:]
    rows, columns = grad_down.shape[3:]
    half = (rows // 2 + 15) // 16 * 16
    cuts = ((0, half), (half, rows))
    return link_call(
        functools.partial(third_kernel, line, cuts),
        2,
        64,
        (jax.ShapeDtypeStruct(shape, jnp.float32), jax.ShapeDtypeStruct((rows, columns), jnp.bfloat16)),
        (parts, grad_down),
        "vhvv",
        ring_space(line, shape) + sum((sum_space(1, high - low, columns) for low, high in cuts), []),
        vmem=40,
    )


def backward_kernel(
    line,
    up_ref,
    middle_ref,
    norm_grad_ref,
    keep_ref,
    gain_ref,
    query,
    kv,
    peak,
    turns,
    mixed_ref,
    out_ref,
    atts_ref,
    weight_ref,
    norm_ref,
    ff_ref,
    middle_grad_ref,
    mixed_total_ref,
    total_ref,
    ffs_ref,
    outs_ref,
    qkvs_ref,
    big,
    slim,
    norm,
    own_rows,
    own_columns,
    branch,
    own_grad,
    att_grad,
    query_back,
    kv_back,
    kv_out,
    kv_in,
    flat,
    parts,
    *scratch,
):
    f32, bf16 = jnp.float32, jnp.bfloat16
    send_sems, recv_sems = scratch[-2:]
    rings, sums = scratch[:3], scratch[3:-2]
    links = Links(send_sems, recv_sems, line)
    far = [1, line - 1] + list(range(2, line - 1))
    order = far + [0]
    links.meet(["x", "y", "c"] + far)
    span_len, width = up_ref.shape
    group_len = line * span_len
    q_cols = query.shape[1]
    heads = q_cols // HD
    rows_z = width // line
    rows_each = rows_z // 8
    scale = 1.0 / math.sqrt(HD)

    def lanes_of(block):
        return pl.ds(pl.multiple_of(block * q_cols, q_cols), q_cols)

    here = pl.ds(pl.multiple_of(links.z * span_len, span_len), span_len)
    loads = [
        links.keep(out_ref, big),
        links.keep(atts_ref.at[here], own_rows),
        links.keep(atts_ref.at[:, lanes_of(links.z)], own_columns),
        links.keep(norm_ref, norm),
        links.keep(weight_ref.at[:, :, :, :, pl.ds(0, slim.shape[4])], slim),
    ]
    mixed_ring = RingSum(links, mixed_ref, mixed_total_ref, *rings[:2])
    ring = RingSum(links, parts, total_ref, rings[2], None)

    def items_of(source, space, in_place):
        items = []
        for index, k in enumerate(order):
            block = links.along(k)
            own = source.at[block, :, :, links.c] if in_place else space[0].at[index]
            core, first, second = space[-3:]
            items.append(
                NearSum(
                    links,
                    lambda c, block=block: source.at[block, :, :, c],
                    own,
                    core.at[index],
                    first.at[index],
                    second.at[index],
                    "xy"[index % 2],
                    in_place,
                )
            )
        return items

    ff_items = items_of(ff_ref, sums[:4], False)
    out_items = items_of(big, sums[4:7], True)
    qkv_items = items_of(slim, sums[7:], True)
    arrived, local = [], []

    def turn(items, target, low, high):
        for item, k in list(zip(items, order))[low:high]:
            total = item.second_done()
            if k == 0:
                local.append(links.keep(total, target.at[links.z]))
            else:
                arrived.append(links.send(total, target.at[links.z], k))

    def core_done(items, low, high):
        for item in items[low:high]:
            item.core_done()

    def first_done(items, low, high):
        for item in items[low:high]:
            item.first_done()

    half = line // 2
    for item in ff_items:
        item.start()
    mixed_ring.step(0)

    def d_middle(index, carry):
        rows = pl.ds(pl.multiple_of(index * 16, 16), 16)
        middle = middle_ref[rows]
        inverse = lax.rsqrt(jnp.mean(middle * middle, axis=-1, keepdims=True) + epsilon)
        scaled = gain_ref[1] * norm_grad_ref[rows]
        grad = (
            up_ref[rows]
            + inverse * scaled
            - middle
            * (inverse * inverse * inverse)
            * jnp.mean(scaled * middle, axis=-1, keepdims=True)
        )
        middle_grad_ref[rows] = grad
        branch[rows] = (grad * keep_ref[0:1, 0:1]).astype(bf16)
        return carry

    lax.fori_loop(0, span_len // 16, d_middle, 0)
    for copy in loads:
        copy.wait()
    for z in range(line):
        weight = big[z].reshape(rows_z, width)
        own_grad[:, z * rows_z : (z + 1) * rows_z] = lax.dot_general(
            branch[...], weight, (((1,), (1,)), ((), ())), preferred_element_type=f32
        ).astype(bf16)
    turned = [links.send(own_grad.at[:, lanes_of(links.along(k))], att_grad.at[here], k) for k in far]
    stayed = links.keep(own_grad.at[:, lanes_of(links.z)], att_grad.at[here])
    core_done(ff_items, 0, half)
    for z in range(line):
        for part in range(4):
            columns = slice(part * width // 4, (part + 1) * width // 4)
            grad = lax.dot_general(
                own_rows[:, z * rows_z : (z + 1) * rows_z],
                branch[:, columns],
                (((0,), (0,)), ((), ())),
                preferred_element_type=f32,
            )
            big[z, :, :, :, :, columns] = grad.astype(bf16).reshape(2, 2, 2, rows_each, width // 4)
    for item in out_items:
        item.start()
    core_done(ff_items, half, line)
    mixed_ring.step(1)
    kv_back[...] = jnp.zeros_like(kv_back)
    for copy in turned:
        copy.wait_recv()
    stayed.wait()

    def attend_back(head, carry):
        lanes = pl.ds(pl.multiple_of(head * HD, HD), HD)
        for block in range(line):
            rows = slice(block * span_len, (block + 1) * span_len)
            reach = (block + 1) * span_len
            part, grad = query[rows, lanes], att_grad[rows, lanes]
            row = lax.broadcasted_iota(jnp.int32, (span_len, reach), 0) + block * span_len
            column = lax.broadcasted_iota(jnp.int32, (span_len, reach), 1)
            allowed = (column <= row, column < (block + links.x) * span_len)
            spot = lax.broadcasted_iota(jnp.int32, (span_len, HD), 1) == head
            top = jnp.sum(jnp.where(spot, peak[rows], 0.0), axis=-1, keepdims=True)
            delta = jnp.sum(
                grad.astype(f32) * own_columns[rows, lanes].astype(f32), axis=-1, keepdims=True
            )
            total = None
            for side in range(2):
                keys, values = kv[side, :reach, :HD], kv[side, :reach, HD:]
                score = lax.dot_general(
                    part, keys, (((1,), (1,)), ((), ())), preferred_element_type=f32
                )
                weight = jnp.where(allowed[side], jnp.exp(score * scale - top), 0.0)
                weight_grad = lax.dot_general(
                    grad, values, (((1,), (1,)), ((), ())), preferred_element_type=f32
                )
                score_grad = (weight * (weight_grad - delta)).astype(bf16)
                term = jnp.dot(score_grad, keys, preferred_element_type=f32)
                total = term if total is None else total + term
                kv_back[side, :reach, :HD] += lax.dot_general(
                    score_grad, part, (((0,), (0,)), ((), ())), preferred_element_type=f32
                )
                kv_back[side, :reach, HD:] += lax.dot_general(
                    weight.astype(bf16), grad, (((0,), (0,)), ((), ())), preferred_element_type=f32
                )
            query_back[rows, lanes] = total * scale
        return carry

    lax.fori_loop(0, heads, attend_back, 0)
    kv_out[:, :HD] = (kv_back[1, :, :HD] * scale).astype(bf16)
    kv_out[:, HD:] = kv_back[1, :, HD:].astype(bf16)
    exchange = links.send(kv_out, kv_in, "x")

    def turn_back(values, rows):
        return values * turns[0, rows] - pltpu.roll(values, HD // 2, 1) * turns[1, rows]

    for block in range(line):
        rows = slice(block * span_len, (block + 1) * span_len)
        for head in range(heads):
            lanes = slice(head * HD, (head + 1) * HD)
            flat[rows, lanes] = turn_back(query_back[rows, lanes], rows).astype(bf16)
    first_done(ff_items, 0, half)
    exchange.wait_recv()
    for block in range(line):
        rows = slice(block * span_len, (block + 1) * span_len)
        key_grad = kv_back[0, rows, :HD] * scale + kv_in[rows, :HD].astype(f32)
        flat[rows, q_cols : q_cols + HD] = turn_back(key_grad, rows).astype(bf16)
        value_grad = kv_back[0, rows, HD:] + kv_in[rows, HD:].astype(f32)
        flat[rows, q_cols + HD :] = value_grad.astype(bf16)
    for z in range(line):
        weight = slim[z].reshape(rows_z, flat.shape[1])
        part = lax.dot_general(
            flat[...], weight, (((1,), (1,)), ((), ())), preferred_element_type=f32
        ).astype(bf16)
        for block in range(line):
            parts[block, :, z * rows_z : (z + 1) * rows_z] = part[
                block * span_len : (block + 1) * span_len
            ]
    ring.step(0)
    for z in range(line):
        grad = lax.dot_general(
            norm[:, z * rows_z : (z + 1) * rows_z],
            flat[...],
            (((0,), (0,)), ((), ())),
            preferred_element_type=f32,
        )
        slim[z] = grad.astype(bf16).reshape(2, 2, 2, rows_each, flat.shape[1])
    for item in qkv_items:
        item.start()
    core_done(out_items, 0, half)
    mixed_ring.step(2)
    first_done(ff_items, half, line)
    turn(ff_items, ffs_ref, 0, half)
    ring.step(1)
    core_done(out_items, half, line)
    first_done(out_items, 0, half)
    turn(ff_items, ffs_ref, half, line)
    ring.step(2)
    core_done(qkv_items, 0, line)
    first_done(out_items, half, line)
    turn(out_items, outs_ref, 0, half)
    mixed_ring.step(3)
    ring.step(3)
    first_done(qkv_items, 0, half)
    turn(out_items, outs_ref, half, line)
    first_done(qkv_items, half, line)
    turn(qkv_items, qkvs_ref, 0, line)
    for copy in arrived:
        copy.wait_recv()
    links.finish()
    for copy in local:
        copy.wait()


def backward_call(small, mixed_parts, out_w, attended, weights, norm, grad_ff, line):
    f32, bf16 = jnp.float32, jnp.bfloat16
    span_len, width = small[0].shape
    group_len = line * span_len
    query = small[5]
    q_cols, rows_each, qkv_cols = query.shape[1], width // line // 8, weights.shape[3]
    weights = weights.reshape(line, 2, 2, 2, -1, qkv_cols)
    wide = (line, 2, 2, 2, rows_each, width)
    slim = (line, 2, 2, 2, rows_each, qkv_cols)
    out_space = sum_space(line, rows_each, width)[1:]
    qkv_space = sum_space(line, rows_each, qkv_cols)[1:]
    token = jax.ShapeDtypeStruct((span_len, width), f32)
    return link_call(
        functools.partial(backward_kernel, line),
        4,
        160,
        (token, token, token)
        + tuple(
            jax.ShapeDtypeStruct((line, rows_each, columns), bf16)
            for columns in (grad_ff.shape[5], width, qkv_cols)
        ),
        small + (mixed_parts, out_w.reshape(wide), attended, weights, norm, grad_ff),
        "v" * 10 + "hhhhh" + "vvvhhh",
        [
            pltpu.VMEM(wide, bf16),
            pltpu.VMEM(slim, bf16),
            pltpu.VMEM((group_len, width), bf16),
            pltpu.VMEM((span_len, width), bf16),
            pltpu.VMEM((group_len, q_cols), bf16),
            pltpu.VMEM((span_len, width), bf16),
            pltpu.VMEM((span_len, width), bf16),
            pltpu.VMEM((group_len, q_cols), bf16),
            pltpu.VMEM((group_len, q_cols), f32),
            pltpu.VMEM((2, group_len, 2 * HD), f32),
            pltpu.VMEM((group_len, 2 * HD), bf16),
            pltpu.VMEM((group_len, 2 * HD), bf16),
            pltpu.VMEM((group_len, qkv_cols), bf16),
            pltpu.VMEM((line, span_len, width), bf16),
        ]
        + ring_space(line, (span_len, width))
        + ring_space(line, (span_len, width))[:1]
        + sum_space(line, rows_each, grad_ff.shape[5])
        + out_space
        + qkv_space,
        vmem=63,
    )


def general_body(
    tokens,
    attn_gain,
    w_query,
    w_key,
    w_value,
    w_out,
    mlp_gain,
    w_gate,
    w_up,
    w_down,
    keep_mask,
    group_ids,
    positions,
    exit_scale,
    out_grad,
):
    seq_count, span_len, model_width = tokens.shape
    kv_heads = KVH
    head_dim = HD
    head_count = HEADS
    group_size = head_count // kv_heads
    row_count = seq_count * span_len
    stripe = group_size * span_len
    wide_count = lax.axis_size("wide")
    wide_place = lax.axis_index("wide")
    full_len = span_len * wide_count
    score_scale = 1.0 / math.sqrt(head_dim)
    gain_one, query_w, key_w, value_w, out_w = (
        lax.all_gather(attn_gain, ("wide", "narrow"), axis=0, tiled=True),
        lax.all_gather(w_query, ("wide", "narrow"), axis=0, tiled=True),
        lax.all_gather(w_key, ("wide", "narrow"), axis=0, tiled=True),
        lax.all_gather(w_value, ("wide", "narrow"), axis=0, tiled=True),
        lax.all_gather(w_out, ("wide", "narrow"), axis=0, tiled=True),
    )
    inputs = tokens.astype(jnp.float32).reshape(row_count, model_width)
    token_pos = positions.reshape(row_count)
    keep_rows = jnp.repeat(keep_mask.astype(jnp.float32), span_len)[:, None]
    inverse_one = lax.rsqrt(jnp.mean(inputs * inputs, axis=-1, keepdims=True) + epsilon)
    first_norm = (inputs * inverse_one * gain_one.astype(jnp.float32)).astype(jnp.bfloat16)
    query_pre = jnp.dot(first_norm, query_w, preferred_element_type=jnp.float32).reshape(
        row_count, head_count, head_dim
    )
    key_pre = jnp.dot(first_norm, key_w, preferred_element_type=jnp.float32).reshape(
        row_count, kv_heads, head_dim
    )
    query_rows = rotate(query_pre, token_pos, 1.0).astype(jnp.bfloat16)
    key_heads = (
        rotate(key_pre, token_pos, 1.0)
        .astype(jnp.bfloat16)
        .reshape(seq_count, span_len, kv_heads * head_dim)
    )
    value_heads = (
        jnp.dot(first_norm, value_w, preferred_element_type=jnp.float32)
        .astype(jnp.bfloat16)
        .reshape(seq_count, span_len, kv_heads * head_dim)
    )
    queries = (
        query_rows.reshape(seq_count, span_len, kv_heads, group_size, head_dim)
        .transpose(0, 2, 3, 1, 4)
        .reshape(seq_count, kv_heads, stripe, head_dim)
    )
    query_index = wide_place * span_len + jnp.arange(stripe, dtype=jnp.int32) % span_len
    last_query = wide_place * span_len + span_len - 1

    def block_scores(key_block, key_first):
        scores = (
            jnp.einsum("skrd,sjkd->skrj", queries, key_block, preferred_element_type=jnp.float32)
            * score_scale
        )
        key_index = key_first + jnp.arange(key_block.shape[1], dtype=jnp.int32)
        allowed = key_index[None, :] <= query_index[:, None]
        return (scores, allowed)

    start_forward = (
        jnp.full((seq_count, kv_heads, stripe), -1e30, jnp.float32),
        jnp.zeros((seq_count, kv_heads, stripe), jnp.float32),
        jnp.zeros((seq_count, kv_heads, stripe, head_dim), jnp.float32),
    )
    running = start_forward
    pieces = (
        lax.all_gather(key_heads, "wide", axis=1, tiled=True),
        lax.all_gather(value_heads, "wide", axis=1, tiled=True),
    )
    key_blocks = split_blocks(pieces[0], seq_count, kv_heads, head_dim)
    value_blocks = split_blocks(pieces[1], seq_count, kv_heads, head_dim)
    block_len = key_blocks.shape[2]

    def advance(carried, block_item):
        key_block, value_block, block_index = block_item
        key_first = block_index * block_len

        def compute_block(current):
            run_max, run_sum, run_acc = current
            scores, allowed = block_scores(key_block, key_first)
            scores = jnp.where(allowed, scores, -1e30)
            new_max = jnp.maximum(run_max, jnp.max(scores, axis=-1))
            factor = jnp.exp(run_max - new_max)
            weights = jnp.where(allowed, jnp.exp(scores - new_max[..., None]), 0.0)
            new_sum = run_sum * factor + jnp.sum(weights, axis=-1)
            new_acc = run_acc * factor[..., None] + jnp.einsum(
                "skrj,sjkd->skrd",
                weights.astype(jnp.bfloat16),
                value_block,
                preferred_element_type=jnp.float32,
            )
            return (new_max, new_sum, new_acc)

        return (lax.cond(key_first <= last_query, compute_block, unchanged, carried), None)

    running, _ = lax.scan(
        advance,
        running,
        (key_blocks, value_blocks, jnp.arange(key_blocks.shape[0], dtype=jnp.int32)),
    )
    run_max, run_sum, run_acc = running
    attended = run_acc / run_sum[..., None]
    log_total = run_max + jnp.log(run_sum)
    attended_rows = (
        attended.reshape(seq_count, kv_heads, group_size, span_len, head_dim)
        .transpose(0, 3, 1, 2, 4)
        .reshape(row_count, head_count * head_dim)
        .astype(jnp.bfloat16)
    )
    middle = inputs + keep_rows * jnp.dot(attended_rows, out_w, preferred_element_type=jnp.float32)
    gain_two, gate_w, up_w, down_w = (
        lax.all_gather(mlp_gain, ("wide", "narrow"), axis=0, tiled=True),
        lax.all_gather(w_gate, ("wide", "narrow"), axis=0, tiled=True),
        lax.all_gather(w_up, ("wide", "narrow"), axis=0, tiled=True),
        lax.all_gather(w_down, ("wide", "narrow"), axis=0, tiled=True),
    )
    inverse_two = lax.rsqrt(jnp.mean(middle * middle, axis=-1, keepdims=True) + epsilon)
    second_norm = (middle * inverse_two * gain_two.astype(jnp.float32)).astype(jnp.bfloat16)
    gate_value = jnp.dot(second_norm, gate_w, preferred_element_type=jnp.float32)
    up_value = jnp.dot(second_norm, up_w, preferred_element_type=jnp.float32)
    gate_sigmoid = jax.nn.sigmoid(gate_value)
    swish_value = gate_value * gate_sigmoid
    hidden = (swish_value * up_value).astype(jnp.bfloat16)
    output = (
        middle + keep_rows * jnp.dot(hidden, down_w, preferred_element_type=jnp.float32)
    ).astype(jnp.bfloat16)
    group_match = (
        group_ids.reshape(row_count)[:, None]
        == jnp.arange(exit_scale.shape[0], dtype=jnp.int32)[None, :]
    )
    token_scale = jnp.sum(jnp.where(group_match, exit_scale[None, :], 0.0), axis=1, keepdims=True)
    upstream = out_grad.astype(jnp.float32).reshape(row_count, model_width) * token_scale
    gain_two, gate_w, up_w, down_w = (
        lax.all_gather(mlp_gain, ("wide", "narrow"), axis=0, tiled=True),
        lax.all_gather(w_gate, ("wide", "narrow"), axis=0, tiled=True),
        lax.all_gather(w_up, ("wide", "narrow"), axis=0, tiled=True),
        lax.all_gather(w_down, ("wide", "narrow"), axis=0, tiled=True),
    )
    mixed_grad = (keep_rows * upstream).astype(jnp.bfloat16)
    grad_down = over_rows(hidden, mixed_grad)
    hidden_grad = against(mixed_grad, down_w)
    gate_grad = (
        hidden_grad * up_value * gate_sigmoid * (1.0 + gate_value * (1.0 - gate_sigmoid))
    ).astype(jnp.bfloat16)
    up_grad = (hidden_grad * swish_value).astype(jnp.bfloat16)
    grad_gate = over_rows(second_norm, gate_grad)
    grad_up = over_rows(second_norm, up_grad)
    norm_grad = against(gate_grad, gate_w) + against(up_grad, up_w)
    grad_gain_two = jnp.sum(norm_grad * middle * inverse_two, axis=0)
    scaled_two = gain_two.astype(jnp.float32) * norm_grad
    middle_grad = (
        upstream
        + inverse_two * scaled_two
        - middle
        * (inverse_two * inverse_two * inverse_two)
        * jnp.mean(scaled_two * middle, axis=-1, keepdims=True)
    )
    gain_two_share, gate_share, up_share, down_share = (
        lax.psum_scatter(grad_gain_two, ("wide", "narrow"), scatter_dimension=0, tiled=True),
        lax.psum_scatter(grad_gate, ("wide", "narrow"), scatter_dimension=0, tiled=True),
        lax.psum_scatter(grad_up, ("wide", "narrow"), scatter_dimension=0, tiled=True),
        lax.psum_scatter(grad_down, ("wide", "narrow"), scatter_dimension=0, tiled=True),
    )
    gain_one, query_w, key_w, value_w, out_w = (
        lax.all_gather(attn_gain, ("wide", "narrow"), axis=0, tiled=True),
        lax.all_gather(w_query, ("wide", "narrow"), axis=0, tiled=True),
        lax.all_gather(w_key, ("wide", "narrow"), axis=0, tiled=True),
        lax.all_gather(w_value, ("wide", "narrow"), axis=0, tiled=True),
        lax.all_gather(w_out, ("wide", "narrow"), axis=0, tiled=True),
    )
    branch_grad = (keep_rows * middle_grad).astype(jnp.bfloat16)
    grad_out = over_rows(attended_rows, branch_grad)
    attended_grad = against(branch_grad, out_w).astype(jnp.bfloat16)
    grouped_grad = (
        attended_grad.reshape(seq_count, span_len, kv_heads, group_size, head_dim)
        .transpose(0, 2, 3, 1, 4)
        .reshape(seq_count, kv_heads, stripe, head_dim)
    )
    row_delta = jnp.sum(grouped_grad.astype(jnp.float32) * attended, axis=-1)
    start_backward = (
        jnp.zeros((seq_count, kv_heads, stripe, head_dim), jnp.float32),
        jnp.zeros((seq_count, full_len, kv_heads * head_dim), jnp.float32),
        jnp.zeros((seq_count, full_len, kv_heads * head_dim), jnp.float32),
    )
    running = start_backward
    pieces = (
        lax.all_gather(key_heads, "wide", axis=1, tiled=True),
        lax.all_gather(value_heads, "wide", axis=1, tiled=True),
    )
    key_blocks = split_blocks(pieces[0], seq_count, kv_heads, head_dim)
    value_blocks = split_blocks(pieces[1], seq_count, kv_heads, head_dim)
    fold_block_len = key_blocks.shape[2]

    def advance(carried, block_item):
        key_block, value_block, block_index = block_item
        key_first = block_index * fold_block_len

        def compute_block(current):
            query_acc, key_acc, value_acc = current
            scores, allowed = block_scores(key_block, key_first)
            probabilities = jnp.where(allowed, jnp.exp(scores - log_total[..., None]), 0.0)
            value_part = jnp.einsum(
                "skrj,skrd->sjkd",
                probabilities.astype(jnp.bfloat16),
                grouped_grad,
                preferred_element_type=jnp.float32,
            )
            prob_grad = jnp.einsum(
                "skrd,sjkd->skrj", grouped_grad, value_block, preferred_element_type=jnp.float32
            )
            score_grad = (probabilities * (prob_grad - row_delta[..., None])).astype(jnp.bfloat16)
            query_acc = (
                query_acc
                + jnp.einsum(
                    "skrj,sjkd->skrd", score_grad, key_block, preferred_element_type=jnp.float32
                )
                * score_scale
            )
            key_part = (
                jnp.einsum(
                    "skrj,skrd->sjkd", score_grad, queries, preferred_element_type=jnp.float32
                )
                * score_scale
            )
            key_acc = add_rows(
                key_acc, key_part.reshape(seq_count, fold_block_len, kv_heads * head_dim), key_first
            )
            value_acc = add_rows(
                value_acc,
                value_part.reshape(seq_count, fold_block_len, kv_heads * head_dim),
                key_first,
            )
            return (query_acc, key_acc, value_acc)

        return (lax.cond(key_first <= last_query, compute_block, unchanged, carried), None)

    running, _ = lax.scan(
        advance,
        running,
        (key_blocks, value_blocks, jnp.arange(key_blocks.shape[0], dtype=jnp.int32)),
    )
    query_acc, key_acc, value_acc = running
    key_sum, value_sum = (
        lax.psum_scatter(
            key_acc.astype(jnp.bfloat16), "wide", scatter_dimension=1, tiled=True
        ).astype(jnp.float32),
        lax.psum_scatter(
            value_acc.astype(jnp.bfloat16), "wide", scatter_dimension=1, tiled=True
        ).astype(jnp.float32),
    )
    query_back = (
        query_acc.reshape(seq_count, kv_heads, group_size, span_len, head_dim)
        .transpose(0, 3, 1, 2, 4)
        .reshape(row_count, head_count, head_dim)
    )
    query_grad = (
        rotate(query_back, token_pos, -1.0)
        .reshape(row_count, head_count * head_dim)
        .astype(jnp.bfloat16)
    )
    key_grad = (
        rotate(key_sum.reshape(row_count, kv_heads, head_dim), token_pos, -1.0)
        .reshape(row_count, kv_heads * head_dim)
        .astype(jnp.bfloat16)
    )
    value_grad = value_sum.reshape(row_count, kv_heads * head_dim).astype(jnp.bfloat16)
    grad_query = over_rows(first_norm, query_grad)
    grad_key = over_rows(first_norm, key_grad)
    grad_value = over_rows(first_norm, value_grad)
    input_norm_grad = (
        against(query_grad, query_w) + against(key_grad, key_w) + against(value_grad, value_w)
    )
    grad_gain_one = jnp.sum(input_norm_grad * inputs * inverse_one, axis=0)
    scaled_one = gain_one.astype(jnp.float32) * input_norm_grad
    input_grad = (
        middle_grad
        + inverse_one * scaled_one
        - inputs
        * (inverse_one * inverse_one * inverse_one)
        * jnp.mean(scaled_one * inputs, axis=-1, keepdims=True)
    )
    gain_one_share, query_share, key_share, value_share, out_share = (
        lax.psum_scatter(grad_gain_one, ("wide", "narrow"), scatter_dimension=0, tiled=True),
        lax.psum_scatter(grad_query, ("wide", "narrow"), scatter_dimension=0, tiled=True),
        lax.psum_scatter(grad_key, ("wide", "narrow"), scatter_dimension=0, tiled=True),
        lax.psum_scatter(grad_value, ("wide", "narrow"), scatter_dimension=0, tiled=True),
        lax.psum_scatter(grad_out, ("wide", "narrow"), scatter_dimension=0, tiled=True),
    )
    return (
        output.reshape(seq_count, span_len, model_width),
        input_grad.astype(jnp.bfloat16).reshape(seq_count, span_len, model_width),
        gain_one_share,
        query_share,
        key_share,
        value_share,
        out_share,
        gain_two_share,
        gate_share,
        up_share,
        down_share,
    )


def line_body(
    tokens,
    attn_gain,
    w_query,
    w_key,
    w_value,
    w_out,
    mlp_gain,
    w_gate,
    w_up,
    w_down,
    keep_mask,
    group_ids,
    positions,
    exit_scale,
    out_grad,
):
    f32 = jnp.float32
    bf16 = jnp.bfloat16
    _, span_len, model_width = tokens.shape
    line = lax.axis_size("z")
    place = lax.axis_index("z")
    rows_each = w_query.shape[0]
    q_cols = HEADS // line * HD
    ff_cols = w_gate.shape[1] // line
    group_len = span_len * line

    def by_columns(weight, columns):
        return weight.reshape(rows_each, line, columns).transpose(1, 0, 2)

    out_w = lax.all_gather(w_out, ("z", "x", "y", "c"), axis=0, tiled=True)
    down_w = lax.all_gather(w_down, ("x", "y", "c"), axis=0, tiled=True)
    own_x = tokens[0].astype(f32)
    keep = keep_mask[0].astype(f32)
    group_match = group_ids[0][:, None] == jnp.arange(exit_scale.shape[0], dtype=jnp.int32)[None, :]
    token_scale = jnp.sum(jnp.where(group_match, exit_scale[None, :], 0.0), axis=1, keepdims=True)
    upstream = out_grad[0].astype(f32) * token_scale

    core = lax.axis_index("c")
    gain_row = jnp.zeros((q_cols + 2 * HD,), bf16)
    gain_row = lax.dynamic_update_slice_in_dim(gain_row, attn_gain, core * rows_each, 0)
    gain_row = lax.dynamic_update_slice_in_dim(gain_row, mlp_gain, HD + core * rows_each, 0)
    gain_rows = jnp.broadcast_to(gain_row, (line, 16, gain_row.shape[0]))
    pack_attn = jnp.concatenate(
        [by_columns(w_query, q_cols), by_columns(w_key, HD), by_columns(w_value, HD)], axis=2
    )
    pack_attn = jnp.concatenate([pack_attn, gain_rows], axis=1)
    pack_ff = jnp.concatenate([by_columns(w_gate, ff_cols), by_columns(w_up, ff_cols)], axis=2)
    freqs = 10000.0 ** (-2.0 * jnp.arange(HD // 2, dtype=f32) / HD)
    angles = positions[0].astype(f32)[:, None] * freqs[None, :]
    table = jnp.concatenate([jnp.cos(angles), jnp.sin(angles)], axis=1)
    (
        x_blocks,
        near_w,
        gain_all,
        first_norm,
        queries,
        both_kv,
        log_total,
        turns,
        attended_rows,
        mixed_grad,
        ff_w,
    ) = forward_call(tokens[0], table, pack_attn, pack_ff, (keep * upstream).astype(bf16), line)
    inputs = x_blocks.reshape(group_len, model_width).astype(f32)
    gain_one, gain_two = gain_all[0, :1], gain_all[1, :1]
    mixed_grad = mixed_grad.reshape(group_len, model_width)
    ff_w = ff_w.reshape(model_width, 2 * ff_cols)
    def own_rows(values):
        return lax.dynamic_slice_in_dim(values, place * span_len, span_len, 0)

    branch = jnp.dot(attended_rows, out_w, preferred_element_type=f32)
    middle_all = inputs + keep * branch
    inverse_mid = lax.rsqrt(jnp.mean(middle_all * middle_all, axis=-1, keepdims=True) + epsilon)
    second_norm = (middle_all * inverse_mid * gain_two).astype(bf16)
    middle = own_rows(middle_all)

    gate_up = jnp.dot(second_norm, ff_w, preferred_element_type=f32)
    gate_value = gate_up[:, :ff_cols]
    up_value = gate_up[:, ff_cols:]
    gate_sigmoid = jax.nn.sigmoid(gate_value)
    swish_value = gate_value * gate_sigmoid
    hidden = (swish_value * up_value).astype(bf16)
    hidden_grad = against(mixed_grad, down_w)
    gate_grad = hidden_grad * up_value * gate_sigmoid * (1.0 + gate_value * (1.0 - gate_sigmoid))
    up_grad = hidden_grad * swish_value
    both_grad = jnp.concatenate([gate_grad, up_grad], axis=1).astype(bf16)

    def split(values):
        return values.astype(bf16).reshape(line, span_len, model_width)

    grad_down = over_rows(hidden, mixed_grad).astype(bf16).reshape(2, 2, 2, -1, model_width)
    norm_grad, grad_down = third_sum(split(against(both_grad, ff_w)), grad_down, line)
    grad_down = grad_down.astype(f32)
    grad_ff = over_rows(second_norm, both_grad).astype(bf16)
    mixed_parts = split(jnp.dot(hidden, down_w, preferred_element_type=f32))
    middle_grad, mixed, input_norm_grad, ff_back, out_back, qkv_back = backward_call(
        (
            upstream,
            middle,
            norm_grad,
            jnp.broadcast_to(keep, (8, HD)),
            gain_all,
            queries,
            both_kv,
            log_total,
            turns,
        ),
        mixed_parts,
        out_w,
        attended_rows,
        near_w,
        first_norm,
        grad_ff.reshape(line, 2, 2, 2, rows_each, 2 * ff_cols),
        line,
    )
    output = (middle + keep * mixed).astype(bf16)
    ff_back = ff_back.astype(f32)
    qkv_back = qkv_back.astype(f32)
    grad_out = jnp.sum(out_back.astype(f32), axis=0)
    inverse_one = lax.rsqrt(jnp.mean(own_x * own_x, axis=-1, keepdims=True) + epsilon)
    scaled_one = gain_one * input_norm_grad
    input_grad = (
        middle_grad
        + inverse_one * scaled_one
        - own_x
        * (inverse_one * inverse_one * inverse_one)
        * jnp.mean(scaled_one * own_x, axis=-1, keepdims=True)
    )

    def side_by_side(blocks):
        return blocks.transpose(1, 0, 2).reshape(rows_each, -1)

    grad_query = side_by_side(qkv_back[:, :, :q_cols])
    grad_key = side_by_side(qkv_back[:, :, q_cols : q_cols + HD])
    grad_value = side_by_side(qkv_back[:, :, q_cols + HD :])
    grad_gate = side_by_side(ff_back[:, :, :ff_cols])
    grad_up = side_by_side(ff_back[:, :, ff_cols:])

    def gain_grad(pairs, gain):
        total = sum(jnp.sum(weight.astype(f32) * grad, axis=1) for weight, grad in pairs)
        return total / gain.astype(f32)

    return (
        output[None],
        input_grad.astype(bf16)[None],
        gain_grad([(w_query, grad_query), (w_key, grad_key), (w_value, grad_value)], attn_gain),
        grad_query,
        grad_key,
        grad_value,
        grad_out,
        gain_grad([(w_gate, grad_gate), (w_up, grad_up)], mlp_gain),
        grad_gate,
        grad_up,
        grad_down,
    )


def solution(mesh):
    wide, narrow = mesh.shape["wide"], mesh.shape["narrow"]
    if wide == 2 * KVH and narrow == 4:
        mesh = Mesh(mesh.devices.reshape(wide // 2, 2, 2, 2), ("z", "x", "y", "c"))
        body, wide, narrow = line_body, ("z", "x"), ("y", "c")
    else:
        body, wide, narrow = general_body, ("wide",), ("narrow",)
    token_spec = P(narrow, wide, None)
    id_spec = P(narrow, wide)
    gain_spec = P(wide + narrow)
    weight_spec = P(wide + narrow, None)
    return jax.shard_map(
        body,
        mesh=mesh,
        in_specs=(
            token_spec,
            gain_spec,
            weight_spec,
            weight_spec,
            weight_spec,
            weight_spec,
            gain_spec,
            weight_spec,
            weight_spec,
            weight_spec,
            P(narrow),
            id_spec,
            id_spec,
            P(),
            token_spec,
        ),
        out_specs=(
            token_spec,
            token_spec,
            gain_spec,
            weight_spec,
            weight_spec,
            weight_spec,
            weight_spec,
            gain_spec,
            weight_spec,
            weight_spec,
            weight_spec,
        ),
        check_vma=False,
    )
```

```python
import functools
import math

import jax
import jax.numpy as jnp
from jax import lax
from jax.experimental import pallas as pl
from jax.experimental.pallas import tpu as pltpu
from jax.sharding import Mesh
from jax.sharding import PartitionSpec as P

HEADS = 16
KVH = 4
HD = 128


epsilon = 1e-05


def rotate(vectors, token_pos, direction):
    half_size = vectors.shape[-1] // 2
    freqs = 10000.0 ** (-2.0 * jnp.arange(half_size, dtype=jnp.float32) / vectors.shape[-1])
    angles = token_pos.astype(jnp.float32)[:, None] * freqs[None, :]
    cosine = jnp.cos(angles)[:, None, :]
    sine = direction * jnp.sin(angles)[:, None, :]
    first_half = vectors[..., :half_size]
    second_half = vectors[..., half_size:]
    return jnp.concatenate(
        [first_half * cosine - second_half * sine, second_half * cosine + first_half * sine],
        axis=-1,
    )


def split_blocks(piece_arr, seq_count, kv_heads, head_dim):
    piece_len = piece_arr.shape[1]
    block_len = math.gcd(piece_len, 512)
    shaped = piece_arr.reshape(seq_count, piece_len // block_len, block_len, kv_heads, head_dim)
    return shaped.transpose(1, 0, 2, 3, 4)


def add_rows(whole_arr, update, first_row):
    current = lax.dynamic_slice_in_dim(whole_arr, first_row, update.shape[1], 1)
    return lax.dynamic_update_slice_in_dim(whole_arr, current + update, first_row, 1)


def over_rows(left, right):
    return lax.dot_general(
        left, right, (((0,), (0,)), ((), ())), preferred_element_type=jnp.float32
    )


def against(left, right):
    return lax.dot_general(
        left, right, (((1,), (1,)), ((), ())), preferred_element_type=jnp.float32
    )


def unchanged(carried):
    return carried


MESH = pl.DeviceIdType.MESH
AXES = ("z", "x", "y", "c")


class Links:
    def __init__(self, send_sems, recv_sems, line):
        self.send_sems, self.recv_sems, self.line = send_sems, recv_sems, line
        self.z, self.x, self.y, self.c = (lax.axis_index(name) for name in AXES)
        self.slot = self.x * 4 + self.y * 2 + self.c
        self.used = 0
        self.sent = []

    def device(self, to):
        if to == "x":
            return (self.z, 1 - self.x, self.y, self.c)
        if to == "y":
            return (self.z, self.x, 1 - self.y, self.c)
        if to == "c":
            return (self.z, self.x, self.y, 1 - self.c)
        return (self.along(to), self.x, self.y, self.c)

    def along(self, step):
        return lax.rem(self.z + step + self.line, self.line)

    def other(self, to):
        slot = self.slot
        for name in to:
            bit = {"x": 4, "y": 2, "c": 1}[name]
            here = {"x": self.x, "y": self.y, "c": self.c}[name]
            slot = slot + bit * (1 - 2 * here)
        return slot

    def meet(self, targets):
        barrier = pltpu.get_barrier_semaphore()
        for to in targets:
            pl.semaphore_signal(barrier, inc=1, device_id=self.device(to), device_id_type=MESH)
        pl.semaphore_wait(barrier, len(targets))

    def send(self, source, target, to):
        copy = pltpu.make_async_remote_copy(
            src_ref=source,
            dst_ref=target,
            send_sem=self.send_sems.at[self.used],
            recv_sem=self.recv_sems.at[self.used],
            device_id=self.device(to),
            device_id_type=MESH,
        )
        copy.start()
        self.used += 1
        self.sent.append(copy)
        return copy

    def keep(self, source, target):
        copy = pltpu.make_async_copy(source, target, self.send_sems.at[self.used])
        copy.start()
        self.used += 1
        return copy

    def finish(self):
        for copy in self.sent:
            copy.wait_send()


class NearGather:
    def __init__(self, links, slot):
        self.links, self.slot = links, slot
        self.got = {}

    def offer(self, block, source):
        target = self.slot(block, self.links.slot)
        for to in ("x", "y", "c"):
            self.got[block, to] = self.links.send(source, target, to)

    def relay(self, block, first):
        links = self.links
        for to, then in (("x", "y"), ("y", "x")):
            self.got[block, to].wait_recv()
            place = self.slot(block, links.other(to))
            self.got[block, to + "c"] = links.send(place, place, "c")
            if to == first:
                self.got[block, "xy"] = links.send(place, place, then)

    def close(self, block):
        self.got[block, "xy"].wait_recv()
        place = self.slot(block, self.links.other("xy"))
        self.got[block, "xyc"] = self.links.send(place, place, "c")

    def wait(self, blocks):
        for block in blocks:
            for to in ("c", "xc", "yc", "xyc"):
                self.got[block, to].wait_recv()


class RingGather:
    def __init__(self, links, source, place, pieces=4):
        self.links, self.source, self.place, self.pieces = links, source, place, pieces
        self.rows = source.shape[0] // pieces
        self.last = [None] * pieces

    def step(self, number):
        for piece in range(self.pieces):
            way = 1 if piece < self.pieces // 2 else -1
            rows = pl.ds(piece * self.rows, self.rows)
            place = self.place(self.links.along(-way * number), rows)
            if number > 0:
                self.last[piece].wait_recv()
            if number < self.links.line - 1:
                origin = self.source.at[rows] if number == 0 else place
                self.last[piece] = self.links.send(origin, place, way)


def first_kernel(
    line,
    x_ref,
    table_ref,
    pack_ref,
    ff_ref,
    xs_ref,
    weight_ref,
    gain_ref,
    norm_ref,
    query_ref,
    kv_ref,
    peak_ref,
    turn_ref,
    atts_ref,
    ffs_ref,
    x_all,
    tables,
    weights,
    gains,
    norm,
    turns,
    flat,
    query,
    kv,
    peak,
    att,
    send_sems,
    recv_sems,
):
    f32, bf16 = jnp.float32, jnp.bfloat16
    links = Links(send_sems, recv_sems, line)
    far = [1, line - 1] + list(range(2, line - 1))
    links.meet(["x", "y", "c"] + far)
    here = links.slot
    span_len, width = x_ref.shape
    group_len = line * span_len
    rows_each = ff_ref.shape[1]
    q_cols = query.shape[1]
    heads = q_cols // HD
    local = []

    near = NearGather(links, lambda block, place: weights.at[links.along(-block), place])
    far_ff = NearGather(links, lambda block, place: ffs_ref.at[links.along(-block), place])
    ring = RingGather(links, x_ref, lambda block, rows: x_all.at[block, rows])
    own = [
        links.keep(x_ref, x_all.at[links.z]),
        links.keep(table_ref, tables.at[links.z]),
        links.keep(pack_ref.at[links.z], weights.at[links.z, here]),
    ]
    turned = {k: links.send(pack_ref.at[links.along(k)], weights.at[links.z, here], k) for k in far}
    placed = [links.send(table_ref, tables.at[links.z], k) for k in far]
    ring.step(0)
    near.offer(0, pack_ref.at[links.z])
    local.append(links.keep(ff_ref.at[links.z], ffs_ref.at[links.z, here]))
    for k in far:
        turned[k].wait_recv()
        near.offer(k, weights.at[links.along(-k), here])
    ring.step(1)
    for k in [0] + far:
        near.relay(k, "x" if k < line // 2 else "y")
    far_ff.offer(0, ff_ref.at[links.z])
    ring.step(2)
    turned_ff = {k: links.send(ff_ref.at[links.along(k)], ffs_ref.at[links.z, here], k) for k in far}
    for k in [0] + far:
        near.close(k)
    for copy in own:
        copy.wait()
    for copy in placed:
        copy.wait_recv()

    lane = lax.broadcasted_iota(jnp.int32, (span_len, HD), 1)
    for block in range(line):
        table = tables[block]
        swapped = pltpu.roll(table, HD // 2, 1)
        rows = slice(block * span_len, (block + 1) * span_len)
        turns[0, rows] = jnp.where(lane < HD // 2, table, swapped)
        turns[1, rows] = jnp.where(lane < HD // 2, -swapped, table)
    local.append(links.keep(turns, turn_ref))
    near.wait(range(line))
    for index in range(line * 4):
        z, q = divmod(index, 4)
        for which in range(2):
            lanes = slice(which * HD, (which + 1) * HD)
            both = [weights[z, 2 * q + c, rows_each : rows_each + 16, lanes].astype(f32) for c in range(2)]
            gains[which, :, index * HD : (index + 1) * HD] = both[0] + both[1]
    local.append(links.keep(weights, weight_ref))
    local.append(links.keep(gains, gain_ref))
    ring.step(3)
    local.append(links.keep(x_all, xs_ref))

    def normalise(index, carry):
        block = index // (span_len // 16)
        rows = pl.ds(pl.multiple_of(lax.rem(index, span_len // 16) * 16, 16), 16)
        values = x_all[block, rows].astype(f32)
        inverse = lax.rsqrt(jnp.mean(values * values, axis=-1, keepdims=True) + epsilon)
        target = pl.ds(pl.multiple_of(index * 16, 16), 16)
        norm[target] = (values * inverse * gains[0]).astype(bf16)
        return carry

    lax.fori_loop(0, group_len // 16, normalise, 0)
    local.append(links.keep(norm, norm_ref))

    def project(low, high):
        step = group_len // 2
        for part in range(2):
            rows = slice(part * step, (part + 1) * step)
            total = None
            for z in range(line):
                weight = weights[z, :, :rows_each, low:high].reshape(8 * rows_each, high - low)
                term = jnp.dot(
                    norm[rows, z * 8 * rows_each : (z + 1) * 8 * rows_each],
                    weight,
                    preferred_element_type=f32,
                )
                total = term if total is None else total + term
            flat[rows, low:high] = total

    def turn(values, rows):
        return values * turns[0, rows] + pltpu.roll(values, HD // 2, 1) * turns[1, rows]

    project(q_cols, q_cols + 2 * HD)
    for block in range(line):
        rows = slice(block * span_len, (block + 1) * span_len)
        kv[0, rows, :HD] = turn(flat[rows, q_cols : q_cols + HD], rows).astype(bf16)
        kv[0, rows, HD:] = flat[rows, q_cols + HD : q_cols + 2 * HD].astype(bf16)
    exchange = links.send(kv.at[0], kv.at[1], "x")
    project(0, q_cols)
    for block in range(line):
        rows = slice(block * span_len, (block + 1) * span_len)
        for head in range(heads):
            lanes = slice(head * HD, (head + 1) * HD)
            query[rows, lanes] = turn(flat[rows, lanes], rows).astype(bf16)
    local.append(links.keep(query, query_ref))
    exchange.wait_recv()
    local.append(links.keep(kv, kv_ref))

    scale = 1.0 / math.sqrt(HD)
    peak[...] = jnp.zeros_like(peak)

    def attend(head, carry):
        lanes = pl.ds(pl.multiple_of(head * HD, HD), HD)
        for block in range(line):
            rows = slice(block * span_len, (block + 1) * span_len)
            reach = (block + 1) * span_len
            part = query[rows, lanes]
            row = lax.broadcasted_iota(jnp.int32, (span_len, reach), 0) + block * span_len
            column = lax.broadcasted_iota(jnp.int32, (span_len, reach), 1)
            allowed = (column <= row, column < (block + links.x) * span_len)
            scores = []
            for half in range(2):
                score = lax.dot_general(
                    part, kv[half, :reach, :HD], (((1,), (1,)), ((), ())), preferred_element_type=f32
                )
                scores.append(jnp.where(allowed[half], score * scale, -1e30))
            top = jnp.maximum(
                jnp.max(scores[0], axis=-1, keepdims=True), jnp.max(scores[1], axis=-1, keepdims=True)
            )
            total, mixed = None, None
            for half in range(2):
                weight = jnp.exp(scores[half] - top)
                count = jnp.sum(weight, axis=-1, keepdims=True)
                term = jnp.dot(weight.astype(bf16), kv[half, :reach, HD:], preferred_element_type=f32)
                total = count if total is None else total + count
                mixed = term if mixed is None else mixed + term
            att[rows, lanes] = (mixed / total).astype(bf16)
            spot = lax.broadcasted_iota(jnp.int32, (span_len, HD), 1) == head
            peak[rows] = jnp.where(spot, top + jnp.log(total), peak[rows])
        return carry

    lax.fori_loop(0, heads, attend, 0)
    local.append(links.keep(peak, peak_ref))

    def place(block, rows):
        return atts_ref.at[rows, pl.ds(pl.multiple_of(block * q_cols, q_cols), q_cols)]

    att_ring = RingGather(links, att, place)
    local.append(links.keep(att, place(links.z, pl.ds(0, group_len))))
    att_ring.step(0)
    for k in far:
        turned_ff[k].wait_recv()
        far_ff.offer(k, ffs_ref.at[links.along(-k), here])
    far_ff.relay(0, "x")
    far_ff.close(0)
    far_ff.relay(far[0], "x")
    att_ring.step(1)
    for k in far[1:]:
        far_ff.relay(k, "x" if k < line // 2 else "y")
    att_ring.step(2)
    for k in far:
        far_ff.close(k)
    att_ring.step(3)
    far_ff.wait(range(line))
    links.finish()
    for copy in local:
        copy.wait()


def add_rows_of(target, values, count):
    def add(index, carry):
        rows = pl.ds(pl.multiple_of(index * 16, 16), 16)
        target[rows] = target[rows] + values[rows]
        return carry

    lax.fori_loop(0, count // 16, add, 0)


class NearSum:
    def __init__(self, links, source, own, from_core, from_first, from_second, first, in_place=False):
        self.links, self.source, self.own, self.first = links, source, own, first
        self.in_place = in_place
        self.from_core, self.from_first, self.from_second = from_core, from_first, from_second

    def start(self):
        links = self.links
        if not self.in_place:
            self.local = links.keep(self.source(links.c), self.own)
        self.copy = links.send(self.source(1 - links.c), self.from_core, "c")

    def add(self, target, values):
        add_rows_of(target, values, target.shape[0])

    def core_done(self):
        links = self.links
        self.copy.wait_recv()
        if not self.in_place:
            self.local.wait()
        for x in range(2):
            for y in range(2):
                self.add(self.own.at[x, y], self.from_core.at[x, y])
        if self.first == "x":
            self.copy = links.send(self.own.at[1 - links.x], self.from_first, "x")
        else:
            self.copy = links.send(self.own.at[:, 1 - links.y], self.from_first, "y")

    def first_done(self):
        links = self.links
        self.copy.wait_recv()
        for other in range(2):
            place = (links.x, other) if self.first == "x" else (other, links.y)
            self.add(self.own.at[place], self.from_first.at[other])
        if self.first == "x":
            self.copy = links.send(self.own.at[links.x, 1 - links.y], self.from_second, "y")
        else:
            self.copy = links.send(self.own.at[1 - links.x, links.y], self.from_second, "x")

    def second_done(self):
        self.copy.wait_recv()
        total = self.own.at[self.links.x, self.links.y]
        self.add(total, self.from_second)
        return total


def sum_space(blocks, rows, columns):
    shape = (rows, columns)
    return [
        pltpu.VMEM((blocks, 2, 2) + shape, jnp.bfloat16),
        pltpu.VMEM((blocks, 2, 2) + shape, jnp.bfloat16),
        pltpu.VMEM((blocks, 2) + shape, jnp.bfloat16),
        pltpu.VMEM((blocks,) + shape, jnp.bfloat16),
    ]


class RingSum:
    def __init__(self, links, parts, total, got, pieces=4):
        self.links, self.parts, self.total, self.got = links, parts, total, got
        self.pieces, self.last = pieces, [None] * pieces
        self.rows = parts.shape[1] // pieces

    def step(self, number):
        links = self.links
        for piece in range(self.pieces):
            way = 1 if piece < self.pieces // 2 else -1
            block = links.along(-way * (number + 1))
            where = pl.ds(piece * self.rows, self.rows)
            if number == 0:
                source = self.parts.at[block, where]
            else:
                self.last[piece].wait_recv()
                total = self.got[number - 1, where].astype(jnp.float32) + self.parts[
                    block, where
                ].astype(jnp.float32)
                if number == links.line - 1:
                    self.total[where] = total
                    continue
                self.parts[block, where] = total.astype(self.parts.dtype)
                source = self.parts.at[block, where]
            self.last[piece] = links.send(source, self.got.at[number, where], way)


def link_call(kernel, collective_id, copies, shapes, arguments, spaces=None, scratch=(), vmem=16):
    any_space = pl.BlockSpec(memory_space=pl.ANY)
    near_space = pl.BlockSpec(memory_space=pltpu.VMEM)
    many = isinstance(shapes, tuple)
    if spaces is None:
        spaces = "h" * (len(arguments) + (len(shapes) if many else 1))
    specs = [near_space if space == "v" else any_space for space in spaces]
    return pl.pallas_call(
        kernel,
        out_shape=shapes,
        in_specs=specs[: len(arguments)],
        out_specs=tuple(specs[len(arguments) :]) if many else specs[-1],
        scratch_shapes=list(scratch)
        + [pltpu.SemaphoreType.DMA((copies,)), pltpu.SemaphoreType.DMA((copies,))],
        compiler_params=pltpu.CompilerParams(
            collective_id=collective_id, has_side_effects=True, vmem_limit_bytes=vmem * 2**20
        ),
    )(*arguments)


def forward_call(tokens, table, pack, pack_ff, line):
    span_len, width = tokens.shape
    group_len = line * span_len
    rows_each = pack_ff.shape[1]
    qkv_cols = pack.shape[2]
    q_cols = qkv_cols - 2 * HD
    f32, bf16 = jnp.float32, jnp.bfloat16
    outs = (
        ((line, span_len, width), bf16),
        ((line, 8) + pack.shape[1:], bf16),
        ((2, 16, width), f32),
        ((group_len, width), bf16),
        ((group_len, q_cols), bf16),
        ((2, group_len, 2 * HD), bf16),
        ((group_len, HD), f32),
        ((2, group_len, HD), f32),
        ((group_len, line * q_cols), bf16),
        ((line, 8) + pack_ff.shape[1:], bf16),
    )
    return link_call(
        functools.partial(first_kernel, line),
        0,
        176,
        tuple(jax.ShapeDtypeStruct(*out) for out in outs),
        (tokens, table, pack, pack_ff),
        scratch=[
            pltpu.VMEM((line, span_len, width), bf16),
            pltpu.VMEM((line,) + table.shape, f32),
            pltpu.VMEM((line, 8) + pack.shape[1:], bf16),
            pltpu.VMEM((2, 16, width), f32),
            pltpu.VMEM((group_len, width), bf16),
            pltpu.VMEM((2, group_len, HD), f32),
            pltpu.VMEM((group_len, qkv_cols), f32),
            pltpu.VMEM((group_len, q_cols), bf16),
            pltpu.VMEM((2, group_len, 2 * HD), bf16),
            pltpu.VMEM((group_len, HD), f32),
            pltpu.VMEM((group_len, q_cols), bf16),
        ],
        vmem=48,
    )


def mlp_kernel(
    line,
    cuts,
    keep_ref,
    gain_ref,
    mix_ref,
    xs_ref,
    atts_ref,
    out_ref,
    ff_ref,
    down_ref,
    middle_ref,
    total_ref,
    mixed_total_ref,
    sum_ref,
    grad_ff_ref,
    big,
    ff,
    down,
    norm,
    parts,
    mixed,
    gate_up,
    hidden,
    both_grad,
    got,
    mixed_parts,
    mixed_got,
    *scratch,
):
    f32, bf16 = jnp.float32, jnp.bfloat16
    space, (send_sems, recv_sems) = scratch[:-2], scratch[-2:]
    links = Links(send_sems, recv_sems, line)
    links.meet(["x", "y", "c", 1, line - 1])
    span_len, width = mix_ref.shape
    group_len = line * span_len
    ff_cols = hidden.shape[1]
    chunk = 2 * HD
    stay = links.keep(mix_ref, mixed.at[links.z])
    mix_ring = RingGather(links, mix_ref, lambda block, rows: mixed.at[block, rows])
    mix_ring.step(0)
    early = [
        links.keep(out_ref, big),
        links.keep(atts_ref, norm),
        links.keep(xs_ref, parts),
    ]
    late = [links.keep(ff_ref, ff), links.keep(down_ref, down)]
    ring = RingSum(links, parts, total_ref, got)
    mixed_ring = RingSum(links, mixed_parts, mixed_total_ref, mixed_got)
    items = []
    for index, (low, high) in enumerate(cuts):
        rows = pl.ds(low, high - low)
        core, first, second = space[3 * index : 3 * index + 3]
        items.append(
            NearSum(
                links,
                lambda c, rows=rows: big.at[:, :, c, rows],
                big.at[:, :, links.c, rows],
                core.at[0],
                first.at[0],
                second.at[0],
                "xy"[index % 2],
                True,
            )
        )
    for copy in early:
        copy.wait()

    half = group_len // 2
    out_rows = width // 8
    for part in range(2):
        low = part * half
        for column in range(4):
            lanes = slice(column * width // 4, (column + 1) * width // 4)
            value = None
            for k in range(8):
                term = jnp.dot(
                    norm[low : low + half, k * out_rows : (k + 1) * out_rows],
                    big[k // 4, k // 2 % 2, k % 2, :, lanes],
                    preferred_element_type=f32,
                )
                value = term if value is None else value + term
            gate_up[:half, lanes] = value * keep_ref[0:1, 0:1]

        def normalise(index, carry, low=low):
            block = (low // 16 + index) // (span_len // 16)
            rows = pl.ds(pl.multiple_of(index * 16, 16), 16)
            inside = pl.ds(pl.multiple_of(lax.rem(index, span_len // 16) * 16, 16), 16)
            values = parts[block, inside].astype(f32) + gate_up[rows, :width]
            gate_up[rows, :width] = values
            inverse = lax.rsqrt(jnp.mean(values * values, axis=-1, keepdims=True) + epsilon)
            target = pl.ds(pl.multiple_of(low + index * 16, 16), 16)
            norm[target] = (values * inverse * gain_ref[1]).astype(bf16)
            return carry

        lax.fori_loop(0, half // 16, normalise, 0)

        @pl.when(links.z // (line // 2) == part)
        def _():
            where = pl.multiple_of(lax.rem(links.z, line // 2) * span_len, span_len)
            middle_ref[...] = gate_up[pl.ds(where, span_len), :width]

    mix_ring.step(1)
    for copy in late:
        copy.wait()

    def forward(low, size):
        gates, ups = pl.ds(low, size), pl.ds(low + ff_cols, size)
        gate = jnp.dot(norm[...], ff[:, gates], preferred_element_type=f32)
        gate_up[:, gates] = gate
        swish = gate * jax.nn.sigmoid(gate)
        up = jnp.dot(norm[...], ff[:, ups], preferred_element_type=f32)
        gate_up[:, ups] = up
        hidden[:, gates] = (swish * up).astype(bf16)

    def backward(low, size):
        gates, ups = pl.ds(low, size), pl.ds(low + ff_cols, size)
        grad = lax.dot_general(
            mixed[...].reshape(group_len, width),
            down[gates],
            (((1,), (1,)), ((), ())),
            preferred_element_type=f32,
        )
        gate, up = gate_up[:, gates], gate_up[:, ups]
        sigmoid = jax.nn.sigmoid(gate)
        both_grad[:, gates] = (grad * up * sigmoid * (1.0 + gate * (1.0 - sigmoid))).astype(bf16)
        both_grad[:, ups] = (grad * (gate * sigmoid)).astype(bf16)

    def over_chunks(work, extent):
        def one(index, carry):
            work(pl.multiple_of(index * chunk, chunk), chunk)
            return carry

        lax.fori_loop(0, extent // chunk, one, 0)
        if extent % chunk:
            work(extent // chunk * chunk, extent % chunk)

    over_chunks(forward, ff_cols)
    mix_ring.step(2)

    def mixed_part(low, size):
        lanes = pl.ds(low, size)
        value = jnp.dot(hidden[...], down[:, lanes], preferred_element_type=f32).astype(bf16)
        mixed_parts[:, :, lanes] = value.reshape(line, span_len, size)

    over_chunks(mixed_part, width)
    mixed_ring.step(0)
    stay.wait()
    mix_ring.step(3)
    over_chunks(backward, ff_cols)

    def norm_part(low, size):
        value = lax.dot_general(
            both_grad[...], ff[pl.ds(low, size)], (((1,), (1,)), ((), ())), preferred_element_type=f32
        ).astype(bf16)
        parts[:, :, pl.ds(low, size)] = value.reshape(line, span_len, size)

    over_chunks(norm_part, width)
    ring.step(0)
    mixed_ring.step(1)
    hidden_rows = hidden[...].T

    def down_part(low, size):
        lanes = pl.ds(low, size)
        value = jnp.dot(
            hidden_rows,
            mixed[:, :, lanes].reshape(group_len, size),
            preferred_element_type=f32,
        ).astype(bf16)
        big[:, :, :, : cuts[-1][1], lanes] = value.reshape(2, 2, 2, cuts[-1][1], size)

    over_chunks(down_part, width)
    for item in items:
        item.start()
    ring.step(1)
    sent = []
    block_rows = width // line
    for z in range(line):
        norm_rows = norm[:, z * block_rows : (z + 1) * block_rows].T

        def ff_part(low, size, z=z, norm_rows=norm_rows):
            lanes = pl.ds(low, size)
            value = jnp.dot(norm_rows, both_grad[:, lanes], preferred_element_type=f32)
            ff[z * block_rows : (z + 1) * block_rows, lanes] = value.astype(bf16)

        over_chunks(ff_part, 2 * ff_cols)
        rows = pl.ds(z * block_rows, block_rows)
        sent.append(links.keep(ff.at[rows], grad_ff_ref.at[rows]))
        if z == 0:
            mixed_ring.step(2)
            for item in items:
                item.core_done()
        if z == 1:
            ring.step(2)
    for item in items:
        item.first_done()
    ring.step(3)
    mixed_ring.step(3)
    for item, (low, high) in zip(items, cuts):
        sum_ref[low:high] = item.second_done()[...]
    links.finish()
    for copy in sent:
        copy.wait()


def mlp_call(keep, gains, mixed, x_blocks, attended, out_w, ff_w, down_w, line):
    f32, bf16 = jnp.float32, jnp.bfloat16
    span_len, width = mixed.shape
    group_len = line * span_len
    ff_rows, both_cols = down_w.shape[0], ff_w.shape[1]
    rows = ff_rows // 8
    half = (rows // 2 + 15) // 16 * 16
    cuts = ((0, half), (half, rows))
    blocks = (line, span_len, width)
    token = jax.ShapeDtypeStruct((span_len, width), f32)
    return link_call(
        functools.partial(mlp_kernel, line, cuts),
        2,
        96,
        (
            token,
            token,
            token,
            jax.ShapeDtypeStruct((rows, width), bf16),
            jax.ShapeDtypeStruct(ff_w.shape, bf16),
        ),
        (keep, gains, mixed, x_blocks, attended, out_w.reshape(2, 2, 2, width // 8, width), ff_w, down_w),
        "vvhhhhhh" + "vvvvh",
        [
            pltpu.VMEM((2, 2, 2, width // 8, width), bf16),
            pltpu.VMEM(ff_w.shape, bf16),
            pltpu.VMEM(down_w.shape, bf16),
            pltpu.VMEM((group_len, width), bf16),
            pltpu.VMEM(blocks, bf16),
            pltpu.VMEM(blocks, bf16),
            pltpu.VMEM((group_len, both_cols), f32),
            pltpu.VMEM((group_len, ff_rows), bf16),
            pltpu.VMEM((group_len, both_cols), bf16),
            pltpu.VMEM((line - 1, span_len, width), bf16),
            pltpu.VMEM(blocks, bf16),
            pltpu.VMEM((line - 1, span_len, width), bf16),
        ]
        + sum((sum_space(1, high - low, width)[1:] for low, high in cuts), []),
        vmem=63,
    )


def backward_kernel(
    line,
    up_ref,
    middle_ref,
    norm_grad_ref,
    keep_ref,
    gain_ref,
    query,
    kv,
    peak,
    turns,
    out_ref,
    atts_ref,
    weight_ref,
    norm_ref,
    ff_ref,
    middle_grad_ref,
    total_ref,
    ffs_ref,
    outs_ref,
    qkvs_ref,
    big,
    slim,
    norm,
    own_rows,
    own_columns,
    branch,
    own_grad,
    att_grad,
    query_back,
    kv_back,
    kv_out,
    kv_in,
    flat,
    parts,
    *scratch,
):
    f32, bf16 = jnp.float32, jnp.bfloat16
    send_sems, recv_sems = scratch[-2:]
    got, sums = scratch[0], scratch[1:-2]
    links = Links(send_sems, recv_sems, line)
    far = [1, line - 1] + list(range(2, line - 1))
    order = far + [0]
    links.meet(["x", "y", "c"] + far)
    span_len, width = up_ref.shape
    group_len = line * span_len
    q_cols = query.shape[1]
    heads = q_cols // HD
    rows_z = width // line
    rows_each = rows_z // 8
    scale = 1.0 / math.sqrt(HD)

    def lanes_of(block):
        return pl.ds(pl.multiple_of(block * q_cols, q_cols), q_cols)

    here = pl.ds(pl.multiple_of(links.z * span_len, span_len), span_len)
    loads = [
        links.keep(out_ref, big),
        links.keep(atts_ref.at[here], own_rows),
        links.keep(atts_ref.at[:, lanes_of(links.z)], own_columns),
        links.keep(norm_ref, norm),
        links.keep(weight_ref.at[:, :, :, :, pl.ds(0, slim.shape[4])], slim),
    ]
    ring = RingSum(links, parts, total_ref, got)

    def items_of(source, space, in_place):
        items = []
        for index, k in enumerate(order):
            block = links.along(k)
            own = source.at[block, :, :, links.c] if in_place else space[0].at[index]
            core, first, second = space[-3:]
            items.append(
                NearSum(
                    links,
                    lambda c, block=block: source.at[block, :, :, c],
                    own,
                    core.at[index],
                    first.at[index],
                    second.at[index],
                    "xy"[index % 2],
                    in_place,
                )
            )
        return items

    ff_items = items_of(ff_ref, sums[:4], False)
    out_items = items_of(big, sums[4:7], True)
    qkv_items = items_of(slim, sums[7:], True)
    arrived, local = [], []

    def turn(items, target, low, high):
        for item, k in list(zip(items, order))[low:high]:
            total = item.second_done()
            if k == 0:
                local.append(links.keep(total, target.at[links.z]))
            else:
                arrived.append(links.send(total, target.at[links.z], k))

    def core_done(items, low, high):
        for item in items[low:high]:
            item.core_done()

    def first_done(items, low, high):
        for item in items[low:high]:
            item.first_done()

    half = line // 2
    for item in ff_items:
        item.start()

    def d_middle(index, carry):
        rows = pl.ds(pl.multiple_of(index * 16, 16), 16)
        middle = middle_ref[rows]
        inverse = lax.rsqrt(jnp.mean(middle * middle, axis=-1, keepdims=True) + epsilon)
        scaled = gain_ref[1] * norm_grad_ref[rows]
        grad = (
            up_ref[rows]
            + inverse * scaled
            - middle
            * (inverse * inverse * inverse)
            * jnp.mean(scaled * middle, axis=-1, keepdims=True)
        )
        middle_grad_ref[rows] = grad
        branch[rows] = (grad * keep_ref[0:1, 0:1]).astype(bf16)
        return carry

    lax.fori_loop(0, span_len // 16, d_middle, 0)
    for copy in loads:
        copy.wait()
    for z in range(line):
        weight = big[z].reshape(rows_z, width)
        own_grad[:, z * rows_z : (z + 1) * rows_z] = lax.dot_general(
            branch[...], weight, (((1,), (1,)), ((), ())), preferred_element_type=f32
        ).astype(bf16)
    turned = [links.send(own_grad.at[:, lanes_of(links.along(k))], att_grad.at[here], k) for k in far]
    stayed = links.keep(own_grad.at[:, lanes_of(links.z)], att_grad.at[here])
    core_done(ff_items, 0, half)
    for z in range(line):
        for part in range(4):
            columns = slice(part * width // 4, (part + 1) * width // 4)
            grad = lax.dot_general(
                own_rows[:, z * rows_z : (z + 1) * rows_z],
                branch[:, columns],
                (((0,), (0,)), ((), ())),
                preferred_element_type=f32,
            )
            big[z, :, :, :, :, columns] = grad.astype(bf16).reshape(2, 2, 2, rows_each, width // 4)
    for item in out_items:
        item.start()
    core_done(ff_items, half, line)
    kv_back[...] = jnp.zeros_like(kv_back)
    for copy in turned:
        copy.wait_recv()
    stayed.wait()

    def attend_back(head, carry):
        lanes = pl.ds(pl.multiple_of(head * HD, HD), HD)
        for block in range(line):
            rows = slice(block * span_len, (block + 1) * span_len)
            reach = (block + 1) * span_len
            part, grad = query[rows, lanes], att_grad[rows, lanes]
            row = lax.broadcasted_iota(jnp.int32, (span_len, reach), 0) + block * span_len
            column = lax.broadcasted_iota(jnp.int32, (span_len, reach), 1)
            allowed = (column <= row, column < (block + links.x) * span_len)
            spot = lax.broadcasted_iota(jnp.int32, (span_len, HD), 1) == head
            top = jnp.sum(jnp.where(spot, peak[rows], 0.0), axis=-1, keepdims=True)
            delta = jnp.sum(
                grad.astype(f32) * own_columns[rows, lanes].astype(f32), axis=-1, keepdims=True
            )
            total = None
            for side in range(2):
                keys, values = kv[side, :reach, :HD], kv[side, :reach, HD:]
                score = lax.dot_general(
                    part, keys, (((1,), (1,)), ((), ())), preferred_element_type=f32
                )
                weight = jnp.where(allowed[side], jnp.exp(score * scale - top), 0.0)
                weight_grad = lax.dot_general(
                    grad, values, (((1,), (1,)), ((), ())), preferred_element_type=f32
                )
                score_grad = (weight * (weight_grad - delta)).astype(bf16)
                term = jnp.dot(score_grad, keys, preferred_element_type=f32)
                total = term if total is None else total + term
                kv_back[side, :reach, :HD] += lax.dot_general(
                    score_grad, part, (((0,), (0,)), ((), ())), preferred_element_type=f32
                )
                kv_back[side, :reach, HD:] += lax.dot_general(
                    weight.astype(bf16), grad, (((0,), (0,)), ((), ())), preferred_element_type=f32
                )
            query_back[rows, lanes] = total * scale
        return carry

    lax.fori_loop(0, heads, attend_back, 0)
    kv_out[:, :HD] = (kv_back[1, :, :HD] * scale).astype(bf16)
    kv_out[:, HD:] = kv_back[1, :, HD:].astype(bf16)
    exchange = links.send(kv_out, kv_in, "x")

    def turn_back(values, rows):
        return values * turns[0, rows] - pltpu.roll(values, HD // 2, 1) * turns[1, rows]

    for block in range(line):
        rows = slice(block * span_len, (block + 1) * span_len)
        for head in range(heads):
            lanes = slice(head * HD, (head + 1) * HD)
            flat[rows, lanes] = turn_back(query_back[rows, lanes], rows).astype(bf16)
    first_done(ff_items, 0, half)
    exchange.wait_recv()
    for block in range(line):
        rows = slice(block * span_len, (block + 1) * span_len)
        key_grad = kv_back[0, rows, :HD] * scale + kv_in[rows, :HD].astype(f32)
        flat[rows, q_cols : q_cols + HD] = turn_back(key_grad, rows).astype(bf16)
        value_grad = kv_back[0, rows, HD:] + kv_in[rows, HD:].astype(f32)
        flat[rows, q_cols + HD :] = value_grad.astype(bf16)
    for z in range(line):
        weight = slim[z].reshape(rows_z, flat.shape[1])
        part = lax.dot_general(
            flat[...], weight, (((1,), (1,)), ((), ())), preferred_element_type=f32
        ).astype(bf16)
        for block in range(line):
            parts[block, :, z * rows_z : (z + 1) * rows_z] = part[
                block * span_len : (block + 1) * span_len
            ]
    ring.step(0)
    for z in range(line):
        grad = lax.dot_general(
            norm[:, z * rows_z : (z + 1) * rows_z],
            flat[...],
            (((0,), (0,)), ((), ())),
            preferred_element_type=f32,
        )
        slim[z] = grad.astype(bf16).reshape(2, 2, 2, rows_each, flat.shape[1])
    for item in qkv_items:
        item.start()
    core_done(out_items, 0, half)
    first_done(ff_items, half, line)
    turn(ff_items, ffs_ref, 0, half)
    ring.step(1)
    core_done(out_items, half, line)
    first_done(out_items, 0, half)
    turn(ff_items, ffs_ref, half, line)
    ring.step(2)
    core_done(qkv_items, 0, line)
    first_done(out_items, half, line)
    turn(out_items, outs_ref, 0, half)
    ring.step(3)
    first_done(qkv_items, 0, half)
    turn(out_items, outs_ref, half, line)
    first_done(qkv_items, half, line)
    turn(qkv_items, qkvs_ref, 0, line)
    for copy in arrived:
        copy.wait_recv()
    links.finish()
    for copy in local:
        copy.wait()


def backward_call(small, out_w, attended, weights, norm, grad_ff, line):
    f32, bf16 = jnp.float32, jnp.bfloat16
    span_len, width = small[0].shape
    group_len = line * span_len
    query = small[5]
    q_cols, rows_each, qkv_cols = query.shape[1], width // line // 8, weights.shape[3]
    weights = weights.reshape(line, 2, 2, 2, -1, qkv_cols)
    wide = (line, 2, 2, 2, rows_each, width)
    slim = (line, 2, 2, 2, rows_each, qkv_cols)
    out_space = sum_space(line, rows_each, width)[1:]
    qkv_space = sum_space(line, rows_each, qkv_cols)[1:]
    token = jax.ShapeDtypeStruct((span_len, width), f32)
    return link_call(
        functools.partial(backward_kernel, line),
        4,
        160,
        (token, token)
        + tuple(
            jax.ShapeDtypeStruct((line, rows_each, columns), bf16)
            for columns in (grad_ff.shape[5], width, qkv_cols)
        ),
        small + (out_w.reshape(wide), attended, weights, norm, grad_ff),
        "v" * 9 + "hhhhh" + "vvhhh",
        [
            pltpu.VMEM(wide, bf16),
            pltpu.VMEM(slim, bf16),
            pltpu.VMEM((group_len, width), bf16),
            pltpu.VMEM((span_len, width), bf16),
            pltpu.VMEM((group_len, q_cols), bf16),
            pltpu.VMEM((span_len, width), bf16),
            pltpu.VMEM((span_len, width), bf16),
            pltpu.VMEM((group_len, q_cols), bf16),
            pltpu.VMEM((group_len, q_cols), f32),
            pltpu.VMEM((2, group_len, 2 * HD), f32),
            pltpu.VMEM((group_len, 2 * HD), bf16),
            pltpu.VMEM((group_len, 2 * HD), bf16),
            pltpu.VMEM((group_len, qkv_cols), bf16),
            pltpu.VMEM((line, span_len, width), bf16),
        ]
        + [pltpu.VMEM((line - 1, span_len, width), bf16)]
        + sum_space(line, rows_each, grad_ff.shape[5])
        + out_space
        + qkv_space,
        vmem=63,
    )


def general_body(
    tokens,
    attn_gain,
    w_query,
    w_key,
    w_value,
    w_out,
    mlp_gain,
    w_gate,
    w_up,
    w_down,
    keep_mask,
    group_ids,
    positions,
    exit_scale,
    out_grad,
):
    seq_count, span_len, model_width = tokens.shape
    kv_heads = KVH
    head_dim = HD
    head_count = HEADS
    group_size = head_count // kv_heads
    row_count = seq_count * span_len
    stripe = group_size * span_len
    wide_count = lax.axis_size("wide")
    wide_place = lax.axis_index("wide")
    full_len = span_len * wide_count
    score_scale = 1.0 / math.sqrt(head_dim)
    gain_one, query_w, key_w, value_w, out_w = (
        lax.all_gather(attn_gain, ("wide", "narrow"), axis=0, tiled=True),
        lax.all_gather(w_query, ("wide", "narrow"), axis=0, tiled=True),
        lax.all_gather(w_key, ("wide", "narrow"), axis=0, tiled=True),
        lax.all_gather(w_value, ("wide", "narrow"), axis=0, tiled=True),
        lax.all_gather(w_out, ("wide", "narrow"), axis=0, tiled=True),
    )
    inputs = tokens.astype(jnp.float32).reshape(row_count, model_width)
    token_pos = positions.reshape(row_count)
    keep_rows = jnp.repeat(keep_mask.astype(jnp.float32), span_len)[:, None]
    inverse_one = lax.rsqrt(jnp.mean(inputs * inputs, axis=-1, keepdims=True) + epsilon)
    first_norm = (inputs * inverse_one * gain_one.astype(jnp.float32)).astype(jnp.bfloat16)
    query_pre = jnp.dot(first_norm, query_w, preferred_element_type=jnp.float32).reshape(
        row_count, head_count, head_dim
    )
    key_pre = jnp.dot(first_norm, key_w, preferred_element_type=jnp.float32).reshape(
        row_count, kv_heads, head_dim
    )
    query_rows = rotate(query_pre, token_pos, 1.0).astype(jnp.bfloat16)
    key_heads = (
        rotate(key_pre, token_pos, 1.0)
        .astype(jnp.bfloat16)
        .reshape(seq_count, span_len, kv_heads * head_dim)
    )
    value_heads = (
        jnp.dot(first_norm, value_w, preferred_element_type=jnp.float32)
        .astype(jnp.bfloat16)
        .reshape(seq_count, span_len, kv_heads * head_dim)
    )
    queries = (
        query_rows.reshape(seq_count, span_len, kv_heads, group_size, head_dim)
        .transpose(0, 2, 3, 1, 4)
        .reshape(seq_count, kv_heads, stripe, head_dim)
    )
    query_index = wide_place * span_len + jnp.arange(stripe, dtype=jnp.int32) % span_len
    last_query = wide_place * span_len + span_len - 1

    def block_scores(key_block, key_first):
        scores = (
            jnp.einsum("skrd,sjkd->skrj", queries, key_block, preferred_element_type=jnp.float32)
            * score_scale
        )
        key_index = key_first + jnp.arange(key_block.shape[1], dtype=jnp.int32)
        allowed = key_index[None, :] <= query_index[:, None]
        return (scores, allowed)

    start_forward = (
        jnp.full((seq_count, kv_heads, stripe), -1e30, jnp.float32),
        jnp.zeros((seq_count, kv_heads, stripe), jnp.float32),
        jnp.zeros((seq_count, kv_heads, stripe, head_dim), jnp.float32),
    )
    running = start_forward
    pieces = (
        lax.all_gather(key_heads, "wide", axis=1, tiled=True),
        lax.all_gather(value_heads, "wide", axis=1, tiled=True),
    )
    key_blocks = split_blocks(pieces[0], seq_count, kv_heads, head_dim)
    value_blocks = split_blocks(pieces[1], seq_count, kv_heads, head_dim)
    block_len = key_blocks.shape[2]

    def advance(carried, block_item):
        key_block, value_block, block_index = block_item
        key_first = block_index * block_len

        def compute_block(current):
            run_max, run_sum, run_acc = current
            scores, allowed = block_scores(key_block, key_first)
            scores = jnp.where(allowed, scores, -1e30)
            new_max = jnp.maximum(run_max, jnp.max(scores, axis=-1))
            factor = jnp.exp(run_max - new_max)
            weights = jnp.where(allowed, jnp.exp(scores - new_max[..., None]), 0.0)
            new_sum = run_sum * factor + jnp.sum(weights, axis=-1)
            new_acc = run_acc * factor[..., None] + jnp.einsum(
                "skrj,sjkd->skrd",
                weights.astype(jnp.bfloat16),
                value_block,
                preferred_element_type=jnp.float32,
            )
            return (new_max, new_sum, new_acc)

        return (lax.cond(key_first <= last_query, compute_block, unchanged, carried), None)

    running, _ = lax.scan(
        advance,
        running,
        (key_blocks, value_blocks, jnp.arange(key_blocks.shape[0], dtype=jnp.int32)),
    )
    run_max, run_sum, run_acc = running
    attended = run_acc / run_sum[..., None]
    log_total = run_max + jnp.log(run_sum)
    attended_rows = (
        attended.reshape(seq_count, kv_heads, group_size, span_len, head_dim)
        .transpose(0, 3, 1, 2, 4)
        .reshape(row_count, head_count * head_dim)
        .astype(jnp.bfloat16)
    )
    middle = inputs + keep_rows * jnp.dot(attended_rows, out_w, preferred_element_type=jnp.float32)
    gain_two, gate_w, up_w, down_w = (
        lax.all_gather(mlp_gain, ("wide", "narrow"), axis=0, tiled=True),
        lax.all_gather(w_gate, ("wide", "narrow"), axis=0, tiled=True),
        lax.all_gather(w_up, ("wide", "narrow"), axis=0, tiled=True),
        lax.all_gather(w_down, ("wide", "narrow"), axis=0, tiled=True),
    )
    inverse_two = lax.rsqrt(jnp.mean(middle * middle, axis=-1, keepdims=True) + epsilon)
    second_norm = (middle * inverse_two * gain_two.astype(jnp.float32)).astype(jnp.bfloat16)
    gate_value = jnp.dot(second_norm, gate_w, preferred_element_type=jnp.float32)
    up_value = jnp.dot(second_norm, up_w, preferred_element_type=jnp.float32)
    gate_sigmoid = jax.nn.sigmoid(gate_value)
    swish_value = gate_value * gate_sigmoid
    hidden = (swish_value * up_value).astype(jnp.bfloat16)
    output = (
        middle + keep_rows * jnp.dot(hidden, down_w, preferred_element_type=jnp.float32)
    ).astype(jnp.bfloat16)
    group_match = (
        group_ids.reshape(row_count)[:, None]
        == jnp.arange(exit_scale.shape[0], dtype=jnp.int32)[None, :]
    )
    token_scale = jnp.sum(jnp.where(group_match, exit_scale[None, :], 0.0), axis=1, keepdims=True)
    upstream = out_grad.astype(jnp.float32).reshape(row_count, model_width) * token_scale
    gain_two, gate_w, up_w, down_w = (
        lax.all_gather(mlp_gain, ("wide", "narrow"), axis=0, tiled=True),
        lax.all_gather(w_gate, ("wide", "narrow"), axis=0, tiled=True),
        lax.all_gather(w_up, ("wide", "narrow"), axis=0, tiled=True),
        lax.all_gather(w_down, ("wide", "narrow"), axis=0, tiled=True),
    )
    mixed_grad = (keep_rows * upstream).astype(jnp.bfloat16)
    grad_down = over_rows(hidden, mixed_grad)
    hidden_grad = against(mixed_grad, down_w)
    gate_grad = (
        hidden_grad * up_value * gate_sigmoid * (1.0 + gate_value * (1.0 - gate_sigmoid))
    ).astype(jnp.bfloat16)
    up_grad = (hidden_grad * swish_value).astype(jnp.bfloat16)
    grad_gate = over_rows(second_norm, gate_grad)
    grad_up = over_rows(second_norm, up_grad)
    norm_grad = against(gate_grad, gate_w) + against(up_grad, up_w)
    grad_gain_two = jnp.sum(norm_grad * middle * inverse_two, axis=0)
    scaled_two = gain_two.astype(jnp.float32) * norm_grad
    middle_grad = (
        upstream
        + inverse_two * scaled_two
        - middle
        * (inverse_two * inverse_two * inverse_two)
        * jnp.mean(scaled_two * middle, axis=-1, keepdims=True)
    )
    gain_two_share, gate_share, up_share, down_share = (
        lax.psum_scatter(grad_gain_two, ("wide", "narrow"), scatter_dimension=0, tiled=True),
        lax.psum_scatter(grad_gate, ("wide", "narrow"), scatter_dimension=0, tiled=True),
        lax.psum_scatter(grad_up, ("wide", "narrow"), scatter_dimension=0, tiled=True),
        lax.psum_scatter(grad_down, ("wide", "narrow"), scatter_dimension=0, tiled=True),
    )
    gain_one, query_w, key_w, value_w, out_w = (
        lax.all_gather(attn_gain, ("wide", "narrow"), axis=0, tiled=True),
        lax.all_gather(w_query, ("wide", "narrow"), axis=0, tiled=True),
        lax.all_gather(w_key, ("wide", "narrow"), axis=0, tiled=True),
        lax.all_gather(w_value, ("wide", "narrow"), axis=0, tiled=True),
        lax.all_gather(w_out, ("wide", "narrow"), axis=0, tiled=True),
    )
    branch_grad = (keep_rows * middle_grad).astype(jnp.bfloat16)
    grad_out = over_rows(attended_rows, branch_grad)
    attended_grad = against(branch_grad, out_w).astype(jnp.bfloat16)
    grouped_grad = (
        attended_grad.reshape(seq_count, span_len, kv_heads, group_size, head_dim)
        .transpose(0, 2, 3, 1, 4)
        .reshape(seq_count, kv_heads, stripe, head_dim)
    )
    row_delta = jnp.sum(grouped_grad.astype(jnp.float32) * attended, axis=-1)
    start_backward = (
        jnp.zeros((seq_count, kv_heads, stripe, head_dim), jnp.float32),
        jnp.zeros((seq_count, full_len, kv_heads * head_dim), jnp.float32),
        jnp.zeros((seq_count, full_len, kv_heads * head_dim), jnp.float32),
    )
    running = start_backward
    pieces = (
        lax.all_gather(key_heads, "wide", axis=1, tiled=True),
        lax.all_gather(value_heads, "wide", axis=1, tiled=True),
    )
    key_blocks = split_blocks(pieces[0], seq_count, kv_heads, head_dim)
    value_blocks = split_blocks(pieces[1], seq_count, kv_heads, head_dim)
    fold_block_len = key_blocks.shape[2]

    def advance(carried, block_item):
        key_block, value_block, block_index = block_item
        key_first = block_index * fold_block_len

        def compute_block(current):
            query_acc, key_acc, value_acc = current
            scores, allowed = block_scores(key_block, key_first)
            probabilities = jnp.where(allowed, jnp.exp(scores - log_total[..., None]), 0.0)
            value_part = jnp.einsum(
                "skrj,skrd->sjkd",
                probabilities.astype(jnp.bfloat16),
                grouped_grad,
                preferred_element_type=jnp.float32,
            )
            prob_grad = jnp.einsum(
                "skrd,sjkd->skrj", grouped_grad, value_block, preferred_element_type=jnp.float32
            )
            score_grad = (probabilities * (prob_grad - row_delta[..., None])).astype(jnp.bfloat16)
            query_acc = (
                query_acc
                + jnp.einsum(
                    "skrj,sjkd->skrd", score_grad, key_block, preferred_element_type=jnp.float32
                )
                * score_scale
            )
            key_part = (
                jnp.einsum(
                    "skrj,skrd->sjkd", score_grad, queries, preferred_element_type=jnp.float32
                )
                * score_scale
            )
            key_acc = add_rows(
                key_acc, key_part.reshape(seq_count, fold_block_len, kv_heads * head_dim), key_first
            )
            value_acc = add_rows(
                value_acc,
                value_part.reshape(seq_count, fold_block_len, kv_heads * head_dim),
                key_first,
            )
            return (query_acc, key_acc, value_acc)

        return (lax.cond(key_first <= last_query, compute_block, unchanged, carried), None)

    running, _ = lax.scan(
        advance,
        running,
        (key_blocks, value_blocks, jnp.arange(key_blocks.shape[0], dtype=jnp.int32)),
    )
    query_acc, key_acc, value_acc = running
    key_sum, value_sum = (
        lax.psum_scatter(
            key_acc.astype(jnp.bfloat16), "wide", scatter_dimension=1, tiled=True
        ).astype(jnp.float32),
        lax.psum_scatter(
            value_acc.astype(jnp.bfloat16), "wide", scatter_dimension=1, tiled=True
        ).astype(jnp.float32),
    )
    query_back = (
        query_acc.reshape(seq_count, kv_heads, group_size, span_len, head_dim)
        .transpose(0, 3, 1, 2, 4)
        .reshape(row_count, head_count, head_dim)
    )
    query_grad = (
        rotate(query_back, token_pos, -1.0)
        .reshape(row_count, head_count * head_dim)
        .astype(jnp.bfloat16)
    )
    key_grad = (
        rotate(key_sum.reshape(row_count, kv_heads, head_dim), token_pos, -1.0)
        .reshape(row_count, kv_heads * head_dim)
        .astype(jnp.bfloat16)
    )
    value_grad = value_sum.reshape(row_count, kv_heads * head_dim).astype(jnp.bfloat16)
    grad_query = over_rows(first_norm, query_grad)
    grad_key = over_rows(first_norm, key_grad)
    grad_value = over_rows(first_norm, value_grad)
    input_norm_grad = (
        against(query_grad, query_w) + against(key_grad, key_w) + against(value_grad, value_w)
    )
    grad_gain_one = jnp.sum(input_norm_grad * inputs * inverse_one, axis=0)
    scaled_one = gain_one.astype(jnp.float32) * input_norm_grad
    input_grad = (
        middle_grad
        + inverse_one * scaled_one
        - inputs
        * (inverse_one * inverse_one * inverse_one)
        * jnp.mean(scaled_one * inputs, axis=-1, keepdims=True)
    )
    gain_one_share, query_share, key_share, value_share, out_share = (
        lax.psum_scatter(grad_gain_one, ("wide", "narrow"), scatter_dimension=0, tiled=True),
        lax.psum_scatter(grad_query, ("wide", "narrow"), scatter_dimension=0, tiled=True),
        lax.psum_scatter(grad_key, ("wide", "narrow"), scatter_dimension=0, tiled=True),
        lax.psum_scatter(grad_value, ("wide", "narrow"), scatter_dimension=0, tiled=True),
        lax.psum_scatter(grad_out, ("wide", "narrow"), scatter_dimension=0, tiled=True),
    )
    return (
        output.reshape(seq_count, span_len, model_width),
        input_grad.astype(jnp.bfloat16).reshape(seq_count, span_len, model_width),
        gain_one_share,
        query_share,
        key_share,
        value_share,
        out_share,
        gain_two_share,
        gate_share,
        up_share,
        down_share,
    )


def line_body(
    tokens,
    attn_gain,
    w_query,
    w_key,
    w_value,
    w_out,
    mlp_gain,
    w_gate,
    w_up,
    w_down,
    keep_mask,
    group_ids,
    positions,
    exit_scale,
    out_grad,
):
    f32 = jnp.float32
    bf16 = jnp.bfloat16
    _, span_len, model_width = tokens.shape
    line = lax.axis_size("z")
    rows_each = w_query.shape[0]
    q_cols = HEADS // line * HD
    ff_cols = w_gate.shape[1] // line
    group_len = span_len * line

    def by_columns(weight, columns):
        return weight.reshape(rows_each, line, columns).transpose(1, 0, 2)

    out_w = lax.all_gather(w_out, ("z", "x", "y", "c"), axis=0, tiled=True)
    down_w = lax.all_gather(w_down, ("x", "y", "c"), axis=0, tiled=True)
    own_x = tokens[0].astype(f32)
    keep = keep_mask[0].astype(f32)
    group_match = group_ids[0][:, None] == jnp.arange(exit_scale.shape[0], dtype=jnp.int32)[None, :]
    token_scale = jnp.sum(jnp.where(group_match, exit_scale[None, :], 0.0), axis=1, keepdims=True)
    upstream = out_grad[0].astype(f32) * token_scale

    core = lax.axis_index("c")
    gain_row = jnp.zeros((q_cols + 2 * HD,), bf16)
    gain_row = lax.dynamic_update_slice_in_dim(gain_row, attn_gain, core * rows_each, 0)
    gain_row = lax.dynamic_update_slice_in_dim(gain_row, mlp_gain, HD + core * rows_each, 0)
    gain_rows = jnp.broadcast_to(gain_row, (line, 16, gain_row.shape[0]))
    pack_attn = jnp.concatenate(
        [by_columns(w_query, q_cols), by_columns(w_key, HD), by_columns(w_value, HD)], axis=2
    )
    pack_attn = jnp.concatenate([pack_attn, gain_rows], axis=1)
    pack_ff = jnp.concatenate([by_columns(w_gate, ff_cols), by_columns(w_up, ff_cols)], axis=2)
    freqs = 10000.0 ** (-2.0 * jnp.arange(HD // 2, dtype=f32) / HD)
    angles = positions[0].astype(f32)[:, None] * freqs[None, :]
    table = jnp.concatenate([jnp.cos(angles), jnp.sin(angles)], axis=1)
    (
        x_blocks,
        near_w,
        gain_all,
        first_norm,
        queries,
        both_kv,
        log_total,
        turns,
        attended_rows,
        ff_w,
    ) = forward_call(tokens[0], table, pack_attn, pack_ff, line)
    keep_tile = jnp.broadcast_to(keep, (8, HD))
    middle, norm_grad, mixed, grad_down, grad_ff = mlp_call(
        keep_tile,
        gain_all,
        (keep * upstream).astype(bf16),
        x_blocks,
        attended_rows,
        out_w,
        ff_w.reshape(model_width, 2 * ff_cols),
        down_w,
        line,
    )
    grad_down = grad_down.astype(f32)
    output = (middle + keep * mixed).astype(bf16)
    middle_grad, input_norm_grad, ff_back, out_back, qkv_back = backward_call(
        (
            upstream,
            middle,
            norm_grad,
            keep_tile,
            gain_all,
            queries,
            both_kv,
            log_total,
            turns,
        ),
        out_w,
        attended_rows,
        near_w,
        first_norm,
        grad_ff.reshape(line, 2, 2, 2, rows_each, 2 * ff_cols),
        line,
    )
    ff_back = ff_back.astype(f32)
    qkv_back = qkv_back.astype(f32)
    grad_out = jnp.sum(out_back.astype(f32), axis=0)
    gain_one = gain_all[0, :1]
    inverse_one = lax.rsqrt(jnp.mean(own_x * own_x, axis=-1, keepdims=True) + epsilon)
    scaled_one = gain_one * input_norm_grad
    input_grad = (
        middle_grad
        + inverse_one * scaled_one
        - own_x
        * (inverse_one * inverse_one * inverse_one)
        * jnp.mean(scaled_one * own_x, axis=-1, keepdims=True)
    )

    def side_by_side(blocks):
        return blocks.transpose(1, 0, 2).reshape(rows_each, -1)

    grad_query = side_by_side(qkv_back[:, :, :q_cols])
    grad_key = side_by_side(qkv_back[:, :, q_cols : q_cols + HD])
    grad_value = side_by_side(qkv_back[:, :, q_cols + HD :])
    grad_gate = side_by_side(ff_back[:, :, :ff_cols])
    grad_up = side_by_side(ff_back[:, :, ff_cols:])

    def gain_grad(pairs, gain):
        total = sum(jnp.sum(weight.astype(f32) * grad, axis=1) for weight, grad in pairs)
        return total / gain.astype(f32)

    return (
        output[None],
        input_grad.astype(bf16)[None],
        gain_grad([(w_query, grad_query), (w_key, grad_key), (w_value, grad_value)], attn_gain),
        grad_query,
        grad_key,
        grad_value,
        grad_out,
        gain_grad([(w_gate, grad_gate), (w_up, grad_up)], mlp_gain),
        grad_gate,
        grad_up,
        grad_down,
    )


def solution(mesh):
    wide, narrow = mesh.shape["wide"], mesh.shape["narrow"]
    if wide == 2 * KVH and narrow == 4:
        mesh = Mesh(mesh.devices.reshape(wide // 2, 2, 2, 2), ("z", "x", "y", "c"))
        body, wide, narrow = line_body, ("z", "x"), ("y", "c")
    else:
        body, wide, narrow = general_body, ("wide",), ("narrow",)
    token_spec = P(narrow, wide, None)
    id_spec = P(narrow, wide)
    gain_spec = P(wide + narrow)
    weight_spec = P(wide + narrow, None)
    return jax.shard_map(
        body,
        mesh=mesh,
        in_specs=(
            token_spec,
            gain_spec,
            weight_spec,
            weight_spec,
            weight_spec,
            weight_spec,
            gain_spec,
            weight_spec,
            weight_spec,
            weight_spec,
            P(narrow),
            id_spec,
            id_spec,
            P(),
            token_spec,
        ),
        out_specs=(
            token_spec,
            token_spec,
            gain_spec,
            weight_spec,
            weight_spec,
            weight_spec,
            weight_spec,
            gain_spec,
            weight_spec,
            weight_spec,
            weight_spec,
        ),
        check_vma=False,
    )
```

```python
import functools
import math

import jax
import jax.numpy as jnp
from jax import lax
from jax.experimental import pallas as pl
from jax.experimental.pallas import tpu as pltpu
from jax.sharding import Mesh
from jax.sharding import PartitionSpec as P

HEADS = 16
KVH = 4
HD = 128


epsilon = 1e-05


def rotate(vectors, token_pos, direction):
    half_size = vectors.shape[-1] // 2
    freqs = 10000.0 ** (-2.0 * jnp.arange(half_size, dtype=jnp.float32) / vectors.shape[-1])
    angles = token_pos.astype(jnp.float32)[:, None] * freqs[None, :]
    cosine = jnp.cos(angles)[:, None, :]
    sine = direction * jnp.sin(angles)[:, None, :]
    first_half = vectors[..., :half_size]
    second_half = vectors[..., half_size:]
    return jnp.concatenate(
        [first_half * cosine - second_half * sine, second_half * cosine + first_half * sine],
        axis=-1,
    )


def split_blocks(piece_arr, seq_count, kv_heads, head_dim):
    piece_len = piece_arr.shape[1]
    block_len = math.gcd(piece_len, 512)
    shaped = piece_arr.reshape(seq_count, piece_len // block_len, block_len, kv_heads, head_dim)
    return shaped.transpose(1, 0, 2, 3, 4)


def add_rows(whole_arr, update, first_row):
    current = lax.dynamic_slice_in_dim(whole_arr, first_row, update.shape[1], 1)
    return lax.dynamic_update_slice_in_dim(whole_arr, current + update, first_row, 1)


def over_rows(left, right):
    return lax.dot_general(
        left, right, (((0,), (0,)), ((), ())), preferred_element_type=jnp.float32
    )


def against(left, right):
    return lax.dot_general(
        left, right, (((1,), (1,)), ((), ())), preferred_element_type=jnp.float32
    )


def unchanged(carried):
    return carried


MESH = pl.DeviceIdType.MESH
AXES = ("z", "x", "y", "c")


class Links:
    def __init__(self, send_sems, recv_sems, line):
        self.send_sems, self.recv_sems, self.line = send_sems, recv_sems, line
        self.z, self.x, self.y, self.c = (lax.axis_index(name) for name in AXES)
        self.slot = self.x * 4 + self.y * 2 + self.c
        self.used = 0
        self.sent = []

    def device(self, to):
        if to == "x":
            return (self.z, 1 - self.x, self.y, self.c)
        if to == "y":
            return (self.z, self.x, 1 - self.y, self.c)
        if to == "c":
            return (self.z, self.x, self.y, 1 - self.c)
        return (self.along(to), self.x, self.y, self.c)

    def along(self, step):
        return lax.rem(self.z + step + self.line, self.line)

    def other(self, to):
        slot = self.slot
        for name in to:
            bit = {"x": 4, "y": 2, "c": 1}[name]
            here = {"x": self.x, "y": self.y, "c": self.c}[name]
            slot = slot + bit * (1 - 2 * here)
        return slot

    def meet(self, targets):
        barrier = pltpu.get_barrier_semaphore()
        for to in targets:
            pl.semaphore_signal(barrier, inc=1, device_id=self.device(to), device_id_type=MESH)
        pl.semaphore_wait(barrier, len(targets))

    def send(self, source, target, to):
        copy = pltpu.make_async_remote_copy(
            src_ref=source,
            dst_ref=target,
            send_sem=self.send_sems.at[self.used],
            recv_sem=self.recv_sems.at[self.used],
            device_id=self.device(to),
            device_id_type=MESH,
        )
        copy.start()
        self.used += 1
        self.sent.append(copy)
        return copy

    def keep(self, source, target):
        copy = pltpu.make_async_copy(source, target, self.send_sems.at[self.used])
        copy.start()
        self.used += 1
        return copy

    def finish(self):
        for copy in self.sent:
            copy.wait_send()


class NearGather:
    def __init__(self, links, slot):
        self.links, self.slot = links, slot
        self.got = {}

    def offer(self, block, source):
        target = self.slot(block, self.links.slot)
        for to in ("x", "y", "c"):
            self.got[block, to] = self.links.send(source, target, to)

    def relay(self, block, first):
        links = self.links
        for to, then in (("x", "y"), ("y", "x")):
            self.got[block, to].wait_recv()
            place = self.slot(block, links.other(to))
            self.got[block, to + "c"] = links.send(place, place, "c")
            if to == first:
                self.got[block, "xy"] = links.send(place, place, then)

    def close(self, block):
        self.got[block, "xy"].wait_recv()
        place = self.slot(block, self.links.other("xy"))
        self.got[block, "xyc"] = self.links.send(place, place, "c")

    def wait(self, blocks):
        for block in blocks:
            for to in ("c", "xc", "yc", "xyc"):
                self.got[block, to].wait_recv()


class RingGather:
    def __init__(self, links, source, place, pieces=4):
        self.links, self.source, self.place, self.pieces = links, source, place, pieces
        self.rows = source.shape[0] // pieces
        self.last = [None] * pieces

    def step(self, number):
        for piece in range(self.pieces):
            way = 1 if piece < self.pieces // 2 else -1
            rows = pl.ds(piece * self.rows, self.rows)
            place = self.place(self.links.along(-way * number), rows)
            if number > 0:
                self.last[piece].wait_recv()
            if number < self.links.line - 1:
                origin = self.source.at[rows] if number == 0 else place
                self.last[piece] = self.links.send(origin, place, way)


def first_kernel(
    line,
    x_ref,
    table_ref,
    pack_ref,
    ff_ref,
    xs_ref,
    weight_ref,
    gain_ref,
    norm_ref,
    query_ref,
    kv_ref,
    peak_ref,
    turn_ref,
    atts_ref,
    ffs_ref,
    x_all,
    tables,
    weights,
    gains,
    norm,
    turns,
    flat,
    query,
    kv,
    peak,
    att,
    send_sems,
    recv_sems,
):
    f32, bf16 = jnp.float32, jnp.bfloat16
    links = Links(send_sems, recv_sems, line)
    far = [1, line - 1] + list(range(2, line - 1))
    links.meet(["x", "y", "c"] + far)
    here = links.slot
    span_len, width = x_ref.shape
    group_len = line * span_len
    rows_each = ff_ref.shape[1]
    q_cols = query.shape[1]
    heads = q_cols // HD
    local = []

    near = NearGather(links, lambda block, place: weights.at[links.along(-block), place])
    far_ff = NearGather(links, lambda block, place: ffs_ref.at[links.along(-block), place])
    ring = RingGather(links, x_ref, lambda block, rows: x_all.at[block, rows])
    own = [
        links.keep(x_ref, x_all.at[links.z]),
        links.keep(table_ref, tables.at[links.z]),
        links.keep(pack_ref.at[links.z], weights.at[links.z, here]),
    ]
    turned = {k: links.send(pack_ref.at[links.along(k)], weights.at[links.z, here], k) for k in far}
    placed = [links.send(table_ref, tables.at[links.z], k) for k in far]
    ring.step(0)
    near.offer(0, pack_ref.at[links.z])
    local.append(links.keep(ff_ref.at[links.z], ffs_ref.at[links.z, here]))
    for k in far:
        turned[k].wait_recv()
        near.offer(k, weights.at[links.along(-k), here])
    ring.step(1)
    for k in [0] + far:
        near.relay(k, "x" if k < line // 2 else "y")
    far_ff.offer(0, ff_ref.at[links.z])
    ring.step(2)
    turned_ff = {k: links.send(ff_ref.at[links.along(k)], ffs_ref.at[links.z, here], k) for k in far}
    for k in [0] + far:
        near.close(k)
    for copy in own:
        copy.wait()
    for copy in placed:
        copy.wait_recv()

    lane = lax.broadcasted_iota(jnp.int32, (span_len, HD), 1)
    for block in range(line):
        table = tables[block]
        swapped = pltpu.roll(table, HD // 2, 1)
        rows = slice(block * span_len, (block + 1) * span_len)
        turns[0, rows] = jnp.where(lane < HD // 2, table, swapped)
        turns[1, rows] = jnp.where(lane < HD // 2, -swapped, table)
    local.append(links.keep(turns, turn_ref))
    near.wait(range(line))
    for index in range(line * 4):
        z, q = divmod(index, 4)
        for which in range(2):
            lanes = slice(which * HD, (which + 1) * HD)
            both = [weights[z, 2 * q + c, rows_each : rows_each + 16, lanes].astype(f32) for c in range(2)]
            gains[which, :, index * HD : (index + 1) * HD] = both[0] + both[1]
    local.append(links.keep(weights, weight_ref))
    local.append(links.keep(gains, gain_ref))
    ring.step(3)
    local.append(links.keep(x_all, xs_ref))

    def normalise(index, carry):
        block = index // (span_len // 16)
        rows = pl.ds(pl.multiple_of(lax.rem(index, span_len // 16) * 16, 16), 16)
        values = x_all[block, rows].astype(f32)
        inverse = lax.rsqrt(jnp.mean(values * values, axis=-1, keepdims=True) + epsilon)
        target = pl.ds(pl.multiple_of(index * 16, 16), 16)
        norm[target] = (values * inverse * gains[0]).astype(bf16)
        return carry

    lax.fori_loop(0, group_len // 16, normalise, 0)
    local.append(links.keep(norm, norm_ref))

    def project(low, high):
        step = group_len // 2
        for part in range(2):
            rows = slice(part * step, (part + 1) * step)
            total = None
            for z in range(line):
                weight = weights[z, :, :rows_each, low:high].reshape(8 * rows_each, high - low)
                term = jnp.dot(
                    norm[rows, z * 8 * rows_each : (z + 1) * 8 * rows_each],
                    weight,
                    preferred_element_type=f32,
                )
                total = term if total is None else total + term
            flat[rows, low:high] = total

    def turn(values, rows):
        return values * turns[0, rows] + pltpu.roll(values, HD // 2, 1) * turns[1, rows]

    project(q_cols, q_cols + 2 * HD)
    for block in range(line):
        rows = slice(block * span_len, (block + 1) * span_len)
        kv[0, rows, :HD] = turn(flat[rows, q_cols : q_cols + HD], rows).astype(bf16)
        kv[0, rows, HD:] = flat[rows, q_cols + HD : q_cols + 2 * HD].astype(bf16)
    exchange = links.send(kv.at[0], kv.at[1], "x")
    project(0, q_cols)
    for block in range(line):
        rows = slice(block * span_len, (block + 1) * span_len)
        for head in range(heads):
            lanes = slice(head * HD, (head + 1) * HD)
            query[rows, lanes] = turn(flat[rows, lanes], rows).astype(bf16)
    local.append(links.keep(query, query_ref))
    exchange.wait_recv()
    local.append(links.keep(kv, kv_ref))

    scale = 1.0 / math.sqrt(HD)
    peak[...] = jnp.zeros_like(peak)

    def attend(head, carry):
        lanes = pl.ds(pl.multiple_of(head * HD, HD), HD)
        for block in range(line):
            rows = slice(block * span_len, (block + 1) * span_len)
            reach = (block + 1) * span_len
            part = query[rows, lanes]
            row = lax.broadcasted_iota(jnp.int32, (span_len, reach), 0) + block * span_len
            column = lax.broadcasted_iota(jnp.int32, (span_len, reach), 1)
            allowed = (column <= row, column < (block + links.x) * span_len)
            scores = []
            for half in range(2):
                score = lax.dot_general(
                    part, kv[half, :reach, :HD], (((1,), (1,)), ((), ())), preferred_element_type=f32
                )
                scores.append(jnp.where(allowed[half], score * scale, -1e30))
            top = jnp.maximum(
                jnp.max(scores[0], axis=-1, keepdims=True), jnp.max(scores[1], axis=-1, keepdims=True)
            )
            total, mixed = None, None
            for half in range(2):
                weight = jnp.exp(scores[half] - top)
                count = jnp.sum(weight, axis=-1, keepdims=True)
                term = jnp.dot(weight.astype(bf16), kv[half, :reach, HD:], preferred_element_type=f32)
                total = count if total is None else total + count
                mixed = term if mixed is None else mixed + term
            att[rows, lanes] = (mixed / total).astype(bf16)
            spot = lax.broadcasted_iota(jnp.int32, (span_len, HD), 1) == head
            peak[rows] = jnp.where(spot, top + jnp.log(total), peak[rows])
        return carry

    lax.fori_loop(0, heads, attend, 0)
    local.append(links.keep(peak, peak_ref))

    def place(block, rows):
        return atts_ref.at[rows, pl.ds(pl.multiple_of(block * q_cols, q_cols), q_cols)]

    att_ring = RingGather(links, att, place)
    local.append(links.keep(att, place(links.z, pl.ds(0, group_len))))
    att_ring.step(0)
    for k in far:
        turned_ff[k].wait_recv()
        far_ff.offer(k, ffs_ref.at[links.along(-k), here])
    far_ff.relay(0, "x")
    far_ff.close(0)
    far_ff.relay(far[0], "x")
    att_ring.step(1)
    for k in far[1:]:
        far_ff.relay(k, "x" if k < line // 2 else "y")
    att_ring.step(2)
    for k in far:
        far_ff.close(k)
    att_ring.step(3)
    far_ff.wait(range(line))
    links.finish()
    for copy in local:
        copy.wait()


def add_rows_of(target, values, count):
    def add(index, carry):
        rows = pl.ds(pl.multiple_of(index * 16, 16), 16)
        target[rows] = target[rows] + values[rows]
        return carry

    lax.fori_loop(0, count // 16, add, 0)


class NearSum:
    def __init__(self, links, source, own, from_core, from_first, from_second, first, in_place=False):
        self.links, self.source, self.own, self.first = links, source, own, first
        self.in_place = in_place
        self.from_core, self.from_first, self.from_second = from_core, from_first, from_second

    def start(self):
        links = self.links
        if not self.in_place:
            self.local = links.keep(self.source(links.c), self.own)
        self.copy = links.send(self.source(1 - links.c), self.from_core, "c")

    def add(self, target, values):
        add_rows_of(target, values, target.shape[0])

    def core_done(self):
        links = self.links
        self.copy.wait_recv()
        if not self.in_place:
            self.local.wait()
        for x in range(2):
            for y in range(2):
                self.add(self.own.at[x, y], self.from_core.at[x, y])
        if self.first == "x":
            self.copy = links.send(self.own.at[1 - links.x], self.from_first, "x")
        else:
            self.copy = links.send(self.own.at[:, 1 - links.y], self.from_first, "y")

    def first_done(self):
        links = self.links
        self.copy.wait_recv()
        for other in range(2):
            place = (links.x, other) if self.first == "x" else (other, links.y)
            self.add(self.own.at[place], self.from_first.at[other])
        if self.first == "x":
            self.copy = links.send(self.own.at[links.x, 1 - links.y], self.from_second, "y")
        else:
            self.copy = links.send(self.own.at[1 - links.x, links.y], self.from_second, "x")

    def second_done(self):
        self.copy.wait_recv()
        total = self.own.at[self.links.x, self.links.y]
        self.add(total, self.from_second)
        return total


def sum_space(blocks, rows, columns):
    shape = (rows, columns)
    return [
        pltpu.VMEM((blocks, 2, 2) + shape, jnp.bfloat16),
        pltpu.VMEM((blocks, 2, 2) + shape, jnp.bfloat16),
        pltpu.VMEM((blocks, 2) + shape, jnp.bfloat16),
        pltpu.VMEM((blocks,) + shape, jnp.bfloat16),
    ]


class RingSum:
    def __init__(self, links, parts, total, got, pieces=4):
        self.links, self.parts, self.total, self.got = links, parts, total, got
        self.pieces, self.last = pieces, [None] * pieces
        self.rows = parts.shape[1] // pieces

    def step(self, number):
        links = self.links
        for piece in range(self.pieces):
            way = 1 if piece < self.pieces // 2 else -1
            block = links.along(-way * (number + 1))
            where = pl.ds(piece * self.rows, self.rows)
            if number == 0:
                source = self.parts.at[block, where]
            else:
                self.last[piece].wait_recv()
                total = self.got[number - 1, where].astype(jnp.float32) + self.parts[
                    block, where
                ].astype(jnp.float32)
                if number == links.line - 1:
                    self.total[where] = total
                    continue
                self.parts[block, where] = total.astype(self.parts.dtype)
                source = self.parts.at[block, where]
            self.last[piece] = links.send(source, self.got.at[number, where], way)


def link_call(kernel, collective_id, copies, shapes, arguments, spaces=None, scratch=(), vmem=16):
    any_space = pl.BlockSpec(memory_space=pl.ANY)
    near_space = pl.BlockSpec(memory_space=pltpu.VMEM)
    many = isinstance(shapes, tuple)
    if spaces is None:
        spaces = "h" * (len(arguments) + (len(shapes) if many else 1))
    specs = [near_space if space == "v" else any_space for space in spaces]
    return pl.pallas_call(
        kernel,
        out_shape=shapes,
        in_specs=specs[: len(arguments)],
        out_specs=tuple(specs[len(arguments) :]) if many else specs[-1],
        scratch_shapes=list(scratch)
        + [pltpu.SemaphoreType.DMA((copies,)), pltpu.SemaphoreType.DMA((copies,))],
        compiler_params=pltpu.CompilerParams(
            collective_id=collective_id, has_side_effects=True, vmem_limit_bytes=vmem * 2**20
        ),
    )(*arguments)


def forward_call(tokens, table, pack, pack_ff, line):
    span_len, width = tokens.shape
    group_len = line * span_len
    rows_each = pack_ff.shape[1]
    qkv_cols = pack.shape[2]
    q_cols = qkv_cols - 2 * HD
    f32, bf16 = jnp.float32, jnp.bfloat16
    outs = (
        ((line, span_len, width), bf16),
        ((line, 8) + pack.shape[1:], bf16),
        ((2, 16, width), f32),
        ((group_len, width), bf16),
        ((group_len, q_cols), bf16),
        ((2, group_len, 2 * HD), bf16),
        ((group_len, HD), f32),
        ((2, group_len, HD), f32),
        ((group_len, line * q_cols), bf16),
        ((line, 8) + pack_ff.shape[1:], bf16),
    )
    return link_call(
        functools.partial(first_kernel, line),
        0,
        176,
        tuple(jax.ShapeDtypeStruct(*out) for out in outs),
        (tokens, table, pack, pack_ff),
        scratch=[
            pltpu.VMEM((line, span_len, width), bf16),
            pltpu.VMEM((line,) + table.shape, f32),
            pltpu.VMEM((line, 8) + pack.shape[1:], bf16),
            pltpu.VMEM((2, 16, width), f32),
            pltpu.VMEM((group_len, width), bf16),
            pltpu.VMEM((2, group_len, HD), f32),
            pltpu.VMEM((group_len, qkv_cols), f32),
            pltpu.VMEM((group_len, q_cols), bf16),
            pltpu.VMEM((2, group_len, 2 * HD), bf16),
            pltpu.VMEM((group_len, HD), f32),
            pltpu.VMEM((group_len, q_cols), bf16),
        ],
        vmem=48,
    )


def mlp_kernel(
    line,
    cuts,
    keep_ref,
    gain_ref,
    mix_ref,
    xs_ref,
    atts_ref,
    out_ref,
    ff_ref,
    down_ref,
    middle_ref,
    total_ref,
    mixed_total_ref,
    sum_ref,
    grad_ff_ref,
    ff_half_ref,
    big,
    ff,
    down,
    norm,
    parts,
    mixed,
    gate_up,
    hidden,
    both_grad,
    got,
    mixed_parts,
    mixed_got,
    *scratch,
):
    f32, bf16 = jnp.float32, jnp.bfloat16
    space, (send_sems, recv_sems) = scratch[:-2], scratch[-2:]
    links = Links(send_sems, recv_sems, line)
    links.meet(["x", "y", "c", 1, line - 1])
    far = [1, line - 1] + list(range(2, line - 1))
    span_len, width = mix_ref.shape
    group_len = line * span_len
    ff_cols = hidden.shape[1]
    block_rows = width // line
    rows_each = block_rows // 8
    chunk = 2 * HD
    stay = links.keep(mix_ref, mixed.at[links.z])
    mix_ring = RingGather(links, mix_ref, lambda block, rows: mixed.at[block, rows])
    mix_ring.step(0)
    early = [
        links.keep(out_ref, big),
        links.keep(atts_ref, norm),
        links.keep(xs_ref, parts),
    ]
    late = [links.keep(ff_ref, ff), links.keep(down_ref, down)]
    ring = RingSum(links, parts, total_ref, got)
    mixed_ring = RingSum(links, mixed_parts, mixed_total_ref, mixed_got)
    items = []
    ff_items = []
    for index, k in enumerate(far[:2]):
        block = links.along(k)
        core, first, second = space[:3]
        ff_items.append(
            NearSum(
                links,
                lambda c, block=block: ff.at[block, :, :, c],
                ff.at[block, :, :, links.c],
                core.at[index],
                first.at[index],
                second.at[index],
                "xy"[index % 2],
                True,
            )
        )
    for index, (low, high) in enumerate(cuts):
        rows = pl.ds(low, high - low)
        core, first, second = space[3 * index + 3 : 3 * index + 6]
        items.append(
            NearSum(
                links,
                lambda c, rows=rows: big.at[:, :, c, rows],
                big.at[:, :, links.c, rows],
                core.at[0],
                first.at[0],
                second.at[0],
                "xy"[index % 2],
                True,
            )
        )
    for copy in early:
        copy.wait()

    half = group_len // 2
    out_rows = width // 8
    for part in range(2):
        low = part * half
        for column in range(4):
            lanes = slice(column * width // 4, (column + 1) * width // 4)
            value = None
            for k in range(8):
                term = jnp.dot(
                    norm[low : low + half, k * out_rows : (k + 1) * out_rows],
                    big[k // 4, k // 2 % 2, k % 2, :, lanes],
                    preferred_element_type=f32,
                )
                value = term if value is None else value + term
            gate_up[:half, lanes] = value * keep_ref[0:1, 0:1]

        def normalise(index, carry, low=low):
            block = (low // 16 + index) // (span_len // 16)
            rows = pl.ds(pl.multiple_of(index * 16, 16), 16)
            inside = pl.ds(pl.multiple_of(lax.rem(index, span_len // 16) * 16, 16), 16)
            values = parts[block, inside].astype(f32) + gate_up[rows, :width]
            gate_up[rows, :width] = values
            inverse = lax.rsqrt(jnp.mean(values * values, axis=-1, keepdims=True) + epsilon)
            target = pl.ds(pl.multiple_of(low + index * 16, 16), 16)
            norm[target] = (values * inverse * gain_ref[1]).astype(bf16)
            return carry

        lax.fori_loop(0, half // 16, normalise, 0)

        @pl.when(links.z // (line // 2) == part)
        def _():
            where = pl.multiple_of(lax.rem(links.z, line // 2) * span_len, span_len)
            middle_ref[...] = gate_up[pl.ds(where, span_len), :width]

    mix_ring.step(1)
    for copy in late:
        copy.wait()

    def columns_of(lanes, size):
        return ff[:, :, :, :, :, lanes].reshape(width, size)

    def forward(low, size):
        gates, ups = pl.ds(low, size), pl.ds(low + ff_cols, size)
        gate = jnp.dot(norm[...], columns_of(gates, size), preferred_element_type=f32)
        gate_up[:, gates] = gate
        swish = gate * jax.nn.sigmoid(gate)
        up = jnp.dot(norm[...], columns_of(ups, size), preferred_element_type=f32)
        gate_up[:, ups] = up
        hidden[:, gates] = (swish * up).astype(bf16)

    def backward(low, size):
        gates, ups = pl.ds(low, size), pl.ds(low + ff_cols, size)
        grad = lax.dot_general(
            mixed[...].reshape(group_len, width),
            down[gates],
            (((1,), (1,)), ((), ())),
            preferred_element_type=f32,
        )
        gate, up = gate_up[:, gates], gate_up[:, ups]
        sigmoid = jax.nn.sigmoid(gate)
        both_grad[:, gates] = (grad * up * sigmoid * (1.0 + gate * (1.0 - sigmoid))).astype(bf16)
        both_grad[:, ups] = (grad * (gate * sigmoid)).astype(bf16)

    def over_chunks(work, extent):
        def one(index, carry):
            work(pl.multiple_of(index * chunk, chunk), chunk)
            return carry

        lax.fori_loop(0, extent // chunk, one, 0)
        if extent % chunk:
            work(extent // chunk * chunk, extent % chunk)

    over_chunks(forward, ff_cols)
    mix_ring.step(2)

    def mixed_part(low, size):
        lanes = pl.ds(low, size)
        value = jnp.dot(hidden[...], down[:, lanes], preferred_element_type=f32).astype(bf16)
        mixed_parts[:, :, lanes] = value.reshape(line, span_len, size)

    over_chunks(mixed_part, width)
    mixed_ring.step(0)
    stay.wait()
    mix_ring.step(3)
    over_chunks(backward, ff_cols)

    def norm_part(index, carry):
        size = 4 * rows_each
        weight = ff[index // 2, lax.rem(index, 2)].reshape(size, 2 * ff_cols)
        value = lax.dot_general(
            both_grad[...], weight, (((1,), (1,)), ((), ())), preferred_element_type=f32
        ).astype(bf16)
        lanes = pl.ds(pl.multiple_of(index * size, size), size)
        parts[:, :, lanes] = value.reshape(line, span_len, size)
        return carry

    lax.fori_loop(0, 2 * line, norm_part, 0)
    ring.step(0)
    mixed_ring.step(1)

    def ff_block(block):
        norm_rows = norm[:, pl.ds(pl.multiple_of(block * block_rows, block_rows), block_rows)].T

        def ff_part(low, size):
            lanes = pl.ds(low, size)
            value = jnp.dot(norm_rows, both_grad[:, lanes], preferred_element_type=f32)
            ff[block, :, :, :, :, lanes] = value.astype(bf16).reshape(2, 2, 2, rows_each, size)

        over_chunks(ff_part, 2 * ff_cols)

    for item, k in zip(ff_items, far):
        ff_block(links.along(k))
        item.start()
    hidden_rows = hidden[...].T

    def down_part(low, size):
        lanes = pl.ds(low, size)
        value = jnp.dot(
            hidden_rows,
            mixed[:, :, lanes].reshape(group_len, size),
            preferred_element_type=f32,
        ).astype(bf16)
        big[:, :, :, : cuts[-1][1], lanes] = value.reshape(2, 2, 2, cuts[-1][1], size)

    ring.step(1)
    for item in ff_items:
        item.core_done()
    over_chunks(down_part, width)
    for item in items:
        item.start()
    mixed_ring.step(2)
    ring.step(2)
    for item in items:
        item.core_done()
    sent = []
    for k in far[2:] + [0]:
        block = links.along(k)
        ff_block(block)
        sent.append(links.keep(ff.at[block], grad_ff_ref.at[block]))
    for item in ff_items:
        item.first_done()
    ring.step(3)
    for item in items:
        item.first_done()
    for index, item in enumerate(ff_items):
        sent.append(links.keep(item.second_done(), ff_half_ref.at[index]))
    mixed_ring.step(3)
    for item, (low, high) in zip(items, cuts):
        sum_ref[low:high] = item.second_done()[...]
    links.finish()
    for copy in sent:
        copy.wait()


def mlp_call(keep, gains, mixed, x_blocks, attended, out_w, ff_w, down_w, line):
    f32, bf16 = jnp.float32, jnp.bfloat16
    span_len, width = mixed.shape
    group_len = line * span_len
    ff_rows, both_cols, rows_each = down_w.shape[0], ff_w.shape[3], ff_w.shape[2]
    ff_w = ff_w.reshape(line, 2, 2, 2, rows_each, both_cols)
    rows = ff_rows // 8
    half = (rows // 2 + 15) // 16 * 16
    cuts = ((0, half), (half, rows))
    blocks = (line, span_len, width)
    token = jax.ShapeDtypeStruct((span_len, width), f32)
    return link_call(
        functools.partial(mlp_kernel, line, cuts),
        2,
        96,
        (
            token,
            token,
            token,
            jax.ShapeDtypeStruct((rows, width), bf16),
            jax.ShapeDtypeStruct(ff_w.shape, bf16),
            jax.ShapeDtypeStruct((2, rows_each, both_cols), bf16),
        ),
        (keep, gains, mixed, x_blocks, attended, out_w.reshape(2, 2, 2, width // 8, width), ff_w, down_w),
        "vvhhhhhh" + "vvvvhh",
        [
            pltpu.VMEM((2, 2, 2, width // 8, width), bf16),
            pltpu.VMEM(ff_w.shape, bf16),
            pltpu.VMEM(down_w.shape, bf16),
            pltpu.VMEM((group_len, width), bf16),
            pltpu.VMEM(blocks, bf16),
            pltpu.VMEM(blocks, bf16),
            pltpu.VMEM((group_len, both_cols), f32),
            pltpu.VMEM((group_len, ff_rows), bf16),
            pltpu.VMEM((group_len, both_cols), bf16),
            pltpu.VMEM((line - 1, span_len, width), bf16),
            pltpu.VMEM(blocks, bf16),
            pltpu.VMEM((line - 1, span_len, width), bf16),
        ]
        + sum_space(2, rows_each, both_cols)[1:]
        + sum((sum_space(1, high - low, width)[1:] for low, high in cuts), []),
        vmem=63,
    )


def backward_kernel(
    line,
    up_ref,
    middle_ref,
    norm_grad_ref,
    keep_ref,
    gain_ref,
    query_ref,
    kv_ref,
    peak_ref,
    turn_ref,
    out_ref,
    atts_ref,
    weight_ref,
    norm_ref,
    ff_ref,
    ff_half_ref,
    middle_grad_ref,
    total_ref,
    ffs_ref,
    outs_ref,
    qkvs_ref,
    big,
    slim,
    norm,
    own_rows,
    own_columns,
    branch,
    own_grad,
    att_grad,
    query_back,
    kv_back,
    kv_out,
    kv_in,
    flat,
    parts,
    query,
    kv,
    peak,
    turns,
    *scratch,
):
    f32, bf16 = jnp.float32, jnp.bfloat16
    send_sems, recv_sems = scratch[-2:]
    got, sums = scratch[0], scratch[1:-2]
    links = Links(send_sems, recv_sems, line)
    far = [1, line - 1] + list(range(2, line - 1))
    order = far + [0]
    links.meet(["x", "y", "c"] + far)
    span_len, width = up_ref.shape
    group_len = line * span_len
    q_cols = query.shape[1]
    heads = q_cols // HD
    rows_z = width // line
    rows_each = rows_z // 8
    scale = 1.0 / math.sqrt(HD)

    def lanes_of(block):
        return pl.ds(pl.multiple_of(block * q_cols, q_cols), q_cols)

    here = pl.ds(pl.multiple_of(links.z * span_len, span_len), span_len)
    loads = [
        links.keep(out_ref, big),
        links.keep(atts_ref.at[here], own_rows),
        links.keep(atts_ref.at[:, lanes_of(links.z)], own_columns),
        links.keep(query_ref, query),
        links.keep(kv_ref, kv),
        links.keep(peak_ref, peak),
        links.keep(turn_ref, turns),
        links.keep(norm_ref, norm),
        links.keep(weight_ref.at[:, :, :, :, pl.ds(0, slim.shape[4])], slim),
    ]
    ring = RingSum(links, parts, total_ref, got)

    def items_of(source, space, in_place, order=order):
        items = []
        for index, k in enumerate(order):
            block = links.along(k)
            own = source.at[block, :, :, links.c] if in_place else space[0].at[index]
            core, first, second = space[-3:]
            items.append(
                NearSum(
                    links,
                    lambda c, block=block: source.at[block, :, :, c],
                    own,
                    core.at[index],
                    first.at[index],
                    second.at[index],
                    "xy"[index % 2],
                    in_place,
                )
            )
        return items

    ff_order = order[2:]
    ff_items = items_of(ff_ref, sums[:4], False, ff_order)
    out_items = items_of(big, sums[4:7], True)
    qkv_items = items_of(slim, sums[7:], True)
    local = []
    arrived = [
        links.send(ff_half_ref.at[index], ffs_ref.at[links.z], k) for index, k in enumerate(order[:2])
    ]

    def turn(items, target, low, high, order=order):
        for item, k in list(zip(items, order))[low:high]:
            total = item.second_done()
            if k == 0:
                local.append(links.keep(total, target.at[links.z]))
            else:
                arrived.append(links.send(total, target.at[links.z], k))

    def core_done(items, low, high):
        for item in items[low:high]:
            item.core_done()

    def first_done(items, low, high):
        for item in items[low:high]:
            item.first_done()

    half = line // 2
    for item in ff_items:
        item.start()

    def d_middle(index, carry):
        rows = pl.ds(pl.multiple_of(index * 16, 16), 16)
        middle = middle_ref[rows]
        inverse = lax.rsqrt(jnp.mean(middle * middle, axis=-1, keepdims=True) + epsilon)
        scaled = gain_ref[1] * norm_grad_ref[rows]
        grad = (
            up_ref[rows]
            + inverse * scaled
            - middle
            * (inverse * inverse * inverse)
            * jnp.mean(scaled * middle, axis=-1, keepdims=True)
        )
        middle_grad_ref[rows] = grad
        branch[rows] = (grad * keep_ref[0:1, 0:1]).astype(bf16)
        return carry

    lax.fori_loop(0, span_len // 16, d_middle, 0)
    for copy in loads:
        copy.wait()
    for z in range(line):
        weight = big[z].reshape(rows_z, width)
        own_grad[:, z * rows_z : (z + 1) * rows_z] = lax.dot_general(
            branch[...], weight, (((1,), (1,)), ((), ())), preferred_element_type=f32
        ).astype(bf16)
    turned = [links.send(own_grad.at[:, lanes_of(links.along(k))], att_grad.at[here], k) for k in far]
    stayed = links.keep(own_grad.at[:, lanes_of(links.z)], att_grad.at[here])
    core_done(ff_items, 0, line)
    for z in range(line):
        for part in range(4):
            columns = slice(part * width // 4, (part + 1) * width // 4)
            grad = lax.dot_general(
                own_rows[:, z * rows_z : (z + 1) * rows_z],
                branch[:, columns],
                (((0,), (0,)), ((), ())),
                preferred_element_type=f32,
            )
            big[z, :, :, :, :, columns] = grad.astype(bf16).reshape(2, 2, 2, rows_each, width // 4)
    for item in out_items:
        item.start()
    kv_back[...] = jnp.zeros_like(kv_back)
    for copy in turned:
        copy.wait_recv()
    stayed.wait()

    def attend_back(head, carry):
        lanes = pl.ds(pl.multiple_of(head * HD, HD), HD)
        for block in range(line):
            rows = slice(block * span_len, (block + 1) * span_len)
            reach = (block + 1) * span_len
            part, grad = query[rows, lanes], att_grad[rows, lanes]
            row = lax.broadcasted_iota(jnp.int32, (span_len, reach), 0) + block * span_len
            column = lax.broadcasted_iota(jnp.int32, (span_len, reach), 1)
            allowed = (column <= row, column < (block + links.x) * span_len)
            spot = lax.broadcasted_iota(jnp.int32, (span_len, HD), 1) == head
            top = jnp.sum(jnp.where(spot, peak[rows], 0.0), axis=-1, keepdims=True)
            delta = jnp.sum(
                grad.astype(f32) * own_columns[rows, lanes].astype(f32), axis=-1, keepdims=True
            )
            total = None
            for side in range(2):
                keys, values = kv[side, :reach, :HD], kv[side, :reach, HD:]
                score = lax.dot_general(
                    part, keys, (((1,), (1,)), ((), ())), preferred_element_type=f32
                )
                weight = jnp.where(allowed[side], jnp.exp(score * scale - top), 0.0)
                weight_grad = lax.dot_general(
                    grad, values, (((1,), (1,)), ((), ())), preferred_element_type=f32
                )
                score_grad = (weight * (weight_grad - delta)).astype(bf16)
                term = jnp.dot(score_grad, keys, preferred_element_type=f32)
                total = term if total is None else total + term
                kv_back[side, :reach, :HD] += lax.dot_general(
                    score_grad, part, (((0,), (0,)), ((), ())), preferred_element_type=f32
                )
                kv_back[side, :reach, HD:] += lax.dot_general(
                    weight.astype(bf16), grad, (((0,), (0,)), ((), ())), preferred_element_type=f32
                )
            query_back[rows, lanes] = total * scale
        return carry

    lax.fori_loop(0, heads, attend_back, 0)
    kv_out[:, :HD] = (kv_back[1, :, :HD] * scale).astype(bf16)
    kv_out[:, HD:] = kv_back[1, :, HD:].astype(bf16)
    exchange = links.send(kv_out, kv_in, "x")

    def turn_back(values, rows):
        return values * turns[0, rows] - pltpu.roll(values, HD // 2, 1) * turns[1, rows]

    for block in range(line):
        rows = slice(block * span_len, (block + 1) * span_len)
        for head in range(heads):
            lanes = slice(head * HD, (head + 1) * HD)
            flat[rows, lanes] = turn_back(query_back[rows, lanes], rows).astype(bf16)
    first_done(ff_items, 0, line)
    exchange.wait_recv()
    for block in range(line):
        rows = slice(block * span_len, (block + 1) * span_len)
        key_grad = kv_back[0, rows, :HD] * scale + kv_in[rows, :HD].astype(f32)
        flat[rows, q_cols : q_cols + HD] = turn_back(key_grad, rows).astype(bf16)
        value_grad = kv_back[0, rows, HD:] + kv_in[rows, HD:].astype(f32)
        flat[rows, q_cols + HD :] = value_grad.astype(bf16)
    for z in range(line):
        weight = slim[z].reshape(rows_z, flat.shape[1])
        part = lax.dot_general(
            flat[...], weight, (((1,), (1,)), ((), ())), preferred_element_type=f32
        ).astype(bf16)
        for block in range(line):
            parts[block, :, z * rows_z : (z + 1) * rows_z] = part[
                block * span_len : (block + 1) * span_len
            ]
    ring.step(0)
    for z in range(line):
        grad = lax.dot_general(
            norm[:, z * rows_z : (z + 1) * rows_z],
            flat[...],
            (((0,), (0,)), ((), ())),
            preferred_element_type=f32,
        )
        slim[z] = grad.astype(bf16).reshape(2, 2, 2, rows_each, flat.shape[1])
    for item in qkv_items:
        item.start()
    core_done(out_items, 0, half)
    turn(ff_items, ffs_ref, 0, line, ff_order)
    ring.step(1)
    core_done(out_items, half, line)
    first_done(out_items, 0, half)
    ring.step(2)
    core_done(qkv_items, 0, line)
    first_done(out_items, half, line)
    turn(out_items, outs_ref, 0, half)
    ring.step(3)
    first_done(qkv_items, 0, half)
    turn(out_items, outs_ref, half, line)
    first_done(qkv_items, half, line)
    turn(qkv_items, qkvs_ref, 0, line)
    for copy in arrived:
        copy.wait_recv()
    links.finish()
    for copy in local:
        copy.wait()


def backward_call(small, saved, out_w, attended, weights, norm, grad_ff, ff_half, line):
    f32, bf16 = jnp.float32, jnp.bfloat16
    span_len, width = small[0].shape
    group_len = line * span_len
    query = saved[0]
    q_cols, rows_each, qkv_cols = query.shape[1], width // line // 8, weights.shape[3]
    weights = weights.reshape(line, 2, 2, 2, -1, qkv_cols)
    wide = (line, 2, 2, 2, rows_each, width)
    slim = (line, 2, 2, 2, rows_each, qkv_cols)
    out_space = sum_space(line, rows_each, width)[1:]
    qkv_space = sum_space(line, rows_each, qkv_cols)[1:]
    token = jax.ShapeDtypeStruct((span_len, width), f32)
    return link_call(
        functools.partial(backward_kernel, line),
        4,
        160,
        (token, token)
        + tuple(
            jax.ShapeDtypeStruct((line, rows_each, columns), bf16)
            for columns in (grad_ff.shape[5], width, qkv_cols)
        ),
        small + saved + (out_w.reshape(wide), attended, weights, norm, grad_ff, ff_half),
        "v" * 5 + "h" * 10 + "vvhhh",
        [
            pltpu.VMEM(wide, bf16),
            pltpu.VMEM(slim, bf16),
            pltpu.VMEM((group_len, width), bf16),
            pltpu.VMEM((span_len, width), bf16),
            pltpu.VMEM((group_len, q_cols), bf16),
            pltpu.VMEM((span_len, width), bf16),
            pltpu.VMEM((span_len, width), bf16),
            pltpu.VMEM((group_len, q_cols), bf16),
            pltpu.VMEM((group_len, q_cols), f32),
            pltpu.VMEM((2, group_len, 2 * HD), f32),
            pltpu.VMEM((group_len, 2 * HD), bf16),
            pltpu.VMEM((group_len, 2 * HD), bf16),
            pltpu.VMEM((group_len, qkv_cols), bf16),
            pltpu.VMEM((line, span_len, width), bf16),
        ]
        + [pltpu.VMEM(value.shape, value.dtype) for value in saved]
        + [pltpu.VMEM((line - 1, span_len, width), bf16)]
        + sum_space(line - 2, rows_each, grad_ff.shape[5])
        + out_space
        + qkv_space,
        vmem=63,
    )


def general_body(
    tokens,
    attn_gain,
    w_query,
    w_key,
    w_value,
    w_out,
    mlp_gain,
    w_gate,
    w_up,
    w_down,
    keep_mask,
    group_ids,
    positions,
    exit_scale,
    out_grad,
):
    seq_count, span_len, model_width = tokens.shape
    kv_heads = KVH
    head_dim = HD
    head_count = HEADS
    group_size = head_count // kv_heads
    row_count = seq_count * span_len
    stripe = group_size * span_len
    wide_count = lax.axis_size("wide")
    wide_place = lax.axis_index("wide")
    full_len = span_len * wide_count
    score_scale = 1.0 / math.sqrt(head_dim)
    gain_one, query_w, key_w, value_w, out_w = (
        lax.all_gather(attn_gain, ("wide", "narrow"), axis=0, tiled=True),
        lax.all_gather(w_query, ("wide", "narrow"), axis=0, tiled=True),
        lax.all_gather(w_key, ("wide", "narrow"), axis=0, tiled=True),
        lax.all_gather(w_value, ("wide", "narrow"), axis=0, tiled=True),
        lax.all_gather(w_out, ("wide", "narrow"), axis=0, tiled=True),
    )
    inputs = tokens.astype(jnp.float32).reshape(row_count, model_width)
    token_pos = positions.reshape(row_count)
    keep_rows = jnp.repeat(keep_mask.astype(jnp.float32), span_len)[:, None]
    inverse_one = lax.rsqrt(jnp.mean(inputs * inputs, axis=-1, keepdims=True) + epsilon)
    first_norm = (inputs * inverse_one * gain_one.astype(jnp.float32)).astype(jnp.bfloat16)
    query_pre = jnp.dot(first_norm, query_w, preferred_element_type=jnp.float32).reshape(
        row_count, head_count, head_dim
    )
    key_pre = jnp.dot(first_norm, key_w, preferred_element_type=jnp.float32).reshape(
        row_count, kv_heads, head_dim
    )
    query_rows = rotate(query_pre, token_pos, 1.0).astype(jnp.bfloat16)
    key_heads = (
        rotate(key_pre, token_pos, 1.0)
        .astype(jnp.bfloat16)
        .reshape(seq_count, span_len, kv_heads * head_dim)
    )
    value_heads = (
        jnp.dot(first_norm, value_w, preferred_element_type=jnp.float32)
        .astype(jnp.bfloat16)
        .reshape(seq_count, span_len, kv_heads * head_dim)
    )
    queries = (
        query_rows.reshape(seq_count, span_len, kv_heads, group_size, head_dim)
        .transpose(0, 2, 3, 1, 4)
        .reshape(seq_count, kv_heads, stripe, head_dim)
    )
    query_index = wide_place * span_len + jnp.arange(stripe, dtype=jnp.int32) % span_len
    last_query = wide_place * span_len + span_len - 1

    def block_scores(key_block, key_first):
        scores = (
            jnp.einsum("skrd,sjkd->skrj", queries, key_block, preferred_element_type=jnp.float32)
            * score_scale
        )
        key_index = key_first + jnp.arange(key_block.shape[1], dtype=jnp.int32)
        allowed = key_index[None, :] <= query_index[:, None]
        return (scores, allowed)

    start_forward = (
        jnp.full((seq_count, kv_heads, stripe), -1e30, jnp.float32),
        jnp.zeros((seq_count, kv_heads, stripe), jnp.float32),
        jnp.zeros((seq_count, kv_heads, stripe, head_dim), jnp.float32),
    )
    running = start_forward
    pieces = (
        lax.all_gather(key_heads, "wide", axis=1, tiled=True),
        lax.all_gather(value_heads, "wide", axis=1, tiled=True),
    )
    key_blocks = split_blocks(pieces[0], seq_count, kv_heads, head_dim)
    value_blocks = split_blocks(pieces[1], seq_count, kv_heads, head_dim)
    block_len = key_blocks.shape[2]

    def advance(carried, block_item):
        key_block, value_block, block_index = block_item
        key_first = block_index * block_len

        def compute_block(current):
            run_max, run_sum, run_acc = current
            scores, allowed = block_scores(key_block, key_first)
            scores = jnp.where(allowed, scores, -1e30)
            new_max = jnp.maximum(run_max, jnp.max(scores, axis=-1))
            factor = jnp.exp(run_max - new_max)
            weights = jnp.where(allowed, jnp.exp(scores - new_max[..., None]), 0.0)
            new_sum = run_sum * factor + jnp.sum(weights, axis=-1)
            new_acc = run_acc * factor[..., None] + jnp.einsum(
                "skrj,sjkd->skrd",
                weights.astype(jnp.bfloat16),
                value_block,
                preferred_element_type=jnp.float32,
            )
            return (new_max, new_sum, new_acc)

        return (lax.cond(key_first <= last_query, compute_block, unchanged, carried), None)

    running, _ = lax.scan(
        advance,
        running,
        (key_blocks, value_blocks, jnp.arange(key_blocks.shape[0], dtype=jnp.int32)),
    )
    run_max, run_sum, run_acc = running
    attended = run_acc / run_sum[..., None]
    log_total = run_max + jnp.log(run_sum)
    attended_rows = (
        attended.reshape(seq_count, kv_heads, group_size, span_len, head_dim)
        .transpose(0, 3, 1, 2, 4)
        .reshape(row_count, head_count * head_dim)
        .astype(jnp.bfloat16)
    )
    middle = inputs + keep_rows * jnp.dot(attended_rows, out_w, preferred_element_type=jnp.float32)
    gain_two, gate_w, up_w, down_w = (
        lax.all_gather(mlp_gain, ("wide", "narrow"), axis=0, tiled=True),
        lax.all_gather(w_gate, ("wide", "narrow"), axis=0, tiled=True),
        lax.all_gather(w_up, ("wide", "narrow"), axis=0, tiled=True),
        lax.all_gather(w_down, ("wide", "narrow"), axis=0, tiled=True),
    )
    inverse_two = lax.rsqrt(jnp.mean(middle * middle, axis=-1, keepdims=True) + epsilon)
    second_norm = (middle * inverse_two * gain_two.astype(jnp.float32)).astype(jnp.bfloat16)
    gate_value = jnp.dot(second_norm, gate_w, preferred_element_type=jnp.float32)
    up_value = jnp.dot(second_norm, up_w, preferred_element_type=jnp.float32)
    gate_sigmoid = jax.nn.sigmoid(gate_value)
    swish_value = gate_value * gate_sigmoid
    hidden = (swish_value * up_value).astype(jnp.bfloat16)
    output = (
        middle + keep_rows * jnp.dot(hidden, down_w, preferred_element_type=jnp.float32)
    ).astype(jnp.bfloat16)
    group_match = (
        group_ids.reshape(row_count)[:, None]
        == jnp.arange(exit_scale.shape[0], dtype=jnp.int32)[None, :]
    )
    token_scale = jnp.sum(jnp.where(group_match, exit_scale[None, :], 0.0), axis=1, keepdims=True)
    upstream = out_grad.astype(jnp.float32).reshape(row_count, model_width) * token_scale
    gain_two, gate_w, up_w, down_w = (
        lax.all_gather(mlp_gain, ("wide", "narrow"), axis=0, tiled=True),
        lax.all_gather(w_gate, ("wide", "narrow"), axis=0, tiled=True),
        lax.all_gather(w_up, ("wide", "narrow"), axis=0, tiled=True),
        lax.all_gather(w_down, ("wide", "narrow"), axis=0, tiled=True),
    )
    mixed_grad = (keep_rows * upstream).astype(jnp.bfloat16)
    grad_down = over_rows(hidden, mixed_grad)
    hidden_grad = against(mixed_grad, down_w)
    gate_grad = (
        hidden_grad * up_value * gate_sigmoid * (1.0 + gate_value * (1.0 - gate_sigmoid))
    ).astype(jnp.bfloat16)
    up_grad = (hidden_grad * swish_value).astype(jnp.bfloat16)
    grad_gate = over_rows(second_norm, gate_grad)
    grad_up = over_rows(second_norm, up_grad)
    norm_grad = against(gate_grad, gate_w) + against(up_grad, up_w)
    grad_gain_two = jnp.sum(norm_grad * middle * inverse_two, axis=0)
    scaled_two = gain_two.astype(jnp.float32) * norm_grad
    middle_grad = (
        upstream
        + inverse_two * scaled_two
        - middle
        * (inverse_two * inverse_two * inverse_two)
        * jnp.mean(scaled_two * middle, axis=-1, keepdims=True)
    )
    gain_two_share, gate_share, up_share, down_share = (
        lax.psum_scatter(grad_gain_two, ("wide", "narrow"), scatter_dimension=0, tiled=True),
        lax.psum_scatter(grad_gate, ("wide", "narrow"), scatter_dimension=0, tiled=True),
        lax.psum_scatter(grad_up, ("wide", "narrow"), scatter_dimension=0, tiled=True),
        lax.psum_scatter(grad_down, ("wide", "narrow"), scatter_dimension=0, tiled=True),
    )
    gain_one, query_w, key_w, value_w, out_w = (
        lax.all_gather(attn_gain, ("wide", "narrow"), axis=0, tiled=True),
        lax.all_gather(w_query, ("wide", "narrow"), axis=0, tiled=True),
        lax.all_gather(w_key, ("wide", "narrow"), axis=0, tiled=True),
        lax.all_gather(w_value, ("wide", "narrow"), axis=0, tiled=True),
        lax.all_gather(w_out, ("wide", "narrow"), axis=0, tiled=True),
    )
    branch_grad = (keep_rows * middle_grad).astype(jnp.bfloat16)
    grad_out = over_rows(attended_rows, branch_grad)
    attended_grad = against(branch_grad, out_w).astype(jnp.bfloat16)
    grouped_grad = (
        attended_grad.reshape(seq_count, span_len, kv_heads, group_size, head_dim)
        .transpose(0, 2, 3, 1, 4)
        .reshape(seq_count, kv_heads, stripe, head_dim)
    )
    row_delta = jnp.sum(grouped_grad.astype(jnp.float32) * attended, axis=-1)
    start_backward = (
        jnp.zeros((seq_count, kv_heads, stripe, head_dim), jnp.float32),
        jnp.zeros((seq_count, full_len, kv_heads * head_dim), jnp.float32),
        jnp.zeros((seq_count, full_len, kv_heads * head_dim), jnp.float32),
    )
    running = start_backward
    pieces = (
        lax.all_gather(key_heads, "wide", axis=1, tiled=True),
        lax.all_gather(value_heads, "wide", axis=1, tiled=True),
    )
    key_blocks = split_blocks(pieces[0], seq_count, kv_heads, head_dim)
    value_blocks = split_blocks(pieces[1], seq_count, kv_heads, head_dim)
    fold_block_len = key_blocks.shape[2]

    def advance(carried, block_item):
        key_block, value_block, block_index = block_item
        key_first = block_index * fold_block_len

        def compute_block(current):
            query_acc, key_acc, value_acc = current
            scores, allowed = block_scores(key_block, key_first)
            probabilities = jnp.where(allowed, jnp.exp(scores - log_total[..., None]), 0.0)
            value_part = jnp.einsum(
                "skrj,skrd->sjkd",
                probabilities.astype(jnp.bfloat16),
                grouped_grad,
                preferred_element_type=jnp.float32,
            )
            prob_grad = jnp.einsum(
                "skrd,sjkd->skrj", grouped_grad, value_block, preferred_element_type=jnp.float32
            )
            score_grad = (probabilities * (prob_grad - row_delta[..., None])).astype(jnp.bfloat16)
            query_acc = (
                query_acc
                + jnp.einsum(
                    "skrj,sjkd->skrd", score_grad, key_block, preferred_element_type=jnp.float32
                )
                * score_scale
            )
            key_part = (
                jnp.einsum(
                    "skrj,skrd->sjkd", score_grad, queries, preferred_element_type=jnp.float32
                )
                * score_scale
            )
            key_acc = add_rows(
                key_acc, key_part.reshape(seq_count, fold_block_len, kv_heads * head_dim), key_first
            )
            value_acc = add_rows(
                value_acc,
                value_part.reshape(seq_count, fold_block_len, kv_heads * head_dim),
                key_first,
            )
            return (query_acc, key_acc, value_acc)

        return (lax.cond(key_first <= last_query, compute_block, unchanged, carried), None)

    running, _ = lax.scan(
        advance,
        running,
        (key_blocks, value_blocks, jnp.arange(key_blocks.shape[0], dtype=jnp.int32)),
    )
    query_acc, key_acc, value_acc = running
    key_sum, value_sum = (
        lax.psum_scatter(
            key_acc.astype(jnp.bfloat16), "wide", scatter_dimension=1, tiled=True
        ).astype(jnp.float32),
        lax.psum_scatter(
            value_acc.astype(jnp.bfloat16), "wide", scatter_dimension=1, tiled=True
        ).astype(jnp.float32),
    )
    query_back = (
        query_acc.reshape(seq_count, kv_heads, group_size, span_len, head_dim)
        .transpose(0, 3, 1, 2, 4)
        .reshape(row_count, head_count, head_dim)
    )
    query_grad = (
        rotate(query_back, token_pos, -1.0)
        .reshape(row_count, head_count * head_dim)
        .astype(jnp.bfloat16)
    )
    key_grad = (
        rotate(key_sum.reshape(row_count, kv_heads, head_dim), token_pos, -1.0)
        .reshape(row_count, kv_heads * head_dim)
        .astype(jnp.bfloat16)
    )
    value_grad = value_sum.reshape(row_count, kv_heads * head_dim).astype(jnp.bfloat16)
    grad_query = over_rows(first_norm, query_grad)
    grad_key = over_rows(first_norm, key_grad)
    grad_value = over_rows(first_norm, value_grad)
    input_norm_grad = (
        against(query_grad, query_w) + against(key_grad, key_w) + against(value_grad, value_w)
    )
    grad_gain_one = jnp.sum(input_norm_grad * inputs * inverse_one, axis=0)
    scaled_one = gain_one.astype(jnp.float32) * input_norm_grad
    input_grad = (
        middle_grad
        + inverse_one * scaled_one
        - inputs
        * (inverse_one * inverse_one * inverse_one)
        * jnp.mean(scaled_one * inputs, axis=-1, keepdims=True)
    )
    gain_one_share, query_share, key_share, value_share, out_share = (
        lax.psum_scatter(grad_gain_one, ("wide", "narrow"), scatter_dimension=0, tiled=True),
        lax.psum_scatter(grad_query, ("wide", "narrow"), scatter_dimension=0, tiled=True),
        lax.psum_scatter(grad_key, ("wide", "narrow"), scatter_dimension=0, tiled=True),
        lax.psum_scatter(grad_value, ("wide", "narrow"), scatter_dimension=0, tiled=True),
        lax.psum_scatter(grad_out, ("wide", "narrow"), scatter_dimension=0, tiled=True),
    )
    return (
        output.reshape(seq_count, span_len, model_width),
        input_grad.astype(jnp.bfloat16).reshape(seq_count, span_len, model_width),
        gain_one_share,
        query_share,
        key_share,
        value_share,
        out_share,
        gain_two_share,
        gate_share,
        up_share,
        down_share,
    )


def line_body(
    tokens,
    attn_gain,
    w_query,
    w_key,
    w_value,
    w_out,
    mlp_gain,
    w_gate,
    w_up,
    w_down,
    keep_mask,
    group_ids,
    positions,
    exit_scale,
    out_grad,
):
    f32 = jnp.float32
    bf16 = jnp.bfloat16
    _, span_len, model_width = tokens.shape
    line = lax.axis_size("z")
    rows_each = w_query.shape[0]
    q_cols = HEADS // line * HD
    ff_cols = w_gate.shape[1] // line
    group_len = span_len * line

    def by_columns(weight, columns):
        return weight.reshape(rows_each, line, columns).transpose(1, 0, 2)

    out_w = lax.all_gather(w_out, ("z", "x", "y", "c"), axis=0, tiled=True)
    down_w = lax.all_gather(w_down, ("x", "y", "c"), axis=0, tiled=True)
    own_x = tokens[0].astype(f32)
    keep = keep_mask[0].astype(f32)
    group_match = group_ids[0][:, None] == jnp.arange(exit_scale.shape[0], dtype=jnp.int32)[None, :]
    token_scale = jnp.sum(jnp.where(group_match, exit_scale[None, :], 0.0), axis=1, keepdims=True)
    upstream = out_grad[0].astype(f32) * token_scale

    core = lax.axis_index("c")
    gain_row = jnp.zeros((q_cols + 2 * HD,), bf16)
    gain_row = lax.dynamic_update_slice_in_dim(gain_row, attn_gain, core * rows_each, 0)
    gain_row = lax.dynamic_update_slice_in_dim(gain_row, mlp_gain, HD + core * rows_each, 0)
    gain_rows = jnp.broadcast_to(gain_row, (line, 16, gain_row.shape[0]))
    pack_attn = jnp.concatenate(
        [by_columns(w_query, q_cols), by_columns(w_key, HD), by_columns(w_value, HD)], axis=2
    )
    pack_attn = jnp.concatenate([pack_attn, gain_rows], axis=1)
    pack_ff = jnp.concatenate([by_columns(w_gate, ff_cols), by_columns(w_up, ff_cols)], axis=2)
    freqs = 10000.0 ** (-2.0 * jnp.arange(HD // 2, dtype=f32) / HD)
    angles = positions[0].astype(f32)[:, None] * freqs[None, :]
    table = jnp.concatenate([jnp.cos(angles), jnp.sin(angles)], axis=1)
    own_mixed = (keep * upstream).astype(bf16)
    first_tokens, own_mixed, upstream = lax.optimization_barrier((tokens[0], own_mixed, upstream))
    (
        x_blocks,
        near_w,
        gain_all,
        first_norm,
        queries,
        both_kv,
        log_total,
        turns,
        attended_rows,
        ff_w,
    ) = forward_call(first_tokens, table, pack_attn, pack_ff, line)
    keep_tile = jnp.broadcast_to(keep, (8, HD))
    middle, norm_grad, mixed, grad_down, grad_ff, ff_half = mlp_call(
        keep_tile,
        gain_all,
        own_mixed,
        x_blocks,
        attended_rows,
        out_w,
        ff_w,
        down_w,
        line,
    )
    grad_down = grad_down.astype(f32)
    output = (middle + keep * mixed).astype(bf16)
    middle_grad, input_norm_grad, ff_back, out_back, qkv_back = backward_call(
        (
            upstream,
            middle,
            norm_grad,
            keep_tile,
            gain_all,
        ),
        (queries, both_kv, log_total, turns),
        out_w,
        attended_rows,
        near_w,
        first_norm,
        grad_ff,
        ff_half,
        line,
    )
    ff_back = ff_back.astype(f32)
    qkv_back = qkv_back.astype(f32)
    grad_out = jnp.sum(out_back.astype(f32), axis=0)
    gain_one = gain_all[0, :1]
    inverse_one = lax.rsqrt(jnp.mean(own_x * own_x, axis=-1, keepdims=True) + epsilon)
    scaled_one = gain_one * input_norm_grad
    input_grad = (
        middle_grad
        + inverse_one * scaled_one
        - own_x
        * (inverse_one * inverse_one * inverse_one)
        * jnp.mean(scaled_one * own_x, axis=-1, keepdims=True)
    )

    def side_by_side(blocks):
        return blocks.transpose(1, 0, 2).reshape(rows_each, -1)

    grad_query = side_by_side(qkv_back[:, :, :q_cols])
    grad_key = side_by_side(qkv_back[:, :, q_cols : q_cols + HD])
    grad_value = side_by_side(qkv_back[:, :, q_cols + HD :])
    grad_gate = side_by_side(ff_back[:, :, :ff_cols])
    grad_up = side_by_side(ff_back[:, :, ff_cols:])

    def gain_grad(pairs, gain):
        total = sum(jnp.sum(weight.astype(f32) * grad, axis=1) for weight, grad in pairs)
        return total / gain.astype(f32)

    return (
        output[None],
        input_grad.astype(bf16)[None],
        gain_grad([(w_query, grad_query), (w_key, grad_key), (w_value, grad_value)], attn_gain),
        grad_query,
        grad_key,
        grad_value,
        grad_out,
        gain_grad([(w_gate, grad_gate), (w_up, grad_up)], mlp_gain),
        grad_gate,
        grad_up,
        grad_down,
    )


def solution(mesh):
    wide, narrow = mesh.shape["wide"], mesh.shape["narrow"]
    if wide == 2 * KVH and narrow == 4:
        mesh = Mesh(mesh.devices.reshape(wide // 2, 2, 2, 2), ("z", "x", "y", "c"))
        body, wide, narrow = line_body, ("z", "x"), ("y", "c")
    else:
        body, wide, narrow = general_body, ("wide",), ("narrow",)
    token_spec = P(narrow, wide, None)
    id_spec = P(narrow, wide)
    gain_spec = P(wide + narrow)
    weight_spec = P(wide + narrow, None)
    return jax.shard_map(
        body,
        mesh=mesh,
        in_specs=(
            token_spec,
            gain_spec,
            weight_spec,
            weight_spec,
            weight_spec,
            weight_spec,
            gain_spec,
            weight_spec,
            weight_spec,
            weight_spec,
            P(narrow),
            id_spec,
            id_spec,
            P(),
            token_spec,
        ),
        out_specs=(
            token_spec,
            token_spec,
            gain_spec,
            weight_spec,
            weight_spec,
            weight_spec,
            weight_spec,
            gain_spec,
            weight_spec,
            weight_spec,
            weight_spec,
        ),
        check_vma=False,
    )
```

```python
import functools
import math

import jax
import jax.numpy as jnp
from jax import lax
from jax.experimental import pallas as pl
from jax.experimental.pallas import tpu as pltpu
from jax.sharding import Mesh
from jax.sharding import PartitionSpec as P

HEADS = 16
KVH = 4
HD = 128


epsilon = 1e-05


def rotate(vectors, token_pos, direction):
    half_size = vectors.shape[-1] // 2
    freqs = 10000.0 ** (-2.0 * jnp.arange(half_size, dtype=jnp.float32) / vectors.shape[-1])
    angles = token_pos.astype(jnp.float32)[:, None] * freqs[None, :]
    cosine = jnp.cos(angles)[:, None, :]
    sine = direction * jnp.sin(angles)[:, None, :]
    first_half = vectors[..., :half_size]
    second_half = vectors[..., half_size:]
    return jnp.concatenate(
        [first_half * cosine - second_half * sine, second_half * cosine + first_half * sine],
        axis=-1,
    )


def split_blocks(piece_arr, seq_count, kv_heads, head_dim):
    piece_len = piece_arr.shape[1]
    block_len = math.gcd(piece_len, 512)
    shaped = piece_arr.reshape(seq_count, piece_len // block_len, block_len, kv_heads, head_dim)
    return shaped.transpose(1, 0, 2, 3, 4)


def add_rows(whole_arr, update, first_row):
    current = lax.dynamic_slice_in_dim(whole_arr, first_row, update.shape[1], 1)
    return lax.dynamic_update_slice_in_dim(whole_arr, current + update, first_row, 1)


def over_rows(left, right):
    return lax.dot_general(
        left, right, (((0,), (0,)), ((), ())), preferred_element_type=jnp.float32
    )


def against(left, right):
    return lax.dot_general(
        left, right, (((1,), (1,)), ((), ())), preferred_element_type=jnp.float32
    )


def unchanged(carried):
    return carried


MESH = pl.DeviceIdType.MESH
AXES = ("z", "x", "y", "c")


class Links:
    def __init__(self, send_sems, recv_sems, line):
        self.send_sems, self.recv_sems, self.line = send_sems, recv_sems, line
        self.z, self.x, self.y, self.c = (lax.axis_index(name) for name in AXES)
        self.slot = self.x * 4 + self.y * 2 + self.c
        self.used = 0
        self.sent = []

    def device(self, to):
        if to == "x":
            return (self.z, 1 - self.x, self.y, self.c)
        if to == "y":
            return (self.z, self.x, 1 - self.y, self.c)
        if to == "c":
            return (self.z, self.x, self.y, 1 - self.c)
        return (self.along(to), self.x, self.y, self.c)

    def along(self, step):
        return lax.rem(self.z + step + self.line, self.line)

    def other(self, to):
        slot = self.slot
        for name in to:
            bit = {"x": 4, "y": 2, "c": 1}[name]
            here = {"x": self.x, "y": self.y, "c": self.c}[name]
            slot = slot + bit * (1 - 2 * here)
        return slot

    def meet(self, targets):
        barrier = pltpu.get_barrier_semaphore()
        for to in targets:
            pl.semaphore_signal(barrier, inc=1, device_id=self.device(to), device_id_type=MESH)
        pl.semaphore_wait(barrier, len(targets))

    def send(self, source, target, to):
        copy = pltpu.make_async_remote_copy(
            src_ref=source,
            dst_ref=target,
            send_sem=self.send_sems.at[self.used],
            recv_sem=self.recv_sems.at[self.used],
            device_id=self.device(to),
            device_id_type=MESH,
        )
        copy.start()
        self.used += 1
        self.sent.append(copy)
        return copy

    def keep(self, source, target):
        copy = pltpu.make_async_copy(source, target, self.send_sems.at[self.used])
        copy.start()
        self.used += 1
        return copy

    def finish(self):
        for copy in self.sent:
            copy.wait_send()


class NearGather:
    def __init__(self, links, slot):
        self.links, self.slot = links, slot
        self.got = {}

    def offer(self, block, source):
        target = self.slot(block, self.links.slot)
        for to in ("x", "y", "c"):
            self.got[block, to] = self.links.send(source, target, to)

    def relay(self, block, first):
        links = self.links
        for to, then in (("x", "y"), ("y", "x")):
            self.got[block, to].wait_recv()
            place = self.slot(block, links.other(to))
            self.got[block, to + "c"] = links.send(place, place, "c")
            if to == first:
                self.got[block, "xy"] = links.send(place, place, then)

    def close(self, block):
        self.got[block, "xy"].wait_recv()
        place = self.slot(block, self.links.other("xy"))
        self.got[block, "xyc"] = self.links.send(place, place, "c")

    def wait(self, blocks):
        for block in blocks:
            for to in ("c", "xc", "yc", "xyc"):
                self.got[block, to].wait_recv()

    def settle(self):
        for copy in self.got.values():
            copy.wait_send()
        mine = [id(copy) for copy in self.got.values()]
        self.links.sent = [copy for copy in self.links.sent if id(copy) not in mine]


class RingGather:
    def __init__(self, links, source, place, pieces=4):
        self.links, self.source, self.place, self.pieces = links, source, place, pieces
        self.rows = source.shape[0] // pieces
        self.last = [None] * pieces

    def step(self, number):
        for piece in range(self.pieces):
            way = 1 if piece < self.pieces // 2 else -1
            rows = pl.ds(piece * self.rows, self.rows)
            place = self.place(self.links.along(-way * number), rows)
            if number > 0:
                self.last[piece].wait_recv()
            if number < self.links.line - 1:
                origin = self.source.at[rows] if number == 0 else place
                self.last[piece] = self.links.send(origin, place, way)


def first_kernel(
    line,
    freq_ref,
    x_ref,
    place_ref,
    pack_ref,
    ff_ref,
    out_ref,
    xs_ref,
    weight_ref,
    gain_ref,
    norm_ref,
    query_ref,
    kv_ref,
    peak_ref,
    turn_ref,
    atts_ref,
    ffs_ref,
    outs_ref,
    x_all,
    places,
    weights,
    gains,
    norm,
    turns,
    flat,
    query,
    kv,
    peak,
    att,
    send_sems,
    recv_sems,
):
    f32, bf16 = jnp.float32, jnp.bfloat16
    links = Links(send_sems, recv_sems, line)
    far = [1, line - 1] + list(range(2, line - 1))
    links.meet(["x", "y", "c"] + far)
    here = links.slot
    span_len, width = x_ref.shape
    group_len = line * span_len
    rows_each = ff_ref.shape[1]
    q_cols = query.shape[1]
    heads = q_cols // HD
    local = []

    near = NearGather(links, lambda block, place: weights.at[links.along(-block), place])
    far_ff = NearGather(links, lambda block, place: ffs_ref.at[links.along(-block), place])
    far_out = NearGather(links, lambda block, place: outs_ref.at[links.along(-block), place])
    ring = RingGather(links, x_ref, lambda block, rows: x_all.at[block, rows])
    own = [
        links.keep(x_ref, x_all.at[links.z]),
        links.keep(place_ref, places.at[links.z]),
        links.keep(pack_ref.at[links.z], weights.at[links.z, here]),
    ]
    turned = {k: links.send(pack_ref.at[links.along(k)], weights.at[links.z, here], k) for k in far}
    placed = [links.send(place_ref, places.at[links.z], k) for k in far]
    turned_ff = {k: links.send(ff_ref.at[links.along(k)], ffs_ref.at[links.z, here], k) for k in far}
    near.offer(0, pack_ref.at[links.z])
    far_ff.offer(0, ff_ref.at[links.z])
    local.append(links.keep(ff_ref.at[links.z], ffs_ref.at[links.z, here]))
    local.append(links.keep(out_ref, outs_ref.at[links.z, here]))

    def move_out(k):
        moved.wait_recv()
        block = outs_ref.at[links.along(-k), here]
        onward = links.send(block, block, 1) if k < line - 1 else None
        far_out.offer(k, block)
        return onward

    for k in far:
        turned[k].wait_recv()
        near.offer(k, weights.at[links.along(-k), here])
    ring.step(0)
    for k in [0] + far:
        near.relay(k, "x" if k < line // 2 else "y")
    turned_ff[far[0]].wait_recv()
    far_ff.offer(far[0], ffs_ref.at[links.along(-far[0]), here])
    ring.step(1)
    for k in [0] + far:
        near.close(k)
    far_ff.relay(0, "x")
    ring.step(2)
    moved = links.send(out_ref, outs_ref.at[links.z, here], 1)
    far_out.offer(0, out_ref)
    for copy in own:
        copy.wait()
    for copy in placed:
        copy.wait_recv()

    lane = lax.broadcasted_iota(jnp.int32, (span_len, HD), 1)
    token = lax.broadcasted_iota(jnp.int32, (span_len, span_len), 0)
    across = lax.broadcasted_iota(jnp.int32, (span_len, span_len), 1)
    for block in range(line):
        row = jnp.broadcast_to(places[block, 0:1], (span_len, span_len))
        column = jnp.sum(jnp.where(token == across, row, 0.0), axis=1, keepdims=True)
        angles = column * freq_ref[0:1]
        rows = slice(block * span_len, (block + 1) * span_len)
        sine = jnp.sin(angles)
        turns[0, rows] = jnp.cos(angles)
        turns[1, rows] = jnp.where(lane < HD // 2, -sine, sine)
    local.append(links.keep(turns, turn_ref))
    near.wait(range(line))
    for index in range(line * 4):
        z, q = divmod(index, 4)
        for which in range(2):
            lanes = slice(which * HD, (which + 1) * HD)
            both = [weights[z, 2 * q + c, rows_each : rows_each + 16, lanes].astype(f32) for c in range(2)]
            gains[which, :, index * HD : (index + 1) * HD] = both[0] + both[1]
    local.append(links.keep(weights, weight_ref))
    local.append(links.keep(gains, gain_ref))
    far_ff.relay(far[0], "y")
    ring.step(3)
    local.append(links.keep(x_all, xs_ref))

    def normalise(index, carry):
        block = index // (span_len // 16)
        rows = pl.ds(pl.multiple_of(lax.rem(index, span_len // 16) * 16, 16), 16)
        values = x_all[block, rows].astype(f32)
        inverse = lax.rsqrt(jnp.mean(values * values, axis=-1, keepdims=True) + epsilon)
        target = pl.ds(pl.multiple_of(index * 16, 16), 16)
        norm[target] = (values * inverse * gains[0]).astype(bf16)
        return carry

    lax.fori_loop(0, group_len // 16, normalise, 0)
    local.append(links.keep(norm, norm_ref))

    def project(low, high):
        step = group_len // 2
        for part in range(2):
            rows = slice(part * step, (part + 1) * step)
            total = None
            for z in range(line):
                weight = weights[z, :, :rows_each, low:high].reshape(8 * rows_each, high - low)
                term = jnp.dot(
                    norm[rows, z * 8 * rows_each : (z + 1) * 8 * rows_each],
                    weight,
                    preferred_element_type=f32,
                )
                total = term if total is None else total + term
            flat[rows, low:high] = total

    def turn(values, rows):
        return values * turns[0, rows] + pltpu.roll(values, HD // 2, 1) * turns[1, rows]

    project(q_cols, q_cols + 2 * HD)
    for block in range(line):
        rows = slice(block * span_len, (block + 1) * span_len)
        kv[0, rows, :HD] = turn(flat[rows, q_cols : q_cols + HD], rows).astype(bf16)
        kv[0, rows, HD:] = flat[rows, q_cols + HD : q_cols + 2 * HD].astype(bf16)
    exchange = links.send(kv.at[0], kv.at[1], "x")
    project(0, q_cols)
    for block in range(line):
        rows = slice(block * span_len, (block + 1) * span_len)
        for head in range(heads):
            lanes = slice(head * HD, (head + 1) * HD)
            query[rows, lanes] = turn(flat[rows, lanes], rows).astype(bf16)
    local.append(links.keep(query, query_ref))
    exchange.wait_recv()
    moved = move_out(1)
    local.append(links.keep(kv, kv_ref))

    scale = 1.0 / math.sqrt(HD)
    peak[...] = jnp.zeros_like(peak)

    def attend(head, carry):
        lanes = pl.ds(pl.multiple_of(head * HD, HD), HD)
        for block in range(line):
            rows = slice(block * span_len, (block + 1) * span_len)
            reach = (block + 1) * span_len
            part = query[rows, lanes]
            row = lax.broadcasted_iota(jnp.int32, (span_len, reach), 0) + block * span_len
            column = lax.broadcasted_iota(jnp.int32, (span_len, reach), 1)
            allowed = (column <= row, column < (block + links.x) * span_len)
            scores = []
            for half in range(2):
                score = lax.dot_general(
                    part, kv[half, :reach, :HD], (((1,), (1,)), ((), ())), preferred_element_type=f32
                )
                scores.append(jnp.where(allowed[half], score * scale, -1e30))
            top = jnp.maximum(
                jnp.max(scores[0], axis=-1, keepdims=True), jnp.max(scores[1], axis=-1, keepdims=True)
            )
            total, mixed = None, None
            for half in range(2):
                weight = jnp.exp(scores[half] - top)
                count = jnp.sum(weight, axis=-1, keepdims=True)
                term = jnp.dot(weight.astype(bf16), kv[half, :reach, HD:], preferred_element_type=f32)
                total = count if total is None else total + count
                mixed = term if mixed is None else mixed + term
            att[rows, lanes] = (mixed / total).astype(bf16)
            spot = lax.broadcasted_iota(jnp.int32, (span_len, HD), 1) == head
            peak[rows] = jnp.where(spot, top + jnp.log(total), peak[rows])
        return carry

    lax.fori_loop(0, heads, attend, 0)
    local.append(links.keep(peak, peak_ref))

    def place(block, rows):
        return atts_ref.at[rows, pl.ds(pl.multiple_of(block * q_cols, q_cols), q_cols)]

    att_ring = RingGather(links, att, place)
    local.append(links.keep(att, place(links.z, pl.ds(0, group_len))))
    att_ring.step(0)
    far_ff.close(0)
    far_ff.close(far[0])
    far_out.relay(0, "x")
    moved = move_out(2)
    far_out.relay(1, "x")
    att_ring.step(1)
    for k in range(3, line):
        moved = move_out(k)
    far_out.relay(2, "y")
    att_ring.step(2)
    for k in range(3, line):
        far_out.relay(k, "y")
    for k in range(line):
        far_out.close(k)
    att_ring.step(3)
    far_out.wait(range(line))
    far_ff.wait([0, far[0]])
    for k in far[1:]:
        turned_ff[k].wait_recv()
    links.finish()
    for copy in local:
        copy.wait()


def add_rows_of(target, values, count):
    def add(index, carry):
        rows = pl.ds(pl.multiple_of(index * 16, 16), 16)
        target[rows] = target[rows] + values[rows]
        return carry

    lax.fori_loop(0, count // 16, add, 0)


class NearSum:
    def __init__(self, links, source, own, from_core, from_first, from_second, first, in_place=False):
        self.links, self.source, self.own, self.first = links, source, own, first
        self.in_place = in_place
        self.from_core, self.from_first, self.from_second = from_core, from_first, from_second

    def start(self):
        links = self.links
        if not self.in_place:
            self.local = links.keep(self.source(links.c), self.own)
        self.copy = links.send(self.source(1 - links.c), self.from_core, "c")

    def add(self, target, values):
        add_rows_of(target, values, target.shape[0])

    def core_done(self):
        links = self.links
        self.copy.wait_recv()
        if not self.in_place:
            self.local.wait()
        for x in range(2):
            for y in range(2):
                self.add(self.own.at[x, y], self.from_core.at[x, y])
        if self.first == "x":
            self.copy = links.send(self.own.at[1 - links.x], self.from_first, "x")
        else:
            self.copy = links.send(self.own.at[:, 1 - links.y], self.from_first, "y")

    def first_done(self):
        links = self.links
        self.copy.wait_recv()
        for other in range(2):
            place = (links.x, other) if self.first == "x" else (other, links.y)
            self.add(self.own.at[place], self.from_first.at[other])
        if self.first == "x":
            self.copy = links.send(self.own.at[links.x, 1 - links.y], self.from_second, "y")
        else:
            self.copy = links.send(self.own.at[1 - links.x, links.y], self.from_second, "x")

    def second_done(self):
        self.copy.wait_recv()
        total = self.own.at[self.links.x, self.links.y]
        self.add(total, self.from_second)
        return total


def sum_space(blocks, rows, columns):
    shape = (rows, columns)
    return [
        pltpu.VMEM((blocks, 2, 2) + shape, jnp.bfloat16),
        pltpu.VMEM((blocks, 2, 2) + shape, jnp.bfloat16),
        pltpu.VMEM((blocks, 2) + shape, jnp.bfloat16),
        pltpu.VMEM((blocks,) + shape, jnp.bfloat16),
    ]


class RingSum:
    def __init__(self, links, parts, total, got, pieces=4):
        self.links, self.parts, self.total, self.got = links, parts, total, got
        self.pieces, self.last = pieces, [None] * pieces
        self.rows = parts.shape[1] // pieces

    def step(self, number):
        links = self.links
        for piece in range(self.pieces):
            way = 1 if piece < self.pieces // 2 else -1
            block = links.along(-way * (number + 1))
            where = pl.ds(piece * self.rows, self.rows)
            if number == 0:
                source = self.parts.at[block, where]
            else:
                self.last[piece].wait_recv()
                total = self.got[number - 1, where].astype(jnp.float32) + self.parts[
                    block, where
                ].astype(jnp.float32)
                if number == links.line - 1:
                    self.total[where] = total
                    continue
                self.parts[block, where] = total.astype(self.parts.dtype)
                source = self.parts.at[block, where]
            self.last[piece] = links.send(source, self.got.at[number, where], way)


def link_call(kernel, collective_id, copies, shapes, arguments, spaces=None, scratch=(), vmem=16):
    any_space = pl.BlockSpec(memory_space=pl.ANY)
    near_space = pl.BlockSpec(memory_space=pltpu.VMEM)
    many = isinstance(shapes, tuple)
    if spaces is None:
        spaces = "h" * (len(arguments) + (len(shapes) if many else 1))
    specs = [near_space if space == "v" else any_space for space in spaces]
    return pl.pallas_call(
        kernel,
        out_shape=shapes,
        in_specs=specs[: len(arguments)],
        out_specs=tuple(specs[len(arguments) :]) if many else specs[-1],
        scratch_shapes=list(scratch)
        + [pltpu.SemaphoreType.DMA((copies,)), pltpu.SemaphoreType.DMA((copies,))],
        compiler_params=pltpu.CompilerParams(
            collective_id=collective_id, has_side_effects=True, vmem_limit_bytes=vmem * 2**20
        ),
    )(*arguments)


def forward_call(freqs, tokens, places, pack, pack_ff, w_out, line):
    span_len, width = tokens.shape
    group_len = line * span_len
    rows_each = pack_ff.shape[1]
    qkv_cols = pack.shape[2]
    q_cols = qkv_cols - 2 * HD
    f32, bf16 = jnp.float32, jnp.bfloat16
    outs = (
        ((line, span_len, width), bf16),
        ((line, 8) + pack.shape[1:], bf16),
        ((2, 16, width), f32),
        ((group_len, width), bf16),
        ((group_len, q_cols), bf16),
        ((2, group_len, 2 * HD), bf16),
        ((group_len, HD), f32),
        ((2, group_len, HD), f32),
        ((group_len, line * q_cols), bf16),
        ((line, 8) + pack_ff.shape[1:], bf16),
        ((line, 8) + w_out.shape, bf16),
    )
    return link_call(
        functools.partial(first_kernel, line),
        0,
        176,
        tuple(jax.ShapeDtypeStruct(*out) for out in outs),
        (freqs, tokens, places, pack, pack_ff, w_out),
        "v" + "h" * 16,
        scratch=[
            pltpu.VMEM((line, span_len, width), bf16),
            pltpu.VMEM((line,) + places.shape, f32),
            pltpu.VMEM((line, 8) + pack.shape[1:], bf16),
            pltpu.VMEM((2, 16, width), f32),
            pltpu.VMEM((group_len, width), bf16),
            pltpu.VMEM((2, group_len, HD), f32),
            pltpu.VMEM((group_len, qkv_cols), f32),
            pltpu.VMEM((group_len, q_cols), bf16),
            pltpu.VMEM((2, group_len, 2 * HD), bf16),
            pltpu.VMEM((group_len, HD), f32),
            pltpu.VMEM((group_len, q_cols), bf16),
        ],
        vmem=48,
    )


def mlp_kernel(
    line,
    cuts,
    keep_ref,
    gain_ref,
    mix_ref,
    xs_ref,
    atts_ref,
    out_ref,
    ff_ref,
    down_ref,
    middle_ref,
    total_ref,
    mixed_total_ref,
    sum_ref,
    grad_ff_ref,
    ff_half_ref,
    big,
    ff,
    down,
    norm,
    parts,
    mixed,
    gate_up,
    hidden,
    both_grad,
    got,
    mixed_parts,
    mixed_got,
    *scratch,
):
    f32, bf16 = jnp.float32, jnp.bfloat16
    space, (send_sems, recv_sems) = scratch[:-2], scratch[-2:]
    links = Links(send_sems, recv_sems, line)
    links.meet(["x", "y", "c", 1, line - 1])
    far = [1, line - 1] + list(range(2, line - 1))
    span_len, width = mix_ref.shape
    group_len = line * span_len
    ff_cols = hidden.shape[1]
    block_rows = width // line
    rows_each = block_rows // 8
    chunk = 2 * HD
    stay = links.keep(mix_ref, mixed.at[links.z])
    mix_ring = RingGather(links, mix_ref, lambda block, rows: mixed.at[block, rows])
    mix_ring.step(0)
    early = [
        links.keep(out_ref, big),
        links.keep(atts_ref, norm),
        links.keep(xs_ref, parts),
    ]
    here = (links.x, links.y, links.c)
    near = NearGather(
        links, lambda block, place: ff.at[links.along(-block), place // 4, place // 2 % 2, place % 2]
    )
    late = [links.keep(down_ref, down)]
    for k in (0, far[0]):
        late.append(links.keep(ff_ref.at[links.along(-k)], ff.at[links.along(-k)]))
    for k in far[1:]:
        block = ff_ref.at[(links.along(-k),) + here]
        late.append(links.keep(block, ff.at[(links.along(-k),) + here]))
        near.offer(k, block)
    ring = RingSum(links, parts, total_ref, got)
    mixed_ring = RingSum(links, mixed_parts, mixed_total_ref, mixed_got)
    items = []
    ff_items = []
    for index, k in enumerate(far[:2]):
        block = links.along(k)
        core, first, second = space[:3]
        ff_items.append(
            NearSum(
                links,
                lambda c, block=block: ff.at[block, :, :, c],
                ff.at[block, :, :, links.c],
                core.at[index],
                first.at[index],
                second.at[index],
                "xy"[index % 2],
                True,
            )
        )
    for index, (low, high) in enumerate(cuts):
        rows = pl.ds(low, high - low)
        core, first, second = space[3 * index + 3 : 3 * index + 6]
        items.append(
            NearSum(
                links,
                lambda c, rows=rows: big.at[:, :, c, rows],
                big.at[:, :, links.c, rows],
                core.at[0],
                first.at[0],
                second.at[0],
                "xy"[index % 2],
                True,
            )
        )
    for copy in early:
        copy.wait()

    half = group_len // 2
    out_rows = width // 8
    for part in range(2):
        low = part * half
        for column in range(4):
            lanes = slice(column * width // 4, (column + 1) * width // 4)
            value = None
            for k in range(8):
                term = jnp.dot(
                    norm[low : low + half, k * out_rows : (k + 1) * out_rows],
                    big[k // 4, k // 2 % 2, k % 2, :, lanes],
                    preferred_element_type=f32,
                )
                value = term if value is None else value + term
            gate_up[:half, lanes] = value * keep_ref[0:1, 0:1]

        def normalise(index, carry, low=low):
            block = (low // 16 + index) // (span_len // 16)
            rows = pl.ds(pl.multiple_of(index * 16, 16), 16)
            inside = pl.ds(pl.multiple_of(lax.rem(index, span_len // 16) * 16, 16), 16)
            values = parts[block, inside].astype(f32) + gate_up[rows, :width]
            gate_up[rows, :width] = values
            inverse = lax.rsqrt(jnp.mean(values * values, axis=-1, keepdims=True) + epsilon)
            target = pl.ds(pl.multiple_of(low + index * 16, 16), 16)
            norm[target] = (values * inverse * gain_ref[1]).astype(bf16)
            return carry

        lax.fori_loop(0, half // 16, normalise, 0)

        @pl.when(links.z // (line // 2) == part)
        def _():
            where = pl.multiple_of(lax.rem(links.z, line // 2) * span_len, span_len)
            middle_ref[...] = gate_up[pl.ds(where, span_len), :width]

        for index, k in enumerate(far[1:]):
            if part == 0:
                near.relay(k, "xy"[index % 2])
            else:
                near.close(k)
    mix_ring.step(1)
    near.wait(far[1:])
    for copy in late:
        copy.wait()

    def columns_of(lanes, size):
        return ff[:, :, :, :, :, lanes].reshape(width, size)

    def forward(low, size):
        gates, ups = pl.ds(low, size), pl.ds(low + ff_cols, size)
        gate = jnp.dot(norm[...], columns_of(gates, size), preferred_element_type=f32)
        gate_up[:, gates] = gate
        swish = gate * jax.nn.sigmoid(gate)
        up = jnp.dot(norm[...], columns_of(ups, size), preferred_element_type=f32)
        gate_up[:, ups] = up
        hidden[:, gates] = (swish * up).astype(bf16)

    def backward(low, size):
        gates, ups = pl.ds(low, size), pl.ds(low + ff_cols, size)
        grad = lax.dot_general(
            mixed[...].reshape(group_len, width),
            down[gates],
            (((1,), (1,)), ((), ())),
            preferred_element_type=f32,
        )
        gate, up = gate_up[:, gates], gate_up[:, ups]
        sigmoid = jax.nn.sigmoid(gate)
        both_grad[:, gates] = (grad * up * sigmoid * (1.0 + gate * (1.0 - sigmoid))).astype(bf16)
        both_grad[:, ups] = (grad * (gate * sigmoid)).astype(bf16)

    def over_chunks(work, extent):
        def one(index, carry):
            work(pl.multiple_of(index * chunk, chunk), chunk)
            return carry

        lax.fori_loop(0, extent // chunk, one, 0)
        if extent % chunk:
            work(extent // chunk * chunk, extent % chunk)

    over_chunks(forward, ff_cols)
    mix_ring.step(2)

    def mixed_part(low, size):
        lanes = pl.ds(low, size)
        value = jnp.dot(hidden[...], down[:, lanes], preferred_element_type=f32).astype(bf16)
        mixed_parts[:, :, lanes] = value.reshape(line, span_len, size)

    over_chunks(mixed_part, width)
    mixed_ring.step(0)
    stay.wait()
    mix_ring.step(3)
    over_chunks(backward, ff_cols)

    def norm_part(index, carry):
        size = 4 * rows_each
        weight = ff[index // 2, lax.rem(index, 2)].reshape(size, 2 * ff_cols)
        value = lax.dot_general(
            both_grad[...], weight, (((1,), (1,)), ((), ())), preferred_element_type=f32
        ).astype(bf16)
        lanes = pl.ds(pl.multiple_of(index * size, size), size)
        parts[:, :, lanes] = value.reshape(line, span_len, size)
        return carry

    lax.fori_loop(0, 2 * line, norm_part, 0)
    near.settle()
    ring.step(0)
    mixed_ring.step(1)

    def ff_block(block):
        norm_rows = norm[:, pl.ds(pl.multiple_of(block * block_rows, block_rows), block_rows)].T

        def ff_part(low, size):
            lanes = pl.ds(low, size)
            value = jnp.dot(norm_rows, both_grad[:, lanes], preferred_element_type=f32)
            ff[block, :, :, :, :, lanes] = value.astype(bf16).reshape(2, 2, 2, rows_each, size)

        over_chunks(ff_part, 2 * ff_cols)

    for item, k in zip(ff_items, far):
        ff_block(links.along(k))
        item.start()
    hidden_rows = hidden[...].T

    def down_part(low, size):
        lanes = pl.ds(low, size)
        value = jnp.dot(
            hidden_rows,
            mixed[:, :, lanes].reshape(group_len, size),
            preferred_element_type=f32,
        ).astype(bf16)
        big[:, :, :, : cuts[-1][1], lanes] = value.reshape(2, 2, 2, cuts[-1][1], size)

    ring.step(1)
    for item in ff_items:
        item.core_done()
    over_chunks(down_part, width)
    for item in items:
        item.start()
    mixed_ring.step(2)
    ring.step(2)
    for item in items:
        item.core_done()
    sent = []
    for k in far[2:] + [0]:
        block = links.along(k)
        ff_block(block)
        sent.append(links.keep(ff.at[block], grad_ff_ref.at[block]))
    for item in ff_items:
        item.first_done()
    ring.step(3)
    for item in items:
        item.first_done()
    for index, item in enumerate(ff_items):
        sent.append(links.keep(item.second_done(), ff_half_ref.at[index]))
    mixed_ring.step(3)
    for item, (low, high) in zip(items, cuts):
        sum_ref[low:high] = item.second_done()[...]
    links.finish()
    for copy in sent:
        copy.wait()


def mlp_call(keep, gains, mixed, x_blocks, attended, out_w, ff_w, down_w, line):
    f32, bf16 = jnp.float32, jnp.bfloat16
    span_len, width = mixed.shape
    group_len = line * span_len
    ff_rows, both_cols, rows_each = down_w.shape[0], ff_w.shape[3], ff_w.shape[2]
    ff_w = ff_w.reshape(line, 2, 2, 2, rows_each, both_cols)
    rows = ff_rows // 8
    half = (rows // 2 + 15) // 16 * 16
    cuts = ((0, half), (half, rows))
    blocks = (line, span_len, width)
    token = jax.ShapeDtypeStruct((span_len, width), f32)
    return link_call(
        functools.partial(mlp_kernel, line, cuts),
        2,
        96,
        (
            token,
            token,
            token,
            jax.ShapeDtypeStruct((rows, width), bf16),
            jax.ShapeDtypeStruct(ff_w.shape, bf16),
            jax.ShapeDtypeStruct((2, rows_each, both_cols), bf16),
        ),
        (keep, gains, mixed, x_blocks, attended, out_w.reshape(2, 2, 2, width // 8, width), ff_w, down_w),
        "vvhhhhhh" + "vvvvhh",
        [
            pltpu.VMEM((2, 2, 2, width // 8, width), bf16),
            pltpu.VMEM(ff_w.shape, bf16),
            pltpu.VMEM(down_w.shape, bf16),
            pltpu.VMEM((group_len, width), bf16),
            pltpu.VMEM(blocks, bf16),
            pltpu.VMEM(blocks, bf16),
            pltpu.VMEM((group_len, both_cols), f32),
            pltpu.VMEM((group_len, ff_rows), bf16),
            pltpu.VMEM((group_len, both_cols), bf16),
            pltpu.VMEM((line - 1, span_len, width), bf16),
            pltpu.VMEM(blocks, bf16),
            pltpu.VMEM((line - 1, span_len, width), bf16),
        ]
        + sum_space(2, rows_each, both_cols)[1:]
        + sum((sum_space(1, high - low, width)[1:] for low, high in cuts), []),
        vmem=63,
    )


def backward_kernel(
    line,
    up_ref,
    middle_ref,
    norm_grad_ref,
    keep_ref,
    gain_ref,
    query_ref,
    kv_ref,
    peak_ref,
    turn_ref,
    out_ref,
    atts_ref,
    weight_ref,
    norm_ref,
    ff_ref,
    ff_half_ref,
    middle_grad_ref,
    total_ref,
    ffs_ref,
    outs_ref,
    qkvs_ref,
    big,
    slim,
    norm,
    own_rows,
    own_columns,
    branch,
    own_grad,
    att_grad,
    query_back,
    kv_back,
    kv_out,
    kv_in,
    flat,
    parts,
    query,
    kv,
    peak,
    turns,
    *scratch,
):
    f32, bf16 = jnp.float32, jnp.bfloat16
    send_sems, recv_sems = scratch[-2:]
    got, sums = scratch[0], scratch[1:-2]
    links = Links(send_sems, recv_sems, line)
    far = [1, line - 1] + list(range(2, line - 1))
    order = far + [0]
    links.meet(["x", "y", "c"] + far)
    span_len, width = up_ref.shape
    group_len = line * span_len
    q_cols = query.shape[1]
    heads = q_cols // HD
    rows_z = width // line
    rows_each = rows_z // 8
    scale = 1.0 / math.sqrt(HD)

    def lanes_of(block):
        return pl.ds(pl.multiple_of(block * q_cols, q_cols), q_cols)

    here = pl.ds(pl.multiple_of(links.z * span_len, span_len), span_len)
    loads = [
        links.keep(out_ref, big),
        links.keep(atts_ref.at[here], own_rows),
        links.keep(atts_ref.at[:, lanes_of(links.z)], own_columns),
        links.keep(query_ref, query),
        links.keep(kv_ref, kv),
        links.keep(peak_ref, peak),
        links.keep(turn_ref, turns),
        links.keep(norm_ref, norm),
        links.keep(weight_ref.at[:, :, :, :, pl.ds(0, slim.shape[4])], slim),
    ]
    ring = RingSum(links, parts, total_ref, got)

    def items_of(source, space, in_place, order=order):
        items = []
        for index, k in enumerate(order):
            block = links.along(k)
            own = source.at[block, :, :, links.c] if in_place else space[0].at[index]
            core, first, second = space[-3:]
            items.append(
                NearSum(
                    links,
                    lambda c, block=block: source.at[block, :, :, c],
                    own,
                    core.at[index],
                    first.at[index],
                    second.at[index],
                    "xy"[index % 2],
                    in_place,
                )
            )
        return items

    ff_order = order[2:]
    ff_items = items_of(ff_ref, sums[:4], False, ff_order)
    out_items = items_of(big, sums[4:7], True)
    qkv_items = items_of(slim, sums[7:], True)
    local = []
    arrived = [
        links.send(ff_half_ref.at[index], ffs_ref.at[links.z], k) for index, k in enumerate(order[:2])
    ]

    def turn(items, target, low, high, order=order):
        for item, k in list(zip(items, order))[low:high]:
            total = item.second_done()
            if k == 0:
                local.append(links.keep(total, target.at[links.z]))
            else:
                arrived.append(links.send(total, target.at[links.z], k))

    def core_done(items, low, high):
        for item in items[low:high]:
            item.core_done()

    def first_done(items, low, high):
        for item in items[low:high]:
            item.first_done()

    half = line // 2
    for item in ff_items:
        item.start()

    def d_middle(index, carry):
        rows = pl.ds(pl.multiple_of(index * 16, 16), 16)
        middle = middle_ref[rows]
        inverse = lax.rsqrt(jnp.mean(middle * middle, axis=-1, keepdims=True) + epsilon)
        scaled = gain_ref[1] * norm_grad_ref[rows]
        grad = (
            up_ref[rows]
            + inverse * scaled
            - middle
            * (inverse * inverse * inverse)
            * jnp.mean(scaled * middle, axis=-1, keepdims=True)
        )
        middle_grad_ref[rows] = grad
        branch[rows] = (grad * keep_ref[0:1, 0:1]).astype(bf16)
        return carry

    lax.fori_loop(0, span_len // 16, d_middle, 0)
    for copy in loads:
        copy.wait()
    for z in range(line):
        weight = big[z].reshape(rows_z, width)
        own_grad[:, z * rows_z : (z + 1) * rows_z] = lax.dot_general(
            branch[...], weight, (((1,), (1,)), ((), ())), preferred_element_type=f32
        ).astype(bf16)
    turned = [links.send(own_grad.at[:, lanes_of(links.along(k))], att_grad.at[here], k) for k in far]
    stayed = links.keep(own_grad.at[:, lanes_of(links.z)], att_grad.at[here])
    core_done(ff_items, 0, line)
    for z in range(line):
        for part in range(4):
            columns = slice(part * width // 4, (part + 1) * width // 4)
            grad = lax.dot_general(
                own_rows[:, z * rows_z : (z + 1) * rows_z],
                branch[:, columns],
                (((0,), (0,)), ((), ())),
                preferred_element_type=f32,
            )
            big[z, :, :, :, :, columns] = grad.astype(bf16).reshape(2, 2, 2, rows_each, width // 4)
    for item in out_items:
        item.start()
    kv_back[...] = jnp.zeros_like(kv_back)
    for copy in turned:
        copy.wait_recv()
    stayed.wait()

    def attend_back(head, carry):
        lanes = pl.ds(pl.multiple_of(head * HD, HD), HD)
        for block in range(line):
            rows = slice(block * span_len, (block + 1) * span_len)
            reach = (block + 1) * span_len
            part, grad = query[rows, lanes], att_grad[rows, lanes]
            row = lax.broadcasted_iota(jnp.int32, (span_len, reach), 0) + block * span_len
            column = lax.broadcasted_iota(jnp.int32, (span_len, reach), 1)
            allowed = (column <= row, column < (block + links.x) * span_len)
            spot = lax.broadcasted_iota(jnp.int32, (span_len, HD), 1) == head
            top = jnp.sum(jnp.where(spot, peak[rows], 0.0), axis=-1, keepdims=True)
            delta = jnp.sum(
                grad.astype(f32) * own_columns[rows, lanes].astype(f32), axis=-1, keepdims=True
            )
            total = None
            for side in range(2):
                keys, values = kv[side, :reach, :HD], kv[side, :reach, HD:]
                score = lax.dot_general(
                    part, keys, (((1,), (1,)), ((), ())), preferred_element_type=f32
                )
                weight = jnp.where(allowed[side], jnp.exp(score * scale - top), 0.0)
                weight_grad = lax.dot_general(
                    grad, values, (((1,), (1,)), ((), ())), preferred_element_type=f32
                )
                score_grad = (weight * (weight_grad - delta)).astype(bf16)
                term = jnp.dot(score_grad, keys, preferred_element_type=f32)
                total = term if total is None else total + term
                kv_back[side, :reach, :HD] += lax.dot_general(
                    score_grad, part, (((0,), (0,)), ((), ())), preferred_element_type=f32
                )
                kv_back[side, :reach, HD:] += lax.dot_general(
                    weight.astype(bf16), grad, (((0,), (0,)), ((), ())), preferred_element_type=f32
                )
            query_back[rows, lanes] = total * scale
        return carry

    lax.fori_loop(0, heads, attend_back, 0)
    kv_out[:, :HD] = (kv_back[1, :, :HD] * scale).astype(bf16)
    kv_out[:, HD:] = kv_back[1, :, HD:].astype(bf16)
    exchange = links.send(kv_out, kv_in, "x")

    def turn_back(values, rows):
        return values * turns[0, rows] - pltpu.roll(values, HD // 2, 1) * turns[1, rows]

    for block in range(line):
        rows = slice(block * span_len, (block + 1) * span_len)
        for head in range(heads):
            lanes = slice(head * HD, (head + 1) * HD)
            flat[rows, lanes] = turn_back(query_back[rows, lanes], rows).astype(bf16)
    first_done(ff_items, 0, line)
    exchange.wait_recv()
    for block in range(line):
        rows = slice(block * span_len, (block + 1) * span_len)
        key_grad = kv_back[0, rows, :HD] * scale + kv_in[rows, :HD].astype(f32)
        flat[rows, q_cols : q_cols + HD] = turn_back(key_grad, rows).astype(bf16)
        value_grad = kv_back[0, rows, HD:] + kv_in[rows, HD:].astype(f32)
        flat[rows, q_cols + HD :] = value_grad.astype(bf16)
    for z in range(line):
        weight = slim[z].reshape(rows_z, flat.shape[1])
        part = lax.dot_general(
            flat[...], weight, (((1,), (1,)), ((), ())), preferred_element_type=f32
        ).astype(bf16)
        for block in range(line):
            parts[block, :, z * rows_z : (z + 1) * rows_z] = part[
                block * span_len : (block + 1) * span_len
            ]
    ring.step(0)
    for z in range(line):
        grad = lax.dot_general(
            norm[:, z * rows_z : (z + 1) * rows_z],
            flat[...],
            (((0,), (0,)), ((), ())),
            preferred_element_type=f32,
        )
        slim[z] = grad.astype(bf16).reshape(2, 2, 2, rows_each, flat.shape[1])
    for item in qkv_items:
        item.start()
    core_done(out_items, 0, half)
    turn(ff_items, ffs_ref, 0, line, ff_order)
    ring.step(1)
    core_done(out_items, half, line)
    first_done(out_items, 0, half)
    ring.step(2)
    core_done(qkv_items, 0, line)
    first_done(out_items, half, line)
    turn(out_items, outs_ref, 0, half)
    ring.step(3)
    first_done(qkv_items, 0, half)
    turn(out_items, outs_ref, half, line)
    first_done(qkv_items, half, line)
    turn(qkv_items, qkvs_ref, 0, line)
    for copy in arrived:
        copy.wait_recv()
    links.finish()
    for copy in local:
        copy.wait()


def backward_call(small, saved, out_w, attended, weights, norm, grad_ff, ff_half, line):
    f32, bf16 = jnp.float32, jnp.bfloat16
    span_len, width = small[0].shape
    group_len = line * span_len
    query = saved[0]
    q_cols, rows_each, qkv_cols = query.shape[1], width // line // 8, weights.shape[3]
    weights = weights.reshape(line, 2, 2, 2, -1, qkv_cols)
    wide = (line, 2, 2, 2, rows_each, width)
    slim = (line, 2, 2, 2, rows_each, qkv_cols)
    out_space = sum_space(line, rows_each, width)[1:]
    qkv_space = sum_space(line, rows_each, qkv_cols)[1:]
    token = jax.ShapeDtypeStruct((span_len, width), f32)
    return link_call(
        functools.partial(backward_kernel, line),
        4,
        160,
        (token, token)
        + tuple(
            jax.ShapeDtypeStruct((line, rows_each, columns), bf16)
            for columns in (grad_ff.shape[5], width, qkv_cols)
        ),
        small + saved + (out_w.reshape(wide), attended, weights, norm, grad_ff, ff_half),
        "v" * 5 + "h" * 10 + "vvhhh",
        [
            pltpu.VMEM(wide, bf16),
            pltpu.VMEM(slim, bf16),
            pltpu.VMEM((group_len, width), bf16),
            pltpu.VMEM((span_len, width), bf16),
            pltpu.VMEM((group_len, q_cols), bf16),
            pltpu.VMEM((span_len, width), bf16),
            pltpu.VMEM((span_len, width), bf16),
            pltpu.VMEM((group_len, q_cols), bf16),
            pltpu.VMEM((group_len, q_cols), f32),
            pltpu.VMEM((2, group_len, 2 * HD), f32),
            pltpu.VMEM((group_len, 2 * HD), bf16),
            pltpu.VMEM((group_len, 2 * HD), bf16),
            pltpu.VMEM((group_len, qkv_cols), bf16),
            pltpu.VMEM((line, span_len, width), bf16),
        ]
        + [pltpu.VMEM(value.shape, value.dtype) for value in saved]
        + [pltpu.VMEM((line - 1, span_len, width), bf16)]
        + sum_space(line - 2, rows_each, grad_ff.shape[5])
        + out_space
        + qkv_space,
        vmem=63,
    )


def general_body(
    tokens,
    attn_gain,
    w_query,
    w_key,
    w_value,
    w_out,
    mlp_gain,
    w_gate,
    w_up,
    w_down,
    keep_mask,
    group_ids,
    positions,
    exit_scale,
    out_grad,
):
    seq_count, span_len, model_width = tokens.shape
    kv_heads = KVH
    head_dim = HD
    head_count = HEADS
    group_size = head_count // kv_heads
    row_count = seq_count * span_len
    stripe = group_size * span_len
    wide_count = lax.axis_size("wide")
    wide_place = lax.axis_index("wide")
    full_len = span_len * wide_count
    score_scale = 1.0 / math.sqrt(head_dim)
    gain_one, query_w, key_w, value_w, out_w = (
        lax.all_gather(attn_gain, ("wide", "narrow"), axis=0, tiled=True),
        lax.all_gather(w_query, ("wide", "narrow"), axis=0, tiled=True),
        lax.all_gather(w_key, ("wide", "narrow"), axis=0, tiled=True),
        lax.all_gather(w_value, ("wide", "narrow"), axis=0, tiled=True),
        lax.all_gather(w_out, ("wide", "narrow"), axis=0, tiled=True),
    )
    inputs = tokens.astype(jnp.float32).reshape(row_count, model_width)
    token_pos = positions.reshape(row_count)
    keep_rows = jnp.repeat(keep_mask.astype(jnp.float32), span_len)[:, None]
    inverse_one = lax.rsqrt(jnp.mean(inputs * inputs, axis=-1, keepdims=True) + epsilon)
    first_norm = (inputs * inverse_one * gain_one.astype(jnp.float32)).astype(jnp.bfloat16)
    query_pre = jnp.dot(first_norm, query_w, preferred_element_type=jnp.float32).reshape(
        row_count, head_count, head_dim
    )
    key_pre = jnp.dot(first_norm, key_w, preferred_element_type=jnp.float32).reshape(
        row_count, kv_heads, head_dim
    )
    query_rows = rotate(query_pre, token_pos, 1.0).astype(jnp.bfloat16)
    key_heads = (
        rotate(key_pre, token_pos, 1.0)
        .astype(jnp.bfloat16)
        .reshape(seq_count, span_len, kv_heads * head_dim)
    )
    value_heads = (
        jnp.dot(first_norm, value_w, preferred_element_type=jnp.float32)
        .astype(jnp.bfloat16)
        .reshape(seq_count, span_len, kv_heads * head_dim)
    )
    queries = (
        query_rows.reshape(seq_count, span_len, kv_heads, group_size, head_dim)
        .transpose(0, 2, 3, 1, 4)
        .reshape(seq_count, kv_heads, stripe, head_dim)
    )
    query_index = wide_place * span_len + jnp.arange(stripe, dtype=jnp.int32) % span_len
    last_query = wide_place * span_len + span_len - 1

    def block_scores(key_block, key_first):
        scores = (
            jnp.einsum("skrd,sjkd->skrj", queries, key_block, preferred_element_type=jnp.float32)
            * score_scale
        )
        key_index = key_first + jnp.arange(key_block.shape[1], dtype=jnp.int32)
        allowed = key_index[None, :] <= query_index[:, None]
        return (scores, allowed)

    start_forward = (
        jnp.full((seq_count, kv_heads, stripe), -1e30, jnp.float32),
        jnp.zeros((seq_count, kv_heads, stripe), jnp.float32),
        jnp.zeros((seq_count, kv_heads, stripe, head_dim), jnp.float32),
    )
    running = start_forward
    pieces = (
        lax.all_gather(key_heads, "wide", axis=1, tiled=True),
        lax.all_gather(value_heads, "wide", axis=1, tiled=True),
    )
    key_blocks = split_blocks(pieces[0], seq_count, kv_heads, head_dim)
    value_blocks = split_blocks(pieces[1], seq_count, kv_heads, head_dim)
    block_len = key_blocks.shape[2]

    def advance(carried, block_item):
        key_block, value_block, block_index = block_item
        key_first = block_index * block_len

        def compute_block(current):
            run_max, run_sum, run_acc = current
            scores, allowed = block_scores(key_block, key_first)
            scores = jnp.where(allowed, scores, -1e30)
            new_max = jnp.maximum(run_max, jnp.max(scores, axis=-1))
            factor = jnp.exp(run_max - new_max)
            weights = jnp.where(allowed, jnp.exp(scores - new_max[..., None]), 0.0)
            new_sum = run_sum * factor + jnp.sum(weights, axis=-1)
            new_acc = run_acc * factor[..., None] + jnp.einsum(
                "skrj,sjkd->skrd",
                weights.astype(jnp.bfloat16),
                value_block,
                preferred_element_type=jnp.float32,
            )
            return (new_max, new_sum, new_acc)

        return (lax.cond(key_first <= last_query, compute_block, unchanged, carried), None)

    running, _ = lax.scan(
        advance,
        running,
        (key_blocks, value_blocks, jnp.arange(key_blocks.shape[0], dtype=jnp.int32)),
    )
    run_max, run_sum, run_acc = running
    attended = run_acc / run_sum[..., None]
    log_total = run_max + jnp.log(run_sum)
    attended_rows = (
        attended.reshape(seq_count, kv_heads, group_size, span_len, head_dim)
        .transpose(0, 3, 1, 2, 4)
        .reshape(row_count, head_count * head_dim)
        .astype(jnp.bfloat16)
    )
    middle = inputs + keep_rows * jnp.dot(attended_rows, out_w, preferred_element_type=jnp.float32)
    gain_two, gate_w, up_w, down_w = (
        lax.all_gather(mlp_gain, ("wide", "narrow"), axis=0, tiled=True),
        lax.all_gather(w_gate, ("wide", "narrow"), axis=0, tiled=True),
        lax.all_gather(w_up, ("wide", "narrow"), axis=0, tiled=True),
        lax.all_gather(w_down, ("wide", "narrow"), axis=0, tiled=True),
    )
    inverse_two = lax.rsqrt(jnp.mean(middle * middle, axis=-1, keepdims=True) + epsilon)
    second_norm = (middle * inverse_two * gain_two.astype(jnp.float32)).astype(jnp.bfloat16)
    gate_value = jnp.dot(second_norm, gate_w, preferred_element_type=jnp.float32)
    up_value = jnp.dot(second_norm, up_w, preferred_element_type=jnp.float32)
    gate_sigmoid = jax.nn.sigmoid(gate_value)
    swish_value = gate_value * gate_sigmoid
    hidden = (swish_value * up_value).astype(jnp.bfloat16)
    output = (
        middle + keep_rows * jnp.dot(hidden, down_w, preferred_element_type=jnp.float32)
    ).astype(jnp.bfloat16)
    group_match = (
        group_ids.reshape(row_count)[:, None]
        == jnp.arange(exit_scale.shape[0], dtype=jnp.int32)[None, :]
    )
    token_scale = jnp.sum(jnp.where(group_match, exit_scale[None, :], 0.0), axis=1, keepdims=True)
    upstream = out_grad.astype(jnp.float32).reshape(row_count, model_width) * token_scale
    gain_two, gate_w, up_w, down_w = (
        lax.all_gather(mlp_gain, ("wide", "narrow"), axis=0, tiled=True),
        lax.all_gather(w_gate, ("wide", "narrow"), axis=0, tiled=True),
        lax.all_gather(w_up, ("wide", "narrow"), axis=0, tiled=True),
        lax.all_gather(w_down, ("wide", "narrow"), axis=0, tiled=True),
    )
    mixed_grad = (keep_rows * upstream).astype(jnp.bfloat16)
    grad_down = over_rows(hidden, mixed_grad)
    hidden_grad = against(mixed_grad, down_w)
    gate_grad = (
        hidden_grad * up_value * gate_sigmoid * (1.0 + gate_value * (1.0 - gate_sigmoid))
    ).astype(jnp.bfloat16)
    up_grad = (hidden_grad * swish_value).astype(jnp.bfloat16)
    grad_gate = over_rows(second_norm, gate_grad)
    grad_up = over_rows(second_norm, up_grad)
    norm_grad = against(gate_grad, gate_w) + against(up_grad, up_w)
    grad_gain_two = jnp.sum(norm_grad * middle * inverse_two, axis=0)
    scaled_two = gain_two.astype(jnp.float32) * norm_grad
    middle_grad = (
        upstream
        + inverse_two * scaled_two
        - middle
        * (inverse_two * inverse_two * inverse_two)
        * jnp.mean(scaled_two * middle, axis=-1, keepdims=True)
    )
    gain_two_share, gate_share, up_share, down_share = (
        lax.psum_scatter(grad_gain_two, ("wide", "narrow"), scatter_dimension=0, tiled=True),
        lax.psum_scatter(grad_gate, ("wide", "narrow"), scatter_dimension=0, tiled=True),
        lax.psum_scatter(grad_up, ("wide", "narrow"), scatter_dimension=0, tiled=True),
        lax.psum_scatter(grad_down, ("wide", "narrow"), scatter_dimension=0, tiled=True),
    )
    gain_one, query_w, key_w, value_w, out_w = (
        lax.all_gather(attn_gain, ("wide", "narrow"), axis=0, tiled=True),
        lax.all_gather(w_query, ("wide", "narrow"), axis=0, tiled=True),
        lax.all_gather(w_key, ("wide", "narrow"), axis=0, tiled=True),
        lax.all_gather(w_value, ("wide", "narrow"), axis=0, tiled=True),
        lax.all_gather(w_out, ("wide", "narrow"), axis=0, tiled=True),
    )
    branch_grad = (keep_rows * middle_grad).astype(jnp.bfloat16)
    grad_out = over_rows(attended_rows, branch_grad)
    attended_grad = against(branch_grad, out_w).astype(jnp.bfloat16)
    grouped_grad = (
        attended_grad.reshape(seq_count, span_len, kv_heads, group_size, head_dim)
        .transpose(0, 2, 3, 1, 4)
        .reshape(seq_count, kv_heads, stripe, head_dim)
    )
    row_delta = jnp.sum(grouped_grad.astype(jnp.float32) * attended, axis=-1)
    start_backward = (
        jnp.zeros((seq_count, kv_heads, stripe, head_dim), jnp.float32),
        jnp.zeros((seq_count, full_len, kv_heads * head_dim), jnp.float32),
        jnp.zeros((seq_count, full_len, kv_heads * head_dim), jnp.float32),
    )
    running = start_backward
    pieces = (
        lax.all_gather(key_heads, "wide", axis=1, tiled=True),
        lax.all_gather(value_heads, "wide", axis=1, tiled=True),
    )
    key_blocks = split_blocks(pieces[0], seq_count, kv_heads, head_dim)
    value_blocks = split_blocks(pieces[1], seq_count, kv_heads, head_dim)
    fold_block_len = key_blocks.shape[2]

    def advance(carried, block_item):
        key_block, value_block, block_index = block_item
        key_first = block_index * fold_block_len

        def compute_block(current):
            query_acc, key_acc, value_acc = current
            scores, allowed = block_scores(key_block, key_first)
            probabilities = jnp.where(allowed, jnp.exp(scores - log_total[..., None]), 0.0)
            value_part = jnp.einsum(
                "skrj,skrd->sjkd",
                probabilities.astype(jnp.bfloat16),
                grouped_grad,
                preferred_element_type=jnp.float32,
            )
            prob_grad = jnp.einsum(
                "skrd,sjkd->skrj", grouped_grad, value_block, preferred_element_type=jnp.float32
            )
            score_grad = (probabilities * (prob_grad - row_delta[..., None])).astype(jnp.bfloat16)
            query_acc = (
                query_acc
                + jnp.einsum(
                    "skrj,sjkd->skrd", score_grad, key_block, preferred_element_type=jnp.float32
                )
                * score_scale
            )
            key_part = (
                jnp.einsum(
                    "skrj,skrd->sjkd", score_grad, queries, preferred_element_type=jnp.float32
                )
                * score_scale
            )
            key_acc = add_rows(
                key_acc, key_part.reshape(seq_count, fold_block_len, kv_heads * head_dim), key_first
            )
            value_acc = add_rows(
                value_acc,
                value_part.reshape(seq_count, fold_block_len, kv_heads * head_dim),
                key_first,
            )
            return (query_acc, key_acc, value_acc)

        return (lax.cond(key_first <= last_query, compute_block, unchanged, carried), None)

    running, _ = lax.scan(
        advance,
        running,
        (key_blocks, value_blocks, jnp.arange(key_blocks.shape[0], dtype=jnp.int32)),
    )
    query_acc, key_acc, value_acc = running
    key_sum, value_sum = (
        lax.psum_scatter(
            key_acc.astype(jnp.bfloat16), "wide", scatter_dimension=1, tiled=True
        ).astype(jnp.float32),
        lax.psum_scatter(
            value_acc.astype(jnp.bfloat16), "wide", scatter_dimension=1, tiled=True
        ).astype(jnp.float32),
    )
    query_back = (
        query_acc.reshape(seq_count, kv_heads, group_size, span_len, head_dim)
        .transpose(0, 3, 1, 2, 4)
        .reshape(row_count, head_count, head_dim)
    )
    query_grad = (
        rotate(query_back, token_pos, -1.0)
        .reshape(row_count, head_count * head_dim)
        .astype(jnp.bfloat16)
    )
    key_grad = (
        rotate(key_sum.reshape(row_count, kv_heads, head_dim), token_pos, -1.0)
        .reshape(row_count, kv_heads * head_dim)
        .astype(jnp.bfloat16)
    )
    value_grad = value_sum.reshape(row_count, kv_heads * head_dim).astype(jnp.bfloat16)
    grad_query = over_rows(first_norm, query_grad)
    grad_key = over_rows(first_norm, key_grad)
    grad_value = over_rows(first_norm, value_grad)
    input_norm_grad = (
        against(query_grad, query_w) + against(key_grad, key_w) + against(value_grad, value_w)
    )
    grad_gain_one = jnp.sum(input_norm_grad * inputs * inverse_one, axis=0)
    scaled_one = gain_one.astype(jnp.float32) * input_norm_grad
    input_grad = (
        middle_grad
        + inverse_one * scaled_one
        - inputs
        * (inverse_one * inverse_one * inverse_one)
        * jnp.mean(scaled_one * inputs, axis=-1, keepdims=True)
    )
    gain_one_share, query_share, key_share, value_share, out_share = (
        lax.psum_scatter(grad_gain_one, ("wide", "narrow"), scatter_dimension=0, tiled=True),
        lax.psum_scatter(grad_query, ("wide", "narrow"), scatter_dimension=0, tiled=True),
        lax.psum_scatter(grad_key, ("wide", "narrow"), scatter_dimension=0, tiled=True),
        lax.psum_scatter(grad_value, ("wide", "narrow"), scatter_dimension=0, tiled=True),
        lax.psum_scatter(grad_out, ("wide", "narrow"), scatter_dimension=0, tiled=True),
    )
    return (
        output.reshape(seq_count, span_len, model_width),
        input_grad.astype(jnp.bfloat16).reshape(seq_count, span_len, model_width),
        gain_one_share,
        query_share,
        key_share,
        value_share,
        out_share,
        gain_two_share,
        gate_share,
        up_share,
        down_share,
    )


def line_body(
    tokens,
    attn_gain,
    w_query,
    w_key,
    w_value,
    w_out,
    mlp_gain,
    w_gate,
    w_up,
    w_down,
    keep_mask,
    group_ids,
    positions,
    exit_scale,
    out_grad,
):
    f32 = jnp.float32
    bf16 = jnp.bfloat16
    _, span_len, model_width = tokens.shape
    line = lax.axis_size("z")
    rows_each = w_query.shape[0]
    q_cols = HEADS // line * HD
    ff_cols = w_gate.shape[1] // line
    group_len = span_len * line

    def by_columns(weight, columns):
        return weight.reshape(rows_each, line, columns).transpose(1, 0, 2)

    down_w = lax.all_gather(w_down, ("x", "y", "c"), axis=0, tiled=True)
    own_x = tokens[0].astype(f32)
    keep = keep_mask[0].astype(f32)
    group_match = group_ids[0][:, None] == jnp.arange(exit_scale.shape[0], dtype=jnp.int32)[None, :]
    token_scale = jnp.sum(jnp.where(group_match, exit_scale[None, :], 0.0), axis=1, keepdims=True)
    upstream = out_grad[0].astype(f32) * token_scale

    core = lax.axis_index("c")
    gain_row = jnp.zeros((q_cols + 2 * HD,), bf16)
    gain_row = lax.dynamic_update_slice_in_dim(gain_row, attn_gain, core * rows_each, 0)
    gain_row = lax.dynamic_update_slice_in_dim(gain_row, mlp_gain, HD + core * rows_each, 0)
    gain_rows = jnp.broadcast_to(gain_row, (line, 16, gain_row.shape[0]))
    pack_attn = jnp.concatenate(
        [by_columns(w_query, q_cols), by_columns(w_key, HD), by_columns(w_value, HD)], axis=2
    )
    pack_attn = jnp.concatenate([pack_attn, gain_rows], axis=1)
    pack_ff = jnp.concatenate([by_columns(w_gate, ff_cols), by_columns(w_up, ff_cols)], axis=2)
    freqs = 10000.0 ** (-2.0 * jnp.arange(HD // 2, dtype=f32) / HD)
    freqs = jnp.broadcast_to(jnp.concatenate([freqs, freqs])[None], (8, HD))
    places = jnp.broadcast_to(positions[0].astype(f32)[None], (8, span_len))
    own_mixed = (keep * upstream).astype(bf16)
    first_tokens, own_mixed, upstream = lax.optimization_barrier((tokens[0], own_mixed, upstream))
    (
        x_blocks,
        near_w,
        gain_all,
        first_norm,
        queries,
        both_kv,
        log_total,
        turns,
        attended_rows,
        ff_w,
        out_w,
    ) = forward_call(freqs, first_tokens, places, pack_attn, pack_ff, w_out, line)
    keep_tile = jnp.broadcast_to(keep, (8, HD))
    middle, norm_grad, mixed, grad_down, grad_ff, ff_half = mlp_call(
        keep_tile,
        gain_all,
        own_mixed,
        x_blocks,
        attended_rows,
        out_w,
        ff_w,
        down_w,
        line,
    )
    grad_down = grad_down.astype(f32)
    output = (middle + keep * mixed).astype(bf16)
    middle_grad, input_norm_grad, ff_back, out_back, qkv_back = backward_call(
        (
            upstream,
            middle,
            norm_grad,
            keep_tile,
            gain_all,
        ),
        (queries, both_kv, log_total, turns),
        out_w,
        attended_rows,
        near_w,
        first_norm,
        grad_ff,
        ff_half,
        line,
    )
    ff_back = ff_back.astype(f32)
    qkv_back = qkv_back.astype(f32)
    grad_out = jnp.sum(out_back.astype(f32), axis=0)
    gain_one = gain_all[0, :1]
    inverse_one = lax.rsqrt(jnp.mean(own_x * own_x, axis=-1, keepdims=True) + epsilon)
    scaled_one = gain_one * input_norm_grad
    input_grad = (
        middle_grad
        + inverse_one * scaled_one
        - own_x
        * (inverse_one * inverse_one * inverse_one)
        * jnp.mean(scaled_one * own_x, axis=-1, keepdims=True)
    )

    def side_by_side(blocks):
        return blocks.transpose(1, 0, 2).reshape(rows_each, -1)

    grad_query = side_by_side(qkv_back[:, :, :q_cols])
    grad_key = side_by_side(qkv_back[:, :, q_cols : q_cols + HD])
    grad_value = side_by_side(qkv_back[:, :, q_cols + HD :])
    grad_gate = side_by_side(ff_back[:, :, :ff_cols])
    grad_up = side_by_side(ff_back[:, :, ff_cols:])

    def gain_grad(pairs, gain):
        total = sum(jnp.sum(weight.astype(f32) * grad, axis=1) for weight, grad in pairs)
        return total / gain.astype(f32)

    return (
        output[None],
        input_grad.astype(bf16)[None],
        gain_grad([(w_query, grad_query), (w_key, grad_key), (w_value, grad_value)], attn_gain),
        grad_query,
        grad_key,
        grad_value,
        grad_out,
        gain_grad([(w_gate, grad_gate), (w_up, grad_up)], mlp_gain),
        grad_gate,
        grad_up,
        grad_down,
    )


def solution(mesh):
    wide, narrow = mesh.shape["wide"], mesh.shape["narrow"]
    if wide == 2 * KVH and narrow == 4:
        mesh = Mesh(mesh.devices.reshape(wide // 2, 2, 2, 2), ("z", "x", "y", "c"))
        body, wide, narrow = line_body, ("z", "x"), ("y", "c")
    else:
        body, wide, narrow = general_body, ("wide",), ("narrow",)
    token_spec = P(narrow, wide, None)
    id_spec = P(narrow, wide)
    gain_spec = P(wide + narrow)
    weight_spec = P(wide + narrow, None)
    return jax.shard_map(
        body,
        mesh=mesh,
        in_specs=(
            token_spec,
            gain_spec,
            weight_spec,
            weight_spec,
            weight_spec,
            weight_spec,
            gain_spec,
            weight_spec,
            weight_spec,
            weight_spec,
            P(narrow),
            id_spec,
            id_spec,
            P(),
            token_spec,
        ),
        out_specs=(
            token_spec,
            token_spec,
            gain_spec,
            weight_spec,
            weight_spec,
            weight_spec,
            weight_spec,
            gain_spec,
            weight_spec,
            weight_spec,
            weight_spec,
        ),
        check_vma=False,
    )
```

```python
import functools
import math

import jax
import jax.numpy as jnp
from jax import lax
from jax.experimental import pallas as pl
from jax.experimental.pallas import tpu as pltpu
from jax.sharding import Mesh
from jax.sharding import PartitionSpec as P

HEADS = 16
KVH = 4
HD = 128


epsilon = 1e-05


def rotate(vectors, token_pos, direction):
    half_size = vectors.shape[-1] // 2
    freqs = 10000.0 ** (-2.0 * jnp.arange(half_size, dtype=jnp.float32) / vectors.shape[-1])
    angles = token_pos.astype(jnp.float32)[:, None] * freqs[None, :]
    cosine = jnp.cos(angles)[:, None, :]
    sine = direction * jnp.sin(angles)[:, None, :]
    first_half = vectors[..., :half_size]
    second_half = vectors[..., half_size:]
    return jnp.concatenate(
        [first_half * cosine - second_half * sine, second_half * cosine + first_half * sine],
        axis=-1,
    )


def split_blocks(piece_arr, seq_count, kv_heads, head_dim):
    piece_len = piece_arr.shape[1]
    block_len = math.gcd(piece_len, 512)
    shaped = piece_arr.reshape(seq_count, piece_len // block_len, block_len, kv_heads, head_dim)
    return shaped.transpose(1, 0, 2, 3, 4)


def add_rows(whole_arr, update, first_row):
    current = lax.dynamic_slice_in_dim(whole_arr, first_row, update.shape[1], 1)
    return lax.dynamic_update_slice_in_dim(whole_arr, current + update, first_row, 1)


def over_rows(left, right):
    return lax.dot_general(
        left, right, (((0,), (0,)), ((), ())), preferred_element_type=jnp.float32
    )


def against(left, right):
    return lax.dot_general(
        left, right, (((1,), (1,)), ((), ())), preferred_element_type=jnp.float32
    )


def unchanged(carried):
    return carried


MESH = pl.DeviceIdType.MESH
AXES = ("z", "x", "y", "c")


class Links:
    def __init__(self, send_sems, recv_sems, line):
        self.send_sems, self.recv_sems, self.line = send_sems, recv_sems, line
        self.z, self.x, self.y, self.c = (lax.axis_index(name) for name in AXES)
        self.slot = self.x * 4 + self.y * 2 + self.c
        self.used = 0
        self.sent = []

    def device(self, to):
        if to == "x":
            return (self.z, 1 - self.x, self.y, self.c)
        if to == "y":
            return (self.z, self.x, 1 - self.y, self.c)
        if to == "c":
            return (self.z, self.x, self.y, 1 - self.c)
        return (self.along(to), self.x, self.y, self.c)

    def along(self, step):
        return lax.rem(self.z + step + self.line, self.line)

    def other(self, to):
        slot = self.slot
        for name in to:
            bit = {"x": 4, "y": 2, "c": 1}[name]
            here = {"x": self.x, "y": self.y, "c": self.c}[name]
            slot = slot + bit * (1 - 2 * here)
        return slot

    def meet(self, targets):
        barrier = pltpu.get_barrier_semaphore()
        for to in targets:
            pl.semaphore_signal(barrier, inc=1, device_id=self.device(to), device_id_type=MESH)
        pl.semaphore_wait(barrier, len(targets))

    def send(self, source, target, to):
        copy = pltpu.make_async_remote_copy(
            src_ref=source,
            dst_ref=target,
            send_sem=self.send_sems.at[self.used],
            recv_sem=self.recv_sems.at[self.used],
            device_id=self.device(to),
            device_id_type=MESH,
        )
        copy.start()
        self.used += 1
        self.sent.append(copy)
        return copy

    def keep(self, source, target):
        copy = pltpu.make_async_copy(source, target, self.send_sems.at[self.used])
        copy.start()
        self.used += 1
        return copy

    def finish(self):
        for copy in self.sent:
            copy.wait_send()


class NearGather:
    def __init__(self, links, slot):
        self.links, self.slot = links, slot
        self.got = {}

    def offer(self, block, source):
        target = self.slot(block, self.links.slot)
        for to in ("x", "y", "c"):
            self.got[block, to] = self.links.send(source, target, to)

    def relay(self, block, first):
        links = self.links
        for to, then in (("x", "y"), ("y", "x")):
            self.got[block, to].wait_recv()
            place = self.slot(block, links.other(to))
            self.got[block, to + "c"] = links.send(place, place, "c")
            if to == first:
                self.got[block, "xy"] = links.send(place, place, then)

    def close(self, block):
        self.got[block, "xy"].wait_recv()
        place = self.slot(block, self.links.other("xy"))
        self.got[block, "xyc"] = self.links.send(place, place, "c")

    def wait(self, blocks):
        for block in blocks:
            for to in ("c", "xc", "yc", "xyc"):
                self.got[block, to].wait_recv()


class RingGather:
    def __init__(self, links, source, place, pieces=4):
        self.links, self.source, self.place, self.pieces = links, source, place, pieces
        self.rows = source.shape[0] // pieces
        self.last = [None] * pieces

    def step(self, number):
        for piece in range(self.pieces):
            way = 1 if piece < self.pieces // 2 else -1
            rows = pl.ds(piece * self.rows, self.rows)
            place = self.place(self.links.along(-way * number), rows)
            if number > 0:
                self.last[piece].wait_recv()
            if number < self.links.line - 1:
                origin = self.source.at[rows] if number == 0 else place
                self.last[piece] = self.links.send(origin, place, way)


def first_kernel(
    line,
    freq_ref,
    x_ref,
    place_ref,
    pack_ref,
    ff_ref,
    out_ref,
    xs_ref,
    weight_ref,
    gain_ref,
    norm_ref,
    query_ref,
    kv_ref,
    peak_ref,
    turn_ref,
    atts_ref,
    ffs_ref,
    outs_ref,
    x_all,
    places,
    weights,
    gains,
    norm,
    turns,
    flat,
    query,
    kv,
    peak,
    att,
    send_sems,
    recv_sems,
):
    f32, bf16 = jnp.float32, jnp.bfloat16
    links = Links(send_sems, recv_sems, line)
    far = [1, line - 1] + list(range(2, line - 1))
    links.meet(["x", "y", "c"] + far)
    here = links.slot
    span_len, width = x_ref.shape
    group_len = line * span_len
    rows_each = ff_ref.shape[1]
    q_cols = query.shape[1]
    heads = q_cols // HD
    local = []

    near = NearGather(links, lambda block, place: weights.at[links.along(-block), place])
    far_ff = NearGather(links, lambda block, place: ffs_ref.at[links.along(-block), place])
    far_out = NearGather(links, lambda block, place: outs_ref.at[links.along(-block), place])
    ring = RingGather(links, x_ref, lambda block, rows: x_all.at[block, rows])
    own = [
        links.keep(x_ref, x_all.at[links.z]),
        links.keep(place_ref, places.at[links.z]),
        links.keep(pack_ref.at[links.z], weights.at[links.z, here]),
    ]
    turned = {k: links.send(pack_ref.at[links.along(k)], weights.at[links.z, here], k) for k in far}
    placed = [links.send(place_ref, places.at[links.z], k) for k in far]
    turned_ff = {k: links.send(ff_ref.at[links.along(k)], ffs_ref.at[links.z, here], k) for k in far}
    near.offer(0, pack_ref.at[links.z])
    far_ff.offer(0, ff_ref.at[links.z])
    local.append(links.keep(ff_ref.at[links.z], ffs_ref.at[links.z, here]))
    local.append(links.keep(out_ref, outs_ref.at[links.z, here]))

    def move_out(k):
        moved.wait_recv()
        block = outs_ref.at[links.along(-k), here]
        onward = links.send(block, block, 1) if k < line - 1 else None
        far_out.offer(k, block)
        return onward

    for k in far:
        turned[k].wait_recv()
        near.offer(k, weights.at[links.along(-k), here])
    ring.step(0)
    for k in [0] + far:
        near.relay(k, "x" if k < line // 2 else "y")
    for k in far:
        turned_ff[k].wait_recv()
        far_ff.offer(k, ffs_ref.at[links.along(-k), here])
    ring.step(1)
    for k in [0] + far:
        near.close(k)
    far_ff.relay(0, "x")
    ring.step(2)
    moved = links.send(out_ref, outs_ref.at[links.z, here], 1)
    far_out.offer(0, out_ref)
    for copy in own:
        copy.wait()
    for copy in placed:
        copy.wait_recv()

    lane = lax.broadcasted_iota(jnp.int32, (span_len, HD), 1)
    token = lax.broadcasted_iota(jnp.int32, (span_len, span_len), 0)
    across = lax.broadcasted_iota(jnp.int32, (span_len, span_len), 1)
    for block in range(line):
        row = jnp.broadcast_to(places[block, 0:1], (span_len, span_len))
        column = jnp.sum(jnp.where(token == across, row, 0.0), axis=1, keepdims=True)
        angles = column * freq_ref[0:1]
        rows = slice(block * span_len, (block + 1) * span_len)
        sine = jnp.sin(angles)
        turns[0, rows] = jnp.cos(angles)
        turns[1, rows] = jnp.where(lane < HD // 2, -sine, sine)
    local.append(links.keep(turns, turn_ref))
    near.wait(range(line))
    for index in range(line * 4):
        z, q = divmod(index, 4)
        for which in range(2):
            lanes = slice(which * HD, (which + 1) * HD)
            both = [weights[z, 2 * q + c, rows_each : rows_each + 16, lanes].astype(f32) for c in range(2)]
            gains[which, :, index * HD : (index + 1) * HD] = both[0] + both[1]
    local.append(links.keep(weights, weight_ref))
    local.append(links.keep(gains, gain_ref))
    far_ff.relay(far[0], "x")
    ring.step(3)
    local.append(links.keep(x_all, xs_ref))

    def normalise(index, carry):
        block = index // (span_len // 16)
        rows = pl.ds(pl.multiple_of(lax.rem(index, span_len // 16) * 16, 16), 16)
        values = x_all[block, rows].astype(f32)
        inverse = lax.rsqrt(jnp.mean(values * values, axis=-1, keepdims=True) + epsilon)
        target = pl.ds(pl.multiple_of(index * 16, 16), 16)
        norm[target] = (values * inverse * gains[0]).astype(bf16)
        return carry

    lax.fori_loop(0, group_len // 16, normalise, 0)
    local.append(links.keep(norm, norm_ref))

    def project(low, high):
        step = group_len // 2
        for part in range(2):
            rows = slice(part * step, (part + 1) * step)
            total = None
            for z in range(line):
                weight = weights[z, :, :rows_each, low:high].reshape(8 * rows_each, high - low)
                term = jnp.dot(
                    norm[rows, z * 8 * rows_each : (z + 1) * 8 * rows_each],
                    weight,
                    preferred_element_type=f32,
                )
                total = term if total is None else total + term
            flat[rows, low:high] = total

    def turn(values, rows):
        return values * turns[0, rows] + pltpu.roll(values, HD // 2, 1) * turns[1, rows]

    project(q_cols, q_cols + 2 * HD)
    for block in range(line):
        rows = slice(block * span_len, (block + 1) * span_len)
        kv[0, rows, :HD] = turn(flat[rows, q_cols : q_cols + HD], rows).astype(bf16)
        kv[0, rows, HD:] = flat[rows, q_cols + HD : q_cols + 2 * HD].astype(bf16)
    exchange = links.send(kv.at[0], kv.at[1], "x")
    project(0, q_cols)
    for block in range(line):
        rows = slice(block * span_len, (block + 1) * span_len)
        for head in range(heads):
            lanes = slice(head * HD, (head + 1) * HD)
            query[rows, lanes] = turn(flat[rows, lanes], rows).astype(bf16)
    local.append(links.keep(query, query_ref))
    for k in far[1:]:
        far_ff.relay(k, "x" if k < line // 2 else "y")
    exchange.wait_recv()
    moved = move_out(1)
    local.append(links.keep(kv, kv_ref))

    scale = 1.0 / math.sqrt(HD)
    peak[...] = jnp.zeros_like(peak)

    def attend(head, carry):
        lanes = pl.ds(pl.multiple_of(head * HD, HD), HD)
        for block in range(line):
            rows = slice(block * span_len, (block + 1) * span_len)
            reach = (block + 1) * span_len
            part = query[rows, lanes]
            row = lax.broadcasted_iota(jnp.int32, (span_len, reach), 0) + block * span_len
            column = lax.broadcasted_iota(jnp.int32, (span_len, reach), 1)
            allowed = (column <= row, column < (block + links.x) * span_len)
            scores = []
            for half in range(2):
                score = lax.dot_general(
                    part, kv[half, :reach, :HD], (((1,), (1,)), ((), ())), preferred_element_type=f32
                )
                scores.append(jnp.where(allowed[half], score * scale, -1e30))
            top = jnp.maximum(
                jnp.max(scores[0], axis=-1, keepdims=True), jnp.max(scores[1], axis=-1, keepdims=True)
            )
            total, mixed = None, None
            for half in range(2):
                weight = jnp.exp(scores[half] - top)
                count = jnp.sum(weight, axis=-1, keepdims=True)
                term = jnp.dot(weight.astype(bf16), kv[half, :reach, HD:], preferred_element_type=f32)
                total = count if total is None else total + count
                mixed = term if mixed is None else mixed + term
            att[rows, lanes] = (mixed / total).astype(bf16)
            spot = lax.broadcasted_iota(jnp.int32, (span_len, HD), 1) == head
            peak[rows] = jnp.where(spot, top + jnp.log(total), peak[rows])
        return carry

    lax.fori_loop(0, heads, attend, 0)
    local.append(links.keep(peak, peak_ref))

    def place(block, rows):
        return atts_ref.at[rows, pl.ds(pl.multiple_of(block * q_cols, q_cols), q_cols)]

    att_ring = RingGather(links, att, place)
    local.append(links.keep(att, place(links.z, pl.ds(0, group_len))))
    att_ring.step(0)
    for k in [0] + far:
        far_ff.close(k)
    far_out.relay(0, "x")
    moved = move_out(2)
    far_out.relay(1, "x")
    att_ring.step(1)
    for k in range(3, line):
        moved = move_out(k)
    far_out.relay(2, "y")
    att_ring.step(2)
    for k in range(3, line):
        far_out.relay(k, "y")
    for k in range(line):
        far_out.close(k)
    att_ring.step(3)
    far_out.wait(range(line))
    far_ff.wait(range(line))
    links.finish()
    for copy in local:
        copy.wait()


def add_rows_of(target, values, count):
    def add(index, carry):
        rows = pl.ds(pl.multiple_of(index * 16, 16), 16)
        target[rows] = target[rows] + values[rows]
        return carry

    lax.fori_loop(0, count // 16, add, 0)


class NearSum:
    def __init__(self, links, source, own, from_core, from_first, from_second, first, in_place=False):
        self.links, self.source, self.own, self.first = links, source, own, first
        self.in_place = in_place
        self.from_core, self.from_first, self.from_second = from_core, from_first, from_second

    def start(self):
        links = self.links
        if not self.in_place:
            self.local = links.keep(self.source(links.c), self.own)
        self.copy = links.send(self.source(1 - links.c), self.from_core, "c")

    def add(self, target, values):
        add_rows_of(target, values, target.shape[0])

    def core_done(self):
        links = self.links
        self.copy.wait_recv()
        if not self.in_place:
            self.local.wait()
        for x in range(2):
            for y in range(2):
                self.add(self.own.at[x, y], self.from_core.at[x, y])
        if self.first == "x":
            self.copy = links.send(self.own.at[1 - links.x], self.from_first, "x")
        else:
            self.copy = links.send(self.own.at[:, 1 - links.y], self.from_first, "y")

    def first_done(self):
        links = self.links
        self.copy.wait_recv()
        for other in range(2):
            place = (links.x, other) if self.first == "x" else (other, links.y)
            self.add(self.own.at[place], self.from_first.at[other])
        if self.first == "x":
            self.copy = links.send(self.own.at[links.x, 1 - links.y], self.from_second, "y")
        else:
            self.copy = links.send(self.own.at[1 - links.x, links.y], self.from_second, "x")

    def second_done(self):
        self.copy.wait_recv()
        total = self.own.at[self.links.x, self.links.y]
        self.add(total, self.from_second)
        return total


def sum_space(blocks, rows, columns):
    shape = (rows, columns)
    return [
        pltpu.VMEM((blocks, 2, 2) + shape, jnp.bfloat16),
        pltpu.VMEM((blocks, 2, 2) + shape, jnp.bfloat16),
        pltpu.VMEM((blocks, 2) + shape, jnp.bfloat16),
        pltpu.VMEM((blocks,) + shape, jnp.bfloat16),
    ]


class RingSum:
    def __init__(self, links, parts, total, got, pieces=4):
        self.links, self.parts, self.total, self.got = links, parts, total, got
        self.pieces, self.last = pieces, [None] * pieces
        self.rows = parts.shape[1] // pieces

    def step(self, number):
        links = self.links
        for piece in range(self.pieces):
            way = 1 if piece < self.pieces // 2 else -1
            block = links.along(-way * (number + 1))
            where = pl.ds(piece * self.rows, self.rows)
            if number == 0:
                source = self.parts.at[block, where]
            else:
                self.last[piece].wait_recv()
                total = self.got[number - 1, where].astype(jnp.float32) + self.parts[
                    block, where
                ].astype(jnp.float32)
                if number == links.line - 1:
                    self.total[where] = total
                    continue
                self.parts[block, where] = total.astype(self.parts.dtype)
                source = self.parts.at[block, where]
            self.last[piece] = links.send(source, self.got.at[number, where], way)


def link_call(kernel, collective_id, copies, shapes, arguments, spaces=None, scratch=(), vmem=16):
    any_space = pl.BlockSpec(memory_space=pl.ANY)
    near_space = pl.BlockSpec(memory_space=pltpu.VMEM)
    many = isinstance(shapes, tuple)
    if spaces is None:
        spaces = "h" * (len(arguments) + (len(shapes) if many else 1))
    specs = [near_space if space == "v" else any_space for space in spaces]
    return pl.pallas_call(
        kernel,
        out_shape=shapes,
        in_specs=specs[: len(arguments)],
        out_specs=tuple(specs[len(arguments) :]) if many else specs[-1],
        scratch_shapes=list(scratch)
        + [pltpu.SemaphoreType.DMA((copies,)), pltpu.SemaphoreType.DMA((copies,))],
        compiler_params=pltpu.CompilerParams(
            collective_id=collective_id, has_side_effects=True, vmem_limit_bytes=vmem * 2**20
        ),
    )(*arguments)


def forward_call(freqs, tokens, places, pack, pack_ff, w_out, line):
    span_len, width = tokens.shape
    group_len = line * span_len
    rows_each = pack_ff.shape[1]
    qkv_cols = pack.shape[2]
    q_cols = qkv_cols - 2 * HD
    f32, bf16 = jnp.float32, jnp.bfloat16
    outs = (
        ((line, span_len, width), bf16),
        ((line, 8) + pack.shape[1:], bf16),
        ((2, 16, width), f32),
        ((group_len, width), bf16),
        ((group_len, q_cols), bf16),
        ((2, group_len, 2 * HD), bf16),
        ((group_len, HD), f32),
        ((2, group_len, HD), f32),
        ((group_len, line * q_cols), bf16),
        ((line, 8) + pack_ff.shape[1:], bf16),
        ((line, 8) + w_out.shape, bf16),
    )
    return link_call(
        functools.partial(first_kernel, line),
        0,
        176,
        tuple(jax.ShapeDtypeStruct(*out) for out in outs),
        (freqs, tokens, places, pack, pack_ff, w_out),
        "v" + "h" * 16,
        scratch=[
            pltpu.VMEM((line, span_len, width), bf16),
            pltpu.VMEM((line,) + places.shape, f32),
            pltpu.VMEM((line, 8) + pack.shape[1:], bf16),
            pltpu.VMEM((2, 16, width), f32),
            pltpu.VMEM((group_len, width), bf16),
            pltpu.VMEM((2, group_len, HD), f32),
            pltpu.VMEM((group_len, qkv_cols), f32),
            pltpu.VMEM((group_len, q_cols), bf16),
            pltpu.VMEM((2, group_len, 2 * HD), bf16),
            pltpu.VMEM((group_len, HD), f32),
            pltpu.VMEM((group_len, q_cols), bf16),
        ],
        vmem=63,
    )


def mlp_kernel(
    line,
    cuts,
    keep_ref,
    gain_ref,
    mix_ref,
    xs_ref,
    atts_ref,
    out_ref,
    ff_ref,
    down_ref,
    middle_ref,
    total_ref,
    mixed_total_ref,
    sum_ref,
    grad_ff_ref,
    ff_half_ref,
    big,
    ff,
    down,
    norm,
    parts,
    mixed,
    gate_up,
    hidden,
    both_grad,
    got,
    mixed_parts,
    mixed_got,
    *scratch,
):
    f32, bf16 = jnp.float32, jnp.bfloat16
    space, (send_sems, recv_sems) = scratch[:-2], scratch[-2:]
    links = Links(send_sems, recv_sems, line)
    links.meet(["x", "y", "c", 1, line - 1])
    far = [1, line - 1] + list(range(2, line - 1))
    span_len, width = mix_ref.shape
    group_len = line * span_len
    ff_cols = hidden.shape[1]
    block_rows = width // line
    rows_each = block_rows // 8
    chunk = 2 * HD
    stay = links.keep(mix_ref, mixed.at[links.z])
    mix_ring = RingGather(links, mix_ref, lambda block, rows: mixed.at[block, rows])
    mix_ring.step(0)
    early = [
        links.keep(out_ref, big),
        links.keep(atts_ref, norm),
        links.keep(xs_ref, parts),
    ]
    late = [links.keep(ff_ref, ff), links.keep(down_ref, down)]
    ring = RingSum(links, parts, total_ref, got)
    mixed_ring = RingSum(links, mixed_parts, mixed_total_ref, mixed_got)
    items = []
    ff_items = []
    for index, k in enumerate(far[:2]):
        block = links.along(k)
        core, first, second = space[:3]
        ff_items.append(
            NearSum(
                links,
                lambda c, block=block: ff.at[block, :, :, c],
                ff.at[block, :, :, links.c],
                core.at[index],
                first.at[index],
                second.at[index],
                "xy"[index % 2],
                True,
            )
        )
    for index, (low, high) in enumerate(cuts):
        rows = pl.ds(low, high - low)
        core, first, second = space[3 * index + 3 : 3 * index + 6]
        items.append(
            NearSum(
                links,
                lambda c, rows=rows: big.at[:, :, c, rows],
                big.at[:, :, links.c, rows],
                core.at[0],
                first.at[0],
                second.at[0],
                "xy"[index % 2],
                True,
            )
        )
    for copy in early:
        copy.wait()

    half = group_len // 2
    out_rows = width // 8
    for part in range(2):
        low = part * half
        for column in range(4):
            lanes = slice(column * width // 4, (column + 1) * width // 4)
            value = None
            for k in range(8):
                term = jnp.dot(
                    norm[low : low + half, k * out_rows : (k + 1) * out_rows],
                    big[k // 4, k // 2 % 2, k % 2, :, lanes],
                    preferred_element_type=f32,
                )
                value = term if value is None else value + term
            gate_up[:half, lanes] = value * keep_ref[0:1, 0:1]

        def normalise(index, carry, low=low):
            block = (low // 16 + index) // (span_len // 16)
            rows = pl.ds(pl.multiple_of(index * 16, 16), 16)
            inside = pl.ds(pl.multiple_of(lax.rem(index, span_len // 16) * 16, 16), 16)
            values = parts[block, inside].astype(f32) + gate_up[rows, :width]
            gate_up[rows, :width] = values
            inverse = lax.rsqrt(jnp.mean(values * values, axis=-1, keepdims=True) + epsilon)
            target = pl.ds(pl.multiple_of(low + index * 16, 16), 16)
            norm[target] = (values * inverse * gain_ref[1]).astype(bf16)
            return carry

        lax.fori_loop(0, half // 16, normalise, 0)

        @pl.when(links.z // (line // 2) == part)
        def _():
            where = pl.multiple_of(lax.rem(links.z, line // 2) * span_len, span_len)
            middle_ref[...] = gate_up[pl.ds(where, span_len), :width]
        if part == 0:
            mix_ring.step(1)

    for copy in late:
        copy.wait()

    def columns_of(lanes, size):
        return ff[:, :, :, :, :, lanes].reshape(width, size)

    def forward(low, size):
        gates, ups = pl.ds(low, size), pl.ds(low + ff_cols, size)
        gate = jnp.dot(norm[...], columns_of(gates, size), preferred_element_type=f32)
        gate_up[:, gates] = gate
        swish = gate * jax.nn.sigmoid(gate)
        up = jnp.dot(norm[...], columns_of(ups, size), preferred_element_type=f32)
        gate_up[:, ups] = up
        hidden[:, gates] = (swish * up).astype(bf16)

    def backward(low, size):
        gates, ups = pl.ds(low, size), pl.ds(low + ff_cols, size)
        grad = lax.dot_general(
            mixed[...].reshape(group_len, width),
            down[gates],
            (((1,), (1,)), ((), ())),
            preferred_element_type=f32,
        )
        gate, up = gate_up[:, gates], gate_up[:, ups]
        sigmoid = jax.nn.sigmoid(gate)
        both_grad[:, gates] = (grad * up * sigmoid * (1.0 + gate * (1.0 - sigmoid))).astype(bf16)
        both_grad[:, ups] = (grad * (gate * sigmoid)).astype(bf16)

    def over_chunks(work, extent):
        def one(index, carry):
            work(pl.multiple_of(index * chunk, chunk), chunk)
            return carry

        lax.fori_loop(0, extent // chunk, one, 0)
        if extent % chunk:
            work(extent // chunk * chunk, extent % chunk)

    over_chunks(forward, ff_cols)
    mix_ring.step(2)

    def mixed_part(low, size):
        lanes = pl.ds(low, size)
        value = jnp.dot(hidden[...], down[:, lanes], preferred_element_type=f32).astype(bf16)
        mixed_parts[:, :, lanes] = value.reshape(line, span_len, size)

    over_chunks(mixed_part, width)
    mixed_ring.step(0)
    stay.wait()
    mix_ring.step(3)
    hidden_rows = hidden[...].T

    def down_part(low, size):
        lanes = pl.ds(low, size)
        value = jnp.dot(
            hidden_rows,
            mixed[:, :, lanes].reshape(group_len, size),
            preferred_element_type=f32,
        ).astype(bf16)
        big[:, :, :, : cuts[-1][1], lanes] = value.reshape(2, 2, 2, cuts[-1][1], size)

    over_chunks(down_part, width)
    for item in items:
        item.start()
    over_chunks(backward, ff_cols)
    mixed_ring.step(1)
    for item in items:
        item.core_done()

    def norm_part(index, carry):
        size = 4 * rows_each
        weight = ff[index // 2, lax.rem(index, 2)].reshape(size, 2 * ff_cols)
        value = lax.dot_general(
            both_grad[...], weight, (((1,), (1,)), ((), ())), preferred_element_type=f32
        ).astype(bf16)
        lanes = pl.ds(pl.multiple_of(index * size, size), size)
        parts[:, :, lanes] = value.reshape(line, span_len, size)
        return carry

    lax.fori_loop(0, 2 * line, norm_part, 0)
    ring.step(0)

    def ff_block(block):
        norm_rows = norm[:, pl.ds(pl.multiple_of(block * block_rows, block_rows), block_rows)].T

        def ff_part(low, size):
            lanes = pl.ds(low, size)
            value = jnp.dot(norm_rows, both_grad[:, lanes], preferred_element_type=f32)
            ff[block, :, :, :, :, lanes] = value.astype(bf16).reshape(2, 2, 2, rows_each, size)

        over_chunks(ff_part, 2 * ff_cols)

    for item, k in zip(ff_items, far):
        ff_block(links.along(k))
        item.start()
    for item in items:
        item.first_done()
    ring.step(1)
    for item in ff_items:
        item.core_done()
    mixed_ring.step(2)
    sent = []
    for k in far[2:] + [0]:
        block = links.along(k)
        ff_block(block)
        sent.append(links.keep(ff.at[block], grad_ff_ref.at[block]))
    for item, (low, high) in zip(items, cuts):
        sum_ref[low:high] = item.second_done()[...]
    ring.step(2)
    for item in ff_items:
        item.first_done()
    mixed_ring.step(3)
    ring.step(3)
    for index, item in enumerate(ff_items):
        sent.append(links.keep(item.second_done(), ff_half_ref.at[index]))
    links.finish()
    for copy in sent:
        copy.wait()


def mlp_call(keep, gains, mixed, x_blocks, attended, out_w, ff_w, down_w, line):
    f32, bf16 = jnp.float32, jnp.bfloat16
    span_len, width = mixed.shape
    group_len = line * span_len
    ff_rows, both_cols, rows_each = down_w.shape[0], ff_w.shape[3], ff_w.shape[2]
    ff_w = ff_w.reshape(line, 2, 2, 2, rows_each, both_cols)
    rows = ff_rows // 8
    half = (rows // 2 + 15) // 16 * 16
    cuts = ((0, half), (half, rows))
    blocks = (line, span_len, width)
    token = jax.ShapeDtypeStruct((span_len, width), f32)
    return link_call(
        functools.partial(mlp_kernel, line, cuts),
        2,
        96,
        (
            token,
            token,
            token,
            jax.ShapeDtypeStruct((rows, width), bf16),
            jax.ShapeDtypeStruct(ff_w.shape, bf16),
            jax.ShapeDtypeStruct((2, rows_each, both_cols), bf16),
        ),
        (keep, gains, mixed, x_blocks, attended, out_w.reshape(2, 2, 2, width // 8, width), ff_w, down_w),
        "vvhhhhhh" + "vvvvhh",
        [
            pltpu.VMEM((2, 2, 2, width // 8, width), bf16),
            pltpu.VMEM(ff_w.shape, bf16),
            pltpu.VMEM(down_w.shape, bf16),
            pltpu.VMEM((group_len, width), bf16),
            pltpu.VMEM(blocks, bf16),
            pltpu.VMEM(blocks, bf16),
            pltpu.VMEM((group_len, both_cols), f32),
            pltpu.VMEM((group_len, ff_rows), bf16),
            pltpu.VMEM((group_len, both_cols), bf16),
            pltpu.VMEM((line - 1, span_len, width), bf16),
            pltpu.VMEM(blocks, bf16),
            pltpu.VMEM((line - 1, span_len, width), bf16),
        ]
        + sum_space(2, rows_each, both_cols)[1:]
        + sum((sum_space(1, high - low, width)[1:] for low, high in cuts), []),
        vmem=63,
    )


def backward_kernel(
    line,
    up_ref,
    middle_ref,
    norm_grad_ref,
    keep_ref,
    gain_ref,
    query_ref,
    kv_ref,
    peak_ref,
    turn_ref,
    out_ref,
    atts_ref,
    weight_ref,
    norm_ref,
    ff_ref,
    ff_half_ref,
    middle_grad_ref,
    total_ref,
    ffs_ref,
    outs_ref,
    qkvs_ref,
    big,
    slim,
    norm,
    own_rows,
    own_columns,
    branch,
    own_grad,
    att_grad,
    query_back,
    kv_back,
    kv_out,
    kv_in,
    flat,
    parts,
    query,
    kv,
    peak,
    turns,
    *scratch,
):
    f32, bf16 = jnp.float32, jnp.bfloat16
    send_sems, recv_sems = scratch[-2:]
    got, sums = scratch[0], scratch[1:-2]
    links = Links(send_sems, recv_sems, line)
    far = [1, line - 1] + list(range(2, line - 1))
    order = far + [0]
    links.meet(["x", "y", "c"] + far)
    span_len, width = up_ref.shape
    group_len = line * span_len
    q_cols = query.shape[1]
    heads = q_cols // HD
    rows_z = width // line
    rows_each = rows_z // 8
    scale = 1.0 / math.sqrt(HD)

    def lanes_of(block):
        return pl.ds(pl.multiple_of(block * q_cols, q_cols), q_cols)

    here = pl.ds(pl.multiple_of(links.z * span_len, span_len), span_len)
    loads = [
        links.keep(out_ref, big),
        links.keep(atts_ref.at[here], own_rows),
        links.keep(atts_ref.at[:, lanes_of(links.z)], own_columns),
        links.keep(query_ref, query),
        links.keep(kv_ref, kv),
        links.keep(peak_ref, peak),
        links.keep(turn_ref, turns),
        links.keep(norm_ref, norm),
        links.keep(weight_ref.at[:, :, :, :, pl.ds(0, slim.shape[4])], slim),
    ]
    ring = RingSum(links, parts, total_ref, got)

    def items_of(source, space, in_place, order=order):
        items = []
        for index, k in enumerate(order):
            block = links.along(k)
            own = source.at[block, :, :, links.c] if in_place else space[0].at[index]
            core, first, second = space[-3:]
            items.append(
                NearSum(
                    links,
                    lambda c, block=block: source.at[block, :, :, c],
                    own,
                    core.at[index],
                    first.at[index],
                    second.at[index],
                    "xy"[index % 2],
                    in_place,
                )
            )
        return items

    ff_order = order[2:]
    ff_items = items_of(ff_ref, sums[:4], False, ff_order)
    out_items = items_of(big, sums[4:7], True)
    qkv_items = items_of(slim, sums[7:], True)
    local = []
    arrived = [
        links.send(ff_half_ref.at[index], ffs_ref.at[links.z], k) for index, k in enumerate(order[:2])
    ]

    def turn(items, target, low, high, order=order):
        for item, k in list(zip(items, order))[low:high]:
            total = item.second_done()
            if k == 0:
                local.append(links.keep(total, target.at[links.z]))
            else:
                arrived.append(links.send(total, target.at[links.z], k))

    def core_done(items, low, high):
        for item in items[low:high]:
            item.core_done()

    def first_done(items, low, high):
        for item in items[low:high]:
            item.first_done()

    half = line // 2
    for item in ff_items:
        item.start()

    def d_middle(index, carry):
        rows = pl.ds(pl.multiple_of(index * 16, 16), 16)
        middle = middle_ref[rows]
        inverse = lax.rsqrt(jnp.mean(middle * middle, axis=-1, keepdims=True) + epsilon)
        scaled = gain_ref[1] * norm_grad_ref[rows]
        grad = (
            up_ref[rows]
            + inverse * scaled
            - middle
            * (inverse * inverse * inverse)
            * jnp.mean(scaled * middle, axis=-1, keepdims=True)
        )
        middle_grad_ref[rows] = grad
        branch[rows] = (grad * keep_ref[0:1, 0:1]).astype(bf16)
        return carry

    lax.fori_loop(0, span_len // 16, d_middle, 0)
    for copy in loads:
        copy.wait()
    for z in range(line):
        weight = big[z].reshape(rows_z, width)
        own_grad[:, z * rows_z : (z + 1) * rows_z] = lax.dot_general(
            branch[...], weight, (((1,), (1,)), ((), ())), preferred_element_type=f32
        ).astype(bf16)
    turned = [links.send(own_grad.at[:, lanes_of(links.along(k))], att_grad.at[here], k) for k in far]
    stayed = links.keep(own_grad.at[:, lanes_of(links.z)], att_grad.at[here])
    core_done(ff_items, 0, line)
    for z in range(line):
        for part in range(4):
            columns = slice(part * width // 4, (part + 1) * width // 4)
            grad = lax.dot_general(
                own_rows[:, z * rows_z : (z + 1) * rows_z],
                branch[:, columns],
                (((0,), (0,)), ((), ())),
                preferred_element_type=f32,
            )
            big[z, :, :, :, :, columns] = grad.astype(bf16).reshape(2, 2, 2, rows_each, width // 4)
    for item in out_items:
        item.start()
    kv_back[...] = jnp.zeros_like(kv_back)
    for copy in turned:
        copy.wait_recv()
    stayed.wait()

    def attend_back(head, carry):
        lanes = pl.ds(pl.multiple_of(head * HD, HD), HD)
        for block in range(line):
            rows = slice(block * span_len, (block + 1) * span_len)
            reach = (block + 1) * span_len
            part, grad = query[rows, lanes], att_grad[rows, lanes]
            row = lax.broadcasted_iota(jnp.int32, (span_len, reach), 0) + block * span_len
            column = lax.broadcasted_iota(jnp.int32, (span_len, reach), 1)
            allowed = (column <= row, column < (block + links.x) * span_len)
            spot = lax.broadcasted_iota(jnp.int32, (span_len, HD), 1) == head
            top = jnp.sum(jnp.where(spot, peak[rows], 0.0), axis=-1, keepdims=True)
            delta = jnp.sum(
                grad.astype(f32) * own_columns[rows, lanes].astype(f32), axis=-1, keepdims=True
            )
            total = None
            for side in range(2):
                keys, values = kv[side, :reach, :HD], kv[side, :reach, HD:]
                score = lax.dot_general(
                    part, keys, (((1,), (1,)), ((), ())), preferred_element_type=f32
                )
                weight = jnp.where(allowed[side], jnp.exp(score * scale - top), 0.0)
                weight_grad = lax.dot_general(
                    grad, values, (((1,), (1,)), ((), ())), preferred_element_type=f32
                )
                score_grad = (weight * (weight_grad - delta)).astype(bf16)
                term = jnp.dot(score_grad, keys, preferred_element_type=f32)
                total = term if total is None else total + term
                kv_back[side, :reach, :HD] += lax.dot_general(
                    score_grad, part, (((0,), (0,)), ((), ())), preferred_element_type=f32
                )
                kv_back[side, :reach, HD:] += lax.dot_general(
                    weight.astype(bf16), grad, (((0,), (0,)), ((), ())), preferred_element_type=f32
                )
            query_back[rows, lanes] = total * scale
        return carry

    lax.fori_loop(0, heads, attend_back, 0)
    kv_out[:, :HD] = (kv_back[1, :, :HD] * scale).astype(bf16)
    kv_out[:, HD:] = kv_back[1, :, HD:].astype(bf16)
    exchange = links.send(kv_out, kv_in, "x")

    def turn_back(values, rows):
        return values * turns[0, rows] - pltpu.roll(values, HD // 2, 1) * turns[1, rows]

    for block in range(line):
        rows = slice(block * span_len, (block + 1) * span_len)
        for head in range(heads):
            lanes = slice(head * HD, (head + 1) * HD)
            flat[rows, lanes] = turn_back(query_back[rows, lanes], rows).astype(bf16)
    first_done(ff_items, 0, line)
    exchange.wait_recv()
    for block in range(line):
        rows = slice(block * span_len, (block + 1) * span_len)
        key_grad = kv_back[0, rows, :HD] * scale + kv_in[rows, :HD].astype(f32)
        flat[rows, q_cols : q_cols + HD] = turn_back(key_grad, rows).astype(bf16)
        value_grad = kv_back[0, rows, HD:] + kv_in[rows, HD:].astype(f32)
        flat[rows, q_cols + HD :] = value_grad.astype(bf16)
    for z in range(line):
        weight = slim[z].reshape(rows_z, flat.shape[1])
        part = lax.dot_general(
            flat[...], weight, (((1,), (1,)), ((), ())), preferred_element_type=f32
        ).astype(bf16)
        for block in range(line):
            parts[block, :, z * rows_z : (z + 1) * rows_z] = part[
                block * span_len : (block + 1) * span_len
            ]
    ring.step(0)
    for z in range(line):
        grad = lax.dot_general(
            norm[:, z * rows_z : (z + 1) * rows_z],
            flat[...],
            (((0,), (0,)), ((), ())),
            preferred_element_type=f32,
        )
        slim[z] = grad.astype(bf16).reshape(2, 2, 2, rows_each, flat.shape[1])
    for item in qkv_items:
        item.start()
    core_done(out_items, 0, half)
    turn(ff_items, ffs_ref, 0, line, ff_order)
    ring.step(1)
    core_done(out_items, half, line)
    first_done(out_items, 0, half)
    ring.step(2)
    core_done(qkv_items, 0, line)
    first_done(out_items, half, line)
    turn(out_items, outs_ref, 0, half)
    ring.step(3)
    first_done(qkv_items, 0, half)
    turn(out_items, outs_ref, half, line)
    first_done(qkv_items, half, line)
    turn(qkv_items, qkvs_ref, 0, line)
    for copy in arrived:
        copy.wait_recv()
    links.finish()
    for copy in local:
        copy.wait()


def backward_call(small, saved, out_w, attended, weights, norm, grad_ff, ff_half, line):
    f32, bf16 = jnp.float32, jnp.bfloat16
    span_len, width = small[0].shape
    group_len = line * span_len
    query = saved[0]
    q_cols, rows_each, qkv_cols = query.shape[1], width // line // 8, weights.shape[3]
    weights = weights.reshape(line, 2, 2, 2, -1, qkv_cols)
    wide = (line, 2, 2, 2, rows_each, width)
    slim = (line, 2, 2, 2, rows_each, qkv_cols)
    out_space = sum_space(line, rows_each, width)[1:]
    qkv_space = sum_space(line, rows_each, qkv_cols)[1:]
    token = jax.ShapeDtypeStruct((span_len, width), f32)
    return link_call(
        functools.partial(backward_kernel, line),
        4,
        160,
        (token, token)
        + tuple(
            jax.ShapeDtypeStruct((line, rows_each, columns), bf16)
            for columns in (grad_ff.shape[5], width, qkv_cols)
        ),
        small + saved + (out_w.reshape(wide), attended, weights, norm, grad_ff, ff_half),
        "v" * 5 + "h" * 10 + "vvhhh",
        [
            pltpu.VMEM(wide, bf16),
            pltpu.VMEM(slim, bf16),
            pltpu.VMEM((group_len, width), bf16),
            pltpu.VMEM((span_len, width), bf16),
            pltpu.VMEM((group_len, q_cols), bf16),
            pltpu.VMEM((span_len, width), bf16),
            pltpu.VMEM((span_len, width), bf16),
            pltpu.VMEM((group_len, q_cols), bf16),
            pltpu.VMEM((group_len, q_cols), f32),
            pltpu.VMEM((2, group_len, 2 * HD), f32),
            pltpu.VMEM((group_len, 2 * HD), bf16),
            pltpu.VMEM((group_len, 2 * HD), bf16),
            pltpu.VMEM((group_len, qkv_cols), bf16),
            pltpu.VMEM((line, span_len, width), bf16),
        ]
        + [pltpu.VMEM(value.shape, value.dtype) for value in saved]
        + [pltpu.VMEM((line - 1, span_len, width), bf16)]
        + sum_space(line - 2, rows_each, grad_ff.shape[5])
        + out_space
        + qkv_space,
        vmem=63,
    )


def general_body(
    tokens,
    attn_gain,
    w_query,
    w_key,
    w_value,
    w_out,
    mlp_gain,
    w_gate,
    w_up,
    w_down,
    keep_mask,
    group_ids,
    positions,
    exit_scale,
    out_grad,
):
    seq_count, span_len, model_width = tokens.shape
    kv_heads = KVH
    head_dim = HD
    head_count = HEADS
    group_size = head_count // kv_heads
    row_count = seq_count * span_len
    stripe = group_size * span_len
    wide_count = lax.axis_size("wide")
    wide_place = lax.axis_index("wide")
    full_len = span_len * wide_count
    score_scale = 1.0 / math.sqrt(head_dim)
    gain_one, query_w, key_w, value_w, out_w = (
        lax.all_gather(attn_gain, ("wide", "narrow"), axis=0, tiled=True),
        lax.all_gather(w_query, ("wide", "narrow"), axis=0, tiled=True),
        lax.all_gather(w_key, ("wide", "narrow"), axis=0, tiled=True),
        lax.all_gather(w_value, ("wide", "narrow"), axis=0, tiled=True),
        lax.all_gather(w_out, ("wide", "narrow"), axis=0, tiled=True),
    )
    inputs = tokens.astype(jnp.float32).reshape(row_count, model_width)
    token_pos = positions.reshape(row_count)
    keep_rows = jnp.repeat(keep_mask.astype(jnp.float32), span_len)[:, None]
    inverse_one = lax.rsqrt(jnp.mean(inputs * inputs, axis=-1, keepdims=True) + epsilon)
    first_norm = (inputs * inverse_one * gain_one.astype(jnp.float32)).astype(jnp.bfloat16)
    query_pre = jnp.dot(first_norm, query_w, preferred_element_type=jnp.float32).reshape(
        row_count, head_count, head_dim
    )
    key_pre = jnp.dot(first_norm, key_w, preferred_element_type=jnp.float32).reshape(
        row_count, kv_heads, head_dim
    )
    query_rows = rotate(query_pre, token_pos, 1.0).astype(jnp.bfloat16)
    key_heads = (
        rotate(key_pre, token_pos, 1.0)
        .astype(jnp.bfloat16)
        .reshape(seq_count, span_len, kv_heads * head_dim)
    )
    value_heads = (
        jnp.dot(first_norm, value_w, preferred_element_type=jnp.float32)
        .astype(jnp.bfloat16)
        .reshape(seq_count, span_len, kv_heads * head_dim)
    )
    queries = (
        query_rows.reshape(seq_count, span_len, kv_heads, group_size, head_dim)
        .transpose(0, 2, 3, 1, 4)
        .reshape(seq_count, kv_heads, stripe, head_dim)
    )
    query_index = wide_place * span_len + jnp.arange(stripe, dtype=jnp.int32) % span_len
    last_query = wide_place * span_len + span_len - 1

    def block_scores(key_block, key_first):
        scores = (
            jnp.einsum("skrd,sjkd->skrj", queries, key_block, preferred_element_type=jnp.float32)
            * score_scale
        )
        key_index = key_first + jnp.arange(key_block.shape[1], dtype=jnp.int32)
        allowed = key_index[None, :] <= query_index[:, None]
        return (scores, allowed)

    start_forward = (
        jnp.full((seq_count, kv_heads, stripe), -1e30, jnp.float32),
        jnp.zeros((seq_count, kv_heads, stripe), jnp.float32),
        jnp.zeros((seq_count, kv_heads, stripe, head_dim), jnp.float32),
    )
    running = start_forward
    pieces = (
        lax.all_gather(key_heads, "wide", axis=1, tiled=True),
        lax.all_gather(value_heads, "wide", axis=1, tiled=True),
    )
    key_blocks = split_blocks(pieces[0], seq_count, kv_heads, head_dim)
    value_blocks = split_blocks(pieces[1], seq_count, kv_heads, head_dim)
    block_len = key_blocks.shape[2]

    def advance(carried, block_item):
        key_block, value_block, block_index = block_item
        key_first = block_index * block_len

        def compute_block(current):
            run_max, run_sum, run_acc = current
            scores, allowed = block_scores(key_block, key_first)
            scores = jnp.where(allowed, scores, -1e30)
            new_max = jnp.maximum(run_max, jnp.max(scores, axis=-1))
            factor = jnp.exp(run_max - new_max)
            weights = jnp.where(allowed, jnp.exp(scores - new_max[..., None]), 0.0)
            new_sum = run_sum * factor + jnp.sum(weights, axis=-1)
            new_acc = run_acc * factor[..., None] + jnp.einsum(
                "skrj,sjkd->skrd",
                weights.astype(jnp.bfloat16),
                value_block,
                preferred_element_type=jnp.float32,
            )
            return (new_max, new_sum, new_acc)

        return (lax.cond(key_first <= last_query, compute_block, unchanged, carried), None)

    running, _ = lax.scan(
        advance,
        running,
        (key_blocks, value_blocks, jnp.arange(key_blocks.shape[0], dtype=jnp.int32)),
    )
    run_max, run_sum, run_acc = running
    attended = run_acc / run_sum[..., None]
    log_total = run_max + jnp.log(run_sum)
    attended_rows = (
        attended.reshape(seq_count, kv_heads, group_size, span_len, head_dim)
        .transpose(0, 3, 1, 2, 4)
        .reshape(row_count, head_count * head_dim)
        .astype(jnp.bfloat16)
    )
    middle = inputs + keep_rows * jnp.dot(attended_rows, out_w, preferred_element_type=jnp.float32)
    gain_two, gate_w, up_w, down_w = (
        lax.all_gather(mlp_gain, ("wide", "narrow"), axis=0, tiled=True),
        lax.all_gather(w_gate, ("wide", "narrow"), axis=0, tiled=True),
        lax.all_gather(w_up, ("wide", "narrow"), axis=0, tiled=True),
        lax.all_gather(w_down, ("wide", "narrow"), axis=0, tiled=True),
    )
    inverse_two = lax.rsqrt(jnp.mean(middle * middle, axis=-1, keepdims=True) + epsilon)
    second_norm = (middle * inverse_two * gain_two.astype(jnp.float32)).astype(jnp.bfloat16)
    gate_value = jnp.dot(second_norm, gate_w, preferred_element_type=jnp.float32)
    up_value = jnp.dot(second_norm, up_w, preferred_element_type=jnp.float32)
    gate_sigmoid = jax.nn.sigmoid(gate_value)
    swish_value = gate_value * gate_sigmoid
    hidden = (swish_value * up_value).astype(jnp.bfloat16)
    output = (
        middle + keep_rows * jnp.dot(hidden, down_w, preferred_element_type=jnp.float32)
    ).astype(jnp.bfloat16)
    group_match = (
        group_ids.reshape(row_count)[:, None]
        == jnp.arange(exit_scale.shape[0], dtype=jnp.int32)[None, :]
    )
    token_scale = jnp.sum(jnp.where(group_match, exit_scale[None, :], 0.0), axis=1, keepdims=True)
    upstream = out_grad.astype(jnp.float32).reshape(row_count, model_width) * token_scale
    gain_two, gate_w, up_w, down_w = (
        lax.all_gather(mlp_gain, ("wide", "narrow"), axis=0, tiled=True),
        lax.all_gather(w_gate, ("wide", "narrow"), axis=0, tiled=True),
        lax.all_gather(w_up, ("wide", "narrow"), axis=0, tiled=True),
        lax.all_gather(w_down, ("wide", "narrow"), axis=0, tiled=True),
    )
    mixed_grad = (keep_rows * upstream).astype(jnp.bfloat16)
    grad_down = over_rows(hidden, mixed_grad)
    hidden_grad = against(mixed_grad, down_w)
    gate_grad = (
        hidden_grad * up_value * gate_sigmoid * (1.0 + gate_value * (1.0 - gate_sigmoid))
    ).astype(jnp.bfloat16)
    up_grad = (hidden_grad * swish_value).astype(jnp.bfloat16)
    grad_gate = over_rows(second_norm, gate_grad)
    grad_up = over_rows(second_norm, up_grad)
    norm_grad = against(gate_grad, gate_w) + against(up_grad, up_w)
    grad_gain_two = jnp.sum(norm_grad * middle * inverse_two, axis=0)
    scaled_two = gain_two.astype(jnp.float32) * norm_grad
    middle_grad = (
        upstream
        + inverse_two * scaled_two
        - middle
        * (inverse_two * inverse_two * inverse_two)
        * jnp.mean(scaled_two * middle, axis=-1, keepdims=True)
    )
    gain_two_share, gate_share, up_share, down_share = (
        lax.psum_scatter(grad_gain_two, ("wide", "narrow"), scatter_dimension=0, tiled=True),
        lax.psum_scatter(grad_gate, ("wide", "narrow"), scatter_dimension=0, tiled=True),
        lax.psum_scatter(grad_up, ("wide", "narrow"), scatter_dimension=0, tiled=True),
        lax.psum_scatter(grad_down, ("wide", "narrow"), scatter_dimension=0, tiled=True),
    )
    gain_one, query_w, key_w, value_w, out_w = (
        lax.all_gather(attn_gain, ("wide", "narrow"), axis=0, tiled=True),
        lax.all_gather(w_query, ("wide", "narrow"), axis=0, tiled=True),
        lax.all_gather(w_key, ("wide", "narrow"), axis=0, tiled=True),
        lax.all_gather(w_value, ("wide", "narrow"), axis=0, tiled=True),
        lax.all_gather(w_out, ("wide", "narrow"), axis=0, tiled=True),
    )
    branch_grad = (keep_rows * middle_grad).astype(jnp.bfloat16)
    grad_out = over_rows(attended_rows, branch_grad)
    attended_grad = against(branch_grad, out_w).astype(jnp.bfloat16)
    grouped_grad = (
        attended_grad.reshape(seq_count, span_len, kv_heads, group_size, head_dim)
        .transpose(0, 2, 3, 1, 4)
        .reshape(seq_count, kv_heads, stripe, head_dim)
    )
    row_delta = jnp.sum(grouped_grad.astype(jnp.float32) * attended, axis=-1)
    start_backward = (
        jnp.zeros((seq_count, kv_heads, stripe, head_dim), jnp.float32),
        jnp.zeros((seq_count, full_len, kv_heads * head_dim), jnp.float32),
        jnp.zeros((seq_count, full_len, kv_heads * head_dim), jnp.float32),
    )
    running = start_backward
    pieces = (
        lax.all_gather(key_heads, "wide", axis=1, tiled=True),
        lax.all_gather(value_heads, "wide", axis=1, tiled=True),
    )
    key_blocks = split_blocks(pieces[0], seq_count, kv_heads, head_dim)
    value_blocks = split_blocks(pieces[1], seq_count, kv_heads, head_dim)
    fold_block_len = key_blocks.shape[2]

    def advance(carried, block_item):
        key_block, value_block, block_index = block_item
        key_first = block_index * fold_block_len

        def compute_block(current):
            query_acc, key_acc, value_acc = current
            scores, allowed = block_scores(key_block, key_first)
            probabilities = jnp.where(allowed, jnp.exp(scores - log_total[..., None]), 0.0)
            value_part = jnp.einsum(
                "skrj,skrd->sjkd",
                probabilities.astype(jnp.bfloat16),
                grouped_grad,
                preferred_element_type=jnp.float32,
            )
            prob_grad = jnp.einsum(
                "skrd,sjkd->skrj", grouped_grad, value_block, preferred_element_type=jnp.float32
            )
            score_grad = (probabilities * (prob_grad - row_delta[..., None])).astype(jnp.bfloat16)
            query_acc = (
                query_acc
                + jnp.einsum(
                    "skrj,sjkd->skrd", score_grad, key_block, preferred_element_type=jnp.float32
                )
                * score_scale
            )
            key_part = (
                jnp.einsum(
                    "skrj,skrd->sjkd", score_grad, queries, preferred_element_type=jnp.float32
                )
                * score_scale
            )
            key_acc = add_rows(
                key_acc, key_part.reshape(seq_count, fold_block_len, kv_heads * head_dim), key_first
            )
            value_acc = add_rows(
                value_acc,
                value_part.reshape(seq_count, fold_block_len, kv_heads * head_dim),
                key_first,
            )
            return (query_acc, key_acc, value_acc)

        return (lax.cond(key_first <= last_query, compute_block, unchanged, carried), None)

    running, _ = lax.scan(
        advance,
        running,
        (key_blocks, value_blocks, jnp.arange(key_blocks.shape[0], dtype=jnp.int32)),
    )
    query_acc, key_acc, value_acc = running
    key_sum, value_sum = (
        lax.psum_scatter(
            key_acc.astype(jnp.bfloat16), "wide", scatter_dimension=1, tiled=True
        ).astype(jnp.float32),
        lax.psum_scatter(
            value_acc.astype(jnp.bfloat16), "wide", scatter_dimension=1, tiled=True
        ).astype(jnp.float32),
    )
    query_back = (
        query_acc.reshape(seq_count, kv_heads, group_size, span_len, head_dim)
        .transpose(0, 3, 1, 2, 4)
        .reshape(row_count, head_count, head_dim)
    )
    query_grad = (
        rotate(query_back, token_pos, -1.0)
        .reshape(row_count, head_count * head_dim)
        .astype(jnp.bfloat16)
    )
    key_grad = (
        rotate(key_sum.reshape(row_count, kv_heads, head_dim), token_pos, -1.0)
        .reshape(row_count, kv_heads * head_dim)
        .astype(jnp.bfloat16)
    )
    value_grad = value_sum.reshape(row_count, kv_heads * head_dim).astype(jnp.bfloat16)
    grad_query = over_rows(first_norm, query_grad)
    grad_key = over_rows(first_norm, key_grad)
    grad_value = over_rows(first_norm, value_grad)
    input_norm_grad = (
        against(query_grad, query_w) + against(key_grad, key_w) + against(value_grad, value_w)
    )
    grad_gain_one = jnp.sum(input_norm_grad * inputs * inverse_one, axis=0)
    scaled_one = gain_one.astype(jnp.float32) * input_norm_grad
    input_grad = (
        middle_grad
        + inverse_one * scaled_one
        - inputs
        * (inverse_one * inverse_one * inverse_one)
        * jnp.mean(scaled_one * inputs, axis=-1, keepdims=True)
    )
    gain_one_share, query_share, key_share, value_share, out_share = (
        lax.psum_scatter(grad_gain_one, ("wide", "narrow"), scatter_dimension=0, tiled=True),
        lax.psum_scatter(grad_query, ("wide", "narrow"), scatter_dimension=0, tiled=True),
        lax.psum_scatter(grad_key, ("wide", "narrow"), scatter_dimension=0, tiled=True),
        lax.psum_scatter(grad_value, ("wide", "narrow"), scatter_dimension=0, tiled=True),
        lax.psum_scatter(grad_out, ("wide", "narrow"), scatter_dimension=0, tiled=True),
    )
    return (
        output.reshape(seq_count, span_len, model_width),
        input_grad.astype(jnp.bfloat16).reshape(seq_count, span_len, model_width),
        gain_one_share,
        query_share,
        key_share,
        value_share,
        out_share,
        gain_two_share,
        gate_share,
        up_share,
        down_share,
    )


def line_body(
    tokens,
    attn_gain,
    w_query,
    w_key,
    w_value,
    w_out,
    mlp_gain,
    w_gate,
    w_up,
    w_down,
    keep_mask,
    group_ids,
    positions,
    exit_scale,
    out_grad,
):
    f32 = jnp.float32
    bf16 = jnp.bfloat16
    _, span_len, model_width = tokens.shape
    line = lax.axis_size("z")
    rows_each = w_query.shape[0]
    q_cols = HEADS // line * HD
    ff_cols = w_gate.shape[1] // line
    group_len = span_len * line

    def by_columns(weight, columns):
        return weight.reshape(rows_each, line, columns).transpose(1, 0, 2)

    down_w = lax.all_gather(w_down, ("x", "y", "c"), axis=0, tiled=True)
    own_x = tokens[0].astype(f32)
    keep = keep_mask[0].astype(f32)
    group_match = group_ids[0][:, None] == jnp.arange(exit_scale.shape[0], dtype=jnp.int32)[None, :]
    token_scale = jnp.sum(jnp.where(group_match, exit_scale[None, :], 0.0), axis=1, keepdims=True)
    upstream = out_grad[0].astype(f32) * token_scale

    core = lax.axis_index("c")
    gain_row = jnp.zeros((q_cols + 2 * HD,), bf16)
    gain_row = lax.dynamic_update_slice_in_dim(gain_row, attn_gain, core * rows_each, 0)
    gain_row = lax.dynamic_update_slice_in_dim(gain_row, mlp_gain, HD + core * rows_each, 0)
    gain_rows = jnp.broadcast_to(gain_row, (line, 16, gain_row.shape[0]))
    pack_attn = jnp.concatenate(
        [by_columns(w_query, q_cols), by_columns(w_key, HD), by_columns(w_value, HD)], axis=2
    )
    pack_attn = jnp.concatenate([pack_attn, gain_rows], axis=1)
    pack_ff = jnp.concatenate([by_columns(w_gate, ff_cols), by_columns(w_up, ff_cols)], axis=2)
    freqs = 10000.0 ** (-2.0 * jnp.arange(HD // 2, dtype=f32) / HD)
    freqs = jnp.broadcast_to(jnp.concatenate([freqs, freqs])[None], (8, HD))
    places = jnp.broadcast_to(positions[0].astype(f32)[None], (8, span_len))
    own_mixed = (keep * upstream).astype(bf16)
    first_tokens, own_mixed, upstream = lax.optimization_barrier((tokens[0], own_mixed, upstream))
    (
        x_blocks,
        near_w,
        gain_all,
        first_norm,
        queries,
        both_kv,
        log_total,
        turns,
        attended_rows,
        ff_w,
        out_w,
    ) = forward_call(freqs, first_tokens, places, pack_attn, pack_ff, w_out, line)
    keep_tile = jnp.broadcast_to(keep, (8, HD))
    middle, norm_grad, mixed, grad_down, grad_ff, ff_half = mlp_call(
        keep_tile,
        gain_all,
        own_mixed,
        x_blocks,
        attended_rows,
        out_w,
        ff_w,
        down_w,
        line,
    )
    grad_down = grad_down.astype(f32)
    output = (middle + keep * mixed).astype(bf16)
    middle_grad, input_norm_grad, ff_back, out_back, qkv_back = backward_call(
        (
            upstream,
            middle,
            norm_grad,
            keep_tile,
            gain_all,
        ),
        (queries, both_kv, log_total, turns),
        out_w,
        attended_rows,
        near_w,
        first_norm,
        grad_ff,
        ff_half,
        line,
    )
    ff_back = ff_back.astype(f32)
    qkv_back = qkv_back.astype(f32)
    grad_out = jnp.sum(out_back.astype(f32), axis=0)
    gain_one = gain_all[0, :1]
    inverse_one = lax.rsqrt(jnp.mean(own_x * own_x, axis=-1, keepdims=True) + epsilon)
    scaled_one = gain_one * input_norm_grad
    input_grad = (
        middle_grad
        + inverse_one * scaled_one
        - own_x
        * (inverse_one * inverse_one * inverse_one)
        * jnp.mean(scaled_one * own_x, axis=-1, keepdims=True)
    )

    def side_by_side(blocks):
        return blocks.transpose(1, 0, 2).reshape(rows_each, -1)

    grad_query = side_by_side(qkv_back[:, :, :q_cols])
    grad_key = side_by_side(qkv_back[:, :, q_cols : q_cols + HD])
    grad_value = side_by_side(qkv_back[:, :, q_cols + HD :])
    grad_gate = side_by_side(ff_back[:, :, :ff_cols])
    grad_up = side_by_side(ff_back[:, :, ff_cols:])

    def gain_grad(pairs, gain):
        total = sum(jnp.sum(weight.astype(f32) * grad, axis=1) for weight, grad in pairs)
        return total / gain.astype(f32)

    return (
        output[None],
        input_grad.astype(bf16)[None],
        gain_grad([(w_query, grad_query), (w_key, grad_key), (w_value, grad_value)], attn_gain),
        grad_query,
        grad_key,
        grad_value,
        grad_out,
        gain_grad([(w_gate, grad_gate), (w_up, grad_up)], mlp_gain),
        grad_gate,
        grad_up,
        grad_down,
    )


def solution(mesh):
    wide, narrow = mesh.shape["wide"], mesh.shape["narrow"]
    if wide == 2 * KVH and narrow == 4:
        mesh = Mesh(mesh.devices.reshape(wide // 2, 2, 2, 2), ("z", "x", "y", "c"))
        body, wide, narrow = line_body, ("z", "x"), ("y", "c")
    else:
        body, wide, narrow = general_body, ("wide",), ("narrow",)
    token_spec = P(narrow, wide, None)
    id_spec = P(narrow, wide)
    gain_spec = P(wide + narrow)
    weight_spec = P(wide + narrow, None)
    return jax.shard_map(
        body,
        mesh=mesh,
        in_specs=(
            token_spec,
            gain_spec,
            weight_spec,
            weight_spec,
            weight_spec,
            weight_spec,
            gain_spec,
            weight_spec,
            weight_spec,
            weight_spec,
            P(narrow),
            id_spec,
            id_spec,
            P(),
            token_spec,
        ),
        out_specs=(
            token_spec,
            token_spec,
            gain_spec,
            weight_spec,
            weight_spec,
            weight_spec,
            weight_spec,
            gain_spec,
            weight_spec,
            weight_spec,
            weight_spec,
        ),
        check_vma=False,
    )
```

```python
import functools
import math

import jax
import jax.numpy as jnp
from jax import lax
from jax.experimental import pallas as pl
from jax.experimental.pallas import tpu as pltpu
from jax.sharding import Mesh
from jax.sharding import PartitionSpec as P

HEADS = 16
KVH = 4
HD = 128


epsilon = 1e-05


def rotate(vectors, token_pos, direction):
    half_size = vectors.shape[-1] // 2
    freqs = 10000.0 ** (-2.0 * jnp.arange(half_size, dtype=jnp.float32) / vectors.shape[-1])
    angles = token_pos.astype(jnp.float32)[:, None] * freqs[None, :]
    cosine = jnp.cos(angles)[:, None, :]
    sine = direction * jnp.sin(angles)[:, None, :]
    first_half = vectors[..., :half_size]
    second_half = vectors[..., half_size:]
    return jnp.concatenate(
        [first_half * cosine - second_half * sine, second_half * cosine + first_half * sine],
        axis=-1,
    )


def split_blocks(piece_arr, seq_count, kv_heads, head_dim):
    piece_len = piece_arr.shape[1]
    block_len = math.gcd(piece_len, 512)
    shaped = piece_arr.reshape(seq_count, piece_len // block_len, block_len, kv_heads, head_dim)
    return shaped.transpose(1, 0, 2, 3, 4)


def add_rows(whole_arr, update, first_row):
    current = lax.dynamic_slice_in_dim(whole_arr, first_row, update.shape[1], 1)
    return lax.dynamic_update_slice_in_dim(whole_arr, current + update, first_row, 1)


def over_rows(left, right):
    return lax.dot_general(
        left, right, (((0,), (0,)), ((), ())), preferred_element_type=jnp.float32
    )


def against(left, right):
    return lax.dot_general(
        left, right, (((1,), (1,)), ((), ())), preferred_element_type=jnp.float32
    )


def unchanged(carried):
    return carried


MESH = pl.DeviceIdType.MESH
AXES = ("z", "x", "y", "c")


class Links:
    def __init__(self, send_sems, recv_sems, line):
        self.send_sems, self.recv_sems, self.line = send_sems, recv_sems, line
        self.z, self.x, self.y, self.c = (lax.axis_index(name) for name in AXES)
        self.slot = self.x * 4 + self.y * 2 + self.c
        self.used = 0
        self.sent = []

    def device(self, to):
        if to == "x":
            return (self.z, 1 - self.x, self.y, self.c)
        if to == "y":
            return (self.z, self.x, 1 - self.y, self.c)
        if to == "c":
            return (self.z, self.x, self.y, 1 - self.c)
        return (self.along(to), self.x, self.y, self.c)

    def along(self, step):
        return lax.rem(self.z + step + self.line, self.line)

    def other(self, to):
        slot = self.slot
        for name in to:
            bit = {"x": 4, "y": 2, "c": 1}[name]
            here = {"x": self.x, "y": self.y, "c": self.c}[name]
            slot = slot + bit * (1 - 2 * here)
        return slot

    def meet(self, targets):
        barrier = pltpu.get_barrier_semaphore()
        for to in targets:
            pl.semaphore_signal(barrier, inc=1, device_id=self.device(to), device_id_type=MESH)
        pl.semaphore_wait(barrier, len(targets))

    def send(self, source, target, to):
        copy = pltpu.make_async_remote_copy(
            src_ref=source,
            dst_ref=target,
            send_sem=self.send_sems.at[self.used],
            recv_sem=self.recv_sems.at[self.used],
            device_id=self.device(to),
            device_id_type=MESH,
        )
        copy.start()
        self.used += 1
        self.sent.append(copy)
        return copy

    def keep(self, source, target):
        copy = pltpu.make_async_copy(source, target, self.send_sems.at[self.used])
        copy.start()
        self.used += 1
        return copy

    def finish(self):
        for copy in self.sent:
            copy.wait_send()


class NearGather:
    def __init__(self, links, slot):
        self.links, self.slot = links, slot
        self.got = {}

    def offer(self, block, source):
        target = self.slot(block, self.links.slot)
        for to in ("x", "y", "c"):
            self.got[block, to] = self.links.send(source, target, to)

    def relay(self, block, first):
        links = self.links
        for to, then in (("x", "y"), ("y", "x")):
            self.got[block, to].wait_recv()
            place = self.slot(block, links.other(to))
            self.got[block, to + "c"] = links.send(place, place, "c")
            if to == first:
                self.got[block, "xy"] = links.send(place, place, then)

    def close(self, block):
        self.got[block, "xy"].wait_recv()
        place = self.slot(block, self.links.other("xy"))
        self.got[block, "xyc"] = self.links.send(place, place, "c")

    def wait(self, blocks):
        for block in blocks:
            for to in ("c", "xc", "yc", "xyc"):
                self.got[block, to].wait_recv()


class RingGather:
    def __init__(self, links, source, place, pieces=4):
        self.links, self.source, self.place, self.pieces = links, source, place, pieces
        self.rows = source.shape[0] // pieces
        self.last = [None] * pieces

    def step(self, number):
        for piece in range(self.pieces):
            way = 1 if piece < self.pieces // 2 else -1
            rows = pl.ds(piece * self.rows, self.rows)
            place = self.place(self.links.along(-way * number), rows)
            if number > 0:
                self.last[piece].wait_recv()
            if number < self.links.line - 1:
                origin = self.source.at[rows] if number == 0 else place
                self.last[piece] = self.links.send(origin, place, way)


def first_kernel(
    line,
    freq_ref,
    x_ref,
    place_ref,
    gain_rows_ref,
    query_w_ref,
    key_w_ref,
    value_w_ref,
    gate_w_ref,
    up_w_ref,
    out_ref,
    xs_ref,
    weight_ref,
    gain_ref,
    norm_ref,
    query_ref,
    kv_ref,
    peak_ref,
    turn_ref,
    atts_ref,
    ffs_ref,
    outs_ref,
    x_all,
    places,
    weights,
    gains,
    norm,
    turns,
    flat,
    query,
    kv,
    peak,
    att,
    send_sems,
    recv_sems,
):
    f32, bf16 = jnp.float32, jnp.bfloat16
    links = Links(send_sems, recv_sems, line)
    far = [1, line - 1] + list(range(2, line - 1))
    links.meet(["x", "y", "c"] + far)
    here = links.slot
    span_len, width = x_ref.shape
    group_len = line * span_len
    rows_each = gate_w_ref.shape[0]
    q_cols = query.shape[1]
    ff_cols = gate_w_ref.shape[1] // line
    heads = q_cols // HD
    local = []

    near = NearGather(links, lambda block, place: weights.at[links.along(-block), place])
    far_ff = NearGather(links, lambda block, place: ffs_ref.at[links.along(-block), place])
    far_out = NearGather(links, lambda block, place: outs_ref.at[links.along(-block), place])
    ring = RingGather(links, x_ref, lambda block, rows: x_all.at[block, rows])

    def columns(weight, block, size):
        return weight.at[:, pl.ds(pl.multiple_of(block * size, HD), size)]

    def near_pieces(block):
        target = weights.at[links.z, here]
        rows = pl.ds(0, rows_each)
        return [
            (columns(query_w_ref, block, q_cols), target.at[rows, pl.ds(0, q_cols)]),
            (columns(key_w_ref, block, HD), target.at[rows, pl.ds(q_cols, HD)]),
            (columns(value_w_ref, block, HD), target.at[rows, pl.ds(q_cols + HD, HD)]),
            (gain_rows_ref, target.at[pl.ds(rows_each, 16)]),
        ]

    def ff_pieces(block):
        target = ffs_ref.at[links.z, here]
        return [
            (columns(gate_w_ref, block, ff_cols), target.at[:, pl.ds(0, ff_cols)]),
            (columns(up_w_ref, block, ff_cols), target.at[:, pl.ds(ff_cols, ff_cols)]),
        ]

    def turn_out(pieces):
        return {k: [links.send(*piece, k) for piece in pieces(links.along(k))] for k in far}

    def arrived(copies):
        for copy in copies:
            copy.wait_recv()

    own = [links.keep(*piece) for piece in near_pieces(links.z)]
    own_ff = [links.keep(*piece) for piece in ff_pieces(links.z)]
    turned = turn_out(near_pieces)
    placed = [links.send(place_ref, places.at[links.z], k) for k in far]
    turned_ff = turn_out(ff_pieces)
    for copy in own:
        copy.wait()
    near.offer(0, weights.at[links.z, here])
    for copy in own_ff:
        copy.wait()
    far_ff.offer(0, ffs_ref.at[links.z, here])
    own = [links.keep(x_ref, x_all.at[links.z]), links.keep(place_ref, places.at[links.z])]
    local.append(links.keep(out_ref, outs_ref.at[links.z, here]))

    def move_out(k):
        moved.wait_recv()
        block = outs_ref.at[links.along(-k), here]
        onward = links.send(block, block, 1) if k < line - 1 else None
        far_out.offer(k, block)
        return onward

    for k in far:
        arrived(turned[k])
        near.offer(k, weights.at[links.along(-k), here])
    ring.step(0)
    for k in [0] + far:
        near.relay(k, "x" if k < line // 2 else "y")
    for k in far:
        arrived(turned_ff[k])
        far_ff.offer(k, ffs_ref.at[links.along(-k), here])
    ring.step(1)
    for k in [0] + far:
        near.close(k)
    far_ff.relay(0, "x")
    ring.step(2)
    moved = links.send(out_ref, outs_ref.at[links.z, here], 1)
    far_out.offer(0, out_ref)
    for copy in own:
        copy.wait()
    for copy in placed:
        copy.wait_recv()

    lane = lax.broadcasted_iota(jnp.int32, (span_len, HD), 1)
    token = lax.broadcasted_iota(jnp.int32, (span_len, span_len), 0)
    across = lax.broadcasted_iota(jnp.int32, (span_len, span_len), 1)
    for block in range(line):
        row = jnp.broadcast_to(places[block, 0:1], (span_len, span_len))
        column = jnp.sum(jnp.where(token == across, row, 0.0), axis=1, keepdims=True)
        angles = column * freq_ref[0:1]
        rows = slice(block * span_len, (block + 1) * span_len)
        sine = jnp.sin(angles)
        turns[0, rows] = jnp.cos(angles)
        turns[1, rows] = jnp.where(lane < HD // 2, -sine, sine)
    local.append(links.keep(turns, turn_ref))
    near.wait(range(line))
    for index in range(line * 4):
        z, q = divmod(index, 4)
        for which in range(2):
            lanes = slice(which * HD, (which + 1) * HD)
            both = [weights[z, 2 * q + c, rows_each : rows_each + 16, lanes].astype(f32) for c in range(2)]
            gains[which, :, index * HD : (index + 1) * HD] = both[0] + both[1]
    local.append(links.keep(weights, weight_ref))
    local.append(links.keep(gains, gain_ref))
    far_ff.relay(far[0], "x")
    ring.step(3)
    local.append(links.keep(x_all, xs_ref))

    def normalise(index, carry):
        block = index // (span_len // 16)
        rows = pl.ds(pl.multiple_of(lax.rem(index, span_len // 16) * 16, 16), 16)
        values = x_all[block, rows].astype(f32)
        inverse = lax.rsqrt(jnp.mean(values * values, axis=-1, keepdims=True) + epsilon)
        target = pl.ds(pl.multiple_of(index * 16, 16), 16)
        norm[target] = (values * inverse * gains[0]).astype(bf16)
        return carry

    lax.fori_loop(0, group_len // 16, normalise, 0)
    local.append(links.keep(norm, norm_ref))

    def project(low, high):
        step = group_len // 2
        for part in range(2):
            rows = slice(part * step, (part + 1) * step)
            total = None
            for z in range(line):
                weight = weights[z, :, :rows_each, low:high].reshape(8 * rows_each, high - low)
                term = jnp.dot(
                    norm[rows, z * 8 * rows_each : (z + 1) * 8 * rows_each],
                    weight,
                    preferred_element_type=f32,
                )
                total = term if total is None else total + term
            flat[rows, low:high] = total

    def turn(values, rows):
        return values * turns[0, rows] + pltpu.roll(values, HD // 2, 1) * turns[1, rows]

    project(q_cols, q_cols + 2 * HD)
    for block in range(line):
        rows = slice(block * span_len, (block + 1) * span_len)
        kv[0, rows, :HD] = turn(flat[rows, q_cols : q_cols + HD], rows).astype(bf16)
        kv[0, rows, HD:] = flat[rows, q_cols + HD : q_cols + 2 * HD].astype(bf16)
    exchange = links.send(kv.at[0], kv.at[1], "x")
    project(0, q_cols)
    for block in range(line):
        rows = slice(block * span_len, (block + 1) * span_len)
        for head in range(heads):
            lanes = slice(head * HD, (head + 1) * HD)
            query[rows, lanes] = turn(flat[rows, lanes], rows).astype(bf16)
    local.append(links.keep(query, query_ref))
    for k in far[1:]:
        far_ff.relay(k, "x" if k < line // 2 else "y")
    exchange.wait_recv()
    moved = move_out(1)
    local.append(links.keep(kv, kv_ref))

    scale = 1.0 / math.sqrt(HD)
    peak[...] = jnp.zeros_like(peak)

    def attend(head, carry):
        lanes = pl.ds(pl.multiple_of(head * HD, HD), HD)
        for block in range(line):
            rows = slice(block * span_len, (block + 1) * span_len)
            reach = (block + 1) * span_len
            part = query[rows, lanes]
            row = lax.broadcasted_iota(jnp.int32, (span_len, reach), 0) + block * span_len
            column = lax.broadcasted_iota(jnp.int32, (span_len, reach), 1)
            allowed = (column <= row, column < (block + links.x) * span_len)
            scores = []
            for half in range(2):
                score = lax.dot_general(
                    part, kv[half, :reach, :HD], (((1,), (1,)), ((), ())), preferred_element_type=f32
                )
                scores.append(jnp.where(allowed[half], score * scale, -1e30))
            top = jnp.maximum(
                jnp.max(scores[0], axis=-1, keepdims=True), jnp.max(scores[1], axis=-1, keepdims=True)
            )
            total, mixed = None, None
            for half in range(2):
                weight = jnp.exp(scores[half] - top)
                count = jnp.sum(weight, axis=-1, keepdims=True)
                term = jnp.dot(weight.astype(bf16), kv[half, :reach, HD:], preferred_element_type=f32)
                total = count if total is None else total + count
                mixed = term if mixed is None else mixed + term
            att[rows, lanes] = (mixed / total).astype(bf16)
            spot = lax.broadcasted_iota(jnp.int32, (span_len, HD), 1) == head
            peak[rows] = jnp.where(spot, top + jnp.log(total), peak[rows])
        return carry

    lax.fori_loop(0, heads, attend, 0)
    local.append(links.keep(peak, peak_ref))

    def place(block, rows):
        return atts_ref.at[rows, pl.ds(pl.multiple_of(block * q_cols, q_cols), q_cols)]

    att_ring = RingGather(links, att, place)
    local.append(links.keep(att, place(links.z, pl.ds(0, group_len))))
    att_ring.step(0)
    for k in [0] + far:
        far_ff.close(k)
    far_out.relay(0, "x")
    moved = move_out(2)
    far_out.relay(1, "x")
    att_ring.step(1)
    for k in range(3, line):
        moved = move_out(k)
    far_out.relay(2, "y")
    att_ring.step(2)
    for k in range(3, line):
        far_out.relay(k, "y")
    for k in range(line):
        far_out.close(k)
    att_ring.step(3)
    far_out.wait(range(line))
    far_ff.wait(range(line))
    links.finish()
    for copy in local:
        copy.wait()


def add_rows_of(target, values, count):
    def add(index, carry):
        rows = pl.ds(pl.multiple_of(index * 16, 16), 16)
        target[rows] = target[rows] + values[rows]
        return carry

    lax.fori_loop(0, count // 16, add, 0)


class NearSum:
    def __init__(self, links, source, own, from_core, from_first, from_second, first, in_place=False):
        self.links, self.source, self.own, self.first = links, source, own, first
        self.in_place = in_place
        self.from_core, self.from_first, self.from_second = from_core, from_first, from_second

    def start(self):
        links = self.links
        if not self.in_place:
            self.local = links.keep(self.source(links.c), self.own)
        self.copy = links.send(self.source(1 - links.c), self.from_core, "c")

    def add(self, target, values):
        add_rows_of(target, values, target.shape[0])

    def core_done(self):
        links = self.links
        self.copy.wait_recv()
        if not self.in_place:
            self.local.wait()
        for x in range(2):
            for y in range(2):
                self.add(self.own.at[x, y], self.from_core.at[x, y])
        if self.first == "x":
            self.copy = links.send(self.own.at[1 - links.x], self.from_first, "x")
        else:
            self.copy = links.send(self.own.at[:, 1 - links.y], self.from_first, "y")

    def first_done(self):
        links = self.links
        self.copy.wait_recv()
        for other in range(2):
            place = (links.x, other) if self.first == "x" else (other, links.y)
            self.add(self.own.at[place], self.from_first.at[other])
        if self.first == "x":
            self.copy = links.send(self.own.at[links.x, 1 - links.y], self.from_second, "y")
        else:
            self.copy = links.send(self.own.at[1 - links.x, links.y], self.from_second, "x")

    def second_done(self):
        self.copy.wait_recv()
        total = self.own.at[self.links.x, self.links.y]
        self.add(total, self.from_second)
        return total


def sum_space(blocks, rows, columns):
    shape = (rows, columns)
    return [
        pltpu.VMEM((blocks, 2, 2) + shape, jnp.bfloat16),
        pltpu.VMEM((blocks, 2, 2) + shape, jnp.bfloat16),
        pltpu.VMEM((blocks, 2) + shape, jnp.bfloat16),
        pltpu.VMEM((blocks,) + shape, jnp.bfloat16),
    ]


class RingSum:
    def __init__(self, links, parts, total, got, pieces=4):
        self.links, self.parts, self.total, self.got = links, parts, total, got
        self.pieces, self.last = pieces, [None] * pieces
        self.rows = parts.shape[1] // pieces

    def step(self, number):
        links = self.links
        for piece in range(self.pieces):
            way = 1 if piece < self.pieces // 2 else -1
            block = links.along(-way * (number + 1))
            where = pl.ds(piece * self.rows, self.rows)
            if number == 0:
                source = self.parts.at[block, where]
            else:
                self.last[piece].wait_recv()
                total = self.got[number - 1, where].astype(jnp.float32) + self.parts[
                    block, where
                ].astype(jnp.float32)
                if number == links.line - 1:
                    self.total[where] = total
                    continue
                self.parts[block, where] = total.astype(self.parts.dtype)
                source = self.parts.at[block, where]
            self.last[piece] = links.send(source, self.got.at[number, where], way)


def link_call(kernel, collective_id, copies, shapes, arguments, spaces=None, scratch=(), vmem=16):
    any_space = pl.BlockSpec(memory_space=pl.ANY)
    near_space = pl.BlockSpec(memory_space=pltpu.VMEM)
    many = isinstance(shapes, tuple)
    if spaces is None:
        spaces = "h" * (len(arguments) + (len(shapes) if many else 1))
    specs = [near_space if space == "v" else any_space for space in spaces]
    return pl.pallas_call(
        kernel,
        out_shape=shapes,
        in_specs=specs[: len(arguments)],
        out_specs=tuple(specs[len(arguments) :]) if many else specs[-1],
        scratch_shapes=list(scratch)
        + [pltpu.SemaphoreType.DMA((copies,)), pltpu.SemaphoreType.DMA((copies,))],
        compiler_params=pltpu.CompilerParams(
            collective_id=collective_id, has_side_effects=True, vmem_limit_bytes=vmem * 2**20
        ),
    )(*arguments)


def forward_call(freqs, tokens, places, gain_rows, weights, line):
    span_len, width = tokens.shape
    group_len = line * span_len
    rows_each, qkv_cols = weights[0].shape[0], gain_rows.shape[1]
    q_cols = qkv_cols - 2 * HD
    both_cols = 2 * weights[3].shape[1] // line
    f32, bf16 = jnp.float32, jnp.bfloat16
    near = (line, 8, rows_each + 16, qkv_cols)
    outs = (
        ((line, span_len, width), bf16),
        (near, bf16),
        ((2, 16, width), f32),
        ((group_len, width), bf16),
        ((group_len, q_cols), bf16),
        ((2, group_len, 2 * HD), bf16),
        ((group_len, HD), f32),
        ((2, group_len, HD), f32),
        ((group_len, line * q_cols), bf16),
        ((line, 8, rows_each, both_cols), bf16),
        ((line, 8, rows_each, width), bf16),
    )
    return link_call(
        functools.partial(first_kernel, line),
        0,
        208,
        tuple(jax.ShapeDtypeStruct(*out) for out in outs),
        (freqs, tokens, places, gain_rows) + weights,
        "v" + "h" * 20,
        scratch=[
            pltpu.VMEM((line, span_len, width), bf16),
            pltpu.VMEM((line,) + places.shape, f32),
            pltpu.VMEM(near, bf16),
            pltpu.VMEM((2, 16, width), f32),
            pltpu.VMEM((group_len, width), bf16),
            pltpu.VMEM((2, group_len, HD), f32),
            pltpu.VMEM((group_len, qkv_cols), f32),
            pltpu.VMEM((group_len, q_cols), bf16),
            pltpu.VMEM((2, group_len, 2 * HD), bf16),
            pltpu.VMEM((group_len, HD), f32),
            pltpu.VMEM((group_len, q_cols), bf16),
        ],
        vmem=63,
    )


def mlp_kernel(
    line,
    cuts,
    keep_ref,
    gain_ref,
    mix_ref,
    xs_ref,
    atts_ref,
    out_ref,
    ff_ref,
    down_ref,
    middle_ref,
    total_ref,
    mixed_total_ref,
    sum_ref,
    grad_ff_ref,
    ff_half_ref,
    big,
    ff,
    down,
    norm,
    parts,
    mixed,
    gate_up,
    hidden,
    both_grad,
    got,
    mixed_parts,
    mixed_got,
    *scratch,
):
    f32, bf16 = jnp.float32, jnp.bfloat16
    space, (send_sems, recv_sems) = scratch[:-2], scratch[-2:]
    links = Links(send_sems, recv_sems, line)
    links.meet(["x", "y", "c", 1, line - 1])
    far = [1, line - 1] + list(range(2, line - 1))
    span_len, width = mix_ref.shape
    group_len = line * span_len
    ff_cols = hidden.shape[1]
    block_rows = width // line
    rows_each = block_rows // 8
    chunk = 2 * HD
    stay = links.keep(mix_ref, mixed.at[links.z])
    mix_ring = RingGather(links, mix_ref, lambda block, rows: mixed.at[block, rows])
    mix_ring.step(0)
    early = [
        links.keep(out_ref, big),
        links.keep(atts_ref, norm),
        links.keep(xs_ref, parts),
    ]
    late = [links.keep(ff_ref, ff)]
    down_rows = down_ref.shape[0]

    def down_place(block, place):
        low, high = cuts[block]
        return down.at[pl.ds(pl.multiple_of(place * down_rows + low, 16), high - low)]

    near = NearGather(links, down_place)
    for block, (low, high) in enumerate(cuts):
        rows = down_ref.at[pl.ds(low, high - low)]
        late.append(links.keep(rows, down_place(block, links.slot)))
        near.offer(block, rows)
    ring = RingSum(links, parts, total_ref, got)
    mixed_ring = RingSum(links, mixed_parts, mixed_total_ref, mixed_got)
    items = []
    ff_items = []
    for index, k in enumerate(far[:2]):
        block = links.along(k)
        core, first, second = space[:3]
        ff_items.append(
            NearSum(
                links,
                lambda c, block=block: ff.at[block, :, :, c],
                ff.at[block, :, :, links.c],
                core.at[index],
                first.at[index],
                second.at[index],
                "xy"[index % 2],
                True,
            )
        )
    for index, (low, high) in enumerate(cuts):
        rows = pl.ds(low, high - low)
        core, first, second = space[3 * index + 3 : 3 * index + 6]
        items.append(
            NearSum(
                links,
                lambda c, rows=rows: big.at[:, :, c, rows],
                big.at[:, :, links.c, rows],
                core.at[0],
                first.at[0],
                second.at[0],
                "xy"[index % 2],
                True,
            )
        )
    for copy in early:
        copy.wait()

    half = group_len // 2
    out_rows = width // 8
    for part in range(2):
        low = part * half
        for column in range(4):
            lanes = slice(column * width // 4, (column + 1) * width // 4)
            value = None
            for k in range(8):
                term = jnp.dot(
                    norm[low : low + half, k * out_rows : (k + 1) * out_rows],
                    big[k // 4, k // 2 % 2, k % 2, :, lanes],
                    preferred_element_type=f32,
                )
                value = term if value is None else value + term
            gate_up[:half, lanes] = value * keep_ref[0:1, 0:1]

        def normalise(index, carry, low=low):
            block = (low // 16 + index) // (span_len // 16)
            rows = pl.ds(pl.multiple_of(index * 16, 16), 16)
            inside = pl.ds(pl.multiple_of(lax.rem(index, span_len // 16) * 16, 16), 16)
            values = parts[block, inside].astype(f32) + gate_up[rows, :width]
            gate_up[rows, :width] = values
            inverse = lax.rsqrt(jnp.mean(values * values, axis=-1, keepdims=True) + epsilon)
            target = pl.ds(pl.multiple_of(low + index * 16, 16), 16)
            norm[target] = (values * inverse * gain_ref[1]).astype(bf16)
            return carry

        lax.fori_loop(0, half // 16, normalise, 0)

        @pl.when(links.z // (line // 2) == part)
        def _():
            where = pl.multiple_of(lax.rem(links.z, line // 2) * span_len, span_len)
            middle_ref[...] = gate_up[pl.ds(where, span_len), :width]
        if part == 0:
            mix_ring.step(1)

    for block in range(2):
        near.relay(block, "xy"[block])
    for copy in late:
        copy.wait()

    def columns_of(lanes, size):
        return ff[:, :, :, :, :, lanes].reshape(width, size)

    def forward(low, size):
        gates, ups = pl.ds(low, size), pl.ds(low + ff_cols, size)
        gate = jnp.dot(norm[...], columns_of(gates, size), preferred_element_type=f32)
        gate_up[:, gates] = gate
        swish = gate * jax.nn.sigmoid(gate)
        up = jnp.dot(norm[...], columns_of(ups, size), preferred_element_type=f32)
        gate_up[:, ups] = up
        hidden[:, gates] = (swish * up).astype(bf16)

    def backward(low, size):
        gates, ups = pl.ds(low, size), pl.ds(low + ff_cols, size)
        grad = lax.dot_general(
            mixed[...].reshape(group_len, width),
            down[gates],
            (((1,), (1,)), ((), ())),
            preferred_element_type=f32,
        )
        gate, up = gate_up[:, gates], gate_up[:, ups]
        sigmoid = jax.nn.sigmoid(gate)
        both_grad[:, gates] = (grad * up * sigmoid * (1.0 + gate * (1.0 - sigmoid))).astype(bf16)
        both_grad[:, ups] = (grad * (gate * sigmoid)).astype(bf16)

    def over_chunks(work, extent):
        def one(index, carry):
            work(pl.multiple_of(index * chunk, chunk), chunk)
            return carry

        lax.fori_loop(0, extent // chunk, one, 0)
        if extent % chunk:
            work(extent // chunk * chunk, extent % chunk)

    over_chunks(forward, ff_cols)
    mix_ring.step(2)
    for block in range(2):
        near.close(block)
    near.wait(range(2))

    def mixed_part(low, size):
        lanes = pl.ds(low, size)
        value = jnp.dot(hidden[...], down[:, lanes], preferred_element_type=f32).astype(bf16)
        mixed_parts[:, :, lanes] = value.reshape(line, span_len, size)

    over_chunks(mixed_part, width)
    mixed_ring.step(0)
    stay.wait()
    mix_ring.step(3)
    hidden_rows = hidden[...].T

    def down_part(low, size):
        lanes = pl.ds(low, size)
        value = jnp.dot(
            hidden_rows,
            mixed[:, :, lanes].reshape(group_len, size),
            preferred_element_type=f32,
        ).astype(bf16)
        big[:, :, :, : cuts[-1][1], lanes] = value.reshape(2, 2, 2, cuts[-1][1], size)

    over_chunks(down_part, width)
    for item in items:
        item.start()
    over_chunks(backward, ff_cols)
    mixed_ring.step(1)
    for item in items:
        item.core_done()

    def norm_part(index, carry):
        size = 4 * rows_each
        weight = ff[index // 2, lax.rem(index, 2)].reshape(size, 2 * ff_cols)
        value = lax.dot_general(
            both_grad[...], weight, (((1,), (1,)), ((), ())), preferred_element_type=f32
        ).astype(bf16)
        lanes = pl.ds(pl.multiple_of(index * size, size), size)
        parts[:, :, lanes] = value.reshape(line, span_len, size)
        return carry

    lax.fori_loop(0, 2 * line, norm_part, 0)
    ring.step(0)

    def ff_block(block):
        norm_rows = norm[:, pl.ds(pl.multiple_of(block * block_rows, block_rows), block_rows)].T

        def ff_part(low, size):
            lanes = pl.ds(low, size)
            value = jnp.dot(norm_rows, both_grad[:, lanes], preferred_element_type=f32)
            ff[block, :, :, :, :, lanes] = value.astype(bf16).reshape(2, 2, 2, rows_each, size)

        over_chunks(ff_part, 2 * ff_cols)

    for item, k in zip(ff_items, far):
        ff_block(links.along(k))
        item.start()
    for item in items:
        item.first_done()
    ring.step(1)
    for item in ff_items:
        item.core_done()
    mixed_ring.step(2)
    sent = []
    for k in far[2:] + [0]:
        block = links.along(k)
        ff_block(block)
        sent.append(links.keep(ff.at[block], grad_ff_ref.at[block]))
    for item, (low, high) in zip(items, cuts):
        sum_ref[low:high] = item.second_done()[...]
    ring.step(2)
    for item in ff_items:
        item.first_done()
    mixed_ring.step(3)
    ring.step(3)
    for index, item in enumerate(ff_items):
        sent.append(links.keep(item.second_done(), ff_half_ref.at[index]))
    links.finish()
    for copy in sent:
        copy.wait()


def mlp_call(keep, gains, mixed, x_blocks, attended, out_w, ff_w, w_down, line):
    f32, bf16 = jnp.float32, jnp.bfloat16
    span_len, width = mixed.shape
    group_len = line * span_len
    rows, both_cols, rows_each = w_down.shape[0], ff_w.shape[3], ff_w.shape[2]
    ff_rows = 8 * rows
    ff_w = ff_w.reshape(line, 2, 2, 2, rows_each, both_cols)
    half = (rows // 2 + 15) // 16 * 16
    cuts = ((0, half), (half, rows))
    blocks = (line, span_len, width)
    token = jax.ShapeDtypeStruct((span_len, width), f32)
    return link_call(
        functools.partial(mlp_kernel, line, cuts),
        2,
        112,
        (
            token,
            token,
            token,
            jax.ShapeDtypeStruct((rows, width), bf16),
            jax.ShapeDtypeStruct(ff_w.shape, bf16),
            jax.ShapeDtypeStruct((2, rows_each, both_cols), bf16),
        ),
        (keep, gains, mixed, x_blocks, attended, out_w.reshape(2, 2, 2, width // 8, width), ff_w, w_down),
        "vvhhhhhh" + "vvvvhh",
        [
            pltpu.VMEM((2, 2, 2, width // 8, width), bf16),
            pltpu.VMEM(ff_w.shape, bf16),
            pltpu.VMEM((ff_rows, width), bf16),
            pltpu.VMEM((group_len, width), bf16),
            pltpu.VMEM(blocks, bf16),
            pltpu.VMEM(blocks, bf16),
            pltpu.VMEM((group_len, both_cols), f32),
            pltpu.VMEM((group_len, ff_rows), bf16),
            pltpu.VMEM((group_len, both_cols), bf16),
            pltpu.VMEM((line - 1, span_len, width), bf16),
            pltpu.VMEM(blocks, bf16),
            pltpu.VMEM((line - 1, span_len, width), bf16),
        ]
        + sum_space(2, rows_each, both_cols)[1:]
        + sum((sum_space(1, high - low, width)[1:] for low, high in cuts), []),
        vmem=63,
    )


def backward_kernel(
    line,
    up_ref,
    middle_ref,
    norm_grad_ref,
    keep_ref,
    gain_ref,
    query_ref,
    kv_ref,
    peak_ref,
    turn_ref,
    out_ref,
    atts_ref,
    weight_ref,
    norm_ref,
    ff_ref,
    ff_half_ref,
    middle_grad_ref,
    total_ref,
    ffs_ref,
    outs_ref,
    qkvs_ref,
    big,
    slim,
    norm,
    own_rows,
    own_columns,
    branch,
    own_grad,
    att_grad,
    query_back,
    kv_back,
    kv_out,
    kv_in,
    flat,
    parts,
    query,
    kv,
    peak,
    turns,
    *scratch,
):
    f32, bf16 = jnp.float32, jnp.bfloat16
    send_sems, recv_sems = scratch[-2:]
    got, sums = scratch[0], scratch[1:-2]
    links = Links(send_sems, recv_sems, line)
    far = [1, line - 1] + list(range(2, line - 1))
    order = far + [0]
    links.meet(["x", "y", "c"] + far)
    span_len, width = up_ref.shape
    group_len = line * span_len
    q_cols = query.shape[1]
    heads = q_cols // HD
    rows_z = width // line
    rows_each = rows_z // 8
    scale = 1.0 / math.sqrt(HD)

    def lanes_of(block):
        return pl.ds(pl.multiple_of(block * q_cols, q_cols), q_cols)

    here = pl.ds(pl.multiple_of(links.z * span_len, span_len), span_len)
    loads = [
        links.keep(out_ref, big),
        links.keep(atts_ref.at[here], own_rows),
        links.keep(atts_ref.at[:, lanes_of(links.z)], own_columns),
        links.keep(query_ref, query),
        links.keep(kv_ref, kv),
        links.keep(peak_ref, peak),
        links.keep(turn_ref, turns),
        links.keep(norm_ref, norm),
        links.keep(weight_ref.at[:, :, :, :, pl.ds(0, slim.shape[4])], slim),
    ]
    ring = RingSum(links, parts, total_ref, got)

    def items_of(source, space, in_place, order=order):
        items = []
        for index, k in enumerate(order):
            block = links.along(k)
            own = source.at[block, :, :, links.c] if in_place else space[0].at[index]
            core, first, second = space[-3:]
            items.append(
                NearSum(
                    links,
                    lambda c, block=block: source.at[block, :, :, c],
                    own,
                    core.at[index],
                    first.at[index],
                    second.at[index],
                    "xy"[index % 2],
                    in_place,
                )
            )
        return items

    ff_order = order[2:]
    ff_items = items_of(ff_ref, sums[:4], False, ff_order)
    out_items = items_of(big, sums[4:7], True)
    qkv_items = items_of(slim, sums[7:], True)
    local, arrived = [], []
    ff_cols = ff_ref.shape[5] // 2
    ff_pieces = ((0, ff_cols), (ff_cols, ff_cols))
    qkv_pieces = ((0, q_cols), (q_cols, HD), (q_cols + HD, HD))

    def deliver(total, target, k, pieces):
        for low, size in pieces:
            if pieces == out_pieces:
                place = target.at[links.z]
            else:
                lanes = pl.multiple_of(line * low + links.z * size, HD)
                place = target.at[:, pl.ds(lanes, size)]
            part = total.at[:, pl.ds(low, size)]
            if k == 0:
                local.append(links.keep(part, place))
            else:
                arrived.append(links.send(part, place, k))

    out_pieces = ((0, width),)
    for index, k in enumerate(order[:2]):
        deliver(ff_half_ref.at[index], ffs_ref, k, ff_pieces)

    def turn(items, target, low, high, pieces, order=order):
        for item, k in list(zip(items, order))[low:high]:
            deliver(item.second_done(), target, k, pieces)

    def core_done(items, low, high):
        for item in items[low:high]:
            item.core_done()

    def first_done(items, low, high):
        for item in items[low:high]:
            item.first_done()

    half = line // 2
    for item in ff_items:
        item.start()

    def d_middle(index, carry):
        rows = pl.ds(pl.multiple_of(index * 16, 16), 16)
        middle = middle_ref[rows]
        inverse = lax.rsqrt(jnp.mean(middle * middle, axis=-1, keepdims=True) + epsilon)
        scaled = gain_ref[1] * norm_grad_ref[rows]
        grad = (
            up_ref[rows]
            + inverse * scaled
            - middle
            * (inverse * inverse * inverse)
            * jnp.mean(scaled * middle, axis=-1, keepdims=True)
        )
        middle_grad_ref[rows] = grad
        branch[rows] = (grad * keep_ref[0:1, 0:1]).astype(bf16)
        return carry

    lax.fori_loop(0, span_len // 16, d_middle, 0)
    for copy in loads:
        copy.wait()
    for z in range(line):
        weight = big[z].reshape(rows_z, width)
        own_grad[:, z * rows_z : (z + 1) * rows_z] = lax.dot_general(
            branch[...], weight, (((1,), (1,)), ((), ())), preferred_element_type=f32
        ).astype(bf16)
    turned = [links.send(own_grad.at[:, lanes_of(links.along(k))], att_grad.at[here], k) for k in far]
    stayed = links.keep(own_grad.at[:, lanes_of(links.z)], att_grad.at[here])
    core_done(ff_items, 0, line)
    for z in range(line):
        for part in range(4):
            columns = slice(part * width // 4, (part + 1) * width // 4)
            grad = lax.dot_general(
                own_rows[:, z * rows_z : (z + 1) * rows_z],
                branch[:, columns],
                (((0,), (0,)), ((), ())),
                preferred_element_type=f32,
            )
            big[z, :, :, :, :, columns] = grad.astype(bf16).reshape(2, 2, 2, rows_each, width // 4)
    for item in out_items:
        item.start()
    kv_back[...] = jnp.zeros_like(kv_back)
    for copy in turned:
        copy.wait_recv()
    stayed.wait()

    def attend_back(head, carry):
        lanes = pl.ds(pl.multiple_of(head * HD, HD), HD)
        for block in range(line):
            rows = slice(block * span_len, (block + 1) * span_len)
            reach = (block + 1) * span_len
            part, grad = query[rows, lanes], att_grad[rows, lanes]
            row = lax.broadcasted_iota(jnp.int32, (span_len, reach), 0) + block * span_len
            column = lax.broadcasted_iota(jnp.int32, (span_len, reach), 1)
            allowed = (column <= row, column < (block + links.x) * span_len)
            spot = lax.broadcasted_iota(jnp.int32, (span_len, HD), 1) == head
            top = jnp.sum(jnp.where(spot, peak[rows], 0.0), axis=-1, keepdims=True)
            delta = jnp.sum(
                grad.astype(f32) * own_columns[rows, lanes].astype(f32), axis=-1, keepdims=True
            )
            total = None
            for side in range(2):
                keys, values = kv[side, :reach, :HD], kv[side, :reach, HD:]
                score = lax.dot_general(
                    part, keys, (((1,), (1,)), ((), ())), preferred_element_type=f32
                )
                weight = jnp.where(allowed[side], jnp.exp(score * scale - top), 0.0)
                weight_grad = lax.dot_general(
                    grad, values, (((1,), (1,)), ((), ())), preferred_element_type=f32
                )
                score_grad = (weight * (weight_grad - delta)).astype(bf16)
                term = jnp.dot(score_grad, keys, preferred_element_type=f32)
                total = term if total is None else total + term
                kv_back[side, :reach, :HD] += lax.dot_general(
                    score_grad, part, (((0,), (0,)), ((), ())), preferred_element_type=f32
                )
                kv_back[side, :reach, HD:] += lax.dot_general(
                    weight.astype(bf16), grad, (((0,), (0,)), ((), ())), preferred_element_type=f32
                )
            query_back[rows, lanes] = total * scale
        return carry

    lax.fori_loop(0, heads, attend_back, 0)
    kv_out[:, :HD] = (kv_back[1, :, :HD] * scale).astype(bf16)
    kv_out[:, HD:] = kv_back[1, :, HD:].astype(bf16)
    exchange = links.send(kv_out, kv_in, "x")

    def turn_back(values, rows):
        return values * turns[0, rows] - pltpu.roll(values, HD // 2, 1) * turns[1, rows]

    for block in range(line):
        rows = slice(block * span_len, (block + 1) * span_len)
        for head in range(heads):
            lanes = slice(head * HD, (head + 1) * HD)
            flat[rows, lanes] = turn_back(query_back[rows, lanes], rows).astype(bf16)
    first_done(ff_items, 0, line)
    exchange.wait_recv()
    for block in range(line):
        rows = slice(block * span_len, (block + 1) * span_len)
        key_grad = kv_back[0, rows, :HD] * scale + kv_in[rows, :HD].astype(f32)
        flat[rows, q_cols : q_cols + HD] = turn_back(key_grad, rows).astype(bf16)
        value_grad = kv_back[0, rows, HD:] + kv_in[rows, HD:].astype(f32)
        flat[rows, q_cols + HD :] = value_grad.astype(bf16)
    for z in range(line):
        weight = slim[z].reshape(rows_z, flat.shape[1])
        part = lax.dot_general(
            flat[...], weight, (((1,), (1,)), ((), ())), preferred_element_type=f32
        ).astype(bf16)
        for block in range(line):
            parts[block, :, z * rows_z : (z + 1) * rows_z] = part[
                block * span_len : (block + 1) * span_len
            ]
    ring.step(0)
    for z in range(line):
        grad = lax.dot_general(
            norm[:, z * rows_z : (z + 1) * rows_z],
            flat[...],
            (((0,), (0,)), ((), ())),
            preferred_element_type=f32,
        )
        slim[z] = grad.astype(bf16).reshape(2, 2, 2, rows_each, flat.shape[1])
    for item in qkv_items:
        item.start()
    core_done(out_items, 0, half)
    turn(ff_items, ffs_ref, 0, line, ff_pieces, ff_order)
    ring.step(1)
    core_done(out_items, half, line)
    first_done(out_items, 0, half)
    ring.step(2)
    core_done(qkv_items, 0, line)
    first_done(out_items, half, line)
    turn(out_items, outs_ref, 0, half, out_pieces)
    ring.step(3)
    first_done(qkv_items, 0, half)
    turn(out_items, outs_ref, half, line, out_pieces)
    first_done(qkv_items, half, line)
    turn(qkv_items, qkvs_ref, 0, line, qkv_pieces)
    for copy in arrived:
        copy.wait_recv()
    links.finish()
    for copy in local:
        copy.wait()


def backward_call(small, saved, out_w, attended, weights, norm, grad_ff, ff_half, line):
    f32, bf16 = jnp.float32, jnp.bfloat16
    span_len, width = small[0].shape
    group_len = line * span_len
    query = saved[0]
    q_cols, rows_each, qkv_cols = query.shape[1], width // line // 8, weights.shape[3]
    weights = weights.reshape(line, 2, 2, 2, -1, qkv_cols)
    wide = (line, 2, 2, 2, rows_each, width)
    slim = (line, 2, 2, 2, rows_each, qkv_cols)
    out_space = sum_space(line, rows_each, width)[1:]
    qkv_space = sum_space(line, rows_each, qkv_cols)[1:]
    token = jax.ShapeDtypeStruct((span_len, width), f32)
    return link_call(
        functools.partial(backward_kernel, line),
        4,
        160,
        (token, token)
        + (
            jax.ShapeDtypeStruct((rows_each, line * grad_ff.shape[5]), bf16),
            jax.ShapeDtypeStruct((line, rows_each, width), bf16),
            jax.ShapeDtypeStruct((rows_each, line * qkv_cols), bf16),
        ),
        small + saved + (out_w.reshape(wide), attended, weights, norm, grad_ff, ff_half),
        "v" * 5 + "h" * 10 + "vvhhh",
        [
            pltpu.VMEM(wide, bf16),
            pltpu.VMEM(slim, bf16),
            pltpu.VMEM((group_len, width), bf16),
            pltpu.VMEM((span_len, width), bf16),
            pltpu.VMEM((group_len, q_cols), bf16),
            pltpu.VMEM((span_len, width), bf16),
            pltpu.VMEM((span_len, width), bf16),
            pltpu.VMEM((group_len, q_cols), bf16),
            pltpu.VMEM((group_len, q_cols), f32),
            pltpu.VMEM((2, group_len, 2 * HD), f32),
            pltpu.VMEM((group_len, 2 * HD), bf16),
            pltpu.VMEM((group_len, 2 * HD), bf16),
            pltpu.VMEM((group_len, qkv_cols), bf16),
            pltpu.VMEM((line, span_len, width), bf16),
        ]
        + [pltpu.VMEM(value.shape, value.dtype) for value in saved]
        + [pltpu.VMEM((line - 1, span_len, width), bf16)]
        + sum_space(line - 2, rows_each, grad_ff.shape[5])
        + out_space
        + qkv_space,
        vmem=63,
    )


def general_body(
    tokens,
    attn_gain,
    w_query,
    w_key,
    w_value,
    w_out,
    mlp_gain,
    w_gate,
    w_up,
    w_down,
    keep_mask,
    group_ids,
    positions,
    exit_scale,
    out_grad,
):
    seq_count, span_len, model_width = tokens.shape
    kv_heads = KVH
    head_dim = HD
    head_count = HEADS
    group_size = head_count // kv_heads
    row_count = seq_count * span_len
    stripe = group_size * span_len
    wide_count = lax.axis_size("wide")
    wide_place = lax.axis_index("wide")
    full_len = span_len * wide_count
    score_scale = 1.0 / math.sqrt(head_dim)
    gain_one, query_w, key_w, value_w, out_w = (
        lax.all_gather(attn_gain, ("wide", "narrow"), axis=0, tiled=True),
        lax.all_gather(w_query, ("wide", "narrow"), axis=0, tiled=True),
        lax.all_gather(w_key, ("wide", "narrow"), axis=0, tiled=True),
        lax.all_gather(w_value, ("wide", "narrow"), axis=0, tiled=True),
        lax.all_gather(w_out, ("wide", "narrow"), axis=0, tiled=True),
    )
    inputs = tokens.astype(jnp.float32).reshape(row_count, model_width)
    token_pos = positions.reshape(row_count)
    keep_rows = jnp.repeat(keep_mask.astype(jnp.float32), span_len)[:, None]
    inverse_one = lax.rsqrt(jnp.mean(inputs * inputs, axis=-1, keepdims=True) + epsilon)
    first_norm = (inputs * inverse_one * gain_one.astype(jnp.float32)).astype(jnp.bfloat16)
    query_pre = jnp.dot(first_norm, query_w, preferred_element_type=jnp.float32).reshape(
        row_count, head_count, head_dim
    )
    key_pre = jnp.dot(first_norm, key_w, preferred_element_type=jnp.float32).reshape(
        row_count, kv_heads, head_dim
    )
    query_rows = rotate(query_pre, token_pos, 1.0).astype(jnp.bfloat16)
    key_heads = (
        rotate(key_pre, token_pos, 1.0)
        .astype(jnp.bfloat16)
        .reshape(seq_count, span_len, kv_heads * head_dim)
    )
    value_heads = (
        jnp.dot(first_norm, value_w, preferred_element_type=jnp.float32)
        .astype(jnp.bfloat16)
        .reshape(seq_count, span_len, kv_heads * head_dim)
    )
    queries = (
        query_rows.reshape(seq_count, span_len, kv_heads, group_size, head_dim)
        .transpose(0, 2, 3, 1, 4)
        .reshape(seq_count, kv_heads, stripe, head_dim)
    )
    query_index = wide_place * span_len + jnp.arange(stripe, dtype=jnp.int32) % span_len
    last_query = wide_place * span_len + span_len - 1

    def block_scores(key_block, key_first):
        scores = (
            jnp.einsum("skrd,sjkd->skrj", queries, key_block, preferred_element_type=jnp.float32)
            * score_scale
        )
        key_index = key_first + jnp.arange(key_block.shape[1], dtype=jnp.int32)
        allowed = key_index[None, :] <= query_index[:, None]
        return (scores, allowed)

    start_forward = (
        jnp.full((seq_count, kv_heads, stripe), -1e30, jnp.float32),
        jnp.zeros((seq_count, kv_heads, stripe), jnp.float32),
        jnp.zeros((seq_count, kv_heads, stripe, head_dim), jnp.float32),
    )
    running = start_forward
    pieces = (
        lax.all_gather(key_heads, "wide", axis=1, tiled=True),
        lax.all_gather(value_heads, "wide", axis=1, tiled=True),
    )
    key_blocks = split_blocks(pieces[0], seq_count, kv_heads, head_dim)
    value_blocks = split_blocks(pieces[1], seq_count, kv_heads, head_dim)
    block_len = key_blocks.shape[2]

    def advance(carried, block_item):
        key_block, value_block, block_index = block_item
        key_first = block_index * block_len

        def compute_block(current):
            run_max, run_sum, run_acc = current
            scores, allowed = block_scores(key_block, key_first)
            scores = jnp.where(allowed, scores, -1e30)
            new_max = jnp.maximum(run_max, jnp.max(scores, axis=-1))
            factor = jnp.exp(run_max - new_max)
            weights = jnp.where(allowed, jnp.exp(scores - new_max[..., None]), 0.0)
            new_sum = run_sum * factor + jnp.sum(weights, axis=-1)
            new_acc = run_acc * factor[..., None] + jnp.einsum(
                "skrj,sjkd->skrd",
                weights.astype(jnp.bfloat16),
                value_block,
                preferred_element_type=jnp.float32,
            )
            return (new_max, new_sum, new_acc)

        return (lax.cond(key_first <= last_query, compute_block, unchanged, carried), None)

    running, _ = lax.scan(
        advance,
        running,
        (key_blocks, value_blocks, jnp.arange(key_blocks.shape[0], dtype=jnp.int32)),
    )
    run_max, run_sum, run_acc = running
    attended = run_acc / run_sum[..., None]
    log_total = run_max + jnp.log(run_sum)
    attended_rows = (
        attended.reshape(seq_count, kv_heads, group_size, span_len, head_dim)
        .transpose(0, 3, 1, 2, 4)
        .reshape(row_count, head_count * head_dim)
        .astype(jnp.bfloat16)
    )
    middle = inputs + keep_rows * jnp.dot(attended_rows, out_w, preferred_element_type=jnp.float32)
    gain_two, gate_w, up_w, down_w = (
        lax.all_gather(mlp_gain, ("wide", "narrow"), axis=0, tiled=True),
        lax.all_gather(w_gate, ("wide", "narrow"), axis=0, tiled=True),
        lax.all_gather(w_up, ("wide", "narrow"), axis=0, tiled=True),
        lax.all_gather(w_down, ("wide", "narrow"), axis=0, tiled=True),
    )
    inverse_two = lax.rsqrt(jnp.mean(middle * middle, axis=-1, keepdims=True) + epsilon)
    second_norm = (middle * inverse_two * gain_two.astype(jnp.float32)).astype(jnp.bfloat16)
    gate_value = jnp.dot(second_norm, gate_w, preferred_element_type=jnp.float32)
    up_value = jnp.dot(second_norm, up_w, preferred_element_type=jnp.float32)
    gate_sigmoid = jax.nn.sigmoid(gate_value)
    swish_value = gate_value * gate_sigmoid
    hidden = (swish_value * up_value).astype(jnp.bfloat16)
    output = (
        middle + keep_rows * jnp.dot(hidden, down_w, preferred_element_type=jnp.float32)
    ).astype(jnp.bfloat16)
    group_match = (
        group_ids.reshape(row_count)[:, None]
        == jnp.arange(exit_scale.shape[0], dtype=jnp.int32)[None, :]
    )
    token_scale = jnp.sum(jnp.where(group_match, exit_scale[None, :], 0.0), axis=1, keepdims=True)
    upstream = out_grad.astype(jnp.float32).reshape(row_count, model_width) * token_scale
    gain_two, gate_w, up_w, down_w = (
        lax.all_gather(mlp_gain, ("wide", "narrow"), axis=0, tiled=True),
        lax.all_gather(w_gate, ("wide", "narrow"), axis=0, tiled=True),
        lax.all_gather(w_up, ("wide", "narrow"), axis=0, tiled=True),
        lax.all_gather(w_down, ("wide", "narrow"), axis=0, tiled=True),
    )
    mixed_grad = (keep_rows * upstream).astype(jnp.bfloat16)
    grad_down = over_rows(hidden, mixed_grad)
    hidden_grad = against(mixed_grad, down_w)
    gate_grad = (
        hidden_grad * up_value * gate_sigmoid * (1.0 + gate_value * (1.0 - gate_sigmoid))
    ).astype(jnp.bfloat16)
    up_grad = (hidden_grad * swish_value).astype(jnp.bfloat16)
    grad_gate = over_rows(second_norm, gate_grad)
    grad_up = over_rows(second_norm, up_grad)
    norm_grad = against(gate_grad, gate_w) + against(up_grad, up_w)
    grad_gain_two = jnp.sum(norm_grad * middle * inverse_two, axis=0)
    scaled_two = gain_two.astype(jnp.float32) * norm_grad
    middle_grad = (
        upstream
        + inverse_two * scaled_two
        - middle
        * (inverse_two * inverse_two * inverse_two)
        * jnp.mean(scaled_two * middle, axis=-1, keepdims=True)
    )
    gain_two_share, gate_share, up_share, down_share = (
        lax.psum_scatter(grad_gain_two, ("wide", "narrow"), scatter_dimension=0, tiled=True),
        lax.psum_scatter(grad_gate, ("wide", "narrow"), scatter_dimension=0, tiled=True),
        lax.psum_scatter(grad_up, ("wide", "narrow"), scatter_dimension=0, tiled=True),
        lax.psum_scatter(grad_down, ("wide", "narrow"), scatter_dimension=0, tiled=True),
    )
    gain_one, query_w, key_w, value_w, out_w = (
        lax.all_gather(attn_gain, ("wide", "narrow"), axis=0, tiled=True),
        lax.all_gather(w_query, ("wide", "narrow"), axis=0, tiled=True),
        lax.all_gather(w_key, ("wide", "narrow"), axis=0, tiled=True),
        lax.all_gather(w_value, ("wide", "narrow"), axis=0, tiled=True),
        lax.all_gather(w_out, ("wide", "narrow"), axis=0, tiled=True),
    )
    branch_grad = (keep_rows * middle_grad).astype(jnp.bfloat16)
    grad_out = over_rows(attended_rows, branch_grad)
    attended_grad = against(branch_grad, out_w).astype(jnp.bfloat16)
    grouped_grad = (
        attended_grad.reshape(seq_count, span_len, kv_heads, group_size, head_dim)
        .transpose(0, 2, 3, 1, 4)
        .reshape(seq_count, kv_heads, stripe, head_dim)
    )
    row_delta = jnp.sum(grouped_grad.astype(jnp.float32) * attended, axis=-1)
    start_backward = (
        jnp.zeros((seq_count, kv_heads, stripe, head_dim), jnp.float32),
        jnp.zeros((seq_count, full_len, kv_heads * head_dim), jnp.float32),
        jnp.zeros((seq_count, full_len, kv_heads * head_dim), jnp.float32),
    )
    running = start_backward
    pieces = (
        lax.all_gather(key_heads, "wide", axis=1, tiled=True),
        lax.all_gather(value_heads, "wide", axis=1, tiled=True),
    )
    key_blocks = split_blocks(pieces[0], seq_count, kv_heads, head_dim)
    value_blocks = split_blocks(pieces[1], seq_count, kv_heads, head_dim)
    fold_block_len = key_blocks.shape[2]

    def advance(carried, block_item):
        key_block, value_block, block_index = block_item
        key_first = block_index * fold_block_len

        def compute_block(current):
            query_acc, key_acc, value_acc = current
            scores, allowed = block_scores(key_block, key_first)
            probabilities = jnp.where(allowed, jnp.exp(scores - log_total[..., None]), 0.0)
            value_part = jnp.einsum(
                "skrj,skrd->sjkd",
                probabilities.astype(jnp.bfloat16),
                grouped_grad,
                preferred_element_type=jnp.float32,
            )
            prob_grad = jnp.einsum(
                "skrd,sjkd->skrj", grouped_grad, value_block, preferred_element_type=jnp.float32
            )
            score_grad = (probabilities * (prob_grad - row_delta[..., None])).astype(jnp.bfloat16)
            query_acc = (
                query_acc
                + jnp.einsum(
                    "skrj,sjkd->skrd", score_grad, key_block, preferred_element_type=jnp.float32
                )
                * score_scale
            )
            key_part = (
                jnp.einsum(
                    "skrj,skrd->sjkd", score_grad, queries, preferred_element_type=jnp.float32
                )
                * score_scale
            )
            key_acc = add_rows(
                key_acc, key_part.reshape(seq_count, fold_block_len, kv_heads * head_dim), key_first
            )
            value_acc = add_rows(
                value_acc,
                value_part.reshape(seq_count, fold_block_len, kv_heads * head_dim),
                key_first,
            )
            return (query_acc, key_acc, value_acc)

        return (lax.cond(key_first <= last_query, compute_block, unchanged, carried), None)

    running, _ = lax.scan(
        advance,
        running,
        (key_blocks, value_blocks, jnp.arange(key_blocks.shape[0], dtype=jnp.int32)),
    )
    query_acc, key_acc, value_acc = running
    key_sum, value_sum = (
        lax.psum_scatter(
            key_acc.astype(jnp.bfloat16), "wide", scatter_dimension=1, tiled=True
        ).astype(jnp.float32),
        lax.psum_scatter(
            value_acc.astype(jnp.bfloat16), "wide", scatter_dimension=1, tiled=True
        ).astype(jnp.float32),
    )
    query_back = (
        query_acc.reshape(seq_count, kv_heads, group_size, span_len, head_dim)
        .transpose(0, 3, 1, 2, 4)
        .reshape(row_count, head_count, head_dim)
    )
    query_grad = (
        rotate(query_back, token_pos, -1.0)
        .reshape(row_count, head_count * head_dim)
        .astype(jnp.bfloat16)
    )
    key_grad = (
        rotate(key_sum.reshape(row_count, kv_heads, head_dim), token_pos, -1.0)
        .reshape(row_count, kv_heads * head_dim)
        .astype(jnp.bfloat16)
    )
    value_grad = value_sum.reshape(row_count, kv_heads * head_dim).astype(jnp.bfloat16)
    grad_query = over_rows(first_norm, query_grad)
    grad_key = over_rows(first_norm, key_grad)
    grad_value = over_rows(first_norm, value_grad)
    input_norm_grad = (
        against(query_grad, query_w) + against(key_grad, key_w) + against(value_grad, value_w)
    )
    grad_gain_one = jnp.sum(input_norm_grad * inputs * inverse_one, axis=0)
    scaled_one = gain_one.astype(jnp.float32) * input_norm_grad
    input_grad = (
        middle_grad
        + inverse_one * scaled_one
        - inputs
        * (inverse_one * inverse_one * inverse_one)
        * jnp.mean(scaled_one * inputs, axis=-1, keepdims=True)
    )
    gain_one_share, query_share, key_share, value_share, out_share = (
        lax.psum_scatter(grad_gain_one, ("wide", "narrow"), scatter_dimension=0, tiled=True),
        lax.psum_scatter(grad_query, ("wide", "narrow"), scatter_dimension=0, tiled=True),
        lax.psum_scatter(grad_key, ("wide", "narrow"), scatter_dimension=0, tiled=True),
        lax.psum_scatter(grad_value, ("wide", "narrow"), scatter_dimension=0, tiled=True),
        lax.psum_scatter(grad_out, ("wide", "narrow"), scatter_dimension=0, tiled=True),
    )
    return (
        output.reshape(seq_count, span_len, model_width),
        input_grad.astype(jnp.bfloat16).reshape(seq_count, span_len, model_width),
        gain_one_share,
        query_share,
        key_share,
        value_share,
        out_share,
        gain_two_share,
        gate_share,
        up_share,
        down_share,
    )


def line_body(
    tokens,
    attn_gain,
    w_query,
    w_key,
    w_value,
    w_out,
    mlp_gain,
    w_gate,
    w_up,
    w_down,
    keep_mask,
    group_ids,
    positions,
    exit_scale,
    out_grad,
):
    f32 = jnp.float32
    bf16 = jnp.bfloat16
    _, span_len, model_width = tokens.shape
    line = lax.axis_size("z")
    rows_each = w_query.shape[0]
    q_cols = HEADS // line * HD

    own_x = tokens[0].astype(f32)
    keep = keep_mask[0].astype(f32)
    group_match = group_ids[0][:, None] == jnp.arange(exit_scale.shape[0], dtype=jnp.int32)[None, :]
    token_scale = jnp.sum(jnp.where(group_match, exit_scale[None, :], 0.0), axis=1, keepdims=True)
    upstream = out_grad[0].astype(f32) * token_scale

    core = lax.axis_index("c")
    gain_row = jnp.zeros((q_cols + 2 * HD,), bf16)
    gain_row = lax.dynamic_update_slice_in_dim(gain_row, attn_gain, core * rows_each, 0)
    gain_row = lax.dynamic_update_slice_in_dim(gain_row, mlp_gain, HD + core * rows_each, 0)
    gain_rows = jnp.broadcast_to(gain_row, (16, gain_row.shape[0]))
    freqs = 10000.0 ** (-2.0 * jnp.arange(HD // 2, dtype=f32) / HD)
    freqs = jnp.broadcast_to(jnp.concatenate([freqs, freqs])[None], (8, HD))
    places = jnp.broadcast_to(positions[0].astype(f32)[None], (8, span_len))
    own_mixed = (keep * upstream).astype(bf16)
    first_tokens, own_mixed, upstream = lax.optimization_barrier((tokens[0], own_mixed, upstream))
    (
        x_blocks,
        near_w,
        gain_all,
        first_norm,
        queries,
        both_kv,
        log_total,
        turns,
        attended_rows,
        ff_w,
        out_w,
    ) = forward_call(
        freqs,
        first_tokens,
        places,
        gain_rows,
        (w_query, w_key, w_value, w_gate, w_up, w_out),
        line,
    )
    keep_tile = jnp.broadcast_to(keep, (8, HD))
    middle, norm_grad, mixed, grad_down, grad_ff, ff_half = mlp_call(
        keep_tile,
        gain_all,
        own_mixed,
        x_blocks,
        attended_rows,
        out_w,
        ff_w,
        w_down,
        line,
    )
    grad_down = grad_down.astype(f32)
    output = (middle + keep * mixed).astype(bf16)
    middle_grad, input_norm_grad, ff_back, out_back, qkv_back = backward_call(
        (
            upstream,
            middle,
            norm_grad,
            keep_tile,
            gain_all,
        ),
        (queries, both_kv, log_total, turns),
        out_w,
        attended_rows,
        near_w,
        first_norm,
        grad_ff,
        ff_half,
        line,
    )
    ff_back = ff_back.astype(f32)
    qkv_back = qkv_back.astype(f32)
    grad_out = jnp.sum(out_back.astype(f32), axis=0)
    gain_one = gain_all[0, :1]
    inverse_one = lax.rsqrt(jnp.mean(own_x * own_x, axis=-1, keepdims=True) + epsilon)
    scaled_one = gain_one * input_norm_grad
    input_grad = (
        middle_grad
        + inverse_one * scaled_one
        - own_x
        * (inverse_one * inverse_one * inverse_one)
        * jnp.mean(scaled_one * own_x, axis=-1, keepdims=True)
    )

    heads_end, keys_end = w_query.shape[1], w_query.shape[1] + w_key.shape[1]
    grad_query = qkv_back[:, :heads_end]
    grad_key = qkv_back[:, heads_end:keys_end]
    grad_value = qkv_back[:, keys_end:]
    grad_gate = ff_back[:, : w_gate.shape[1]]
    grad_up = ff_back[:, w_gate.shape[1] :]

    def gain_grad(pairs, gain):
        total = sum(jnp.sum(weight.astype(f32) * grad, axis=1) for weight, grad in pairs)
        return total / gain.astype(f32)

    return (
        output[None],
        input_grad.astype(bf16)[None],
        gain_grad([(w_query, grad_query), (w_key, grad_key), (w_value, grad_value)], attn_gain),
        grad_query,
        grad_key,
        grad_value,
        grad_out,
        gain_grad([(w_gate, grad_gate), (w_up, grad_up)], mlp_gain),
        grad_gate,
        grad_up,
        grad_down,
    )


def solution(mesh):
    wide, narrow = mesh.shape["wide"], mesh.shape["narrow"]
    if wide == 2 * KVH and narrow == 4:
        mesh = Mesh(mesh.devices.reshape(wide // 2, 2, 2, 2), ("z", "x", "y", "c"))
        body, wide, narrow = line_body, ("z", "x"), ("y", "c")
    else:
        body, wide, narrow = general_body, ("wide",), ("narrow",)
    token_spec = P(narrow, wide, None)
    id_spec = P(narrow, wide)
    gain_spec = P(wide + narrow)
    weight_spec = P(wide + narrow, None)
    return jax.shard_map(
        body,
        mesh=mesh,
        in_specs=(
            token_spec,
            gain_spec,
            weight_spec,
            weight_spec,
            weight_spec,
            weight_spec,
            gain_spec,
            weight_spec,
            weight_spec,
            weight_spec,
            P(narrow),
            id_spec,
            id_spec,
            P(),
            token_spec,
        ),
        out_specs=(
            token_spec,
            token_spec,
            gain_spec,
            weight_spec,
            weight_spec,
            weight_spec,
            weight_spec,
            gain_spec,
            weight_spec,
            weight_spec,
            weight_spec,
        ),
        check_vma=False,
    )
```

```python
import functools
import math

import jax
import jax.numpy as jnp
from jax import lax
from jax.experimental import pallas as pl
from jax.experimental.pallas import tpu as pltpu
from jax.sharding import Mesh
from jax.sharding import PartitionSpec as P

HEADS = 16
KVH = 4
HD = 128


epsilon = 1e-05


def rotate(vectors, token_pos, direction):
    half_size = vectors.shape[-1] // 2
    freqs = 10000.0 ** (-2.0 * jnp.arange(half_size, dtype=jnp.float32) / vectors.shape[-1])
    angles = token_pos.astype(jnp.float32)[:, None] * freqs[None, :]
    cosine = jnp.cos(angles)[:, None, :]
    sine = direction * jnp.sin(angles)[:, None, :]
    first_half = vectors[..., :half_size]
    second_half = vectors[..., half_size:]
    return jnp.concatenate(
        [first_half * cosine - second_half * sine, second_half * cosine + first_half * sine],
        axis=-1,
    )


def split_blocks(piece_arr, seq_count, kv_heads, head_dim):
    piece_len = piece_arr.shape[1]
    block_len = math.gcd(piece_len, 512)
    shaped = piece_arr.reshape(seq_count, piece_len // block_len, block_len, kv_heads, head_dim)
    return shaped.transpose(1, 0, 2, 3, 4)


def add_rows(whole_arr, update, first_row):
    current = lax.dynamic_slice_in_dim(whole_arr, first_row, update.shape[1], 1)
    return lax.dynamic_update_slice_in_dim(whole_arr, current + update, first_row, 1)


def over_rows(left, right):
    return lax.dot_general(
        left, right, (((0,), (0,)), ((), ())), preferred_element_type=jnp.float32
    )


def against(left, right):
    return lax.dot_general(
        left, right, (((1,), (1,)), ((), ())), preferred_element_type=jnp.float32
    )


def unchanged(carried):
    return carried


MESH = pl.DeviceIdType.MESH
AXES = ("z", "x", "y", "c")


class Links:
    def __init__(self, send_sems, recv_sems, line):
        self.send_sems, self.recv_sems, self.line = send_sems, recv_sems, line
        self.z, self.x, self.y, self.c = (lax.axis_index(name) for name in AXES)
        self.slot = self.x * 4 + self.y * 2 + self.c
        self.used = 0
        self.sent = []

    def device(self, to):
        if to == "x":
            return (self.z, 1 - self.x, self.y, self.c)
        if to == "y":
            return (self.z, self.x, 1 - self.y, self.c)
        if to == "c":
            return (self.z, self.x, self.y, 1 - self.c)
        return (self.along(to), self.x, self.y, self.c)

    def along(self, step):
        return lax.rem(self.z + step + self.line, self.line)

    def other(self, to):
        slot = self.slot
        for name in to:
            bit = {"x": 4, "y": 2, "c": 1}[name]
            here = {"x": self.x, "y": self.y, "c": self.c}[name]
            slot = slot + bit * (1 - 2 * here)
        return slot

    def meet(self, targets):
        barrier = pltpu.get_barrier_semaphore()
        for to in targets:
            pl.semaphore_signal(barrier, inc=1, device_id=self.device(to), device_id_type=MESH)
        pl.semaphore_wait(barrier, len(targets))

    def send(self, source, target, to):
        copy = pltpu.make_async_remote_copy(
            src_ref=source,
            dst_ref=target,
            send_sem=self.send_sems.at[self.used],
            recv_sem=self.recv_sems.at[self.used],
            device_id=self.device(to),
            device_id_type=MESH,
        )
        copy.start()
        self.used += 1
        self.sent.append(copy)
        return copy

    def keep(self, source, target):
        copy = pltpu.make_async_copy(source, target, self.send_sems.at[self.used])
        copy.start()
        self.used += 1
        return copy

    def finish(self):
        for copy in self.sent:
            copy.wait_send()


class NearGather:
    def __init__(self, links, slot):
        self.links, self.slot = links, slot
        self.got = {}

    def offer(self, block, source):
        target = self.slot(block, self.links.slot)
        for to in ("x", "y", "c"):
            self.got[block, to] = self.links.send(source, target, to)

    def relay(self, block, first):
        links = self.links
        for to, then in (("x", "y"), ("y", "x")):
            self.got[block, to].wait_recv()
            place = self.slot(block, links.other(to))
            self.got[block, to + "c"] = links.send(place, place, "c")
            if to == first:
                self.got[block, "xy"] = links.send(place, place, then)

    def close(self, block):
        self.got[block, "xy"].wait_recv()
        place = self.slot(block, self.links.other("xy"))
        self.got[block, "xyc"] = self.links.send(place, place, "c")

    def wait(self, blocks):
        for block in blocks:
            for to in ("c", "xc", "yc", "xyc"):
                self.got[block, to].wait_recv()


class RingGather:
    def __init__(self, links, rows, origin, place, first=0, pieces=4):
        self.links, self.origin, self.place, self.first = links, origin, place, first
        self.pieces, self.rows = pieces, rows // pieces
        self.last = [None] * pieces

    def step(self, number):
        if number > self.first:
            self.wait()
        if number == self.links.line - 1:
            return
        for piece in range(self.pieces):
            way = 1 if piece < self.pieces // 2 else -1
            rows = pl.ds(piece * self.rows, self.rows)
            block = self.links.along(-way * number)
            place = self.place(block, rows)
            source = self.origin(block, rows) if number == self.first else place
            self.last[piece] = self.links.send(source, place, way)

    def wait(self):
        for copy in self.last:
            copy.wait_recv()


def column_of(row):
    size = row.shape[1]
    down = lax.broadcasted_iota(jnp.int32, (size, size), 0)
    across = lax.broadcasted_iota(jnp.int32, (size, size), 1)
    values = jnp.where(down == across, jnp.broadcast_to(row, (size, size)), 0.0)
    return jnp.sum(values, axis=1, keepdims=True)


def first_kernel(
    line,
    small_ref,
    x_ref,
    grad_ref,
    gain_rows_ref,
    query_w_ref,
    key_w_ref,
    value_w_ref,
    gate_w_ref,
    up_w_ref,
    out_ref,
    xs_ref,
    weight_ref,
    gain_ref,
    norm_ref,
    query_ref,
    kv_ref,
    peak_ref,
    turn_ref,
    atts_ref,
    ffs_ref,
    outs_ref,
    mixs_ref,
    x_all,
    grad,
    mix,
    places,
    weights,
    gains,
    norm,
    turns,
    flat,
    query,
    kv,
    peak,
    att,
    send_sems,
    recv_sems,
):
    f32, bf16 = jnp.float32, jnp.bfloat16
    links = Links(send_sems, recv_sems, line)
    far = [1, line - 1] + list(range(2, line - 1))
    links.meet(["x", "y", "c"] + far)
    here = links.slot
    span_len, width = x_ref.shape
    group_len = line * span_len
    rows_each = gate_w_ref.shape[0]
    q_cols = query.shape[1]
    ff_cols = gate_w_ref.shape[1] // line
    heads = q_cols // HD
    local = []

    near = NearGather(links, lambda block, place: weights.at[links.along(-block), place])
    far_ff = NearGather(links, lambda block, place: ffs_ref.at[links.along(-block), place])
    far_out = NearGather(links, lambda block, place: outs_ref.at[links.along(-block), place])
    ring = RingGather(
        links, span_len, lambda block, rows: x_ref.at[rows], lambda block, rows: x_all.at[block, rows]
    )
    place_ref = small_ref.at[0]

    def columns(weight, block, size):
        return weight.at[:, pl.ds(pl.multiple_of(block * size, HD), size)]

    def near_pieces(block):
        target = weights.at[links.z, here]
        rows = pl.ds(0, rows_each)
        return [
            (columns(query_w_ref, block, q_cols), target.at[rows, pl.ds(0, q_cols)]),
            (columns(key_w_ref, block, HD), target.at[rows, pl.ds(q_cols, HD)]),
            (columns(value_w_ref, block, HD), target.at[rows, pl.ds(q_cols + HD, HD)]),
            (gain_rows_ref, target.at[pl.ds(rows_each, 16)]),
        ]

    def ff_pieces(block):
        target = ffs_ref.at[links.z, here]
        return [
            (columns(gate_w_ref, block, ff_cols), target.at[:, pl.ds(0, ff_cols)]),
            (columns(up_w_ref, block, ff_cols), target.at[:, pl.ds(ff_cols, ff_cols)]),
        ]

    def turn_out(pieces):
        return {k: [links.send(*piece, k) for piece in pieces(links.along(k))] for k in far}

    def arrived(copies):
        for copy in copies:
            copy.wait_recv()

    own = [links.keep(*piece) for piece in near_pieces(links.z)]
    own_ff = [links.keep(*piece) for piece in ff_pieces(links.z)]
    turned = turn_out(near_pieces)
    placed = [links.send(place_ref, places.at[links.z], k) for k in far]
    turned_ff = turn_out(ff_pieces)
    for copy in own:
        copy.wait()
    near.offer(0, weights.at[links.z, here])
    for copy in own_ff:
        copy.wait()
    far_ff.offer(0, ffs_ref.at[links.z, here])
    own = [
        links.keep(x_ref, x_all.at[links.z]),
        links.keep(place_ref, places.at[links.z]),
        links.keep(grad_ref, grad),
    ]
    local.append(links.keep(out_ref, outs_ref.at[links.z, here]))

    def move_out(k):
        moved.wait_recv()
        block = outs_ref.at[links.along(-k), here]
        onward = links.send(block, block, 1) if k < line - 1 else None
        far_out.offer(k, block)
        return onward

    for k in far:
        arrived(turned[k])
        near.offer(k, weights.at[links.along(-k), here])
    ring.step(0)
    for k in [0] + far:
        near.relay(k, "x" if k < line // 2 else "y")
    for k in far:
        arrived(turned_ff[k])
        far_ff.offer(k, ffs_ref.at[links.along(-k), here])
    ring.step(1)
    for k in [0] + far:
        near.close(k)
    far_ff.relay(0, "x")
    ring.step(2)
    moved = links.send(out_ref, outs_ref.at[links.z, here], 1)
    far_out.offer(0, out_ref)
    for copy in own:
        copy.wait()
    for copy in placed:
        copy.wait_recv()

    lane = lax.broadcasted_iota(jnp.int32, (span_len, HD), 1)
    for block in range(line):
        angles = column_of(places[block, 0:1]) * small_ref[2, 0:1]
        rows = slice(block * span_len, (block + 1) * span_len)
        sine = jnp.sin(angles)
        turns[0, rows] = jnp.cos(angles)
        turns[1, rows] = jnp.where(lane < HD // 2, -sine, sine)
    local.append(links.keep(turns, turn_ref))
    token_scale = column_of(small_ref[1, 0:1])
    for low in range(0, span_len, 16):
        rows = slice(low, low + 16)
        upstream = grad[rows].astype(f32) * token_scale[rows]
        mix[rows] = (upstream * small_ref[3, 0:1, 0:1]).astype(bf16)
    local.append(links.keep(mix, mixs_ref.at[links.z]))
    near.wait(range(line))
    for index in range(line * 4):
        z, q = divmod(index, 4)
        for which in range(2):
            lanes = slice(which * HD, (which + 1) * HD)
            both = [weights[z, 2 * q + c, rows_each : rows_each + 16, lanes].astype(f32) for c in range(2)]
            gains[which, :, index * HD : (index + 1) * HD] = both[0] + both[1]
    local.append(links.keep(weights, weight_ref))
    local.append(links.keep(gains, gain_ref))
    far_ff.relay(far[0], "x")
    ring.step(3)
    local.append(links.keep(x_all, xs_ref))

    def normalise(index, carry):
        block = index // (span_len // 16)
        rows = pl.ds(pl.multiple_of(lax.rem(index, span_len // 16) * 16, 16), 16)
        values = x_all[block, rows].astype(f32)
        inverse = lax.rsqrt(jnp.mean(values * values, axis=-1, keepdims=True) + epsilon)
        target = pl.ds(pl.multiple_of(index * 16, 16), 16)
        norm[target] = (values * inverse * gains[0]).astype(bf16)
        return carry

    lax.fori_loop(0, group_len // 16, normalise, 0)
    local.append(links.keep(norm, norm_ref))

    def project(low, high):
        step = group_len // 2
        for part in range(2):
            rows = slice(part * step, (part + 1) * step)
            total = None
            for z in range(line):
                weight = weights[z, :, :rows_each, low:high].reshape(8 * rows_each, high - low)
                term = jnp.dot(
                    norm[rows, z * 8 * rows_each : (z + 1) * 8 * rows_each],
                    weight,
                    preferred_element_type=f32,
                )
                total = term if total is None else total + term
            flat[rows, low:high] = total

    def turn(values, rows):
        return values * turns[0, rows] + pltpu.roll(values, HD // 2, 1) * turns[1, rows]

    project(q_cols, q_cols + 2 * HD)
    for block in range(line):
        rows = slice(block * span_len, (block + 1) * span_len)
        kv[0, rows, :HD] = turn(flat[rows, q_cols : q_cols + HD], rows).astype(bf16)
        kv[0, rows, HD:] = flat[rows, q_cols + HD : q_cols + 2 * HD].astype(bf16)
    exchange = links.send(kv.at[0], kv.at[1], "x")
    project(0, q_cols)
    for block in range(line):
        rows = slice(block * span_len, (block + 1) * span_len)
        for head in range(heads):
            lanes = slice(head * HD, (head + 1) * HD)
            query[rows, lanes] = turn(flat[rows, lanes], rows).astype(bf16)
    local.append(links.keep(query, query_ref))
    for k in far[1:]:
        far_ff.relay(k, "x" if k < line // 2 else "y")
    exchange.wait_recv()
    moved = move_out(1)
    local.append(links.keep(kv, kv_ref))

    scale = 1.0 / math.sqrt(HD)
    peak[...] = jnp.zeros_like(peak)

    def attend(head, carry):
        lanes = pl.ds(pl.multiple_of(head * HD, HD), HD)
        for block in range(line):
            rows = slice(block * span_len, (block + 1) * span_len)
            reach = (block + 1) * span_len
            part = query[rows, lanes]
            row = lax.broadcasted_iota(jnp.int32, (span_len, reach), 0) + block * span_len
            column = lax.broadcasted_iota(jnp.int32, (span_len, reach), 1)
            allowed = (column <= row, column < (block + links.x) * span_len)
            scores = []
            for half in range(2):
                score = lax.dot_general(
                    part, kv[half, :reach, :HD], (((1,), (1,)), ((), ())), preferred_element_type=f32
                )
                scores.append(jnp.where(allowed[half], score * scale, -1e30))
            top = jnp.maximum(
                jnp.max(scores[0], axis=-1, keepdims=True), jnp.max(scores[1], axis=-1, keepdims=True)
            )
            total, mixed = None, None
            for half in range(2):
                weight = jnp.exp(scores[half] - top)
                count = jnp.sum(weight, axis=-1, keepdims=True)
                term = jnp.dot(weight.astype(bf16), kv[half, :reach, HD:], preferred_element_type=f32)
                total = count if total is None else total + count
                mixed = term if mixed is None else mixed + term
            att[rows, lanes] = (mixed / total).astype(bf16)
            spot = lax.broadcasted_iota(jnp.int32, (span_len, HD), 1) == head
            peak[rows] = jnp.where(spot, top + jnp.log(total), peak[rows])
        return carry

    lax.fori_loop(0, heads, attend, 0)
    local.append(links.keep(peak, peak_ref))

    def place(block, rows):
        return atts_ref.at[rows, pl.ds(pl.multiple_of(block * q_cols, q_cols), q_cols)]

    att_ring = RingGather(links, group_len, lambda block, rows: att.at[rows], place)
    mix_ring = RingGather(
        links, span_len, lambda block, rows: mix.at[rows], lambda block, rows: mixs_ref.at[block, rows]
    )
    local.append(links.keep(att, place(links.z, pl.ds(0, group_len))))
    att_ring.step(0)
    for k in [0] + far:
        far_ff.close(k)
    far_out.relay(0, "x")
    moved = move_out(2)
    far_out.relay(1, "x")
    att_ring.step(1)
    for k in range(3, line):
        moved = move_out(k)
    far_out.relay(2, "y")
    att_ring.step(2)
    mix_ring.step(0)
    for k in range(3, line):
        far_out.relay(k, "y")
    for k in range(line):
        far_out.close(k)
    att_ring.step(3)
    mix_ring.wait()
    far_out.wait(range(line))
    far_ff.wait(range(line))
    links.finish()
    for copy in local:
        copy.wait()


def add_rows_of(target, values, count):
    def add(index, carry):
        rows = pl.ds(pl.multiple_of(index * 16, 16), 16)
        target[rows] = target[rows] + values[rows]
        return carry

    lax.fori_loop(0, count // 16, add, 0)


class NearSum:
    def __init__(self, links, source, own, from_core, from_first, from_second, first, in_place=False):
        self.links, self.source, self.own, self.first = links, source, own, first
        self.in_place = in_place
        self.from_core, self.from_first, self.from_second = from_core, from_first, from_second

    def start(self):
        links = self.links
        if not self.in_place:
            self.local = links.keep(self.source(links.c), self.own)
        self.copy = links.send(self.source(1 - links.c), self.from_core, "c")

    def add(self, target, values):
        add_rows_of(target, values, target.shape[0])

    def core_done(self):
        links = self.links
        self.copy.wait_recv()
        if not self.in_place:
            self.local.wait()
        for x in range(2):
            for y in range(2):
                self.add(self.own.at[x, y], self.from_core.at[x, y])
        if self.first == "x":
            self.copy = links.send(self.own.at[1 - links.x], self.from_first, "x")
        else:
            self.copy = links.send(self.own.at[:, 1 - links.y], self.from_first, "y")

    def first_done(self):
        links = self.links
        self.copy.wait_recv()
        for other in range(2):
            place = (links.x, other) if self.first == "x" else (other, links.y)
            self.add(self.own.at[place], self.from_first.at[other])
        if self.first == "x":
            self.copy = links.send(self.own.at[links.x, 1 - links.y], self.from_second, "y")
        else:
            self.copy = links.send(self.own.at[1 - links.x, links.y], self.from_second, "x")

    def second_done(self):
        self.copy.wait_recv()
        total = self.own.at[self.links.x, self.links.y]
        self.add(total, self.from_second)
        return total


def sum_space(blocks, rows, columns):
    shape = (rows, columns)
    return [
        pltpu.VMEM((blocks, 2, 2) + shape, jnp.bfloat16),
        pltpu.VMEM((blocks, 2, 2) + shape, jnp.bfloat16),
        pltpu.VMEM((blocks, 2) + shape, jnp.bfloat16),
        pltpu.VMEM((blocks,) + shape, jnp.bfloat16),
    ]


class RingSum:
    def __init__(self, links, parts, total, got, pieces=4):
        self.links, self.parts, self.total, self.got = links, parts, total, got
        self.pieces, self.last = pieces, [None] * pieces
        self.rows = parts.shape[1] // pieces

    def step(self, number, carry=None):
        links = self.links
        for piece in range(self.pieces):
            way = 1 if piece < self.pieces // 2 else -1
            block = links.along(-way * (number + 1))
            where = pl.ds(piece * self.rows, self.rows)
            if number == 0:
                source = self.parts.at[block, where]
            else:
                self.last[piece].wait_recv()
                total = self.got[number - 1, where].astype(jnp.float32) + self.parts[
                    block, where
                ].astype(jnp.float32)
                if number == links.line - 1:
                    self.total[where] = total
                    continue
                if carry is not None:
                    carry[where] = total.astype(carry.dtype)
                    continue
                self.parts[block, where] = total.astype(self.parts.dtype)
                source = self.parts.at[block, where]
            self.last[piece] = links.send(source, self.got.at[number, where], way)


def link_call(kernel, collective_id, copies, shapes, arguments, spaces=None, scratch=(), vmem=16):
    any_space = pl.BlockSpec(memory_space=pl.ANY)
    near_space = pl.BlockSpec(memory_space=pltpu.VMEM)
    many = isinstance(shapes, tuple)
    if spaces is None:
        spaces = "h" * (len(arguments) + (len(shapes) if many else 1))
    specs = [near_space if space == "v" else any_space for space in spaces]
    return pl.pallas_call(
        kernel,
        out_shape=shapes,
        in_specs=specs[: len(arguments)],
        out_specs=tuple(specs[len(arguments) :]) if many else specs[-1],
        scratch_shapes=list(scratch)
        + [pltpu.SemaphoreType.DMA((copies,)), pltpu.SemaphoreType.DMA((copies,))],
        compiler_params=pltpu.CompilerParams(
            collective_id=collective_id, has_side_effects=True, vmem_limit_bytes=vmem * 2**20
        ),
    )(*arguments)


def forward_call(small, tokens, out_grad, gain_rows, weights, line):
    span_len, width = tokens.shape
    group_len = line * span_len
    rows_each, qkv_cols = weights[0].shape[0], gain_rows.shape[1]
    q_cols = qkv_cols - 2 * HD
    both_cols = 2 * weights[3].shape[1] // line
    f32, bf16 = jnp.float32, jnp.bfloat16
    near = (line, 8, rows_each + 16, qkv_cols)
    outs = (
        ((line, span_len, width), bf16),
        (near, bf16),
        ((2, 16, width), f32),
        ((group_len, width), bf16),
        ((group_len, q_cols), bf16),
        ((2, group_len, 2 * HD), bf16),
        ((group_len, HD), f32),
        ((2, group_len, HD), f32),
        ((group_len, line * q_cols), bf16),
        ((line, 8, rows_each, both_cols), bf16),
        ((line, 8, rows_each, width), bf16),
        ((line, span_len, width), bf16),
    )
    return link_call(
        functools.partial(first_kernel, line),
        0,
        208,
        tuple(jax.ShapeDtypeStruct(*out) for out in outs),
        (small, tokens, out_grad, gain_rows) + weights,
        "v" + "h" * 21,
        scratch=[
            pltpu.VMEM((line, span_len, width), bf16),
            pltpu.VMEM((span_len, width), bf16),
            pltpu.VMEM((span_len, width), bf16),
            pltpu.VMEM((line,) + small.shape[1:], f32),
            pltpu.VMEM(near, bf16),
            pltpu.VMEM((2, 16, width), f32),
            pltpu.VMEM((group_len, width), bf16),
            pltpu.VMEM((2, group_len, HD), f32),
            pltpu.VMEM((group_len, qkv_cols), f32),
            pltpu.VMEM((group_len, q_cols), bf16),
            pltpu.VMEM((2, group_len, 2 * HD), bf16),
            pltpu.VMEM((group_len, HD), f32),
            pltpu.VMEM((group_len, q_cols), bf16),
        ],
        vmem=63,
    )


def mlp_kernel(
    line,
    cuts,
    small_ref,
    gain_ref,
    mixs_ref,
    xs_ref,
    atts_ref,
    out_ref,
    ff_ref,
    down_ref,
    middle_ref,
    total_ref,
    carry_ref,
    mixed_own_ref,
    sum_ref,
    grad_ff_ref,
    ff_half_ref,
    big,
    ff,
    down,
    norm,
    parts,
    mixed,
    gate_up,
    hidden,
    both_grad,
    got,
    mixed_parts,
    mixed_got,
    *scratch,
):
    f32, bf16 = jnp.float32, jnp.bfloat16
    space, (send_sems, recv_sems) = scratch[:-2], scratch[-2:]
    links = Links(send_sems, recv_sems, line)
    links.meet(["x", "y", "c", 1, line - 1])
    far = [1, line - 1] + list(range(2, line - 1))
    span_len, width = mixs_ref.shape[1:]
    group_len = line * span_len
    ff_cols = hidden.shape[1]
    block_rows = width // line
    rows_each = block_rows // 8
    chunk = 2 * HD
    mix_ring = RingGather(
        links,
        span_len,
        lambda block, rows: mixs_ref.at[block, rows],
        lambda block, rows: mixed.at[block, rows],
        1,
    )
    mix_ring.step(1)
    stay = [links.keep(mixs_ref.at[links.z], mixed.at[links.z])]
    for low, step in ((0, -1), (span_len // 2, 1)):
        rows = pl.ds(low, span_len // 2)
        stay.append(links.keep(mixs_ref.at[links.along(step), rows], mixed.at[links.along(step), rows]))
    early = [
        links.keep(out_ref, big),
        links.keep(atts_ref, norm),
        links.keep(xs_ref, parts),
    ]
    late = [links.keep(ff_ref, ff)]
    down_rows = down_ref.shape[0]

    def down_place(block, place):
        low, high = cuts[block]
        return down.at[pl.ds(pl.multiple_of(place * down_rows + low, 16), high - low)]

    near = NearGather(links, down_place)
    for block, (low, high) in enumerate(cuts):
        rows = down_ref.at[pl.ds(low, high - low)]
        late.append(links.keep(rows, down_place(block, links.slot)))
        near.offer(block, rows)
    ring = RingSum(links, parts, total_ref, got)
    mixed_ring = RingSum(links, mixed_parts, None, mixed_got)
    items = []
    ff_items = []
    for index, k in enumerate(far[:2]):
        block = links.along(k)
        core, first, second = space[:3]
        ff_items.append(
            NearSum(
                links,
                lambda c, block=block: ff.at[block, :, :, c],
                ff.at[block, :, :, links.c],
                core.at[index],
                first.at[index],
                second.at[index],
                "xy"[index % 2],
                True,
            )
        )
    for index, (low, high) in enumerate(cuts):
        rows = pl.ds(low, high - low)
        core, first, second = space[3 * index + 3 : 3 * index + 6]
        items.append(
            NearSum(
                links,
                lambda c, rows=rows: big.at[:, :, c, rows],
                big.at[:, :, links.c, rows],
                core.at[0],
                first.at[0],
                second.at[0],
                "xy"[index % 2],
                True,
            )
        )
    for copy in early:
        copy.wait()

    half = group_len // 2
    out_rows = width // 8
    for part in range(2):
        low = part * half
        for column in range(4):
            lanes = slice(column * width // 4, (column + 1) * width // 4)
            value = None
            for k in range(8):
                term = jnp.dot(
                    norm[low : low + half, k * out_rows : (k + 1) * out_rows],
                    big[k // 4, k // 2 % 2, k % 2, :, lanes],
                    preferred_element_type=f32,
                )
                value = term if value is None else value + term
            gate_up[:half, lanes] = value * small_ref[3, 0:1, 0:1]

        def normalise(index, carry, low=low):
            block = (low // 16 + index) // (span_len // 16)
            rows = pl.ds(pl.multiple_of(index * 16, 16), 16)
            inside = pl.ds(pl.multiple_of(lax.rem(index, span_len // 16) * 16, 16), 16)
            values = parts[block, inside].astype(f32) + gate_up[rows, :width]
            gate_up[rows, :width] = values
            inverse = lax.rsqrt(jnp.mean(values * values, axis=-1, keepdims=True) + epsilon)
            target = pl.ds(pl.multiple_of(low + index * 16, 16), 16)
            norm[target] = (values * inverse * gain_ref[1]).astype(bf16)
            return carry

        lax.fori_loop(0, half // 16, normalise, 0)

        @pl.when(links.z // (line // 2) == part)
        def _():
            where = pl.multiple_of(lax.rem(links.z, line // 2) * span_len, span_len)
            middle_ref[...] = gate_up[pl.ds(where, span_len), :width]
        if part == 0:
            mix_ring.step(2)

    for block in range(2):
        near.relay(block, "xy"[block])
    for copy in late:
        copy.wait()

    def columns_of(lanes, size):
        return ff[:, :, :, :, :, lanes].reshape(width, size)

    def forward(low, size):
        gates, ups = pl.ds(low, size), pl.ds(low + ff_cols, size)
        gate = jnp.dot(norm[...], columns_of(gates, size), preferred_element_type=f32)
        gate_up[:, gates] = gate
        swish = gate * jax.nn.sigmoid(gate)
        up = jnp.dot(norm[...], columns_of(ups, size), preferred_element_type=f32)
        gate_up[:, ups] = up
        hidden[:, gates] = (swish * up).astype(bf16)

    def backward(low, size):
        gates, ups = pl.ds(low, size), pl.ds(low + ff_cols, size)
        grad = lax.dot_general(
            mixed[...].reshape(group_len, width),
            down[gates],
            (((1,), (1,)), ((), ())),
            preferred_element_type=f32,
        )
        gate, up = gate_up[:, gates], gate_up[:, ups]
        sigmoid = jax.nn.sigmoid(gate)
        both_grad[:, gates] = (grad * up * sigmoid * (1.0 + gate * (1.0 - sigmoid))).astype(bf16)
        both_grad[:, ups] = (grad * (gate * sigmoid)).astype(bf16)

    def over_chunks(work, extent):
        def one(index, carry):
            work(pl.multiple_of(index * chunk, chunk), chunk)
            return carry

        lax.fori_loop(0, extent // chunk, one, 0)
        if extent % chunk:
            work(extent // chunk * chunk, extent % chunk)

    over_chunks(forward, ff_cols)
    for block in range(2):
        near.close(block)
    near.wait(range(2))

    def mixed_part(low, size):
        lanes = pl.ds(low, size)
        value = jnp.dot(hidden[...], down[:, lanes], preferred_element_type=f32).astype(bf16)
        mixed_parts[:, :, lanes] = value.reshape(line, span_len, size)

    over_chunks(mixed_part, width)
    mixed_ring.step(0)
    mixed_own_ref[...] = mixed_parts[links.z]
    for copy in stay:
        copy.wait()
    mix_ring.step(3)
    hidden_rows = hidden[...].T

    def down_part(low, size):
        lanes = pl.ds(low, size)
        value = jnp.dot(
            hidden_rows,
            mixed[:, :, lanes].reshape(group_len, size),
            preferred_element_type=f32,
        ).astype(bf16)
        big[:, :, :, : cuts[-1][1], lanes] = value.reshape(2, 2, 2, cuts[-1][1], size)

    over_chunks(down_part, width)
    for item in items:
        item.start()
    over_chunks(backward, ff_cols)
    mixed_ring.step(1)
    for item in items:
        item.core_done()

    def norm_part(index, carry):
        size = 4 * rows_each
        weight = ff[index // 2, lax.rem(index, 2)].reshape(size, 2 * ff_cols)
        value = lax.dot_general(
            both_grad[...], weight, (((1,), (1,)), ((), ())), preferred_element_type=f32
        ).astype(bf16)
        lanes = pl.ds(pl.multiple_of(index * size, size), size)
        parts[:, :, lanes] = value.reshape(line, span_len, size)
        return carry

    lax.fori_loop(0, 2 * line, norm_part, 0)
    ring.step(0)

    def ff_block(block):
        norm_rows = norm[:, pl.ds(pl.multiple_of(block * block_rows, block_rows), block_rows)].T

        def ff_part(low, size):
            lanes = pl.ds(low, size)
            value = jnp.dot(norm_rows, both_grad[:, lanes], preferred_element_type=f32)
            ff[block, :, :, :, :, lanes] = value.astype(bf16).reshape(2, 2, 2, rows_each, size)

        over_chunks(ff_part, 2 * ff_cols)

    for item, k in zip(ff_items, far):
        ff_block(links.along(k))
        item.start()
    for item in items:
        item.first_done()
    ring.step(1)
    for item in ff_items:
        item.core_done()
    mixed_ring.step(2, carry_ref)
    sent = []
    for k in far[2:] + [0]:
        block = links.along(k)
        ff_block(block)
        sent.append(links.keep(ff.at[block], grad_ff_ref.at[block]))
    for item, (low, high) in zip(items, cuts):
        sum_ref[low:high] = item.second_done()[...]
    ring.step(2)
    for item in ff_items:
        item.first_done()
    ring.step(3)
    for index, item in enumerate(ff_items):
        sent.append(links.keep(item.second_done(), ff_half_ref.at[index]))
    links.finish()
    for copy in sent:
        copy.wait()


def mlp_call(small, gains, mixed, x_blocks, attended, out_w, ff_w, w_down, line):
    f32, bf16 = jnp.float32, jnp.bfloat16
    span_len, width = mixed.shape[1:]
    group_len = line * span_len
    rows, both_cols, rows_each = w_down.shape[0], ff_w.shape[3], ff_w.shape[2]
    ff_rows = 8 * rows
    ff_w = ff_w.reshape(line, 2, 2, 2, rows_each, both_cols)
    half = (rows // 2 + 15) // 16 * 16
    cuts = ((0, half), (half, rows))
    blocks = (line, span_len, width)
    token = jax.ShapeDtypeStruct((span_len, width), f32)
    return link_call(
        functools.partial(mlp_kernel, line, cuts),
        2,
        112,
        (
            token,
            token,
            jax.ShapeDtypeStruct((span_len, width), bf16),
            jax.ShapeDtypeStruct((span_len, width), bf16),
            jax.ShapeDtypeStruct((rows, width), bf16),
            jax.ShapeDtypeStruct(ff_w.shape, bf16),
            jax.ShapeDtypeStruct((2, rows_each, both_cols), bf16),
        ),
        (small, gains, mixed, x_blocks, attended, out_w.reshape(2, 2, 2, width // 8, width), ff_w, w_down),
        "vvhhhhhh" + "vvvvvhh",
        [
            pltpu.VMEM((2, 2, 2, width // 8, width), bf16),
            pltpu.VMEM(ff_w.shape, bf16),
            pltpu.VMEM((ff_rows, width), bf16),
            pltpu.VMEM((group_len, width), bf16),
            pltpu.VMEM(blocks, bf16),
            pltpu.VMEM(blocks, bf16),
            pltpu.VMEM((group_len, both_cols), f32),
            pltpu.VMEM((group_len, ff_rows), bf16),
            pltpu.VMEM((group_len, both_cols), bf16),
            pltpu.VMEM((line - 1, span_len, width), bf16),
            pltpu.VMEM(blocks, bf16),
            pltpu.VMEM((line - 2, span_len, width), bf16),
        ]
        + sum_space(2, rows_each, both_cols)[1:]
        + sum((sum_space(1, high - low, width)[1:] for low, high in cuts), []),
        vmem=63,
    )


def backward_kernel(
    line,
    small_ref,
    gain_ref,
    middle_ref,
    norm_grad_ref,
    x_ref,
    grad_ref,
    carry_ref,
    mixed_own_ref,
    query_ref,
    kv_ref,
    peak_ref,
    turn_ref,
    out_ref,
    atts_ref,
    weight_ref,
    norm_ref,
    ff_ref,
    ff_half_ref,
    output_ref,
    token_ref,
    ffs_ref,
    outs_ref,
    qkvs_ref,
    x_own,
    grad_own,
    mixed_own,
    mixed_in,
    middle_grad,
    total,
    big,
    slim,
    norm,
    own_rows,
    own_columns,
    branch,
    own_grad,
    att_grad,
    query_back,
    kv_back,
    kv_out,
    kv_in,
    flat,
    parts,
    query,
    kv,
    peak,
    turns,
    *scratch,
):
    f32, bf16 = jnp.float32, jnp.bfloat16
    send_sems, recv_sems = scratch[-2:]
    got, sums = scratch[0], scratch[1:-2]
    links = Links(send_sems, recv_sems, line)
    far = [1, line - 1] + list(range(2, line - 1))
    order = far + [0]
    links.meet(["x", "y", "c"] + far)
    span_len, width = x_ref.shape
    group_len = line * span_len
    q_cols = query.shape[1]
    heads = q_cols // HD
    rows_z = width // line
    rows_each = rows_z // 8
    scale = 1.0 / math.sqrt(HD)

    def lanes_of(block):
        return pl.ds(pl.multiple_of(block * q_cols, q_cols), q_cols)

    here = pl.ds(pl.multiple_of(links.z * span_len, span_len), span_len)
    loads = [
        links.keep(out_ref, big),
        links.keep(atts_ref.at[here], own_rows),
        links.keep(atts_ref.at[:, lanes_of(links.z)], own_columns),
        links.keep(grad_ref, grad_own),
        links.keep(x_ref, x_own),
        links.keep(mixed_own_ref, mixed_own),
        links.keep(query_ref, query),
        links.keep(kv_ref, kv),
        links.keep(peak_ref, peak),
        links.keep(turn_ref, turns),
        links.keep(norm_ref, norm),
        links.keep(weight_ref.at[:, :, :, :, pl.ds(0, slim.shape[4])], slim),
    ]
    ring = RingSum(links, parts, total, got)

    def items_of(source, space, in_place, order=order):
        items = []
        for index, k in enumerate(order):
            block = links.along(k)
            own = source.at[block, :, :, links.c] if in_place else space[0].at[index]
            core, first, second = space[-3:]
            items.append(
                NearSum(
                    links,
                    lambda c, block=block: source.at[block, :, :, c],
                    own,
                    core.at[index],
                    first.at[index],
                    second.at[index],
                    "xy"[index % 2],
                    in_place,
                )
            )
        return items

    ff_order = order[2:]
    ff_items = items_of(ff_ref, sums[:4], False, ff_order)
    out_items = items_of(big, sums[4:7], True)
    qkv_items = items_of(slim, sums[7:], True)
    local, arrived = [], []
    ff_cols = ff_ref.shape[5] // 2
    ff_pieces = ((0, ff_cols), (ff_cols, ff_cols))
    qkv_pieces = ((0, q_cols), (q_cols, HD), (q_cols + HD, HD))

    def deliver(total, target, k, pieces):
        for low, size in pieces:
            if pieces == out_pieces:
                place = target.at[links.z]
            else:
                lanes = pl.multiple_of(line * low + links.z * size, HD)
                place = target.at[:, pl.ds(lanes, size)]
            part = total.at[:, pl.ds(low, size)]
            if k == 0:
                local.append(links.keep(part, place))
            else:
                arrived.append(links.send(part, place, k))

    out_pieces = ((0, width),)
    for index, k in enumerate(order[:2]):
        deliver(ff_half_ref.at[index], ffs_ref, k, ff_pieces)
    mixed_last = []
    for piece in range(4):
        rows = pl.ds(piece * (span_len // 4), span_len // 4)
        way = 1 if piece < 2 else -1
        mixed_last.append(links.send(carry_ref.at[rows], mixed_in.at[rows], way))

    def turn(items, target, low, high, pieces, order=order):
        for item, k in list(zip(items, order))[low:high]:
            deliver(item.second_done(), target, k, pieces)

    def core_done(items, low, high):
        for item in items[low:high]:
            item.core_done()

    def first_done(items, low, high):
        for item in items[low:high]:
            item.first_done()

    half = line // 2
    for item in ff_items:
        item.start()

    for copy in loads:
        copy.wait()
    keep = small_ref[3, 0:1, 0:1]
    token_scale = column_of(small_ref[1, 0:1])

    def norm_back(values, grad, gain):
        inverse = lax.rsqrt(jnp.mean(values * values, axis=-1, keepdims=True) + epsilon)
        scaled = gain * grad
        return inverse * scaled - values * (inverse * inverse * inverse) * jnp.mean(
            scaled * values, axis=-1, keepdims=True
        )

    for low in range(0, span_len, 16):
        rows = slice(low, low + 16)
        upstream = grad_own[rows].astype(f32) * token_scale[rows]
        grad = upstream + norm_back(middle_ref[rows], norm_grad_ref[rows], gain_ref[1])
        middle_grad[rows] = grad
        branch[rows] = (grad * keep).astype(bf16)
    for z in range(line):
        weight = big[z].reshape(rows_z, width)
        own_grad[:, z * rows_z : (z + 1) * rows_z] = lax.dot_general(
            branch[...], weight, (((1,), (1,)), ((), ())), preferred_element_type=f32
        ).astype(bf16)
    turned = [links.send(own_grad.at[:, lanes_of(links.along(k))], att_grad.at[here], k) for k in far]
    stayed = links.keep(own_grad.at[:, lanes_of(links.z)], att_grad.at[here])
    core_done(ff_items, 0, line)
    for z in range(line):
        for part in range(4):
            columns = slice(part * width // 4, (part + 1) * width // 4)
            grad = lax.dot_general(
                own_rows[:, z * rows_z : (z + 1) * rows_z],
                branch[:, columns],
                (((0,), (0,)), ((), ())),
                preferred_element_type=f32,
            )
            big[z, :, :, :, :, columns] = grad.astype(bf16).reshape(2, 2, 2, rows_each, width // 4)
    for item in out_items:
        item.start()
    kv_back[...] = jnp.zeros_like(kv_back)
    for copy in turned:
        copy.wait_recv()
    stayed.wait()

    def attend_back(head, carry):
        lanes = pl.ds(pl.multiple_of(head * HD, HD), HD)
        for block in range(line):
            rows = slice(block * span_len, (block + 1) * span_len)
            reach = (block + 1) * span_len
            part, grad = query[rows, lanes], att_grad[rows, lanes]
            row = lax.broadcasted_iota(jnp.int32, (span_len, reach), 0) + block * span_len
            column = lax.broadcasted_iota(jnp.int32, (span_len, reach), 1)
            allowed = (column <= row, column < (block + links.x) * span_len)
            spot = lax.broadcasted_iota(jnp.int32, (span_len, HD), 1) == head
            top = jnp.sum(jnp.where(spot, peak[rows], 0.0), axis=-1, keepdims=True)
            delta = jnp.sum(
                grad.astype(f32) * own_columns[rows, lanes].astype(f32), axis=-1, keepdims=True
            )
            back = None
            for side in range(2):
                keys, values = kv[side, :reach, :HD], kv[side, :reach, HD:]
                score = lax.dot_general(
                    part, keys, (((1,), (1,)), ((), ())), preferred_element_type=f32
                )
                weight = jnp.where(allowed[side], jnp.exp(score * scale - top), 0.0)
                weight_grad = lax.dot_general(
                    grad, values, (((1,), (1,)), ((), ())), preferred_element_type=f32
                )
                score_grad = (weight * (weight_grad - delta)).astype(bf16)
                term = jnp.dot(score_grad, keys, preferred_element_type=f32)
                back = term if back is None else back + term
                kv_back[side, :reach, :HD] += lax.dot_general(
                    score_grad, part, (((0,), (0,)), ((), ())), preferred_element_type=f32
                )
                kv_back[side, :reach, HD:] += lax.dot_general(
                    weight.astype(bf16), grad, (((0,), (0,)), ((), ())), preferred_element_type=f32
                )
            query_back[rows, lanes] = back * scale
        return carry

    lax.fori_loop(0, heads, attend_back, 0)
    kv_out[:, :HD] = (kv_back[1, :, :HD] * scale).astype(bf16)
    kv_out[:, HD:] = kv_back[1, :, HD:].astype(bf16)
    exchange = links.send(kv_out, kv_in, "x")

    def turn_back(values, rows):
        return values * turns[0, rows] - pltpu.roll(values, HD // 2, 1) * turns[1, rows]

    for block in range(line):
        rows = slice(block * span_len, (block + 1) * span_len)
        for head in range(heads):
            lanes = slice(head * HD, (head + 1) * HD)
            flat[rows, lanes] = turn_back(query_back[rows, lanes], rows).astype(bf16)
    first_done(ff_items, 0, line)
    exchange.wait_recv()
    for block in range(line):
        rows = slice(block * span_len, (block + 1) * span_len)
        key_grad = kv_back[0, rows, :HD] * scale + kv_in[rows, :HD].astype(f32)
        flat[rows, q_cols : q_cols + HD] = turn_back(key_grad, rows).astype(bf16)
        value_grad = kv_back[0, rows, HD:] + kv_in[rows, HD:].astype(f32)
        flat[rows, q_cols + HD :] = value_grad.astype(bf16)
    for z in range(line):
        weight = slim[z].reshape(rows_z, flat.shape[1])
        part = lax.dot_general(
            flat[...], weight, (((1,), (1,)), ((), ())), preferred_element_type=f32
        ).astype(bf16)
        for block in range(line):
            parts[block, :, z * rows_z : (z + 1) * rows_z] = part[
                block * span_len : (block + 1) * span_len
            ]
    ring.step(0)
    for z in range(line):
        grad = lax.dot_general(
            norm[:, z * rows_z : (z + 1) * rows_z],
            flat[...],
            (((0,), (0,)), ((), ())),
            preferred_element_type=f32,
        )
        slim[z] = grad.astype(bf16).reshape(2, 2, 2, rows_each, flat.shape[1])
    for item in qkv_items:
        item.start()
    core_done(out_items, 0, half)
    turn(ff_items, ffs_ref, 0, line, ff_pieces, ff_order)
    for copy in mixed_last:
        copy.wait_recv()
    for low in range(0, span_len, 16):
        rows = slice(low, low + 16)
        mixed = mixed_in[rows].astype(f32) + mixed_own[rows].astype(f32)
        output_ref[rows] = (middle_ref[rows] + keep * mixed).astype(bf16)
    ring.step(1)
    core_done(out_items, half, line)
    first_done(out_items, 0, half)
    ring.step(2)
    core_done(qkv_items, 0, line)
    first_done(out_items, half, line)
    turn(out_items, outs_ref, 0, half, out_pieces)
    ring.step(3)
    for low in range(0, span_len, 16):
        rows = slice(low, low + 16)
        grad = middle_grad[rows] + norm_back(x_own[rows].astype(f32), total[rows], gain_ref[0])
        token_ref[rows] = grad.astype(bf16)
    first_done(qkv_items, 0, half)
    turn(out_items, outs_ref, half, line, out_pieces)
    first_done(qkv_items, half, line)
    turn(qkv_items, qkvs_ref, 0, line, qkv_pieces)
    for copy in arrived:
        copy.wait_recv()
    links.finish()
    for copy in local:
        copy.wait()


def backward_call(near, tokens, saved, out_w, attended, weights, norm, grad_ff, ff_half, line):
    f32, bf16 = jnp.float32, jnp.bfloat16
    span_len, width = tokens[0].shape
    group_len = line * span_len
    query = saved[0]
    q_cols, rows_each, qkv_cols = query.shape[1], width // line // 8, weights.shape[3]
    weights = weights.reshape(line, 2, 2, 2, -1, qkv_cols)
    wide = (line, 2, 2, 2, rows_each, width)
    slim = (line, 2, 2, 2, rows_each, qkv_cols)
    out_space = sum_space(line, rows_each, width)[1:]
    qkv_space = sum_space(line, rows_each, qkv_cols)[1:]
    token = jax.ShapeDtypeStruct((span_len, width), bf16)
    return link_call(
        functools.partial(backward_kernel, line),
        4,
        160,
        (token, token)
        + (
            jax.ShapeDtypeStruct((rows_each, line * grad_ff.shape[5]), bf16),
            jax.ShapeDtypeStruct((line, rows_each, width), bf16),
            jax.ShapeDtypeStruct((rows_each, line * qkv_cols), bf16),
        ),
        near + tokens + saved + (out_w.reshape(wide), attended, weights, norm, grad_ff, ff_half),
        "v" * 4 + "h" * 14 + "vvhhh",
        [pltpu.VMEM((span_len, width), bf16)] * 4
        + [pltpu.VMEM((span_len, width), f32)] * 2
        + [
            pltpu.VMEM(wide, bf16),
            pltpu.VMEM(slim, bf16),
            pltpu.VMEM((group_len, width), bf16),
            pltpu.VMEM((span_len, width), bf16),
            pltpu.VMEM((group_len, q_cols), bf16),
            pltpu.VMEM((span_len, width), bf16),
            pltpu.VMEM((span_len, width), bf16),
            pltpu.VMEM((group_len, q_cols), bf16),
            pltpu.VMEM((group_len, q_cols), f32),
            pltpu.VMEM((2, group_len, 2 * HD), f32),
            pltpu.VMEM((group_len, 2 * HD), bf16),
            pltpu.VMEM((group_len, 2 * HD), bf16),
            pltpu.VMEM((group_len, qkv_cols), bf16),
            pltpu.VMEM((line, span_len, width), bf16),
        ]
        + [pltpu.VMEM(value.shape, value.dtype) for value in saved]
        + [pltpu.VMEM((line - 1, span_len, width), bf16)]
        + sum_space(line - 2, rows_each, grad_ff.shape[5])
        + out_space
        + qkv_space,
        vmem=63,
    )


def general_body(
    tokens,
    attn_gain,
    w_query,
    w_key,
    w_value,
    w_out,
    mlp_gain,
    w_gate,
    w_up,
    w_down,
    keep_mask,
    group_ids,
    positions,
    exit_scale,
    out_grad,
):
    seq_count, span_len, model_width = tokens.shape
    kv_heads = KVH
    head_dim = HD
    head_count = HEADS
    group_size = head_count // kv_heads
    row_count = seq_count * span_len
    stripe = group_size * span_len
    wide_count = lax.axis_size("wide")
    wide_place = lax.axis_index("wide")
    full_len = span_len * wide_count
    score_scale = 1.0 / math.sqrt(head_dim)
    gain_one, query_w, key_w, value_w, out_w = (
        lax.all_gather(attn_gain, ("wide", "narrow"), axis=0, tiled=True),
        lax.all_gather(w_query, ("wide", "narrow"), axis=0, tiled=True),
        lax.all_gather(w_key, ("wide", "narrow"), axis=0, tiled=True),
        lax.all_gather(w_value, ("wide", "narrow"), axis=0, tiled=True),
        lax.all_gather(w_out, ("wide", "narrow"), axis=0, tiled=True),
    )
    inputs = tokens.astype(jnp.float32).reshape(row_count, model_width)
    token_pos = positions.reshape(row_count)
    keep_rows = jnp.repeat(keep_mask.astype(jnp.float32), span_len)[:, None]
    inverse_one = lax.rsqrt(jnp.mean(inputs * inputs, axis=-1, keepdims=True) + epsilon)
    first_norm = (inputs * inverse_one * gain_one.astype(jnp.float32)).astype(jnp.bfloat16)
    query_pre = jnp.dot(first_norm, query_w, preferred_element_type=jnp.float32).reshape(
        row_count, head_count, head_dim
    )
    key_pre = jnp.dot(first_norm, key_w, preferred_element_type=jnp.float32).reshape(
        row_count, kv_heads, head_dim
    )
    query_rows = rotate(query_pre, token_pos, 1.0).astype(jnp.bfloat16)
    key_heads = (
        rotate(key_pre, token_pos, 1.0)
        .astype(jnp.bfloat16)
        .reshape(seq_count, span_len, kv_heads * head_dim)
    )
    value_heads = (
        jnp.dot(first_norm, value_w, preferred_element_type=jnp.float32)
        .astype(jnp.bfloat16)
        .reshape(seq_count, span_len, kv_heads * head_dim)
    )
    queries = (
        query_rows.reshape(seq_count, span_len, kv_heads, group_size, head_dim)
        .transpose(0, 2, 3, 1, 4)
        .reshape(seq_count, kv_heads, stripe, head_dim)
    )
    query_index = wide_place * span_len + jnp.arange(stripe, dtype=jnp.int32) % span_len
    last_query = wide_place * span_len + span_len - 1

    def block_scores(key_block, key_first):
        scores = (
            jnp.einsum("skrd,sjkd->skrj", queries, key_block, preferred_element_type=jnp.float32)
            * score_scale
        )
        key_index = key_first + jnp.arange(key_block.shape[1], dtype=jnp.int32)
        allowed = key_index[None, :] <= query_index[:, None]
        return (scores, allowed)

    start_forward = (
        jnp.full((seq_count, kv_heads, stripe), -1e30, jnp.float32),
        jnp.zeros((seq_count, kv_heads, stripe), jnp.float32),
        jnp.zeros((seq_count, kv_heads, stripe, head_dim), jnp.float32),
    )
    running = start_forward
    pieces = (
        lax.all_gather(key_heads, "wide", axis=1, tiled=True),
        lax.all_gather(value_heads, "wide", axis=1, tiled=True),
    )
    key_blocks = split_blocks(pieces[0], seq_count, kv_heads, head_dim)
    value_blocks = split_blocks(pieces[1], seq_count, kv_heads, head_dim)
    block_len = key_blocks.shape[2]

    def advance(carried, block_item):
        key_block, value_block, block_index = block_item
        key_first = block_index * block_len

        def compute_block(current):
            run_max, run_sum, run_acc = current
            scores, allowed = block_scores(key_block, key_first)
            scores = jnp.where(allowed, scores, -1e30)
            new_max = jnp.maximum(run_max, jnp.max(scores, axis=-1))
            factor = jnp.exp(run_max - new_max)
            weights = jnp.where(allowed, jnp.exp(scores - new_max[..., None]), 0.0)
            new_sum = run_sum * factor + jnp.sum(weights, axis=-1)
            new_acc = run_acc * factor[..., None] + jnp.einsum(
                "skrj,sjkd->skrd",
                weights.astype(jnp.bfloat16),
                value_block,
                preferred_element_type=jnp.float32,
            )
            return (new_max, new_sum, new_acc)

        return (lax.cond(key_first <= last_query, compute_block, unchanged, carried), None)

    running, _ = lax.scan(
        advance,
        running,
        (key_blocks, value_blocks, jnp.arange(key_blocks.shape[0], dtype=jnp.int32)),
    )
    run_max, run_sum, run_acc = running
    attended = run_acc / run_sum[..., None]
    log_total = run_max + jnp.log(run_sum)
    attended_rows = (
        attended.reshape(seq_count, kv_heads, group_size, span_len, head_dim)
        .transpose(0, 3, 1, 2, 4)
        .reshape(row_count, head_count * head_dim)
        .astype(jnp.bfloat16)
    )
    middle = inputs + keep_rows * jnp.dot(attended_rows, out_w, preferred_element_type=jnp.float32)
    gain_two, gate_w, up_w, down_w = (
        lax.all_gather(mlp_gain, ("wide", "narrow"), axis=0, tiled=True),
        lax.all_gather(w_gate, ("wide", "narrow"), axis=0, tiled=True),
        lax.all_gather(w_up, ("wide", "narrow"), axis=0, tiled=True),
        lax.all_gather(w_down, ("wide", "narrow"), axis=0, tiled=True),
    )
    inverse_two = lax.rsqrt(jnp.mean(middle * middle, axis=-1, keepdims=True) + epsilon)
    second_norm = (middle * inverse_two * gain_two.astype(jnp.float32)).astype(jnp.bfloat16)
    gate_value = jnp.dot(second_norm, gate_w, preferred_element_type=jnp.float32)
    up_value = jnp.dot(second_norm, up_w, preferred_element_type=jnp.float32)
    gate_sigmoid = jax.nn.sigmoid(gate_value)
    swish_value = gate_value * gate_sigmoid
    hidden = (swish_value * up_value).astype(jnp.bfloat16)
    output = (
        middle + keep_rows * jnp.dot(hidden, down_w, preferred_element_type=jnp.float32)
    ).astype(jnp.bfloat16)
    group_match = (
        group_ids.reshape(row_count)[:, None]
        == jnp.arange(exit_scale.shape[0], dtype=jnp.int32)[None, :]
    )
    token_scale = jnp.sum(jnp.where(group_match, exit_scale[None, :], 0.0), axis=1, keepdims=True)
    upstream = out_grad.astype(jnp.float32).reshape(row_count, model_width) * token_scale
    gain_two, gate_w, up_w, down_w = (
        lax.all_gather(mlp_gain, ("wide", "narrow"), axis=0, tiled=True),
        lax.all_gather(w_gate, ("wide", "narrow"), axis=0, tiled=True),
        lax.all_gather(w_up, ("wide", "narrow"), axis=0, tiled=True),
        lax.all_gather(w_down, ("wide", "narrow"), axis=0, tiled=True),
    )
    mixed_grad = (keep_rows * upstream).astype(jnp.bfloat16)
    grad_down = over_rows(hidden, mixed_grad)
    hidden_grad = against(mixed_grad, down_w)
    gate_grad = (
        hidden_grad * up_value * gate_sigmoid * (1.0 + gate_value * (1.0 - gate_sigmoid))
    ).astype(jnp.bfloat16)
    up_grad = (hidden_grad * swish_value).astype(jnp.bfloat16)
    grad_gate = over_rows(second_norm, gate_grad)
    grad_up = over_rows(second_norm, up_grad)
    norm_grad = against(gate_grad, gate_w) + against(up_grad, up_w)
    grad_gain_two = jnp.sum(norm_grad * middle * inverse_two, axis=0)
    scaled_two = gain_two.astype(jnp.float32) * norm_grad
    middle_grad = (
        upstream
        + inverse_two * scaled_two
        - middle
        * (inverse_two * inverse_two * inverse_two)
        * jnp.mean(scaled_two * middle, axis=-1, keepdims=True)
    )
    gain_two_share, gate_share, up_share, down_share = (
        lax.psum_scatter(grad_gain_two, ("wide", "narrow"), scatter_dimension=0, tiled=True),
        lax.psum_scatter(grad_gate, ("wide", "narrow"), scatter_dimension=0, tiled=True),
        lax.psum_scatter(grad_up, ("wide", "narrow"), scatter_dimension=0, tiled=True),
        lax.psum_scatter(grad_down, ("wide", "narrow"), scatter_dimension=0, tiled=True),
    )
    gain_one, query_w, key_w, value_w, out_w = (
        lax.all_gather(attn_gain, ("wide", "narrow"), axis=0, tiled=True),
        lax.all_gather(w_query, ("wide", "narrow"), axis=0, tiled=True),
        lax.all_gather(w_key, ("wide", "narrow"), axis=0, tiled=True),
        lax.all_gather(w_value, ("wide", "narrow"), axis=0, tiled=True),
        lax.all_gather(w_out, ("wide", "narrow"), axis=0, tiled=True),
    )
    branch_grad = (keep_rows * middle_grad).astype(jnp.bfloat16)
    grad_out = over_rows(attended_rows, branch_grad)
    attended_grad = against(branch_grad, out_w).astype(jnp.bfloat16)
    grouped_grad = (
        attended_grad.reshape(seq_count, span_len, kv_heads, group_size, head_dim)
        .transpose(0, 2, 3, 1, 4)
        .reshape(seq_count, kv_heads, stripe, head_dim)
    )
    row_delta = jnp.sum(grouped_grad.astype(jnp.float32) * attended, axis=-1)
    start_backward = (
        jnp.zeros((seq_count, kv_heads, stripe, head_dim), jnp.float32),
        jnp.zeros((seq_count, full_len, kv_heads * head_dim), jnp.float32),
        jnp.zeros((seq_count, full_len, kv_heads * head_dim), jnp.float32),
    )
    running = start_backward
    pieces = (
        lax.all_gather(key_heads, "wide", axis=1, tiled=True),
        lax.all_gather(value_heads, "wide", axis=1, tiled=True),
    )
    key_blocks = split_blocks(pieces[0], seq_count, kv_heads, head_dim)
    value_blocks = split_blocks(pieces[1], seq_count, kv_heads, head_dim)
    fold_block_len = key_blocks.shape[2]

    def advance(carried, block_item):
        key_block, value_block, block_index = block_item
        key_first = block_index * fold_block_len

        def compute_block(current):
            query_acc, key_acc, value_acc = current
            scores, allowed = block_scores(key_block, key_first)
            probabilities = jnp.where(allowed, jnp.exp(scores - log_total[..., None]), 0.0)
            value_part = jnp.einsum(
                "skrj,skrd->sjkd",
                probabilities.astype(jnp.bfloat16),
                grouped_grad,
                preferred_element_type=jnp.float32,
            )
            prob_grad = jnp.einsum(
                "skrd,sjkd->skrj", grouped_grad, value_block, preferred_element_type=jnp.float32
            )
            score_grad = (probabilities * (prob_grad - row_delta[..., None])).astype(jnp.bfloat16)
            query_acc = (
                query_acc
                + jnp.einsum(
                    "skrj,sjkd->skrd", score_grad, key_block, preferred_element_type=jnp.float32
                )
                * score_scale
            )
            key_part = (
                jnp.einsum(
                    "skrj,skrd->sjkd", score_grad, queries, preferred_element_type=jnp.float32
                )
                * score_scale
            )
            key_acc = add_rows(
                key_acc, key_part.reshape(seq_count, fold_block_len, kv_heads * head_dim), key_first
            )
            value_acc = add_rows(
                value_acc,
                value_part.reshape(seq_count, fold_block_len, kv_heads * head_dim),
                key_first,
            )
            return (query_acc, key_acc, value_acc)

        return (lax.cond(key_first <= last_query, compute_block, unchanged, carried), None)

    running, _ = lax.scan(
        advance,
        running,
        (key_blocks, value_blocks, jnp.arange(key_blocks.shape[0], dtype=jnp.int32)),
    )
    query_acc, key_acc, value_acc = running
    key_sum, value_sum = (
        lax.psum_scatter(
            key_acc.astype(jnp.bfloat16), "wide", scatter_dimension=1, tiled=True
        ).astype(jnp.float32),
        lax.psum_scatter(
            value_acc.astype(jnp.bfloat16), "wide", scatter_dimension=1, tiled=True
        ).astype(jnp.float32),
    )
    query_back = (
        query_acc.reshape(seq_count, kv_heads, group_size, span_len, head_dim)
        .transpose(0, 3, 1, 2, 4)
        .reshape(row_count, head_count, head_dim)
    )
    query_grad = (
        rotate(query_back, token_pos, -1.0)
        .reshape(row_count, head_count * head_dim)
        .astype(jnp.bfloat16)
    )
    key_grad = (
        rotate(key_sum.reshape(row_count, kv_heads, head_dim), token_pos, -1.0)
        .reshape(row_count, kv_heads * head_dim)
        .astype(jnp.bfloat16)
    )
    value_grad = value_sum.reshape(row_count, kv_heads * head_dim).astype(jnp.bfloat16)
    grad_query = over_rows(first_norm, query_grad)
    grad_key = over_rows(first_norm, key_grad)
    grad_value = over_rows(first_norm, value_grad)
    input_norm_grad = (
        against(query_grad, query_w) + against(key_grad, key_w) + against(value_grad, value_w)
    )
    grad_gain_one = jnp.sum(input_norm_grad * inputs * inverse_one, axis=0)
    scaled_one = gain_one.astype(jnp.float32) * input_norm_grad
    input_grad = (
        middle_grad
        + inverse_one * scaled_one
        - inputs
        * (inverse_one * inverse_one * inverse_one)
        * jnp.mean(scaled_one * inputs, axis=-1, keepdims=True)
    )
    gain_one_share, query_share, key_share, value_share, out_share = (
        lax.psum_scatter(grad_gain_one, ("wide", "narrow"), scatter_dimension=0, tiled=True),
        lax.psum_scatter(grad_query, ("wide", "narrow"), scatter_dimension=0, tiled=True),
        lax.psum_scatter(grad_key, ("wide", "narrow"), scatter_dimension=0, tiled=True),
        lax.psum_scatter(grad_value, ("wide", "narrow"), scatter_dimension=0, tiled=True),
        lax.psum_scatter(grad_out, ("wide", "narrow"), scatter_dimension=0, tiled=True),
    )
    return (
        output.reshape(seq_count, span_len, model_width),
        input_grad.astype(jnp.bfloat16).reshape(seq_count, span_len, model_width),
        gain_one_share,
        query_share,
        key_share,
        value_share,
        out_share,
        gain_two_share,
        gate_share,
        up_share,
        down_share,
    )


def line_body(
    tokens,
    attn_gain,
    w_query,
    w_key,
    w_value,
    w_out,
    mlp_gain,
    w_gate,
    w_up,
    w_down,
    keep_mask,
    group_ids,
    positions,
    exit_scale,
    out_grad,
):
    f32 = jnp.float32
    bf16 = jnp.bfloat16
    _, span_len, model_width = tokens.shape
    line = lax.axis_size("z")
    rows_each = w_query.shape[0]
    q_cols = HEADS // line * HD

    group_match = group_ids[0][:, None] == jnp.arange(exit_scale.shape[0], dtype=jnp.int32)[None, :]
    token_scale = jnp.sum(jnp.where(group_match, exit_scale[None, :], 0.0), axis=1)
    freqs = 10000.0 ** (-2.0 * jnp.arange(HD // 2, dtype=f32) / HD)
    small = jnp.stack(
        [
            positions[0].astype(f32),
            token_scale,
            jnp.concatenate([freqs, freqs]),
            jnp.broadcast_to(keep_mask.astype(f32), (span_len,)),
        ]
    )
    small = jnp.broadcast_to(small[:, None], (4, 8, span_len))

    core = lax.axis_index("c")
    gain_row = jnp.zeros((q_cols + 2 * HD,), bf16)
    gain_row = lax.dynamic_update_slice_in_dim(gain_row, attn_gain, core * rows_each, 0)
    gain_row = lax.dynamic_update_slice_in_dim(gain_row, mlp_gain, HD + core * rows_each, 0)
    gain_rows = jnp.broadcast_to(gain_row, (16, gain_row.shape[0]))
    (
        x_blocks,
        near_w,
        gain_all,
        first_norm,
        queries,
        both_kv,
        log_total,
        turns,
        attended_rows,
        ff_w,
        out_w,
        mixed_blocks,
    ) = forward_call(
        small,
        tokens[0],
        out_grad[0],
        gain_rows,
        (w_query, w_key, w_value, w_gate, w_up, w_out),
        line,
    )
    middle, norm_grad, carry, mixed_own, grad_down, grad_ff, ff_half = mlp_call(
        small,
        gain_all,
        mixed_blocks,
        x_blocks,
        attended_rows,
        out_w,
        ff_w,
        w_down,
        line,
    )
    grad_down = grad_down.astype(f32)
    output, token_grad, ff_back, out_back, qkv_back = backward_call(
        (small, gain_all, middle, norm_grad),
        (tokens[0], out_grad[0], carry, mixed_own),
        (queries, both_kv, log_total, turns),
        out_w,
        attended_rows,
        near_w,
        first_norm,
        grad_ff,
        ff_half,
        line,
    )
    ff_back = ff_back.astype(f32)
    qkv_back = qkv_back.astype(f32)
    grad_out = jnp.sum(out_back.astype(f32), axis=0)
    heads_end, keys_end = w_query.shape[1], w_query.shape[1] + w_key.shape[1]
    grad_query = qkv_back[:, :heads_end]
    grad_key = qkv_back[:, heads_end:keys_end]
    grad_value = qkv_back[:, keys_end:]
    grad_gate = ff_back[:, : w_gate.shape[1]]
    grad_up = ff_back[:, w_gate.shape[1] :]

    def gain_grad(pairs, gain):
        total = sum(jnp.sum(weight.astype(f32) * grad, axis=1) for weight, grad in pairs)
        return total / gain.astype(f32)

    return (
        output[None],
        token_grad[None],
        gain_grad([(w_query, grad_query), (w_key, grad_key), (w_value, grad_value)], attn_gain),
        grad_query,
        grad_key,
        grad_value,
        grad_out,
        gain_grad([(w_gate, grad_gate), (w_up, grad_up)], mlp_gain),
        grad_gate,
        grad_up,
        grad_down,
    )


def solution(mesh):
    wide, narrow = mesh.shape["wide"], mesh.shape["narrow"]
    if wide == 2 * KVH and narrow == 4:
        mesh = Mesh(mesh.devices.reshape(wide // 2, 2, 2, 2), ("z", "x", "y", "c"))
        body, wide, narrow = line_body, ("z", "x"), ("y", "c")
    else:
        body, wide, narrow = general_body, ("wide",), ("narrow",)
    token_spec = P(narrow, wide, None)
    id_spec = P(narrow, wide)
    gain_spec = P(wide + narrow)
    weight_spec = P(wide + narrow, None)
    return jax.shard_map(
        body,
        mesh=mesh,
        in_specs=(
            token_spec,
            gain_spec,
            weight_spec,
            weight_spec,
            weight_spec,
            weight_spec,
            gain_spec,
            weight_spec,
            weight_spec,
            weight_spec,
            P(narrow),
            id_spec,
            id_spec,
            P(),
            token_spec,
        ),
        out_specs=(
            token_spec,
            token_spec,
            gain_spec,
            weight_spec,
            weight_spec,
            weight_spec,
            weight_spec,
            gain_spec,
            weight_spec,
            weight_spec,
            weight_spec,
        ),
        check_vma=False,
    )
```

```python
import functools
import math

import jax
import jax.numpy as jnp
from jax import lax
from jax.experimental import pallas as pl
from jax.experimental.pallas import tpu as pltpu
from jax.sharding import Mesh
from jax.sharding import PartitionSpec as P

HEADS = 16
KVH = 4
HD = 128


epsilon = 1e-05


def rotate(vectors, token_pos, direction):
    half_size = vectors.shape[-1] // 2
    freqs = 10000.0 ** (-2.0 * jnp.arange(half_size, dtype=jnp.float32) / vectors.shape[-1])
    angles = token_pos.astype(jnp.float32)[:, None] * freqs[None, :]
    cosine = jnp.cos(angles)[:, None, :]
    sine = direction * jnp.sin(angles)[:, None, :]
    first_half = vectors[..., :half_size]
    second_half = vectors[..., half_size:]
    return jnp.concatenate(
        [first_half * cosine - second_half * sine, second_half * cosine + first_half * sine],
        axis=-1,
    )


def split_blocks(piece_arr, seq_count, kv_heads, head_dim):
    piece_len = piece_arr.shape[1]
    block_len = math.gcd(piece_len, 512)
    shaped = piece_arr.reshape(seq_count, piece_len // block_len, block_len, kv_heads, head_dim)
    return shaped.transpose(1, 0, 2, 3, 4)


def add_rows(whole_arr, update, first_row):
    current = lax.dynamic_slice_in_dim(whole_arr, first_row, update.shape[1], 1)
    return lax.dynamic_update_slice_in_dim(whole_arr, current + update, first_row, 1)


def over_rows(left, right):
    return lax.dot_general(
        left, right, (((0,), (0,)), ((), ())), preferred_element_type=jnp.float32
    )


def against(left, right):
    return lax.dot_general(
        left, right, (((1,), (1,)), ((), ())), preferred_element_type=jnp.float32
    )


def unchanged(carried):
    return carried


MESH = pl.DeviceIdType.MESH
AXES = ("z", "x", "y", "c")


class Links:
    def __init__(self, send_sems, recv_sems, line):
        self.send_sems, self.recv_sems, self.line = send_sems, recv_sems, line
        self.z, self.x, self.y, self.c = (lax.axis_index(name) for name in AXES)
        self.slot = self.x * 4 + self.y * 2 + self.c
        self.used = 0
        self.sent = []

    def device(self, to):
        if to == "x":
            return (self.z, 1 - self.x, self.y, self.c)
        if to == "y":
            return (self.z, self.x, 1 - self.y, self.c)
        if to == "c":
            return (self.z, self.x, self.y, 1 - self.c)
        return (self.along(to), self.x, self.y, self.c)

    def along(self, step):
        return lax.rem(self.z + step + self.line, self.line)

    def other(self, to):
        slot = self.slot
        for name in to:
            bit = {"x": 4, "y": 2, "c": 1}[name]
            here = {"x": self.x, "y": self.y, "c": self.c}[name]
            slot = slot + bit * (1 - 2 * here)
        return slot

    def meet(self, targets):
        barrier = pltpu.get_barrier_semaphore()
        for to in targets:
            pl.semaphore_signal(barrier, inc=1, device_id=self.device(to), device_id_type=MESH)
        pl.semaphore_wait(barrier, len(targets))

    def send(self, source, target, to):
        copy = pltpu.make_async_remote_copy(
            src_ref=source,
            dst_ref=target,
            send_sem=self.send_sems.at[self.used],
            recv_sem=self.recv_sems.at[self.used],
            device_id=self.device(to),
            device_id_type=MESH,
        )
        copy.start()
        self.used += 1
        self.sent.append(copy)
        return copy

    def keep(self, source, target):
        copy = pltpu.make_async_copy(source, target, self.send_sems.at[self.used])
        copy.start()
        self.used += 1
        return copy

    def finish(self):
        for copy in self.sent:
            copy.wait_send()


class NearGather:
    def __init__(self, links, slot):
        self.links, self.slot = links, slot
        self.got = {}

    def offer(self, block, source):
        target = self.slot(block, self.links.slot)
        for to in ("x", "y", "c"):
            self.got[block, to] = self.links.send(source, target, to)

    def relay(self, block, first):
        links = self.links
        for to, then in (("x", "y"), ("y", "x")):
            self.got[block, to].wait_recv()
            place = self.slot(block, links.other(to))
            self.got[block, to + "c"] = links.send(place, place, "c")
            if to == first:
                self.got[block, "xy"] = links.send(place, place, then)

    def close(self, block):
        self.got[block, "xy"].wait_recv()
        place = self.slot(block, self.links.other("xy"))
        self.got[block, "xyc"] = self.links.send(place, place, "c")

    def wait(self, blocks):
        for block in blocks:
            for to in ("c", "xc", "yc", "xyc"):
                self.got[block, to].wait_recv()


class RingGather:
    def __init__(self, links, rows, origin, place, pieces=4):
        self.links, self.origin, self.place = links, origin, place
        self.pieces, self.rows = pieces, rows // pieces
        self.last = [None] * pieces

    def step(self, number):
        if number > 0:
            for copy in self.last:
                copy.wait_recv()
        if number == self.links.line - 1:
            return
        for piece in range(self.pieces):
            way = 1 if piece < self.pieces // 2 else -1
            rows = pl.ds(piece * self.rows, self.rows)
            block = self.links.along(-way * number)
            place = self.place(block, rows)
            source = self.origin(rows) if number == 0 else place
            self.last[piece] = self.links.send(source, place, way)


def column_of(row):
    size = row.shape[1]
    down = lax.broadcasted_iota(jnp.int32, (size, size), 0)
    across = lax.broadcasted_iota(jnp.int32, (size, size), 1)
    values = jnp.where(down == across, jnp.broadcast_to(row, (size, size)), 0.0)
    return jnp.sum(values, axis=1, keepdims=True)


def first_kernel(
    line,
    small_ref,
    x_ref,
    grad_ref,
    gain_rows_ref,
    query_w_ref,
    key_w_ref,
    value_w_ref,
    gate_w_ref,
    up_w_ref,
    out_ref,
    xs_ref,
    weight_ref,
    gain_ref,
    norm_ref,
    query_ref,
    kv_ref,
    peak_ref,
    turn_ref,
    atts_ref,
    ffs_ref,
    outs_ref,
    mix_ref,
    x_all,
    grad,
    mix,
    places,
    weights,
    gains,
    norm,
    turns,
    flat,
    query,
    kv,
    peak,
    att,
    send_sems,
    recv_sems,
):
    f32, bf16 = jnp.float32, jnp.bfloat16
    links = Links(send_sems, recv_sems, line)
    far = [1, line - 1] + list(range(2, line - 1))
    links.meet(["x", "y", "c"] + far)
    here = links.slot
    span_len, width = x_ref.shape
    group_len = line * span_len
    rows_each = gate_w_ref.shape[0]
    q_cols = query.shape[1]
    ff_cols = gate_w_ref.shape[1] // line
    heads = q_cols // HD
    local = []

    near = NearGather(links, lambda block, place: weights.at[links.along(-block), place])
    far_ff = NearGather(links, lambda block, place: ffs_ref.at[links.along(-block), place])
    far_out = NearGather(links, lambda block, place: outs_ref.at[links.along(-block), place])
    ring = RingGather(
        links, span_len, lambda rows: x_ref.at[rows], lambda block, rows: x_all.at[block, rows]
    )
    place_ref = small_ref.at[0]

    def columns(weight, block, size):
        return weight.at[:, pl.ds(pl.multiple_of(block * size, HD), size)]

    def near_pieces(block):
        target = weights.at[links.z, here]
        rows = pl.ds(0, rows_each)
        return [
            (columns(query_w_ref, block, q_cols), target.at[rows, pl.ds(0, q_cols)]),
            (columns(key_w_ref, block, HD), target.at[rows, pl.ds(q_cols, HD)]),
            (columns(value_w_ref, block, HD), target.at[rows, pl.ds(q_cols + HD, HD)]),
            (gain_rows_ref, target.at[pl.ds(rows_each, 16)]),
        ]

    def ff_pieces(block):
        target = ffs_ref.at[links.z, here]
        return [
            (columns(gate_w_ref, block, ff_cols), target.at[:, pl.ds(0, ff_cols)]),
            (columns(up_w_ref, block, ff_cols), target.at[:, pl.ds(ff_cols, ff_cols)]),
        ]

    def turn_out(pieces):
        return {k: [links.send(*piece, k) for piece in pieces(links.along(k))] for k in far}

    def arrived(copies):
        for copy in copies:
            copy.wait_recv()

    own = [links.keep(*piece) for piece in near_pieces(links.z)]
    own_ff = [links.keep(*piece) for piece in ff_pieces(links.z)]
    turned = turn_out(near_pieces)
    placed = [links.send(place_ref, places.at[links.z], k) for k in far]
    turned_ff = turn_out(ff_pieces)
    for copy in own:
        copy.wait()
    near.offer(0, weights.at[links.z, here])
    for copy in own_ff:
        copy.wait()
    far_ff.offer(0, ffs_ref.at[links.z, here])
    own = [
        links.keep(x_ref, x_all.at[links.z]),
        links.keep(place_ref, places.at[links.z]),
        links.keep(grad_ref, grad),
    ]
    local.append(links.keep(out_ref, outs_ref.at[links.z, here]))

    def move_out(k):
        moved.wait_recv()
        block = outs_ref.at[links.along(-k), here]
        onward = links.send(block, block, 1) if k < line - 1 else None
        far_out.offer(k, block)
        return onward

    for k in far:
        arrived(turned[k])
        near.offer(k, weights.at[links.along(-k), here])
    ring.step(0)
    for k in [0] + far:
        near.relay(k, "x" if k < line // 2 else "y")
    for k in far:
        arrived(turned_ff[k])
        far_ff.offer(k, ffs_ref.at[links.along(-k), here])
    ring.step(1)
    for k in [0] + far:
        near.close(k)
    far_ff.relay(0, "x")
    ring.step(2)
    moved = links.send(out_ref, outs_ref.at[links.z, here], 1)
    far_out.offer(0, out_ref)
    for copy in own:
        copy.wait()
    for copy in placed:
        copy.wait_recv()

    lane = lax.broadcasted_iota(jnp.int32, (span_len, HD), 1)
    for block in range(line):
        angles = column_of(places[block, 0:1]) * small_ref[2, 0:1]
        rows = slice(block * span_len, (block + 1) * span_len)
        sine = jnp.sin(angles)
        turns[0, rows] = jnp.cos(angles)
        turns[1, rows] = jnp.where(lane < HD // 2, -sine, sine)
    local.append(links.keep(turns, turn_ref))
    token_scale = column_of(small_ref[1, 0:1])
    for low in range(0, span_len, 16):
        rows = slice(low, low + 16)
        upstream = grad[rows].astype(f32) * token_scale[rows]
        mix[rows] = (upstream * small_ref[3, 0:1, 0:1]).astype(bf16)
    local.append(links.keep(mix, mix_ref))
    near.wait(range(line))
    for index in range(line * 4):
        z, q = divmod(index, 4)
        for which in range(2):
            lanes = slice(which * HD, (which + 1) * HD)
            both = [weights[z, 2 * q + c, rows_each : rows_each + 16, lanes].astype(f32) for c in range(2)]
            gains[which, :, index * HD : (index + 1) * HD] = both[0] + both[1]
    local.append(links.keep(weights, weight_ref))
    local.append(links.keep(gains, gain_ref))
    far_ff.relay(far[0], "x")
    ring.step(3)
    local.append(links.keep(x_all, xs_ref))

    def normalise(index, carry):
        block = index // (span_len // 16)
        rows = pl.ds(pl.multiple_of(lax.rem(index, span_len // 16) * 16, 16), 16)
        values = x_all[block, rows].astype(f32)
        inverse = lax.rsqrt(jnp.mean(values * values, axis=-1, keepdims=True) + epsilon)
        target = pl.ds(pl.multiple_of(index * 16, 16), 16)
        norm[target] = (values * inverse * gains[0]).astype(bf16)
        return carry

    lax.fori_loop(0, group_len // 16, normalise, 0)
    local.append(links.keep(norm, norm_ref))

    def project(low, high):
        step = group_len // 2
        for part in range(2):
            rows = slice(part * step, (part + 1) * step)
            total = None
            for z in range(line):
                weight = weights[z, :, :rows_each, low:high].reshape(8 * rows_each, high - low)
                term = jnp.dot(
                    norm[rows, z * 8 * rows_each : (z + 1) * 8 * rows_each],
                    weight,
                    preferred_element_type=f32,
                )
                total = term if total is None else total + term
            flat[rows, low:high] = total

    def turn(values, rows):
        return values * turns[0, rows] + pltpu.roll(values, HD // 2, 1) * turns[1, rows]

    project(q_cols, q_cols + 2 * HD)
    for block in range(line):
        rows = slice(block * span_len, (block + 1) * span_len)
        kv[0, rows, :HD] = turn(flat[rows, q_cols : q_cols + HD], rows).astype(bf16)
        kv[0, rows, HD:] = flat[rows, q_cols + HD : q_cols + 2 * HD].astype(bf16)
    exchange = links.send(kv.at[0], kv.at[1], "x")
    project(0, q_cols)
    for block in range(line):
        rows = slice(block * span_len, (block + 1) * span_len)
        for head in range(heads):
            lanes = slice(head * HD, (head + 1) * HD)
            query[rows, lanes] = turn(flat[rows, lanes], rows).astype(bf16)
    local.append(links.keep(query, query_ref))
    for k in far[1:]:
        far_ff.relay(k, "x" if k < line // 2 else "y")
    exchange.wait_recv()
    moved = move_out(1)
    local.append(links.keep(kv, kv_ref))

    scale = 1.0 / math.sqrt(HD)
    peak[...] = jnp.zeros_like(peak)

    def attend(head, carry):
        lanes = pl.ds(pl.multiple_of(head * HD, HD), HD)
        for block in range(line):
            rows = slice(block * span_len, (block + 1) * span_len)
            reach = (block + 1) * span_len
            part = query[rows, lanes]
            row = lax.broadcasted_iota(jnp.int32, (span_len, reach), 0) + block * span_len
            column = lax.broadcasted_iota(jnp.int32, (span_len, reach), 1)
            allowed = (column <= row, column < (block + links.x) * span_len)
            scores = []
            for half in range(2):
                score = lax.dot_general(
                    part, kv[half, :reach, :HD], (((1,), (1,)), ((), ())), preferred_element_type=f32
                )
                scores.append(jnp.where(allowed[half], score * scale, -1e30))
            top = jnp.maximum(
                jnp.max(scores[0], axis=-1, keepdims=True), jnp.max(scores[1], axis=-1, keepdims=True)
            )
            total, mixed = None, None
            for half in range(2):
                weight = jnp.exp(scores[half] - top)
                count = jnp.sum(weight, axis=-1, keepdims=True)
                term = jnp.dot(weight.astype(bf16), kv[half, :reach, HD:], preferred_element_type=f32)
                total = count if total is None else total + count
                mixed = term if mixed is None else mixed + term
            att[rows, lanes] = (mixed / total).astype(bf16)
            spot = lax.broadcasted_iota(jnp.int32, (span_len, HD), 1) == head
            peak[rows] = jnp.where(spot, top + jnp.log(total), peak[rows])
        return carry

    lax.fori_loop(0, heads, attend, 0)
    local.append(links.keep(peak, peak_ref))

    def place(block, rows):
        return atts_ref.at[rows, pl.ds(pl.multiple_of(block * q_cols, q_cols), q_cols)]

    att_ring = RingGather(links, group_len, lambda rows: att.at[rows], place)
    local.append(links.keep(att, place(links.z, pl.ds(0, group_len))))
    att_ring.step(0)
    for k in [0] + far:
        far_ff.close(k)
    far_out.relay(0, "x")
    moved = move_out(2)
    far_out.relay(1, "x")
    att_ring.step(1)
    for k in range(3, line):
        moved = move_out(k)
    far_out.relay(2, "y")
    att_ring.step(2)
    for k in range(3, line):
        far_out.relay(k, "y")
    for k in range(line):
        far_out.close(k)
    att_ring.step(3)
    far_out.wait(range(line))
    far_ff.wait(range(line))
    links.finish()
    for copy in local:
        copy.wait()


def add_rows_of(target, values, count):
    def add(index, carry):
        rows = pl.ds(pl.multiple_of(index * 16, 16), 16)
        target[rows] = target[rows] + values[rows]
        return carry

    lax.fori_loop(0, count // 16, add, 0)


class NearSum:
    def __init__(self, links, source, own, from_core, from_first, from_second, first, in_place=False):
        self.links, self.source, self.own, self.first = links, source, own, first
        self.in_place = in_place
        self.from_core, self.from_first, self.from_second = from_core, from_first, from_second

    def start(self):
        links = self.links
        if not self.in_place:
            self.local = links.keep(self.source(links.c), self.own)
        self.copy = links.send(self.source(1 - links.c), self.from_core, "c")

    def add(self, target, values):
        add_rows_of(target, values, target.shape[0])

    def core_done(self):
        links = self.links
        self.copy.wait_recv()
        if not self.in_place:
            self.local.wait()
        for x in range(2):
            for y in range(2):
                self.add(self.own.at[x, y], self.from_core.at[x, y])
        if self.first == "x":
            self.copy = links.send(self.own.at[1 - links.x], self.from_first, "x")
        else:
            self.copy = links.send(self.own.at[:, 1 - links.y], self.from_first, "y")

    def first_done(self):
        links = self.links
        self.copy.wait_recv()
        for other in range(2):
            place = (links.x, other) if self.first == "x" else (other, links.y)
            self.add(self.own.at[place], self.from_first.at[other])
        if self.first == "x":
            self.copy = links.send(self.own.at[links.x, 1 - links.y], self.from_second, "y")
        else:
            self.copy = links.send(self.own.at[1 - links.x, links.y], self.from_second, "x")

    def second_done(self):
        self.copy.wait_recv()
        total = self.own.at[self.links.x, self.links.y]
        self.add(total, self.from_second)
        return total


def sum_space(blocks, rows, columns):
    shape = (rows, columns)
    return [
        pltpu.VMEM((blocks, 2, 2) + shape, jnp.bfloat16),
        pltpu.VMEM((blocks, 2, 2) + shape, jnp.bfloat16),
        pltpu.VMEM((blocks, 2) + shape, jnp.bfloat16),
        pltpu.VMEM((blocks,) + shape, jnp.bfloat16),
    ]


class RingSum:
    def __init__(self, links, parts, total, got, pieces=4):
        self.links, self.parts, self.total, self.got = links, parts, total, got
        self.pieces, self.last = pieces, [None] * pieces
        self.rows = parts.shape[1] // pieces

    def step(self, number):
        links = self.links
        for piece in range(self.pieces):
            way = 1 if piece < self.pieces // 2 else -1
            block = links.along(-way * (number + 1))
            where = pl.ds(piece * self.rows, self.rows)
            if number == 0:
                source = self.parts.at[block, where]
            else:
                self.last[piece].wait_recv()
                total = self.got[number - 1, where].astype(jnp.float32) + self.parts[
                    block, where
                ].astype(jnp.float32)
                if number == links.line - 1:
                    self.total[where] = total
                    continue
                self.parts[block, where] = total.astype(self.parts.dtype)
                source = self.parts.at[block, where]
            self.last[piece] = links.send(source, self.got.at[number, where], way)


def link_call(kernel, collective_id, copies, shapes, arguments, spaces=None, scratch=(), vmem=16):
    any_space = pl.BlockSpec(memory_space=pl.ANY)
    near_space = pl.BlockSpec(memory_space=pltpu.VMEM)
    many = isinstance(shapes, tuple)
    if spaces is None:
        spaces = "h" * (len(arguments) + (len(shapes) if many else 1))
    specs = [near_space if space == "v" else any_space for space in spaces]
    return pl.pallas_call(
        kernel,
        out_shape=shapes,
        in_specs=specs[: len(arguments)],
        out_specs=tuple(specs[len(arguments) :]) if many else specs[-1],
        scratch_shapes=list(scratch)
        + [pltpu.SemaphoreType.DMA((copies,)), pltpu.SemaphoreType.DMA((copies,))],
        compiler_params=pltpu.CompilerParams(
            collective_id=collective_id, has_side_effects=True, vmem_limit_bytes=vmem * 2**20
        ),
    )(*arguments)


def forward_call(small, tokens, out_grad, gain_rows, weights, line):
    span_len, width = tokens.shape
    group_len = line * span_len
    rows_each, qkv_cols = weights[0].shape[0], gain_rows.shape[1]
    q_cols = qkv_cols - 2 * HD
    both_cols = 2 * weights[3].shape[1] // line
    f32, bf16 = jnp.float32, jnp.bfloat16
    near = (line, 8, rows_each + 16, qkv_cols)
    outs = (
        ((line, span_len, width), bf16),
        (near, bf16),
        ((2, 16, width), f32),
        ((group_len, width), bf16),
        ((group_len, q_cols), bf16),
        ((2, group_len, 2 * HD), bf16),
        ((group_len, HD), f32),
        ((2, group_len, HD), f32),
        ((group_len, line * q_cols), bf16),
        ((line, 8, rows_each, both_cols), bf16),
        ((line, 8, rows_each, width), bf16),
        ((span_len, width), bf16),
    )
    return link_call(
        functools.partial(first_kernel, line),
        0,
        208,
        tuple(jax.ShapeDtypeStruct(*out) for out in outs),
        (small, tokens, out_grad, gain_rows) + weights,
        "v" + "h" * 21,
        scratch=[
            pltpu.VMEM((line, span_len, width), bf16),
            pltpu.VMEM((span_len, width), bf16),
            pltpu.VMEM((span_len, width), bf16),
            pltpu.VMEM((line,) + small.shape[1:], f32),
            pltpu.VMEM(near, bf16),
            pltpu.VMEM((2, 16, width), f32),
            pltpu.VMEM((group_len, width), bf16),
            pltpu.VMEM((2, group_len, HD), f32),
            pltpu.VMEM((group_len, qkv_cols), f32),
            pltpu.VMEM((group_len, q_cols), bf16),
            pltpu.VMEM((2, group_len, 2 * HD), bf16),
            pltpu.VMEM((group_len, HD), f32),
            pltpu.VMEM((group_len, q_cols), bf16),
        ],
        vmem=63,
    )


def mlp_kernel(
    line,
    cuts,
    small_ref,
    gain_ref,
    mix_ref,
    xs_ref,
    atts_ref,
    out_ref,
    ff_ref,
    down_ref,
    middle_ref,
    total_ref,
    output_ref,
    sum_ref,
    grad_ff_ref,
    ff_half_ref,
    big,
    ff,
    down,
    norm,
    parts,
    mixed,
    gate_up,
    hidden,
    both_grad,
    got,
    mixed_parts,
    mixed_got,
    mixed_total,
    *scratch,
):
    f32, bf16 = jnp.float32, jnp.bfloat16
    space, (send_sems, recv_sems) = scratch[:-2], scratch[-2:]
    links = Links(send_sems, recv_sems, line)
    links.meet(["x", "y", "c", 1, line - 1])
    far = [1, line - 1] + list(range(2, line - 1))
    span_len, width = mix_ref.shape
    group_len = line * span_len
    ff_cols = hidden.shape[1]
    block_rows = width // line
    rows_each = block_rows // 8
    chunk = 2 * HD
    mix_ring = RingGather(
        links, span_len, lambda rows: mix_ref.at[rows], lambda block, rows: mixed.at[block, rows]
    )
    mix_ring.step(0)
    stay = links.keep(mix_ref, mixed.at[links.z])
    early = [
        links.keep(out_ref, big),
        links.keep(atts_ref, norm),
        links.keep(xs_ref, parts),
    ]
    late = [links.keep(ff_ref, ff)]
    down_rows = down_ref.shape[0]

    def down_place(block, place):
        low, high = cuts[block]
        return down.at[pl.ds(pl.multiple_of(place * down_rows + low, 16), high - low)]

    near = NearGather(links, down_place)
    for block, (low, high) in enumerate(cuts):
        rows = down_ref.at[pl.ds(low, high - low)]
        late.append(links.keep(rows, down_place(block, links.slot)))
        near.offer(block, rows)
    ring = RingSum(links, parts, total_ref, got)
    mixed_ring = RingSum(links, mixed_parts, mixed_total, mixed_got)
    items = []
    ff_items = []
    for index, k in enumerate(far[:2]):
        block = links.along(k)
        core, first, second = space[:3]
        ff_items.append(
            NearSum(
                links,
                lambda c, block=block: ff.at[block, :, :, c],
                ff.at[block, :, :, links.c],
                core.at[index],
                first.at[index],
                second.at[index],
                "xy"[index % 2],
                True,
            )
        )
    for index, (low, high) in enumerate(cuts):
        rows = pl.ds(low, high - low)
        core, first, second = space[3 * index + 3 : 3 * index + 6]
        items.append(
            NearSum(
                links,
                lambda c, rows=rows: big.at[:, :, c, rows],
                big.at[:, :, links.c, rows],
                core.at[0],
                first.at[0],
                second.at[0],
                "xy"[index % 2],
                True,
            )
        )
    for copy in early:
        copy.wait()

    half = group_len // 2
    out_rows = width // 8
    for part in range(2):
        low = part * half
        for column in range(4):
            lanes = slice(column * width // 4, (column + 1) * width // 4)
            value = None
            for k in range(8):
                term = jnp.dot(
                    norm[low : low + half, k * out_rows : (k + 1) * out_rows],
                    big[k // 4, k // 2 % 2, k % 2, :, lanes],
                    preferred_element_type=f32,
                )
                value = term if value is None else value + term
            gate_up[:half, lanes] = value * small_ref[3, 0:1, 0:1]

        def normalise(index, carry, low=low):
            block = (low // 16 + index) // (span_len // 16)
            rows = pl.ds(pl.multiple_of(index * 16, 16), 16)
            inside = pl.ds(pl.multiple_of(lax.rem(index, span_len // 16) * 16, 16), 16)
            values = parts[block, inside].astype(f32) + gate_up[rows, :width]
            gate_up[rows, :width] = values
            inverse = lax.rsqrt(jnp.mean(values * values, axis=-1, keepdims=True) + epsilon)
            target = pl.ds(pl.multiple_of(low + index * 16, 16), 16)
            norm[target] = (values * inverse * gain_ref[1]).astype(bf16)
            return carry

        lax.fori_loop(0, half // 16, normalise, 0)

        @pl.when(links.z // (line // 2) == part)
        def _():
            where = pl.multiple_of(lax.rem(links.z, line // 2) * span_len, span_len)
            middle_ref[...] = gate_up[pl.ds(where, span_len), :width]
        if part == 0:
            mix_ring.step(1)

    for block in range(2):
        near.relay(block, "xy"[block])
    for copy in late:
        copy.wait()

    def columns_of(lanes, size):
        return ff[:, :, :, :, :, lanes].reshape(width, size)

    def forward(low, size):
        gates, ups = pl.ds(low, size), pl.ds(low + ff_cols, size)
        gate = jnp.dot(norm[...], columns_of(gates, size), preferred_element_type=f32)
        gate_up[:, gates] = gate
        swish = gate * jax.nn.sigmoid(gate)
        up = jnp.dot(norm[...], columns_of(ups, size), preferred_element_type=f32)
        gate_up[:, ups] = up
        hidden[:, gates] = (swish * up).astype(bf16)

    def backward(low, size):
        gates, ups = pl.ds(low, size), pl.ds(low + ff_cols, size)
        grad = lax.dot_general(
            mixed[...].reshape(group_len, width),
            down[gates],
            (((1,), (1,)), ((), ())),
            preferred_element_type=f32,
        )
        gate, up = gate_up[:, gates], gate_up[:, ups]
        sigmoid = jax.nn.sigmoid(gate)
        both_grad[:, gates] = (grad * up * sigmoid * (1.0 + gate * (1.0 - sigmoid))).astype(bf16)
        both_grad[:, ups] = (grad * (gate * sigmoid)).astype(bf16)

    def over_chunks(work, extent):
        def one(index, carry):
            work(pl.multiple_of(index * chunk, chunk), chunk)
            return carry

        lax.fori_loop(0, extent // chunk, one, 0)
        if extent % chunk:
            work(extent // chunk * chunk, extent % chunk)

    over_chunks(forward, ff_cols)
    mix_ring.step(2)
    for block in range(2):
        near.close(block)
    near.wait(range(2))

    def mixed_part(low, size):
        lanes = pl.ds(low, size)
        value = jnp.dot(hidden[...], down[:, lanes], preferred_element_type=f32).astype(bf16)
        mixed_parts[:, :, lanes] = value.reshape(line, span_len, size)

    over_chunks(mixed_part, width)
    mixed_ring.step(0)
    stay.wait()
    mix_ring.step(3)
    hidden_rows = hidden[...].T

    def down_part(low, size):
        lanes = pl.ds(low, size)
        value = jnp.dot(
            hidden_rows,
            mixed[:, :, lanes].reshape(group_len, size),
            preferred_element_type=f32,
        ).astype(bf16)
        big[:, :, :, : cuts[-1][1], lanes] = value.reshape(2, 2, 2, cuts[-1][1], size)

    over_chunks(down_part, width)
    for item in items:
        item.start()
    over_chunks(backward, ff_cols)
    mixed_ring.step(1)
    for item in items:
        item.core_done()

    def norm_part(index, carry):
        size = 4 * rows_each
        weight = ff[index // 2, lax.rem(index, 2)].reshape(size, 2 * ff_cols)
        value = lax.dot_general(
            both_grad[...], weight, (((1,), (1,)), ((), ())), preferred_element_type=f32
        ).astype(bf16)
        lanes = pl.ds(pl.multiple_of(index * size, size), size)
        parts[:, :, lanes] = value.reshape(line, span_len, size)
        return carry

    lax.fori_loop(0, 2 * line, norm_part, 0)
    ring.step(0)

    def ff_block(block):
        norm_rows = norm[:, pl.ds(pl.multiple_of(block * block_rows, block_rows), block_rows)].T

        def ff_part(low, size):
            lanes = pl.ds(low, size)
            value = jnp.dot(norm_rows, both_grad[:, lanes], preferred_element_type=f32)
            ff[block, :, :, :, :, lanes] = value.astype(bf16).reshape(2, 2, 2, rows_each, size)

        over_chunks(ff_part, 2 * ff_cols)

    for item, k in zip(ff_items, far):
        ff_block(links.along(k))
        item.start()
    for item in items:
        item.first_done()
    ring.step(1)
    for item in ff_items:
        item.core_done()
    mixed_ring.step(2)
    sent = []
    for k in far[2:] + [0]:
        block = links.along(k)
        ff_block(block)
        sent.append(links.keep(ff.at[block], grad_ff_ref.at[block]))
    for item, (low, high) in zip(items, cuts):
        sum_ref[low:high] = item.second_done()[...]
    ring.step(2)
    for item in ff_items:
        item.first_done()
    mixed_ring.step(3)
    for low in range(0, span_len, 16):
        rows = slice(low, low + 16)
        output_ref[rows] = (middle_ref[rows] + small_ref[3, 0:1, 0:1] * mixed_total[rows]).astype(bf16)
    ring.step(3)
    for index, item in enumerate(ff_items):
        sent.append(links.keep(item.second_done(), ff_half_ref.at[index]))
    links.finish()
    for copy in sent:
        copy.wait()


def mlp_call(small, gains, mixed, x_blocks, attended, out_w, ff_w, w_down, line):
    f32, bf16 = jnp.float32, jnp.bfloat16
    span_len, width = mixed.shape
    group_len = line * span_len
    rows, both_cols, rows_each = w_down.shape[0], ff_w.shape[3], ff_w.shape[2]
    ff_rows = 8 * rows
    ff_w = ff_w.reshape(line, 2, 2, 2, rows_each, both_cols)
    half = (rows // 2 + 15) // 16 * 16
    cuts = ((0, half), (half, rows))
    blocks = (line, span_len, width)
    token = jax.ShapeDtypeStruct((span_len, width), f32)
    return link_call(
        functools.partial(mlp_kernel, line, cuts),
        2,
        112,
        (
            token,
            token,
            jax.ShapeDtypeStruct((span_len, width), bf16),
            jax.ShapeDtypeStruct((rows, width), bf16),
            jax.ShapeDtypeStruct(ff_w.shape, bf16),
            jax.ShapeDtypeStruct((2, rows_each, both_cols), bf16),
        ),
        (small, gains, mixed, x_blocks, attended, out_w.reshape(2, 2, 2, width // 8, width), ff_w, w_down),
        "vvhhhhhh" + "vvvvhh",
        [
            pltpu.VMEM((2, 2, 2, width // 8, width), bf16),
            pltpu.VMEM(ff_w.shape, bf16),
            pltpu.VMEM((ff_rows, width), bf16),
            pltpu.VMEM((group_len, width), bf16),
            pltpu.VMEM(blocks, bf16),
            pltpu.VMEM(blocks, bf16),
            pltpu.VMEM((group_len, both_cols), f32),
            pltpu.VMEM((group_len, ff_rows), bf16),
            pltpu.VMEM((group_len, both_cols), bf16),
            pltpu.VMEM((line - 1, span_len, width), bf16),
            pltpu.VMEM(blocks, bf16),
            pltpu.VMEM((line - 1, span_len, width), bf16),
            pltpu.VMEM((span_len, width), f32),
        ]
        + sum_space(2, rows_each, both_cols)[1:]
        + sum((sum_space(1, high - low, width)[1:] for low, high in cuts), []),
        vmem=63,
    )


def backward_kernel(
    line,
    small_ref,
    gain_ref,
    middle_ref,
    norm_grad_ref,
    x_ref,
    grad_ref,
    query_ref,
    kv_ref,
    peak_ref,
    turn_ref,
    out_ref,
    atts_ref,
    weight_ref,
    norm_ref,
    ff_ref,
    ff_half_ref,
    token_ref,
    ffs_ref,
    outs_ref,
    qkvs_ref,
    x_own,
    grad_own,
    middle_grad,
    total,
    big,
    slim,
    norm,
    own_rows,
    own_columns,
    branch,
    own_grad,
    att_grad,
    query_back,
    kv_back,
    kv_out,
    kv_in,
    flat,
    parts,
    query,
    kv,
    peak,
    turns,
    *scratch,
):
    f32, bf16 = jnp.float32, jnp.bfloat16
    send_sems, recv_sems = scratch[-2:]
    got, sums = scratch[0], scratch[1:-2]
    links = Links(send_sems, recv_sems, line)
    far = [1, line - 1] + list(range(2, line - 1))
    order = far + [0]
    links.meet(["x", "y", "c"] + far)
    span_len, width = x_ref.shape
    group_len = line * span_len
    q_cols = query.shape[1]
    heads = q_cols // HD
    rows_z = width // line
    rows_each = rows_z // 8
    scale = 1.0 / math.sqrt(HD)

    def lanes_of(block):
        return pl.ds(pl.multiple_of(block * q_cols, q_cols), q_cols)

    here = pl.ds(pl.multiple_of(links.z * span_len, span_len), span_len)
    first_load = links.keep(grad_ref, grad_own)
    loads = [
        links.keep(out_ref, big),
        links.keep(atts_ref.at[here], own_rows),
        links.keep(atts_ref.at[:, lanes_of(links.z)], own_columns),
        links.keep(x_ref, x_own),
        links.keep(query_ref, query),
        links.keep(kv_ref, kv),
        links.keep(peak_ref, peak),
        links.keep(turn_ref, turns),
        links.keep(norm_ref, norm),
        links.keep(weight_ref.at[:, :, :, :, pl.ds(0, slim.shape[4])], slim),
    ]
    ring = RingSum(links, parts, total, got)

    def items_of(source, space, in_place, order=order):
        items = []
        for index, k in enumerate(order):
            block = links.along(k)
            own = source.at[block, :, :, links.c] if in_place else space[0].at[index]
            core, first, second = space[-3:]
            items.append(
                NearSum(
                    links,
                    lambda c, block=block: source.at[block, :, :, c],
                    own,
                    core.at[index],
                    first.at[index],
                    second.at[index],
                    "xy"[index % 2],
                    in_place,
                )
            )
        return items

    ff_order = order[2:]
    ff_items = items_of(ff_ref, sums[:4], False, ff_order)
    out_items = items_of(big, sums[4:7], True)
    qkv_items = items_of(slim, sums[7:], True)
    local, arrived = [], []
    ff_cols = ff_ref.shape[5] // 2
    ff_pieces = ((0, ff_cols), (ff_cols, ff_cols))
    qkv_pieces = ((0, q_cols), (q_cols, HD), (q_cols + HD, HD))

    def deliver(total, target, k, pieces):
        for low, size in pieces:
            if pieces == out_pieces:
                place = target.at[links.z]
            else:
                lanes = pl.multiple_of(line * low + links.z * size, HD)
                place = target.at[:, pl.ds(lanes, size)]
            part = total.at[:, pl.ds(low, size)]
            if k == 0:
                local.append(links.keep(part, place))
            else:
                arrived.append(links.send(part, place, k))

    out_pieces = ((0, width),)
    for index, k in enumerate(order[:2]):
        deliver(ff_half_ref.at[index], ffs_ref, k, ff_pieces)
    def turn(items, target, low, high, pieces, order=order):
        for item, k in list(zip(items, order))[low:high]:
            deliver(item.second_done(), target, k, pieces)

    def core_done(items, low, high):
        for item in items[low:high]:
            item.core_done()

    def first_done(items, low, high):
        for item in items[low:high]:
            item.first_done()

    half = line // 2
    for item in ff_items:
        item.start()

    first_load.wait()
    keep = small_ref[3, 0:1, 0:1]
    token_scale = column_of(small_ref[1, 0:1])

    def norm_back(values, grad, gain):
        inverse = lax.rsqrt(jnp.mean(values * values, axis=-1, keepdims=True) + epsilon)
        scaled = gain * grad
        return inverse * scaled - values * (inverse * inverse * inverse) * jnp.mean(
            scaled * values, axis=-1, keepdims=True
        )

    for low in range(0, span_len, 16):
        rows = slice(low, low + 16)
        upstream = grad_own[rows].astype(f32) * token_scale[rows]
        grad = upstream + norm_back(middle_ref[rows], norm_grad_ref[rows], gain_ref[1])
        middle_grad[rows] = grad
        branch[rows] = (grad * keep).astype(bf16)
    for copy in loads:
        copy.wait()
    for z in range(line):
        weight = big[z].reshape(rows_z, width)
        own_grad[:, z * rows_z : (z + 1) * rows_z] = lax.dot_general(
            branch[...], weight, (((1,), (1,)), ((), ())), preferred_element_type=f32
        ).astype(bf16)
    turned = [links.send(own_grad.at[:, lanes_of(links.along(k))], att_grad.at[here], k) for k in far]
    stayed = links.keep(own_grad.at[:, lanes_of(links.z)], att_grad.at[here])
    core_done(ff_items, 0, line)
    for z in range(line):
        for part in range(4):
            columns = slice(part * width // 4, (part + 1) * width // 4)
            grad = lax.dot_general(
                own_rows[:, z * rows_z : (z + 1) * rows_z],
                branch[:, columns],
                (((0,), (0,)), ((), ())),
                preferred_element_type=f32,
            )
            big[z, :, :, :, :, columns] = grad.astype(bf16).reshape(2, 2, 2, rows_each, width // 4)
    for item in out_items:
        item.start()
    kv_back[...] = jnp.zeros_like(kv_back)
    for copy in turned:
        copy.wait_recv()
    stayed.wait()

    def attend_back(head, carry):
        lanes = pl.ds(pl.multiple_of(head * HD, HD), HD)
        for block in range(line):
            rows = slice(block * span_len, (block + 1) * span_len)
            reach = (block + 1) * span_len
            part, grad = query[rows, lanes], att_grad[rows, lanes]
            row = lax.broadcasted_iota(jnp.int32, (span_len, reach), 0) + block * span_len
            column = lax.broadcasted_iota(jnp.int32, (span_len, reach), 1)
            allowed = (column <= row, column < (block + links.x) * span_len)
            spot = lax.broadcasted_iota(jnp.int32, (span_len, HD), 1) == head
            top = jnp.sum(jnp.where(spot, peak[rows], 0.0), axis=-1, keepdims=True)
            delta = jnp.sum(
                grad.astype(f32) * own_columns[rows, lanes].astype(f32), axis=-1, keepdims=True
            )
            back = None
            for side in range(2):
                keys, values = kv[side, :reach, :HD], kv[side, :reach, HD:]
                score = lax.dot_general(
                    part, keys, (((1,), (1,)), ((), ())), preferred_element_type=f32
                )
                weight = jnp.where(allowed[side], jnp.exp(score * scale - top), 0.0)
                weight_grad = lax.dot_general(
                    grad, values, (((1,), (1,)), ((), ())), preferred_element_type=f32
                )
                score_grad = (weight * (weight_grad - delta)).astype(bf16)
                term = jnp.dot(score_grad, keys, preferred_element_type=f32)
                back = term if back is None else back + term
                kv_back[side, :reach, :HD] += lax.dot_general(
                    score_grad, part, (((0,), (0,)), ((), ())), preferred_element_type=f32
                )
                kv_back[side, :reach, HD:] += lax.dot_general(
                    weight.astype(bf16), grad, (((0,), (0,)), ((), ())), preferred_element_type=f32
                )
            query_back[rows, lanes] = back * scale
        return carry

    lax.fori_loop(0, heads, attend_back, 0)
    kv_out[:, :HD] = (kv_back[1, :, :HD] * scale).astype(bf16)
    kv_out[:, HD:] = kv_back[1, :, HD:].astype(bf16)
    exchange = links.send(kv_out, kv_in, "x")

    def turn_back(values, rows):
        return values * turns[0, rows] - pltpu.roll(values, HD // 2, 1) * turns[1, rows]

    for block in range(line):
        rows = slice(block * span_len, (block + 1) * span_len)
        for head in range(heads):
            lanes = slice(head * HD, (head + 1) * HD)
            flat[rows, lanes] = turn_back(query_back[rows, lanes], rows).astype(bf16)
    first_done(ff_items, 0, line)
    exchange.wait_recv()
    for block in range(line):
        rows = slice(block * span_len, (block + 1) * span_len)
        key_grad = kv_back[0, rows, :HD] * scale + kv_in[rows, :HD].astype(f32)
        flat[rows, q_cols : q_cols + HD] = turn_back(key_grad, rows).astype(bf16)
        value_grad = kv_back[0, rows, HD:] + kv_in[rows, HD:].astype(f32)
        flat[rows, q_cols + HD :] = value_grad.astype(bf16)
    for z in range(line):
        weight = slim[z].reshape(rows_z, flat.shape[1])
        part = lax.dot_general(
            flat[...], weight, (((1,), (1,)), ((), ())), preferred_element_type=f32
        ).astype(bf16)
        for block in range(line):
            parts[block, :, z * rows_z : (z + 1) * rows_z] = part[
                block * span_len : (block + 1) * span_len
            ]
    ring.step(0)
    for z in range(line):
        grad = lax.dot_general(
            norm[:, z * rows_z : (z + 1) * rows_z],
            flat[...],
            (((0,), (0,)), ((), ())),
            preferred_element_type=f32,
        )
        slim[z] = grad.astype(bf16).reshape(2, 2, 2, rows_each, flat.shape[1])
    for item in qkv_items:
        item.start()
    core_done(out_items, 0, half)
    turn(ff_items, ffs_ref, 0, line, ff_pieces, ff_order)
    ring.step(1)
    core_done(out_items, half, line)
    first_done(out_items, 0, half)
    ring.step(2)
    core_done(qkv_items, 0, line)
    first_done(out_items, half, line)
    turn(out_items, outs_ref, 0, half, out_pieces)
    ring.step(3)
    for low in range(0, span_len, 16):
        rows = slice(low, low + 16)
        grad = middle_grad[rows] + norm_back(x_own[rows].astype(f32), total[rows], gain_ref[0])
        token_ref[rows] = grad.astype(bf16)
    first_done(qkv_items, 0, half)
    turn(out_items, outs_ref, half, line, out_pieces)
    first_done(qkv_items, half, line)
    turn(qkv_items, qkvs_ref, 0, line, qkv_pieces)
    for copy in arrived:
        copy.wait_recv()
    links.finish()
    for copy in local:
        copy.wait()


def backward_call(near, tokens, saved, out_w, attended, weights, norm, grad_ff, ff_half, line):
    f32, bf16 = jnp.float32, jnp.bfloat16
    span_len, width = tokens[0].shape
    group_len = line * span_len
    query = saved[0]
    q_cols, rows_each, qkv_cols = query.shape[1], width // line // 8, weights.shape[3]
    weights = weights.reshape(line, 2, 2, 2, -1, qkv_cols)
    wide = (line, 2, 2, 2, rows_each, width)
    slim = (line, 2, 2, 2, rows_each, qkv_cols)
    out_space = sum_space(line, rows_each, width)[1:]
    qkv_space = sum_space(line, rows_each, qkv_cols)[1:]
    token = jax.ShapeDtypeStruct((span_len, width), bf16)
    return link_call(
        functools.partial(backward_kernel, line),
        4,
        160,
        (token,)
        + (
            jax.ShapeDtypeStruct((rows_each, line * grad_ff.shape[5]), bf16),
            jax.ShapeDtypeStruct((line, rows_each, width), bf16),
            jax.ShapeDtypeStruct((rows_each, line * qkv_cols), bf16),
        ),
        near + tokens + saved + (out_w.reshape(wide), attended, weights, norm, grad_ff, ff_half),
        "v" * 4 + "h" * 12 + "vhhh",
        [pltpu.VMEM((span_len, width), bf16)] * 2
        + [pltpu.VMEM((span_len, width), f32)] * 2
        + [
            pltpu.VMEM(wide, bf16),
            pltpu.VMEM(slim, bf16),
            pltpu.VMEM((group_len, width), bf16),
            pltpu.VMEM((span_len, width), bf16),
            pltpu.VMEM((group_len, q_cols), bf16),
            pltpu.VMEM((span_len, width), bf16),
            pltpu.VMEM((span_len, width), bf16),
            pltpu.VMEM((group_len, q_cols), bf16),
            pltpu.VMEM((group_len, q_cols), f32),
            pltpu.VMEM((2, group_len, 2 * HD), f32),
            pltpu.VMEM((group_len, 2 * HD), bf16),
            pltpu.VMEM((group_len, 2 * HD), bf16),
            pltpu.VMEM((group_len, qkv_cols), bf16),
            pltpu.VMEM((line, span_len, width), bf16),
        ]
        + [pltpu.VMEM(value.shape, value.dtype) for value in saved]
        + [pltpu.VMEM((line - 1, span_len, width), bf16)]
        + sum_space(line - 2, rows_each, grad_ff.shape[5])
        + out_space
        + qkv_space,
        vmem=63,
    )


def general_body(
    tokens,
    attn_gain,
    w_query,
    w_key,
    w_value,
    w_out,
    mlp_gain,
    w_gate,
    w_up,
    w_down,
    keep_mask,
    group_ids,
    positions,
    exit_scale,
    out_grad,
):
    seq_count, span_len, model_width = tokens.shape
    kv_heads = KVH
    head_dim = HD
    head_count = HEADS
    group_size = head_count // kv_heads
    row_count = seq_count * span_len
    stripe = group_size * span_len
    wide_count = lax.axis_size("wide")
    wide_place = lax.axis_index("wide")
    full_len = span_len * wide_count
    score_scale = 1.0 / math.sqrt(head_dim)
    gain_one, query_w, key_w, value_w, out_w = (
        lax.all_gather(attn_gain, ("wide", "narrow"), axis=0, tiled=True),
        lax.all_gather(w_query, ("wide", "narrow"), axis=0, tiled=True),
        lax.all_gather(w_key, ("wide", "narrow"), axis=0, tiled=True),
        lax.all_gather(w_value, ("wide", "narrow"), axis=0, tiled=True),
        lax.all_gather(w_out, ("wide", "narrow"), axis=0, tiled=True),
    )
    inputs = tokens.astype(jnp.float32).reshape(row_count, model_width)
    token_pos = positions.reshape(row_count)
    keep_rows = jnp.repeat(keep_mask.astype(jnp.float32), span_len)[:, None]
    inverse_one = lax.rsqrt(jnp.mean(inputs * inputs, axis=-1, keepdims=True) + epsilon)
    first_norm = (inputs * inverse_one * gain_one.astype(jnp.float32)).astype(jnp.bfloat16)
    query_pre = jnp.dot(first_norm, query_w, preferred_element_type=jnp.float32).reshape(
        row_count, head_count, head_dim
    )
    key_pre = jnp.dot(first_norm, key_w, preferred_element_type=jnp.float32).reshape(
        row_count, kv_heads, head_dim
    )
    query_rows = rotate(query_pre, token_pos, 1.0).astype(jnp.bfloat16)
    key_heads = (
        rotate(key_pre, token_pos, 1.0)
        .astype(jnp.bfloat16)
        .reshape(seq_count, span_len, kv_heads * head_dim)
    )
    value_heads = (
        jnp.dot(first_norm, value_w, preferred_element_type=jnp.float32)
        .astype(jnp.bfloat16)
        .reshape(seq_count, span_len, kv_heads * head_dim)
    )
    queries = (
        query_rows.reshape(seq_count, span_len, kv_heads, group_size, head_dim)
        .transpose(0, 2, 3, 1, 4)
        .reshape(seq_count, kv_heads, stripe, head_dim)
    )
    query_index = wide_place * span_len + jnp.arange(stripe, dtype=jnp.int32) % span_len
    last_query = wide_place * span_len + span_len - 1

    def block_scores(key_block, key_first):
        scores = (
            jnp.einsum("skrd,sjkd->skrj", queries, key_block, preferred_element_type=jnp.float32)
            * score_scale
        )
        key_index = key_first + jnp.arange(key_block.shape[1], dtype=jnp.int32)
        allowed = key_index[None, :] <= query_index[:, None]
        return (scores, allowed)

    start_forward = (
        jnp.full((seq_count, kv_heads, stripe), -1e30, jnp.float32),
        jnp.zeros((seq_count, kv_heads, stripe), jnp.float32),
        jnp.zeros((seq_count, kv_heads, stripe, head_dim), jnp.float32),
    )
    running = start_forward
    pieces = (
        lax.all_gather(key_heads, "wide", axis=1, tiled=True),
        lax.all_gather(value_heads, "wide", axis=1, tiled=True),
    )
    key_blocks = split_blocks(pieces[0], seq_count, kv_heads, head_dim)
    value_blocks = split_blocks(pieces[1], seq_count, kv_heads, head_dim)
    block_len = key_blocks.shape[2]

    def advance(carried, block_item):
        key_block, value_block, block_index = block_item
        key_first = block_index * block_len

        def compute_block(current):
            run_max, run_sum, run_acc = current
            scores, allowed = block_scores(key_block, key_first)
            scores = jnp.where(allowed, scores, -1e30)
            new_max = jnp.maximum(run_max, jnp.max(scores, axis=-1))
            factor = jnp.exp(run_max - new_max)
            weights = jnp.where(allowed, jnp.exp(scores - new_max[..., None]), 0.0)
            new_sum = run_sum * factor + jnp.sum(weights, axis=-1)
            new_acc = run_acc * factor[..., None] + jnp.einsum(
                "skrj,sjkd->skrd",
                weights.astype(jnp.bfloat16),
                value_block,
                preferred_element_type=jnp.float32,
            )
            return (new_max, new_sum, new_acc)

        return (lax.cond(key_first <= last_query, compute_block, unchanged, carried), None)

    running, _ = lax.scan(
        advance,
        running,
        (key_blocks, value_blocks, jnp.arange(key_blocks.shape[0], dtype=jnp.int32)),
    )
    run_max, run_sum, run_acc = running
    attended = run_acc / run_sum[..., None]
    log_total = run_max + jnp.log(run_sum)
    attended_rows = (
        attended.reshape(seq_count, kv_heads, group_size, span_len, head_dim)
        .transpose(0, 3, 1, 2, 4)
        .reshape(row_count, head_count * head_dim)
        .astype(jnp.bfloat16)
    )
    middle = inputs + keep_rows * jnp.dot(attended_rows, out_w, preferred_element_type=jnp.float32)
    gain_two, gate_w, up_w, down_w = (
        lax.all_gather(mlp_gain, ("wide", "narrow"), axis=0, tiled=True),
        lax.all_gather(w_gate, ("wide", "narrow"), axis=0, tiled=True),
        lax.all_gather(w_up, ("wide", "narrow"), axis=0, tiled=True),
        lax.all_gather(w_down, ("wide", "narrow"), axis=0, tiled=True),
    )
    inverse_two = lax.rsqrt(jnp.mean(middle * middle, axis=-1, keepdims=True) + epsilon)
    second_norm = (middle * inverse_two * gain_two.astype(jnp.float32)).astype(jnp.bfloat16)
    gate_value = jnp.dot(second_norm, gate_w, preferred_element_type=jnp.float32)
    up_value = jnp.dot(second_norm, up_w, preferred_element_type=jnp.float32)
    gate_sigmoid = jax.nn.sigmoid(gate_value)
    swish_value = gate_value * gate_sigmoid
    hidden = (swish_value * up_value).astype(jnp.bfloat16)
    output = (
        middle + keep_rows * jnp.dot(hidden, down_w, preferred_element_type=jnp.float32)
    ).astype(jnp.bfloat16)
    group_match = (
        group_ids.reshape(row_count)[:, None]
        == jnp.arange(exit_scale.shape[0], dtype=jnp.int32)[None, :]
    )
    token_scale = jnp.sum(jnp.where(group_match, exit_scale[None, :], 0.0), axis=1, keepdims=True)
    upstream = out_grad.astype(jnp.float32).reshape(row_count, model_width) * token_scale
    gain_two, gate_w, up_w, down_w = (
        lax.all_gather(mlp_gain, ("wide", "narrow"), axis=0, tiled=True),
        lax.all_gather(w_gate, ("wide", "narrow"), axis=0, tiled=True),
        lax.all_gather(w_up, ("wide", "narrow"), axis=0, tiled=True),
        lax.all_gather(w_down, ("wide", "narrow"), axis=0, tiled=True),
    )
    mixed_grad = (keep_rows * upstream).astype(jnp.bfloat16)
    grad_down = over_rows(hidden, mixed_grad)
    hidden_grad = against(mixed_grad, down_w)
    gate_grad = (
        hidden_grad * up_value * gate_sigmoid * (1.0 + gate_value * (1.0 - gate_sigmoid))
    ).astype(jnp.bfloat16)
    up_grad = (hidden_grad * swish_value).astype(jnp.bfloat16)
    grad_gate = over_rows(second_norm, gate_grad)
    grad_up = over_rows(second_norm, up_grad)
    norm_grad = against(gate_grad, gate_w) + against(up_grad, up_w)
    grad_gain_two = jnp.sum(norm_grad * middle * inverse_two, axis=0)
    scaled_two = gain_two.astype(jnp.float32) * norm_grad
    middle_grad = (
        upstream
        + inverse_two * scaled_two
        - middle
        * (inverse_two * inverse_two * inverse_two)
        * jnp.mean(scaled_two * middle, axis=-1, keepdims=True)
    )
    gain_two_share, gate_share, up_share, down_share = (
        lax.psum_scatter(grad_gain_two, ("wide", "narrow"), scatter_dimension=0, tiled=True),
        lax.psum_scatter(grad_gate, ("wide", "narrow"), scatter_dimension=0, tiled=True),
        lax.psum_scatter(grad_up, ("wide", "narrow"), scatter_dimension=0, tiled=True),
        lax.psum_scatter(grad_down, ("wide", "narrow"), scatter_dimension=0, tiled=True),
    )
    gain_one, query_w, key_w, value_w, out_w = (
        lax.all_gather(attn_gain, ("wide", "narrow"), axis=0, tiled=True),
        lax.all_gather(w_query, ("wide", "narrow"), axis=0, tiled=True),
        lax.all_gather(w_key, ("wide", "narrow"), axis=0, tiled=True),
        lax.all_gather(w_value, ("wide", "narrow"), axis=0, tiled=True),
        lax.all_gather(w_out, ("wide", "narrow"), axis=0, tiled=True),
    )
    branch_grad = (keep_rows * middle_grad).astype(jnp.bfloat16)
    grad_out = over_rows(attended_rows, branch_grad)
    attended_grad = against(branch_grad, out_w).astype(jnp.bfloat16)
    grouped_grad = (
        attended_grad.reshape(seq_count, span_len, kv_heads, group_size, head_dim)
        .transpose(0, 2, 3, 1, 4)
        .reshape(seq_count, kv_heads, stripe, head_dim)
    )
    row_delta = jnp.sum(grouped_grad.astype(jnp.float32) * attended, axis=-1)
    start_backward = (
        jnp.zeros((seq_count, kv_heads, stripe, head_dim), jnp.float32),
        jnp.zeros((seq_count, full_len, kv_heads * head_dim), jnp.float32),
        jnp.zeros((seq_count, full_len, kv_heads * head_dim), jnp.float32),
    )
    running = start_backward
    pieces = (
        lax.all_gather(key_heads, "wide", axis=1, tiled=True),
        lax.all_gather(value_heads, "wide", axis=1, tiled=True),
    )
    key_blocks = split_blocks(pieces[0], seq_count, kv_heads, head_dim)
    value_blocks = split_blocks(pieces[1], seq_count, kv_heads, head_dim)
    fold_block_len = key_blocks.shape[2]

    def advance(carried, block_item):
        key_block, value_block, block_index = block_item
        key_first = block_index * fold_block_len

        def compute_block(current):
            query_acc, key_acc, value_acc = current
            scores, allowed = block_scores(key_block, key_first)
            probabilities = jnp.where(allowed, jnp.exp(scores - log_total[..., None]), 0.0)
            value_part = jnp.einsum(
                "skrj,skrd->sjkd",
                probabilities.astype(jnp.bfloat16),
                grouped_grad,
                preferred_element_type=jnp.float32,
            )
            prob_grad = jnp.einsum(
                "skrd,sjkd->skrj", grouped_grad, value_block, preferred_element_type=jnp.float32
            )
            score_grad = (probabilities * (prob_grad - row_delta[..., None])).astype(jnp.bfloat16)
            query_acc = (
                query_acc
                + jnp.einsum(
                    "skrj,sjkd->skrd", score_grad, key_block, preferred_element_type=jnp.float32
                )
                * score_scale
            )
            key_part = (
                jnp.einsum(
                    "skrj,skrd->sjkd", score_grad, queries, preferred_element_type=jnp.float32
                )
                * score_scale
            )
            key_acc = add_rows(
                key_acc, key_part.reshape(seq_count, fold_block_len, kv_heads * head_dim), key_first
            )
            value_acc = add_rows(
                value_acc,
                value_part.reshape(seq_count, fold_block_len, kv_heads * head_dim),
                key_first,
            )
            return (query_acc, key_acc, value_acc)

        return (lax.cond(key_first <= last_query, compute_block, unchanged, carried), None)

    running, _ = lax.scan(
        advance,
        running,
        (key_blocks, value_blocks, jnp.arange(key_blocks.shape[0], dtype=jnp.int32)),
    )
    query_acc, key_acc, value_acc = running
    key_sum, value_sum = (
        lax.psum_scatter(
            key_acc.astype(jnp.bfloat16), "wide", scatter_dimension=1, tiled=True
        ).astype(jnp.float32),
        lax.psum_scatter(
            value_acc.astype(jnp.bfloat16), "wide", scatter_dimension=1, tiled=True
        ).astype(jnp.float32),
    )
    query_back = (
        query_acc.reshape(seq_count, kv_heads, group_size, span_len, head_dim)
        .transpose(0, 3, 1, 2, 4)
        .reshape(row_count, head_count, head_dim)
    )
    query_grad = (
        rotate(query_back, token_pos, -1.0)
        .reshape(row_count, head_count * head_dim)
        .astype(jnp.bfloat16)
    )
    key_grad = (
        rotate(key_sum.reshape(row_count, kv_heads, head_dim), token_pos, -1.0)
        .reshape(row_count, kv_heads * head_dim)
        .astype(jnp.bfloat16)
    )
    value_grad = value_sum.reshape(row_count, kv_heads * head_dim).astype(jnp.bfloat16)
    grad_query = over_rows(first_norm, query_grad)
    grad_key = over_rows(first_norm, key_grad)
    grad_value = over_rows(first_norm, value_grad)
    input_norm_grad = (
        against(query_grad, query_w) + against(key_grad, key_w) + against(value_grad, value_w)
    )
    grad_gain_one = jnp.sum(input_norm_grad * inputs * inverse_one, axis=0)
    scaled_one = gain_one.astype(jnp.float32) * input_norm_grad
    input_grad = (
        middle_grad
        + inverse_one * scaled_one
        - inputs
        * (inverse_one * inverse_one * inverse_one)
        * jnp.mean(scaled_one * inputs, axis=-1, keepdims=True)
    )
    gain_one_share, query_share, key_share, value_share, out_share = (
        lax.psum_scatter(grad_gain_one, ("wide", "narrow"), scatter_dimension=0, tiled=True),
        lax.psum_scatter(grad_query, ("wide", "narrow"), scatter_dimension=0, tiled=True),
        lax.psum_scatter(grad_key, ("wide", "narrow"), scatter_dimension=0, tiled=True),
        lax.psum_scatter(grad_value, ("wide", "narrow"), scatter_dimension=0, tiled=True),
        lax.psum_scatter(grad_out, ("wide", "narrow"), scatter_dimension=0, tiled=True),
    )
    return (
        output.reshape(seq_count, span_len, model_width),
        input_grad.astype(jnp.bfloat16).reshape(seq_count, span_len, model_width),
        gain_one_share,
        query_share,
        key_share,
        value_share,
        out_share,
        gain_two_share,
        gate_share,
        up_share,
        down_share,
    )


def line_body(
    tokens,
    attn_gain,
    w_query,
    w_key,
    w_value,
    w_out,
    mlp_gain,
    w_gate,
    w_up,
    w_down,
    keep_mask,
    group_ids,
    positions,
    exit_scale,
    out_grad,
):
    f32 = jnp.float32
    bf16 = jnp.bfloat16
    _, span_len, model_width = tokens.shape
    line = lax.axis_size("z")
    rows_each = w_query.shape[0]
    q_cols = HEADS // line * HD

    group_match = group_ids[0][:, None] == jnp.arange(exit_scale.shape[0], dtype=jnp.int32)[None, :]
    token_scale = jnp.sum(jnp.where(group_match, exit_scale[None, :], 0.0), axis=1)
    freqs = 10000.0 ** (-2.0 * jnp.arange(HD // 2, dtype=f32) / HD)
    small = jnp.stack(
        [
            positions[0].astype(f32),
            token_scale,
            jnp.concatenate([freqs, freqs]),
            jnp.broadcast_to(keep_mask.astype(f32), (span_len,)),
        ]
    )
    small = jnp.broadcast_to(small[:, None], (4, 8, span_len))

    core = lax.axis_index("c")
    gain_row = jnp.zeros((q_cols + 2 * HD,), bf16)
    gain_row = lax.dynamic_update_slice_in_dim(gain_row, attn_gain, core * rows_each, 0)
    gain_row = lax.dynamic_update_slice_in_dim(gain_row, mlp_gain, HD + core * rows_each, 0)
    gain_rows = jnp.broadcast_to(gain_row, (16, gain_row.shape[0]))
    (
        x_blocks,
        near_w,
        gain_all,
        first_norm,
        queries,
        both_kv,
        log_total,
        turns,
        attended_rows,
        ff_w,
        out_w,
        own_mixed,
    ) = forward_call(
        small,
        tokens[0],
        out_grad[0],
        gain_rows,
        (w_query, w_key, w_value, w_gate, w_up, w_out),
        line,
    )
    middle, norm_grad, output, grad_down, grad_ff, ff_half = mlp_call(
        small,
        gain_all,
        own_mixed,
        x_blocks,
        attended_rows,
        out_w,
        ff_w,
        w_down,
        line,
    )
    grad_down = grad_down.astype(f32)
    token_grad, ff_back, out_back, qkv_back = backward_call(
        (small, gain_all, middle, norm_grad),
        (tokens[0], out_grad[0]),
        (queries, both_kv, log_total, turns),
        out_w,
        attended_rows,
        near_w,
        first_norm,
        grad_ff,
        ff_half,
        line,
    )
    ff_back = ff_back.astype(f32)
    qkv_back = qkv_back.astype(f32)
    grad_out = jnp.sum(out_back.astype(f32), axis=0)
    heads_end, keys_end = w_query.shape[1], w_query.shape[1] + w_key.shape[1]
    grad_query = qkv_back[:, :heads_end]
    grad_key = qkv_back[:, heads_end:keys_end]
    grad_value = qkv_back[:, keys_end:]
    grad_gate = ff_back[:, : w_gate.shape[1]]
    grad_up = ff_back[:, w_gate.shape[1] :]

    def gain_grad(pairs, gain):
        total = sum(jnp.sum(weight.astype(f32) * grad, axis=1) for weight, grad in pairs)
        return total / gain.astype(f32)

    return (
        output[None],
        token_grad[None],
        gain_grad([(w_query, grad_query), (w_key, grad_key), (w_value, grad_value)], attn_gain),
        grad_query,
        grad_key,
        grad_value,
        grad_out,
        gain_grad([(w_gate, grad_gate), (w_up, grad_up)], mlp_gain),
        grad_gate,
        grad_up,
        grad_down,
    )


def solution(mesh):
    wide, narrow = mesh.shape["wide"], mesh.shape["narrow"]
    if wide == 2 * KVH and narrow == 4:
        mesh = Mesh(mesh.devices.reshape(wide // 2, 2, 2, 2), ("z", "x", "y", "c"))
        body, wide, narrow = line_body, ("z", "x"), ("y", "c")
    else:
        body, wide, narrow = general_body, ("wide",), ("narrow",)
    token_spec = P(narrow, wide, None)
    id_spec = P(narrow, wide)
    gain_spec = P(wide + narrow)
    weight_spec = P(wide + narrow, None)
    return jax.shard_map(
        body,
        mesh=mesh,
        in_specs=(
            token_spec,
            gain_spec,
            weight_spec,
            weight_spec,
            weight_spec,
            weight_spec,
            gain_spec,
            weight_spec,
            weight_spec,
            weight_spec,
            P(narrow),
            id_spec,
            id_spec,
            P(),
            token_spec,
        ),
        out_specs=(
            token_spec,
            token_spec,
            gain_spec,
            weight_spec,
            weight_spec,
            weight_spec,
            weight_spec,
            gain_spec,
            weight_spec,
            weight_spec,
            weight_spec,
        ),
        check_vma=False,
    )
```

```python
import functools
import math

import jax
import jax.numpy as jnp
from jax import lax
from jax.experimental import pallas as pl
from jax.experimental.pallas import tpu as pltpu
from jax.sharding import Mesh
from jax.sharding import PartitionSpec as P

HEADS = 16
KVH = 4
HD = 128


epsilon = 1e-05


def rotate(vectors, token_pos, direction):
    half_size = vectors.shape[-1] // 2
    freqs = 10000.0 ** (-2.0 * jnp.arange(half_size, dtype=jnp.float32) / vectors.shape[-1])
    angles = token_pos.astype(jnp.float32)[:, None] * freqs[None, :]
    cosine = jnp.cos(angles)[:, None, :]
    sine = direction * jnp.sin(angles)[:, None, :]
    first_half = vectors[..., :half_size]
    second_half = vectors[..., half_size:]
    return jnp.concatenate(
        [first_half * cosine - second_half * sine, second_half * cosine + first_half * sine],
        axis=-1,
    )


def split_blocks(piece_arr, seq_count, kv_heads, head_dim):
    piece_len = piece_arr.shape[1]
    block_len = math.gcd(piece_len, 512)
    shaped = piece_arr.reshape(seq_count, piece_len // block_len, block_len, kv_heads, head_dim)
    return shaped.transpose(1, 0, 2, 3, 4)


def add_rows(whole_arr, update, first_row):
    current = lax.dynamic_slice_in_dim(whole_arr, first_row, update.shape[1], 1)
    return lax.dynamic_update_slice_in_dim(whole_arr, current + update, first_row, 1)


def over_rows(left, right):
    return lax.dot_general(
        left, right, (((0,), (0,)), ((), ())), preferred_element_type=jnp.float32
    )


def against(left, right):
    return lax.dot_general(
        left, right, (((1,), (1,)), ((), ())), preferred_element_type=jnp.float32
    )


def unchanged(carried):
    return carried


MESH = pl.DeviceIdType.MESH
AXES = ("z", "x", "y", "c")


def only(when, act):
    if when is None:
        act()
    else:
        pl.when(when)(act)


class Links:
    def __init__(self, send_sems, recv_sems, line):
        self.send_sems, self.recv_sems, self.line = send_sems, recv_sems, line
        self.z, self.x, self.y, self.c = (lax.axis_index(name) for name in AXES)
        self.slot = self.x * 4 + self.y * 2 + self.c
        self.used = 0
        self.sent = []

    def device(self, to):
        if to == "x":
            return (self.z, 1 - self.x, self.y, self.c)
        if to == "y":
            return (self.z, self.x, 1 - self.y, self.c)
        if to == "c":
            return (self.z, self.x, self.y, 1 - self.c)
        return (self.along(to), self.x, self.y, self.c)

    def along(self, step):
        return lax.rem(self.z + step + self.line, self.line)

    def other(self, to):
        slot = self.slot
        for name in to:
            bit = {"x": 4, "y": 2, "c": 1}[name]
            here = {"x": self.x, "y": self.y, "c": self.c}[name]
            slot = slot + bit * (1 - 2 * here)
        return slot

    def meet(self, targets):
        barrier = pltpu.get_barrier_semaphore()
        for to in targets:
            pl.semaphore_signal(barrier, inc=1, device_id=self.device(to), device_id_type=MESH)
        pl.semaphore_wait(barrier, len(targets))

    def send(self, source, target, to, when=None):
        copy = pltpu.make_async_remote_copy(
            src_ref=source,
            dst_ref=target,
            send_sem=self.send_sems.at[self.used],
            recv_sem=self.recv_sems.at[self.used],
            device_id=self.device(to),
            device_id_type=MESH,
        )
        only(when, copy.start)
        self.used += 1
        self.sent.append((copy, when))
        return copy

    def keep(self, source, target):
        copy = pltpu.make_async_copy(source, target, self.send_sems.at[self.used])
        copy.start()
        self.used += 1
        return copy

    def finish(self):
        for copy, when in self.sent:
            only(when, copy.wait_send)


class NearGather:
    def __init__(self, links, slot):
        self.links, self.slot = links, slot
        self.got = {}

    def offer(self, block, source):
        target = self.slot(block, self.links.slot)
        for to in ("x", "y", "c"):
            self.got[block, to] = self.links.send(source, target, to)

    def relay(self, block, first):
        links = self.links
        for to, then in (("x", "y"), ("y", "x")):
            self.got[block, to].wait_recv()
            place = self.slot(block, links.other(to))
            self.got[block, to + "c"] = links.send(place, place, "c")
            if to == first:
                self.got[block, "xy"] = links.send(place, place, then)

    def close(self, block):
        self.got[block, "xy"].wait_recv()
        place = self.slot(block, self.links.other("xy"))
        self.got[block, "xyc"] = self.links.send(place, place, "c")

    def wait(self, blocks):
        for block in blocks:
            for to in ("c", "xc", "yc", "xyc"):
                self.got[block, to].wait_recv()


class LineGather:
    def __init__(self, links, rows, origin, place, pieces=2):
        self.links, self.origin, self.place = links, origin, place
        self.pieces, self.rows = pieces, rows // pieces
        self.last = {}

    def inside(self, block):
        return jnp.logical_and(block >= 0, block < self.links.line)

    def step(self, number):
        z = self.links.z
        for piece in range(self.pieces):
            for way in (1, -1):
                held = self.inside(z - way * number)
                if number > 0:
                    only(held, self.last[piece, way].wait_recv)
                if number == self.links.line - 1:
                    continue
                rows = pl.ds(piece * self.rows, self.rows)
                place = self.place(self.links.along(-way * number), rows)
                source = self.origin(rows) if number == 0 else place
                when = jnp.logical_and(held, self.inside(z + way))
                self.last[piece, way] = self.links.send(source, place, way, when)


def column_of(row):
    size = row.shape[1]
    down = lax.broadcasted_iota(jnp.int32, (size, size), 0)
    across = lax.broadcasted_iota(jnp.int32, (size, size), 1)
    values = jnp.where(down == across, jnp.broadcast_to(row, (size, size)), 0.0)
    return jnp.sum(values, axis=1, keepdims=True)


def first_kernel(
    line,
    small_ref,
    x_ref,
    grad_ref,
    gain_rows_ref,
    query_w_ref,
    key_w_ref,
    value_w_ref,
    gate_w_ref,
    up_w_ref,
    out_ref,
    xs_ref,
    weight_ref,
    gain_ref,
    norm_ref,
    query_ref,
    kv_ref,
    peak_ref,
    turn_ref,
    atts_ref,
    ffs_ref,
    outs_ref,
    mix_ref,
    x_all,
    grad,
    mix,
    places,
    weights,
    gains,
    norm,
    turns,
    flat,
    query,
    kv,
    peak,
    att,
    send_sems,
    recv_sems,
):
    f32, bf16 = jnp.float32, jnp.bfloat16
    links = Links(send_sems, recv_sems, line)
    far = [1, line - 1] + list(range(2, line - 1))
    links.meet(["x", "y", "c"] + far)
    here = links.slot
    span_len, width = x_ref.shape
    group_len = line * span_len
    rows_each = gate_w_ref.shape[0]
    q_cols = query.shape[1]
    ff_cols = gate_w_ref.shape[1] // line
    heads = q_cols // HD
    local = []

    near = NearGather(links, lambda block, place: weights.at[links.along(-block), place])
    far_ff = NearGather(links, lambda block, place: ffs_ref.at[links.along(-block), place])
    far_out = NearGather(links, lambda block, place: outs_ref.at[links.along(-block), place])
    ring = LineGather(
        links, span_len, lambda rows: x_ref.at[rows], lambda block, rows: x_all.at[block, rows]
    )
    place_ref = small_ref.at[0]

    def columns(weight, block, size):
        return weight.at[:, pl.ds(pl.multiple_of(block * size, HD), size)]

    def near_pieces(block):
        target = weights.at[links.z, here]
        rows = pl.ds(0, rows_each)
        return [
            (columns(query_w_ref, block, q_cols), target.at[rows, pl.ds(0, q_cols)]),
            (columns(key_w_ref, block, HD), target.at[rows, pl.ds(q_cols, HD)]),
            (columns(value_w_ref, block, HD), target.at[rows, pl.ds(q_cols + HD, HD)]),
            (gain_rows_ref, target.at[pl.ds(rows_each, 16)]),
        ]

    def ff_pieces(block):
        target = ffs_ref.at[links.z, here]
        return [
            (columns(gate_w_ref, block, ff_cols), target.at[:, pl.ds(0, ff_cols)]),
            (columns(up_w_ref, block, ff_cols), target.at[:, pl.ds(ff_cols, ff_cols)]),
        ]

    def turn_out(pieces):
        return {k: [links.send(*piece, k) for piece in pieces(links.along(k))] for k in far}

    def arrived(copies):
        for copy in copies:
            copy.wait_recv()

    own = [links.keep(*piece) for piece in near_pieces(links.z)]
    own_ff = [links.keep(*piece) for piece in ff_pieces(links.z)]
    turned = turn_out(near_pieces)
    placed = [links.send(place_ref, places.at[links.z], k) for k in far]
    turned_ff = turn_out(ff_pieces)
    for copy in own:
        copy.wait()
    near.offer(0, weights.at[links.z, here])
    for copy in own_ff:
        copy.wait()
    far_ff.offer(0, ffs_ref.at[links.z, here])
    own = [
        links.keep(x_ref, x_all.at[links.z]),
        links.keep(place_ref, places.at[links.z]),
        links.keep(grad_ref, grad),
    ]
    local.append(links.keep(out_ref, outs_ref.at[links.z, here]))

    def move_out(k):
        moved.wait_recv()
        block = outs_ref.at[links.along(-k), here]
        onward = links.send(block, block, 1) if k < line - 1 else None
        far_out.offer(k, block)
        return onward

    for k in far:
        arrived(turned[k])
        near.offer(k, weights.at[links.along(-k), here])
    ring.step(0)
    for k in [0] + far:
        near.relay(k, "x" if k < line // 2 else "y")
    for k in far:
        arrived(turned_ff[k])
        far_ff.offer(k, ffs_ref.at[links.along(-k), here])
    ring.step(1)
    for k in [0] + far:
        near.close(k)
    far_ff.relay(0, "x")
    ring.step(2)
    moved = links.send(out_ref, outs_ref.at[links.z, here], 1)
    far_out.offer(0, out_ref)
    for copy in own:
        copy.wait()
    for copy in placed:
        copy.wait_recv()

    lane = lax.broadcasted_iota(jnp.int32, (span_len, HD), 1)
    for block in range(line):
        angles = column_of(places[block, 0:1]) * small_ref[2, 0:1]
        rows = slice(block * span_len, (block + 1) * span_len)
        sine = jnp.sin(angles)
        turns[0, rows] = jnp.cos(angles)
        turns[1, rows] = jnp.where(lane < HD // 2, -sine, sine)
    local.append(links.keep(turns, turn_ref))
    token_scale = column_of(small_ref[1, 0:1])
    for low in range(0, span_len, 16):
        rows = slice(low, low + 16)
        upstream = grad[rows].astype(f32) * token_scale[rows]
        mix[rows] = (upstream * small_ref[3, 0:1, 0:1]).astype(bf16)
    local.append(links.keep(mix, mix_ref))
    near.wait(range(line))
    for index in range(line * 4):
        z, q = divmod(index, 4)
        for which in range(2):
            lanes = slice(which * HD, (which + 1) * HD)
            both = [weights[z, 2 * q + c, rows_each : rows_each + 16, lanes].astype(f32) for c in range(2)]
            gains[which, :, index * HD : (index + 1) * HD] = both[0] + both[1]
    local.append(links.keep(weights, weight_ref))
    local.append(links.keep(gains, gain_ref))
    far_ff.relay(far[0], "x")
    ring.step(3)
    local.append(links.keep(x_all, xs_ref))

    def normalise(index, carry):
        block = index // (span_len // 16)
        rows = pl.ds(pl.multiple_of(lax.rem(index, span_len // 16) * 16, 16), 16)
        values = x_all[block, rows].astype(f32)
        inverse = lax.rsqrt(jnp.mean(values * values, axis=-1, keepdims=True) + epsilon)
        target = pl.ds(pl.multiple_of(index * 16, 16), 16)
        norm[target] = (values * inverse * gains[0]).astype(bf16)
        return carry

    lax.fori_loop(0, group_len // 16, normalise, 0)
    local.append(links.keep(norm, norm_ref))

    def project(low, high):
        step = group_len // 2
        for part in range(2):
            rows = slice(part * step, (part + 1) * step)
            total = None
            for z in range(line):
                weight = weights[z, :, :rows_each, low:high].reshape(8 * rows_each, high - low)
                term = jnp.dot(
                    norm[rows, z * 8 * rows_each : (z + 1) * 8 * rows_each],
                    weight,
                    preferred_element_type=f32,
                )
                total = term if total is None else total + term
            flat[rows, low:high] = total

    def turn(values, rows):
        return values * turns[0, rows] + pltpu.roll(values, HD // 2, 1) * turns[1, rows]

    project(q_cols, q_cols + 2 * HD)
    for block in range(line):
        rows = slice(block * span_len, (block + 1) * span_len)
        kv[0, rows, :HD] = turn(flat[rows, q_cols : q_cols + HD], rows).astype(bf16)
        kv[0, rows, HD:] = flat[rows, q_cols + HD : q_cols + 2 * HD].astype(bf16)
    exchange = links.send(kv.at[0], kv.at[1], "x")
    project(0, q_cols)
    for block in range(line):
        rows = slice(block * span_len, (block + 1) * span_len)
        for head in range(heads):
            lanes = slice(head * HD, (head + 1) * HD)
            query[rows, lanes] = turn(flat[rows, lanes], rows).astype(bf16)
    local.append(links.keep(query, query_ref))
    for k in far[1:]:
        far_ff.relay(k, "x" if k < line // 2 else "y")
    exchange.wait_recv()
    moved = move_out(1)
    local.append(links.keep(kv, kv_ref))

    scale = 1.0 / math.sqrt(HD)
    peak[...] = jnp.zeros_like(peak)

    def attend(head, carry):
        lanes = pl.ds(pl.multiple_of(head * HD, HD), HD)
        for block in range(line):
            rows = slice(block * span_len, (block + 1) * span_len)
            reach = (block + 1) * span_len
            part = query[rows, lanes]
            row = lax.broadcasted_iota(jnp.int32, (span_len, reach), 0) + block * span_len
            column = lax.broadcasted_iota(jnp.int32, (span_len, reach), 1)
            allowed = (column <= row, column < (block + links.x) * span_len)
            scores = []
            for half in range(2):
                score = lax.dot_general(
                    part, kv[half, :reach, :HD], (((1,), (1,)), ((), ())), preferred_element_type=f32
                )
                scores.append(jnp.where(allowed[half], score * scale, -1e30))
            top = jnp.maximum(
                jnp.max(scores[0], axis=-1, keepdims=True), jnp.max(scores[1], axis=-1, keepdims=True)
            )
            total, mixed = None, None
            for half in range(2):
                weight = jnp.exp(scores[half] - top)
                count = jnp.sum(weight, axis=-1, keepdims=True)
                term = jnp.dot(weight.astype(bf16), kv[half, :reach, HD:], preferred_element_type=f32)
                total = count if total is None else total + count
                mixed = term if mixed is None else mixed + term
            att[rows, lanes] = (mixed / total).astype(bf16)
            spot = lax.broadcasted_iota(jnp.int32, (span_len, HD), 1) == head
            peak[rows] = jnp.where(spot, top + jnp.log(total), peak[rows])
        return carry

    lax.fori_loop(0, heads, attend, 0)
    local.append(links.keep(peak, peak_ref))

    def place(block, rows):
        return atts_ref.at[rows, pl.ds(pl.multiple_of(block * q_cols, q_cols), q_cols)]

    att_ring = LineGather(links, group_len, lambda rows: att.at[rows], place)
    local.append(links.keep(att, place(links.z, pl.ds(0, group_len))))
    att_ring.step(0)
    for k in [0] + far:
        far_ff.close(k)
    far_out.relay(0, "x")
    moved = move_out(2)
    far_out.relay(1, "x")
    att_ring.step(1)
    for k in range(3, line):
        moved = move_out(k)
    far_out.relay(2, "y")
    att_ring.step(2)
    for k in range(3, line):
        far_out.relay(k, "y")
    for k in range(line):
        far_out.close(k)
    att_ring.step(3)
    far_out.wait(range(line))
    far_ff.wait(range(line))
    links.finish()
    for copy in local:
        copy.wait()


def add_rows_of(target, values, count):
    def add(index, carry):
        rows = pl.ds(pl.multiple_of(index * 16, 16), 16)
        target[rows] = target[rows] + values[rows]
        return carry

    lax.fori_loop(0, count // 16, add, 0)


class NearSum:
    def __init__(self, links, source, own, from_core, from_first, from_second, first, in_place=False):
        self.links, self.source, self.own, self.first = links, source, own, first
        self.in_place = in_place
        self.from_core, self.from_first, self.from_second = from_core, from_first, from_second

    def start(self):
        links = self.links
        if not self.in_place:
            self.local = links.keep(self.source(links.c), self.own)
        self.copy = links.send(self.source(1 - links.c), self.from_core, "c")

    def add(self, target, values):
        add_rows_of(target, values, target.shape[0])

    def core_done(self):
        links = self.links
        self.copy.wait_recv()
        if not self.in_place:
            self.local.wait()
        for x in range(2):
            for y in range(2):
                self.add(self.own.at[x, y], self.from_core.at[x, y])
        if self.first == "x":
            self.copy = links.send(self.own.at[1 - links.x], self.from_first, "x")
        else:
            self.copy = links.send(self.own.at[:, 1 - links.y], self.from_first, "y")

    def first_done(self):
        links = self.links
        self.copy.wait_recv()
        for other in range(2):
            place = (links.x, other) if self.first == "x" else (other, links.y)
            self.add(self.own.at[place], self.from_first.at[other])
        if self.first == "x":
            self.copy = links.send(self.own.at[links.x, 1 - links.y], self.from_second, "y")
        else:
            self.copy = links.send(self.own.at[1 - links.x, links.y], self.from_second, "x")

    def second_done(self):
        self.copy.wait_recv()
        total = self.own.at[self.links.x, self.links.y]
        self.add(total, self.from_second)
        return total


def sum_space(blocks, rows, columns):
    shape = (rows, columns)
    return [
        pltpu.VMEM((blocks, 2, 2) + shape, jnp.bfloat16),
        pltpu.VMEM((blocks, 2, 2) + shape, jnp.bfloat16),
        pltpu.VMEM((blocks, 2) + shape, jnp.bfloat16),
        pltpu.VMEM((blocks,) + shape, jnp.bfloat16),
    ]


class RingSum:
    def __init__(self, links, parts, total, got, pieces=4):
        self.links, self.parts, self.total, self.got = links, parts, total, got
        self.pieces, self.last = pieces, [None] * pieces
        self.rows = parts.shape[1] // pieces

    def step(self, number):
        links = self.links
        for piece in range(self.pieces):
            way = 1 if piece < self.pieces // 2 else -1
            block = links.along(-way * (number + 1))
            where = pl.ds(piece * self.rows, self.rows)
            if number == 0:
                source = self.parts.at[block, where]
            else:
                self.last[piece].wait_recv()
                total = self.got[number - 1, where].astype(jnp.float32) + self.parts[
                    block, where
                ].astype(jnp.float32)
                if number == links.line - 1:
                    self.total[where] = total
                    continue
                self.parts[block, where] = total.astype(self.parts.dtype)
                source = self.parts.at[block, where]
            self.last[piece] = links.send(source, self.got.at[number, where], way)


def link_call(kernel, collective_id, copies, shapes, arguments, spaces=None, scratch=(), vmem=16):
    any_space = pl.BlockSpec(memory_space=pl.ANY)
    near_space = pl.BlockSpec(memory_space=pltpu.VMEM)
    many = isinstance(shapes, tuple)
    if spaces is None:
        spaces = "h" * (len(arguments) + (len(shapes) if many else 1))
    specs = [near_space if space == "v" else any_space for space in spaces]
    return pl.pallas_call(
        kernel,
        out_shape=shapes,
        in_specs=specs[: len(arguments)],
        out_specs=tuple(specs[len(arguments) :]) if many else specs[-1],
        scratch_shapes=list(scratch)
        + [pltpu.SemaphoreType.DMA((copies,)), pltpu.SemaphoreType.DMA((copies,))],
        compiler_params=pltpu.CompilerParams(
            collective_id=collective_id, has_side_effects=True, vmem_limit_bytes=vmem * 2**20
        ),
    )(*arguments)


def forward_call(small, tokens, out_grad, gain_rows, weights, line):
    span_len, width = tokens.shape
    group_len = line * span_len
    rows_each, qkv_cols = weights[0].shape[0], gain_rows.shape[1]
    q_cols = qkv_cols - 2 * HD
    both_cols = 2 * weights[3].shape[1] // line
    f32, bf16 = jnp.float32, jnp.bfloat16
    near = (line, 8, rows_each + 16, qkv_cols)
    outs = (
        ((line, span_len, width), bf16),
        (near, bf16),
        ((2, 16, width), f32),
        ((group_len, width), bf16),
        ((group_len, q_cols), bf16),
        ((2, group_len, 2 * HD), bf16),
        ((group_len, HD), f32),
        ((2, group_len, HD), f32),
        ((group_len, line * q_cols), bf16),
        ((line, 8, rows_each, both_cols), bf16),
        ((line, 8, rows_each, width), bf16),
        ((span_len, width), bf16),
    )
    return link_call(
        functools.partial(first_kernel, line),
        0,
        208,
        tuple(jax.ShapeDtypeStruct(*out) for out in outs),
        (small, tokens, out_grad, gain_rows) + weights,
        "v" + "h" * 21,
        scratch=[
            pltpu.VMEM((line, span_len, width), bf16),
            pltpu.VMEM((span_len, width), bf16),
            pltpu.VMEM((span_len, width), bf16),
            pltpu.VMEM((line,) + small.shape[1:], f32),
            pltpu.VMEM(near, bf16),
            pltpu.VMEM((2, 16, width), f32),
            pltpu.VMEM((group_len, width), bf16),
            pltpu.VMEM((2, group_len, HD), f32),
            pltpu.VMEM((group_len, qkv_cols), f32),
            pltpu.VMEM((group_len, q_cols), bf16),
            pltpu.VMEM((2, group_len, 2 * HD), bf16),
            pltpu.VMEM((group_len, HD), f32),
            pltpu.VMEM((group_len, q_cols), bf16),
        ],
        vmem=63,
    )


def mlp_kernel(
    line,
    cuts,
    small_ref,
    gain_ref,
    mix_ref,
    xs_ref,
    atts_ref,
    out_ref,
    ff_ref,
    down_ref,
    middle_ref,
    total_ref,
    output_ref,
    sum_ref,
    grad_ff_ref,
    ff_half_ref,
    big,
    ff,
    down,
    norm,
    parts,
    mixed,
    gate_up,
    hidden,
    both_grad,
    got,
    mixed_parts,
    mixed_got,
    mixed_total,
    *scratch,
):
    f32, bf16 = jnp.float32, jnp.bfloat16
    space, (send_sems, recv_sems) = scratch[:-2], scratch[-2:]
    links = Links(send_sems, recv_sems, line)
    links.meet(["x", "y", "c", 1, line - 1])
    far = [1, line - 1] + list(range(2, line - 1))
    span_len, width = mix_ref.shape
    group_len = line * span_len
    ff_cols = hidden.shape[1]
    block_rows = width // line
    rows_each = block_rows // 8
    chunk = 2 * HD
    mix_ring = LineGather(
        links, span_len, lambda rows: mix_ref.at[rows], lambda block, rows: mixed.at[block, rows]
    )
    mix_ring.step(0)
    stay = links.keep(mix_ref, mixed.at[links.z])
    early = [
        links.keep(out_ref, big),
        links.keep(atts_ref, norm),
        links.keep(xs_ref, parts),
    ]
    late = [links.keep(ff_ref, ff)]
    down_rows = down_ref.shape[0]

    def down_place(block, place):
        low, high = cuts[block]
        return down.at[pl.ds(pl.multiple_of(place * down_rows + low, 16), high - low)]

    near = NearGather(links, down_place)
    for block, (low, high) in enumerate(cuts):
        rows = down_ref.at[pl.ds(low, high - low)]
        late.append(links.keep(rows, down_place(block, links.slot)))
        near.offer(block, rows)
    ring = RingSum(links, parts, total_ref, got)
    mixed_ring = RingSum(links, mixed_parts, mixed_total, mixed_got)
    items = []
    ff_items = []
    for index, k in enumerate(far[:2]):
        block = links.along(k)
        core, first, second = space[:3]
        ff_items.append(
            NearSum(
                links,
                lambda c, block=block: ff.at[block, :, :, c],
                ff.at[block, :, :, links.c],
                core.at[index],
                first.at[index],
                second.at[index],
                "xy"[index % 2],
                True,
            )
        )
    for index, (low, high) in enumerate(cuts):
        rows = pl.ds(low, high - low)
        core, first, second = space[3 * index + 3 : 3 * index + 6]
        items.append(
            NearSum(
                links,
                lambda c, rows=rows: big.at[:, :, c, rows],
                big.at[:, :, links.c, rows],
                core.at[0],
                first.at[0],
                second.at[0],
                "xy"[index % 2],
                True,
            )
        )
    for copy in early:
        copy.wait()

    half = group_len // 2
    out_rows = width // 8
    for part in range(2):
        low = part * half
        for column in range(4):
            lanes = slice(column * width // 4, (column + 1) * width // 4)
            value = None
            for k in range(8):
                term = jnp.dot(
                    norm[low : low + half, k * out_rows : (k + 1) * out_rows],
                    big[k // 4, k // 2 % 2, k % 2, :, lanes],
                    preferred_element_type=f32,
                )
                value = term if value is None else value + term
            gate_up[:half, lanes] = value * small_ref[3, 0:1, 0:1]

        def normalise(index, carry, low=low):
            block = (low // 16 + index) // (span_len // 16)
            rows = pl.ds(pl.multiple_of(index * 16, 16), 16)
            inside = pl.ds(pl.multiple_of(lax.rem(index, span_len // 16) * 16, 16), 16)
            values = parts[block, inside].astype(f32) + gate_up[rows, :width]
            gate_up[rows, :width] = values
            inverse = lax.rsqrt(jnp.mean(values * values, axis=-1, keepdims=True) + epsilon)
            target = pl.ds(pl.multiple_of(low + index * 16, 16), 16)
            norm[target] = (values * inverse * gain_ref[1]).astype(bf16)
            return carry

        lax.fori_loop(0, half // 16, normalise, 0)

        @pl.when(links.z // (line // 2) == part)
        def _():
            where = pl.multiple_of(lax.rem(links.z, line // 2) * span_len, span_len)
            middle_ref[...] = gate_up[pl.ds(where, span_len), :width]
        if part == 0:
            mix_ring.step(1)

    for block in range(2):
        near.relay(block, "xy"[block])
    for copy in late:
        copy.wait()

    def columns_of(lanes, size):
        return ff[:, :, :, :, :, lanes].reshape(width, size)

    def forward(low, size):
        gates, ups = pl.ds(low, size), pl.ds(low + ff_cols, size)
        gate = jnp.dot(norm[...], columns_of(gates, size), preferred_element_type=f32)
        gate_up[:, gates] = gate
        swish = gate * jax.nn.sigmoid(gate)
        up = jnp.dot(norm[...], columns_of(ups, size), preferred_element_type=f32)
        gate_up[:, ups] = up
        hidden[:, gates] = (swish * up).astype(bf16)

    def backward(low, size):
        gates, ups = pl.ds(low, size), pl.ds(low + ff_cols, size)
        grad = lax.dot_general(
            mixed[...].reshape(group_len, width),
            down[gates],
            (((1,), (1,)), ((), ())),
            preferred_element_type=f32,
        )
        gate, up = gate_up[:, gates], gate_up[:, ups]
        sigmoid = jax.nn.sigmoid(gate)
        both_grad[:, gates] = (grad * up * sigmoid * (1.0 + gate * (1.0 - sigmoid))).astype(bf16)
        both_grad[:, ups] = (grad * (gate * sigmoid)).astype(bf16)

    def over_chunks(work, extent):
        def one(index, carry):
            work(pl.multiple_of(index * chunk, chunk), chunk)
            return carry

        lax.fori_loop(0, extent // chunk, one, 0)
        if extent % chunk:
            work(extent // chunk * chunk, extent % chunk)

    over_chunks(forward, ff_cols)
    mix_ring.step(2)
    for block in range(2):
        near.close(block)
    near.wait(range(2))

    def mixed_part(low, size):
        lanes = pl.ds(low, size)
        value = jnp.dot(hidden[...], down[:, lanes], preferred_element_type=f32).astype(bf16)
        mixed_parts[:, :, lanes] = value.reshape(line, span_len, size)

    over_chunks(mixed_part, width)
    mixed_ring.step(0)
    stay.wait()
    mix_ring.step(3)
    hidden_rows = hidden[...].T

    def down_part(low, size):
        lanes = pl.ds(low, size)
        value = jnp.dot(
            hidden_rows,
            mixed[:, :, lanes].reshape(group_len, size),
            preferred_element_type=f32,
        ).astype(bf16)
        big[:, :, :, : cuts[-1][1], lanes] = value.reshape(2, 2, 2, cuts[-1][1], size)

    over_chunks(down_part, width)
    for item in items:
        item.start()
    over_chunks(backward, ff_cols)
    mixed_ring.step(1)
    for item in items:
        item.core_done()

    def norm_part(index, carry):
        size = 4 * rows_each
        weight = ff[index // 2, lax.rem(index, 2)].reshape(size, 2 * ff_cols)
        value = lax.dot_general(
            both_grad[...], weight, (((1,), (1,)), ((), ())), preferred_element_type=f32
        ).astype(bf16)
        lanes = pl.ds(pl.multiple_of(index * size, size), size)
        parts[:, :, lanes] = value.reshape(line, span_len, size)
        return carry

    lax.fori_loop(0, 2 * line, norm_part, 0)
    ring.step(0)

    def ff_block(block):
        norm_rows = norm[:, pl.ds(pl.multiple_of(block * block_rows, block_rows), block_rows)].T

        def ff_part(low, size):
            lanes = pl.ds(low, size)
            value = jnp.dot(norm_rows, both_grad[:, lanes], preferred_element_type=f32)
            ff[block, :, :, :, :, lanes] = value.astype(bf16).reshape(2, 2, 2, rows_each, size)

        over_chunks(ff_part, 2 * ff_cols)

    for item, k in zip(ff_items, far):
        ff_block(links.along(k))
        item.start()
    for item in items:
        item.first_done()
    ring.step(1)
    for item in ff_items:
        item.core_done()
    mixed_ring.step(2)
    sent = []
    for k in far[2:] + [0]:
        block = links.along(k)
        ff_block(block)
        sent.append(links.keep(ff.at[block], grad_ff_ref.at[block]))
    for item, (low, high) in zip(items, cuts):
        sum_ref[low:high] = item.second_done()[...]
    ring.step(2)
    for item in ff_items:
        item.first_done()
    mixed_ring.step(3)
    for low in range(0, span_len, 16):
        rows = slice(low, low + 16)
        output_ref[rows] = (middle_ref[rows] + small_ref[3, 0:1, 0:1] * mixed_total[rows]).astype(bf16)
    ring.step(3)
    for index, item in enumerate(ff_items):
        sent.append(links.keep(item.second_done(), ff_half_ref.at[index]))
    links.finish()
    for copy in sent:
        copy.wait()


def mlp_call(small, gains, mixed, x_blocks, attended, out_w, ff_w, w_down, line):
    f32, bf16 = jnp.float32, jnp.bfloat16
    span_len, width = mixed.shape
    group_len = line * span_len
    rows, both_cols, rows_each = w_down.shape[0], ff_w.shape[3], ff_w.shape[2]
    ff_rows = 8 * rows
    ff_w = ff_w.reshape(line, 2, 2, 2, rows_each, both_cols)
    half = (rows // 2 + 15) // 16 * 16
    cuts = ((0, half), (half, rows))
    blocks = (line, span_len, width)
    token = jax.ShapeDtypeStruct((span_len, width), f32)
    return link_call(
        functools.partial(mlp_kernel, line, cuts),
        2,
        112,
        (
            token,
            token,
            jax.ShapeDtypeStruct((span_len, width), bf16),
            jax.ShapeDtypeStruct((rows, width), bf16),
            jax.ShapeDtypeStruct(ff_w.shape, bf16),
            jax.ShapeDtypeStruct((2, rows_each, both_cols), bf16),
        ),
        (small, gains, mixed, x_blocks, attended, out_w.reshape(2, 2, 2, width // 8, width), ff_w, w_down),
        "vvhhhhhh" + "vvvvhh",
        [
            pltpu.VMEM((2, 2, 2, width // 8, width), bf16),
            pltpu.VMEM(ff_w.shape, bf16),
            pltpu.VMEM((ff_rows, width), bf16),
            pltpu.VMEM((group_len, width), bf16),
            pltpu.VMEM(blocks, bf16),
            pltpu.VMEM(blocks, bf16),
            pltpu.VMEM((group_len, both_cols), f32),
            pltpu.VMEM((group_len, ff_rows), bf16),
            pltpu.VMEM((group_len, both_cols), bf16),
            pltpu.VMEM((line - 1, span_len, width), bf16),
            pltpu.VMEM(blocks, bf16),
            pltpu.VMEM((line - 1, span_len, width), bf16),
            pltpu.VMEM((span_len, width), f32),
        ]
        + sum_space(2, rows_each, both_cols)[1:]
        + sum((sum_space(1, high - low, width)[1:] for low, high in cuts), []),
        vmem=63,
    )


def backward_kernel(
    line,
    small_ref,
    gain_ref,
    middle_ref,
    norm_grad_ref,
    x_ref,
    grad_ref,
    query_ref,
    kv_ref,
    peak_ref,
    turn_ref,
    out_ref,
    atts_ref,
    weight_ref,
    norm_ref,
    ff_ref,
    ff_half_ref,
    token_ref,
    ffs_ref,
    outs_ref,
    qkvs_ref,
    x_own,
    grad_own,
    middle_grad,
    total,
    big,
    slim,
    norm,
    own_rows,
    own_columns,
    branch,
    own_grad,
    att_grad,
    query_back,
    kv_back,
    kv_out,
    kv_in,
    flat,
    parts,
    query,
    kv,
    peak,
    turns,
    *scratch,
):
    f32, bf16 = jnp.float32, jnp.bfloat16
    send_sems, recv_sems = scratch[-2:]
    got, sums = scratch[0], scratch[1:-2]
    links = Links(send_sems, recv_sems, line)
    far = [1, line - 1] + list(range(2, line - 1))
    order = far + [0]
    links.meet(["x", "y", "c"] + far)
    span_len, width = x_ref.shape
    group_len = line * span_len
    q_cols = query.shape[1]
    heads = q_cols // HD
    rows_z = width // line
    rows_each = rows_z // 8
    scale = 1.0 / math.sqrt(HD)

    def lanes_of(block):
        return pl.ds(pl.multiple_of(block * q_cols, q_cols), q_cols)

    here = pl.ds(pl.multiple_of(links.z * span_len, span_len), span_len)
    first_load = links.keep(grad_ref, grad_own)
    loads = [
        links.keep(out_ref, big),
        links.keep(atts_ref.at[here], own_rows),
        links.keep(atts_ref.at[:, lanes_of(links.z)], own_columns),
        links.keep(x_ref, x_own),
        links.keep(query_ref, query),
        links.keep(kv_ref, kv),
        links.keep(peak_ref, peak),
        links.keep(turn_ref, turns),
        links.keep(norm_ref, norm),
        links.keep(weight_ref.at[:, :, :, :, pl.ds(0, slim.shape[4])], slim),
    ]
    ring = RingSum(links, parts, total, got)

    def items_of(source, space, in_place, order=order):
        items = []
        for index, k in enumerate(order):
            block = links.along(k)
            own = source.at[block, :, :, links.c] if in_place else space[0].at[index]
            core, first, second = space[-3:]
            items.append(
                NearSum(
                    links,
                    lambda c, block=block: source.at[block, :, :, c],
                    own,
                    core.at[index],
                    first.at[index],
                    second.at[index],
                    "xy"[index % 2],
                    in_place,
                )
            )
        return items

    ff_order = order[2:]
    ff_items = items_of(ff_ref, sums[:4], False, ff_order)
    out_items = items_of(big, sums[4:7], True)
    qkv_items = items_of(slim, sums[7:], True)
    local, arrived = [], []
    ff_cols = ff_ref.shape[5] // 2
    ff_pieces = ((0, ff_cols), (ff_cols, ff_cols))
    qkv_pieces = ((0, q_cols), (q_cols, HD), (q_cols + HD, HD))

    def deliver(total, target, k, pieces):
        for low, size in pieces:
            if pieces == out_pieces:
                place = target.at[links.z]
            else:
                lanes = pl.multiple_of(line * low + links.z * size, HD)
                place = target.at[:, pl.ds(lanes, size)]
            part = total.at[:, pl.ds(low, size)]
            if k == 0:
                local.append(links.keep(part, place))
            else:
                arrived.append(links.send(part, place, k))

    out_pieces = ((0, width),)
    for index, k in enumerate(order[:2]):
        deliver(ff_half_ref.at[index], ffs_ref, k, ff_pieces)
    def turn(items, target, low, high, pieces, order=order):
        for item, k in list(zip(items, order))[low:high]:
            deliver(item.second_done(), target, k, pieces)

    def core_done(items, low, high):
        for item in items[low:high]:
            item.core_done()

    def first_done(items, low, high):
        for item in items[low:high]:
            item.first_done()

    half = line // 2
    for item in ff_items:
        item.start()

    first_load.wait()
    keep = small_ref[3, 0:1, 0:1]
    token_scale = column_of(small_ref[1, 0:1])

    def norm_back(values, grad, gain):
        inverse = lax.rsqrt(jnp.mean(values * values, axis=-1, keepdims=True) + epsilon)
        scaled = gain * grad
        return inverse * scaled - values * (inverse * inverse * inverse) * jnp.mean(
            scaled * values, axis=-1, keepdims=True
        )

    for low in range(0, span_len, 16):
        rows = slice(low, low + 16)
        upstream = grad_own[rows].astype(f32) * token_scale[rows]
        grad = upstream + norm_back(middle_ref[rows], norm_grad_ref[rows], gain_ref[1])
        middle_grad[rows] = grad
        branch[rows] = (grad * keep).astype(bf16)
    for copy in loads:
        copy.wait()
    for z in range(line):
        weight = big[z].reshape(rows_z, width)
        own_grad[:, z * rows_z : (z + 1) * rows_z] = lax.dot_general(
            branch[...], weight, (((1,), (1,)), ((), ())), preferred_element_type=f32
        ).astype(bf16)
    turned = [links.send(own_grad.at[:, lanes_of(links.along(k))], att_grad.at[here], k) for k in far]
    stayed = links.keep(own_grad.at[:, lanes_of(links.z)], att_grad.at[here])
    core_done(ff_items, 0, line)
    for z in range(line):
        for part in range(4):
            columns = slice(part * width // 4, (part + 1) * width // 4)
            grad = lax.dot_general(
                own_rows[:, z * rows_z : (z + 1) * rows_z],
                branch[:, columns],
                (((0,), (0,)), ((), ())),
                preferred_element_type=f32,
            )
            big[z, :, :, :, :, columns] = grad.astype(bf16).reshape(2, 2, 2, rows_each, width // 4)
    for item in out_items:
        item.start()
    kv_back[...] = jnp.zeros_like(kv_back)
    for copy in turned:
        copy.wait_recv()
    stayed.wait()

    def attend_back(head, carry):
        lanes = pl.ds(pl.multiple_of(head * HD, HD), HD)
        for block in range(line):
            rows = slice(block * span_len, (block + 1) * span_len)
            reach = (block + 1) * span_len
            part, grad = query[rows, lanes], att_grad[rows, lanes]
            row = lax.broadcasted_iota(jnp.int32, (span_len, reach), 0) + block * span_len
            column = lax.broadcasted_iota(jnp.int32, (span_len, reach), 1)
            allowed = (column <= row, column < (block + links.x) * span_len)
            spot = lax.broadcasted_iota(jnp.int32, (span_len, HD), 1) == head
            top = jnp.sum(jnp.where(spot, peak[rows], 0.0), axis=-1, keepdims=True)
            delta = jnp.sum(
                grad.astype(f32) * own_columns[rows, lanes].astype(f32), axis=-1, keepdims=True
            )
            back = None
            for side in range(2):
                keys, values = kv[side, :reach, :HD], kv[side, :reach, HD:]
                score = lax.dot_general(
                    part, keys, (((1,), (1,)), ((), ())), preferred_element_type=f32
                )
                weight = jnp.where(allowed[side], jnp.exp(score * scale - top), 0.0)
                weight_grad = lax.dot_general(
                    grad, values, (((1,), (1,)), ((), ())), preferred_element_type=f32
                )
                score_grad = (weight * (weight_grad - delta)).astype(bf16)
                term = jnp.dot(score_grad, keys, preferred_element_type=f32)
                back = term if back is None else back + term
                kv_back[side, :reach, :HD] += lax.dot_general(
                    score_grad, part, (((0,), (0,)), ((), ())), preferred_element_type=f32
                )
                kv_back[side, :reach, HD:] += lax.dot_general(
                    weight.astype(bf16), grad, (((0,), (0,)), ((), ())), preferred_element_type=f32
                )
            query_back[rows, lanes] = back * scale
        return carry

    lax.fori_loop(0, heads, attend_back, 0)
    kv_out[:, :HD] = (kv_back[1, :, :HD] * scale).astype(bf16)
    kv_out[:, HD:] = kv_back[1, :, HD:].astype(bf16)
    exchange = links.send(kv_out, kv_in, "x")

    def turn_back(values, rows):
        return values * turns[0, rows] - pltpu.roll(values, HD // 2, 1) * turns[1, rows]

    for block in range(line):
        rows = slice(block * span_len, (block + 1) * span_len)
        for head in range(heads):
            lanes = slice(head * HD, (head + 1) * HD)
            flat[rows, lanes] = turn_back(query_back[rows, lanes], rows).astype(bf16)
    first_done(ff_items, 0, line)
    exchange.wait_recv()
    for block in range(line):
        rows = slice(block * span_len, (block + 1) * span_len)
        key_grad = kv_back[0, rows, :HD] * scale + kv_in[rows, :HD].astype(f32)
        flat[rows, q_cols : q_cols + HD] = turn_back(key_grad, rows).astype(bf16)
        value_grad = kv_back[0, rows, HD:] + kv_in[rows, HD:].astype(f32)
        flat[rows, q_cols + HD :] = value_grad.astype(bf16)
    for z in range(line):
        weight = slim[z].reshape(rows_z, flat.shape[1])
        part = lax.dot_general(
            flat[...], weight, (((1,), (1,)), ((), ())), preferred_element_type=f32
        ).astype(bf16)
        for block in range(line):
            parts[block, :, z * rows_z : (z + 1) * rows_z] = part[
                block * span_len : (block + 1) * span_len
            ]
    ring.step(0)
    for z in range(line):
        grad = lax.dot_general(
            norm[:, z * rows_z : (z + 1) * rows_z],
            flat[...],
            (((0,), (0,)), ((), ())),
            preferred_element_type=f32,
        )
        slim[z] = grad.astype(bf16).reshape(2, 2, 2, rows_each, flat.shape[1])
    for item in qkv_items:
        item.start()
    core_done(out_items, 0, half)
    turn(ff_items, ffs_ref, 0, line, ff_pieces, ff_order)
    ring.step(1)
    core_done(out_items, half, line)
    first_done(out_items, 0, half)
    ring.step(2)
    core_done(qkv_items, 0, line)
    first_done(out_items, half, line)
    turn(out_items, outs_ref, 0, half, out_pieces)
    ring.step(3)
    for low in range(0, span_len, 16):
        rows = slice(low, low + 16)
        grad = middle_grad[rows] + norm_back(x_own[rows].astype(f32), total[rows], gain_ref[0])
        token_ref[rows] = grad.astype(bf16)
    first_done(qkv_items, 0, half)
    turn(out_items, outs_ref, half, line, out_pieces)
    first_done(qkv_items, half, line)
    turn(qkv_items, qkvs_ref, 0, line, qkv_pieces)
    for copy in arrived:
        copy.wait_recv()
    links.finish()
    for copy in local:
        copy.wait()


def backward_call(near, tokens, saved, out_w, attended, weights, norm, grad_ff, ff_half, line):
    f32, bf16 = jnp.float32, jnp.bfloat16
    span_len, width = tokens[0].shape
    group_len = line * span_len
    query = saved[0]
    q_cols, rows_each, qkv_cols = query.shape[1], width // line // 8, weights.shape[3]
    weights = weights.reshape(line, 2, 2, 2, -1, qkv_cols)
    wide = (line, 2, 2, 2, rows_each, width)
    slim = (line, 2, 2, 2, rows_each, qkv_cols)
    out_space = sum_space(line, rows_each, width)[1:]
    qkv_space = sum_space(line, rows_each, qkv_cols)[1:]
    token = jax.ShapeDtypeStruct((span_len, width), bf16)
    return link_call(
        functools.partial(backward_kernel, line),
        4,
        160,
        (token,)
        + (
            jax.ShapeDtypeStruct((rows_each, line * grad_ff.shape[5]), bf16),
            jax.ShapeDtypeStruct((line, rows_each, width), bf16),
            jax.ShapeDtypeStruct((rows_each, line * qkv_cols), bf16),
        ),
        near + tokens + saved + (out_w.reshape(wide), attended, weights, norm, grad_ff, ff_half),
        "v" * 4 + "h" * 12 + "vhhh",
        [pltpu.VMEM((span_len, width), bf16)] * 2
        + [pltpu.VMEM((span_len, width), f32)] * 2
        + [
            pltpu.VMEM(wide, bf16),
            pltpu.VMEM(slim, bf16),
            pltpu.VMEM((group_len, width), bf16),
            pltpu.VMEM((span_len, width), bf16),
            pltpu.VMEM((group_len, q_cols), bf16),
            pltpu.VMEM((span_len, width), bf16),
            pltpu.VMEM((span_len, width), bf16),
            pltpu.VMEM((group_len, q_cols), bf16),
            pltpu.VMEM((group_len, q_cols), f32),
            pltpu.VMEM((2, group_len, 2 * HD), f32),
            pltpu.VMEM((group_len, 2 * HD), bf16),
            pltpu.VMEM((group_len, 2 * HD), bf16),
            pltpu.VMEM((group_len, qkv_cols), bf16),
            pltpu.VMEM((line, span_len, width), bf16),
        ]
        + [pltpu.VMEM(value.shape, value.dtype) for value in saved]
        + [pltpu.VMEM((line - 1, span_len, width), bf16)]
        + sum_space(line - 2, rows_each, grad_ff.shape[5])
        + out_space
        + qkv_space,
        vmem=63,
    )


def general_body(
    tokens,
    attn_gain,
    w_query,
    w_key,
    w_value,
    w_out,
    mlp_gain,
    w_gate,
    w_up,
    w_down,
    keep_mask,
    group_ids,
    positions,
    exit_scale,
    out_grad,
):
    seq_count, span_len, model_width = tokens.shape
    kv_heads = KVH
    head_dim = HD
    head_count = HEADS
    group_size = head_count // kv_heads
    row_count = seq_count * span_len
    stripe = group_size * span_len
    wide_count = lax.axis_size("wide")
    wide_place = lax.axis_index("wide")
    full_len = span_len * wide_count
    score_scale = 1.0 / math.sqrt(head_dim)
    gain_one, query_w, key_w, value_w, out_w = (
        lax.all_gather(attn_gain, ("wide", "narrow"), axis=0, tiled=True),
        lax.all_gather(w_query, ("wide", "narrow"), axis=0, tiled=True),
        lax.all_gather(w_key, ("wide", "narrow"), axis=0, tiled=True),
        lax.all_gather(w_value, ("wide", "narrow"), axis=0, tiled=True),
        lax.all_gather(w_out, ("wide", "narrow"), axis=0, tiled=True),
    )
    inputs = tokens.astype(jnp.float32).reshape(row_count, model_width)
    token_pos = positions.reshape(row_count)
    keep_rows = jnp.repeat(keep_mask.astype(jnp.float32), span_len)[:, None]
    inverse_one = lax.rsqrt(jnp.mean(inputs * inputs, axis=-1, keepdims=True) + epsilon)
    first_norm = (inputs * inverse_one * gain_one.astype(jnp.float32)).astype(jnp.bfloat16)
    query_pre = jnp.dot(first_norm, query_w, preferred_element_type=jnp.float32).reshape(
        row_count, head_count, head_dim
    )
    key_pre = jnp.dot(first_norm, key_w, preferred_element_type=jnp.float32).reshape(
        row_count, kv_heads, head_dim
    )
    query_rows = rotate(query_pre, token_pos, 1.0).astype(jnp.bfloat16)
    key_heads = (
        rotate(key_pre, token_pos, 1.0)
        .astype(jnp.bfloat16)
        .reshape(seq_count, span_len, kv_heads * head_dim)
    )
    value_heads = (
        jnp.dot(first_norm, value_w, preferred_element_type=jnp.float32)
        .astype(jnp.bfloat16)
        .reshape(seq_count, span_len, kv_heads * head_dim)
    )
    queries = (
        query_rows.reshape(seq_count, span_len, kv_heads, group_size, head_dim)
        .transpose(0, 2, 3, 1, 4)
        .reshape(seq_count, kv_heads, stripe, head_dim)
    )
    query_index = wide_place * span_len + jnp.arange(stripe, dtype=jnp.int32) % span_len
    last_query = wide_place * span_len + span_len - 1

    def block_scores(key_block, key_first):
        scores = (
            jnp.einsum("skrd,sjkd->skrj", queries, key_block, preferred_element_type=jnp.float32)
            * score_scale
        )
        key_index = key_first + jnp.arange(key_block.shape[1], dtype=jnp.int32)
        allowed = key_index[None, :] <= query_index[:, None]
        return (scores, allowed)

    start_forward = (
        jnp.full((seq_count, kv_heads, stripe), -1e30, jnp.float32),
        jnp.zeros((seq_count, kv_heads, stripe), jnp.float32),
        jnp.zeros((seq_count, kv_heads, stripe, head_dim), jnp.float32),
    )
    running = start_forward
    pieces = (
        lax.all_gather(key_heads, "wide", axis=1, tiled=True),
        lax.all_gather(value_heads, "wide", axis=1, tiled=True),
    )
    key_blocks = split_blocks(pieces[0], seq_count, kv_heads, head_dim)
    value_blocks = split_blocks(pieces[1], seq_count, kv_heads, head_dim)
    block_len = key_blocks.shape[2]

    def advance(carried, block_item):
        key_block, value_block, block_index = block_item
        key_first = block_index * block_len

        def compute_block(current):
            run_max, run_sum, run_acc = current
            scores, allowed = block_scores(key_block, key_first)
            scores = jnp.where(allowed, scores, -1e30)
            new_max = jnp.maximum(run_max, jnp.max(scores, axis=-1))
            factor = jnp.exp(run_max - new_max)
            weights = jnp.where(allowed, jnp.exp(scores - new_max[..., None]), 0.0)
            new_sum = run_sum * factor + jnp.sum(weights, axis=-1)
            new_acc = run_acc * factor[..., None] + jnp.einsum(
                "skrj,sjkd->skrd",
                weights.astype(jnp.bfloat16),
                value_block,
                preferred_element_type=jnp.float32,
            )
            return (new_max, new_sum, new_acc)

        return (lax.cond(key_first <= last_query, compute_block, unchanged, carried), None)

    running, _ = lax.scan(
        advance,
        running,
        (key_blocks, value_blocks, jnp.arange(key_blocks.shape[0], dtype=jnp.int32)),
    )
    run_max, run_sum, run_acc = running
    attended = run_acc / run_sum[..., None]
    log_total = run_max + jnp.log(run_sum)
    attended_rows = (
        attended.reshape(seq_count, kv_heads, group_size, span_len, head_dim)
        .transpose(0, 3, 1, 2, 4)
        .reshape(row_count, head_count * head_dim)
        .astype(jnp.bfloat16)
    )
    middle = inputs + keep_rows * jnp.dot(attended_rows, out_w, preferred_element_type=jnp.float32)
    gain_two, gate_w, up_w, down_w = (
        lax.all_gather(mlp_gain, ("wide", "narrow"), axis=0, tiled=True),
        lax.all_gather(w_gate, ("wide", "narrow"), axis=0, tiled=True),
        lax.all_gather(w_up, ("wide", "narrow"), axis=0, tiled=True),
        lax.all_gather(w_down, ("wide", "narrow"), axis=0, tiled=True),
    )
    inverse_two = lax.rsqrt(jnp.mean(middle * middle, axis=-1, keepdims=True) + epsilon)
    second_norm = (middle * inverse_two * gain_two.astype(jnp.float32)).astype(jnp.bfloat16)
    gate_value = jnp.dot(second_norm, gate_w, preferred_element_type=jnp.float32)
    up_value = jnp.dot(second_norm, up_w, preferred_element_type=jnp.float32)
    gate_sigmoid = jax.nn.sigmoid(gate_value)
    swish_value = gate_value * gate_sigmoid
    hidden = (swish_value * up_value).astype(jnp.bfloat16)
    output = (
        middle + keep_rows * jnp.dot(hidden, down_w, preferred_element_type=jnp.float32)
    ).astype(jnp.bfloat16)
    group_match = (
        group_ids.reshape(row_count)[:, None]
        == jnp.arange(exit_scale.shape[0], dtype=jnp.int32)[None, :]
    )
    token_scale = jnp.sum(jnp.where(group_match, exit_scale[None, :], 0.0), axis=1, keepdims=True)
    upstream = out_grad.astype(jnp.float32).reshape(row_count, model_width) * token_scale
    gain_two, gate_w, up_w, down_w = (
        lax.all_gather(mlp_gain, ("wide", "narrow"), axis=0, tiled=True),
        lax.all_gather(w_gate, ("wide", "narrow"), axis=0, tiled=True),
        lax.all_gather(w_up, ("wide", "narrow"), axis=0, tiled=True),
        lax.all_gather(w_down, ("wide", "narrow"), axis=0, tiled=True),
    )
    mixed_grad = (keep_rows * upstream).astype(jnp.bfloat16)
    grad_down = over_rows(hidden, mixed_grad)
    hidden_grad = against(mixed_grad, down_w)
    gate_grad = (
        hidden_grad * up_value * gate_sigmoid * (1.0 + gate_value * (1.0 - gate_sigmoid))
    ).astype(jnp.bfloat16)
    up_grad = (hidden_grad * swish_value).astype(jnp.bfloat16)
    grad_gate = over_rows(second_norm, gate_grad)
    grad_up = over_rows(second_norm, up_grad)
    norm_grad = against(gate_grad, gate_w) + against(up_grad, up_w)
    grad_gain_two = jnp.sum(norm_grad * middle * inverse_two, axis=0)
    scaled_two = gain_two.astype(jnp.float32) * norm_grad
    middle_grad = (
        upstream
        + inverse_two * scaled_two
        - middle
        * (inverse_two * inverse_two * inverse_two)
        * jnp.mean(scaled_two * middle, axis=-1, keepdims=True)
    )
    gain_two_share, gate_share, up_share, down_share = (
        lax.psum_scatter(grad_gain_two, ("wide", "narrow"), scatter_dimension=0, tiled=True),
        lax.psum_scatter(grad_gate, ("wide", "narrow"), scatter_dimension=0, tiled=True),
        lax.psum_scatter(grad_up, ("wide", "narrow"), scatter_dimension=0, tiled=True),
        lax.psum_scatter(grad_down, ("wide", "narrow"), scatter_dimension=0, tiled=True),
    )
    gain_one, query_w, key_w, value_w, out_w = (
        lax.all_gather(attn_gain, ("wide", "narrow"), axis=0, tiled=True),
        lax.all_gather(w_query, ("wide", "narrow"), axis=0, tiled=True),
        lax.all_gather(w_key, ("wide", "narrow"), axis=0, tiled=True),
        lax.all_gather(w_value, ("wide", "narrow"), axis=0, tiled=True),
        lax.all_gather(w_out, ("wide", "narrow"), axis=0, tiled=True),
    )
    branch_grad = (keep_rows * middle_grad).astype(jnp.bfloat16)
    grad_out = over_rows(attended_rows, branch_grad)
    attended_grad = against(branch_grad, out_w).astype(jnp.bfloat16)
    grouped_grad = (
        attended_grad.reshape(seq_count, span_len, kv_heads, group_size, head_dim)
        .transpose(0, 2, 3, 1, 4)
        .reshape(seq_count, kv_heads, stripe, head_dim)
    )
    row_delta = jnp.sum(grouped_grad.astype(jnp.float32) * attended, axis=-1)
    start_backward = (
        jnp.zeros((seq_count, kv_heads, stripe, head_dim), jnp.float32),
        jnp.zeros((seq_count, full_len, kv_heads * head_dim), jnp.float32),
        jnp.zeros((seq_count, full_len, kv_heads * head_dim), jnp.float32),
    )
    running = start_backward
    pieces = (
        lax.all_gather(key_heads, "wide", axis=1, tiled=True),
        lax.all_gather(value_heads, "wide", axis=1, tiled=True),
    )
    key_blocks = split_blocks(pieces[0], seq_count, kv_heads, head_dim)
    value_blocks = split_blocks(pieces[1], seq_count, kv_heads, head_dim)
    fold_block_len = key_blocks.shape[2]

    def advance(carried, block_item):
        key_block, value_block, block_index = block_item
        key_first = block_index * fold_block_len

        def compute_block(current):
            query_acc, key_acc, value_acc = current
            scores, allowed = block_scores(key_block, key_first)
            probabilities = jnp.where(allowed, jnp.exp(scores - log_total[..., None]), 0.0)
            value_part = jnp.einsum(
                "skrj,skrd->sjkd",
                probabilities.astype(jnp.bfloat16),
                grouped_grad,
                preferred_element_type=jnp.float32,
            )
            prob_grad = jnp.einsum(
                "skrd,sjkd->skrj", grouped_grad, value_block, preferred_element_type=jnp.float32
            )
            score_grad = (probabilities * (prob_grad - row_delta[..., None])).astype(jnp.bfloat16)
            query_acc = (
                query_acc
                + jnp.einsum(
                    "skrj,sjkd->skrd", score_grad, key_block, preferred_element_type=jnp.float32
                )
                * score_scale
            )
            key_part = (
                jnp.einsum(
                    "skrj,skrd->sjkd", score_grad, queries, preferred_element_type=jnp.float32
                )
                * score_scale
            )
            key_acc = add_rows(
                key_acc, key_part.reshape(seq_count, fold_block_len, kv_heads * head_dim), key_first
            )
            value_acc = add_rows(
                value_acc,
                value_part.reshape(seq_count, fold_block_len, kv_heads * head_dim),
                key_first,
            )
            return (query_acc, key_acc, value_acc)

        return (lax.cond(key_first <= last_query, compute_block, unchanged, carried), None)

    running, _ = lax.scan(
        advance,
        running,
        (key_blocks, value_blocks, jnp.arange(key_blocks.shape[0], dtype=jnp.int32)),
    )
    query_acc, key_acc, value_acc = running
    key_sum, value_sum = (
        lax.psum_scatter(
            key_acc.astype(jnp.bfloat16), "wide", scatter_dimension=1, tiled=True
        ).astype(jnp.float32),
        lax.psum_scatter(
            value_acc.astype(jnp.bfloat16), "wide", scatter_dimension=1, tiled=True
        ).astype(jnp.float32),
    )
    query_back = (
        query_acc.reshape(seq_count, kv_heads, group_size, span_len, head_dim)
        .transpose(0, 3, 1, 2, 4)
        .reshape(row_count, head_count, head_dim)
    )
    query_grad = (
        rotate(query_back, token_pos, -1.0)
        .reshape(row_count, head_count * head_dim)
        .astype(jnp.bfloat16)
    )
    key_grad = (
        rotate(key_sum.reshape(row_count, kv_heads, head_dim), token_pos, -1.0)
        .reshape(row_count, kv_heads * head_dim)
        .astype(jnp.bfloat16)
    )
    value_grad = value_sum.reshape(row_count, kv_heads * head_dim).astype(jnp.bfloat16)
    grad_query = over_rows(first_norm, query_grad)
    grad_key = over_rows(first_norm, key_grad)
    grad_value = over_rows(first_norm, value_grad)
    input_norm_grad = (
        against(query_grad, query_w) + against(key_grad, key_w) + against(value_grad, value_w)
    )
    grad_gain_one = jnp.sum(input_norm_grad * inputs * inverse_one, axis=0)
    scaled_one = gain_one.astype(jnp.float32) * input_norm_grad
    input_grad = (
        middle_grad
        + inverse_one * scaled_one
        - inputs
        * (inverse_one * inverse_one * inverse_one)
        * jnp.mean(scaled_one * inputs, axis=-1, keepdims=True)
    )
    gain_one_share, query_share, key_share, value_share, out_share = (
        lax.psum_scatter(grad_gain_one, ("wide", "narrow"), scatter_dimension=0, tiled=True),
        lax.psum_scatter(grad_query, ("wide", "narrow"), scatter_dimension=0, tiled=True),
        lax.psum_scatter(grad_key, ("wide", "narrow"), scatter_dimension=0, tiled=True),
        lax.psum_scatter(grad_value, ("wide", "narrow"), scatter_dimension=0, tiled=True),
        lax.psum_scatter(grad_out, ("wide", "narrow"), scatter_dimension=0, tiled=True),
    )
    return (
        output.reshape(seq_count, span_len, model_width),
        input_grad.astype(jnp.bfloat16).reshape(seq_count, span_len, model_width),
        gain_one_share,
        query_share,
        key_share,
        value_share,
        out_share,
        gain_two_share,
        gate_share,
        up_share,
        down_share,
    )


def line_body(
    tokens,
    attn_gain,
    w_query,
    w_key,
    w_value,
    w_out,
    mlp_gain,
    w_gate,
    w_up,
    w_down,
    keep_mask,
    group_ids,
    positions,
    exit_scale,
    out_grad,
):
    f32 = jnp.float32
    bf16 = jnp.bfloat16
    _, span_len, model_width = tokens.shape
    line = lax.axis_size("z")
    rows_each = w_query.shape[0]
    q_cols = HEADS // line * HD

    token_scale = jnp.zeros((span_len,), f32)
    for group in range(exit_scale.shape[0]):
        token_scale = jnp.where(group_ids[0] == group, exit_scale[group], token_scale)
    lane = jnp.arange(span_len, dtype=jnp.int32)
    rates = 10000.0 ** (-2.0 * (lane % (HD // 2)).astype(f32) / HD)
    row = lax.broadcasted_iota(jnp.int32, (4, 8, span_len), 0)
    small = jnp.where(row == 2, rates, keep_mask[0].astype(f32))
    small = jnp.where(row == 1, token_scale, small)
    small = jnp.where(row == 0, positions[0].astype(f32), small)

    core = lax.axis_index("c")
    spot = lax.broadcasted_iota(jnp.int32, (16, q_cols + 2 * HD), 1) // rows_each
    repeats = (q_cols + 2 * HD) // rows_each
    gain_rows = jnp.where(spot == 2 + core, jnp.tile(mlp_gain, repeats), 0)
    gain_rows = jnp.where(spot == core, jnp.tile(attn_gain, repeats), gain_rows).astype(bf16)
    (
        x_blocks,
        near_w,
        gain_all,
        first_norm,
        queries,
        both_kv,
        log_total,
        turns,
        attended_rows,
        ff_w,
        out_w,
        own_mixed,
    ) = forward_call(
        small,
        tokens[0],
        out_grad[0],
        gain_rows,
        (w_query, w_key, w_value, w_gate, w_up, w_out),
        line,
    )
    middle, norm_grad, output, grad_down, grad_ff, ff_half = mlp_call(
        small,
        gain_all,
        own_mixed,
        x_blocks,
        attended_rows,
        out_w,
        ff_w,
        w_down,
        line,
    )
    grad_down = grad_down.astype(f32)
    token_grad, ff_back, out_back, qkv_back = backward_call(
        (small, gain_all, middle, norm_grad),
        (tokens[0], out_grad[0]),
        (queries, both_kv, log_total, turns),
        out_w,
        attended_rows,
        near_w,
        first_norm,
        grad_ff,
        ff_half,
        line,
    )
    ff_back = ff_back.astype(f32)
    qkv_back = qkv_back.astype(f32)
    grad_out = jnp.sum(out_back.astype(f32), axis=0)
    heads_end, keys_end = w_query.shape[1], w_query.shape[1] + w_key.shape[1]
    grad_query = qkv_back[:, :heads_end]
    grad_key = qkv_back[:, heads_end:keys_end]
    grad_value = qkv_back[:, keys_end:]
    grad_gate = ff_back[:, : w_gate.shape[1]]
    grad_up = ff_back[:, w_gate.shape[1] :]

    def gain_grad(pairs, gain):
        total = sum(jnp.sum(weight.astype(f32) * grad, axis=1) for weight, grad in pairs)
        return total / gain.astype(f32)

    return (
        output[None],
        token_grad[None],
        gain_grad([(w_query, grad_query), (w_key, grad_key), (w_value, grad_value)], attn_gain),
        grad_query,
        grad_key,
        grad_value,
        grad_out,
        gain_grad([(w_gate, grad_gate), (w_up, grad_up)], mlp_gain),
        grad_gate,
        grad_up,
        grad_down,
    )


def solution(mesh):
    wide, narrow = mesh.shape["wide"], mesh.shape["narrow"]
    if wide == 2 * KVH and narrow == 4:
        mesh = Mesh(mesh.devices.reshape(wide // 2, 2, 2, 2), ("z", "x", "y", "c"))
        body, wide, narrow = line_body, ("z", "x"), ("y", "c")
    else:
        body, wide, narrow = general_body, ("wide",), ("narrow",)
    token_spec = P(narrow, wide, None)
    id_spec = P(narrow, wide)
    gain_spec = P(wide + narrow)
    weight_spec = P(wide + narrow, None)
    return jax.shard_map(
        body,
        mesh=mesh,
        in_specs=(
            token_spec,
            gain_spec,
            weight_spec,
            weight_spec,
            weight_spec,
            weight_spec,
            gain_spec,
            weight_spec,
            weight_spec,
            weight_spec,
            P(narrow),
            id_spec,
            id_spec,
            P(),
            token_spec,
        ),
        out_specs=(
            token_spec,
            token_spec,
            gain_spec,
            weight_spec,
            weight_spec,
            weight_spec,
            weight_spec,
            gain_spec,
            weight_spec,
            weight_spec,
            weight_spec,
        ),
        check_vma=False,
    )
```

```python
import functools
import math

import jax
import jax.numpy as jnp
from jax import lax
from jax.experimental import pallas as pl
from jax.experimental.pallas import tpu as pltpu
from jax.sharding import Mesh
from jax.sharding import PartitionSpec as P

HEADS = 16
KVH = 4
HD = 128


epsilon = 1e-05


def rotate(vectors, token_pos, direction):
    half_size = vectors.shape[-1] // 2
    freqs = 10000.0 ** (-2.0 * jnp.arange(half_size, dtype=jnp.float32) / vectors.shape[-1])
    angles = token_pos.astype(jnp.float32)[:, None] * freqs[None, :]
    cosine = jnp.cos(angles)[:, None, :]
    sine = direction * jnp.sin(angles)[:, None, :]
    first_half = vectors[..., :half_size]
    second_half = vectors[..., half_size:]
    return jnp.concatenate(
        [first_half * cosine - second_half * sine, second_half * cosine + first_half * sine],
        axis=-1,
    )


def split_blocks(piece_arr, seq_count, kv_heads, head_dim):
    piece_len = piece_arr.shape[1]
    block_len = math.gcd(piece_len, 512)
    shaped = piece_arr.reshape(seq_count, piece_len // block_len, block_len, kv_heads, head_dim)
    return shaped.transpose(1, 0, 2, 3, 4)


def add_rows(whole_arr, update, first_row):
    current = lax.dynamic_slice_in_dim(whole_arr, first_row, update.shape[1], 1)
    return lax.dynamic_update_slice_in_dim(whole_arr, current + update, first_row, 1)


def over_rows(left, right):
    return lax.dot_general(
        left, right, (((0,), (0,)), ((), ())), preferred_element_type=jnp.float32
    )


def against(left, right):
    return lax.dot_general(
        left, right, (((1,), (1,)), ((), ())), preferred_element_type=jnp.float32
    )


def unchanged(carried):
    return carried


MESH = pl.DeviceIdType.MESH
AXES = ("z", "x", "y", "c")


def only(when, act):
    if when is None:
        act()
    else:
        pl.when(when)(act)


class Links:
    def __init__(self, send_sems, recv_sems, line):
        self.send_sems, self.recv_sems, self.line = send_sems, recv_sems, line
        self.z, self.x, self.y, self.c = (lax.axis_index(name) for name in AXES)
        self.slot = self.x * 4 + self.y * 2 + self.c
        self.used = 0
        self.sent = []

    def device(self, to):
        if to == "x":
            return (self.z, 1 - self.x, self.y, self.c)
        if to == "y":
            return (self.z, self.x, 1 - self.y, self.c)
        if to == "c":
            return (self.z, self.x, self.y, 1 - self.c)
        return (self.along(to), self.x, self.y, self.c)

    def along(self, step):
        return lax.rem(self.z + step + self.line, self.line)

    def other(self, to):
        slot = self.slot
        for name in to:
            bit = {"x": 4, "y": 2, "c": 1}[name]
            here = {"x": self.x, "y": self.y, "c": self.c}[name]
            slot = slot + bit * (1 - 2 * here)
        return slot

    def meet(self, targets):
        barrier = pltpu.get_barrier_semaphore()
        for to in targets:
            pl.semaphore_signal(barrier, inc=1, device_id=self.device(to), device_id_type=MESH)
        pl.semaphore_wait(barrier, len(targets))

    def send(self, source, target, to, when=None):
        copy = pltpu.make_async_remote_copy(
            src_ref=source,
            dst_ref=target,
            send_sem=self.send_sems.at[self.used],
            recv_sem=self.recv_sems.at[self.used],
            device_id=self.device(to),
            device_id_type=MESH,
        )
        only(when, copy.start)
        self.used += 1
        self.sent.append((copy, when))
        return copy

    def keep(self, source, target):
        copy = pltpu.make_async_copy(source, target, self.send_sems.at[self.used])
        copy.start()
        self.used += 1
        return copy

    def finish(self):
        for copy, when in self.sent:
            only(when, copy.wait_send)


class NearGather:
    def __init__(self, links, slot):
        self.links, self.slot = links, slot
        self.got = {}

    def offer(self, block, source):
        target = self.slot(block, self.links.slot)
        for to in ("x", "y", "c"):
            self.got[block, to] = self.links.send(source, target, to)

    def relay(self, block, first):
        links = self.links
        for to, then in (("x", "y"), ("y", "x")):
            self.got[block, to].wait_recv()
            place = self.slot(block, links.other(to))
            self.got[block, to + "c"] = links.send(place, place, "c")
            if to == first:
                self.got[block, "xy"] = links.send(place, place, then)

    def close(self, block):
        self.got[block, "xy"].wait_recv()
        place = self.slot(block, self.links.other("xy"))
        self.got[block, "xyc"] = self.links.send(place, place, "c")

    def wait(self, blocks):
        for block in blocks:
            for to in ("c", "xc", "yc", "xyc"):
                self.got[block, to].wait_recv()


class LineGather:
    def __init__(self, links, rows, origin, place, pieces=2):
        self.links, self.origin, self.place = links, origin, place
        self.pieces, self.rows = pieces, rows // pieces
        self.last = {}

    def inside(self, block):
        return jnp.logical_and(block >= 0, block < self.links.line)

    def step(self, number):
        z = self.links.z
        for piece in range(self.pieces):
            for way in (1, -1):
                held = self.inside(z - way * number)
                if number > 0:
                    only(held, self.last[piece, way].wait_recv)
                if number == self.links.line - 1:
                    continue
                rows = pl.ds(piece * self.rows, self.rows)
                place = self.place(self.links.along(-way * number), rows)
                source = self.origin(rows) if number == 0 else place
                when = jnp.logical_and(held, self.inside(z + way))
                self.last[piece, way] = self.links.send(source, place, way, when)


class RingGather:
    def __init__(self, links, rows, origin, place, pieces=4):
        self.links, self.origin, self.place = links, origin, place
        self.pieces, self.rows = pieces, rows // pieces
        self.last = [None] * pieces

    def step(self, number):
        if number > 0:
            for copy in self.last:
                copy.wait_recv()
        if number == self.links.line - 1:
            return
        for piece in range(self.pieces):
            way = 1 if piece < self.pieces // 2 else -1
            rows = pl.ds(piece * self.rows, self.rows)
            block = self.links.along(-way * number)
            place = self.place(block, rows)
            source = self.origin(rows) if number == 0 else place
            self.last[piece] = self.links.send(source, place, way)


def column_of(row):
    size = row.shape[1]
    down = lax.broadcasted_iota(jnp.int32, (size, size), 0)
    across = lax.broadcasted_iota(jnp.int32, (size, size), 1)
    values = jnp.where(down == across, jnp.broadcast_to(row, (size, size)), 0.0)
    return jnp.sum(values, axis=1, keepdims=True)


def first_kernel(
    line,
    small_ref,
    x_ref,
    grad_ref,
    gain_rows_ref,
    query_w_ref,
    key_w_ref,
    value_w_ref,
    gate_w_ref,
    up_w_ref,
    out_ref,
    xs_ref,
    weight_ref,
    gain_ref,
    norm_ref,
    query_ref,
    kv_ref,
    peak_ref,
    turn_ref,
    atts_ref,
    ffs_ref,
    outs_ref,
    mix_ref,
    x_all,
    grad,
    mix,
    places,
    weights,
    gains,
    norm,
    turns,
    flat,
    query,
    kv,
    peak,
    att,
    send_sems,
    recv_sems,
):
    f32, bf16 = jnp.float32, jnp.bfloat16
    links = Links(send_sems, recv_sems, line)
    far = [1, line - 1] + list(range(2, line - 1))
    links.meet(["x", "y", "c"] + far)
    here = links.slot
    span_len, width = x_ref.shape
    group_len = line * span_len
    rows_each = gate_w_ref.shape[0]
    q_cols = query.shape[1]
    ff_cols = gate_w_ref.shape[1] // line
    heads = q_cols // HD
    local = []

    near = NearGather(links, lambda block, place: weights.at[links.along(-block), place])
    far_ff = NearGather(links, lambda block, place: ffs_ref.at[links.along(-block), place])
    far_out = NearGather(links, lambda block, place: outs_ref.at[links.along(-block), place])
    ring = LineGather(
        links, span_len, lambda rows: x_ref.at[rows], lambda block, rows: x_all.at[block, rows]
    )
    place_ref = small_ref.at[0]

    def columns(weight, block, size):
        return weight.at[:, pl.ds(pl.multiple_of(block * size, HD), size)]

    def near_pieces(block):
        target = weights.at[links.z, here]
        rows = pl.ds(0, rows_each)
        return [
            (columns(query_w_ref, block, q_cols), target.at[rows, pl.ds(0, q_cols)]),
            (columns(key_w_ref, block, HD), target.at[rows, pl.ds(q_cols, HD)]),
            (columns(value_w_ref, block, HD), target.at[rows, pl.ds(q_cols + HD, HD)]),
            (gain_rows_ref, target.at[pl.ds(rows_each, 16)]),
        ]

    def ff_pieces(block):
        target = ffs_ref.at[links.z, here]
        return [
            (columns(gate_w_ref, block, ff_cols), target.at[:, pl.ds(0, ff_cols)]),
            (columns(up_w_ref, block, ff_cols), target.at[:, pl.ds(ff_cols, ff_cols)]),
        ]

    def turn_out(pieces):
        return {k: [links.send(*piece, k) for piece in pieces(links.along(k))] for k in far}

    def arrived(copies):
        for copy in copies:
            copy.wait_recv()

    own = [links.keep(*piece) for piece in near_pieces(links.z)]
    own_ff = [links.keep(*piece) for piece in ff_pieces(links.z)]
    turned = turn_out(near_pieces)
    placed = [links.send(place_ref, places.at[links.z], k) for k in far]
    turned_ff = turn_out(ff_pieces)
    for copy in own:
        copy.wait()
    near.offer(0, weights.at[links.z, here])
    for copy in own_ff:
        copy.wait()
    far_ff.offer(0, ffs_ref.at[links.z, here])
    own = [
        links.keep(x_ref, x_all.at[links.z]),
        links.keep(place_ref, places.at[links.z]),
        links.keep(grad_ref, grad),
    ]
    local.append(links.keep(out_ref, outs_ref.at[links.z, here]))

    def move_out(k):
        moved.wait_recv()
        block = outs_ref.at[links.along(-k), here]
        onward = links.send(block, block, 1) if k < line - 1 else None
        far_out.offer(k, block)
        return onward

    for k in far:
        arrived(turned[k])
        near.offer(k, weights.at[links.along(-k), here])
    ring.step(0)
    for k in [0] + far:
        near.relay(k, "x" if k < line // 2 else "y")
    for k in far:
        arrived(turned_ff[k])
        far_ff.offer(k, ffs_ref.at[links.along(-k), here])
    ring.step(1)
    for k in [0] + far:
        near.close(k)
    far_ff.relay(0, "x")
    ring.step(2)
    moved = links.send(out_ref, outs_ref.at[links.z, here], 1)
    far_out.offer(0, out_ref)
    for copy in own:
        copy.wait()
    for copy in placed:
        copy.wait_recv()

    lane = lax.broadcasted_iota(jnp.int32, (span_len, HD), 1)
    for block in range(line):
        angles = column_of(places[block, 0:1]) * small_ref[2, 0:1]
        rows = slice(block * span_len, (block + 1) * span_len)
        sine = jnp.sin(angles)
        turns[0, rows] = jnp.cos(angles)
        turns[1, rows] = jnp.where(lane < HD // 2, -sine, sine)
    local.append(links.keep(turns, turn_ref))
    token_scale = column_of(small_ref[1, 0:1])
    for low in range(0, span_len, 16):
        rows = slice(low, low + 16)
        upstream = grad[rows].astype(f32) * token_scale[rows]
        mix[rows] = (upstream * small_ref[3, 0:1, 0:1]).astype(bf16)
    local.append(links.keep(mix, mix_ref))
    near.wait(range(line))
    for index in range(line * 4):
        z, q = divmod(index, 4)
        for which in range(2):
            lanes = slice(which * HD, (which + 1) * HD)
            both = [weights[z, 2 * q + c, rows_each : rows_each + 16, lanes].astype(f32) for c in range(2)]
            gains[which, :, index * HD : (index + 1) * HD] = both[0] + both[1]
    local.append(links.keep(weights, weight_ref))
    local.append(links.keep(gains, gain_ref))
    far_ff.relay(far[0], "x")
    ring.step(3)
    local.append(links.keep(x_all, xs_ref))

    def normalise(index, carry):
        block = index // (span_len // 16)
        rows = pl.ds(pl.multiple_of(lax.rem(index, span_len // 16) * 16, 16), 16)
        values = x_all[block, rows].astype(f32)
        inverse = lax.rsqrt(jnp.mean(values * values, axis=-1, keepdims=True) + epsilon)
        target = pl.ds(pl.multiple_of(index * 16, 16), 16)
        norm[target] = (values * inverse * gains[0]).astype(bf16)
        return carry

    lax.fori_loop(0, group_len // 16, normalise, 0)
    local.append(links.keep(norm, norm_ref))

    def project(low, high):
        step = group_len // 2
        for part in range(2):
            rows = slice(part * step, (part + 1) * step)
            total = None
            for z in range(line):
                weight = weights[z, :, :rows_each, low:high].reshape(8 * rows_each, high - low)
                term = jnp.dot(
                    norm[rows, z * 8 * rows_each : (z + 1) * 8 * rows_each],
                    weight,
                    preferred_element_type=f32,
                )
                total = term if total is None else total + term
            flat[rows, low:high] = total

    def turn(values, rows):
        return values * turns[0, rows] + pltpu.roll(values, HD // 2, 1) * turns[1, rows]

    project(q_cols, q_cols + 2 * HD)
    for block in range(line):
        rows = slice(block * span_len, (block + 1) * span_len)
        kv[0, rows, :HD] = turn(flat[rows, q_cols : q_cols + HD], rows).astype(bf16)
        kv[0, rows, HD:] = flat[rows, q_cols + HD : q_cols + 2 * HD].astype(bf16)
    exchange = links.send(kv.at[0], kv.at[1], "x")
    project(0, q_cols)
    for block in range(line):
        rows = slice(block * span_len, (block + 1) * span_len)
        for head in range(heads):
            lanes = slice(head * HD, (head + 1) * HD)
            query[rows, lanes] = turn(flat[rows, lanes], rows).astype(bf16)
    local.append(links.keep(query, query_ref))
    for k in far[1:]:
        far_ff.relay(k, "x" if k < line // 2 else "y")
    exchange.wait_recv()
    moved = move_out(1)
    local.append(links.keep(kv, kv_ref))

    scale = 1.0 / math.sqrt(HD)
    peak[...] = jnp.zeros_like(peak)

    def attend(head, carry):
        lanes = pl.ds(pl.multiple_of(head * HD, HD), HD)
        for block in range(line):
            rows = slice(block * span_len, (block + 1) * span_len)
            reach = (block + 1) * span_len
            part = query[rows, lanes]
            row = lax.broadcasted_iota(jnp.int32, (span_len, reach), 0) + block * span_len
            column = lax.broadcasted_iota(jnp.int32, (span_len, reach), 1)
            allowed = (column <= row, column < (block + links.x) * span_len)
            scores = []
            for half in range(2):
                score = lax.dot_general(
                    part, kv[half, :reach, :HD], (((1,), (1,)), ((), ())), preferred_element_type=f32
                )
                scores.append(jnp.where(allowed[half], score * scale, -1e30))
            top = jnp.maximum(
                jnp.max(scores[0], axis=-1, keepdims=True), jnp.max(scores[1], axis=-1, keepdims=True)
            )
            total, mixed = None, None
            for half in range(2):
                weight = jnp.exp(scores[half] - top)
                count = jnp.sum(weight, axis=-1, keepdims=True)
                term = jnp.dot(weight.astype(bf16), kv[half, :reach, HD:], preferred_element_type=f32)
                total = count if total is None else total + count
                mixed = term if mixed is None else mixed + term
            att[rows, lanes] = (mixed / total).astype(bf16)
            spot = lax.broadcasted_iota(jnp.int32, (span_len, HD), 1) == head
            peak[rows] = jnp.where(spot, top + jnp.log(total), peak[rows])
        return carry

    lax.fori_loop(0, heads, attend, 0)
    local.append(links.keep(peak, peak_ref))

    def place(block, rows):
        return atts_ref.at[rows, pl.ds(pl.multiple_of(block * q_cols, q_cols), q_cols)]

    att_ring = LineGather(links, group_len, lambda rows: att.at[rows], place)
    local.append(links.keep(att, place(links.z, pl.ds(0, group_len))))
    att_ring.step(0)
    for k in [0] + far:
        far_ff.close(k)
    far_out.relay(0, "x")
    moved = move_out(2)
    far_out.relay(1, "x")
    att_ring.step(1)
    for k in range(3, line):
        moved = move_out(k)
    far_out.relay(2, "y")
    att_ring.step(2)
    for k in range(3, line):
        far_out.relay(k, "y")
    for k in range(line):
        far_out.close(k)
    att_ring.step(3)
    far_out.wait(range(line))
    far_ff.wait(range(line))
    links.finish()
    for copy in local:
        copy.wait()


def add_rows_of(target, values, count):
    def add(index, carry):
        rows = pl.ds(pl.multiple_of(index * 16, 16), 16)
        target[rows] = target[rows] + values[rows]
        return carry

    lax.fori_loop(0, count // 16, add, 0)


class NearSum:
    def __init__(self, links, source, own, from_core, from_first, from_second, first, in_place=False):
        self.links, self.source, self.own, self.first = links, source, own, first
        self.in_place = in_place
        self.from_core, self.from_first, self.from_second = from_core, from_first, from_second

    def start(self):
        links = self.links
        if not self.in_place:
            self.local = links.keep(self.source(links.c), self.own)
        self.copy = links.send(self.source(1 - links.c), self.from_core, "c")

    def add(self, target, values):
        add_rows_of(target, values, target.shape[0])

    def core_done(self):
        links = self.links
        self.copy.wait_recv()
        if not self.in_place:
            self.local.wait()
        for x in range(2):
            for y in range(2):
                self.add(self.own.at[x, y], self.from_core.at[x, y])
        if self.first == "x":
            self.copy = links.send(self.own.at[1 - links.x], self.from_first, "x")
        else:
            self.copy = links.send(self.own.at[:, 1 - links.y], self.from_first, "y")

    def first_done(self):
        links = self.links
        self.copy.wait_recv()
        for other in range(2):
            place = (links.x, other) if self.first == "x" else (other, links.y)
            self.add(self.own.at[place], self.from_first.at[other])
        if self.first == "x":
            self.copy = links.send(self.own.at[links.x, 1 - links.y], self.from_second, "y")
        else:
            self.copy = links.send(self.own.at[1 - links.x, links.y], self.from_second, "x")

    def second_done(self):
        self.copy.wait_recv()
        total = self.own.at[self.links.x, self.links.y]
        self.add(total, self.from_second)
        return total


def sum_space(blocks, rows, columns):
    shape = (rows, columns)
    return [
        pltpu.VMEM((blocks, 2, 2) + shape, jnp.bfloat16),
        pltpu.VMEM((blocks, 2, 2) + shape, jnp.bfloat16),
        pltpu.VMEM((blocks, 2) + shape, jnp.bfloat16),
        pltpu.VMEM((blocks,) + shape, jnp.bfloat16),
    ]


class RingSum:
    def __init__(self, links, parts, total, got, pieces=4):
        self.links, self.parts, self.total, self.got = links, parts, total, got
        self.pieces, self.last = pieces, [None] * pieces
        self.rows = parts.shape[1] // pieces

    def step(self, number):
        links = self.links
        for piece in range(self.pieces):
            way = 1 if piece < self.pieces // 2 else -1
            block = links.along(-way * (number + 1))
            where = pl.ds(piece * self.rows, self.rows)
            if number == 0:
                source = self.parts.at[block, where]
            else:
                self.last[piece].wait_recv()
                total = self.got[number - 1, where].astype(jnp.float32) + self.parts[
                    block, where
                ].astype(jnp.float32)
                if number == links.line - 1:
                    self.total[where] = total
                    continue
                self.parts[block, where] = total.astype(self.parts.dtype)
                source = self.parts.at[block, where]
            self.last[piece] = links.send(source, self.got.at[number, where], way)


def link_call(kernel, collective_id, copies, shapes, arguments, spaces=None, scratch=(), vmem=16):
    any_space = pl.BlockSpec(memory_space=pl.ANY)
    near_space = pl.BlockSpec(memory_space=pltpu.VMEM)
    many = isinstance(shapes, tuple)
    if spaces is None:
        spaces = "h" * (len(arguments) + (len(shapes) if many else 1))
    specs = [near_space if space == "v" else any_space for space in spaces]
    return pl.pallas_call(
        kernel,
        out_shape=shapes,
        in_specs=specs[: len(arguments)],
        out_specs=tuple(specs[len(arguments) :]) if many else specs[-1],
        scratch_shapes=list(scratch)
        + [pltpu.SemaphoreType.DMA((copies,)), pltpu.SemaphoreType.DMA((copies,))],
        compiler_params=pltpu.CompilerParams(
            collective_id=collective_id, has_side_effects=True, vmem_limit_bytes=vmem * 2**20
        ),
    )(*arguments)


def forward_call(small, tokens, out_grad, gain_rows, weights, line):
    span_len, width = tokens.shape
    group_len = line * span_len
    rows_each, qkv_cols = weights[0].shape[0], gain_rows.shape[1]
    q_cols = qkv_cols - 2 * HD
    both_cols = 2 * weights[3].shape[1] // line
    f32, bf16 = jnp.float32, jnp.bfloat16
    near = (line, 8, rows_each + 16, qkv_cols)
    outs = (
        ((line, span_len, width), bf16),
        (near, bf16),
        ((2, 16, width), f32),
        ((group_len, width), bf16),
        ((group_len, q_cols), bf16),
        ((2, group_len, 2 * HD), bf16),
        ((group_len, HD), f32),
        ((2, group_len, HD), f32),
        ((group_len, line * q_cols), bf16),
        ((line, 8, rows_each, both_cols), bf16),
        ((line, 8, rows_each, width), bf16),
        ((span_len, width), bf16),
    )
    return link_call(
        functools.partial(first_kernel, line),
        0,
        208,
        tuple(jax.ShapeDtypeStruct(*out) for out in outs),
        (small, tokens, out_grad, gain_rows) + weights,
        "v" + "h" * 21,
        scratch=[
            pltpu.VMEM((line, span_len, width), bf16),
            pltpu.VMEM((span_len, width), bf16),
            pltpu.VMEM((span_len, width), bf16),
            pltpu.VMEM((line,) + small.shape[1:], f32),
            pltpu.VMEM(near, bf16),
            pltpu.VMEM((2, 16, width), f32),
            pltpu.VMEM((group_len, width), bf16),
            pltpu.VMEM((2, group_len, HD), f32),
            pltpu.VMEM((group_len, qkv_cols), f32),
            pltpu.VMEM((group_len, q_cols), bf16),
            pltpu.VMEM((2, group_len, 2 * HD), bf16),
            pltpu.VMEM((group_len, HD), f32),
            pltpu.VMEM((group_len, q_cols), bf16),
        ],
        vmem=63,
    )


def mlp_kernel(
    line,
    cuts,
    small_ref,
    gain_ref,
    mix_ref,
    xs_ref,
    atts_ref,
    out_ref,
    ff_ref,
    down_ref,
    middle_ref,
    total_ref,
    output_ref,
    sum_ref,
    grad_ff_ref,
    ff_half_ref,
    big,
    ff,
    down,
    norm,
    parts,
    mixed,
    gate_up,
    hidden,
    both_grad,
    got,
    mixed_parts,
    mixed_got,
    mixed_total,
    *scratch,
):
    f32, bf16 = jnp.float32, jnp.bfloat16
    space, (send_sems, recv_sems) = scratch[:-2], scratch[-2:]
    links = Links(send_sems, recv_sems, line)
    links.meet(["x", "y", "c", 1, line - 1])
    far = [1, line - 1] + list(range(2, line - 1))
    span_len, width = mix_ref.shape
    group_len = line * span_len
    ff_cols = hidden.shape[1]
    block_rows = width // line
    rows_each = block_rows // 8
    chunk = 2 * HD
    mix_ring = RingGather(
        links, span_len, lambda rows: mix_ref.at[rows], lambda block, rows: mixed.at[block, rows]
    )
    mix_ring.step(0)
    stay = links.keep(mix_ref, mixed.at[links.z])
    early = [
        links.keep(out_ref, big),
        links.keep(atts_ref, norm),
        links.keep(xs_ref, parts),
    ]
    late = [links.keep(ff_ref, ff)]
    down_rows = down_ref.shape[0]

    def down_place(block, place):
        low, high = cuts[block]
        return down.at[pl.ds(pl.multiple_of(place * down_rows + low, 16), high - low)]

    near = NearGather(links, down_place)
    for block, (low, high) in enumerate(cuts):
        rows = down_ref.at[pl.ds(low, high - low)]
        late.append(links.keep(rows, down_place(block, links.slot)))
        near.offer(block, rows)
    ring = RingSum(links, parts, total_ref, got)
    mixed_ring = RingSum(links, mixed_parts, mixed_total, mixed_got)
    items = []
    ff_items = []
    for index, k in enumerate(far[:2]):
        block = links.along(k)
        core, first, second = space[:3]
        ff_items.append(
            NearSum(
                links,
                lambda c, block=block: ff.at[block, :, :, c],
                ff.at[block, :, :, links.c],
                core.at[index],
                first.at[index],
                second.at[index],
                "xy"[index % 2],
                True,
            )
        )
    for index, (low, high) in enumerate(cuts):
        rows = pl.ds(low, high - low)
        core, first, second = space[3 * index + 3 : 3 * index + 6]
        items.append(
            NearSum(
                links,
                lambda c, rows=rows: big.at[:, :, c, rows],
                big.at[:, :, links.c, rows],
                core.at[0],
                first.at[0],
                second.at[0],
                "xy"[index % 2],
                True,
            )
        )
    for copy in early:
        copy.wait()

    half = group_len // 2
    out_rows = width // 8
    for part in range(2):
        low = part * half
        for column in range(4):
            lanes = slice(column * width // 4, (column + 1) * width // 4)
            value = None
            for k in range(8):
                term = jnp.dot(
                    norm[low : low + half, k * out_rows : (k + 1) * out_rows],
                    big[k // 4, k // 2 % 2, k % 2, :, lanes],
                    preferred_element_type=f32,
                )
                value = term if value is None else value + term
            gate_up[:half, lanes] = value * small_ref[3, 0:1, 0:1]

        def normalise(index, carry, low=low):
            block = (low // 16 + index) // (span_len // 16)
            rows = pl.ds(pl.multiple_of(index * 16, 16), 16)
            inside = pl.ds(pl.multiple_of(lax.rem(index, span_len // 16) * 16, 16), 16)
            values = parts[block, inside].astype(f32) + gate_up[rows, :width]
            gate_up[rows, :width] = values
            inverse = lax.rsqrt(jnp.mean(values * values, axis=-1, keepdims=True) + epsilon)
            target = pl.ds(pl.multiple_of(low + index * 16, 16), 16)
            norm[target] = (values * inverse * gain_ref[1]).astype(bf16)
            return carry

        lax.fori_loop(0, half // 16, normalise, 0)

        @pl.when(links.z // (line // 2) == part)
        def _():
            where = pl.multiple_of(lax.rem(links.z, line // 2) * span_len, span_len)
            middle_ref[...] = gate_up[pl.ds(where, span_len), :width]
        if part == 0:
            mix_ring.step(1)

    for block in range(2):
        near.relay(block, "xy"[block])
    for copy in late:
        copy.wait()

    def columns_of(lanes, size):
        return ff[:, :, :, :, :, lanes].reshape(width, size)

    def forward(low, size):
        gates, ups = pl.ds(low, size), pl.ds(low + ff_cols, size)
        gate = jnp.dot(norm[...], columns_of(gates, size), preferred_element_type=f32)
        gate_up[:, gates] = gate
        swish = gate * jax.nn.sigmoid(gate)
        up = jnp.dot(norm[...], columns_of(ups, size), preferred_element_type=f32)
        gate_up[:, ups] = up
        hidden[:, gates] = (swish * up).astype(bf16)

    def backward(low, size):
        gates, ups = pl.ds(low, size), pl.ds(low + ff_cols, size)
        grad = lax.dot_general(
            mixed[...].reshape(group_len, width),
            down[gates],
            (((1,), (1,)), ((), ())),
            preferred_element_type=f32,
        )
        gate, up = gate_up[:, gates], gate_up[:, ups]
        sigmoid = jax.nn.sigmoid(gate)
        both_grad[:, gates] = (grad * up * sigmoid * (1.0 + gate * (1.0 - sigmoid))).astype(bf16)
        both_grad[:, ups] = (grad * (gate * sigmoid)).astype(bf16)

    def over_chunks(work, extent):
        def one(index, carry):
            work(pl.multiple_of(index * chunk, chunk), chunk)
            return carry

        lax.fori_loop(0, extent // chunk, one, 0)
        if extent % chunk:
            work(extent // chunk * chunk, extent % chunk)

    over_chunks(forward, ff_cols)
    mix_ring.step(2)
    for block in range(2):
        near.close(block)
    near.wait(range(2))

    def mixed_part(low, size):
        lanes = pl.ds(low, size)
        value = jnp.dot(hidden[...], down[:, lanes], preferred_element_type=f32).astype(bf16)
        mixed_parts[:, :, lanes] = value.reshape(line, span_len, size)

    over_chunks(mixed_part, width)
    mixed_ring.step(0)
    stay.wait()
    mix_ring.step(3)
    hidden_rows = hidden[...].T

    def down_part(low, size):
        lanes = pl.ds(low, size)
        value = jnp.dot(
            hidden_rows,
            mixed[:, :, lanes].reshape(group_len, size),
            preferred_element_type=f32,
        ).astype(bf16)
        big[:, :, :, : cuts[-1][1], lanes] = value.reshape(2, 2, 2, cuts[-1][1], size)

    over_chunks(down_part, width)
    for item in items:
        item.start()
    over_chunks(backward, ff_cols)
    mixed_ring.step(1)
    for item in items:
        item.core_done()

    def norm_part(index, carry):
        size = 4 * rows_each
        weight = ff[index // 2, lax.rem(index, 2)].reshape(size, 2 * ff_cols)
        value = lax.dot_general(
            both_grad[...], weight, (((1,), (1,)), ((), ())), preferred_element_type=f32
        ).astype(bf16)
        lanes = pl.ds(pl.multiple_of(index * size, size), size)
        parts[:, :, lanes] = value.reshape(line, span_len, size)
        return carry

    lax.fori_loop(0, 2 * line, norm_part, 0)
    ring.step(0)

    def ff_block(block):
        norm_rows = norm[:, pl.ds(pl.multiple_of(block * block_rows, block_rows), block_rows)].T

        def ff_part(low, size):
            lanes = pl.ds(low, size)
            value = jnp.dot(norm_rows, both_grad[:, lanes], preferred_element_type=f32)
            ff[block, :, :, :, :, lanes] = value.astype(bf16).reshape(2, 2, 2, rows_each, size)

        over_chunks(ff_part, 2 * ff_cols)

    for item, k in zip(ff_items, far):
        ff_block(links.along(k))
        item.start()
    for item in items:
        item.first_done()
    ring.step(1)
    for item in ff_items:
        item.core_done()
    mixed_ring.step(2)
    sent = []
    for k in far[2:] + [0]:
        block = links.along(k)
        ff_block(block)
        sent.append(links.keep(ff.at[block], grad_ff_ref.at[block]))
    for item, (low, high) in zip(items, cuts):
        sum_ref[low:high] = item.second_done()[...]
    ring.step(2)
    for item in ff_items:
        item.first_done()
    mixed_ring.step(3)
    for low in range(0, span_len, 16):
        rows = slice(low, low + 16)
        output_ref[rows] = (middle_ref[rows] + small_ref[3, 0:1, 0:1] * mixed_total[rows]).astype(bf16)
    ring.step(3)
    for index, item in enumerate(ff_items):
        sent.append(links.keep(item.second_done(), ff_half_ref.at[index]))
    links.finish()
    for copy in sent:
        copy.wait()


def mlp_call(small, gains, mixed, x_blocks, attended, out_w, ff_w, w_down, line):
    f32, bf16 = jnp.float32, jnp.bfloat16
    span_len, width = mixed.shape
    group_len = line * span_len
    rows, both_cols, rows_each = w_down.shape[0], ff_w.shape[3], ff_w.shape[2]
    ff_rows = 8 * rows
    ff_w = ff_w.reshape(line, 2, 2, 2, rows_each, both_cols)
    half = (rows // 2 + 15) // 16 * 16
    cuts = ((0, half), (half, rows))
    blocks = (line, span_len, width)
    token = jax.ShapeDtypeStruct((span_len, width), f32)
    return link_call(
        functools.partial(mlp_kernel, line, cuts),
        2,
        112,
        (
            token,
            token,
            jax.ShapeDtypeStruct((span_len, width), bf16),
            jax.ShapeDtypeStruct((rows, width), bf16),
            jax.ShapeDtypeStruct(ff_w.shape, bf16),
            jax.ShapeDtypeStruct((2, rows_each, both_cols), bf16),
        ),
        (small, gains, mixed, x_blocks, attended, out_w.reshape(2, 2, 2, width // 8, width), ff_w, w_down),
        "vvhhhhhh" + "vvvvhh",
        [
            pltpu.VMEM((2, 2, 2, width // 8, width), bf16),
            pltpu.VMEM(ff_w.shape, bf16),
            pltpu.VMEM((ff_rows, width), bf16),
            pltpu.VMEM((group_len, width), bf16),
            pltpu.VMEM(blocks, bf16),
            pltpu.VMEM(blocks, bf16),
            pltpu.VMEM((group_len, both_cols), f32),
            pltpu.VMEM((group_len, ff_rows), bf16),
            pltpu.VMEM((group_len, both_cols), bf16),
            pltpu.VMEM((line - 1, span_len, width), bf16),
            pltpu.VMEM(blocks, bf16),
            pltpu.VMEM((line - 1, span_len, width), bf16),
            pltpu.VMEM((span_len, width), f32),
        ]
        + sum_space(2, rows_each, both_cols)[1:]
        + sum((sum_space(1, high - low, width)[1:] for low, high in cuts), []),
        vmem=63,
    )


def backward_kernel(
    line,
    small_ref,
    gain_ref,
    middle_ref,
    norm_grad_ref,
    x_ref,
    grad_ref,
    query_ref,
    kv_ref,
    peak_ref,
    turn_ref,
    out_ref,
    atts_ref,
    weight_ref,
    norm_ref,
    ff_ref,
    ff_half_ref,
    token_ref,
    ffs_ref,
    outs_ref,
    qkvs_ref,
    x_own,
    grad_own,
    middle_grad,
    total,
    big,
    slim,
    norm,
    own_rows,
    own_columns,
    branch,
    own_grad,
    att_grad,
    query_back,
    kv_back,
    kv_out,
    kv_in,
    flat,
    parts,
    query,
    kv,
    peak,
    turns,
    *scratch,
):
    f32, bf16 = jnp.float32, jnp.bfloat16
    send_sems, recv_sems = scratch[-2:]
    got, sums = scratch[0], scratch[1:-2]
    links = Links(send_sems, recv_sems, line)
    far = [1, line - 1] + list(range(2, line - 1))
    order = far + [0]
    links.meet(["x", "y", "c"] + far)
    span_len, width = x_ref.shape
    group_len = line * span_len
    q_cols = query.shape[1]
    heads = q_cols // HD
    rows_z = width // line
    rows_each = rows_z // 8
    scale = 1.0 / math.sqrt(HD)

    def lanes_of(block):
        return pl.ds(pl.multiple_of(block * q_cols, q_cols), q_cols)

    here = pl.ds(pl.multiple_of(links.z * span_len, span_len), span_len)
    first_load = links.keep(grad_ref, grad_own)
    loads = [
        links.keep(out_ref, big),
        links.keep(atts_ref.at[here], own_rows),
        links.keep(atts_ref.at[:, lanes_of(links.z)], own_columns),
        links.keep(x_ref, x_own),
        links.keep(query_ref, query),
        links.keep(kv_ref, kv),
        links.keep(peak_ref, peak),
        links.keep(turn_ref, turns),
        links.keep(norm_ref, norm),
        links.keep(weight_ref.at[:, :, :, :, pl.ds(0, slim.shape[4])], slim),
    ]
    ring = RingSum(links, parts, total, got)

    def items_of(source, space, in_place, order=order):
        items = []
        for index, k in enumerate(order):
            block = links.along(k)
            own = source.at[block, :, :, links.c] if in_place else space[0].at[index]
            core, first, second = space[-3:]
            items.append(
                NearSum(
                    links,
                    lambda c, block=block: source.at[block, :, :, c],
                    own,
                    core.at[index],
                    first.at[index],
                    second.at[index],
                    "xy"[index % 2],
                    in_place,
                )
            )
        return items

    ff_order = order[2:]
    ff_items = items_of(ff_ref, sums[:4], False, ff_order)
    out_items = items_of(big, sums[4:7], True)
    qkv_items = items_of(slim, sums[7:], True)
    local, arrived = [], []
    ff_cols = ff_ref.shape[5] // 2
    ff_pieces = ((0, ff_cols), (ff_cols, ff_cols))
    qkv_pieces = ((0, q_cols), (q_cols, HD), (q_cols + HD, HD))

    def deliver(total, target, k, pieces):
        for low, size in pieces:
            if pieces == out_pieces:
                place = target.at[links.z]
            else:
                lanes = pl.multiple_of(line * low + links.z * size, HD)
                place = target.at[:, pl.ds(lanes, size)]
            part = total.at[:, pl.ds(low, size)]
            if k == 0:
                local.append(links.keep(part, place))
            else:
                arrived.append(links.send(part, place, k))

    out_pieces = ((0, width),)
    deliver(ff_half_ref.at[0], ffs_ref, order[0], ff_pieces)
    def turn(items, target, low, high, pieces, order=order):
        for item, k in list(zip(items, order))[low:high]:
            deliver(item.second_done(), target, k, pieces)

    def core_done(items, low, high):
        for item in items[low:high]:
            item.core_done()

    def first_done(items, low, high):
        for item in items[low:high]:
            item.first_done()

    half = line // 2
    for item in ff_items:
        item.start()

    first_load.wait()
    keep = small_ref[3, 0:1, 0:1]
    token_scale = column_of(small_ref[1, 0:1])

    def norm_back(values, grad, gain):
        inverse = lax.rsqrt(jnp.mean(values * values, axis=-1, keepdims=True) + epsilon)
        scaled = gain * grad
        return inverse * scaled - values * (inverse * inverse * inverse) * jnp.mean(
            scaled * values, axis=-1, keepdims=True
        )

    for low in range(0, span_len, 16):
        rows = slice(low, low + 16)
        upstream = grad_own[rows].astype(f32) * token_scale[rows]
        grad = upstream + norm_back(middle_ref[rows], norm_grad_ref[rows], gain_ref[1])
        middle_grad[rows] = grad
        branch[rows] = (grad * keep).astype(bf16)
    loads[0].wait()
    for z in range(line):
        weight = big[z].reshape(rows_z, width)
        own_grad[:, z * rows_z : (z + 1) * rows_z] = lax.dot_general(
            branch[...], weight, (((1,), (1,)), ((), ())), preferred_element_type=f32
        ).astype(bf16)
    turned = [links.send(own_grad.at[:, lanes_of(links.along(k))], att_grad.at[here], k) for k in far]
    stayed = links.keep(own_grad.at[:, lanes_of(links.z)], att_grad.at[here])
    for copy in loads[1:]:
        copy.wait()
    deliver(ff_half_ref.at[1], ffs_ref, order[1], ff_pieces)
    core_done(ff_items, 0, line)
    for z in range(line):
        for part in range(4):
            columns = slice(part * width // 4, (part + 1) * width // 4)
            grad = lax.dot_general(
                own_rows[:, z * rows_z : (z + 1) * rows_z],
                branch[:, columns],
                (((0,), (0,)), ((), ())),
                preferred_element_type=f32,
            )
            big[z, :, :, :, :, columns] = grad.astype(bf16).reshape(2, 2, 2, rows_each, width // 4)
    for item in out_items:
        item.start()
    kv_back[...] = jnp.zeros_like(kv_back)
    for copy in turned:
        copy.wait_recv()
    stayed.wait()

    def attend_back(side, head, carry):
        lanes = pl.ds(pl.multiple_of(head * HD, HD), HD)
        for block in range(line):
            rows = slice(block * span_len, (block + 1) * span_len)
            reach = (block + 1) * span_len
            part, grad = query[rows, lanes], att_grad[rows, lanes]
            row = lax.broadcasted_iota(jnp.int32, (span_len, reach), 0) + block * span_len
            column = lax.broadcasted_iota(jnp.int32, (span_len, reach), 1)
            allowed = column <= row if side == 0 else column < (block + links.x) * span_len
            spot = lax.broadcasted_iota(jnp.int32, (span_len, HD), 1) == head
            top = jnp.sum(jnp.where(spot, peak[rows], 0.0), axis=-1, keepdims=True)
            delta = jnp.sum(
                grad.astype(f32) * own_columns[rows, lanes].astype(f32), axis=-1, keepdims=True
            )
            keys, values = kv[side, :reach, :HD], kv[side, :reach, HD:]
            score = lax.dot_general(part, keys, (((1,), (1,)), ((), ())), preferred_element_type=f32)
            weight = jnp.where(allowed, jnp.exp(score * scale - top), 0.0)
            weight_grad = lax.dot_general(
                grad, values, (((1,), (1,)), ((), ())), preferred_element_type=f32
            )
            score_grad = (weight * (weight_grad - delta)).astype(bf16)
            back = jnp.dot(score_grad, keys, preferred_element_type=f32) * scale
            kv_back[side, :reach, :HD] += lax.dot_general(
                score_grad, part, (((0,), (0,)), ((), ())), preferred_element_type=f32
            )
            kv_back[side, :reach, HD:] += lax.dot_general(
                weight.astype(bf16), grad, (((0,), (0,)), ((), ())), preferred_element_type=f32
            )
            query_back[rows, lanes] = back if side == 1 else query_back[rows, lanes] + back
        return carry

    lax.fori_loop(0, heads, functools.partial(attend_back, 1), 0)
    kv_out[:, :HD] = (kv_back[1, :, :HD] * scale).astype(bf16)
    kv_out[:, HD:] = kv_back[1, :, HD:].astype(bf16)
    exchange = links.send(kv_out, kv_in, "x")
    lax.fori_loop(0, heads, functools.partial(attend_back, 0), 0)

    def turn_back(values, rows):
        return values * turns[0, rows] - pltpu.roll(values, HD // 2, 1) * turns[1, rows]

    for block in range(line):
        rows = slice(block * span_len, (block + 1) * span_len)
        for head in range(heads):
            lanes = slice(head * HD, (head + 1) * HD)
            flat[rows, lanes] = turn_back(query_back[rows, lanes], rows).astype(bf16)
    first_done(ff_items, 0, line)
    core_done(out_items, 0, half)
    exchange.wait_recv()
    for block in range(line):
        rows = slice(block * span_len, (block + 1) * span_len)
        key_grad = kv_back[0, rows, :HD] * scale + kv_in[rows, :HD].astype(f32)
        flat[rows, q_cols : q_cols + HD] = turn_back(key_grad, rows).astype(bf16)
        value_grad = kv_back[0, rows, HD:] + kv_in[rows, HD:].astype(f32)
        flat[rows, q_cols + HD :] = value_grad.astype(bf16)
    for z in range(line):
        weight = slim[z].reshape(rows_z, flat.shape[1])
        part = lax.dot_general(
            flat[...], weight, (((1,), (1,)), ((), ())), preferred_element_type=f32
        ).astype(bf16)
        for block in range(line):
            parts[block, :, z * rows_z : (z + 1) * rows_z] = part[
                block * span_len : (block + 1) * span_len
            ]
    ring.step(0)
    turn(ff_items, ffs_ref, 0, line, ff_pieces, ff_order)
    for z in range(line):
        grad = lax.dot_general(
            norm[:, z * rows_z : (z + 1) * rows_z],
            flat[...],
            (((0,), (0,)), ((), ())),
            preferred_element_type=f32,
        )
        slim[z] = grad.astype(bf16).reshape(2, 2, 2, rows_each, flat.shape[1])
    for item in qkv_items:
        item.start()
    core_done(out_items, half, line)
    first_done(out_items, 0, half)
    ring.step(1)
    core_done(qkv_items, 0, line)
    turn(out_items, outs_ref, 0, half, out_pieces)
    first_done(out_items, half, line)
    ring.step(2)
    first_done(qkv_items, 0, half)
    turn(out_items, outs_ref, half, line, out_pieces)
    first_done(qkv_items, half, line)
    ring.step(3)
    for low in range(0, span_len, 16):
        rows = slice(low, low + 16)
        grad = middle_grad[rows] + norm_back(x_own[rows].astype(f32), total[rows], gain_ref[0])
        token_ref[rows] = grad.astype(bf16)
    turn(qkv_items, qkvs_ref, 0, line, qkv_pieces)
    for copy in arrived:
        copy.wait_recv()
    links.finish()
    for copy in local:
        copy.wait()


def backward_call(near, tokens, saved, out_w, attended, weights, norm, grad_ff, ff_half, line):
    f32, bf16 = jnp.float32, jnp.bfloat16
    span_len, width = tokens[0].shape
    group_len = line * span_len
    query = saved[0]
    q_cols, rows_each, qkv_cols = query.shape[1], width // line // 8, weights.shape[3]
    weights = weights.reshape(line, 2, 2, 2, -1, qkv_cols)
    wide = (line, 2, 2, 2, rows_each, width)
    slim = (line, 2, 2, 2, rows_each, qkv_cols)
    out_space = sum_space(line, rows_each, width)[1:]
    qkv_space = sum_space(line, rows_each, qkv_cols)[1:]
    token = jax.ShapeDtypeStruct((span_len, width), bf16)
    return link_call(
        functools.partial(backward_kernel, line),
        4,
        160,
        (token,)
        + (
            jax.ShapeDtypeStruct((rows_each, line * grad_ff.shape[5]), bf16),
            jax.ShapeDtypeStruct((line, rows_each, width), bf16),
            jax.ShapeDtypeStruct((rows_each, line * qkv_cols), bf16),
        ),
        near + tokens + saved + (out_w.reshape(wide), attended, weights, norm, grad_ff, ff_half),
        "v" * 4 + "h" * 12 + "vhhh",
        [pltpu.VMEM((span_len, width), bf16)] * 2
        + [pltpu.VMEM((span_len, width), f32)] * 2
        + [
            pltpu.VMEM(wide, bf16),
            pltpu.VMEM(slim, bf16),
            pltpu.VMEM((group_len, width), bf16),
            pltpu.VMEM((span_len, width), bf16),
            pltpu.VMEM((group_len, q_cols), bf16),
            pltpu.VMEM((span_len, width), bf16),
            pltpu.VMEM((span_len, width), bf16),
            pltpu.VMEM((group_len, q_cols), bf16),
            pltpu.VMEM((group_len, q_cols), f32),
            pltpu.VMEM((2, group_len, 2 * HD), f32),
            pltpu.VMEM((group_len, 2 * HD), bf16),
            pltpu.VMEM((group_len, 2 * HD), bf16),
            pltpu.VMEM((group_len, qkv_cols), bf16),
            pltpu.VMEM((line, span_len, width), bf16),
        ]
        + [pltpu.VMEM(value.shape, value.dtype) for value in saved]
        + [pltpu.VMEM((line - 1, span_len, width), bf16)]
        + sum_space(line - 2, rows_each, grad_ff.shape[5])
        + out_space
        + qkv_space,
        vmem=63,
    )


def general_body(
    tokens,
    attn_gain,
    w_query,
    w_key,
    w_value,
    w_out,
    mlp_gain,
    w_gate,
    w_up,
    w_down,
    keep_mask,
    group_ids,
    positions,
    exit_scale,
    out_grad,
):
    seq_count, span_len, model_width = tokens.shape
    kv_heads = KVH
    head_dim = HD
    head_count = HEADS
    group_size = head_count // kv_heads
    row_count = seq_count * span_len
    stripe = group_size * span_len
    wide_count = lax.axis_size("wide")
    wide_place = lax.axis_index("wide")
    full_len = span_len * wide_count
    score_scale = 1.0 / math.sqrt(head_dim)
    gain_one, query_w, key_w, value_w, out_w = (
        lax.all_gather(attn_gain, ("wide", "narrow"), axis=0, tiled=True),
        lax.all_gather(w_query, ("wide", "narrow"), axis=0, tiled=True),
        lax.all_gather(w_key, ("wide", "narrow"), axis=0, tiled=True),
        lax.all_gather(w_value, ("wide", "narrow"), axis=0, tiled=True),
        lax.all_gather(w_out, ("wide", "narrow"), axis=0, tiled=True),
    )
    inputs = tokens.astype(jnp.float32).reshape(row_count, model_width)
    token_pos = positions.reshape(row_count)
    keep_rows = jnp.repeat(keep_mask.astype(jnp.float32), span_len)[:, None]
    inverse_one = lax.rsqrt(jnp.mean(inputs * inputs, axis=-1, keepdims=True) + epsilon)
    first_norm = (inputs * inverse_one * gain_one.astype(jnp.float32)).astype(jnp.bfloat16)
    query_pre = jnp.dot(first_norm, query_w, preferred_element_type=jnp.float32).reshape(
        row_count, head_count, head_dim
    )
    key_pre = jnp.dot(first_norm, key_w, preferred_element_type=jnp.float32).reshape(
        row_count, kv_heads, head_dim
    )
    query_rows = rotate(query_pre, token_pos, 1.0).astype(jnp.bfloat16)
    key_heads = (
        rotate(key_pre, token_pos, 1.0)
        .astype(jnp.bfloat16)
        .reshape(seq_count, span_len, kv_heads * head_dim)
    )
    value_heads = (
        jnp.dot(first_norm, value_w, preferred_element_type=jnp.float32)
        .astype(jnp.bfloat16)
        .reshape(seq_count, span_len, kv_heads * head_dim)
    )
    queries = (
        query_rows.reshape(seq_count, span_len, kv_heads, group_size, head_dim)
        .transpose(0, 2, 3, 1, 4)
        .reshape(seq_count, kv_heads, stripe, head_dim)
    )
    query_index = wide_place * span_len + jnp.arange(stripe, dtype=jnp.int32) % span_len
    last_query = wide_place * span_len + span_len - 1

    def block_scores(key_block, key_first):
        scores = (
            jnp.einsum("skrd,sjkd->skrj", queries, key_block, preferred_element_type=jnp.float32)
            * score_scale
        )
        key_index = key_first + jnp.arange(key_block.shape[1], dtype=jnp.int32)
        allowed = key_index[None, :] <= query_index[:, None]
        return (scores, allowed)

    start_forward = (
        jnp.full((seq_count, kv_heads, stripe), -1e30, jnp.float32),
        jnp.zeros((seq_count, kv_heads, stripe), jnp.float32),
        jnp.zeros((seq_count, kv_heads, stripe, head_dim), jnp.float32),
    )
    running = start_forward
    pieces = (
        lax.all_gather(key_heads, "wide", axis=1, tiled=True),
        lax.all_gather(value_heads, "wide", axis=1, tiled=True),
    )
    key_blocks = split_blocks(pieces[0], seq_count, kv_heads, head_dim)
    value_blocks = split_blocks(pieces[1], seq_count, kv_heads, head_dim)
    block_len = key_blocks.shape[2]

    def advance(carried, block_item):
        key_block, value_block, block_index = block_item
        key_first = block_index * block_len

        def compute_block(current):
            run_max, run_sum, run_acc = current
            scores, allowed = block_scores(key_block, key_first)
            scores = jnp.where(allowed, scores, -1e30)
            new_max = jnp.maximum(run_max, jnp.max(scores, axis=-1))
            factor = jnp.exp(run_max - new_max)
            weights = jnp.where(allowed, jnp.exp(scores - new_max[..., None]), 0.0)
            new_sum = run_sum * factor + jnp.sum(weights, axis=-1)
            new_acc = run_acc * factor[..., None] + jnp.einsum(
                "skrj,sjkd->skrd",
                weights.astype(jnp.bfloat16),
                value_block,
                preferred_element_type=jnp.float32,
            )
            return (new_max, new_sum, new_acc)

        return (lax.cond(key_first <= last_query, compute_block, unchanged, carried), None)

    running, _ = lax.scan(
        advance,
        running,
        (key_blocks, value_blocks, jnp.arange(key_blocks.shape[0], dtype=jnp.int32)),
    )
    run_max, run_sum, run_acc = running
    attended = run_acc / run_sum[..., None]
    log_total = run_max + jnp.log(run_sum)
    attended_rows = (
        attended.reshape(seq_count, kv_heads, group_size, span_len, head_dim)
        .transpose(0, 3, 1, 2, 4)
        .reshape(row_count, head_count * head_dim)
        .astype(jnp.bfloat16)
    )
    middle = inputs + keep_rows * jnp.dot(attended_rows, out_w, preferred_element_type=jnp.float32)
    gain_two, gate_w, up_w, down_w = (
        lax.all_gather(mlp_gain, ("wide", "narrow"), axis=0, tiled=True),
        lax.all_gather(w_gate, ("wide", "narrow"), axis=0, tiled=True),
        lax.all_gather(w_up, ("wide", "narrow"), axis=0, tiled=True),
        lax.all_gather(w_down, ("wide", "narrow"), axis=0, tiled=True),
    )
    inverse_two = lax.rsqrt(jnp.mean(middle * middle, axis=-1, keepdims=True) + epsilon)
    second_norm = (middle * inverse_two * gain_two.astype(jnp.float32)).astype(jnp.bfloat16)
    gate_value = jnp.dot(second_norm, gate_w, preferred_element_type=jnp.float32)
    up_value = jnp.dot(second_norm, up_w, preferred_element_type=jnp.float32)
    gate_sigmoid = jax.nn.sigmoid(gate_value)
    swish_value = gate_value * gate_sigmoid
    hidden = (swish_value * up_value).astype(jnp.bfloat16)
    output = (
        middle + keep_rows * jnp.dot(hidden, down_w, preferred_element_type=jnp.float32)
    ).astype(jnp.bfloat16)
    group_match = (
        group_ids.reshape(row_count)[:, None]
        == jnp.arange(exit_scale.shape[0], dtype=jnp.int32)[None, :]
    )
    token_scale = jnp.sum(jnp.where(group_match, exit_scale[None, :], 0.0), axis=1, keepdims=True)
    upstream = out_grad.astype(jnp.float32).reshape(row_count, model_width) * token_scale
    gain_two, gate_w, up_w, down_w = (
        lax.all_gather(mlp_gain, ("wide", "narrow"), axis=0, tiled=True),
        lax.all_gather(w_gate, ("wide", "narrow"), axis=0, tiled=True),
        lax.all_gather(w_up, ("wide", "narrow"), axis=0, tiled=True),
        lax.all_gather(w_down, ("wide", "narrow"), axis=0, tiled=True),
    )
    mixed_grad = (keep_rows * upstream).astype(jnp.bfloat16)
    grad_down = over_rows(hidden, mixed_grad)
    hidden_grad = against(mixed_grad, down_w)
    gate_grad = (
        hidden_grad * up_value * gate_sigmoid * (1.0 + gate_value * (1.0 - gate_sigmoid))
    ).astype(jnp.bfloat16)
    up_grad = (hidden_grad * swish_value).astype(jnp.bfloat16)
    grad_gate = over_rows(second_norm, gate_grad)
    grad_up = over_rows(second_norm, up_grad)
    norm_grad = against(gate_grad, gate_w) + against(up_grad, up_w)
    grad_gain_two = jnp.sum(norm_grad * middle * inverse_two, axis=0)
    scaled_two = gain_two.astype(jnp.float32) * norm_grad
    middle_grad = (
        upstream
        + inverse_two * scaled_two
        - middle
        * (inverse_two * inverse_two * inverse_two)
        * jnp.mean(scaled_two * middle, axis=-1, keepdims=True)
    )
    gain_two_share, gate_share, up_share, down_share = (
        lax.psum_scatter(grad_gain_two, ("wide", "narrow"), scatter_dimension=0, tiled=True),
        lax.psum_scatter(grad_gate, ("wide", "narrow"), scatter_dimension=0, tiled=True),
        lax.psum_scatter(grad_up, ("wide", "narrow"), scatter_dimension=0, tiled=True),
        lax.psum_scatter(grad_down, ("wide", "narrow"), scatter_dimension=0, tiled=True),
    )
    gain_one, query_w, key_w, value_w, out_w = (
        lax.all_gather(attn_gain, ("wide", "narrow"), axis=0, tiled=True),
        lax.all_gather(w_query, ("wide", "narrow"), axis=0, tiled=True),
        lax.all_gather(w_key, ("wide", "narrow"), axis=0, tiled=True),
        lax.all_gather(w_value, ("wide", "narrow"), axis=0, tiled=True),
        lax.all_gather(w_out, ("wide", "narrow"), axis=0, tiled=True),
    )
    branch_grad = (keep_rows * middle_grad).astype(jnp.bfloat16)
    grad_out = over_rows(attended_rows, branch_grad)
    attended_grad = against(branch_grad, out_w).astype(jnp.bfloat16)
    grouped_grad = (
        attended_grad.reshape(seq_count, span_len, kv_heads, group_size, head_dim)
        .transpose(0, 2, 3, 1, 4)
        .reshape(seq_count, kv_heads, stripe, head_dim)
    )
    row_delta = jnp.sum(grouped_grad.astype(jnp.float32) * attended, axis=-1)
    start_backward = (
        jnp.zeros((seq_count, kv_heads, stripe, head_dim), jnp.float32),
        jnp.zeros((seq_count, full_len, kv_heads * head_dim), jnp.float32),
        jnp.zeros((seq_count, full_len, kv_heads * head_dim), jnp.float32),
    )
    running = start_backward
    pieces = (
        lax.all_gather(key_heads, "wide", axis=1, tiled=True),
        lax.all_gather(value_heads, "wide", axis=1, tiled=True),
    )
    key_blocks = split_blocks(pieces[0], seq_count, kv_heads, head_dim)
    value_blocks = split_blocks(pieces[1], seq_count, kv_heads, head_dim)
    fold_block_len = key_blocks.shape[2]

    def advance(carried, block_item):
        key_block, value_block, block_index = block_item
        key_first = block_index * fold_block_len

        def compute_block(current):
            query_acc, key_acc, value_acc = current
            scores, allowed = block_scores(key_block, key_first)
            probabilities = jnp.where(allowed, jnp.exp(scores - log_total[..., None]), 0.0)
            value_part = jnp.einsum(
                "skrj,skrd->sjkd",
                probabilities.astype(jnp.bfloat16),
                grouped_grad,
                preferred_element_type=jnp.float32,
            )
            prob_grad = jnp.einsum(
                "skrd,sjkd->skrj", grouped_grad, value_block, preferred_element_type=jnp.float32
            )
            score_grad = (probabilities * (prob_grad - row_delta[..., None])).astype(jnp.bfloat16)
            query_acc = (
                query_acc
                + jnp.einsum(
                    "skrj,sjkd->skrd", score_grad, key_block, preferred_element_type=jnp.float32
                )
                * score_scale
            )
            key_part = (
                jnp.einsum(
                    "skrj,skrd->sjkd", score_grad, queries, preferred_element_type=jnp.float32
                )
                * score_scale
            )
            key_acc = add_rows(
                key_acc, key_part.reshape(seq_count, fold_block_len, kv_heads * head_dim), key_first
            )
            value_acc = add_rows(
                value_acc,
                value_part.reshape(seq_count, fold_block_len, kv_heads * head_dim),
                key_first,
            )
            return (query_acc, key_acc, value_acc)

        return (lax.cond(key_first <= last_query, compute_block, unchanged, carried), None)

    running, _ = lax.scan(
        advance,
        running,
        (key_blocks, value_blocks, jnp.arange(key_blocks.shape[0], dtype=jnp.int32)),
    )
    query_acc, key_acc, value_acc = running
    key_sum, value_sum = (
        lax.psum_scatter(
            key_acc.astype(jnp.bfloat16), "wide", scatter_dimension=1, tiled=True
        ).astype(jnp.float32),
        lax.psum_scatter(
            value_acc.astype(jnp.bfloat16), "wide", scatter_dimension=1, tiled=True
        ).astype(jnp.float32),
    )
    query_back = (
        query_acc.reshape(seq_count, kv_heads, group_size, span_len, head_dim)
        .transpose(0, 3, 1, 2, 4)
        .reshape(row_count, head_count, head_dim)
    )
    query_grad = (
        rotate(query_back, token_pos, -1.0)
        .reshape(row_count, head_count * head_dim)
        .astype(jnp.bfloat16)
    )
    key_grad = (
        rotate(key_sum.reshape(row_count, kv_heads, head_dim), token_pos, -1.0)
        .reshape(row_count, kv_heads * head_dim)
        .astype(jnp.bfloat16)
    )
    value_grad = value_sum.reshape(row_count, kv_heads * head_dim).astype(jnp.bfloat16)
    grad_query = over_rows(first_norm, query_grad)
    grad_key = over_rows(first_norm, key_grad)
    grad_value = over_rows(first_norm, value_grad)
    input_norm_grad = (
        against(query_grad, query_w) + against(key_grad, key_w) + against(value_grad, value_w)
    )
    grad_gain_one = jnp.sum(input_norm_grad * inputs * inverse_one, axis=0)
    scaled_one = gain_one.astype(jnp.float32) * input_norm_grad
    input_grad = (
        middle_grad
        + inverse_one * scaled_one
        - inputs
        * (inverse_one * inverse_one * inverse_one)
        * jnp.mean(scaled_one * inputs, axis=-1, keepdims=True)
    )
    gain_one_share, query_share, key_share, value_share, out_share = (
        lax.psum_scatter(grad_gain_one, ("wide", "narrow"), scatter_dimension=0, tiled=True),
        lax.psum_scatter(grad_query, ("wide", "narrow"), scatter_dimension=0, tiled=True),
        lax.psum_scatter(grad_key, ("wide", "narrow"), scatter_dimension=0, tiled=True),
        lax.psum_scatter(grad_value, ("wide", "narrow"), scatter_dimension=0, tiled=True),
        lax.psum_scatter(grad_out, ("wide", "narrow"), scatter_dimension=0, tiled=True),
    )
    return (
        output.reshape(seq_count, span_len, model_width),
        input_grad.astype(jnp.bfloat16).reshape(seq_count, span_len, model_width),
        gain_one_share,
        query_share,
        key_share,
        value_share,
        out_share,
        gain_two_share,
        gate_share,
        up_share,
        down_share,
    )


def line_body(
    tokens,
    attn_gain,
    w_query,
    w_key,
    w_value,
    w_out,
    mlp_gain,
    w_gate,
    w_up,
    w_down,
    keep_mask,
    group_ids,
    positions,
    exit_scale,
    out_grad,
):
    f32 = jnp.float32
    bf16 = jnp.bfloat16
    _, span_len, model_width = tokens.shape
    line = lax.axis_size("z")
    rows_each = w_query.shape[0]
    q_cols = HEADS // line * HD

    group_match = group_ids[0][:, None] == jnp.arange(exit_scale.shape[0], dtype=jnp.int32)[None, :]
    token_scale = jnp.sum(jnp.where(group_match, exit_scale[None, :], 0.0), axis=1)
    freqs = 10000.0 ** (-2.0 * jnp.arange(HD // 2, dtype=f32) / HD)
    small = jnp.stack(
        [
            positions[0].astype(f32),
            token_scale,
            jnp.concatenate([freqs, freqs]),
            jnp.broadcast_to(keep_mask.astype(f32), (span_len,)),
        ]
    )
    small = jnp.broadcast_to(small[:, None], (4, 8, span_len))

    core = lax.axis_index("c")
    gain_row = jnp.zeros((q_cols + 2 * HD,), bf16)
    gain_row = lax.dynamic_update_slice_in_dim(gain_row, attn_gain, core * rows_each, 0)
    gain_row = lax.dynamic_update_slice_in_dim(gain_row, mlp_gain, HD + core * rows_each, 0)
    gain_rows = jnp.broadcast_to(gain_row, (16, gain_row.shape[0]))
    (
        x_blocks,
        near_w,
        gain_all,
        first_norm,
        queries,
        both_kv,
        log_total,
        turns,
        attended_rows,
        ff_w,
        out_w,
        own_mixed,
    ) = forward_call(
        small,
        tokens[0],
        out_grad[0],
        gain_rows,
        (w_query, w_key, w_value, w_gate, w_up, w_out),
        line,
    )
    middle, norm_grad, output, grad_down, grad_ff, ff_half = mlp_call(
        small,
        gain_all,
        own_mixed,
        x_blocks,
        attended_rows,
        out_w,
        ff_w,
        w_down,
        line,
    )
    grad_down = grad_down.astype(f32)
    token_grad, ff_back, out_back, qkv_back = backward_call(
        (small, gain_all, middle, norm_grad),
        (tokens[0], out_grad[0]),
        (queries, both_kv, log_total, turns),
        out_w,
        attended_rows,
        near_w,
        first_norm,
        grad_ff,
        ff_half,
        line,
    )
    ff_back = ff_back.astype(f32)
    qkv_back = qkv_back.astype(f32)
    grad_out = jnp.sum(out_back.astype(f32), axis=0)
    heads_end, keys_end = w_query.shape[1], w_query.shape[1] + w_key.shape[1]
    grad_query = qkv_back[:, :heads_end]
    grad_key = qkv_back[:, heads_end:keys_end]
    grad_value = qkv_back[:, keys_end:]
    grad_gate = ff_back[:, : w_gate.shape[1]]
    grad_up = ff_back[:, w_gate.shape[1] :]

    def gain_grad(pairs, gain):
        total = sum(jnp.sum(weight.astype(f32) * grad, axis=1) for weight, grad in pairs)
        return total / gain.astype(f32)

    return (
        output[None],
        token_grad[None],
        gain_grad([(w_query, grad_query), (w_key, grad_key), (w_value, grad_value)], attn_gain),
        grad_query,
        grad_key,
        grad_value,
        grad_out,
        gain_grad([(w_gate, grad_gate), (w_up, grad_up)], mlp_gain),
        grad_gate,
        grad_up,
        grad_down,
    )


def solution(mesh):
    wide, narrow = mesh.shape["wide"], mesh.shape["narrow"]
    if wide == 2 * KVH and narrow == 4:
        mesh = Mesh(mesh.devices.reshape(wide // 2, 2, 2, 2), ("z", "x", "y", "c"))
        body, wide, narrow = line_body, ("z", "x"), ("y", "c")
    else:
        body, wide, narrow = general_body, ("wide",), ("narrow",)
    token_spec = P(narrow, wide, None)
    id_spec = P(narrow, wide)
    gain_spec = P(wide + narrow)
    weight_spec = P(wide + narrow, None)
    return jax.shard_map(
        body,
        mesh=mesh,
        in_specs=(
            token_spec,
            gain_spec,
            weight_spec,
            weight_spec,
            weight_spec,
            weight_spec,
            gain_spec,
            weight_spec,
            weight_spec,
            weight_spec,
            P(narrow),
            id_spec,
            id_spec,
            P(),
            token_spec,
        ),
        out_specs=(
            token_spec,
            token_spec,
            gain_spec,
            weight_spec,
            weight_spec,
            weight_spec,
            weight_spec,
            gain_spec,
            weight_spec,
            weight_spec,
            weight_spec,
        ),
        check_vma=False,
    )
```

```python
import functools
import math

import jax
import jax.numpy as jnp
from jax import lax
from jax.experimental import pallas as pl
from jax.experimental.pallas import tpu as pltpu
from jax.sharding import Mesh
from jax.sharding import PartitionSpec as P

HEADS = 16
KVH = 4
HD = 128


epsilon = 1e-05


def rotate(vectors, token_pos, direction):
    half_size = vectors.shape[-1] // 2
    freqs = 10000.0 ** (-2.0 * jnp.arange(half_size, dtype=jnp.float32) / vectors.shape[-1])
    angles = token_pos.astype(jnp.float32)[:, None] * freqs[None, :]
    cosine = jnp.cos(angles)[:, None, :]
    sine = direction * jnp.sin(angles)[:, None, :]
    first_half = vectors[..., :half_size]
    second_half = vectors[..., half_size:]
    return jnp.concatenate(
        [first_half * cosine - second_half * sine, second_half * cosine + first_half * sine],
        axis=-1,
    )


def split_blocks(piece_arr, seq_count, kv_heads, head_dim):
    piece_len = piece_arr.shape[1]
    block_len = math.gcd(piece_len, 512)
    shaped = piece_arr.reshape(seq_count, piece_len // block_len, block_len, kv_heads, head_dim)
    return shaped.transpose(1, 0, 2, 3, 4)


def add_rows(whole_arr, update, first_row):
    current = lax.dynamic_slice_in_dim(whole_arr, first_row, update.shape[1], 1)
    return lax.dynamic_update_slice_in_dim(whole_arr, current + update, first_row, 1)


def over_rows(left, right):
    return lax.dot_general(
        left, right, (((0,), (0,)), ((), ())), preferred_element_type=jnp.float32
    )


def against(left, right):
    return lax.dot_general(
        left, right, (((1,), (1,)), ((), ())), preferred_element_type=jnp.float32
    )


def unchanged(carried):
    return carried


MESH = pl.DeviceIdType.MESH
AXES = ("z", "x", "y", "c")


def only(when, act):
    if when is None:
        act()
    else:
        pl.when(when)(act)


class Links:
    def __init__(self, send_sems, recv_sems, line):
        self.send_sems, self.recv_sems, self.line = send_sems, recv_sems, line
        self.z, self.x, self.y, self.c = (lax.axis_index(name) for name in AXES)
        self.slot = self.x * 4 + self.y * 2 + self.c
        self.used = 0
        self.sent = []

    def device(self, to):
        if to == "x":
            return (self.z, 1 - self.x, self.y, self.c)
        if to == "y":
            return (self.z, self.x, 1 - self.y, self.c)
        if to == "c":
            return (self.z, self.x, self.y, 1 - self.c)
        return (self.along(to), self.x, self.y, self.c)

    def along(self, step):
        return lax.rem(self.z + step + self.line, self.line)

    def other(self, to):
        slot = self.slot
        for name in to:
            bit = {"x": 4, "y": 2, "c": 1}[name]
            here = {"x": self.x, "y": self.y, "c": self.c}[name]
            slot = slot + bit * (1 - 2 * here)
        return slot

    def meet(self, targets):
        barrier = pltpu.get_barrier_semaphore()
        for to in targets:
            pl.semaphore_signal(barrier, inc=1, device_id=self.device(to), device_id_type=MESH)
        pl.semaphore_wait(barrier, len(targets))

    def send(self, source, target, to, when=None):
        copy = pltpu.make_async_remote_copy(
            src_ref=source,
            dst_ref=target,
            send_sem=self.send_sems.at[self.used],
            recv_sem=self.recv_sems.at[self.used],
            device_id=self.device(to),
            device_id_type=MESH,
        )
        only(when, copy.start)
        self.used += 1
        self.sent.append((copy, when))
        return copy

    def keep(self, source, target):
        copy = pltpu.make_async_copy(source, target, self.send_sems.at[self.used])
        copy.start()
        self.used += 1
        return copy

    def finish(self):
        for copy, when in self.sent:
            only(when, copy.wait_send)


class NearGather:
    def __init__(self, links, slot):
        self.links, self.slot = links, slot
        self.got = {}

    def offer(self, block, source):
        target = self.slot(block, self.links.slot)
        for to in ("x", "y", "c"):
            self.got[block, to] = self.links.send(source, target, to)

    def relay(self, block, first):
        links = self.links
        for to, then in (("x", "y"), ("y", "x")):
            self.got[block, to].wait_recv()
            place = self.slot(block, links.other(to))
            self.got[block, to + "c"] = links.send(place, place, "c")
            if to == first:
                self.got[block, "xy"] = links.send(place, place, then)

    def close(self, block):
        self.got[block, "xy"].wait_recv()
        place = self.slot(block, self.links.other("xy"))
        self.got[block, "xyc"] = self.links.send(place, place, "c")

    def wait(self, blocks):
        for block in blocks:
            for to in ("c", "xc", "yc", "xyc"):
                self.got[block, to].wait_recv()


class LineGather:
    def __init__(self, links, rows, origin, place, pieces=2):
        self.links, self.origin, self.place = links, origin, place
        self.pieces, self.rows = pieces, rows // pieces
        self.last = {}

    def inside(self, block):
        return jnp.logical_and(block >= 0, block < self.links.line)

    def step(self, number):
        z = self.links.z
        for piece in range(self.pieces):
            for way in (1, -1):
                held = self.inside(z - way * number)
                if number > 0:
                    only(held, self.last[piece, way].wait_recv)
                if number == self.links.line - 1:
                    continue
                rows = pl.ds(piece * self.rows, self.rows)
                place = self.place(self.links.along(-way * number), rows)
                source = self.origin(rows) if number == 0 else place
                when = jnp.logical_and(held, self.inside(z + way))
                self.last[piece, way] = self.links.send(source, place, way, when)


class RingGather:
    def __init__(self, links, rows, origin, place, pieces=4):
        self.links, self.origin, self.place = links, origin, place
        self.pieces, self.rows = pieces, rows // pieces
        self.last = [None] * pieces

    def step(self, number):
        if number > 0:
            for copy in self.last:
                copy.wait_recv()
        if number == self.links.line - 1:
            return
        for piece in range(self.pieces):
            way = 1 if piece < self.pieces // 2 else -1
            rows = pl.ds(piece * self.rows, self.rows)
            block = self.links.along(-way * number)
            place = self.place(block, rows)
            source = self.origin(rows) if number == 0 else place
            self.last[piece] = self.links.send(source, place, way)


def column_of(row):
    size = row.shape[1]
    down = lax.broadcasted_iota(jnp.int32, (size, size), 0)
    across = lax.broadcasted_iota(jnp.int32, (size, size), 1)
    values = jnp.where(down == across, jnp.broadcast_to(row, (size, size)), 0.0)
    return jnp.sum(values, axis=1, keepdims=True)


def first_kernel(
    line,
    small_ref,
    x_ref,
    grad_ref,
    gain_rows_ref,
    query_w_ref,
    key_w_ref,
    value_w_ref,
    gate_w_ref,
    up_w_ref,
    out_ref,
    xs_ref,
    weight_ref,
    gain_ref,
    norm_ref,
    query_ref,
    kv_ref,
    peak_ref,
    turn_ref,
    atts_ref,
    ffs_ref,
    outs_ref,
    mix_ref,
    x_all,
    grad,
    mix,
    places,
    weights,
    gains,
    norm,
    turns,
    flat,
    query,
    kv,
    peak,
    att,
    send_sems,
    recv_sems,
):
    f32, bf16 = jnp.float32, jnp.bfloat16
    links = Links(send_sems, recv_sems, line)
    far = [1, line - 1] + list(range(2, line - 1))
    links.meet(["x", "y", "c"] + far)
    here = links.slot
    span_len, width = x_ref.shape
    group_len = line * span_len
    rows_each = gate_w_ref.shape[0]
    q_cols = query.shape[1]
    ff_cols = gate_w_ref.shape[1] // line
    heads = q_cols // HD
    local = []

    near = NearGather(links, lambda block, place: weights.at[links.along(-block), place])
    far_ff = NearGather(links, lambda block, place: ffs_ref.at[links.along(-block), place])
    out_half = out_ref.shape[0] // 2

    def out_part(block, place):
        k, part = block
        rows = pl.ds(part * out_half, out_half)
        return outs_ref.at[links.along(k if part else -k), place, rows]

    far_out = NearGather(links, out_part)
    ring = LineGather(
        links, span_len, lambda rows: x_ref.at[rows], lambda block, rows: x_all.at[block, rows]
    )
    place_ref = small_ref.at[0]

    def columns(weight, block, size):
        return weight.at[:, pl.ds(pl.multiple_of(block * size, HD), size)]

    def near_pieces(block):
        target = weights.at[links.z, here]
        rows = pl.ds(0, rows_each)
        return [
            (columns(query_w_ref, block, q_cols), target.at[rows, pl.ds(0, q_cols)]),
            (columns(key_w_ref, block, HD), target.at[rows, pl.ds(q_cols, HD)]),
            (columns(value_w_ref, block, HD), target.at[rows, pl.ds(q_cols + HD, HD)]),
            (gain_rows_ref, target.at[pl.ds(rows_each, 16)]),
        ]

    def ff_pieces(block):
        target = ffs_ref.at[links.z, here]
        return [
            (columns(gate_w_ref, block, ff_cols), target.at[:, pl.ds(0, ff_cols)]),
            (columns(up_w_ref, block, ff_cols), target.at[:, pl.ds(ff_cols, ff_cols)]),
        ]

    def turn_out(pieces):
        return {k: [links.send(*piece, k) for piece in pieces(links.along(k))] for k in far}

    def arrived(copies):
        for copy in copies:
            copy.wait_recv()

    own = [links.keep(*piece) for piece in near_pieces(links.z)]
    own_ff = [links.keep(*piece) for piece in ff_pieces(links.z)]
    turned = turn_out(near_pieces)
    placed = [links.send(place_ref, places.at[links.z], k) for k in far]
    turned_ff = turn_out(ff_pieces)
    for copy in own:
        copy.wait()
    near.offer(0, weights.at[links.z, here])
    for copy in own_ff:
        copy.wait()
    far_ff.offer(0, ffs_ref.at[links.z, here])
    own = [
        links.keep(x_ref, x_all.at[links.z]),
        links.keep(place_ref, places.at[links.z]),
        links.keep(grad_ref, grad),
    ]
    local.append(links.keep(out_ref, outs_ref.at[links.z, here]))

    def move_out(k):
        for part in range(2):
            if k == 0:
                block = out_ref.at[pl.ds(part * out_half, out_half)]
            else:
                moved[part].wait_recv()
                block = out_part((k, part), here)
            if k < line - 1:
                moved[part] = links.send(block, out_part((0, part), here) if k == 0 else block, 1 - 2 * part)
            far_out.offer((k, part), block)

    def relay_out(k):
        for part in range(2):
            far_out.relay((k, part), "xy"[part])

    def close_out(k):
        for part in range(2):
            far_out.close((k, part))

    moved = [None, None]
    for k in far:
        arrived(turned[k])
        near.offer(k, weights.at[links.along(-k), here])
    ring.step(0)
    for k in [0] + far:
        near.relay(k, "x" if k < line // 2 else "y")
    for k in far:
        arrived(turned_ff[k])
        far_ff.offer(k, ffs_ref.at[links.along(-k), here])
    ring.step(1)
    for k in [0] + far:
        near.close(k)
    far_ff.relay(0, "x")
    ring.step(2)
    move_out(0)
    for copy in own:
        copy.wait()
    for copy in placed:
        copy.wait_recv()

    lane = lax.broadcasted_iota(jnp.int32, (span_len, HD), 1)
    for block in range(line):
        angles = column_of(places[block, 0:1]) * small_ref[2, 0:1]
        rows = slice(block * span_len, (block + 1) * span_len)
        sine = jnp.sin(angles)
        turns[0, rows] = jnp.cos(angles)
        turns[1, rows] = jnp.where(lane < HD // 2, -sine, sine)
    local.append(links.keep(turns, turn_ref))
    token_scale = column_of(small_ref[1, 0:1])
    for low in range(0, span_len, 16):
        rows = slice(low, low + 16)
        upstream = grad[rows].astype(f32) * token_scale[rows]
        mix[rows] = (upstream * small_ref[3, 0:1, 0:1]).astype(bf16)
    local.append(links.keep(mix, mix_ref))
    near.wait(range(line))
    for index in range(line * 4):
        z, q = divmod(index, 4)
        for which in range(2):
            lanes = slice(which * HD, (which + 1) * HD)
            both = [weights[z, 2 * q + c, rows_each : rows_each + 16, lanes].astype(f32) for c in range(2)]
            gains[which, :, index * HD : (index + 1) * HD] = both[0] + both[1]
    local.append(links.keep(weights, weight_ref))
    local.append(links.keep(gains, gain_ref))
    far_ff.relay(far[0], "x")
    ring.step(3)
    local.append(links.keep(x_all, xs_ref))
    move_out(1)

    def normalise(index, carry):
        block = index // (span_len // 16)
        rows = pl.ds(pl.multiple_of(lax.rem(index, span_len // 16) * 16, 16), 16)
        values = x_all[block, rows].astype(f32)
        inverse = lax.rsqrt(jnp.mean(values * values, axis=-1, keepdims=True) + epsilon)
        target = pl.ds(pl.multiple_of(index * 16, 16), 16)
        norm[target] = (values * inverse * gains[0]).astype(bf16)
        return carry

    lax.fori_loop(0, group_len // 16, normalise, 0)
    local.append(links.keep(norm, norm_ref))

    def project(low, high):
        step = group_len // 2
        for part in range(2):
            rows = slice(part * step, (part + 1) * step)
            total = None
            for z in range(line):
                weight = weights[z, :, :rows_each, low:high].reshape(8 * rows_each, high - low)
                term = jnp.dot(
                    norm[rows, z * 8 * rows_each : (z + 1) * 8 * rows_each],
                    weight,
                    preferred_element_type=f32,
                )
                total = term if total is None else total + term
            flat[rows, low:high] = total

    def turn(values, rows):
        return values * turns[0, rows] + pltpu.roll(values, HD // 2, 1) * turns[1, rows]

    project(q_cols, q_cols + 2 * HD)
    for block in range(line):
        rows = slice(block * span_len, (block + 1) * span_len)
        kv[0, rows, :HD] = turn(flat[rows, q_cols : q_cols + HD], rows).astype(bf16)
        kv[0, rows, HD:] = flat[rows, q_cols + HD : q_cols + 2 * HD].astype(bf16)
    exchange = links.send(kv.at[0], kv.at[1], "x")
    project(0, q_cols)
    for block in range(line):
        rows = slice(block * span_len, (block + 1) * span_len)
        for head in range(heads):
            lanes = slice(head * HD, (head + 1) * HD)
            query[rows, lanes] = turn(flat[rows, lanes], rows).astype(bf16)
    local.append(links.keep(query, query_ref))
    for k in far[1:]:
        far_ff.relay(k, "x" if k < line // 2 else "y")
    relay_out(0)
    move_out(2)
    exchange.wait_recv()
    local.append(links.keep(kv, kv_ref))

    scale = 1.0 / math.sqrt(HD)
    peak[...] = jnp.zeros_like(peak)

    def attend(head, carry):
        lanes = pl.ds(pl.multiple_of(head * HD, HD), HD)
        for block in range(line):
            rows = slice(block * span_len, (block + 1) * span_len)
            reach = (block + 1) * span_len
            part = query[rows, lanes]
            row = lax.broadcasted_iota(jnp.int32, (span_len, reach), 0) + block * span_len
            column = lax.broadcasted_iota(jnp.int32, (span_len, reach), 1)
            allowed = (column <= row, column < (block + links.x) * span_len)
            scores = []
            for half in range(2):
                score = lax.dot_general(
                    part, kv[half, :reach, :HD], (((1,), (1,)), ((), ())), preferred_element_type=f32
                )
                scores.append(jnp.where(allowed[half], score * scale, -1e30))
            top = jnp.maximum(
                jnp.max(scores[0], axis=-1, keepdims=True), jnp.max(scores[1], axis=-1, keepdims=True)
            )
            total, mixed = None, None
            for half in range(2):
                weight = jnp.exp(scores[half] - top)
                count = jnp.sum(weight, axis=-1, keepdims=True)
                term = jnp.dot(weight.astype(bf16), kv[half, :reach, HD:], preferred_element_type=f32)
                total = count if total is None else total + count
                mixed = term if mixed is None else mixed + term
            att[rows, lanes] = (mixed / total).astype(bf16)
            spot = lax.broadcasted_iota(jnp.int32, (span_len, HD), 1) == head
            peak[rows] = jnp.where(spot, top + jnp.log(total), peak[rows])
        return carry

    lax.fori_loop(0, heads, attend, 0)
    local.append(links.keep(peak, peak_ref))

    def place(block, rows):
        return atts_ref.at[rows, pl.ds(pl.multiple_of(block * q_cols, q_cols), q_cols)]

    att_ring = LineGather(links, group_len, lambda rows: att.at[rows], place)
    local.append(links.keep(att, place(links.z, pl.ds(0, group_len))))
    att_ring.step(0)
    for k in [0] + far:
        far_ff.close(k)
    for k in range(3, line):
        move_out(k)
    relay_out(1)
    att_ring.step(1)
    relay_out(2)
    att_ring.step(2)
    for k in range(3, line):
        relay_out(k)
    for k in range(line):
        close_out(k)
    att_ring.step(3)
    far_out.wait([(k, part) for k in range(line) for part in range(2)])
    far_ff.wait(range(line))
    links.finish()
    for copy in local:
        copy.wait()


def add_rows_of(target, values, count):
    def add(index, carry):
        rows = pl.ds(pl.multiple_of(index * 16, 16), 16)
        target[rows] = target[rows] + values[rows]
        return carry

    lax.fori_loop(0, count // 16, add, 0)


class NearSum:
    def __init__(self, links, source, own, from_core, from_first, from_second, first, in_place=False):
        self.links, self.source, self.own, self.first = links, source, own, first
        self.in_place = in_place
        self.from_core, self.from_first, self.from_second = from_core, from_first, from_second

    def start(self):
        links = self.links
        if not self.in_place:
            self.local = links.keep(self.source(links.c), self.own)
        self.copy = links.send(self.source(1 - links.c), self.from_core, "c")

    def add(self, target, values):
        add_rows_of(target, values, target.shape[0])

    def core_done(self):
        links = self.links
        self.copy.wait_recv()
        if not self.in_place:
            self.local.wait()
        for x in range(2):
            for y in range(2):
                self.add(self.own.at[x, y], self.from_core.at[x, y])
        if self.first == "x":
            self.copy = links.send(self.own.at[1 - links.x], self.from_first, "x")
        else:
            self.copy = links.send(self.own.at[:, 1 - links.y], self.from_first, "y")

    def first_done(self):
        links = self.links
        self.copy.wait_recv()
        for other in range(2):
            place = (links.x, other) if self.first == "x" else (other, links.y)
            self.add(self.own.at[place], self.from_first.at[other])
        if self.first == "x":
            self.copy = links.send(self.own.at[links.x, 1 - links.y], self.from_second, "y")
        else:
            self.copy = links.send(self.own.at[1 - links.x, links.y], self.from_second, "x")

    def second_done(self):
        self.copy.wait_recv()
        total = self.own.at[self.links.x, self.links.y]
        self.add(total, self.from_second)
        return total


def sum_space(blocks, rows, columns):
    shape = (rows, columns)
    return [
        pltpu.VMEM((blocks, 2, 2) + shape, jnp.bfloat16),
        pltpu.VMEM((blocks, 2, 2) + shape, jnp.bfloat16),
        pltpu.VMEM((blocks, 2) + shape, jnp.bfloat16),
        pltpu.VMEM((blocks,) + shape, jnp.bfloat16),
    ]


class RingSum:
    def __init__(self, links, parts, total, got, pieces=4):
        self.links, self.parts, self.total, self.got = links, parts, total, got
        self.pieces, self.last = pieces, [None] * pieces
        self.rows = parts.shape[1] // pieces

    def step(self, number):
        links = self.links
        for piece in range(self.pieces):
            way = 1 if piece < self.pieces // 2 else -1
            block = links.along(-way * (number + 1))
            where = pl.ds(piece * self.rows, self.rows)
            if number == 0:
                source = self.parts.at[block, where]
            else:
                self.last[piece].wait_recv()
                total = self.got[number - 1, where].astype(jnp.float32) + self.parts[
                    block, where
                ].astype(jnp.float32)
                if number == links.line - 1:
                    self.total[where] = total
                    continue
                self.parts[block, where] = total.astype(self.parts.dtype)
                source = self.parts.at[block, where]
            self.last[piece] = links.send(source, self.got.at[number, where], way)


def link_call(kernel, collective_id, copies, shapes, arguments, spaces=None, scratch=(), vmem=16):
    any_space = pl.BlockSpec(memory_space=pl.ANY)
    near_space = pl.BlockSpec(memory_space=pltpu.VMEM)
    many = isinstance(shapes, tuple)
    if spaces is None:
        spaces = "h" * (len(arguments) + (len(shapes) if many else 1))
    specs = [near_space if space == "v" else any_space for space in spaces]
    return pl.pallas_call(
        kernel,
        out_shape=shapes,
        in_specs=specs[: len(arguments)],
        out_specs=tuple(specs[len(arguments) :]) if many else specs[-1],
        scratch_shapes=list(scratch)
        + [pltpu.SemaphoreType.DMA((copies,)), pltpu.SemaphoreType.DMA((copies,))],
        compiler_params=pltpu.CompilerParams(
            collective_id=collective_id, has_side_effects=True, vmem_limit_bytes=vmem * 2**20
        ),
    )(*arguments)


def forward_call(small, tokens, out_grad, gain_rows, weights, line):
    span_len, width = tokens.shape
    group_len = line * span_len
    rows_each, qkv_cols = weights[0].shape[0], gain_rows.shape[1]
    q_cols = qkv_cols - 2 * HD
    both_cols = 2 * weights[3].shape[1] // line
    f32, bf16 = jnp.float32, jnp.bfloat16
    near = (line, 8, rows_each + 16, qkv_cols)
    outs = (
        ((line, span_len, width), bf16),
        (near, bf16),
        ((2, 16, width), f32),
        ((group_len, width), bf16),
        ((group_len, q_cols), bf16),
        ((2, group_len, 2 * HD), bf16),
        ((group_len, HD), f32),
        ((2, group_len, HD), f32),
        ((group_len, line * q_cols), bf16),
        ((line, 8, rows_each, both_cols), bf16),
        ((line, 8, rows_each, width), bf16),
        ((span_len, width), bf16),
    )
    return link_call(
        functools.partial(first_kernel, line),
        0,
        256,
        tuple(jax.ShapeDtypeStruct(*out) for out in outs),
        (small, tokens, out_grad, gain_rows) + weights,
        "v" + "h" * 21,
        scratch=[
            pltpu.VMEM((line, span_len, width), bf16),
            pltpu.VMEM((span_len, width), bf16),
            pltpu.VMEM((span_len, width), bf16),
            pltpu.VMEM((line,) + small.shape[1:], f32),
            pltpu.VMEM(near, bf16),
            pltpu.VMEM((2, 16, width), f32),
            pltpu.VMEM((group_len, width), bf16),
            pltpu.VMEM((2, group_len, HD), f32),
            pltpu.VMEM((group_len, qkv_cols), f32),
            pltpu.VMEM((group_len, q_cols), bf16),
            pltpu.VMEM((2, group_len, 2 * HD), bf16),
            pltpu.VMEM((group_len, HD), f32),
            pltpu.VMEM((group_len, q_cols), bf16),
        ],
        vmem=63,
    )


def mlp_kernel(
    line,
    cuts,
    small_ref,
    gain_ref,
    mix_ref,
    xs_ref,
    atts_ref,
    out_ref,
    ff_ref,
    down_ref,
    middle_ref,
    total_ref,
    output_ref,
    sum_ref,
    grad_ff_ref,
    ff_half_ref,
    big,
    ff,
    down,
    norm,
    parts,
    mixed,
    gate_up,
    hidden,
    both_grad,
    got,
    mixed_parts,
    mixed_got,
    mixed_total,
    *scratch,
):
    f32, bf16 = jnp.float32, jnp.bfloat16
    space, (send_sems, recv_sems) = scratch[:-2], scratch[-2:]
    links = Links(send_sems, recv_sems, line)
    links.meet(["x", "y", "c", 1, line - 1])
    far = [1, line - 1] + list(range(2, line - 1))
    span_len, width = mix_ref.shape
    group_len = line * span_len
    ff_cols = hidden.shape[1]
    block_rows = width // line
    rows_each = block_rows // 8
    chunk = 2 * HD
    mix_ring = RingGather(
        links, span_len, lambda rows: mix_ref.at[rows], lambda block, rows: mixed.at[block, rows]
    )
    mix_ring.step(0)
    stay = links.keep(mix_ref, mixed.at[links.z])
    early = [
        links.keep(out_ref, big),
        links.keep(atts_ref, norm),
        links.keep(xs_ref, parts),
    ]
    late = [links.keep(ff_ref, ff)]
    down_rows = down_ref.shape[0]

    def down_place(block, place):
        low, high = cuts[block]
        return down.at[pl.ds(pl.multiple_of(place * down_rows + low, 16), high - low)]

    near = NearGather(links, down_place)
    for block, (low, high) in enumerate(cuts):
        rows = down_ref.at[pl.ds(low, high - low)]
        late.append(links.keep(rows, down_place(block, links.slot)))
        near.offer(block, rows)
    ring = RingSum(links, parts, total_ref, got)
    mixed_ring = RingSum(links, mixed_parts, mixed_total, mixed_got)
    items = []
    ff_items = []
    for index, k in enumerate(far[:2]):
        block = links.along(k)
        core, first, second = space[:3]
        ff_items.append(
            NearSum(
                links,
                lambda c, block=block: ff.at[block, :, :, c],
                ff.at[block, :, :, links.c],
                core.at[index],
                first.at[index],
                second.at[index],
                "xy"[index % 2],
                True,
            )
        )
    for index, (low, high) in enumerate(cuts):
        rows = pl.ds(low, high - low)
        core, first, second = space[3 * index + 3 : 3 * index + 6]
        items.append(
            NearSum(
                links,
                lambda c, rows=rows: big.at[:, :, c, rows],
                big.at[:, :, links.c, rows],
                core.at[0],
                first.at[0],
                second.at[0],
                "xy"[index % 2],
                True,
            )
        )
    for copy in early:
        copy.wait()

    half = group_len // 2
    out_rows = width // 8
    for part in range(2):
        low = part * half
        for column in range(4):
            lanes = slice(column * width // 4, (column + 1) * width // 4)
            value = None
            for k in range(8):
                term = jnp.dot(
                    norm[low : low + half, k * out_rows : (k + 1) * out_rows],
                    big[k // 4, k // 2 % 2, k % 2, :, lanes],
                    preferred_element_type=f32,
                )
                value = term if value is None else value + term
            gate_up[:half, lanes] = value * small_ref[3, 0:1, 0:1]

        def normalise(index, carry, low=low):
            block = (low // 16 + index) // (span_len // 16)
            rows = pl.ds(pl.multiple_of(index * 16, 16), 16)
            inside = pl.ds(pl.multiple_of(lax.rem(index, span_len // 16) * 16, 16), 16)
            values = parts[block, inside].astype(f32) + gate_up[rows, :width]
            gate_up[rows, :width] = values
            inverse = lax.rsqrt(jnp.mean(values * values, axis=-1, keepdims=True) + epsilon)
            target = pl.ds(pl.multiple_of(low + index * 16, 16), 16)
            norm[target] = (values * inverse * gain_ref[1]).astype(bf16)
            return carry

        lax.fori_loop(0, half // 16, normalise, 0)

        @pl.when(links.z // (line // 2) == part)
        def _():
            where = pl.multiple_of(lax.rem(links.z, line // 2) * span_len, span_len)
            middle_ref[...] = gate_up[pl.ds(where, span_len), :width]
        if part == 0:
            mix_ring.step(1)

    for block in range(2):
        near.relay(block, "xy"[block])
    for copy in late:
        copy.wait()

    def columns_of(lanes, size):
        return ff[:, :, :, :, :, lanes].reshape(width, size)

    def forward(low, size):
        gates, ups = pl.ds(low, size), pl.ds(low + ff_cols, size)
        gate = jnp.dot(norm[...], columns_of(gates, size), preferred_element_type=f32)
        gate_up[:, gates] = gate
        swish = gate * jax.nn.sigmoid(gate)
        up = jnp.dot(norm[...], columns_of(ups, size), preferred_element_type=f32)
        gate_up[:, ups] = up
        hidden[:, gates] = (swish * up).astype(bf16)

    def backward(low, size):
        gates, ups = pl.ds(low, size), pl.ds(low + ff_cols, size)
        grad = lax.dot_general(
            mixed[...].reshape(group_len, width),
            down[gates],
            (((1,), (1,)), ((), ())),
            preferred_element_type=f32,
        )
        gate, up = gate_up[:, gates], gate_up[:, ups]
        sigmoid = jax.nn.sigmoid(gate)
        both_grad[:, gates] = (grad * up * sigmoid * (1.0 + gate * (1.0 - sigmoid))).astype(bf16)
        both_grad[:, ups] = (grad * (gate * sigmoid)).astype(bf16)

    def over_chunks(work, extent):
        def one(index, carry):
            work(pl.multiple_of(index * chunk, chunk), chunk)
            return carry

        lax.fori_loop(0, extent // chunk, one, 0)
        if extent % chunk:
            work(extent // chunk * chunk, extent % chunk)

    over_chunks(forward, ff_cols)
    mix_ring.step(2)
    for block in range(2):
        near.close(block)
    near.wait(range(2))

    def mixed_part(low, size):
        lanes = pl.ds(low, size)
        value = jnp.dot(hidden[...], down[:, lanes], preferred_element_type=f32).astype(bf16)
        mixed_parts[:, :, lanes] = value.reshape(line, span_len, size)

    over_chunks(mixed_part, width)
    mixed_ring.step(0)
    stay.wait()
    mix_ring.step(3)
    hidden_rows = hidden[...].T

    def down_part(low, size):
        lanes = pl.ds(low, size)
        value = jnp.dot(
            hidden_rows,
            mixed[:, :, lanes].reshape(group_len, size),
            preferred_element_type=f32,
        ).astype(bf16)
        big[:, :, :, : cuts[-1][1], lanes] = value.reshape(2, 2, 2, cuts[-1][1], size)

    over_chunks(down_part, width)
    for item in items:
        item.start()
    over_chunks(backward, ff_cols)
    mixed_ring.step(1)
    for item in items:
        item.core_done()

    def norm_part(index, carry):
        size = 4 * rows_each
        weight = ff[index // 2, lax.rem(index, 2)].reshape(size, 2 * ff_cols)
        value = lax.dot_general(
            both_grad[...], weight, (((1,), (1,)), ((), ())), preferred_element_type=f32
        ).astype(bf16)
        lanes = pl.ds(pl.multiple_of(index * size, size), size)
        parts[:, :, lanes] = value.reshape(line, span_len, size)
        return carry

    lax.fori_loop(0, 2 * line, norm_part, 0)
    ring.step(0)

    def ff_block(block):
        norm_rows = norm[:, pl.ds(pl.multiple_of(block * block_rows, block_rows), block_rows)].T

        def ff_part(low, size):
            lanes = pl.ds(low, size)
            value = jnp.dot(norm_rows, both_grad[:, lanes], preferred_element_type=f32)
            ff[block, :, :, :, :, lanes] = value.astype(bf16).reshape(2, 2, 2, rows_each, size)

        over_chunks(ff_part, 2 * ff_cols)

    for item, k in zip(ff_items, far):
        ff_block(links.along(k))
        item.start()
    for item in items:
        item.first_done()
    ring.step(1)
    for item in ff_items:
        item.core_done()
    mixed_ring.step(2)
    sent = []
    for k in far[2:] + [0]:
        block = links.along(k)
        ff_block(block)
        sent.append(links.keep(ff.at[block], grad_ff_ref.at[block]))
    for item, (low, high) in zip(items, cuts):
        sum_ref[low:high] = item.second_done()[...]
    ring.step(2)
    for item in ff_items:
        item.first_done()
    mixed_ring.step(3)
    for low in range(0, span_len, 16):
        rows = slice(low, low + 16)
        output_ref[rows] = (middle_ref[rows] + small_ref[3, 0:1, 0:1] * mixed_total[rows]).astype(bf16)
    ring.step(3)
    for index, item in enumerate(ff_items):
        sent.append(links.keep(item.second_done(), ff_half_ref.at[index]))
    links.finish()
    for copy in sent:
        copy.wait()


def mlp_call(small, gains, mixed, x_blocks, attended, out_w, ff_w, w_down, line):
    f32, bf16 = jnp.float32, jnp.bfloat16
    span_len, width = mixed.shape
    group_len = line * span_len
    rows, both_cols, rows_each = w_down.shape[0], ff_w.shape[3], ff_w.shape[2]
    ff_rows = 8 * rows
    ff_w = ff_w.reshape(line, 2, 2, 2, rows_each, both_cols)
    half = (rows // 2 + 15) // 16 * 16
    cuts = ((0, half), (half, rows))
    blocks = (line, span_len, width)
    token = jax.ShapeDtypeStruct((span_len, width), f32)
    return link_call(
        functools.partial(mlp_kernel, line, cuts),
        2,
        112,
        (
            token,
            token,
            jax.ShapeDtypeStruct((span_len, width), bf16),
            jax.ShapeDtypeStruct((rows, width), bf16),
            jax.ShapeDtypeStruct(ff_w.shape, bf16),
            jax.ShapeDtypeStruct((2, rows_each, both_cols), bf16),
        ),
        (small, gains, mixed, x_blocks, attended, out_w.reshape(2, 2, 2, width // 8, width), ff_w, w_down),
        "vvhhhhhh" + "vvvvhh",
        [
            pltpu.VMEM((2, 2, 2, width // 8, width), bf16),
            pltpu.VMEM(ff_w.shape, bf16),
            pltpu.VMEM((ff_rows, width), bf16),
            pltpu.VMEM((group_len, width), bf16),
            pltpu.VMEM(blocks, bf16),
            pltpu.VMEM(blocks, bf16),
            pltpu.VMEM((group_len, both_cols), f32),
            pltpu.VMEM((group_len, ff_rows), bf16),
            pltpu.VMEM((group_len, both_cols), bf16),
            pltpu.VMEM((line - 1, span_len, width), bf16),
            pltpu.VMEM(blocks, bf16),
            pltpu.VMEM((line - 1, span_len, width), bf16),
            pltpu.VMEM((span_len, width), f32),
        ]
        + sum_space(2, rows_each, both_cols)[1:]
        + sum((sum_space(1, high - low, width)[1:] for low, high in cuts), []),
        vmem=63,
    )


def backward_kernel(
    line,
    small_ref,
    gain_ref,
    middle_ref,
    norm_grad_ref,
    x_ref,
    grad_ref,
    query_ref,
    kv_ref,
    peak_ref,
    turn_ref,
    out_ref,
    atts_ref,
    weight_ref,
    norm_ref,
    ff_ref,
    ff_half_ref,
    token_ref,
    ffs_ref,
    outs_ref,
    qkvs_ref,
    x_own,
    grad_own,
    middle_grad,
    total,
    big,
    slim,
    norm,
    own_rows,
    own_columns,
    branch,
    own_grad,
    att_grad,
    query_back,
    kv_back,
    kv_out,
    kv_in,
    flat,
    parts,
    query,
    kv,
    peak,
    turns,
    *scratch,
):
    f32, bf16 = jnp.float32, jnp.bfloat16
    send_sems, recv_sems = scratch[-2:]
    got, sums = scratch[0], scratch[1:-2]
    links = Links(send_sems, recv_sems, line)
    far = [1, line - 1] + list(range(2, line - 1))
    order = far + [0]
    links.meet(["x", "y", "c"] + far)
    span_len, width = x_ref.shape
    group_len = line * span_len
    q_cols = query.shape[1]
    heads = q_cols // HD
    rows_z = width // line
    rows_each = rows_z // 8
    scale = 1.0 / math.sqrt(HD)

    def lanes_of(block):
        return pl.ds(pl.multiple_of(block * q_cols, q_cols), q_cols)

    here = pl.ds(pl.multiple_of(links.z * span_len, span_len), span_len)
    first_load = links.keep(grad_ref, grad_own)
    loads = [
        links.keep(out_ref, big),
        links.keep(atts_ref.at[here], own_rows),
        links.keep(atts_ref.at[:, lanes_of(links.z)], own_columns),
        links.keep(x_ref, x_own),
        links.keep(query_ref, query),
        links.keep(kv_ref, kv),
        links.keep(peak_ref, peak),
        links.keep(turn_ref, turns),
        links.keep(norm_ref, norm),
        links.keep(weight_ref.at[:, :, :, :, pl.ds(0, slim.shape[4])], slim),
    ]
    ring = RingSum(links, parts, total, got)

    def items_of(source, space, in_place, order=order):
        items = []
        for index, k in enumerate(order):
            block = links.along(k)
            own = source.at[block, :, :, links.c] if in_place else space[0].at[index]
            core, first, second = space[-3:]
            items.append(
                NearSum(
                    links,
                    lambda c, block=block: source.at[block, :, :, c],
                    own,
                    core.at[index],
                    first.at[index],
                    second.at[index],
                    "xy"[index % 2],
                    in_place,
                )
            )
        return items

    ff_order = order[2:]
    ff_items = items_of(ff_ref, sums[:4], False, ff_order)
    out_items = items_of(big, sums[4:7], True)
    qkv_items = items_of(slim, sums[7:], True)
    local, arrived = [], []
    ff_cols = ff_ref.shape[5] // 2
    ff_pieces = ((0, ff_cols), (ff_cols, ff_cols))
    qkv_pieces = ((0, q_cols), (q_cols, HD), (q_cols + HD, HD))

    def deliver(total, target, k, pieces):
        for low, size in pieces:
            if pieces == out_pieces:
                place = target.at[links.z]
            else:
                lanes = pl.multiple_of(line * low + links.z * size, HD)
                place = target.at[:, pl.ds(lanes, size)]
            part = total.at[:, pl.ds(low, size)]
            if k == 0:
                local.append(links.keep(part, place))
            else:
                arrived.append(links.send(part, place, k))

    out_pieces = ((0, width),)
    deliver(ff_half_ref.at[0], ffs_ref, order[0], ff_pieces)
    def turn(items, target, low, high, pieces, order=order):
        for item, k in list(zip(items, order))[low:high]:
            deliver(item.second_done(), target, k, pieces)

    def core_done(items, low, high):
        for item in items[low:high]:
            item.core_done()

    def first_done(items, low, high):
        for item in items[low:high]:
            item.first_done()

    half = line // 2
    for item in ff_items:
        item.start()

    first_load.wait()
    keep = small_ref[3, 0:1, 0:1]
    token_scale = column_of(small_ref[1, 0:1])

    def norm_back(values, grad, gain):
        inverse = lax.rsqrt(jnp.mean(values * values, axis=-1, keepdims=True) + epsilon)
        scaled = gain * grad
        return inverse * scaled - values * (inverse * inverse * inverse) * jnp.mean(
            scaled * values, axis=-1, keepdims=True
        )

    for low in range(0, span_len, 16):
        rows = slice(low, low + 16)
        upstream = grad_own[rows].astype(f32) * token_scale[rows]
        grad = upstream + norm_back(middle_ref[rows], norm_grad_ref[rows], gain_ref[1])
        middle_grad[rows] = grad
        branch[rows] = (grad * keep).astype(bf16)
    loads[0].wait()
    for z in range(line):
        weight = big[z].reshape(rows_z, width)
        own_grad[:, z * rows_z : (z + 1) * rows_z] = lax.dot_general(
            branch[...], weight, (((1,), (1,)), ((), ())), preferred_element_type=f32
        ).astype(bf16)
    turned = [links.send(own_grad.at[:, lanes_of(links.along(k))], att_grad.at[here], k) for k in far]
    stayed = links.keep(own_grad.at[:, lanes_of(links.z)], att_grad.at[here])
    for copy in loads[1:]:
        copy.wait()
    deliver(ff_half_ref.at[1], ffs_ref, order[1], ff_pieces)
    core_done(ff_items, 0, line)
    for z in range(line):
        for part in range(4):
            columns = slice(part * width // 4, (part + 1) * width // 4)
            grad = lax.dot_general(
                own_rows[:, z * rows_z : (z + 1) * rows_z],
                branch[:, columns],
                (((0,), (0,)), ((), ())),
                preferred_element_type=f32,
            )
            big[z, :, :, :, :, columns] = grad.astype(bf16).reshape(2, 2, 2, rows_each, width // 4)
    for item in out_items:
        item.start()
    kv_back[...] = jnp.zeros_like(kv_back)
    for copy in turned:
        copy.wait_recv()
    stayed.wait()

    def attend_back(side, head, carry):
        lanes = pl.ds(pl.multiple_of(head * HD, HD), HD)
        for block in range(line):
            rows = slice(block * span_len, (block + 1) * span_len)
            reach = (block + 1) * span_len
            part, grad = query[rows, lanes], att_grad[rows, lanes]
            row = lax.broadcasted_iota(jnp.int32, (span_len, reach), 0) + block * span_len
            column = lax.broadcasted_iota(jnp.int32, (span_len, reach), 1)
            allowed = column <= row if side == 0 else column < (block + links.x) * span_len
            spot = lax.broadcasted_iota(jnp.int32, (span_len, HD), 1) == head
            top = jnp.sum(jnp.where(spot, peak[rows], 0.0), axis=-1, keepdims=True)
            delta = jnp.sum(
                grad.astype(f32) * own_columns[rows, lanes].astype(f32), axis=-1, keepdims=True
            )
            keys, values = kv[side, :reach, :HD], kv[side, :reach, HD:]
            score = lax.dot_general(part, keys, (((1,), (1,)), ((), ())), preferred_element_type=f32)
            weight = jnp.where(allowed, jnp.exp(score * scale - top), 0.0)
            weight_grad = lax.dot_general(
                grad, values, (((1,), (1,)), ((), ())), preferred_element_type=f32
            )
            score_grad = (weight * (weight_grad - delta)).astype(bf16)
            back = jnp.dot(score_grad, keys, preferred_element_type=f32) * scale
            kv_back[side, :reach, :HD] += lax.dot_general(
                score_grad, part, (((0,), (0,)), ((), ())), preferred_element_type=f32
            )
            kv_back[side, :reach, HD:] += lax.dot_general(
                weight.astype(bf16), grad, (((0,), (0,)), ((), ())), preferred_element_type=f32
            )
            query_back[rows, lanes] = back if side == 1 else query_back[rows, lanes] + back
        return carry

    lax.fori_loop(0, heads, functools.partial(attend_back, 1), 0)
    kv_out[:, :HD] = (kv_back[1, :, :HD] * scale).astype(bf16)
    kv_out[:, HD:] = kv_back[1, :, HD:].astype(bf16)
    exchange = links.send(kv_out, kv_in, "x")
    lax.fori_loop(0, heads, functools.partial(attend_back, 0), 0)

    def turn_back(values, rows):
        return values * turns[0, rows] - pltpu.roll(values, HD // 2, 1) * turns[1, rows]

    for block in range(line):
        rows = slice(block * span_len, (block + 1) * span_len)
        for head in range(heads):
            lanes = slice(head * HD, (head + 1) * HD)
            flat[rows, lanes] = turn_back(query_back[rows, lanes], rows).astype(bf16)
    first_done(ff_items, 0, line)
    core_done(out_items, 0, half)
    exchange.wait_recv()
    for block in range(line):
        rows = slice(block * span_len, (block + 1) * span_len)
        key_grad = kv_back[0, rows, :HD] * scale + kv_in[rows, :HD].astype(f32)
        flat[rows, q_cols : q_cols + HD] = turn_back(key_grad, rows).astype(bf16)
        value_grad = kv_back[0, rows, HD:] + kv_in[rows, HD:].astype(f32)
        flat[rows, q_cols + HD :] = value_grad.astype(bf16)
    for z in range(line):
        weight = slim[z].reshape(rows_z, flat.shape[1])
        part = lax.dot_general(
            flat[...], weight, (((1,), (1,)), ((), ())), preferred_element_type=f32
        ).astype(bf16)
        for block in range(line):
            parts[block, :, z * rows_z : (z + 1) * rows_z] = part[
                block * span_len : (block + 1) * span_len
            ]
    ring.step(0)
    turn(ff_items, ffs_ref, 0, line, ff_pieces, ff_order)
    for z in range(line):
        grad = lax.dot_general(
            norm[:, z * rows_z : (z + 1) * rows_z],
            flat[...],
            (((0,), (0,)), ((), ())),
            preferred_element_type=f32,
        )
        slim[z] = grad.astype(bf16).reshape(2, 2, 2, rows_each, flat.shape[1])
    for item in qkv_items:
        item.start()
    core_done(out_items, half, line)
    first_done(out_items, 0, half)
    ring.step(1)
    core_done(qkv_items, 0, line)
    turn(out_items, outs_ref, 0, half, out_pieces)
    first_done(out_items, half, line)
    ring.step(2)
    first_done(qkv_items, 0, half)
    turn(out_items, outs_ref, half, line, out_pieces)
    first_done(qkv_items, half, line)
    ring.step(3)
    for low in range(0, span_len, 16):
        rows = slice(low, low + 16)
        grad = middle_grad[rows] + norm_back(x_own[rows].astype(f32), total[rows], gain_ref[0])
        token_ref[rows] = grad.astype(bf16)
    turn(qkv_items, qkvs_ref, 0, line, qkv_pieces)
    for copy in arrived:
        copy.wait_recv()
    links.finish()
    for copy in local:
        copy.wait()


def backward_call(near, tokens, saved, out_w, attended, weights, norm, grad_ff, ff_half, line):
    f32, bf16 = jnp.float32, jnp.bfloat16
    span_len, width = tokens[0].shape
    group_len = line * span_len
    query = saved[0]
    q_cols, rows_each, qkv_cols = query.shape[1], width // line // 8, weights.shape[3]
    weights = weights.reshape(line, 2, 2, 2, -1, qkv_cols)
    wide = (line, 2, 2, 2, rows_each, width)
    slim = (line, 2, 2, 2, rows_each, qkv_cols)
    out_space = sum_space(line, rows_each, width)[1:]
    qkv_space = sum_space(line, rows_each, qkv_cols)[1:]
    token = jax.ShapeDtypeStruct((span_len, width), bf16)
    return link_call(
        functools.partial(backward_kernel, line),
        4,
        160,
        (token,)
        + (
            jax.ShapeDtypeStruct((rows_each, line * grad_ff.shape[5]), bf16),
            jax.ShapeDtypeStruct((line, rows_each, width), bf16),
            jax.ShapeDtypeStruct((rows_each, line * qkv_cols), bf16),
        ),
        near + tokens + saved + (out_w.reshape(wide), attended, weights, norm, grad_ff, ff_half),
        "v" * 4 + "h" * 12 + "vhhh",
        [pltpu.VMEM((span_len, width), bf16)] * 2
        + [pltpu.VMEM((span_len, width), f32)] * 2
        + [
            pltpu.VMEM(wide, bf16),
            pltpu.VMEM(slim, bf16),
            pltpu.VMEM((group_len, width), bf16),
            pltpu.VMEM((span_len, width), bf16),
            pltpu.VMEM((group_len, q_cols), bf16),
            pltpu.VMEM((span_len, width), bf16),
            pltpu.VMEM((span_len, width), bf16),
            pltpu.VMEM((group_len, q_cols), bf16),
            pltpu.VMEM((group_len, q_cols), f32),
            pltpu.VMEM((2, group_len, 2 * HD), f32),
            pltpu.VMEM((group_len, 2 * HD), bf16),
            pltpu.VMEM((group_len, 2 * HD), bf16),
            pltpu.VMEM((group_len, qkv_cols), bf16),
            pltpu.VMEM((line, span_len, width), bf16),
        ]
        + [pltpu.VMEM(value.shape, value.dtype) for value in saved]
        + [pltpu.VMEM((line - 1, span_len, width), bf16)]
        + sum_space(line - 2, rows_each, grad_ff.shape[5])
        + out_space
        + qkv_space,
        vmem=63,
    )


def general_body(
    tokens,
    attn_gain,
    w_query,
    w_key,
    w_value,
    w_out,
    mlp_gain,
    w_gate,
    w_up,
    w_down,
    keep_mask,
    group_ids,
    positions,
    exit_scale,
    out_grad,
):
    seq_count, span_len, model_width = tokens.shape
    kv_heads = KVH
    head_dim = HD
    head_count = HEADS
    group_size = head_count // kv_heads
    row_count = seq_count * span_len
    stripe = group_size * span_len
    wide_count = lax.axis_size("wide")
    wide_place = lax.axis_index("wide")
    full_len = span_len * wide_count
    score_scale = 1.0 / math.sqrt(head_dim)
    gain_one, query_w, key_w, value_w, out_w = (
        lax.all_gather(attn_gain, ("wide", "narrow"), axis=0, tiled=True),
        lax.all_gather(w_query, ("wide", "narrow"), axis=0, tiled=True),
        lax.all_gather(w_key, ("wide", "narrow"), axis=0, tiled=True),
        lax.all_gather(w_value, ("wide", "narrow"), axis=0, tiled=True),
        lax.all_gather(w_out, ("wide", "narrow"), axis=0, tiled=True),
    )
    inputs = tokens.astype(jnp.float32).reshape(row_count, model_width)
    token_pos = positions.reshape(row_count)
    keep_rows = jnp.repeat(keep_mask.astype(jnp.float32), span_len)[:, None]
    inverse_one = lax.rsqrt(jnp.mean(inputs * inputs, axis=-1, keepdims=True) + epsilon)
    first_norm = (inputs * inverse_one * gain_one.astype(jnp.float32)).astype(jnp.bfloat16)
    query_pre = jnp.dot(first_norm, query_w, preferred_element_type=jnp.float32).reshape(
        row_count, head_count, head_dim
    )
    key_pre = jnp.dot(first_norm, key_w, preferred_element_type=jnp.float32).reshape(
        row_count, kv_heads, head_dim
    )
    query_rows = rotate(query_pre, token_pos, 1.0).astype(jnp.bfloat16)
    key_heads = (
        rotate(key_pre, token_pos, 1.0)
        .astype(jnp.bfloat16)
        .reshape(seq_count, span_len, kv_heads * head_dim)
    )
    value_heads = (
        jnp.dot(first_norm, value_w, preferred_element_type=jnp.float32)
        .astype(jnp.bfloat16)
        .reshape(seq_count, span_len, kv_heads * head_dim)
    )
    queries = (
        query_rows.reshape(seq_count, span_len, kv_heads, group_size, head_dim)
        .transpose(0, 2, 3, 1, 4)
        .reshape(seq_count, kv_heads, stripe, head_dim)
    )
    query_index = wide_place * span_len + jnp.arange(stripe, dtype=jnp.int32) % span_len
    last_query = wide_place * span_len + span_len - 1

    def block_scores(key_block, key_first):
        scores = (
            jnp.einsum("skrd,sjkd->skrj", queries, key_block, preferred_element_type=jnp.float32)
            * score_scale
        )
        key_index = key_first + jnp.arange(key_block.shape[1], dtype=jnp.int32)
        allowed = key_index[None, :] <= query_index[:, None]
        return (scores, allowed)

    start_forward = (
        jnp.full((seq_count, kv_heads, stripe), -1e30, jnp.float32),
        jnp.zeros((seq_count, kv_heads, stripe), jnp.float32),
        jnp.zeros((seq_count, kv_heads, stripe, head_dim), jnp.float32),
    )
    running = start_forward
    pieces = (
        lax.all_gather(key_heads, "wide", axis=1, tiled=True),
        lax.all_gather(value_heads, "wide", axis=1, tiled=True),
    )
    key_blocks = split_blocks(pieces[0], seq_count, kv_heads, head_dim)
    value_blocks = split_blocks(pieces[1], seq_count, kv_heads, head_dim)
    block_len = key_blocks.shape[2]

    def advance(carried, block_item):
        key_block, value_block, block_index = block_item
        key_first = block_index * block_len

        def compute_block(current):
            run_max, run_sum, run_acc = current
            scores, allowed = block_scores(key_block, key_first)
            scores = jnp.where(allowed, scores, -1e30)
            new_max = jnp.maximum(run_max, jnp.max(scores, axis=-1))
            factor = jnp.exp(run_max - new_max)
            weights = jnp.where(allowed, jnp.exp(scores - new_max[..., None]), 0.0)
            new_sum = run_sum * factor + jnp.sum(weights, axis=-1)
            new_acc = run_acc * factor[..., None] + jnp.einsum(
                "skrj,sjkd->skrd",
                weights.astype(jnp.bfloat16),
                value_block,
                preferred_element_type=jnp.float32,
            )
            return (new_max, new_sum, new_acc)

        return (lax.cond(key_first <= last_query, compute_block, unchanged, carried), None)

    running, _ = lax.scan(
        advance,
        running,
        (key_blocks, value_blocks, jnp.arange(key_blocks.shape[0], dtype=jnp.int32)),
    )
    run_max, run_sum, run_acc = running
    attended = run_acc / run_sum[..., None]
    log_total = run_max + jnp.log(run_sum)
    attended_rows = (
        attended.reshape(seq_count, kv_heads, group_size, span_len, head_dim)
        .transpose(0, 3, 1, 2, 4)
        .reshape(row_count, head_count * head_dim)
        .astype(jnp.bfloat16)
    )
    middle = inputs + keep_rows * jnp.dot(attended_rows, out_w, preferred_element_type=jnp.float32)
    gain_two, gate_w, up_w, down_w = (
        lax.all_gather(mlp_gain, ("wide", "narrow"), axis=0, tiled=True),
        lax.all_gather(w_gate, ("wide", "narrow"), axis=0, tiled=True),
        lax.all_gather(w_up, ("wide", "narrow"), axis=0, tiled=True),
        lax.all_gather(w_down, ("wide", "narrow"), axis=0, tiled=True),
    )
    inverse_two = lax.rsqrt(jnp.mean(middle * middle, axis=-1, keepdims=True) + epsilon)
    second_norm = (middle * inverse_two * gain_two.astype(jnp.float32)).astype(jnp.bfloat16)
    gate_value = jnp.dot(second_norm, gate_w, preferred_element_type=jnp.float32)
    up_value = jnp.dot(second_norm, up_w, preferred_element_type=jnp.float32)
    gate_sigmoid = jax.nn.sigmoid(gate_value)
    swish_value = gate_value * gate_sigmoid
    hidden = (swish_value * up_value).astype(jnp.bfloat16)
    output = (
        middle + keep_rows * jnp.dot(hidden, down_w, preferred_element_type=jnp.float32)
    ).astype(jnp.bfloat16)
    group_match = (
        group_ids.reshape(row_count)[:, None]
        == jnp.arange(exit_scale.shape[0], dtype=jnp.int32)[None, :]
    )
    token_scale = jnp.sum(jnp.where(group_match, exit_scale[None, :], 0.0), axis=1, keepdims=True)
    upstream = out_grad.astype(jnp.float32).reshape(row_count, model_width) * token_scale
    gain_two, gate_w, up_w, down_w = (
        lax.all_gather(mlp_gain, ("wide", "narrow"), axis=0, tiled=True),
        lax.all_gather(w_gate, ("wide", "narrow"), axis=0, tiled=True),
        lax.all_gather(w_up, ("wide", "narrow"), axis=0, tiled=True),
        lax.all_gather(w_down, ("wide", "narrow"), axis=0, tiled=True),
    )
    mixed_grad = (keep_rows * upstream).astype(jnp.bfloat16)
    grad_down = over_rows(hidden, mixed_grad)
    hidden_grad = against(mixed_grad, down_w)
    gate_grad = (
        hidden_grad * up_value * gate_sigmoid * (1.0 + gate_value * (1.0 - gate_sigmoid))
    ).astype(jnp.bfloat16)
    up_grad = (hidden_grad * swish_value).astype(jnp.bfloat16)
    grad_gate = over_rows(second_norm, gate_grad)
    grad_up = over_rows(second_norm, up_grad)
    norm_grad = against(gate_grad, gate_w) + against(up_grad, up_w)
    grad_gain_two = jnp.sum(norm_grad * middle * inverse_two, axis=0)
    scaled_two = gain_two.astype(jnp.float32) * norm_grad
    middle_grad = (
        upstream
        + inverse_two * scaled_two
        - middle
        * (inverse_two * inverse_two * inverse_two)
        * jnp.mean(scaled_two * middle, axis=-1, keepdims=True)
    )
    gain_two_share, gate_share, up_share, down_share = (
        lax.psum_scatter(grad_gain_two, ("wide", "narrow"), scatter_dimension=0, tiled=True),
        lax.psum_scatter(grad_gate, ("wide", "narrow"), scatter_dimension=0, tiled=True),
        lax.psum_scatter(grad_up, ("wide", "narrow"), scatter_dimension=0, tiled=True),
        lax.psum_scatter(grad_down, ("wide", "narrow"), scatter_dimension=0, tiled=True),
    )
    gain_one, query_w, key_w, value_w, out_w = (
        lax.all_gather(attn_gain, ("wide", "narrow"), axis=0, tiled=True),
        lax.all_gather(w_query, ("wide", "narrow"), axis=0, tiled=True),
        lax.all_gather(w_key, ("wide", "narrow"), axis=0, tiled=True),
        lax.all_gather(w_value, ("wide", "narrow"), axis=0, tiled=True),
        lax.all_gather(w_out, ("wide", "narrow"), axis=0, tiled=True),
    )
    branch_grad = (keep_rows * middle_grad).astype(jnp.bfloat16)
    grad_out = over_rows(attended_rows, branch_grad)
    attended_grad = against(branch_grad, out_w).astype(jnp.bfloat16)
    grouped_grad = (
        attended_grad.reshape(seq_count, span_len, kv_heads, group_size, head_dim)
        .transpose(0, 2, 3, 1, 4)
        .reshape(seq_count, kv_heads, stripe, head_dim)
    )
    row_delta = jnp.sum(grouped_grad.astype(jnp.float32) * attended, axis=-1)
    start_backward = (
        jnp.zeros((seq_count, kv_heads, stripe, head_dim), jnp.float32),
        jnp.zeros((seq_count, full_len, kv_heads * head_dim), jnp.float32),
        jnp.zeros((seq_count, full_len, kv_heads * head_dim), jnp.float32),
    )
    running = start_backward
    pieces = (
        lax.all_gather(key_heads, "wide", axis=1, tiled=True),
        lax.all_gather(value_heads, "wide", axis=1, tiled=True),
    )
    key_blocks = split_blocks(pieces[0], seq_count, kv_heads, head_dim)
    value_blocks = split_blocks(pieces[1], seq_count, kv_heads, head_dim)
    fold_block_len = key_blocks.shape[2]

    def advance(carried, block_item):
        key_block, value_block, block_index = block_item
        key_first = block_index * fold_block_len

        def compute_block(current):
            query_acc, key_acc, value_acc = current
            scores, allowed = block_scores(key_block, key_first)
            probabilities = jnp.where(allowed, jnp.exp(scores - log_total[..., None]), 0.0)
            value_part = jnp.einsum(
                "skrj,skrd->sjkd",
                probabilities.astype(jnp.bfloat16),
                grouped_grad,
                preferred_element_type=jnp.float32,
            )
            prob_grad = jnp.einsum(
                "skrd,sjkd->skrj", grouped_grad, value_block, preferred_element_type=jnp.float32
            )
            score_grad = (probabilities * (prob_grad - row_delta[..., None])).astype(jnp.bfloat16)
            query_acc = (
                query_acc
                + jnp.einsum(
                    "skrj,sjkd->skrd", score_grad, key_block, preferred_element_type=jnp.float32
                )
                * score_scale
            )
            key_part = (
                jnp.einsum(
                    "skrj,skrd->sjkd", score_grad, queries, preferred_element_type=jnp.float32
                )
                * score_scale
            )
            key_acc = add_rows(
                key_acc, key_part.reshape(seq_count, fold_block_len, kv_heads * head_dim), key_first
            )
            value_acc = add_rows(
                value_acc,
                value_part.reshape(seq_count, fold_block_len, kv_heads * head_dim),
                key_first,
            )
            return (query_acc, key_acc, value_acc)

        return (lax.cond(key_first <= last_query, compute_block, unchanged, carried), None)

    running, _ = lax.scan(
        advance,
        running,
        (key_blocks, value_blocks, jnp.arange(key_blocks.shape[0], dtype=jnp.int32)),
    )
    query_acc, key_acc, value_acc = running
    key_sum, value_sum = (
        lax.psum_scatter(
            key_acc.astype(jnp.bfloat16), "wide", scatter_dimension=1, tiled=True
        ).astype(jnp.float32),
        lax.psum_scatter(
            value_acc.astype(jnp.bfloat16), "wide", scatter_dimension=1, tiled=True
        ).astype(jnp.float32),
    )
    query_back = (
        query_acc.reshape(seq_count, kv_heads, group_size, span_len, head_dim)
        .transpose(0, 3, 1, 2, 4)
        .reshape(row_count, head_count, head_dim)
    )
    query_grad = (
        rotate(query_back, token_pos, -1.0)
        .reshape(row_count, head_count * head_dim)
        .astype(jnp.bfloat16)
    )
    key_grad = (
        rotate(key_sum.reshape(row_count, kv_heads, head_dim), token_pos, -1.0)
        .reshape(row_count, kv_heads * head_dim)
        .astype(jnp.bfloat16)
    )
    value_grad = value_sum.reshape(row_count, kv_heads * head_dim).astype(jnp.bfloat16)
    grad_query = over_rows(first_norm, query_grad)
    grad_key = over_rows(first_norm, key_grad)
    grad_value = over_rows(first_norm, value_grad)
    input_norm_grad = (
        against(query_grad, query_w) + against(key_grad, key_w) + against(value_grad, value_w)
    )
    grad_gain_one = jnp.sum(input_norm_grad * inputs * inverse_one, axis=0)
    scaled_one = gain_one.astype(jnp.float32) * input_norm_grad
    input_grad = (
        middle_grad
        + inverse_one * scaled_one
        - inputs
        * (inverse_one * inverse_one * inverse_one)
        * jnp.mean(scaled_one * inputs, axis=-1, keepdims=True)
    )
    gain_one_share, query_share, key_share, value_share, out_share = (
        lax.psum_scatter(grad_gain_one, ("wide", "narrow"), scatter_dimension=0, tiled=True),
        lax.psum_scatter(grad_query, ("wide", "narrow"), scatter_dimension=0, tiled=True),
        lax.psum_scatter(grad_key, ("wide", "narrow"), scatter_dimension=0, tiled=True),
        lax.psum_scatter(grad_value, ("wide", "narrow"), scatter_dimension=0, tiled=True),
        lax.psum_scatter(grad_out, ("wide", "narrow"), scatter_dimension=0, tiled=True),
    )
    return (
        output.reshape(seq_count, span_len, model_width),
        input_grad.astype(jnp.bfloat16).reshape(seq_count, span_len, model_width),
        gain_one_share,
        query_share,
        key_share,
        value_share,
        out_share,
        gain_two_share,
        gate_share,
        up_share,
        down_share,
    )


def line_body(
    tokens,
    attn_gain,
    w_query,
    w_key,
    w_value,
    w_out,
    mlp_gain,
    w_gate,
    w_up,
    w_down,
    keep_mask,
    group_ids,
    positions,
    exit_scale,
    out_grad,
):
    f32 = jnp.float32
    bf16 = jnp.bfloat16
    _, span_len, model_width = tokens.shape
    line = lax.axis_size("z")
    rows_each = w_query.shape[0]
    q_cols = HEADS // line * HD

    group_match = group_ids[0][:, None] == jnp.arange(exit_scale.shape[0], dtype=jnp.int32)[None, :]
    token_scale = jnp.sum(jnp.where(group_match, exit_scale[None, :], 0.0), axis=1)
    freqs = 10000.0 ** (-2.0 * jnp.arange(HD // 2, dtype=f32) / HD)
    small = jnp.stack(
        [
            positions[0].astype(f32),
            token_scale,
            jnp.concatenate([freqs, freqs]),
            jnp.broadcast_to(keep_mask.astype(f32), (span_len,)),
        ]
    )
    small = jnp.broadcast_to(small[:, None], (4, 8, span_len))

    core = lax.axis_index("c")
    gain_row = jnp.zeros((q_cols + 2 * HD,), bf16)
    gain_row = lax.dynamic_update_slice_in_dim(gain_row, attn_gain, core * rows_each, 0)
    gain_row = lax.dynamic_update_slice_in_dim(gain_row, mlp_gain, HD + core * rows_each, 0)
    gain_rows = jnp.broadcast_to(gain_row, (16, gain_row.shape[0]))
    (
        x_blocks,
        near_w,
        gain_all,
        first_norm,
        queries,
        both_kv,
        log_total,
        turns,
        attended_rows,
        ff_w,
        out_w,
        own_mixed,
    ) = forward_call(
        small,
        tokens[0],
        out_grad[0],
        gain_rows,
        (w_query, w_key, w_value, w_gate, w_up, w_out),
        line,
    )
    middle, norm_grad, output, grad_down, grad_ff, ff_half = mlp_call(
        small,
        gain_all,
        own_mixed,
        x_blocks,
        attended_rows,
        out_w,
        ff_w,
        w_down,
        line,
    )
    grad_down = grad_down.astype(f32)
    token_grad, ff_back, out_back, qkv_back = backward_call(
        (small, gain_all, middle, norm_grad),
        (tokens[0], out_grad[0]),
        (queries, both_kv, log_total, turns),
        out_w,
        attended_rows,
        near_w,
        first_norm,
        grad_ff,
        ff_half,
        line,
    )
    ff_back = ff_back.astype(f32)
    qkv_back = qkv_back.astype(f32)
    grad_out = jnp.sum(out_back.astype(f32), axis=0)
    heads_end, keys_end = w_query.shape[1], w_query.shape[1] + w_key.shape[1]
    grad_query = qkv_back[:, :heads_end]
    grad_key = qkv_back[:, heads_end:keys_end]
    grad_value = qkv_back[:, keys_end:]
    grad_gate = ff_back[:, : w_gate.shape[1]]
    grad_up = ff_back[:, w_gate.shape[1] :]

    def gain_grad(pairs, gain):
        total = sum(jnp.sum(weight.astype(f32) * grad, axis=1) for weight, grad in pairs)
        return total / gain.astype(f32)

    return (
        output[None],
        token_grad[None],
        gain_grad([(w_query, grad_query), (w_key, grad_key), (w_value, grad_value)], attn_gain),
        grad_query,
        grad_key,
        grad_value,
        grad_out,
        gain_grad([(w_gate, grad_gate), (w_up, grad_up)], mlp_gain),
        grad_gate,
        grad_up,
        grad_down,
    )


def solution(mesh):
    wide, narrow = mesh.shape["wide"], mesh.shape["narrow"]
    if wide == 2 * KVH and narrow == 4:
        mesh = Mesh(mesh.devices.reshape(wide // 2, 2, 2, 2), ("z", "x", "y", "c"))
        body, wide, narrow = line_body, ("z", "x"), ("y", "c")
    else:
        body, wide, narrow = general_body, ("wide",), ("narrow",)
    token_spec = P(narrow, wide, None)
    id_spec = P(narrow, wide)
    gain_spec = P(wide + narrow)
    weight_spec = P(wide + narrow, None)
    return jax.shard_map(
        body,
        mesh=mesh,
        in_specs=(
            token_spec,
            gain_spec,
            weight_spec,
            weight_spec,
            weight_spec,
            weight_spec,
            gain_spec,
            weight_spec,
            weight_spec,
            weight_spec,
            P(narrow),
            id_spec,
            id_spec,
            P(),
            token_spec,
        ),
        out_specs=(
            token_spec,
            token_spec,
            gain_spec,
            weight_spec,
            weight_spec,
            weight_spec,
            weight_spec,
            gain_spec,
            weight_spec,
            weight_spec,
            weight_spec,
        ),
        check_vma=False,
    )
```

```python
import functools
import math

import jax
import jax.numpy as jnp
from jax import lax
from jax.experimental import pallas as pl
from jax.experimental.pallas import tpu as pltpu
from jax.sharding import Mesh
from jax.sharding import PartitionSpec as P

HEADS = 16
KVH = 4
HD = 128


epsilon = 1e-05


def rotate(vectors, token_pos, direction):
    half_size = vectors.shape[-1] // 2
    freqs = 10000.0 ** (-2.0 * jnp.arange(half_size, dtype=jnp.float32) / vectors.shape[-1])
    angles = token_pos.astype(jnp.float32)[:, None] * freqs[None, :]
    cosine = jnp.cos(angles)[:, None, :]
    sine = direction * jnp.sin(angles)[:, None, :]
    first_half = vectors[..., :half_size]
    second_half = vectors[..., half_size:]
    return jnp.concatenate(
        [first_half * cosine - second_half * sine, second_half * cosine + first_half * sine],
        axis=-1,
    )


def split_blocks(piece_arr, seq_count, kv_heads, head_dim):
    piece_len = piece_arr.shape[1]
    block_len = math.gcd(piece_len, 512)
    shaped = piece_arr.reshape(seq_count, piece_len // block_len, block_len, kv_heads, head_dim)
    return shaped.transpose(1, 0, 2, 3, 4)


def add_rows(whole_arr, update, first_row):
    current = lax.dynamic_slice_in_dim(whole_arr, first_row, update.shape[1], 1)
    return lax.dynamic_update_slice_in_dim(whole_arr, current + update, first_row, 1)


def over_rows(left, right):
    return lax.dot_general(
        left, right, (((0,), (0,)), ((), ())), preferred_element_type=jnp.float32
    )


def against(left, right):
    return lax.dot_general(
        left, right, (((1,), (1,)), ((), ())), preferred_element_type=jnp.float32
    )


def unchanged(carried):
    return carried


MESH = pl.DeviceIdType.MESH
AXES = ("z", "x", "y", "c")


def only(when, act):
    if when is None:
        act()
    else:
        pl.when(when)(act)


class Links:
    def __init__(self, send_sems, recv_sems, line):
        self.send_sems, self.recv_sems, self.line = send_sems, recv_sems, line
        self.z, self.x, self.y, self.c = (lax.axis_index(name) for name in AXES)
        self.slot = self.x * 4 + self.y * 2 + self.c
        self.used = 0
        self.sent = []

    def device(self, to):
        if to == "x":
            return (self.z, 1 - self.x, self.y, self.c)
        if to == "y":
            return (self.z, self.x, 1 - self.y, self.c)
        if to == "c":
            return (self.z, self.x, self.y, 1 - self.c)
        return (self.along(to), self.x, self.y, self.c)

    def along(self, step):
        return lax.rem(self.z + step + self.line, self.line)

    def other(self, to):
        slot = self.slot
        for name in to:
            bit = {"x": 4, "y": 2, "c": 1}[name]
            here = {"x": self.x, "y": self.y, "c": self.c}[name]
            slot = slot + bit * (1 - 2 * here)
        return slot

    def meet(self, targets):
        barrier = pltpu.get_barrier_semaphore()
        for to in targets:
            pl.semaphore_signal(barrier, inc=1, device_id=self.device(to), device_id_type=MESH)
        pl.semaphore_wait(barrier, len(targets))

    def send(self, source, target, to, when=None):
        copy = pltpu.make_async_remote_copy(
            src_ref=source,
            dst_ref=target,
            send_sem=self.send_sems.at[self.used],
            recv_sem=self.recv_sems.at[self.used],
            device_id=self.device(to),
            device_id_type=MESH,
        )
        only(when, copy.start)
        self.used += 1
        self.sent.append((copy, when))
        return copy

    def keep(self, source, target):
        copy = pltpu.make_async_copy(source, target, self.send_sems.at[self.used])
        copy.start()
        self.used += 1
        return copy

    def finish(self):
        for copy, when in self.sent:
            only(when, copy.wait_send)


class NearGather:
    def __init__(self, links, slot):
        self.links, self.slot = links, slot
        self.got = {}

    def offer(self, block, source):
        target = self.slot(block, self.links.slot)
        for to in ("x", "y", "c"):
            self.got[block, to] = self.links.send(source, target, to)

    def relay(self, block, first):
        links = self.links
        for to, then in (("x", "y"), ("y", "x")):
            self.got[block, to].wait_recv()
            place = self.slot(block, links.other(to))
            self.got[block, to + "c"] = links.send(place, place, "c")
            if to == first:
                self.got[block, "xy"] = links.send(place, place, then)

    def close(self, block):
        self.got[block, "xy"].wait_recv()
        place = self.slot(block, self.links.other("xy"))
        self.got[block, "xyc"] = self.links.send(place, place, "c")

    def wait(self, blocks):
        for block in blocks:
            for to in ("c", "xc", "yc", "xyc"):
                self.got[block, to].wait_recv()


class LineGather:
    def __init__(self, links, rows, origin, place, pieces=2):
        self.links, self.origin, self.place = links, origin, place
        self.pieces, self.rows = pieces, rows // pieces
        self.last = {}

    def inside(self, block):
        return jnp.logical_and(block >= 0, block < self.links.line)

    def step(self, number):
        z = self.links.z
        for piece in range(self.pieces):
            for way in (1, -1):
                held = self.inside(z - way * number)
                if number > 0:
                    only(held, self.last[piece, way].wait_recv)
                if number == self.links.line - 1:
                    continue
                rows = pl.ds(piece * self.rows, self.rows)
                place = self.place(self.links.along(-way * number), rows)
                source = self.origin(rows) if number == 0 else place
                when = jnp.logical_and(held, self.inside(z + way))
                self.last[piece, way] = self.links.send(source, place, way, when)


class RingGather:
    def __init__(self, links, rows, origin, place, pieces=4):
        self.links, self.origin, self.place = links, origin, place
        self.pieces, self.rows = pieces, rows // pieces
        self.last = [None] * pieces

    def step(self, number):
        if number > 0:
            for copy in self.last:
                copy.wait_recv()
        if number == self.links.line - 1:
            return
        for piece in range(self.pieces):
            way = 1 if piece < self.pieces // 2 else -1
            rows = pl.ds(piece * self.rows, self.rows)
            block = self.links.along(-way * number)
            place = self.place(block, rows)
            source = self.origin(rows) if number == 0 else place
            self.last[piece] = self.links.send(source, place, way)


def column_of(row):
    size = row.shape[1]
    down = lax.broadcasted_iota(jnp.int32, (size, size), 0)
    across = lax.broadcasted_iota(jnp.int32, (size, size), 1)
    values = jnp.where(down == across, jnp.broadcast_to(row, (size, size)), 0.0)
    return jnp.sum(values, axis=1, keepdims=True)


def first_kernel(
    line,
    small_ref,
    x_ref,
    grad_ref,
    gain_rows_ref,
    query_w_ref,
    key_w_ref,
    value_w_ref,
    gate_w_ref,
    up_w_ref,
    out_ref,
    xs_ref,
    weight_ref,
    gain_ref,
    norm_ref,
    query_ref,
    kv_ref,
    peak_ref,
    turn_ref,
    atts_ref,
    ffs_ref,
    outs_ref,
    mix_ref,
    x_all,
    grad,
    mix,
    places,
    weights,
    gains,
    norm,
    turns,
    flat,
    query,
    kv,
    peak,
    att,
    send_sems,
    recv_sems,
):
    f32, bf16 = jnp.float32, jnp.bfloat16
    links = Links(send_sems, recv_sems, line)
    far = [1, line - 1] + list(range(2, line - 1))
    links.meet(["x", "y", "c"] + far)
    here = links.slot
    span_len, width = x_ref.shape
    group_len = line * span_len
    rows_each = gate_w_ref.shape[0]
    q_cols = query.shape[1]
    ff_cols = gate_w_ref.shape[1] // line
    heads = q_cols // HD
    local = []

    near = NearGather(links, lambda block, place: weights.at[links.along(-block), place])
    far_ff = NearGather(links, lambda block, place: ffs_ref.at[links.along(-block), place])
    out_half = out_ref.shape[0] // 2

    def out_part(block, place):
        k, part = block
        rows = pl.ds(part * out_half, out_half)
        return outs_ref.at[links.along(k if part else -k), place, rows]

    far_out = NearGather(links, out_part)
    ring = LineGather(
        links, span_len, lambda rows: x_ref.at[rows], lambda block, rows: x_all.at[block, rows]
    )
    place_ref = small_ref.at[0]

    def columns(weight, block, size):
        return weight.at[:, pl.ds(pl.multiple_of(block * size, HD), size)]

    def near_pieces(block):
        target = weights.at[links.z, here]
        rows = pl.ds(0, rows_each)
        return [
            (columns(query_w_ref, block, q_cols), target.at[rows, pl.ds(0, q_cols)]),
            (columns(key_w_ref, block, HD), target.at[rows, pl.ds(q_cols, HD)]),
            (columns(value_w_ref, block, HD), target.at[rows, pl.ds(q_cols + HD, HD)]),
            (gain_rows_ref, target.at[pl.ds(rows_each, 16)]),
        ]

    def ff_pieces(block):
        target = ffs_ref.at[links.z, here]
        return [
            (columns(gate_w_ref, block, ff_cols), target.at[:, pl.ds(0, ff_cols)]),
            (columns(up_w_ref, block, ff_cols), target.at[:, pl.ds(ff_cols, ff_cols)]),
        ]

    def turn_out(pieces):
        return {k: [links.send(*piece, k) for piece in pieces(links.along(k))] for k in far}

    def arrived(copies):
        for copy in copies:
            copy.wait_recv()

    own = [links.keep(*piece) for piece in near_pieces(links.z)]
    own_ff = [links.keep(*piece) for piece in ff_pieces(links.z)]
    turned = turn_out(near_pieces)
    placed = [links.send(place_ref, places.at[links.z], k) for k in far]
    turned_ff = turn_out(ff_pieces)
    for copy in own:
        copy.wait()
    near.offer(0, weights.at[links.z, here])
    for copy in own_ff:
        copy.wait()
    far_ff.offer(0, ffs_ref.at[links.z, here])
    own = [
        links.keep(x_ref, x_all.at[links.z]),
        links.keep(place_ref, places.at[links.z]),
        links.keep(grad_ref, grad),
    ]
    local.append(links.keep(out_ref, outs_ref.at[links.z, here]))

    def move_out(k):
        for part in range(2):
            if k == 0:
                block = out_ref.at[pl.ds(part * out_half, out_half)]
            else:
                moved[part].wait_recv()
                block = out_part((k, part), here)
            if k < line - 1:
                moved[part] = links.send(block, out_part((0, part), here) if k == 0 else block, 1 - 2 * part)
            far_out.offer((k, part), block)

    def relay_out(k):
        for part in range(2):
            far_out.relay((k, part), "xy"[part])

    def close_out(k):
        for part in range(2):
            far_out.close((k, part))

    moved = [None, None]
    for k in far:
        arrived(turned[k])
        near.offer(k, weights.at[links.along(-k), here])
    ring.step(0)
    for k in [0] + far:
        near.relay(k, "x" if k < line // 2 else "y")
    for k in far:
        arrived(turned_ff[k])
        far_ff.offer(k, ffs_ref.at[links.along(-k), here])
    ring.step(1)
    for k in [0] + far:
        near.close(k)
    far_ff.relay(0, "x")
    ring.step(2)
    move_out(0)
    for copy in own:
        copy.wait()
    for copy in placed:
        copy.wait_recv()

    lane = lax.broadcasted_iota(jnp.int32, (span_len, HD), 1)
    for block in range(line):
        angles = column_of(places[block, 0:1]) * small_ref[2, 0:1]
        rows = slice(block * span_len, (block + 1) * span_len)
        sine = jnp.sin(angles)
        turns[0, rows] = jnp.cos(angles)
        turns[1, rows] = jnp.where(lane < HD // 2, -sine, sine)
    local.append(links.keep(turns, turn_ref))
    token_scale = column_of(small_ref[1, 0:1])
    for low in range(0, span_len, 16):
        rows = slice(low, low + 16)
        upstream = grad[rows].astype(f32) * token_scale[rows]
        mix[rows] = (upstream * small_ref[3, 0:1, 0:1]).astype(bf16)
    local.append(links.keep(mix, mix_ref))
    near.wait(range(line))
    for index in range(line * 4):
        z, q = divmod(index, 4)
        for which in range(2):
            lanes = slice(which * HD, (which + 1) * HD)
            both = [weights[z, 2 * q + c, rows_each : rows_each + 16, lanes].astype(f32) for c in range(2)]
            first = lax.broadcasted_iota(jnp.int32, both[0].shape, 1) < rows_each
            gains[which, :, index * HD : (index + 1) * HD] = jnp.where(first, both[0], both[1])
    local.append(links.keep(weights, weight_ref))
    local.append(links.keep(gains, gain_ref))
    far_ff.relay(far[0], "x")
    ring.step(3)
    local.append(links.keep(x_all, xs_ref))
    move_out(1)

    def normalise(index, carry):
        block = index // (span_len // 16)
        rows = pl.ds(pl.multiple_of(lax.rem(index, span_len // 16) * 16, 16), 16)
        values = x_all[block, rows].astype(f32)
        inverse = lax.rsqrt(jnp.mean(values * values, axis=-1, keepdims=True) + epsilon)
        target = pl.ds(pl.multiple_of(index * 16, 16), 16)
        norm[target] = (values * inverse * gains[0]).astype(bf16)
        return carry

    lax.fori_loop(0, group_len // 16, normalise, 0)
    local.append(links.keep(norm, norm_ref))

    def project(low, high):
        step = group_len // 2
        for part in range(2):
            rows = slice(part * step, (part + 1) * step)
            total = None
            for z in range(line):
                weight = weights[z, :, :rows_each, low:high].reshape(8 * rows_each, high - low)
                term = jnp.dot(
                    norm[rows, z * 8 * rows_each : (z + 1) * 8 * rows_each],
                    weight,
                    preferred_element_type=f32,
                )
                total = term if total is None else total + term
            flat[rows, low:high] = total

    def turn(values, rows):
        return values * turns[0, rows] + pltpu.roll(values, HD // 2, 1) * turns[1, rows]

    project(q_cols, q_cols + 2 * HD)
    for block in range(line):
        rows = slice(block * span_len, (block + 1) * span_len)
        kv[0, rows, :HD] = turn(flat[rows, q_cols : q_cols + HD], rows).astype(bf16)
        kv[0, rows, HD:] = flat[rows, q_cols + HD : q_cols + 2 * HD].astype(bf16)
    exchange = links.send(kv.at[0], kv.at[1], "x")
    project(0, q_cols)
    for block in range(line):
        rows = slice(block * span_len, (block + 1) * span_len)
        for head in range(heads):
            lanes = slice(head * HD, (head + 1) * HD)
            query[rows, lanes] = turn(flat[rows, lanes], rows).astype(bf16)
    local.append(links.keep(query, query_ref))
    for k in far[1:]:
        far_ff.relay(k, "x" if k < line // 2 else "y")
    relay_out(0)
    move_out(2)
    exchange.wait_recv()
    local.append(links.keep(kv, kv_ref))

    scale = 1.0 / math.sqrt(HD)
    peak[...] = jnp.zeros_like(peak)

    def attend(head, carry):
        lanes = pl.ds(pl.multiple_of(head * HD, HD), HD)
        for block in range(line):
            rows = slice(block * span_len, (block + 1) * span_len)
            reach = (block + 1) * span_len
            part = query[rows, lanes]
            row = lax.broadcasted_iota(jnp.int32, (span_len, reach), 0) + block * span_len
            column = lax.broadcasted_iota(jnp.int32, (span_len, reach), 1)
            allowed = (column <= row, column < (block + links.x) * span_len)
            scores = []
            for half in range(2):
                score = lax.dot_general(
                    part, kv[half, :reach, :HD], (((1,), (1,)), ((), ())), preferred_element_type=f32
                )
                scores.append(jnp.where(allowed[half], score * scale, -1e30))
            top = jnp.maximum(
                jnp.max(scores[0], axis=-1, keepdims=True), jnp.max(scores[1], axis=-1, keepdims=True)
            )
            total, mixed = None, None
            for half in range(2):
                weight = jnp.exp(scores[half] - top)
                count = jnp.sum(weight, axis=-1, keepdims=True)
                term = jnp.dot(weight.astype(bf16), kv[half, :reach, HD:], preferred_element_type=f32)
                total = count if total is None else total + count
                mixed = term if mixed is None else mixed + term
            att[rows, lanes] = (mixed / total).astype(bf16)
            spot = lax.broadcasted_iota(jnp.int32, (span_len, HD), 1) == head
            peak[rows] = jnp.where(spot, top + jnp.log(total), peak[rows])
        return carry

    lax.fori_loop(0, heads, attend, 0)
    local.append(links.keep(peak, peak_ref))

    def place(block, rows):
        return atts_ref.at[rows, pl.ds(pl.multiple_of(block * q_cols, q_cols), q_cols)]

    att_ring = LineGather(links, group_len, lambda rows: att.at[rows], place)
    local.append(links.keep(att, place(links.z, pl.ds(0, group_len))))
    att_ring.step(0)
    for k in [0] + far:
        far_ff.close(k)
    for k in range(3, line):
        move_out(k)
    relay_out(1)
    att_ring.step(1)
    relay_out(2)
    att_ring.step(2)
    for k in range(3, line):
        relay_out(k)
    for k in range(line):
        close_out(k)
    att_ring.step(3)
    far_out.wait([(k, part) for k in range(line) for part in range(2)])
    far_ff.wait(range(line))
    links.finish()
    for copy in local:
        copy.wait()


def add_rows_of(target, values, count):
    def add(index, carry):
        rows = pl.ds(pl.multiple_of(index * 16, 16), 16)
        target[rows] = target[rows] + values[rows]
        return carry

    lax.fori_loop(0, count // 16, add, 0)


class NearSum:
    def __init__(self, links, source, own, from_core, from_first, from_second, first, in_place=False):
        self.links, self.source, self.own, self.first = links, source, own, first
        self.in_place = in_place
        self.from_core, self.from_first, self.from_second = from_core, from_first, from_second

    def start(self):
        links = self.links
        if not self.in_place:
            self.local = links.keep(self.source(links.c), self.own)
        self.copy = links.send(self.source(1 - links.c), self.from_core, "c")

    def add(self, target, values):
        add_rows_of(target, values, target.shape[0])

    def core_done(self):
        links = self.links
        self.copy.wait_recv()
        if not self.in_place:
            self.local.wait()
        for x in range(2):
            for y in range(2):
                self.add(self.own.at[x, y], self.from_core.at[x, y])
        if self.first == "x":
            self.copy = links.send(self.own.at[1 - links.x], self.from_first, "x")
        else:
            self.copy = links.send(self.own.at[:, 1 - links.y], self.from_first, "y")

    def first_done(self):
        links = self.links
        self.copy.wait_recv()
        for other in range(2):
            place = (links.x, other) if self.first == "x" else (other, links.y)
            self.add(self.own.at[place], self.from_first.at[other])
        if self.first == "x":
            self.copy = links.send(self.own.at[links.x, 1 - links.y], self.from_second, "y")
        else:
            self.copy = links.send(self.own.at[1 - links.x, links.y], self.from_second, "x")

    def second_done(self):
        self.copy.wait_recv()
        total = self.own.at[self.links.x, self.links.y]
        self.add(total, self.from_second)
        return total


def sum_space(blocks, rows, columns):
    shape = (rows, columns)
    return [
        pltpu.VMEM((blocks, 2, 2) + shape, jnp.bfloat16),
        pltpu.VMEM((blocks, 2, 2) + shape, jnp.bfloat16),
        pltpu.VMEM((blocks, 2) + shape, jnp.bfloat16),
        pltpu.VMEM((blocks,) + shape, jnp.bfloat16),
    ]


class RingSum:
    def __init__(self, links, parts, total, got, pieces=4):
        self.links, self.parts, self.total, self.got = links, parts, total, got
        self.pieces, self.last = pieces, [None] * pieces
        self.rows = parts.shape[1] // pieces

    def step(self, number):
        links = self.links
        for piece in range(self.pieces):
            way = 1 if piece < self.pieces // 2 else -1
            block = links.along(-way * (number + 1))
            where = pl.ds(piece * self.rows, self.rows)
            if number == 0:
                source = self.parts.at[block, where]
            else:
                self.last[piece].wait_recv()
                total = self.got[number - 1, where].astype(jnp.float32) + self.parts[
                    block, where
                ].astype(jnp.float32)
                if number == links.line - 1:
                    self.total[where] = total
                    continue
                self.parts[block, where] = total.astype(self.parts.dtype)
                source = self.parts.at[block, where]
            self.last[piece] = links.send(source, self.got.at[number, where], way)


def link_call(kernel, collective_id, copies, shapes, arguments, spaces=None, scratch=(), vmem=16):
    any_space = pl.BlockSpec(memory_space=pl.ANY)
    near_space = pl.BlockSpec(memory_space=pltpu.VMEM)
    many = isinstance(shapes, tuple)
    if spaces is None:
        spaces = "h" * (len(arguments) + (len(shapes) if many else 1))
    specs = [near_space if space == "v" else any_space for space in spaces]
    return pl.pallas_call(
        kernel,
        out_shape=shapes,
        in_specs=specs[: len(arguments)],
        out_specs=tuple(specs[len(arguments) :]) if many else specs[-1],
        scratch_shapes=list(scratch)
        + [pltpu.SemaphoreType.DMA((copies,)), pltpu.SemaphoreType.DMA((copies,))],
        compiler_params=pltpu.CompilerParams(
            collective_id=collective_id, has_side_effects=True, vmem_limit_bytes=vmem * 2**20
        ),
    )(*arguments)


def forward_call(small, tokens, out_grad, gain_rows, weights, line):
    span_len, width = tokens.shape
    group_len = line * span_len
    rows_each, qkv_cols = weights[0].shape[0], gain_rows.shape[1]
    q_cols = qkv_cols - 2 * HD
    both_cols = 2 * weights[3].shape[1] // line
    f32, bf16 = jnp.float32, jnp.bfloat16
    near = (line, 8, rows_each + 16, qkv_cols)
    outs = (
        ((line, span_len, width), bf16),
        (near, bf16),
        ((2, 16, width), f32),
        ((group_len, width), bf16),
        ((group_len, q_cols), bf16),
        ((2, group_len, 2 * HD), bf16),
        ((group_len, HD), f32),
        ((2, group_len, HD), f32),
        ((group_len, line * q_cols), bf16),
        ((line, 8, rows_each, both_cols), bf16),
        ((line, 8, rows_each, width), bf16),
        ((span_len, width), bf16),
    )
    return link_call(
        functools.partial(first_kernel, line),
        0,
        256,
        tuple(jax.ShapeDtypeStruct(*out) for out in outs),
        (small, tokens, out_grad, gain_rows) + weights,
        "v" + "h" * 21,
        scratch=[
            pltpu.VMEM((line, span_len, width), bf16),
            pltpu.VMEM((span_len, width), bf16),
            pltpu.VMEM((span_len, width), bf16),
            pltpu.VMEM((line,) + small.shape[1:], f32),
            pltpu.VMEM(near, bf16),
            pltpu.VMEM((2, 16, width), f32),
            pltpu.VMEM((group_len, width), bf16),
            pltpu.VMEM((2, group_len, HD), f32),
            pltpu.VMEM((group_len, qkv_cols), f32),
            pltpu.VMEM((group_len, q_cols), bf16),
            pltpu.VMEM((2, group_len, 2 * HD), bf16),
            pltpu.VMEM((group_len, HD), f32),
            pltpu.VMEM((group_len, q_cols), bf16),
        ],
        vmem=63,
    )


def mlp_kernel(
    line,
    cuts,
    small_ref,
    gain_ref,
    mix_ref,
    xs_ref,
    atts_ref,
    out_ref,
    ff_ref,
    down_ref,
    middle_ref,
    total_ref,
    output_ref,
    sum_ref,
    grad_ff_ref,
    ff_half_ref,
    big,
    ff,
    down,
    norm,
    parts,
    mixed,
    gate_up,
    hidden,
    both_grad,
    got,
    mixed_parts,
    mixed_got,
    mixed_total,
    *scratch,
):
    f32, bf16 = jnp.float32, jnp.bfloat16
    space, (send_sems, recv_sems) = scratch[:-2], scratch[-2:]
    links = Links(send_sems, recv_sems, line)
    far = [1, line - 1] + list(range(2, line - 1))
    span_len, width = mix_ref.shape
    group_len = line * span_len
    ff_cols = hidden.shape[1]
    block_rows = width // line
    rows_each = block_rows // 8
    chunk = 2 * HD
    early = [
        links.keep(out_ref, big),
        links.keep(atts_ref, norm),
        links.keep(xs_ref, parts),
    ]
    links.meet(["x", "y", "c", 1, line - 1])
    mix_ring = RingGather(
        links, span_len, lambda rows: mix_ref.at[rows], lambda block, rows: mixed.at[block, rows]
    )
    mix_ring.step(0)
    stay = links.keep(mix_ref, mixed.at[links.z])
    late = [links.keep(ff_ref, ff)]
    down_rows = down_ref.shape[0]

    def down_place(block, place):
        low, high = cuts[block]
        return down.at[pl.ds(pl.multiple_of(place * down_rows + low, 16), high - low)]

    near = NearGather(links, down_place)
    for block, (low, high) in enumerate(cuts):
        rows = down_ref.at[pl.ds(low, high - low)]
        late.append(links.keep(rows, down_place(block, links.slot)))
        near.offer(block, rows)
    ring = RingSum(links, parts, total_ref, got)
    mixed_ring = RingSum(links, mixed_parts, mixed_total, mixed_got)
    items = []
    ff_items = []
    for index, k in enumerate(far[:2]):
        block = links.along(k)
        core, first, second = space[:3]
        ff_items.append(
            NearSum(
                links,
                lambda c, block=block: ff.at[block, :, :, c],
                ff.at[block, :, :, links.c],
                core.at[index],
                first.at[index],
                second.at[index],
                "xy"[index % 2],
                True,
            )
        )
    for index, (low, high) in enumerate(cuts):
        rows = pl.ds(low, high - low)
        core, first, second = space[3 * index + 3 : 3 * index + 6]
        items.append(
            NearSum(
                links,
                lambda c, rows=rows: big.at[:, :, c, rows],
                big.at[:, :, links.c, rows],
                core.at[0],
                first.at[0],
                second.at[0],
                "xy"[index % 2],
                True,
            )
        )
    for copy in early:
        copy.wait()

    half = group_len // 2
    out_rows = width // 8
    for part in range(2):
        low = part * half
        for column in range(4):
            lanes = slice(column * width // 4, (column + 1) * width // 4)
            value = None
            for k in range(8):
                term = jnp.dot(
                    norm[low : low + half, k * out_rows : (k + 1) * out_rows],
                    big[k // 4, k // 2 % 2, k % 2, :, lanes],
                    preferred_element_type=f32,
                )
                value = term if value is None else value + term
            gate_up[:half, lanes] = value * small_ref[3, 0:1, 0:1]

        def normalise(index, carry, low=low):
            block = (low // 16 + index) // (span_len // 16)
            rows = pl.ds(pl.multiple_of(index * 16, 16), 16)
            inside = pl.ds(pl.multiple_of(lax.rem(index, span_len // 16) * 16, 16), 16)
            values = parts[block, inside].astype(f32) + gate_up[rows, :width]
            gate_up[rows, :width] = values
            inverse = lax.rsqrt(jnp.mean(values * values, axis=-1, keepdims=True) + epsilon)
            target = pl.ds(pl.multiple_of(low + index * 16, 16), 16)
            norm[target] = (values * inverse * gain_ref[1]).astype(bf16)
            return carry

        lax.fori_loop(0, half // 16, normalise, 0)

        @pl.when(links.z // (line // 2) == part)
        def _():
            where = pl.multiple_of(lax.rem(links.z, line // 2) * span_len, span_len)
            middle_ref[...] = gate_up[pl.ds(where, span_len), :width]
        if part == 0:
            mix_ring.step(1)

    for block in range(2):
        near.relay(block, "xy"[block])
    for copy in late:
        copy.wait()

    def columns_of(lanes, size):
        return ff[:, :, :, :, :, lanes].reshape(width, size)

    def forward(low, size):
        gates, ups = pl.ds(low, size), pl.ds(low + ff_cols, size)
        gate = jnp.dot(norm[...], columns_of(gates, size), preferred_element_type=f32)
        gate_up[:, gates] = gate
        swish = gate * jax.nn.sigmoid(gate)
        up = jnp.dot(norm[...], columns_of(ups, size), preferred_element_type=f32)
        gate_up[:, ups] = up
        hidden[:, gates] = (swish * up).astype(bf16)

    def backward(low, size):
        gates, ups = pl.ds(low, size), pl.ds(low + ff_cols, size)
        grad = lax.dot_general(
            mixed[...].reshape(group_len, width),
            down[gates],
            (((1,), (1,)), ((), ())),
            preferred_element_type=f32,
        )
        gate, up = gate_up[:, gates], gate_up[:, ups]
        sigmoid = jax.nn.sigmoid(gate)
        both_grad[:, gates] = (grad * up * sigmoid * (1.0 + gate * (1.0 - sigmoid))).astype(bf16)
        both_grad[:, ups] = (grad * (gate * sigmoid)).astype(bf16)

    def over_chunks(work, extent):
        def one(index, carry):
            work(pl.multiple_of(index * chunk, chunk), chunk)
            return carry

        lax.fori_loop(0, extent // chunk, one, 0)
        if extent % chunk:
            work(extent // chunk * chunk, extent % chunk)

    over_chunks(forward, ff_cols)
    mix_ring.step(2)
    for block in range(2):
        near.close(block)
    near.wait(range(2))

    def mixed_part(low, size):
        lanes = pl.ds(low, size)
        value = jnp.dot(hidden[...], down[:, lanes], preferred_element_type=f32).astype(bf16)
        mixed_parts[:, :, lanes] = value.reshape(line, span_len, size)

    over_chunks(mixed_part, width)
    mixed_ring.step(0)
    stay.wait()
    mix_ring.step(3)
    hidden_rows = hidden[...].T

    def down_part(low, size):
        lanes = pl.ds(low, size)
        value = jnp.dot(
            hidden_rows,
            mixed[:, :, lanes].reshape(group_len, size),
            preferred_element_type=f32,
        ).astype(bf16)
        big[:, :, :, : cuts[-1][1], lanes] = value.reshape(2, 2, 2, cuts[-1][1], size)

    over_chunks(down_part, width)
    for item in items:
        item.start()
    over_chunks(backward, ff_cols)
    mixed_ring.step(1)
    for item in items:
        item.core_done()

    def norm_part(index, carry):
        size = 4 * rows_each
        weight = ff[index // 2, lax.rem(index, 2)].reshape(size, 2 * ff_cols)
        value = lax.dot_general(
            both_grad[...], weight, (((1,), (1,)), ((), ())), preferred_element_type=f32
        ).astype(bf16)
        lanes = pl.ds(pl.multiple_of(index * size, size), size)
        parts[:, :, lanes] = value.reshape(line, span_len, size)
        return carry

    lax.fori_loop(0, 2 * line, norm_part, 0)
    ring.step(0)

    def ff_block(block):
        norm_rows = norm[:, pl.ds(pl.multiple_of(block * block_rows, block_rows), block_rows)].T

        def ff_part(low, size):
            lanes = pl.ds(low, size)
            value = jnp.dot(norm_rows, both_grad[:, lanes], preferred_element_type=f32)
            ff[block, :, :, :, :, lanes] = value.astype(bf16).reshape(2, 2, 2, rows_each, size)

        over_chunks(ff_part, 2 * ff_cols)

    for item, k in zip(ff_items, far):
        ff_block(links.along(k))
        item.start()
    for item in items:
        item.first_done()
    ring.step(1)
    for item in ff_items:
        item.core_done()
    mixed_ring.step(2)
    sent = []
    for k in far[2:] + [0]:
        block = links.along(k)
        ff_block(block)
        sent.append(links.keep(ff.at[block], grad_ff_ref.at[block]))
    for item, (low, high) in zip(items, cuts):
        sum_ref[low:high] = item.second_done()[...]
    ring.step(2)
    for item in ff_items:
        item.first_done()
    mixed_ring.step(3)
    for low in range(0, span_len, 16):
        rows = slice(low, low + 16)
        output_ref[rows] = (middle_ref[rows] + small_ref[3, 0:1, 0:1] * mixed_total[rows]).astype(bf16)
    ring.step(3)
    for index, item in enumerate(ff_items):
        sent.append(links.keep(item.second_done(), ff_half_ref.at[index]))
    links.finish()
    for copy in sent:
        copy.wait()


def mlp_call(small, gains, mixed, x_blocks, attended, out_w, ff_w, w_down, line):
    f32, bf16 = jnp.float32, jnp.bfloat16
    span_len, width = mixed.shape
    group_len = line * span_len
    rows, both_cols, rows_each = w_down.shape[0], ff_w.shape[3], ff_w.shape[2]
    ff_rows = 8 * rows
    ff_w = ff_w.reshape(line, 2, 2, 2, rows_each, both_cols)
    half = (rows // 2 + 15) // 16 * 16
    cuts = ((0, half), (half, rows))
    blocks = (line, span_len, width)
    token = jax.ShapeDtypeStruct((span_len, width), f32)
    return link_call(
        functools.partial(mlp_kernel, line, cuts),
        2,
        112,
        (
            token,
            token,
            jax.ShapeDtypeStruct((span_len, width), bf16),
            jax.ShapeDtypeStruct((rows, width), bf16),
            jax.ShapeDtypeStruct(ff_w.shape, bf16),
            jax.ShapeDtypeStruct((2, rows_each, both_cols), bf16),
        ),
        (small, gains, mixed, x_blocks, attended, out_w.reshape(2, 2, 2, width // 8, width), ff_w, w_down),
        "vvhhhhhh" + "vvvvhh",
        [
            pltpu.VMEM((2, 2, 2, width // 8, width), bf16),
            pltpu.VMEM(ff_w.shape, bf16),
            pltpu.VMEM((ff_rows, width), bf16),
            pltpu.VMEM((group_len, width), bf16),
            pltpu.VMEM(blocks, bf16),
            pltpu.VMEM(blocks, bf16),
            pltpu.VMEM((group_len, both_cols), f32),
            pltpu.VMEM((group_len, ff_rows), bf16),
            pltpu.VMEM((group_len, both_cols), bf16),
            pltpu.VMEM((line - 1, span_len, width), bf16),
            pltpu.VMEM(blocks, bf16),
            pltpu.VMEM((line - 1, span_len, width), bf16),
            pltpu.VMEM((span_len, width), f32),
        ]
        + sum_space(2, rows_each, both_cols)[1:]
        + sum((sum_space(1, high - low, width)[1:] for low, high in cuts), []),
        vmem=63,
    )


def backward_kernel(
    line,
    small_ref,
    gain_ref,
    middle_hbm,
    norm_grad_hbm,
    x_ref,
    grad_ref,
    query_ref,
    kv_ref,
    peak_ref,
    turn_ref,
    out_ref,
    atts_ref,
    weight_ref,
    norm_ref,
    ff_ref,
    ff_half_ref,
    token_ref,
    ffs_ref,
    outs_ref,
    qkvs_ref,
    middle_ref,
    norm_grad_ref,
    x_own,
    grad_own,
    middle_grad,
    total,
    big,
    slim,
    norm,
    own_rows,
    own_columns,
    branch,
    own_grad,
    att_grad,
    query_back,
    kv_back,
    kv_out,
    kv_in,
    flat,
    parts,
    query,
    kv,
    peak,
    turns,
    *scratch,
):
    f32, bf16 = jnp.float32, jnp.bfloat16
    send_sems, recv_sems = scratch[-2:]
    got, sums = scratch[0], scratch[1:-2]
    links = Links(send_sems, recv_sems, line)
    far = [1, line - 1] + list(range(2, line - 1))
    order = far + [0]
    span_len, width = x_ref.shape
    group_len = line * span_len
    q_cols = query.shape[1]
    heads = q_cols // HD
    rows_z = width // line
    rows_each = rows_z // 8
    scale = 1.0 / math.sqrt(HD)

    def lanes_of(block):
        return pl.ds(pl.multiple_of(block * q_cols, q_cols), q_cols)

    here = pl.ds(pl.multiple_of(links.z * span_len, span_len), span_len)
    first_loads = [
        links.keep(grad_ref, grad_own),
        links.keep(middle_hbm, middle_ref),
        links.keep(norm_grad_hbm, norm_grad_ref),
    ]
    loads = [
        links.keep(out_ref, big),
        links.keep(atts_ref.at[here], own_rows),
        links.keep(atts_ref.at[:, lanes_of(links.z)], own_columns),
        links.keep(x_ref, x_own),
        links.keep(query_ref, query),
        links.keep(kv_ref, kv),
        links.keep(peak_ref, peak),
        links.keep(turn_ref, turns),
        links.keep(norm_ref, norm),
        links.keep(weight_ref.at[:, :, :, :, pl.ds(0, slim.shape[4])], slim),
    ]
    links.meet(["x", "y", "c"] + far)
    ring = RingSum(links, parts, total, got)

    def items_of(source, space, in_place, order=order):
        items = []
        for index, k in enumerate(order):
            block = links.along(k)
            own = source.at[block, :, :, links.c] if in_place else space[0].at[index]
            core, first, second = space[-3:]
            items.append(
                NearSum(
                    links,
                    lambda c, block=block: source.at[block, :, :, c],
                    own,
                    core.at[index],
                    first.at[index],
                    second.at[index],
                    "xy"[index % 2],
                    in_place,
                )
            )
        return items

    ff_order = order[2:]
    ff_items = items_of(ff_ref, sums[:4], False, ff_order)
    out_items = items_of(big, sums[4:7], True)
    qkv_items = items_of(slim, sums[7:], True)
    local, arrived = [], []
    ff_cols = ff_ref.shape[5] // 2
    ff_pieces = ((0, ff_cols), (ff_cols, ff_cols))
    qkv_pieces = ((0, q_cols), (q_cols, HD), (q_cols + HD, HD))

    def deliver(total, target, k, pieces):
        for low, size in pieces:
            if pieces == out_pieces:
                place = target.at[links.z]
            else:
                lanes = pl.multiple_of(line * low + links.z * size, HD)
                place = target.at[:, pl.ds(lanes, size)]
            part = total.at[:, pl.ds(low, size)]
            if k == 0:
                local.append(links.keep(part, place))
            else:
                arrived.append(links.send(part, place, k))

    out_pieces = ((0, width),)
    deliver(ff_half_ref.at[0], ffs_ref, order[0], ff_pieces)
    def turn(items, target, low, high, pieces, order=order):
        for item, k in list(zip(items, order))[low:high]:
            deliver(item.second_done(), target, k, pieces)

    def core_done(items, low, high):
        for item in items[low:high]:
            item.core_done()

    def first_done(items, low, high):
        for item in items[low:high]:
            item.first_done()

    half = line // 2
    for item in ff_items:
        item.start()

    for copy in first_loads:
        copy.wait()
    keep = small_ref[3, 0:1, 0:1]
    token_scale = column_of(small_ref[1, 0:1])

    def norm_back(values, grad, gain):
        inverse = lax.rsqrt(jnp.mean(values * values, axis=-1, keepdims=True) + epsilon)
        scaled = gain * grad
        return inverse * scaled - values * (inverse * inverse * inverse) * jnp.mean(
            scaled * values, axis=-1, keepdims=True
        )

    for low in range(0, span_len, 16):
        rows = slice(low, low + 16)
        upstream = grad_own[rows].astype(f32) * token_scale[rows]
        grad = upstream + norm_back(middle_ref[rows], norm_grad_ref[rows], gain_ref[1])
        middle_grad[rows] = grad
        branch[rows] = (grad * keep).astype(bf16)
    loads[0].wait()
    for z in range(line):
        weight = big[z].reshape(rows_z, width)
        own_grad[:, z * rows_z : (z + 1) * rows_z] = lax.dot_general(
            branch[...], weight, (((1,), (1,)), ((), ())), preferred_element_type=f32
        ).astype(bf16)
    turned = [links.send(own_grad.at[:, lanes_of(links.along(k))], att_grad.at[here], k) for k in far]
    stayed = links.keep(own_grad.at[:, lanes_of(links.z)], att_grad.at[here])
    for copy in loads[1:]:
        copy.wait()
    deliver(ff_half_ref.at[1], ffs_ref, order[1], ff_pieces)
    core_done(ff_items, 0, line)
    for z in range(line):
        for part in range(4):
            columns = slice(part * width // 4, (part + 1) * width // 4)
            grad = lax.dot_general(
                own_rows[:, z * rows_z : (z + 1) * rows_z],
                branch[:, columns],
                (((0,), (0,)), ((), ())),
                preferred_element_type=f32,
            )
            big[z, :, :, :, :, columns] = grad.astype(bf16).reshape(2, 2, 2, rows_each, width // 4)
    for item in out_items:
        item.start()
    kv_back[...] = jnp.zeros_like(kv_back)
    for copy in turned:
        copy.wait_recv()
    stayed.wait()

    def attend_back(side, head, carry):
        lanes = pl.ds(pl.multiple_of(head * HD, HD), HD)
        for block in range(line):
            rows = slice(block * span_len, (block + 1) * span_len)
            reach = (block + 1) * span_len
            part, grad = query[rows, lanes], att_grad[rows, lanes]
            row = lax.broadcasted_iota(jnp.int32, (span_len, reach), 0) + block * span_len
            column = lax.broadcasted_iota(jnp.int32, (span_len, reach), 1)
            allowed = column <= row if side == 0 else column < (block + links.x) * span_len
            spot = lax.broadcasted_iota(jnp.int32, (span_len, HD), 1) == head
            top = jnp.sum(jnp.where(spot, peak[rows], 0.0), axis=-1, keepdims=True)
            delta = jnp.sum(
                grad.astype(f32) * own_columns[rows, lanes].astype(f32), axis=-1, keepdims=True
            )
            keys, values = kv[side, :reach, :HD], kv[side, :reach, HD:]
            score = lax.dot_general(part, keys, (((1,), (1,)), ((), ())), preferred_element_type=f32)
            weight = jnp.where(allowed, jnp.exp(score * scale - top), 0.0)
            weight_grad = lax.dot_general(
                grad, values, (((1,), (1,)), ((), ())), preferred_element_type=f32
            )
            score_grad = (weight * (weight_grad - delta)).astype(bf16)
            back = jnp.dot(score_grad, keys, preferred_element_type=f32) * scale
            kv_back[side, :reach, :HD] += lax.dot_general(
                score_grad, part, (((0,), (0,)), ((), ())), preferred_element_type=f32
            )
            kv_back[side, :reach, HD:] += lax.dot_general(
                weight.astype(bf16), grad, (((0,), (0,)), ((), ())), preferred_element_type=f32
            )
            query_back[rows, lanes] = back if side == 1 else query_back[rows, lanes] + back
        return carry

    lax.fori_loop(0, heads, functools.partial(attend_back, 1), 0)
    kv_out[:, :HD] = (kv_back[1, :, :HD] * scale).astype(bf16)
    kv_out[:, HD:] = kv_back[1, :, HD:].astype(bf16)
    exchange = links.send(kv_out, kv_in, "x")
    lax.fori_loop(0, heads, functools.partial(attend_back, 0), 0)

    def turn_back(values, rows):
        return values * turns[0, rows] - pltpu.roll(values, HD // 2, 1) * turns[1, rows]

    for block in range(line):
        rows = slice(block * span_len, (block + 1) * span_len)
        for head in range(heads):
            lanes = slice(head * HD, (head + 1) * HD)
            flat[rows, lanes] = turn_back(query_back[rows, lanes], rows).astype(bf16)
    first_done(ff_items, 0, line)
    core_done(out_items, 0, half)
    exchange.wait_recv()
    for block in range(line):
        rows = slice(block * span_len, (block + 1) * span_len)
        key_grad = kv_back[0, rows, :HD] * scale + kv_in[rows, :HD].astype(f32)
        flat[rows, q_cols : q_cols + HD] = turn_back(key_grad, rows).astype(bf16)
        value_grad = kv_back[0, rows, HD:] + kv_in[rows, HD:].astype(f32)
        flat[rows, q_cols + HD :] = value_grad.astype(bf16)
    for z in range(line):
        weight = slim[z].reshape(rows_z, flat.shape[1])
        part = lax.dot_general(
            flat[...], weight, (((1,), (1,)), ((), ())), preferred_element_type=f32
        ).astype(bf16)
        for block in range(line):
            parts[block, :, z * rows_z : (z + 1) * rows_z] = part[
                block * span_len : (block + 1) * span_len
            ]
    ring.step(0)
    turn(ff_items, ffs_ref, 0, line, ff_pieces, ff_order)
    for z in range(line):
        grad = lax.dot_general(
            norm[:, z * rows_z : (z + 1) * rows_z],
            flat[...],
            (((0,), (0,)), ((), ())),
            preferred_element_type=f32,
        )
        slim[z] = grad.astype(bf16).reshape(2, 2, 2, rows_each, flat.shape[1])
    for item in qkv_items:
        item.start()
    core_done(out_items, half, line)
    first_done(out_items, 0, half)
    ring.step(1)
    core_done(qkv_items, 0, line)
    turn(out_items, outs_ref, 0, half, out_pieces)
    first_done(out_items, half, line)
    ring.step(2)
    first_done(qkv_items, 0, half)
    turn(out_items, outs_ref, half, line, out_pieces)
    first_done(qkv_items, half, line)
    ring.step(3)
    for low in range(0, span_len, 16):
        rows = slice(low, low + 16)
        grad = middle_grad[rows] + norm_back(x_own[rows].astype(f32), total[rows], gain_ref[0])
        token_ref[rows] = grad.astype(bf16)
    turn(qkv_items, qkvs_ref, 0, line, qkv_pieces)
    for copy in arrived:
        copy.wait_recv()
    links.finish()
    for copy in local:
        copy.wait()


def backward_call(near, tokens, saved, out_w, attended, weights, norm, grad_ff, ff_half, line):
    f32, bf16 = jnp.float32, jnp.bfloat16
    span_len, width = tokens[0].shape
    group_len = line * span_len
    query = saved[0]
    q_cols, rows_each, qkv_cols = query.shape[1], width // line // 8, weights.shape[3]
    weights = weights.reshape(line, 2, 2, 2, -1, qkv_cols)
    wide = (line, 2, 2, 2, rows_each, width)
    slim = (line, 2, 2, 2, rows_each, qkv_cols)
    out_space = sum_space(line, rows_each, width)[1:]
    qkv_space = sum_space(line, rows_each, qkv_cols)[1:]
    token = jax.ShapeDtypeStruct((span_len, width), bf16)
    return link_call(
        functools.partial(backward_kernel, line),
        4,
        160,
        (token,)
        + (
            jax.ShapeDtypeStruct((rows_each, line * grad_ff.shape[5]), bf16),
            jax.ShapeDtypeStruct((line, rows_each, width), bf16),
            jax.ShapeDtypeStruct((rows_each, line * qkv_cols), bf16),
        ),
        near + tokens + saved + (out_w.reshape(wide), attended, weights, norm, grad_ff, ff_half),
        "v" * 2 + "h" * 14 + "vhhh",
        [pltpu.VMEM((span_len, width), f32)] * 2
        + [pltpu.VMEM((span_len, width), bf16)] * 2
        + [pltpu.VMEM((span_len, width), f32)] * 2
        + [
            pltpu.VMEM(wide, bf16),
            pltpu.VMEM(slim, bf16),
            pltpu.VMEM((group_len, width), bf16),
            pltpu.VMEM((span_len, width), bf16),
            pltpu.VMEM((group_len, q_cols), bf16),
            pltpu.VMEM((span_len, width), bf16),
            pltpu.VMEM((span_len, width), bf16),
            pltpu.VMEM((group_len, q_cols), bf16),
            pltpu.VMEM((group_len, q_cols), f32),
            pltpu.VMEM((2, group_len, 2 * HD), f32),
            pltpu.VMEM((group_len, 2 * HD), bf16),
            pltpu.VMEM((group_len, 2 * HD), bf16),
            pltpu.VMEM((group_len, qkv_cols), bf16),
            pltpu.VMEM((line, span_len, width), bf16),
        ]
        + [pltpu.VMEM(value.shape, value.dtype) for value in saved]
        + [pltpu.VMEM((line - 1, span_len, width), bf16)]
        + sum_space(line - 2, rows_each, grad_ff.shape[5])
        + out_space
        + qkv_space,
        vmem=63,
    )


def general_body(
    tokens,
    attn_gain,
    w_query,
    w_key,
    w_value,
    w_out,
    mlp_gain,
    w_gate,
    w_up,
    w_down,
    keep_mask,
    group_ids,
    positions,
    exit_scale,
    out_grad,
):
    seq_count, span_len, model_width = tokens.shape
    kv_heads = KVH
    head_dim = HD
    head_count = HEADS
    group_size = head_count // kv_heads
    row_count = seq_count * span_len
    stripe = group_size * span_len
    wide_count = lax.axis_size("wide")
    wide_place = lax.axis_index("wide")
    full_len = span_len * wide_count
    score_scale = 1.0 / math.sqrt(head_dim)
    gain_one, query_w, key_w, value_w, out_w = (
        lax.all_gather(attn_gain, ("wide", "narrow"), axis=0, tiled=True),
        lax.all_gather(w_query, ("wide", "narrow"), axis=0, tiled=True),
        lax.all_gather(w_key, ("wide", "narrow"), axis=0, tiled=True),
        lax.all_gather(w_value, ("wide", "narrow"), axis=0, tiled=True),
        lax.all_gather(w_out, ("wide", "narrow"), axis=0, tiled=True),
    )
    inputs = tokens.astype(jnp.float32).reshape(row_count, model_width)
    token_pos = positions.reshape(row_count)
    keep_rows = jnp.repeat(keep_mask.astype(jnp.float32), span_len)[:, None]
    inverse_one = lax.rsqrt(jnp.mean(inputs * inputs, axis=-1, keepdims=True) + epsilon)
    first_norm = (inputs * inverse_one * gain_one.astype(jnp.float32)).astype(jnp.bfloat16)
    query_pre = jnp.dot(first_norm, query_w, preferred_element_type=jnp.float32).reshape(
        row_count, head_count, head_dim
    )
    key_pre = jnp.dot(first_norm, key_w, preferred_element_type=jnp.float32).reshape(
        row_count, kv_heads, head_dim
    )
    query_rows = rotate(query_pre, token_pos, 1.0).astype(jnp.bfloat16)
    key_heads = (
        rotate(key_pre, token_pos, 1.0)
        .astype(jnp.bfloat16)
        .reshape(seq_count, span_len, kv_heads * head_dim)
    )
    value_heads = (
        jnp.dot(first_norm, value_w, preferred_element_type=jnp.float32)
        .astype(jnp.bfloat16)
        .reshape(seq_count, span_len, kv_heads * head_dim)
    )
    queries = (
        query_rows.reshape(seq_count, span_len, kv_heads, group_size, head_dim)
        .transpose(0, 2, 3, 1, 4)
        .reshape(seq_count, kv_heads, stripe, head_dim)
    )
    query_index = wide_place * span_len + jnp.arange(stripe, dtype=jnp.int32) % span_len
    last_query = wide_place * span_len + span_len - 1

    def block_scores(key_block, key_first):
        scores = (
            jnp.einsum("skrd,sjkd->skrj", queries, key_block, preferred_element_type=jnp.float32)
            * score_scale
        )
        key_index = key_first + jnp.arange(key_block.shape[1], dtype=jnp.int32)
        allowed = key_index[None, :] <= query_index[:, None]
        return (scores, allowed)

    start_forward = (
        jnp.full((seq_count, kv_heads, stripe), -1e30, jnp.float32),
        jnp.zeros((seq_count, kv_heads, stripe), jnp.float32),
        jnp.zeros((seq_count, kv_heads, stripe, head_dim), jnp.float32),
    )
    running = start_forward
    pieces = (
        lax.all_gather(key_heads, "wide", axis=1, tiled=True),
        lax.all_gather(value_heads, "wide", axis=1, tiled=True),
    )
    key_blocks = split_blocks(pieces[0], seq_count, kv_heads, head_dim)
    value_blocks = split_blocks(pieces[1], seq_count, kv_heads, head_dim)
    block_len = key_blocks.shape[2]

    def advance(carried, block_item):
        key_block, value_block, block_index = block_item
        key_first = block_index * block_len

        def compute_block(current):
            run_max, run_sum, run_acc = current
            scores, allowed = block_scores(key_block, key_first)
            scores = jnp.where(allowed, scores, -1e30)
            new_max = jnp.maximum(run_max, jnp.max(scores, axis=-1))
            factor = jnp.exp(run_max - new_max)
            weights = jnp.where(allowed, jnp.exp(scores - new_max[..., None]), 0.0)
            new_sum = run_sum * factor + jnp.sum(weights, axis=-1)
            new_acc = run_acc * factor[..., None] + jnp.einsum(
                "skrj,sjkd->skrd",
                weights.astype(jnp.bfloat16),
                value_block,
                preferred_element_type=jnp.float32,
            )
            return (new_max, new_sum, new_acc)

        return (lax.cond(key_first <= last_query, compute_block, unchanged, carried), None)

    running, _ = lax.scan(
        advance,
        running,
        (key_blocks, value_blocks, jnp.arange(key_blocks.shape[0], dtype=jnp.int32)),
    )
    run_max, run_sum, run_acc = running
    attended = run_acc / run_sum[..., None]
    log_total = run_max + jnp.log(run_sum)
    attended_rows = (
        attended.reshape(seq_count, kv_heads, group_size, span_len, head_dim)
        .transpose(0, 3, 1, 2, 4)
        .reshape(row_count, head_count * head_dim)
        .astype(jnp.bfloat16)
    )
    middle = inputs + keep_rows * jnp.dot(attended_rows, out_w, preferred_element_type=jnp.float32)
    gain_two, gate_w, up_w, down_w = (
        lax.all_gather(mlp_gain, ("wide", "narrow"), axis=0, tiled=True),
        lax.all_gather(w_gate, ("wide", "narrow"), axis=0, tiled=True),
        lax.all_gather(w_up, ("wide", "narrow"), axis=0, tiled=True),
        lax.all_gather(w_down, ("wide", "narrow"), axis=0, tiled=True),
    )
    inverse_two = lax.rsqrt(jnp.mean(middle * middle, axis=-1, keepdims=True) + epsilon)
    second_norm = (middle * inverse_two * gain_two.astype(jnp.float32)).astype(jnp.bfloat16)
    gate_value = jnp.dot(second_norm, gate_w, preferred_element_type=jnp.float32)
    up_value = jnp.dot(second_norm, up_w, preferred_element_type=jnp.float32)
    gate_sigmoid = jax.nn.sigmoid(gate_value)
    swish_value = gate_value * gate_sigmoid
    hidden = (swish_value * up_value).astype(jnp.bfloat16)
    output = (
        middle + keep_rows * jnp.dot(hidden, down_w, preferred_element_type=jnp.float32)
    ).astype(jnp.bfloat16)
    group_match = (
        group_ids.reshape(row_count)[:, None]
        == jnp.arange(exit_scale.shape[0], dtype=jnp.int32)[None, :]
    )
    token_scale = jnp.sum(jnp.where(group_match, exit_scale[None, :], 0.0), axis=1, keepdims=True)
    upstream = out_grad.astype(jnp.float32).reshape(row_count, model_width) * token_scale
    gain_two, gate_w, up_w, down_w = (
        lax.all_gather(mlp_gain, ("wide", "narrow"), axis=0, tiled=True),
        lax.all_gather(w_gate, ("wide", "narrow"), axis=0, tiled=True),
        lax.all_gather(w_up, ("wide", "narrow"), axis=0, tiled=True),
        lax.all_gather(w_down, ("wide", "narrow"), axis=0, tiled=True),
    )
    mixed_grad = (keep_rows * upstream).astype(jnp.bfloat16)
    grad_down = over_rows(hidden, mixed_grad)
    hidden_grad = against(mixed_grad, down_w)
    gate_grad = (
        hidden_grad * up_value * gate_sigmoid * (1.0 + gate_value * (1.0 - gate_sigmoid))
    ).astype(jnp.bfloat16)
    up_grad = (hidden_grad * swish_value).astype(jnp.bfloat16)
    grad_gate = over_rows(second_norm, gate_grad)
    grad_up = over_rows(second_norm, up_grad)
    norm_grad = against(gate_grad, gate_w) + against(up_grad, up_w)
    grad_gain_two = jnp.sum(norm_grad * middle * inverse_two, axis=0)
    scaled_two = gain_two.astype(jnp.float32) * norm_grad
    middle_grad = (
        upstream
        + inverse_two * scaled_two
        - middle
        * (inverse_two * inverse_two * inverse_two)
        * jnp.mean(scaled_two * middle, axis=-1, keepdims=True)
    )
    gain_two_share, gate_share, up_share, down_share = (
        lax.psum_scatter(grad_gain_two, ("wide", "narrow"), scatter_dimension=0, tiled=True),
        lax.psum_scatter(grad_gate, ("wide", "narrow"), scatter_dimension=0, tiled=True),
        lax.psum_scatter(grad_up, ("wide", "narrow"), scatter_dimension=0, tiled=True),
        lax.psum_scatter(grad_down, ("wide", "narrow"), scatter_dimension=0, tiled=True),
    )
    gain_one, query_w, key_w, value_w, out_w = (
        lax.all_gather(attn_gain, ("wide", "narrow"), axis=0, tiled=True),
        lax.all_gather(w_query, ("wide", "narrow"), axis=0, tiled=True),
        lax.all_gather(w_key, ("wide", "narrow"), axis=0, tiled=True),
        lax.all_gather(w_value, ("wide", "narrow"), axis=0, tiled=True),
        lax.all_gather(w_out, ("wide", "narrow"), axis=0, tiled=True),
    )
    branch_grad = (keep_rows * middle_grad).astype(jnp.bfloat16)
    grad_out = over_rows(attended_rows, branch_grad)
    attended_grad = against(branch_grad, out_w).astype(jnp.bfloat16)
    grouped_grad = (
        attended_grad.reshape(seq_count, span_len, kv_heads, group_size, head_dim)
        .transpose(0, 2, 3, 1, 4)
        .reshape(seq_count, kv_heads, stripe, head_dim)
    )
    row_delta = jnp.sum(grouped_grad.astype(jnp.float32) * attended, axis=-1)
    start_backward = (
        jnp.zeros((seq_count, kv_heads, stripe, head_dim), jnp.float32),
        jnp.zeros((seq_count, full_len, kv_heads * head_dim), jnp.float32),
        jnp.zeros((seq_count, full_len, kv_heads * head_dim), jnp.float32),
    )
    running = start_backward
    pieces = (
        lax.all_gather(key_heads, "wide", axis=1, tiled=True),
        lax.all_gather(value_heads, "wide", axis=1, tiled=True),
    )
    key_blocks = split_blocks(pieces[0], seq_count, kv_heads, head_dim)
    value_blocks = split_blocks(pieces[1], seq_count, kv_heads, head_dim)
    fold_block_len = key_blocks.shape[2]

    def advance(carried, block_item):
        key_block, value_block, block_index = block_item
        key_first = block_index * fold_block_len

        def compute_block(current):
            query_acc, key_acc, value_acc = current
            scores, allowed = block_scores(key_block, key_first)
            probabilities = jnp.where(allowed, jnp.exp(scores - log_total[..., None]), 0.0)
            value_part = jnp.einsum(
                "skrj,skrd->sjkd",
                probabilities.astype(jnp.bfloat16),
                grouped_grad,
                preferred_element_type=jnp.float32,
            )
            prob_grad = jnp.einsum(
                "skrd,sjkd->skrj", grouped_grad, value_block, preferred_element_type=jnp.float32
            )
            score_grad = (probabilities * (prob_grad - row_delta[..., None])).astype(jnp.bfloat16)
            query_acc = (
                query_acc
                + jnp.einsum(
                    "skrj,sjkd->skrd", score_grad, key_block, preferred_element_type=jnp.float32
                )
                * score_scale
            )
            key_part = (
                jnp.einsum(
                    "skrj,skrd->sjkd", score_grad, queries, preferred_element_type=jnp.float32
                )
                * score_scale
            )
            key_acc = add_rows(
                key_acc, key_part.reshape(seq_count, fold_block_len, kv_heads * head_dim), key_first
            )
            value_acc = add_rows(
                value_acc,
                value_part.reshape(seq_count, fold_block_len, kv_heads * head_dim),
                key_first,
            )
            return (query_acc, key_acc, value_acc)

        return (lax.cond(key_first <= last_query, compute_block, unchanged, carried), None)

    running, _ = lax.scan(
        advance,
        running,
        (key_blocks, value_blocks, jnp.arange(key_blocks.shape[0], dtype=jnp.int32)),
    )
    query_acc, key_acc, value_acc = running
    key_sum, value_sum = (
        lax.psum_scatter(
            key_acc.astype(jnp.bfloat16), "wide", scatter_dimension=1, tiled=True
        ).astype(jnp.float32),
        lax.psum_scatter(
            value_acc.astype(jnp.bfloat16), "wide", scatter_dimension=1, tiled=True
        ).astype(jnp.float32),
    )
    query_back = (
        query_acc.reshape(seq_count, kv_heads, group_size, span_len, head_dim)
        .transpose(0, 3, 1, 2, 4)
        .reshape(row_count, head_count, head_dim)
    )
    query_grad = (
        rotate(query_back, token_pos, -1.0)
        .reshape(row_count, head_count * head_dim)
        .astype(jnp.bfloat16)
    )
    key_grad = (
        rotate(key_sum.reshape(row_count, kv_heads, head_dim), token_pos, -1.0)
        .reshape(row_count, kv_heads * head_dim)
        .astype(jnp.bfloat16)
    )
    value_grad = value_sum.reshape(row_count, kv_heads * head_dim).astype(jnp.bfloat16)
    grad_query = over_rows(first_norm, query_grad)
    grad_key = over_rows(first_norm, key_grad)
    grad_value = over_rows(first_norm, value_grad)
    input_norm_grad = (
        against(query_grad, query_w) + against(key_grad, key_w) + against(value_grad, value_w)
    )
    grad_gain_one = jnp.sum(input_norm_grad * inputs * inverse_one, axis=0)
    scaled_one = gain_one.astype(jnp.float32) * input_norm_grad
    input_grad = (
        middle_grad
        + inverse_one * scaled_one
        - inputs
        * (inverse_one * inverse_one * inverse_one)
        * jnp.mean(scaled_one * inputs, axis=-1, keepdims=True)
    )
    gain_one_share, query_share, key_share, value_share, out_share = (
        lax.psum_scatter(grad_gain_one, ("wide", "narrow"), scatter_dimension=0, tiled=True),
        lax.psum_scatter(grad_query, ("wide", "narrow"), scatter_dimension=0, tiled=True),
        lax.psum_scatter(grad_key, ("wide", "narrow"), scatter_dimension=0, tiled=True),
        lax.psum_scatter(grad_value, ("wide", "narrow"), scatter_dimension=0, tiled=True),
        lax.psum_scatter(grad_out, ("wide", "narrow"), scatter_dimension=0, tiled=True),
    )
    return (
        output.reshape(seq_count, span_len, model_width),
        input_grad.astype(jnp.bfloat16).reshape(seq_count, span_len, model_width),
        gain_one_share,
        query_share,
        key_share,
        value_share,
        out_share,
        gain_two_share,
        gate_share,
        up_share,
        down_share,
    )


def line_body(
    tokens,
    attn_gain,
    w_query,
    w_key,
    w_value,
    w_out,
    mlp_gain,
    w_gate,
    w_up,
    w_down,
    keep_mask,
    group_ids,
    positions,
    exit_scale,
    out_grad,
):
    f32 = jnp.float32
    bf16 = jnp.bfloat16
    _, span_len, model_width = tokens.shape
    line = lax.axis_size("z")
    rows_each = w_query.shape[0]
    q_cols = HEADS // line * HD

    group_match = group_ids[0][:, None] == jnp.arange(exit_scale.shape[0], dtype=jnp.int32)[None, :]
    token_scale = jnp.sum(jnp.where(group_match, exit_scale[None, :], 0.0), axis=1)
    freqs = 10000.0 ** (-2.0 * jnp.arange(HD // 2, dtype=f32) / HD)
    small = jnp.stack(
        [
            positions[0].astype(f32),
            token_scale,
            jnp.concatenate([freqs, freqs]),
            jnp.broadcast_to(keep_mask.astype(f32), (span_len,)),
        ]
    )
    small = jnp.broadcast_to(small[:, None], (4, 8, span_len))

    gain_row = jnp.concatenate([attn_gain, attn_gain, mlp_gain, mlp_gain])
    gain_row = jnp.pad(gain_row, (0, q_cols + 2 * HD - gain_row.shape[0]))
    gain_rows = jnp.broadcast_to(gain_row, (16, gain_row.shape[0]))
    (
        x_blocks,
        near_w,
        gain_all,
        first_norm,
        queries,
        both_kv,
        log_total,
        turns,
        attended_rows,
        ff_w,
        out_w,
        own_mixed,
    ) = forward_call(
        small,
        tokens[0],
        out_grad[0],
        gain_rows,
        (w_query, w_key, w_value, w_gate, w_up, w_out),
        line,
    )
    middle, norm_grad, output, grad_down, grad_ff, ff_half = mlp_call(
        small,
        gain_all,
        own_mixed,
        x_blocks,
        attended_rows,
        out_w,
        ff_w,
        w_down,
        line,
    )
    grad_down = grad_down.astype(f32)
    token_grad, ff_back, out_back, qkv_back = backward_call(
        (small, gain_all, middle, norm_grad),
        (tokens[0], out_grad[0]),
        (queries, both_kv, log_total, turns),
        out_w,
        attended_rows,
        near_w,
        first_norm,
        grad_ff,
        ff_half,
        line,
    )
    ff_back = ff_back.astype(f32)
    qkv_back = qkv_back.astype(f32)
    grad_out = jnp.sum(out_back.astype(f32), axis=0)
    heads_end, keys_end = w_query.shape[1], w_query.shape[1] + w_key.shape[1]
    grad_query = qkv_back[:, :heads_end]
    grad_key = qkv_back[:, heads_end:keys_end]
    grad_value = qkv_back[:, keys_end:]
    grad_gate = ff_back[:, : w_gate.shape[1]]
    grad_up = ff_back[:, w_gate.shape[1] :]

    def gain_grad(pairs, gain):
        total = sum(jnp.sum(weight.astype(f32) * grad, axis=1) for weight, grad in pairs)
        return total / gain.astype(f32)

    return (
        output[None],
        token_grad[None],
        gain_grad([(w_query, grad_query), (w_key, grad_key), (w_value, grad_value)], attn_gain),
        grad_query,
        grad_key,
        grad_value,
        grad_out,
        gain_grad([(w_gate, grad_gate), (w_up, grad_up)], mlp_gain),
        grad_gate,
        grad_up,
        grad_down,
    )


def solution(mesh):
    wide, narrow = mesh.shape["wide"], mesh.shape["narrow"]
    if wide == 2 * KVH and narrow == 4:
        mesh = Mesh(mesh.devices.reshape(wide // 2, 2, 2, 2), ("z", "x", "y", "c"))
        body, wide, narrow = line_body, ("z", "x"), ("y", "c")
    else:
        body, wide, narrow = general_body, ("wide",), ("narrow",)
    token_spec = P(narrow, wide, None)
    id_spec = P(narrow, wide)
    gain_spec = P(wide + narrow)
    weight_spec = P(wide + narrow, None)
    return jax.shard_map(
        body,
        mesh=mesh,
        in_specs=(
            token_spec,
            gain_spec,
            weight_spec,
            weight_spec,
            weight_spec,
            weight_spec,
            gain_spec,
            weight_spec,
            weight_spec,
            weight_spec,
            P(narrow),
            id_spec,
            id_spec,
            P(),
            token_spec,
        ),
        out_specs=(
            token_spec,
            token_spec,
            gain_spec,
            weight_spec,
            weight_spec,
            weight_spec,
            weight_spec,
            gain_spec,
            weight_spec,
            weight_spec,
            weight_spec,
        ),
        check_vma=False,
    )
```

```python
import functools
import math

import jax
import jax.numpy as jnp
from jax import lax
from jax.experimental import pallas as pl
from jax.experimental.pallas import tpu as pltpu
from jax.sharding import Mesh
from jax.sharding import PartitionSpec as P

HEADS = 16
KVH = 4
HD = 128


epsilon = 1e-05


def rotate(vectors, token_pos, direction):
    half_size = vectors.shape[-1] // 2
    freqs = 10000.0 ** (-2.0 * jnp.arange(half_size, dtype=jnp.float32) / vectors.shape[-1])
    angles = token_pos.astype(jnp.float32)[:, None] * freqs[None, :]
    cosine = jnp.cos(angles)[:, None, :]
    sine = direction * jnp.sin(angles)[:, None, :]
    first_half = vectors[..., :half_size]
    second_half = vectors[..., half_size:]
    return jnp.concatenate(
        [first_half * cosine - second_half * sine, second_half * cosine + first_half * sine],
        axis=-1,
    )


def split_blocks(piece_arr, seq_count, kv_heads, head_dim):
    piece_len = piece_arr.shape[1]
    block_len = math.gcd(piece_len, 512)
    shaped = piece_arr.reshape(seq_count, piece_len // block_len, block_len, kv_heads, head_dim)
    return shaped.transpose(1, 0, 2, 3, 4)


def add_rows(whole_arr, update, first_row):
    current = lax.dynamic_slice_in_dim(whole_arr, first_row, update.shape[1], 1)
    return lax.dynamic_update_slice_in_dim(whole_arr, current + update, first_row, 1)


def over_rows(left, right):
    return lax.dot_general(
        left, right, (((0,), (0,)), ((), ())), preferred_element_type=jnp.float32
    )


def against(left, right):
    return lax.dot_general(
        left, right, (((1,), (1,)), ((), ())), preferred_element_type=jnp.float32
    )


def unchanged(carried):
    return carried


MESH = pl.DeviceIdType.MESH
AXES = ("z", "x", "y", "c")


def only(when, act):
    if when is None:
        act()
    else:
        pl.when(when)(act)


class Links:
    def __init__(self, send_sems, recv_sems, line):
        self.send_sems, self.recv_sems, self.line = send_sems, recv_sems, line
        self.z, self.x, self.y, self.c = (lax.axis_index(name) for name in AXES)
        self.slot = self.x * 4 + self.y * 2 + self.c
        self.used = 0
        self.sent = []

    def device(self, to):
        if to == "x":
            return (self.z, 1 - self.x, self.y, self.c)
        if to == "y":
            return (self.z, self.x, 1 - self.y, self.c)
        if to == "c":
            return (self.z, self.x, self.y, 1 - self.c)
        return (self.along(to), self.x, self.y, self.c)

    def along(self, step):
        return lax.rem(self.z + step + self.line, self.line)

    def other(self, to):
        slot = self.slot
        for name in to:
            bit = {"x": 4, "y": 2, "c": 1}[name]
            here = {"x": self.x, "y": self.y, "c": self.c}[name]
            slot = slot + bit * (1 - 2 * here)
        return slot

    def meet(self, targets):
        barrier = pltpu.get_barrier_semaphore()
        for to in targets:
            pl.semaphore_signal(barrier, inc=1, device_id=self.device(to), device_id_type=MESH)
        pl.semaphore_wait(barrier, len(targets))

    def send(self, source, target, to, when=None):
        copy = pltpu.make_async_remote_copy(
            src_ref=source,
            dst_ref=target,
            send_sem=self.send_sems.at[self.used],
            recv_sem=self.recv_sems.at[self.used],
            device_id=self.device(to),
            device_id_type=MESH,
        )
        only(when, copy.start)
        self.used += 1
        self.sent.append((copy, when))
        return copy

    def keep(self, source, target):
        copy = pltpu.make_async_copy(source, target, self.send_sems.at[self.used])
        copy.start()
        self.used += 1
        return copy

    def finish(self):
        for copy, when in self.sent:
            only(when, copy.wait_send)


class NearGather:
    def __init__(self, links, slot):
        self.links, self.slot = links, slot
        self.got = {}

    def offer(self, block, source):
        target = self.slot(block, self.links.slot)
        for to in ("x", "y", "c"):
            self.got[block, to] = self.links.send(source, target, to)

    def relay(self, block, first):
        links = self.links
        for to, then in (("x", "y"), ("y", "x")):
            self.got[block, to].wait_recv()
            place = self.slot(block, links.other(to))
            self.got[block, to + "c"] = links.send(place, place, "c")
            if to == first:
                self.got[block, "xy"] = links.send(place, place, then)

    def close(self, block):
        self.got[block, "xy"].wait_recv()
        place = self.slot(block, self.links.other("xy"))
        self.got[block, "xyc"] = self.links.send(place, place, "c")

    def wait(self, blocks):
        for block in blocks:
            for to in ("c", "xc", "yc", "xyc"):
                self.got[block, to].wait_recv()


class LineGather:
    def __init__(self, links, rows, origin, place, pieces=2):
        self.links, self.origin, self.place = links, origin, place
        self.pieces, self.rows = pieces, rows // pieces
        self.last = {}

    def inside(self, block):
        return jnp.logical_and(block >= 0, block < self.links.line)

    def step(self, number):
        z = self.links.z
        for piece in range(self.pieces):
            for way in (1, -1):
                held = self.inside(z - way * number)
                if number > 0:
                    only(held, self.last[piece, way].wait_recv)
                if number == self.links.line - 1:
                    continue
                rows = pl.ds(piece * self.rows, self.rows)
                place = self.place(self.links.along(-way * number), rows)
                source = self.origin(rows) if number == 0 else place
                when = jnp.logical_and(held, self.inside(z + way))
                self.last[piece, way] = self.links.send(source, place, way, when)


class RingGather:
    def __init__(self, links, rows, origin, place, pieces=4):
        self.links, self.origin, self.place = links, origin, place
        self.pieces, self.rows = pieces, rows // pieces
        self.last = [None] * pieces

    def step(self, number):
        if number > 0:
            for copy in self.last:
                copy.wait_recv()
        if number == self.links.line - 1:
            return
        for piece in range(self.pieces):
            way = 1 if piece < self.pieces // 2 else -1
            rows = pl.ds(piece * self.rows, self.rows)
            block = self.links.along(-way * number)
            place = self.place(block, rows)
            source = self.origin(rows) if number == 0 else place
            self.last[piece] = self.links.send(source, place, way)


def column_of(row):
    size = row.shape[1]
    down = lax.broadcasted_iota(jnp.int32, (size, size), 0)
    across = lax.broadcasted_iota(jnp.int32, (size, size), 1)
    values = jnp.where(down == across, jnp.broadcast_to(row, (size, size)), 0.0)
    return jnp.sum(values, axis=1, keepdims=True)


def first_kernel(
    line,
    small_ref,
    x_ref,
    grad_ref,
    gain_rows_ref,
    query_w_ref,
    key_w_ref,
    value_w_ref,
    gate_w_ref,
    up_w_ref,
    out_ref,
    xs_ref,
    weight_ref,
    gain_ref,
    norm_ref,
    query_ref,
    kv_ref,
    peak_ref,
    turn_ref,
    atts_ref,
    ffs_ref,
    outs_ref,
    mix_ref,
    x_all,
    grad,
    mix,
    places,
    weights,
    gains,
    norm,
    turns,
    flat,
    query,
    kv,
    peak,
    att,
    send_sems,
    recv_sems,
):
    f32, bf16 = jnp.float32, jnp.bfloat16
    links = Links(send_sems, recv_sems, line)
    far = [1, line - 1] + list(range(2, line - 1))
    here = links.slot
    span_len, width = x_ref.shape
    group_len = line * span_len
    rows_each = gate_w_ref.shape[0]
    q_cols = query.shape[1]
    ff_cols = gate_w_ref.shape[1] // line
    heads = q_cols // HD
    local = []

    near = NearGather(links, lambda block, place: weights.at[links.along(-block), place])
    far_ff = NearGather(links, lambda block, place: ffs_ref.at[links.along(-block), place])
    out_half = out_ref.shape[0] // 2

    def out_part(block, place):
        k, part = block
        rows = pl.ds(part * out_half, out_half)
        return outs_ref.at[links.along(k if part else -k), place, rows]

    far_out = NearGather(links, out_part)
    ring = LineGather(
        links, span_len, lambda rows: x_ref.at[rows], lambda block, rows: x_all.at[block, rows]
    )
    place_ref = small_ref.at[0]

    def columns(weight, block, size):
        return weight.at[:, pl.ds(pl.multiple_of(block * size, HD), size)]

    def near_pieces(block):
        target = weights.at[links.z, here]
        rows = pl.ds(0, rows_each)
        return [
            (columns(query_w_ref, block, q_cols), target.at[rows, pl.ds(0, q_cols)]),
            (columns(key_w_ref, block, HD), target.at[rows, pl.ds(q_cols, HD)]),
            (columns(value_w_ref, block, HD), target.at[rows, pl.ds(q_cols + HD, HD)]),
            (gain_rows_ref, target.at[pl.ds(rows_each, 16)]),
        ]

    def ff_pieces(block):
        target = ffs_ref.at[links.z, here]
        return [
            (columns(gate_w_ref, block, ff_cols), target.at[:, pl.ds(0, ff_cols)]),
            (columns(up_w_ref, block, ff_cols), target.at[:, pl.ds(ff_cols, ff_cols)]),
        ]

    def turn_out(pieces):
        return {k: [links.send(*piece, k) for piece in pieces(links.along(k))] for k in far}

    def arrived(copies):
        for copy in copies:
            copy.wait_recv()

    own = [links.keep(*piece) for piece in near_pieces(links.z)]
    own_ff = [links.keep(*piece) for piece in ff_pieces(links.z)]
    own_tokens = [
        links.keep(x_ref, x_all.at[links.z]),
        links.keep(place_ref, places.at[links.z]),
        links.keep(grad_ref, grad),
    ]
    links.meet(["x", "y", "c"] + far)
    turned = turn_out(near_pieces)
    placed = [links.send(place_ref, places.at[links.z], k) for k in far]
    turned_ff = turn_out(ff_pieces)
    for copy in own:
        copy.wait()
    near.offer(0, weights.at[links.z, here])
    for copy in own_ff:
        copy.wait()
    far_ff.offer(0, ffs_ref.at[links.z, here])
    own = own_tokens
    local.append(links.keep(out_ref, outs_ref.at[links.z, here]))

    def move_out(k):
        for part in range(2):
            if k == 0:
                block = out_ref.at[pl.ds(part * out_half, out_half)]
            else:
                moved[part].wait_recv()
                block = out_part((k, part), here)
            if k < line - 1:
                moved[part] = links.send(block, out_part((0, part), here) if k == 0 else block, 1 - 2 * part)
            far_out.offer((k, part), block)

    def relay_out(k):
        for part in range(2):
            far_out.relay((k, part), "xy"[part])

    def close_out(k):
        for part in range(2):
            far_out.close((k, part))

    moved = [None, None]
    for k in far:
        arrived(turned[k])
        near.offer(k, weights.at[links.along(-k), here])
    ring.step(0)
    for k in [0] + far:
        near.relay(k, "x" if k < line // 2 else "y")
    for k in far:
        arrived(turned_ff[k])
        far_ff.offer(k, ffs_ref.at[links.along(-k), here])
    ring.step(1)
    for k in [0] + far:
        near.close(k)
    far_ff.relay(0, "x")
    ring.step(2)
    move_out(0)
    for copy in own:
        copy.wait()
    for copy in placed:
        copy.wait_recv()

    lane = lax.broadcasted_iota(jnp.int32, (span_len, HD), 1)
    for block in range(line):
        angles = column_of(places[block, 0:1]) * small_ref[2, 0:1]
        rows = slice(block * span_len, (block + 1) * span_len)
        sine = jnp.sin(angles)
        turns[0, rows] = jnp.cos(angles)
        turns[1, rows] = jnp.where(lane < HD // 2, -sine, sine)
    local.append(links.keep(turns, turn_ref))
    token_scale = column_of(small_ref[1, 0:1])
    for low in range(0, span_len, 16):
        rows = slice(low, low + 16)
        upstream = grad[rows].astype(f32) * token_scale[rows]
        mix[rows] = (upstream * small_ref[3, 0:1, 0:1]).astype(bf16)
    local.append(links.keep(mix, mix_ref))
    near.wait(range(line))
    for index in range(line * 4):
        z, q = divmod(index, 4)
        for which in range(2):
            lanes = slice(which * HD, (which + 1) * HD)
            both = [weights[z, 2 * q + c, rows_each : rows_each + 16, lanes].astype(f32) for c in range(2)]
            first = lax.broadcasted_iota(jnp.int32, both[0].shape, 1) < rows_each
            gains[which, :, index * HD : (index + 1) * HD] = jnp.where(first, both[0], both[1])
    local.append(links.keep(weights, weight_ref))
    local.append(links.keep(gains, gain_ref))
    far_ff.relay(far[0], "x")
    ring.step(3)
    local.append(links.keep(x_all, xs_ref))
    move_out(1)

    def normalise(index, carry):
        block = index // (span_len // 16)
        rows = pl.ds(pl.multiple_of(lax.rem(index, span_len // 16) * 16, 16), 16)
        values = x_all[block, rows].astype(f32)
        inverse = lax.rsqrt(jnp.mean(values * values, axis=-1, keepdims=True) + epsilon)
        target = pl.ds(pl.multiple_of(index * 16, 16), 16)
        norm[target] = (values * inverse * gains[0]).astype(bf16)
        return carry

    lax.fori_loop(0, group_len // 16, normalise, 0)
    local.append(links.keep(norm, norm_ref))

    def project(low, high):
        step = group_len // 2
        for part in range(2):
            rows = slice(part * step, (part + 1) * step)
            total = None
            for z in range(line):
                weight = weights[z, :, :rows_each, low:high].reshape(8 * rows_each, high - low)
                term = jnp.dot(
                    norm[rows, z * 8 * rows_each : (z + 1) * 8 * rows_each],
                    weight,
                    preferred_element_type=f32,
                )
                total = term if total is None else total + term
            flat[rows, low:high] = total

    def turn(values, rows):
        return values * turns[0, rows] + pltpu.roll(values, HD // 2, 1) * turns[1, rows]

    project(q_cols, q_cols + 2 * HD)
    for block in range(line):
        rows = slice(block * span_len, (block + 1) * span_len)
        kv[0, rows, :HD] = turn(flat[rows, q_cols : q_cols + HD], rows).astype(bf16)
        kv[0, rows, HD:] = flat[rows, q_cols + HD : q_cols + 2 * HD].astype(bf16)
    exchange = links.send(kv.at[0], kv.at[1], "x")
    project(0, q_cols)
    for block in range(line):
        rows = slice(block * span_len, (block + 1) * span_len)
        for head in range(heads):
            lanes = slice(head * HD, (head + 1) * HD)
            query[rows, lanes] = turn(flat[rows, lanes], rows).astype(bf16)
    local.append(links.keep(query, query_ref))
    for k in far[1:]:
        far_ff.relay(k, "x" if k < line // 2 else "y")
    relay_out(0)
    move_out(2)
    exchange.wait_recv()
    local.append(links.keep(kv, kv_ref))

    scale = 1.0 / math.sqrt(HD)
    peak[...] = jnp.zeros_like(peak)

    def attend(head, carry):
        lanes = pl.ds(pl.multiple_of(head * HD, HD), HD)
        for block in range(line):
            rows = slice(block * span_len, (block + 1) * span_len)
            reach = (block + 1) * span_len
            part = query[rows, lanes]
            row = lax.broadcasted_iota(jnp.int32, (span_len, reach), 0) + block * span_len
            column = lax.broadcasted_iota(jnp.int32, (span_len, reach), 1)
            allowed = (column <= row, column < (block + links.x) * span_len)
            scores = []
            for half in range(2):
                score = lax.dot_general(
                    part, kv[half, :reach, :HD], (((1,), (1,)), ((), ())), preferred_element_type=f32
                )
                scores.append(jnp.where(allowed[half], score * scale, -1e30))
            top = jnp.maximum(
                jnp.max(scores[0], axis=-1, keepdims=True), jnp.max(scores[1], axis=-1, keepdims=True)
            )
            total, mixed = None, None
            for half in range(2):
                weight = jnp.exp(scores[half] - top)
                count = jnp.sum(weight, axis=-1, keepdims=True)
                term = jnp.dot(weight.astype(bf16), kv[half, :reach, HD:], preferred_element_type=f32)
                total = count if total is None else total + count
                mixed = term if mixed is None else mixed + term
            att[rows, lanes] = (mixed / total).astype(bf16)
            spot = lax.broadcasted_iota(jnp.int32, (span_len, HD), 1) == head
            peak[rows] = jnp.where(spot, top + jnp.log(total), peak[rows])
        return carry

    lax.fori_loop(0, heads, attend, 0)
    local.append(links.keep(peak, peak_ref))

    def place(block, rows):
        return atts_ref.at[rows, pl.ds(pl.multiple_of(block * q_cols, q_cols), q_cols)]

    att_ring = LineGather(links, group_len, lambda rows: att.at[rows], place)
    local.append(links.keep(att, place(links.z, pl.ds(0, group_len))))
    att_ring.step(0)
    for k in [0] + far:
        far_ff.close(k)
    for k in range(3, line):
        move_out(k)
    relay_out(1)
    att_ring.step(1)
    relay_out(2)
    att_ring.step(2)
    for k in range(3, line):
        relay_out(k)
    for k in range(line):
        close_out(k)
    att_ring.step(3)
    far_out.wait([(k, part) for k in range(line) for part in range(2)])
    far_ff.wait(range(line))
    links.finish()
    for copy in local:
        copy.wait()


def add_rows_of(target, values, count):
    def add(index, carry):
        rows = pl.ds(pl.multiple_of(index * 16, 16), 16)
        target[rows] = target[rows] + values[rows]
        return carry

    lax.fori_loop(0, count // 16, add, 0)


class NearSum:
    def __init__(self, links, source, own, from_core, from_first, from_second, first, in_place=False):
        self.links, self.source, self.own, self.first = links, source, own, first
        self.in_place = in_place
        self.from_core, self.from_first, self.from_second = from_core, from_first, from_second

    def start(self):
        links = self.links
        if not self.in_place:
            self.local = links.keep(self.source(links.c), self.own)
        self.copy = links.send(self.source(1 - links.c), self.from_core, "c")

    def add(self, target, values):
        add_rows_of(target, values, target.shape[0])

    def core_done(self):
        links = self.links
        self.copy.wait_recv()
        if not self.in_place:
            self.local.wait()
        for x in range(2):
            for y in range(2):
                self.add(self.own.at[x, y], self.from_core.at[x, y])
        if self.first == "x":
            self.copy = links.send(self.own.at[1 - links.x], self.from_first, "x")
        else:
            self.copy = links.send(self.own.at[:, 1 - links.y], self.from_first, "y")

    def first_done(self):
        links = self.links
        self.copy.wait_recv()
        for other in range(2):
            place = (links.x, other) if self.first == "x" else (other, links.y)
            self.add(self.own.at[place], self.from_first.at[other])
        if self.first == "x":
            self.copy = links.send(self.own.at[links.x, 1 - links.y], self.from_second, "y")
        else:
            self.copy = links.send(self.own.at[1 - links.x, links.y], self.from_second, "x")

    def second_done(self):
        self.copy.wait_recv()
        total = self.own.at[self.links.x, self.links.y]
        self.add(total, self.from_second)
        return total


def sum_space(blocks, rows, columns):
    shape = (rows, columns)
    return [
        pltpu.VMEM((blocks, 2, 2) + shape, jnp.bfloat16),
        pltpu.VMEM((blocks, 2, 2) + shape, jnp.bfloat16),
        pltpu.VMEM((blocks, 2) + shape, jnp.bfloat16),
        pltpu.VMEM((blocks,) + shape, jnp.bfloat16),
    ]


class RingSum:
    def __init__(self, links, parts, total, got, pieces=4):
        self.links, self.parts, self.total, self.got = links, parts, total, got
        self.pieces, self.last = pieces, [None] * pieces
        self.rows = parts.shape[1] // pieces

    def step(self, number):
        links = self.links
        for piece in range(self.pieces):
            way = 1 if piece < self.pieces // 2 else -1
            block = links.along(-way * (number + 1))
            where = pl.ds(piece * self.rows, self.rows)
            if number == 0:
                source = self.parts.at[block, where]
            else:
                self.last[piece].wait_recv()
                total = self.got[number - 1, where].astype(jnp.float32) + self.parts[
                    block, where
                ].astype(jnp.float32)
                if number == links.line - 1:
                    self.total[where] = total
                    continue
                self.parts[block, where] = total.astype(self.parts.dtype)
                source = self.parts.at[block, where]
            self.last[piece] = links.send(source, self.got.at[number, where], way)


def link_call(kernel, collective_id, copies, shapes, arguments, spaces=None, scratch=(), vmem=16):
    any_space = pl.BlockSpec(memory_space=pl.ANY)
    near_space = pl.BlockSpec(memory_space=pltpu.VMEM)
    many = isinstance(shapes, tuple)
    if spaces is None:
        spaces = "h" * (len(arguments) + (len(shapes) if many else 1))
    specs = [near_space if space == "v" else any_space for space in spaces]
    return pl.pallas_call(
        kernel,
        out_shape=shapes,
        in_specs=specs[: len(arguments)],
        out_specs=tuple(specs[len(arguments) :]) if many else specs[-1],
        scratch_shapes=list(scratch)
        + [pltpu.SemaphoreType.DMA((copies,)), pltpu.SemaphoreType.DMA((copies,))],
        compiler_params=pltpu.CompilerParams(
            collective_id=collective_id, has_side_effects=True, vmem_limit_bytes=vmem * 2**20
        ),
    )(*arguments)


def forward_call(small, tokens, out_grad, gain_rows, weights, line):
    span_len, width = tokens.shape
    group_len = line * span_len
    rows_each, qkv_cols = weights[0].shape[0], gain_rows.shape[1]
    q_cols = qkv_cols - 2 * HD
    both_cols = 2 * weights[3].shape[1] // line
    f32, bf16 = jnp.float32, jnp.bfloat16
    near = (line, 8, rows_each + 16, qkv_cols)
    outs = (
        ((line, span_len, width), bf16),
        (near, bf16),
        ((2, 16, width), f32),
        ((group_len, width), bf16),
        ((group_len, q_cols), bf16),
        ((2, group_len, 2 * HD), bf16),
        ((group_len, HD), f32),
        ((2, group_len, HD), f32),
        ((group_len, line * q_cols), bf16),
        ((line, 8, rows_each, both_cols), bf16),
        ((line, 8, rows_each, width), bf16),
        ((span_len, width), bf16),
    )
    return link_call(
        functools.partial(first_kernel, line),
        0,
        256,
        tuple(jax.ShapeDtypeStruct(*out) for out in outs),
        (small, tokens, out_grad, gain_rows) + weights,
        "v" + "h" * 21,
        scratch=[
            pltpu.VMEM((line, span_len, width), bf16),
            pltpu.VMEM((span_len, width), bf16),
            pltpu.VMEM((span_len, width), bf16),
            pltpu.VMEM((line,) + small.shape[1:], f32),
            pltpu.VMEM(near, bf16),
            pltpu.VMEM((2, 16, width), f32),
            pltpu.VMEM((group_len, width), bf16),
            pltpu.VMEM((2, group_len, HD), f32),
            pltpu.VMEM((group_len, qkv_cols), f32),
            pltpu.VMEM((group_len, q_cols), bf16),
            pltpu.VMEM((2, group_len, 2 * HD), bf16),
            pltpu.VMEM((group_len, HD), f32),
            pltpu.VMEM((group_len, q_cols), bf16),
        ],
        vmem=63,
    )


def mlp_kernel(
    line,
    cuts,
    small_ref,
    gain_ref,
    mix_ref,
    xs_ref,
    atts_ref,
    out_ref,
    ff_ref,
    down_ref,
    middle_ref,
    total_ref,
    output_ref,
    sum_ref,
    grad_ff_ref,
    ff_half_ref,
    big,
    ff,
    down,
    norm,
    parts,
    mixed,
    gate_up,
    hidden,
    both_grad,
    got,
    mixed_parts,
    mixed_got,
    mixed_total,
    *scratch,
):
    f32, bf16 = jnp.float32, jnp.bfloat16
    space, (send_sems, recv_sems) = scratch[:-2], scratch[-2:]
    links = Links(send_sems, recv_sems, line)
    far = [1, line - 1] + list(range(2, line - 1))
    span_len, width = mix_ref.shape
    group_len = line * span_len
    ff_cols = hidden.shape[1]
    block_rows = width // line
    rows_each = block_rows // 8
    chunk = 2 * HD
    early = [
        links.keep(out_ref, big),
        links.keep(atts_ref, norm),
        links.keep(xs_ref, parts),
    ]
    links.meet(["x", "y", "c", 1, line - 1])
    mix_ring = RingGather(
        links, span_len, lambda rows: mix_ref.at[rows], lambda block, rows: mixed.at[block, rows]
    )
    mix_ring.step(0)
    stay = links.keep(mix_ref, mixed.at[links.z])
    late = [links.keep(ff_ref, ff)]
    down_rows = down_ref.shape[0]

    def down_place(block, place):
        low, high = cuts[block]
        return down.at[pl.ds(pl.multiple_of(place * down_rows + low, 16), high - low)]

    near = NearGather(links, down_place)
    for block, (low, high) in enumerate(cuts):
        rows = down_ref.at[pl.ds(low, high - low)]
        late.append(links.keep(rows, down_place(block, links.slot)))
        near.offer(block, rows)
    ring = RingSum(links, parts, total_ref, got)
    mixed_ring = RingSum(links, mixed_parts, mixed_total, mixed_got)
    items = []
    ff_items = []
    for index, k in enumerate(far[:2]):
        block = links.along(k)
        core, first, second = space[:3]
        ff_items.append(
            NearSum(
                links,
                lambda c, block=block: ff.at[block, :, :, c],
                ff.at[block, :, :, links.c],
                core.at[index],
                first.at[index],
                second.at[index],
                "xy"[index % 2],
                True,
            )
        )
    for index, (low, high) in enumerate(cuts):
        rows = pl.ds(low, high - low)
        core, first, second = space[3 * index + 3 : 3 * index + 6]
        items.append(
            NearSum(
                links,
                lambda c, rows=rows: big.at[:, :, c, rows],
                big.at[:, :, links.c, rows],
                core.at[0],
                first.at[0],
                second.at[0],
                "xy"[index % 2],
                True,
            )
        )
    for copy in early:
        copy.wait()

    half = group_len // 2
    out_rows = width // 8
    for part in range(2):
        low = part * half
        for column in range(4):
            lanes = slice(column * width // 4, (column + 1) * width // 4)
            value = None
            for k in range(8):
                term = jnp.dot(
                    norm[low : low + half, k * out_rows : (k + 1) * out_rows],
                    big[k // 4, k // 2 % 2, k % 2, :, lanes],
                    preferred_element_type=f32,
                )
                value = term if value is None else value + term
            gate_up[:half, lanes] = value * small_ref[3, 0:1, 0:1]

        def normalise(index, carry, low=low):
            block = (low // 16 + index) // (span_len // 16)
            rows = pl.ds(pl.multiple_of(index * 16, 16), 16)
            inside = pl.ds(pl.multiple_of(lax.rem(index, span_len // 16) * 16, 16), 16)
            values = parts[block, inside].astype(f32) + gate_up[rows, :width]
            gate_up[rows, :width] = values
            inverse = lax.rsqrt(jnp.mean(values * values, axis=-1, keepdims=True) + epsilon)
            target = pl.ds(pl.multiple_of(low + index * 16, 16), 16)
            norm[target] = (values * inverse * gain_ref[1]).astype(bf16)
            return carry

        lax.fori_loop(0, half // 16, normalise, 0)

        @pl.when(links.z // (line // 2) == part)
        def _():
            where = pl.multiple_of(lax.rem(links.z, line // 2) * span_len, span_len)
            middle_ref[...] = gate_up[pl.ds(where, span_len), :width]
        if part == 0:
            mix_ring.step(1)

    for block in range(2):
        near.relay(block, "xy"[block])
    for copy in late:
        copy.wait()

    def columns_of(lanes, size):
        return ff[:, :, :, :, :, lanes].reshape(width, size)

    def forward(low, size):
        gates, ups = pl.ds(low, size), pl.ds(low + ff_cols, size)
        gate = jnp.dot(norm[...], columns_of(gates, size), preferred_element_type=f32)
        gate_up[:, gates] = gate
        swish = gate * jax.nn.sigmoid(gate)
        up = jnp.dot(norm[...], columns_of(ups, size), preferred_element_type=f32)
        gate_up[:, ups] = up
        hidden[:, gates] = (swish * up).astype(bf16)

    def backward(low, size):
        gates, ups = pl.ds(low, size), pl.ds(low + ff_cols, size)
        grad = lax.dot_general(
            mixed[...].reshape(group_len, width),
            down[gates],
            (((1,), (1,)), ((), ())),
            preferred_element_type=f32,
        )
        gate, up = gate_up[:, gates], gate_up[:, ups]
        sigmoid = jax.nn.sigmoid(gate)
        both_grad[:, gates] = (grad * up * sigmoid * (1.0 + gate * (1.0 - sigmoid))).astype(bf16)
        both_grad[:, ups] = (grad * (gate * sigmoid)).astype(bf16)

    def over_chunks(work, extent):
        def one(index, carry):
            work(pl.multiple_of(index * chunk, chunk), chunk)
            return carry

        lax.fori_loop(0, extent // chunk, one, 0)
        if extent % chunk:
            work(extent // chunk * chunk, extent % chunk)

    over_chunks(forward, ff_cols)
    mix_ring.step(2)
    for block in range(2):
        near.close(block)
    near.wait(range(2))

    def mixed_part(low, size):
        lanes = pl.ds(low, size)
        value = jnp.dot(hidden[...], down[:, lanes], preferred_element_type=f32).astype(bf16)
        mixed_parts[:, :, lanes] = value.reshape(line, span_len, size)

    over_chunks(mixed_part, width)
    mixed_ring.step(0)
    stay.wait()
    mix_ring.step(3)
    hidden_rows = hidden[...].T

    def down_part(low, size):
        lanes = pl.ds(low, size)
        value = jnp.dot(
            hidden_rows,
            mixed[:, :, lanes].reshape(group_len, size),
            preferred_element_type=f32,
        ).astype(bf16)
        big[:, :, :, : cuts[-1][1], lanes] = value.reshape(2, 2, 2, cuts[-1][1], size)

    over_chunks(down_part, width)
    for item in items:
        item.start()
    over_chunks(backward, ff_cols)
    mixed_ring.step(1)
    for item in items:
        item.core_done()

    def norm_part(index, carry):
        size = 4 * rows_each
        weight = ff[index // 2, lax.rem(index, 2)].reshape(size, 2 * ff_cols)
        value = lax.dot_general(
            both_grad[...], weight, (((1,), (1,)), ((), ())), preferred_element_type=f32
        ).astype(bf16)
        lanes = pl.ds(pl.multiple_of(index * size, size), size)
        parts[:, :, lanes] = value.reshape(line, span_len, size)
        return carry

    lax.fori_loop(0, 2 * line, norm_part, 0)
    ring.step(0)

    def ff_block(block):
        norm_rows = norm[:, pl.ds(pl.multiple_of(block * block_rows, block_rows), block_rows)].T

        def ff_part(low, size):
            lanes = pl.ds(low, size)
            value = jnp.dot(norm_rows, both_grad[:, lanes], preferred_element_type=f32)
            ff[block, :, :, :, :, lanes] = value.astype(bf16).reshape(2, 2, 2, rows_each, size)

        over_chunks(ff_part, 2 * ff_cols)

    for item, k in zip(ff_items, far):
        ff_block(links.along(k))
        item.start()
    for item in items:
        item.first_done()
    ring.step(1)
    for item in ff_items:
        item.core_done()
    mixed_ring.step(2)
    sent = []
    for k in far[2:] + [0]:
        block = links.along(k)
        ff_block(block)
        sent.append(links.keep(ff.at[block], grad_ff_ref.at[block]))
    for item, (low, high) in zip(items, cuts):
        sum_ref[low:high] = item.second_done()[...]
    ring.step(2)
    for item in ff_items:
        item.first_done()
    mixed_ring.step(3)
    for low in range(0, span_len, 16):
        rows = slice(low, low + 16)
        output_ref[rows] = (middle_ref[rows] + small_ref[3, 0:1, 0:1] * mixed_total[rows]).astype(bf16)
    ring.step(3)
    for index, item in enumerate(ff_items):
        sent.append(links.keep(item.second_done(), ff_half_ref.at[index]))
    links.finish()
    for copy in sent:
        copy.wait()


def mlp_call(small, gains, mixed, x_blocks, attended, out_w, ff_w, w_down, line):
    f32, bf16 = jnp.float32, jnp.bfloat16
    span_len, width = mixed.shape
    group_len = line * span_len
    rows, both_cols, rows_each = w_down.shape[0], ff_w.shape[3], ff_w.shape[2]
    ff_rows = 8 * rows
    ff_w = ff_w.reshape(line, 2, 2, 2, rows_each, both_cols)
    half = (rows // 2 + 15) // 16 * 16
    cuts = ((0, half), (half, rows))
    blocks = (line, span_len, width)
    token = jax.ShapeDtypeStruct((span_len, width), f32)
    return link_call(
        functools.partial(mlp_kernel, line, cuts),
        2,
        112,
        (
            token,
            token,
            jax.ShapeDtypeStruct((span_len, width), bf16),
            jax.ShapeDtypeStruct((rows, width), bf16),
            jax.ShapeDtypeStruct(ff_w.shape, bf16),
            jax.ShapeDtypeStruct((2, rows_each, both_cols), bf16),
        ),
        (small, gains, mixed, x_blocks, attended, out_w.reshape(2, 2, 2, width // 8, width), ff_w, w_down),
        "vvhhhhhh" + "vvvvhh",
        [
            pltpu.VMEM((2, 2, 2, width // 8, width), bf16),
            pltpu.VMEM(ff_w.shape, bf16),
            pltpu.VMEM((ff_rows, width), bf16),
            pltpu.VMEM((group_len, width), bf16),
            pltpu.VMEM(blocks, bf16),
            pltpu.VMEM(blocks, bf16),
            pltpu.VMEM((group_len, both_cols), f32),
            pltpu.VMEM((group_len, ff_rows), bf16),
            pltpu.VMEM((group_len, both_cols), bf16),
            pltpu.VMEM((line - 1, span_len, width), bf16),
            pltpu.VMEM(blocks, bf16),
            pltpu.VMEM((line - 1, span_len, width), bf16),
            pltpu.VMEM((span_len, width), f32),
        ]
        + sum_space(2, rows_each, both_cols)[1:]
        + sum((sum_space(1, high - low, width)[1:] for low, high in cuts), []),
        vmem=63,
    )


def backward_kernel(
    line,
    small_ref,
    gain_ref,
    middle_hbm,
    norm_grad_hbm,
    x_ref,
    grad_ref,
    query_ref,
    kv_ref,
    peak_ref,
    turn_ref,
    out_ref,
    atts_ref,
    weight_ref,
    norm_ref,
    ff_ref,
    ff_half_ref,
    token_ref,
    ffs_ref,
    outs_ref,
    qkvs_ref,
    middle_ref,
    norm_grad_ref,
    x_own,
    grad_own,
    middle_grad,
    total,
    big,
    slim,
    norm,
    own_rows,
    own_columns,
    branch,
    own_grad,
    att_grad,
    query_back,
    kv_back,
    kv_out,
    kv_in,
    flat,
    parts,
    query,
    kv,
    peak,
    turns,
    *scratch,
):
    f32, bf16 = jnp.float32, jnp.bfloat16
    send_sems, recv_sems = scratch[-2:]
    got, sums = scratch[0], scratch[1:-2]
    links = Links(send_sems, recv_sems, line)
    far = [1, line - 1] + list(range(2, line - 1))
    order = far + [0]
    span_len, width = x_ref.shape
    group_len = line * span_len
    q_cols = query.shape[1]
    heads = q_cols // HD
    rows_z = width // line
    rows_each = rows_z // 8
    scale = 1.0 / math.sqrt(HD)

    def lanes_of(block):
        return pl.ds(pl.multiple_of(block * q_cols, q_cols), q_cols)

    here = pl.ds(pl.multiple_of(links.z * span_len, span_len), span_len)
    first_loads = [
        links.keep(grad_ref, grad_own),
        links.keep(middle_hbm, middle_ref),
        links.keep(norm_grad_hbm, norm_grad_ref),
    ]
    loads = [
        links.keep(out_ref, big),
        links.keep(atts_ref.at[here], own_rows),
        links.keep(atts_ref.at[:, lanes_of(links.z)], own_columns),
        links.keep(x_ref, x_own),
        links.keep(query_ref, query),
        links.keep(kv_ref, kv),
        links.keep(peak_ref, peak),
        links.keep(turn_ref, turns),
        links.keep(norm_ref, norm),
        links.keep(weight_ref.at[:, :, :, :, pl.ds(0, slim.shape[4])], slim),
    ]
    links.meet(["x", "y", "c"] + far)
    ring = RingSum(links, parts, total, got)

    def items_of(source, space, in_place, order=order):
        items = []
        for index, k in enumerate(order):
            block = links.along(k)
            own = source.at[block, :, :, links.c] if in_place else space[0].at[index]
            core, first, second = space[-3:]
            items.append(
                NearSum(
                    links,
                    lambda c, block=block: source.at[block, :, :, c],
                    own,
                    core.at[index],
                    first.at[index],
                    second.at[index],
                    "xy"[index % 2],
                    in_place,
                )
            )
        return items

    ff_order = order[2:]
    ff_items = items_of(ff_ref, sums[:4], False, ff_order)
    out_items = items_of(big, sums[4:7], True)
    qkv_items = items_of(slim, sums[7:], True)
    local, arrived = [], []
    ff_cols = ff_ref.shape[5] // 2
    ff_pieces = ((0, ff_cols), (ff_cols, ff_cols))
    qkv_pieces = ((0, q_cols), (q_cols, HD), (q_cols + HD, HD))

    def deliver(total, target, k, pieces):
        for low, size in pieces:
            if pieces == out_pieces:
                place = target.at[links.z]
            else:
                lanes = pl.multiple_of(line * low + links.z * size, HD)
                place = target.at[:, pl.ds(lanes, size)]
            part = total.at[:, pl.ds(low, size)]
            if k == 0:
                local.append(links.keep(part, place))
            else:
                arrived.append(links.send(part, place, k))

    out_pieces = ((0, width),)
    deliver(ff_half_ref.at[0], ffs_ref, order[0], ff_pieces)
    def turn(items, target, low, high, pieces, order=order):
        for item, k in list(zip(items, order))[low:high]:
            deliver(item.second_done(), target, k, pieces)

    def core_done(items, low, high):
        for item in items[low:high]:
            item.core_done()

    def first_done(items, low, high):
        for item in items[low:high]:
            item.first_done()

    half = line // 2
    for item in ff_items:
        item.start()

    for copy in first_loads:
        copy.wait()
    keep = small_ref[3, 0:1, 0:1]
    token_scale = column_of(small_ref[1, 0:1])

    def norm_back(values, grad, gain):
        inverse = lax.rsqrt(jnp.mean(values * values, axis=-1, keepdims=True) + epsilon)
        scaled = gain * grad
        return inverse * scaled - values * (inverse * inverse * inverse) * jnp.mean(
            scaled * values, axis=-1, keepdims=True
        )

    for low in range(0, span_len, 16):
        rows = slice(low, low + 16)
        upstream = grad_own[rows].astype(f32) * token_scale[rows]
        grad = upstream + norm_back(middle_ref[rows], norm_grad_ref[rows], gain_ref[1])
        middle_grad[rows] = grad
        branch[rows] = (grad * keep).astype(bf16)
    loads[0].wait()
    for z in range(line):
        weight = big[z].reshape(rows_z, width)
        own_grad[:, z * rows_z : (z + 1) * rows_z] = lax.dot_general(
            branch[...], weight, (((1,), (1,)), ((), ())), preferred_element_type=f32
        ).astype(bf16)
    turned = [links.send(own_grad.at[:, lanes_of(links.along(k))], att_grad.at[here], k) for k in far]
    stayed = links.keep(own_grad.at[:, lanes_of(links.z)], att_grad.at[here])
    for copy in loads[1:]:
        copy.wait()
    deliver(ff_half_ref.at[1], ffs_ref, order[1], ff_pieces)
    core_done(ff_items, 0, line)
    for z in range(line):
        for part in range(4):
            columns = slice(part * width // 4, (part + 1) * width // 4)
            grad = lax.dot_general(
                own_rows[:, z * rows_z : (z + 1) * rows_z],
                branch[:, columns],
                (((0,), (0,)), ((), ())),
                preferred_element_type=f32,
            )
            big[z, :, :, :, :, columns] = grad.astype(bf16).reshape(2, 2, 2, rows_each, width // 4)
    for item in out_items:
        item.start()
    kv_back[...] = jnp.zeros_like(kv_back)
    for copy in turned:
        copy.wait_recv()
    stayed.wait()

    def attend_back(side, head, carry):
        lanes = pl.ds(pl.multiple_of(head * HD, HD), HD)
        for block in range(line):
            rows = slice(block * span_len, (block + 1) * span_len)
            reach = (block + 1) * span_len
            part, grad = query[rows, lanes], att_grad[rows, lanes]
            row = lax.broadcasted_iota(jnp.int32, (span_len, reach), 0) + block * span_len
            column = lax.broadcasted_iota(jnp.int32, (span_len, reach), 1)
            allowed = column <= row if side == 0 else column < (block + links.x) * span_len
            spot = lax.broadcasted_iota(jnp.int32, (span_len, HD), 1) == head
            top = jnp.sum(jnp.where(spot, peak[rows], 0.0), axis=-1, keepdims=True)
            delta = jnp.sum(
                grad.astype(f32) * own_columns[rows, lanes].astype(f32), axis=-1, keepdims=True
            )
            keys, values = kv[side, :reach, :HD], kv[side, :reach, HD:]
            score = lax.dot_general(part, keys, (((1,), (1,)), ((), ())), preferred_element_type=f32)
            weight = jnp.where(allowed, jnp.exp(score * scale - top), 0.0)
            weight_grad = lax.dot_general(
                grad, values, (((1,), (1,)), ((), ())), preferred_element_type=f32
            )
            score_grad = (weight * (weight_grad - delta)).astype(bf16)
            back = jnp.dot(score_grad, keys, preferred_element_type=f32) * scale
            kv_back[side, :reach, :HD] += lax.dot_general(
                score_grad, part, (((0,), (0,)), ((), ())), preferred_element_type=f32
            )
            kv_back[side, :reach, HD:] += lax.dot_general(
                weight.astype(bf16), grad, (((0,), (0,)), ((), ())), preferred_element_type=f32
            )
            query_back[rows, lanes] = back if side == 1 else query_back[rows, lanes] + back
        return carry

    lax.fori_loop(0, heads, functools.partial(attend_back, 1), 0)
    kv_out[:, :HD] = (kv_back[1, :, :HD] * scale).astype(bf16)
    kv_out[:, HD:] = kv_back[1, :, HD:].astype(bf16)
    exchange = links.send(kv_out, kv_in, "x")
    lax.fori_loop(0, heads, functools.partial(attend_back, 0), 0)

    def turn_back(values, rows):
        return values * turns[0, rows] - pltpu.roll(values, HD // 2, 1) * turns[1, rows]

    for block in range(line):
        rows = slice(block * span_len, (block + 1) * span_len)
        for head in range(heads):
            lanes = slice(head * HD, (head + 1) * HD)
            flat[rows, lanes] = turn_back(query_back[rows, lanes], rows).astype(bf16)
    first_done(ff_items, 0, line)
    core_done(out_items, 0, half)
    exchange.wait_recv()
    for block in range(line):
        rows = slice(block * span_len, (block + 1) * span_len)
        key_grad = kv_back[0, rows, :HD] * scale + kv_in[rows, :HD].astype(f32)
        flat[rows, q_cols : q_cols + HD] = turn_back(key_grad, rows).astype(bf16)
        value_grad = kv_back[0, rows, HD:] + kv_in[rows, HD:].astype(f32)
        flat[rows, q_cols + HD :] = value_grad.astype(bf16)
    for z in range(line):
        weight = slim[z].reshape(rows_z, flat.shape[1])
        part = lax.dot_general(
            flat[...], weight, (((1,), (1,)), ((), ())), preferred_element_type=f32
        ).astype(bf16)
        for block in range(line):
            parts[block, :, z * rows_z : (z + 1) * rows_z] = part[
                block * span_len : (block + 1) * span_len
            ]
    ring.step(0)
    turn(ff_items, ffs_ref, 0, line, ff_pieces, ff_order)
    for z in range(line):
        grad = lax.dot_general(
            norm[:, z * rows_z : (z + 1) * rows_z],
            flat[...],
            (((0,), (0,)), ((), ())),
            preferred_element_type=f32,
        )
        slim[z] = grad.astype(bf16).reshape(2, 2, 2, rows_each, flat.shape[1])
    for item in qkv_items:
        item.start()
    core_done(out_items, half, line)
    first_done(out_items, 0, half)
    ring.step(1)
    core_done(qkv_items, 0, line)
    turn(out_items, outs_ref, 0, half, out_pieces)
    first_done(out_items, half, line)
    ring.step(2)
    first_done(qkv_items, 0, half)
    turn(out_items, outs_ref, half, line, out_pieces)
    first_done(qkv_items, half, line)
    ring.step(3)
    for low in range(0, span_len, 16):
        rows = slice(low, low + 16)
        grad = middle_grad[rows] + norm_back(x_own[rows].astype(f32), total[rows], gain_ref[0])
        token_ref[rows] = grad.astype(bf16)
    turn(qkv_items, qkvs_ref, 0, line, qkv_pieces)
    for copy in arrived:
        copy.wait_recv()
    links.finish()
    for copy in local:
        copy.wait()


def backward_call(near, tokens, saved, out_w, attended, weights, norm, grad_ff, ff_half, line):
    f32, bf16 = jnp.float32, jnp.bfloat16
    span_len, width = tokens[0].shape
    group_len = line * span_len
    query = saved[0]
    q_cols, rows_each, qkv_cols = query.shape[1], width // line // 8, weights.shape[3]
    weights = weights.reshape(line, 2, 2, 2, -1, qkv_cols)
    wide = (line, 2, 2, 2, rows_each, width)
    slim = (line, 2, 2, 2, rows_each, qkv_cols)
    out_space = sum_space(line, rows_each, width)[1:]
    qkv_space = sum_space(line, rows_each, qkv_cols)[1:]
    token = jax.ShapeDtypeStruct((span_len, width), bf16)
    return link_call(
        functools.partial(backward_kernel, line),
        4,
        160,
        (token,)
        + (
            jax.ShapeDtypeStruct((rows_each, line * grad_ff.shape[5]), bf16),
            jax.ShapeDtypeStruct((line, rows_each, width), bf16),
            jax.ShapeDtypeStruct((rows_each, line * qkv_cols), bf16),
        ),
        near + tokens + saved + (out_w.reshape(wide), attended, weights, norm, grad_ff, ff_half),
        "v" * 2 + "h" * 14 + "vhhh",
        [pltpu.VMEM((span_len, width), f32)] * 2
        + [pltpu.VMEM((span_len, width), bf16)] * 2
        + [pltpu.VMEM((span_len, width), f32)] * 2
        + [
            pltpu.VMEM(wide, bf16),
            pltpu.VMEM(slim, bf16),
            pltpu.VMEM((group_len, width), bf16),
            pltpu.VMEM((span_len, width), bf16),
            pltpu.VMEM((group_len, q_cols), bf16),
            pltpu.VMEM((span_len, width), bf16),
            pltpu.VMEM((span_len, width), bf16),
            pltpu.VMEM((group_len, q_cols), bf16),
            pltpu.VMEM((group_len, q_cols), f32),
            pltpu.VMEM((2, group_len, 2 * HD), f32),
            pltpu.VMEM((group_len, 2 * HD), bf16),
            pltpu.VMEM((group_len, 2 * HD), bf16),
            pltpu.VMEM((group_len, qkv_cols), bf16),
            pltpu.VMEM((line, span_len, width), bf16),
        ]
        + [pltpu.VMEM(value.shape, value.dtype) for value in saved]
        + [pltpu.VMEM((line - 1, span_len, width), bf16)]
        + sum_space(line - 2, rows_each, grad_ff.shape[5])
        + out_space
        + qkv_space,
        vmem=63,
    )


def general_body(
    tokens,
    attn_gain,
    w_query,
    w_key,
    w_value,
    w_out,
    mlp_gain,
    w_gate,
    w_up,
    w_down,
    keep_mask,
    group_ids,
    positions,
    exit_scale,
    out_grad,
):
    seq_count, span_len, model_width = tokens.shape
    kv_heads = KVH
    head_dim = HD
    head_count = HEADS
    group_size = head_count // kv_heads
    row_count = seq_count * span_len
    stripe = group_size * span_len
    wide_count = lax.axis_size("wide")
    wide_place = lax.axis_index("wide")
    full_len = span_len * wide_count
    score_scale = 1.0 / math.sqrt(head_dim)
    gain_one, query_w, key_w, value_w, out_w = (
        lax.all_gather(attn_gain, ("wide", "narrow"), axis=0, tiled=True),
        lax.all_gather(w_query, ("wide", "narrow"), axis=0, tiled=True),
        lax.all_gather(w_key, ("wide", "narrow"), axis=0, tiled=True),
        lax.all_gather(w_value, ("wide", "narrow"), axis=0, tiled=True),
        lax.all_gather(w_out, ("wide", "narrow"), axis=0, tiled=True),
    )
    inputs = tokens.astype(jnp.float32).reshape(row_count, model_width)
    token_pos = positions.reshape(row_count)
    keep_rows = jnp.repeat(keep_mask.astype(jnp.float32), span_len)[:, None]
    inverse_one = lax.rsqrt(jnp.mean(inputs * inputs, axis=-1, keepdims=True) + epsilon)
    first_norm = (inputs * inverse_one * gain_one.astype(jnp.float32)).astype(jnp.bfloat16)
    query_pre = jnp.dot(first_norm, query_w, preferred_element_type=jnp.float32).reshape(
        row_count, head_count, head_dim
    )
    key_pre = jnp.dot(first_norm, key_w, preferred_element_type=jnp.float32).reshape(
        row_count, kv_heads, head_dim
    )
    query_rows = rotate(query_pre, token_pos, 1.0).astype(jnp.bfloat16)
    key_heads = (
        rotate(key_pre, token_pos, 1.0)
        .astype(jnp.bfloat16)
        .reshape(seq_count, span_len, kv_heads * head_dim)
    )
    value_heads = (
        jnp.dot(first_norm, value_w, preferred_element_type=jnp.float32)
        .astype(jnp.bfloat16)
        .reshape(seq_count, span_len, kv_heads * head_dim)
    )
    queries = (
        query_rows.reshape(seq_count, span_len, kv_heads, group_size, head_dim)
        .transpose(0, 2, 3, 1, 4)
        .reshape(seq_count, kv_heads, stripe, head_dim)
    )
    query_index = wide_place * span_len + jnp.arange(stripe, dtype=jnp.int32) % span_len
    last_query = wide_place * span_len + span_len - 1

    def block_scores(key_block, key_first):
        scores = (
            jnp.einsum("skrd,sjkd->skrj", queries, key_block, preferred_element_type=jnp.float32)
            * score_scale
        )
        key_index = key_first + jnp.arange(key_block.shape[1], dtype=jnp.int32)
        allowed = key_index[None, :] <= query_index[:, None]
        return (scores, allowed)

    start_forward = (
        jnp.full((seq_count, kv_heads, stripe), -1e30, jnp.float32),
        jnp.zeros((seq_count, kv_heads, stripe), jnp.float32),
        jnp.zeros((seq_count, kv_heads, stripe, head_dim), jnp.float32),
    )
    running = start_forward
    pieces = (
        lax.all_gather(key_heads, "wide", axis=1, tiled=True),
        lax.all_gather(value_heads, "wide", axis=1, tiled=True),
    )
    key_blocks = split_blocks(pieces[0], seq_count, kv_heads, head_dim)
    value_blocks = split_blocks(pieces[1], seq_count, kv_heads, head_dim)
    block_len = key_blocks.shape[2]

    def advance(carried, block_item):
        key_block, value_block, block_index = block_item
        key_first = block_index * block_len

        def compute_block(current):
            run_max, run_sum, run_acc = current
            scores, allowed = block_scores(key_block, key_first)
            scores = jnp.where(allowed, scores, -1e30)
            new_max = jnp.maximum(run_max, jnp.max(scores, axis=-1))
            factor = jnp.exp(run_max - new_max)
            weights = jnp.where(allowed, jnp.exp(scores - new_max[..., None]), 0.0)
            new_sum = run_sum * factor + jnp.sum(weights, axis=-1)
            new_acc = run_acc * factor[..., None] + jnp.einsum(
                "skrj,sjkd->skrd",
                weights.astype(jnp.bfloat16),
                value_block,
                preferred_element_type=jnp.float32,
            )
            return (new_max, new_sum, new_acc)

        return (lax.cond(key_first <= last_query, compute_block, unchanged, carried), None)

    running, _ = lax.scan(
        advance,
        running,
        (key_blocks, value_blocks, jnp.arange(key_blocks.shape[0], dtype=jnp.int32)),
    )
    run_max, run_sum, run_acc = running
    attended = run_acc / run_sum[..., None]
    log_total = run_max + jnp.log(run_sum)
    attended_rows = (
        attended.reshape(seq_count, kv_heads, group_size, span_len, head_dim)
        .transpose(0, 3, 1, 2, 4)
        .reshape(row_count, head_count * head_dim)
        .astype(jnp.bfloat16)
    )
    middle = inputs + keep_rows * jnp.dot(attended_rows, out_w, preferred_element_type=jnp.float32)
    gain_two, gate_w, up_w, down_w = (
        lax.all_gather(mlp_gain, ("wide", "narrow"), axis=0, tiled=True),
        lax.all_gather(w_gate, ("wide", "narrow"), axis=0, tiled=True),
        lax.all_gather(w_up, ("wide", "narrow"), axis=0, tiled=True),
        lax.all_gather(w_down, ("wide", "narrow"), axis=0, tiled=True),
    )
    inverse_two = lax.rsqrt(jnp.mean(middle * middle, axis=-1, keepdims=True) + epsilon)
    second_norm = (middle * inverse_two * gain_two.astype(jnp.float32)).astype(jnp.bfloat16)
    gate_value = jnp.dot(second_norm, gate_w, preferred_element_type=jnp.float32)
    up_value = jnp.dot(second_norm, up_w, preferred_element_type=jnp.float32)
    gate_sigmoid = jax.nn.sigmoid(gate_value)
    swish_value = gate_value * gate_sigmoid
    hidden = (swish_value * up_value).astype(jnp.bfloat16)
    output = (
        middle + keep_rows * jnp.dot(hidden, down_w, preferred_element_type=jnp.float32)
    ).astype(jnp.bfloat16)
    group_match = (
        group_ids.reshape(row_count)[:, None]
        == jnp.arange(exit_scale.shape[0], dtype=jnp.int32)[None, :]
    )
    token_scale = jnp.sum(jnp.where(group_match, exit_scale[None, :], 0.0), axis=1, keepdims=True)
    upstream = out_grad.astype(jnp.float32).reshape(row_count, model_width) * token_scale
    gain_two, gate_w, up_w, down_w = (
        lax.all_gather(mlp_gain, ("wide", "narrow"), axis=0, tiled=True),
        lax.all_gather(w_gate, ("wide", "narrow"), axis=0, tiled=True),
        lax.all_gather(w_up, ("wide", "narrow"), axis=0, tiled=True),
        lax.all_gather(w_down, ("wide", "narrow"), axis=0, tiled=True),
    )
    mixed_grad = (keep_rows * upstream).astype(jnp.bfloat16)
    grad_down = over_rows(hidden, mixed_grad)
    hidden_grad = against(mixed_grad, down_w)
    gate_grad = (
        hidden_grad * up_value * gate_sigmoid * (1.0 + gate_value * (1.0 - gate_sigmoid))
    ).astype(jnp.bfloat16)
    up_grad = (hidden_grad * swish_value).astype(jnp.bfloat16)
    grad_gate = over_rows(second_norm, gate_grad)
    grad_up = over_rows(second_norm, up_grad)
    norm_grad = against(gate_grad, gate_w) + against(up_grad, up_w)
    grad_gain_two = jnp.sum(norm_grad * middle * inverse_two, axis=0)
    scaled_two = gain_two.astype(jnp.float32) * norm_grad
    middle_grad = (
        upstream
        + inverse_two * scaled_two
        - middle
        * (inverse_two * inverse_two * inverse_two)
        * jnp.mean(scaled_two * middle, axis=-1, keepdims=True)
    )
    gain_two_share, gate_share, up_share, down_share = (
        lax.psum_scatter(grad_gain_two, ("wide", "narrow"), scatter_dimension=0, tiled=True),
        lax.psum_scatter(grad_gate, ("wide", "narrow"), scatter_dimension=0, tiled=True),
        lax.psum_scatter(grad_up, ("wide", "narrow"), scatter_dimension=0, tiled=True),
        lax.psum_scatter(grad_down, ("wide", "narrow"), scatter_dimension=0, tiled=True),
    )
    gain_one, query_w, key_w, value_w, out_w = (
        lax.all_gather(attn_gain, ("wide", "narrow"), axis=0, tiled=True),
        lax.all_gather(w_query, ("wide", "narrow"), axis=0, tiled=True),
        lax.all_gather(w_key, ("wide", "narrow"), axis=0, tiled=True),
        lax.all_gather(w_value, ("wide", "narrow"), axis=0, tiled=True),
        lax.all_gather(w_out, ("wide", "narrow"), axis=0, tiled=True),
    )
    branch_grad = (keep_rows * middle_grad).astype(jnp.bfloat16)
    grad_out = over_rows(attended_rows, branch_grad)
    attended_grad = against(branch_grad, out_w).astype(jnp.bfloat16)
    grouped_grad = (
        attended_grad.reshape(seq_count, span_len, kv_heads, group_size, head_dim)
        .transpose(0, 2, 3, 1, 4)
        .reshape(seq_count, kv_heads, stripe, head_dim)
    )
    row_delta = jnp.sum(grouped_grad.astype(jnp.float32) * attended, axis=-1)
    start_backward = (
        jnp.zeros((seq_count, kv_heads, stripe, head_dim), jnp.float32),
        jnp.zeros((seq_count, full_len, kv_heads * head_dim), jnp.float32),
        jnp.zeros((seq_count, full_len, kv_heads * head_dim), jnp.float32),
    )
    running = start_backward
    pieces = (
        lax.all_gather(key_heads, "wide", axis=1, tiled=True),
        lax.all_gather(value_heads, "wide", axis=1, tiled=True),
    )
    key_blocks = split_blocks(pieces[0], seq_count, kv_heads, head_dim)
    value_blocks = split_blocks(pieces[1], seq_count, kv_heads, head_dim)
    fold_block_len = key_blocks.shape[2]

    def advance(carried, block_item):
        key_block, value_block, block_index = block_item
        key_first = block_index * fold_block_len

        def compute_block(current):
            query_acc, key_acc, value_acc = current
            scores, allowed = block_scores(key_block, key_first)
            probabilities = jnp.where(allowed, jnp.exp(scores - log_total[..., None]), 0.0)
            value_part = jnp.einsum(
                "skrj,skrd->sjkd",
                probabilities.astype(jnp.bfloat16),
                grouped_grad,
                preferred_element_type=jnp.float32,
            )
            prob_grad = jnp.einsum(
                "skrd,sjkd->skrj", grouped_grad, value_block, preferred_element_type=jnp.float32
            )
            score_grad = (probabilities * (prob_grad - row_delta[..., None])).astype(jnp.bfloat16)
            query_acc = (
                query_acc
                + jnp.einsum(
                    "skrj,sjkd->skrd", score_grad, key_block, preferred_element_type=jnp.float32
                )
                * score_scale
            )
            key_part = (
                jnp.einsum(
                    "skrj,skrd->sjkd", score_grad, queries, preferred_element_type=jnp.float32
                )
                * score_scale
            )
            key_acc = add_rows(
                key_acc, key_part.reshape(seq_count, fold_block_len, kv_heads * head_dim), key_first
            )
            value_acc = add_rows(
                value_acc,
                value_part.reshape(seq_count, fold_block_len, kv_heads * head_dim),
                key_first,
            )
            return (query_acc, key_acc, value_acc)

        return (lax.cond(key_first <= last_query, compute_block, unchanged, carried), None)

    running, _ = lax.scan(
        advance,
        running,
        (key_blocks, value_blocks, jnp.arange(key_blocks.shape[0], dtype=jnp.int32)),
    )
    query_acc, key_acc, value_acc = running
    key_sum, value_sum = (
        lax.psum_scatter(
            key_acc.astype(jnp.bfloat16), "wide", scatter_dimension=1, tiled=True
        ).astype(jnp.float32),
        lax.psum_scatter(
            value_acc.astype(jnp.bfloat16), "wide", scatter_dimension=1, tiled=True
        ).astype(jnp.float32),
    )
    query_back = (
        query_acc.reshape(seq_count, kv_heads, group_size, span_len, head_dim)
        .transpose(0, 3, 1, 2, 4)
        .reshape(row_count, head_count, head_dim)
    )
    query_grad = (
        rotate(query_back, token_pos, -1.0)
        .reshape(row_count, head_count * head_dim)
        .astype(jnp.bfloat16)
    )
    key_grad = (
        rotate(key_sum.reshape(row_count, kv_heads, head_dim), token_pos, -1.0)
        .reshape(row_count, kv_heads * head_dim)
        .astype(jnp.bfloat16)
    )
    value_grad = value_sum.reshape(row_count, kv_heads * head_dim).astype(jnp.bfloat16)
    grad_query = over_rows(first_norm, query_grad)
    grad_key = over_rows(first_norm, key_grad)
    grad_value = over_rows(first_norm, value_grad)
    input_norm_grad = (
        against(query_grad, query_w) + against(key_grad, key_w) + against(value_grad, value_w)
    )
    grad_gain_one = jnp.sum(input_norm_grad * inputs * inverse_one, axis=0)
    scaled_one = gain_one.astype(jnp.float32) * input_norm_grad
    input_grad = (
        middle_grad
        + inverse_one * scaled_one
        - inputs
        * (inverse_one * inverse_one * inverse_one)
        * jnp.mean(scaled_one * inputs, axis=-1, keepdims=True)
    )
    gain_one_share, query_share, key_share, value_share, out_share = (
        lax.psum_scatter(grad_gain_one, ("wide", "narrow"), scatter_dimension=0, tiled=True),
        lax.psum_scatter(grad_query, ("wide", "narrow"), scatter_dimension=0, tiled=True),
        lax.psum_scatter(grad_key, ("wide", "narrow"), scatter_dimension=0, tiled=True),
        lax.psum_scatter(grad_value, ("wide", "narrow"), scatter_dimension=0, tiled=True),
        lax.psum_scatter(grad_out, ("wide", "narrow"), scatter_dimension=0, tiled=True),
    )
    return (
        output.reshape(seq_count, span_len, model_width),
        input_grad.astype(jnp.bfloat16).reshape(seq_count, span_len, model_width),
        gain_one_share,
        query_share,
        key_share,
        value_share,
        out_share,
        gain_two_share,
        gate_share,
        up_share,
        down_share,
    )


def line_body(
    tokens,
    attn_gain,
    w_query,
    w_key,
    w_value,
    w_out,
    mlp_gain,
    w_gate,
    w_up,
    w_down,
    keep_mask,
    group_ids,
    positions,
    exit_scale,
    out_grad,
):
    f32 = jnp.float32
    bf16 = jnp.bfloat16
    _, span_len, model_width = tokens.shape
    line = lax.axis_size("z")
    rows_each = w_query.shape[0]
    q_cols = HEADS // line * HD

    group_match = group_ids[0][:, None] == jnp.arange(exit_scale.shape[0], dtype=jnp.int32)[None, :]
    token_scale = jnp.sum(jnp.where(group_match, exit_scale[None, :], 0.0), axis=1)
    freqs = 10000.0 ** (-2.0 * jnp.arange(HD // 2, dtype=f32) / HD)
    small = jnp.stack(
        [
            positions[0].astype(f32),
            token_scale,
            jnp.concatenate([freqs, freqs]),
            jnp.broadcast_to(keep_mask.astype(f32), (span_len,)),
        ]
    )
    small = jnp.broadcast_to(small[:, None], (4, 8, span_len))

    gain_row = jnp.concatenate([attn_gain, attn_gain, mlp_gain, mlp_gain])
    gain_row = jnp.pad(gain_row, (0, q_cols + 2 * HD - gain_row.shape[0]))
    gain_rows = jnp.broadcast_to(gain_row, (16, gain_row.shape[0]))
    (
        x_blocks,
        near_w,
        gain_all,
        first_norm,
        queries,
        both_kv,
        log_total,
        turns,
        attended_rows,
        ff_w,
        out_w,
        own_mixed,
    ) = forward_call(
        small,
        tokens[0],
        out_grad[0],
        gain_rows,
        (w_query, w_key, w_value, w_gate, w_up, w_out),
        line,
    )
    middle, norm_grad, output, grad_down, grad_ff, ff_half = mlp_call(
        small,
        gain_all,
        own_mixed,
        x_blocks,
        attended_rows,
        out_w,
        ff_w,
        w_down,
        line,
    )
    grad_down = grad_down.astype(f32)
    token_grad, ff_back, out_back, qkv_back = backward_call(
        (small, gain_all, middle, norm_grad),
        (tokens[0], out_grad[0]),
        (queries, both_kv, log_total, turns),
        out_w,
        attended_rows,
        near_w,
        first_norm,
        grad_ff,
        ff_half,
        line,
    )
    ff_back = ff_back.astype(f32)
    qkv_back = qkv_back.astype(f32)
    grad_out = jnp.sum(out_back.astype(f32), axis=0)
    heads_end, keys_end = w_query.shape[1], w_query.shape[1] + w_key.shape[1]
    grad_query = qkv_back[:, :heads_end]
    grad_key = qkv_back[:, heads_end:keys_end]
    grad_value = qkv_back[:, keys_end:]
    grad_gate = ff_back[:, : w_gate.shape[1]]
    grad_up = ff_back[:, w_gate.shape[1] :]

    def gain_grad(pairs, gain):
        total = sum(jnp.sum(weight.astype(f32) * grad, axis=1) for weight, grad in pairs)
        return total / gain.astype(f32)

    return (
        output[None],
        token_grad[None],
        gain_grad([(w_query, grad_query), (w_key, grad_key), (w_value, grad_value)], attn_gain),
        grad_query,
        grad_key,
        grad_value,
        grad_out,
        gain_grad([(w_gate, grad_gate), (w_up, grad_up)], mlp_gain),
        grad_gate,
        grad_up,
        grad_down,
    )


def solution(mesh):
    wide, narrow = mesh.shape["wide"], mesh.shape["narrow"]
    if wide == 2 * KVH and narrow == 4:
        mesh = Mesh(mesh.devices.reshape(wide // 2, 2, 2, 2), ("z", "x", "y", "c"))
        body, wide, narrow = line_body, ("z", "x"), ("y", "c")
    else:
        body, wide, narrow = general_body, ("wide",), ("narrow",)
    token_spec = P(narrow, wide, None)
    id_spec = P(narrow, wide)
    gain_spec = P(wide + narrow)
    weight_spec = P(wide + narrow, None)
    return jax.shard_map(
        body,
        mesh=mesh,
        in_specs=(
            token_spec,
            gain_spec,
            weight_spec,
            weight_spec,
            weight_spec,
            weight_spec,
            gain_spec,
            weight_spec,
            weight_spec,
            weight_spec,
            P(narrow),
            id_spec,
            id_spec,
            P(),
            token_spec,
        ),
        out_specs=(
            token_spec,
            token_spec,
            gain_spec,
            weight_spec,
            weight_spec,
            weight_spec,
            weight_spec,
            gain_spec,
            weight_spec,
            weight_spec,
            weight_spec,
        ),
        check_vma=False,
    )
```
